32 devices in a mesh: snap: 4 (over y, x), sp: 8 (over z, core).
Axes of the slice: x: 2, y: 2, z: 4, core: 2. Of those that a mesh axis runs over, the one named last changes fastest.
Arguments:
- fields: bfloat16 [16, 16, 180, 768], P('snap', 'sp'), may hold values from -6 to 6
- cotangent: bfloat16 [16, 16, 180, 768], P('snap', 'sp'), may hold values from -6 to 6
- valid_mask: int32 [16, 16, 180], P('snap', 'sp'), may hold values from 0 to 1, as said below
- kept_modes: int32 [16, 8], P(None, 'sp'), may hold values 0 or 1
- mlp_master: float32 [2, 768, 3072], P(None, 'sp'), may hold values from -0.21875 to 0.21875
- mlp_first: float32 [2, 768, 3072], P(None, 'sp'), may hold values from -384 to 384
- mlp_second: float32 [2, 768, 3072], P(None, 'sp'), may hold values from 2304 to 18432
- filter_master: float32 [4, 768, 96], P(None, 'sp'), may hold values from -1.25 to 1.25
- filter_first: float32 [4, 768, 96], P(None, 'sp'), may hold values from -448 to 448
- filter_second: float32 [4, 768, 96], P(None, 'sp'), may hold values from 2048 to 16384
- small_master: float32 [13, 768], P(None, 'sp'), may hold values from -1.2 to 1.8, as said below
- small_first: float32 [13, 768], P(None, 'sp'), may hold values from -896 to 896
- small_second: float32 [13, 768], P(None, 'sp'), may hold values from 4608 to 92160
- run_stats: float32 [2, 20], replicated, may hold values from -6 to 6
Outputs:
- block_out: bfloat16 [16, 16, 180, 768], P('snap', 'sp')
- input_grad: float32 [16, 16, 180, 768], P('snap', 'sp')
- mlp_new: float32 [2, 768, 3072], P(None, 'sp')
- mlp_first_new: float32 [2, 768, 3072], P(None, 'sp')
- mlp_second_new: float32 [2, 768, 3072], P(None, 'sp')
- mlp_copy: bfloat16 [2, 768, 3072], P(None, 'sp')
- filter_new: float32 [4, 768, 96], P(None, 'sp')
- filter_first_new: float32 [4, 768, 96], P(None, 'sp')
- filter_second_new: float32 [4, 768, 96], P(None, 'sp')
- filter_copy: bfloat16 [4, 768, 96], P(None, 'sp')
- small_new: float32 [13, 768], P(None, 'sp')
- small_first_new: float32 [13, 768], P(None, 'sp')
- small_second_new: float32 [13, 768], P(None, 'sp')
- small_copy: bfloat16 [13, 768], P(None, 'sp')
- stats_new: float32 [2, 20], replicated
The draws below stay inside these ranges and needn't reach their ends.
Inputs may be any that keep to these rules, and one draw needn't show every extreme that they name: `valid_mask`: the first longitude of every row is valid. `small_master`: gains (rows 0 and 2) lie about 1, the other rows about 0.
All inputs are finite; a program needn't handle non-finite values. No bound on the sum of `kept_modes` on one device may be relied on, other than what follows from the above.
Results may differ from the reference program's by a relative error of at most 0.025.
The reference program's roundings to bfloat16 on the way count: a program that leaves them out, or rounds other values in their place, can miss the bound.
Values may be sent and summed in bfloat16 or wider, within the bound.
A program may use at most 192 MiB of HBM per device.

```python
import functools
import math
import jax
import jax.numpy as jnp
from jax import lax

D = 768
FF = 3072
BLOCKS = 8
LON = 180
NVAR = 20
STEP = 10
BW = 96
LAT = 16
KEPT = 8
SNAPS = 16
PROWS = 13


def draw_valid_mask(key, part):
    key = jax.random.fold_in(key, 11)
    level_key = jax.random.fold_in(key, 5)
    level = jax.random.randint(level_key, (), 15, 101, dtype=jnp.int32)
    snap_index = jnp.arange(SNAPS, dtype=jnp.int32)[:, None, None]
    row_index = jnp.arange(LAT, dtype=jnp.int32)[None, :, None]
    limits = (LAT + 2 * row_index) * (SNAPS - 1 + 2 * snap_index) * 100 // (LAT * (SNAPS - 1))
    limits = limits * level // 100
    tickets = jax.random.randint(key, (SNAPS, LAT, LON), 0, 1000, dtype=jnp.int32)
    chosen = (tickets < limits).astype(jnp.int32)
    return chosen.at[:, :, 0].set(1)


def draw_small_master(key, part):
    key = jax.random.fold_in(key, 12)
    random_part = jnp.clip(jax.random.normal(key, (PROWS, D), jnp.float32), -4.0, 4.0)
    row_index = jnp.arange(PROWS, dtype=jnp.int32)[:, None]
    gain_rows = (row_index == 0) | (row_index == 2)
    return jnp.where(gain_rows, 1.0 + 0.2 * random_part, 0.3 * random_part)


def set_ends(entries, own_key, low, largest):
    spot = [jax.random.randint(jax.random.fold_in(own_key, axis), (), 0, length) for axis, length in enumerate(entries.shape)]
    main_axis = entries.shape.index(max(entries.shape))
    next_to = spot[:main_axis] + [(spot[main_axis] + 1) % entries.shape[main_axis]] + spot[main_axis + 1:]
    return entries.at[tuple(spot)].set(low).at[tuple(next_to)].set(largest)


def levels(stream_key, shape, shards, smallest, largest):
    loudness = 1.0
    for position, blocks in shards:
        steps = jax.random.uniform(jax.random.fold_in(jax.random.fold_in(stream_key, 6), position), (blocks,), jnp.float32, smallest / len(shards), largest / len(shards))
        loudness = loudness * jnp.repeat(jnp.exp(steps), shape[position] // blocks).reshape((-1,) + (1,) * (len(shape) - 1 - position))
    return loudness


def noise(stream_key, extent, deviation, reach, pieces=(), kind=jnp.bfloat16):
    drawn = deviation * jax.random.normal(stream_key, extent, jnp.float32)
    if pieces:
        drawn = drawn * levels(stream_key, extent, pieces, -0.22, 0.18)
    return jnp.clip(drawn, -reach, reach).astype(kind)


def setup_inputs(seed: int = 0) -> dict:
    keys = jax.random.split(jax.random.key(seed), 15)
    fields = noise(keys[0], (SNAPS, LAT, LON, D), 1.0, 6.0, ((0, 4), (1, 8)))
    cotangent = noise(keys[1], (SNAPS, LAT, LON, D), 1.0, 6.0, ((0, 4), (1, 8)))
    valid_mask = draw_valid_mask(jax.random.fold_in(keys[14], 71), 0)
    kept_modes = set_ends((jax.random.randint(keys[3], (LAT, KEPT), 0, 4) < 3).astype(jnp.int32), jax.random.fold_in(keys[3], 1), 0, 1)
    mlp_master = noise(keys[4], (2, D, FF), D ** -0.5, 0.21875, ((1, 8),), jnp.float32)
    mlp_first = noise(keys[5], (2, D, FF), (0.3 * (SNAPS * LAT * LON) ** 0.5), 384.0, ((1, 8),), jnp.float32)
    mlp_second = jnp.clip(jnp.exp(math.log(18432.0) - 2.0794415 * jax.random.uniform(keys[6], (2, D, FF), jnp.float32) ** levels(keys[6], (2, D, FF), ((1, 8),), -0.2, 0.2)), 2304.0, 18432.0)
    filter_master = noise(keys[7], (4, D, BW), (2.0 / BW ** 0.5), 1.25, ((1, 8),), jnp.float32)
    filter_first = noise(keys[8], (4, D, BW), (1.6 * (SNAPS * LAT * KEPT) ** 0.5), 448.0, ((1, 8),), jnp.float32)
    filter_second = jnp.clip(jnp.exp(math.log(16384.0) - 2.0794415 * jax.random.uniform(keys[9], (4, D, BW), jnp.float32) ** levels(keys[9], (4, D, BW), ((1, 8),), -0.2, 0.2)), 2048.0, 16384.0)
    small_master = draw_small_master(jax.random.fold_in(keys[14], 71), 0)
    small_first = noise(keys[11], (PROWS, D), ((0.5 * SNAPS * LAT * LON) ** 0.5), 896.0, ((1, 8),), jnp.float32)
    small_second = jnp.clip(jnp.exp(math.log(92160.0) - 2.9957323 * jax.random.uniform(keys[12], (PROWS, D), jnp.float32) ** levels(keys[12], (PROWS, D), ((1, 8),), -0.2, 0.2)), 4608.0, 92160.0)
    run_stats = noise(keys[13], (2, NVAR), 1.0, 6.0, (), jnp.float32)
    return dict(fields=fields, cotangent=cotangent, valid_mask=valid_mask, kept_modes=kept_modes, mlp_master=mlp_master, mlp_first=mlp_first, mlp_second=mlp_second, filter_master=filter_master, filter_first=filter_first, filter_second=filter_second, small_master=small_master, small_first=small_first, small_second=small_second, run_stats=run_stats)


@jax.custom_vjp
def low(v):
    return lax.optimization_barrier(v.astype(jnp.bfloat16)).astype(jnp.float32)

@jax.custom_vjp
def low_back(v):
    return v

def low_keep(v):
    return (low(v), None)

def low_pass(kept, grad):
    return (grad,)

def back_keep(v):
    return (v, None)

def back_low(kept, grad):
    return (low(grad),)
low.defvjp(low_keep, low_pass)
low_back.defvjp(back_keep, back_low)
eps_norm = 1e-06
shrink_level = 0.01
beta_one = 0.5
beta_two = 0.5
adam_eps = 1e-08
decay_rate = 0.01
rate_mlp = 0.03
rate_filter = 0.1
rate_small = 0.2
stat_decay = 0.5
precise = lax.Precision.HIGHEST

def layer_norm(values, gain_vec, shift_vec):
    centred = values - lax.optimization_barrier(jnp.mean(values, axis=-1, keepdims=True))
    spread = lax.optimization_barrier(jnp.mean(centred * centred, axis=-1, keepdims=True))
    return centred * lax.rsqrt(spread + eps_norm) * gain_vec + shift_vec

def shrink(values):
    return values - shrink_level * jnp.tanh(values / shrink_level)

def lon_tables(lon_total, mode_total):
    places = jnp.arange(lon_total, dtype=jnp.int32)
    orders = jnp.arange(mode_total, dtype=jnp.int32)
    angles = (places[:, None] * orders[None, :] % lon_total).astype(jnp.float32) * (2.0 * math.pi / lon_total)
    scaling = 1.0 / math.sqrt(lon_total)
    forward_tab = jnp.stack([jnp.cos(angles), -jnp.sin(angles)], axis=1) * scaling
    doubling = jnp.where(orders == 0, 1.0, 2.0).astype(jnp.float32)[:, None]
    inverse_tab = jnp.stack([jnp.cos(angles).T * doubling, -jnp.sin(angles).T * doubling], axis=0) * scaling
    return (forward_tab.astype(jnp.bfloat16), inverse_tab.astype(jnp.bfloat16))

def lat_table(lat_total):
    places = jnp.arange(lat_total, dtype=jnp.int32)
    angles = (places[:, None] * places[None, :] % lat_total).astype(jnp.float32) * (2.0 * math.pi / lat_total)
    cosine = jnp.cos(angles)
    sine_part = jnp.sin(angles)
    upper_rows = jnp.stack([cosine, sine_part], axis=1)
    bottom = jnp.stack([-sine_part, cosine], axis=1)
    return (jnp.stack([upper_rows, bottom], axis=0) / math.sqrt(lat_total)).astype(jnp.bfloat16)

def complex_pair(real_part, imag_part):
    return jnp.stack([jnp.stack([real_part, -imag_part]), jnp.stack([imag_part, real_part])])

def widen(table):
    return lax.optimization_barrier(table).astype(jnp.float32)

def copy_low(master):
    return lax.optimization_barrier(master.astype(jnp.bfloat16)).astype(jnp.float32)

def forward(fields_one, mlp_w, filt_w, small_w, kept_float, lon_fwd, lon_inv, lat_fwd):
    lat_total, lon_total, channel = fields_one.shape
    mode_total = kept_float.shape[1]
    block_width = channel // BLOCKS
    normed = layer_norm(fields_one, small_w[0], small_w[1])
    normed_low = low(normed)
    spec_lon = low_back(low(jnp.einsum('rld,lqm->rqmd', normed_low, lon_fwd, precision=precise)))
    spectrum = low_back(low(jnp.einsum('pkqr,rqmd->kpmd', lat_fwd, spec_lon, precision=precise)))
    blocked = spectrum.reshape(lat_total, 2, mode_total, BLOCKS, block_width)
    weights = filt_w.reshape(4, BLOCKS, block_width, block_width)
    first_pair = complex_pair(weights[0], weights[1])
    second_pair = complex_pair(weights[2], weights[3])
    bias_one = small_w[4:6].reshape(2, 1, BLOCKS, block_width)
    bias_two = small_w[6:8].reshape(2, 1, BLOCKS, block_width)
    pre_one = low_back(jnp.einsum('kqmbi,pqbio->kpmbo', blocked, first_pair, precision=precise) + bias_one)
    act_one = low(jax.nn.gelu(pre_one))
    pre_two = low_back(jnp.einsum('kqmbi,pqbio->kpmbo', act_one, second_pair, precision=precise) + bias_two)
    masked = low(shrink(pre_two) * kept_float[:, None, :, None, None])
    masked = masked.reshape(lat_total, 2, mode_total, channel)
    returned = low_back(low(jnp.einsum('pkqr,kpmd->rqmd', lat_fwd, masked, precision=precise)))
    filtered = low_back(jnp.einsum('rqmd,qml->rld', returned, lon_inv, precision=precise))
    mixture = fields_one + normed + filtered
    normed_two = low(layer_norm(mixture, small_w[2], small_w[3]))
    hidden_pre = low_back(jnp.einsum('rld,df->rlf', normed_two, mlp_w[0], precision=precise) + small_w[9:].reshape(-1))
    hidden = low(jax.nn.gelu(hidden_pre))
    return mixture + jnp.einsum('rlf,df->rld', hidden, mlp_w[1], precision=precise) + small_w[8]

def adamw(master, first_mom, second_mom, gradient, step_rate):
    first_next = beta_one * first_mom + (1.0 - beta_one) * gradient
    second_next = beta_two * second_mom + (1.0 - beta_two) * gradient * gradient
    fix_one = 1.0 - beta_one ** STEP
    fix_two = 1.0 - beta_two ** STEP
    direction = first_next / fix_one / (jnp.sqrt(second_next / fix_two) + adam_eps)
    master_next = master - step_rate * (direction + decay_rate * master)
    return (master_next, first_next, second_next, master_next.astype(jnp.bfloat16))

def reference(fields, cotangent, valid_mask, kept_modes, mlp_master, mlp_first, mlp_second, filter_master, filter_first, filter_second, small_master, small_first, small_second, run_stats):
    lon_total = fields.shape[2]
    lat_total = fields.shape[1]
    mode_total = kept_modes.shape[1]
    lon_fwd, lon_inv = lon_tables(lon_total, mode_total)
    lon_fwd = widen(lon_fwd)
    lon_inv = widen(lon_inv)
    lat_fwd = widen(lat_table(lat_total))
    mlp_w = copy_low(mlp_master)
    filt_w = copy_low(filter_master)
    small_w = copy_low(small_master)
    kept_float = kept_modes.astype(jnp.float32)
    apply_block = functools.partial(forward, kept_float=kept_float, lon_fwd=lon_fwd, lon_inv=lon_inv, lat_fwd=lat_fwd)

    def one_snapshot(running, inputs):
        fields_one, cot_one, valid_one = inputs
        output, pull = jax.vjp(apply_block, fields_one.astype(jnp.float32), mlp_w, filt_w, small_w)
        grad_in, grad_mlp, grad_filt, grad_small = pull(cot_one.astype(jnp.float32))
        weight_mask = valid_one.astype(jnp.float32)[:, :, None]
        variables = output[:, :, :NVAR]
        sums = jnp.stack([lax.optimization_barrier(jnp.sum(weight_mask * variables, axis=(0, 1))), lax.optimization_barrier(jnp.sum(weight_mask * variables * variables, axis=(0, 1)))])
        running = (running[0] + grad_mlp, running[1] + grad_filt, running[2] + grad_small, running[3] + sums)
        return (running, (output.astype(jnp.bfloat16), grad_in))
    start = (jnp.zeros(mlp_master.shape, jnp.float32), jnp.zeros(filter_master.shape, jnp.float32), jnp.zeros(small_master.shape, jnp.float32), jnp.zeros((2, NVAR), jnp.float32))
    totals, outputs = lax.scan(one_snapshot, start, (fields, cotangent, valid_mask))
    block_out, input_grad = outputs
    positions = fields.shape[0] * lat_total * lon_total
    stats_new = stat_decay * run_stats + (1.0 - stat_decay) * totals[3] / positions
    mlp_new, mlp_first_new, mlp_second_new, mlp_copy = adamw(mlp_master, mlp_first, mlp_second, totals[0], rate_mlp)
    filter_new, filter_first_new, filter_second_new, filter_copy = adamw(filter_master, filter_first, filter_second, totals[1], rate_filter)
    small_new, small_first_new, small_second_new, small_copy = adamw(small_master, small_first, small_second, totals[2], rate_small)
    return (block_out, input_grad, mlp_new, mlp_first_new, mlp_second_new, mlp_copy, filter_new, filter_first_new, filter_second_new, filter_copy, small_new, small_first_new, small_second_new, small_copy, stats_new)
```

```python
import functools
import math

import jax
import jax.numpy as jnp
from jax import lax
from jax.experimental import pallas as pl
from jax.experimental.pallas import tpu as pltpu
from jax.sharding import PartitionSpec as P

BLOCKS = 8
NVAR = 20
STEP = 10


eps_norm = 1e-06
shrink_level = 0.01
beta_one = 0.5
beta_two = 0.5
adam_eps = 1e-08
decay_rate = 0.01
rate_mlp = 0.03
rate_filter = 0.1
rate_small = 0.2
stat_decay = 0.5


def layer_norm(values, gain_vec, shift_vec):
    centred = values - jnp.mean(values, axis=-1, keepdims=True)
    spread = jnp.mean(centred * centred, axis=-1, keepdims=True)
    return centred * lax.rsqrt(spread + eps_norm) * gain_vec + shift_vec


def shrink(values):
    return values - shrink_level * jnp.tanh(values / shrink_level)


def lon_tables(lon_total, mode_total):
    places = jnp.arange(lon_total, dtype=jnp.int32)
    orders = jnp.arange(mode_total, dtype=jnp.int32)
    angles = (places[:, None] * orders[None, :] % lon_total).astype(jnp.float32) * (
        2.0 * math.pi / lon_total
    )
    scaling = 1.0 / math.sqrt(lon_total)
    forward_tab = jnp.stack([jnp.cos(angles), -jnp.sin(angles)], axis=1) * scaling
    doubling = jnp.where(orders == 0, 1.0, 2.0).astype(jnp.float32)[:, None]
    inverse_tab = (
        jnp.stack([jnp.cos(angles).T * doubling, -jnp.sin(angles).T * doubling], axis=0) * scaling
    )
    return (forward_tab.astype(jnp.bfloat16), inverse_tab.astype(jnp.bfloat16))


def lat_table(lat_total):
    places = jnp.arange(lat_total, dtype=jnp.int32)
    angles = (places[:, None] * places[None, :] % lat_total).astype(jnp.float32) * (
        2.0 * math.pi / lat_total
    )
    cosine = jnp.cos(angles)
    sine_part = jnp.sin(angles)
    upper_rows = jnp.stack([cosine, sine_part], axis=1)
    bottom = jnp.stack([-sine_part, cosine], axis=1)
    return (jnp.stack([upper_rows, bottom], axis=0) / math.sqrt(lat_total)).astype(jnp.bfloat16)


def complex_pair(real_part, imag_part):
    return jnp.stack([jnp.stack([real_part, -imag_part]), jnp.stack([imag_part, real_part])])


gelu_scale = math.sqrt(2.0 / math.pi)
gelu_cubic = 0.044715


def gelu_both(value):
    square = value * value
    bent = jnp.tanh(gelu_scale * value * (1.0 + gelu_cubic * square))
    half = 0.5 + 0.5 * bent
    slope = half + (0.5 * gelu_scale) * value * (1.0 - bent * bent) * (
        1.0 + (3.0 * gelu_cubic) * square
    )
    return value * half, slope


def dot_nt(left, right):
    return lax.dot_general(
        left, right, (((1,), (1,)), ((), ())), preferred_element_type=jnp.float32
    )


def dot_nn(left, right):
    return jnp.dot(left, right, preferred_element_type=jnp.float32)


def divisor(total, unit, most):
    return max(size for size in range(unit, most + 1, unit) if total % size == 0)


def mlp_body(
    tile,
    normed_ref,
    cot_ref,
    up_ref,
    down_ref,
    bias_ref,
    out_ref,
    back_ref,
    grad_up_ref,
    grad_down_ref,
    grad_bias_ref,
    normed_turned,
    cot_turned,
    act_ref,
    slope_ref,
):
    tokens = normed_ref.shape[0]

    @pl.when(pl.program_id(0) == 0)
    def _():
        normed_turned[...] = normed_ref[...].T
        cot_turned[...] = cot_ref[...].T
        out_ref[...] = jnp.zeros_like(out_ref)
        back_ref[...] = jnp.zeros_like(back_ref)

    grad_bias_ref[...] = jnp.zeros_like(grad_bias_ref)

    @pl.loop(0, tokens // tile)
    def _(step):
        rows = pl.ds(pl.multiple_of(step * tile, tile), tile)
        act, slope = gelu_both(dot_nn(normed_ref[rows, :], up_ref[...]) + bias_ref[...])
        act = act.astype(jnp.bfloat16)
        slope = (dot_nn(cot_ref[rows, :], down_ref[...]) * slope).astype(jnp.bfloat16)
        act_ref[rows, :] = act
        slope_ref[rows, :] = slope
        grad_bias_ref[...] += jnp.sum(slope.astype(jnp.float32), axis=0, keepdims=True)
        out_ref[rows, :] += dot_nt(act, down_ref[...])
        back_ref[rows, :] += dot_nt(slope, up_ref[...])

    grad_up_ref[...] = dot_nn(normed_turned[...], slope_ref[...]).astype(grad_up_ref.dtype)
    grad_down_ref[...] = dot_nn(cot_turned[...], act_ref[...]).astype(grad_down_ref.dtype)


def mlp_pass(normed, cot, weights, bias):
    tokens, channel = normed.shape
    hidden = weights.shape[2]
    width = divisor(hidden, 128, 512)
    tile = divisor(tokens, 16, 480)
    whole = pl.BlockSpec((tokens, channel), lambda j: (0, 0))
    block = pl.BlockSpec((channel, width), lambda j: (0, j))
    line = pl.BlockSpec((1, width), lambda j: (0, j))
    part = lambda which: pl.BlockSpec((None, channel, width), lambda j: (which, 0, j))
    total = jax.ShapeDtypeStruct((tokens, channel), jnp.float32)
    grads = jax.ShapeDtypeStruct((channel, hidden), jnp.bfloat16)
    return pl.pallas_call(
        functools.partial(mlp_body, tile),
        grid=(hidden // width,),
        in_specs=[whole, whole, part(0), part(1), line],
        out_specs=[whole, whole, block, block, line],
        out_shape=[total, total, grads, grads, jax.ShapeDtypeStruct((1, hidden), jnp.float32)],
        scratch_shapes=[
            pltpu.VMEM((channel, tokens), jnp.bfloat16),
            pltpu.VMEM((channel, tokens), jnp.bfloat16),
            pltpu.VMEM((tokens, width), jnp.bfloat16),
            pltpu.VMEM((tokens, width), jnp.bfloat16),
        ],
        compiler_params=pltpu.CompilerParams(vmem_limit_bytes=56 * 1024 * 1024),
        cost_estimate=pl.CostEstimate(
            flops=12 * tokens * channel * hidden,
            bytes_accessed=8 * channel * hidden + 12 * tokens * channel,
            transcendentals=tokens * hidden,
        ),
        name="mlp_pass",
    )(normed, cot, weights, weights, bias)


def spectral_front(arrived, lat_fwd, first_pair, second_pair, bias_one, bias_two):
    spectrum = jnp.einsum(
        "pkqr,nrqmd->nkpmd", lat_fwd, arrived, preferred_element_type=jnp.float32
    ).astype(jnp.bfloat16)
    snap_local, lat_total, pair_count, mode_local, channel = spectrum.shape
    blocked = spectrum.reshape(
        snap_local, lat_total, pair_count, mode_local, BLOCKS, channel // BLOCKS
    )
    pre_one = (
        jnp.einsum("nkqmbi,pqbio->nkpmbo", blocked, first_pair, preferred_element_type=jnp.float32)
        + bias_one
    )
    act_one = jax.nn.gelu(pre_one).astype(jnp.bfloat16)
    pre_two = (
        jnp.einsum("nkqmbi,pqbio->nkpmbo", act_one, second_pair, preferred_element_type=jnp.float32)
        + bias_two
    )
    return (blocked, pre_one, act_one, pre_two)


def adamw(master, first_mom, second_mom, gradient, step_rate):
    first_next = beta_one * first_mom + (1.0 - beta_one) * gradient
    second_next = beta_two * second_mom + (1.0 - beta_two) * gradient * gradient
    fix_one = 1.0 - beta_one**STEP
    fix_two = 1.0 - beta_two**STEP
    direction = first_next / fix_one / (jnp.sqrt(second_next / fix_two) + adam_eps)
    master_next = master - step_rate * (direction + decay_rate * master)
    return (master_next, first_next, second_next, master_next.astype(jnp.bfloat16))


def per_device(
    fields,
    cotangent,
    valid_mask,
    kept_modes,
    mlp_master,
    mlp_first,
    mlp_second,
    filter_master,
    filter_first,
    filter_second,
    small_master,
    small_first,
    small_second,
    run_stats,
):
    group_size = lax.axis_size("sp")
    snap_local, row_local, lon_total, channel = fields.shape
    lat_total = row_local * group_size
    mode_local = kept_modes.shape[1]
    mode_total = mode_local * group_size
    block_width = channel // BLOCKS
    lon_fwd, lon_inv = lon_tables(lon_total, mode_total)
    lat_fwd = lat_table(lat_total)
    mlp_w, filt_w, small_w = (
        lax.all_gather(mlp_master.astype(jnp.bfloat16), "sp", axis=1, tiled=True),
        lax.all_gather(filter_master.astype(jnp.bfloat16), "sp", axis=1, tiled=True),
        lax.all_gather(small_master.astype(jnp.bfloat16), "sp", axis=1, tiled=True),
    )
    small_f = small_w.astype(jnp.float32)
    weights = filt_w.reshape(4, BLOCKS, block_width, block_width)
    first_pair = complex_pair(weights[0], weights[1])
    second_pair = complex_pair(weights[2], weights[3])
    bias_one = small_f[4:6].reshape(2, 1, BLOCKS, block_width)
    bias_two = small_f[6:8].reshape(2, 1, BLOCKS, block_width)
    fields_float = fields.astype(jnp.float32)
    normed, norm_pull = jax.vjp(layer_norm, fields_float, small_f[0], small_f[1])
    normed_low = normed.astype(jnp.bfloat16)
    spec_lon = jnp.einsum(
        "nrld,lqm->nrqmd", normed_low, lon_fwd, preferred_element_type=jnp.float32
    ).astype(jnp.bfloat16)
    arrived = lax.all_to_all(spec_lon, "sp", split_axis=3, concat_axis=1, tiled=True)
    spectral = spectral_front(arrived, lat_fwd, first_pair, second_pair, bias_one, bias_two)
    keep_mask = kept_modes.astype(jnp.float32)[None, :, None, :, None, None]
    masked = (shrink(spectral[3]) * keep_mask).astype(jnp.bfloat16)
    masked = masked.reshape(snap_local, lat_total, 2, mode_local, channel)
    returned = jnp.einsum(
        "pkqr,nkpmd->nrqmd", lat_fwd, masked, preferred_element_type=jnp.float32
    ).astype(jnp.bfloat16)
    home_modes = lax.all_to_all(returned, "sp", split_axis=1, concat_axis=3, tiled=True)
    filtered = jnp.einsum(
        "nrqmd,qml->nrld", home_modes, lon_inv, preferred_element_type=jnp.float32
    )
    mixture = fields_float + normed + filtered
    normed_two, norm_two_pull = jax.vjp(layer_norm, mixture, small_f[2], small_f[3])
    normed_two_low = normed_two.astype(jnp.bfloat16)
    tokens = snap_local * row_local * lon_total
    passed = mlp_pass(
        normed_two_low.reshape(tokens, channel),
        cotangent.reshape(tokens, channel),
        mlp_w,
        small_f[9:].reshape(1, -1),
    )
    output = mixture + passed[0].reshape(mixture.shape) + small_f[8]
    weight_mask = valid_mask.astype(jnp.float32)[..., None]
    variables = output[..., :NVAR]
    local_sums = jnp.stack(
        [
            jnp.sum(weight_mask * variables, axis=(0, 1, 2)),
            jnp.sum(weight_mask * variables * variables, axis=(0, 1, 2)),
        ]
    )
    total_sums = lax.psum(local_sums, ("snap", "sp"))
    positions = snap_local * lax.axis_size("snap") * lat_total * lon_total
    stats_new = stat_decay * run_stats + (1.0 - stat_decay) * total_sums / positions
    cot_float = cotangent.astype(jnp.float32)
    grad_normed_two = passed[1].reshape(mixture.shape)
    grad_bias_hidden = passed[4]
    grad_mix_norm, grad_gain_two, grad_shift_two = norm_two_pull(grad_normed_two)
    grad_mixture = cot_float + grad_mix_norm
    grad_bias_out = jnp.sum(cot_float, axis=(0, 1, 2))
    grad_filtered = grad_mixture.astype(jnp.bfloat16)
    grad_home = jnp.einsum(
        "nrld,qml->nrqmd", grad_filtered, lon_inv, preferred_element_type=jnp.float32
    ).astype(jnp.bfloat16)
    grad_returned = lax.all_to_all(grad_home, "sp", split_axis=3, concat_axis=1, tiled=True)
    grad_masked = jnp.einsum(
        "pkqr,nrqmd->nkpmd", lat_fwd, grad_returned, preferred_element_type=jnp.float32
    )
    arrived_again = lax.all_to_all(spec_lon, "sp", split_axis=3, concat_axis=1, tiled=True)
    used_front = spectral_front(arrived_again, lat_fwd, first_pair, second_pair, bias_one, bias_two)
    blocked, pre_one, act_one, pre_two = used_front
    grad_two = jax.vjp(shrink, pre_two)[1](grad_masked.reshape(pre_two.shape) * keep_mask)[
        0
    ].astype(jnp.bfloat16)
    grad_bias_two = jnp.sum(grad_two.astype(jnp.float32), axis=(0, 1, 3))
    grad_second = jnp.einsum(
        "nkqmbi,nkpmbo->pqbio", act_one, grad_two, preferred_element_type=jnp.float32
    )
    grad_act = jnp.einsum(
        "nkpmbo,pqbio->nkqmbi", grad_two, second_pair, preferred_element_type=jnp.float32
    )
    grad_one = jax.vjp(jax.nn.gelu, pre_one)[1](grad_act)[0].astype(jnp.bfloat16)
    grad_bias_one = jnp.sum(grad_one.astype(jnp.float32), axis=(0, 1, 3))
    grad_first = jnp.einsum(
        "nkqmbi,nkpmbo->pqbio", blocked, grad_one, preferred_element_type=jnp.float32
    )
    grad_spectrum = jnp.einsum(
        "nkpmbo,pqbio->nkqmbi", grad_one, first_pair, preferred_element_type=jnp.float32
    ).astype(jnp.bfloat16)
    grad_spectrum = grad_spectrum.reshape(snap_local, lat_total, 2, mode_local, channel)
    grad_lon = jnp.einsum(
        "pkqr,nkpmd->nrqmd", lat_fwd, grad_spectrum, preferred_element_type=jnp.float32
    ).astype(jnp.bfloat16)
    grad_rows = lax.all_to_all(grad_lon, "sp", split_axis=1, concat_axis=3, tiled=True)
    grad_normed = grad_mixture + jnp.einsum(
        "nrqmd,lqm->nrld", grad_rows, lon_fwd, preferred_element_type=jnp.float32
    )
    grad_field_norm, grad_gain_one, grad_shift_one = norm_pull(grad_normed)
    input_grad = grad_mixture + grad_field_norm
    grad_filter = jnp.stack(
        [
            grad_first[0, 0] + grad_first[1, 1],
            grad_first[1, 0] - grad_first[0, 1],
            grad_second[0, 0] + grad_second[1, 1],
            grad_second[1, 0] - grad_second[0, 1],
        ]
    ).reshape(4, channel, block_width)
    grad_small = jnp.concatenate(
        [
            jnp.stack([grad_gain_one, grad_shift_one, grad_gain_two, grad_shift_two]),
            grad_bias_one.reshape(2, channel),
            grad_bias_two.reshape(2, channel),
            grad_bias_out[None, :],
            grad_bias_hidden.reshape(-1, channel),
        ],
        axis=0,
    )
    shares = (
        jnp.stack([
            lax.psum_scatter(part, "sp", scatter_dimension=0, tiled=True) for part in passed[2:4]
        ]),
        lax.psum_scatter(grad_filter, "sp", scatter_dimension=1, tiled=True),
        lax.psum_scatter(grad_small, "sp", scatter_dimension=1, tiled=True),
    )
    owned = (
        lax.psum(shares[0].astype(jnp.bfloat16), "snap").astype(jnp.float32),
        lax.psum(shares[1].astype(jnp.bfloat16), "snap").astype(jnp.float32),
        lax.psum(shares[2].astype(jnp.bfloat16), "snap").astype(jnp.float32),
    )
    mlp_new, mlp_first_new, mlp_second_new, mlp_copy = adamw(
        mlp_master, mlp_first, mlp_second, owned[0], rate_mlp
    )
    filter_new, filter_first_new, filter_second_new, filter_copy = adamw(
        filter_master, filter_first, filter_second, owned[1], rate_filter
    )
    small_new, small_first_new, small_second_new, small_copy = adamw(
        small_master, small_first, small_second, owned[2], rate_small
    )
    return (
        output.astype(jnp.bfloat16),
        input_grad,
        mlp_new,
        mlp_first_new,
        mlp_second_new,
        mlp_copy,
        filter_new,
        filter_first_new,
        filter_second_new,
        filter_copy,
        small_new,
        small_first_new,
        small_second_new,
        small_copy,
        stats_new,
    )


def solution(mesh):
    return jax.shard_map(
        per_device,
        mesh=mesh,
        in_specs=(
            P("snap", "sp", None, None),
            P("snap", "sp", None, None),
            P("snap", "sp", None),
            P(None, "sp"),
            P(None, "sp", None),
            P(None, "sp", None),
            P(None, "sp", None),
            P(None, "sp", None),
            P(None, "sp", None),
            P(None, "sp", None),
            P(None, "sp"),
            P(None, "sp"),
            P(None, "sp"),
            P(),
        ),
        out_specs=(
            P("snap", "sp", None, None),
            P("snap", "sp", None, None),
            P(None, "sp", None),
            P(None, "sp", None),
            P(None, "sp", None),
            P(None, "sp", None),
            P(None, "sp", None),
            P(None, "sp", None),
            P(None, "sp", None),
            P(None, "sp", None),
            P(None, "sp"),
            P(None, "sp"),
            P(None, "sp"),
            P(None, "sp"),
            P(),
        ),
        check_vma=False,
    )
```

```python
import functools
import math

import jax
import jax.numpy as jnp
import ml_dtypes
import numpy as np
from jax import lax
from jax.experimental import pallas as pl
from jax.experimental.pallas import tpu as pltpu
from jax.sharding import PartitionSpec as P

BLOCKS = 8
NVAR = 20
STEP = 10
VMEM_LIMIT = 63 * 1024 * 1024


eps_norm = 1e-06
shrink_level = 0.01
beta_one = 0.5
beta_two = 0.5
adam_eps = 1e-08
decay_rate = 0.01
rate_mlp = 0.03
rate_filter = 0.1
rate_small = 0.2
stat_decay = 0.5


def layer_norm(values, gain_vec, shift_vec):
    centred = values - jnp.mean(values, axis=-1, keepdims=True)
    spread = jnp.mean(centred * centred, axis=-1, keepdims=True)
    return centred * lax.rsqrt(spread + eps_norm) * gain_vec + shift_vec


def shrink(values):
    return values - shrink_level * jnp.tanh(values / shrink_level)


def lon_tables(lon_total, mode_total):
    places = jnp.arange(lon_total, dtype=jnp.int32)
    orders = jnp.arange(mode_total, dtype=jnp.int32)
    angles = (places[:, None] * orders[None, :] % lon_total).astype(jnp.float32) * (
        2.0 * math.pi / lon_total
    )
    scaling = 1.0 / math.sqrt(lon_total)
    forward_tab = jnp.stack([jnp.cos(angles), -jnp.sin(angles)], axis=1) * scaling
    doubling = jnp.where(orders == 0, 1.0, 2.0).astype(jnp.float32)[:, None]
    inverse_tab = (
        jnp.stack([jnp.cos(angles).T * doubling, -jnp.sin(angles).T * doubling], axis=0) * scaling
    )
    return (forward_tab.astype(jnp.bfloat16), inverse_tab.astype(jnp.bfloat16))


def lat_table(lat_total):
    places = jnp.arange(lat_total, dtype=jnp.int32)
    angles = (places[:, None] * places[None, :] % lat_total).astype(jnp.float32) * (
        2.0 * math.pi / lat_total
    )
    cosine = jnp.cos(angles)
    sine_part = jnp.sin(angles)
    upper_rows = jnp.stack([cosine, sine_part], axis=1)
    bottom = jnp.stack([-sine_part, cosine], axis=1)
    return (jnp.stack([upper_rows, bottom], axis=0) / math.sqrt(lat_total)).astype(jnp.bfloat16)


def complex_pair(real_part, imag_part):
    return jnp.stack([jnp.stack([real_part, -imag_part]), jnp.stack([imag_part, real_part])])


gelu_scale = math.sqrt(2.0 / math.pi)
gelu_cubic = 0.044715


def gelu_both(value):
    square = value * value
    bent = jnp.tanh(gelu_scale * value * (1.0 + gelu_cubic * square))
    half = 0.5 + 0.5 * bent
    slope = half + (0.5 * gelu_scale) * value * (1.0 - bent * bent) * (
        1.0 + (3.0 * gelu_cubic) * square
    )
    return value * half, slope


def dot_nt(left, right):
    return lax.dot_general(
        left, right, (((1,), (1,)), ((), ())), preferred_element_type=jnp.float32
    )


def dot_nn(left, right):
    return jnp.dot(left, right, preferred_element_type=jnp.float32)


def divisor(total, unit, most):
    return max(size for size in range(unit, most + 1, unit) if total % size == 0)


def mlp_body(
    tile,
    normed_ref,
    cot_ref,
    up_ref,
    down_ref,
    bias_ref,
    out_ref,
    back_ref,
    grad_up_ref,
    grad_down_ref,
    grad_bias_ref,
    normed_turned,
    cot_turned,
    act_ref,
    slope_ref,
):
    tokens = normed_ref.shape[0]

    @pl.when(pl.program_id(0) == 0)
    def _():
        normed_turned[...] = normed_ref[...].T
        cot_turned[...] = cot_ref[...].T
        out_ref[...] = jnp.zeros_like(out_ref)
        back_ref[...] = jnp.zeros_like(back_ref)

    grad_bias_ref[...] = jnp.zeros_like(grad_bias_ref)

    @pl.loop(0, tokens // tile)
    def _(step):
        rows = pl.ds(pl.multiple_of(step * tile, tile), tile)
        act, slope = gelu_both(dot_nn(normed_ref[rows, :], up_ref[...]) + bias_ref[...])
        act = act.astype(jnp.bfloat16)
        slope = (dot_nn(cot_ref[rows, :], down_ref[...]) * slope).astype(jnp.bfloat16)
        act_ref[rows, :] = act
        slope_ref[rows, :] = slope
        grad_bias_ref[...] += jnp.sum(slope.astype(jnp.float32), axis=0, keepdims=True)
        out_ref[rows, :] += dot_nt(act, down_ref[...])
        back_ref[rows, :] += dot_nt(slope, up_ref[...])

    grad_up_ref[...] = dot_nn(normed_turned[...], slope_ref[...]).astype(grad_up_ref.dtype)
    grad_down_ref[...] = dot_nn(cot_turned[...], act_ref[...]).astype(grad_down_ref.dtype)


def mlp_pass(normed, cot, weights, bias):
    tokens, channel = normed.shape
    hidden = weights.shape[2]
    width = divisor(hidden, 128, 512)
    tile = divisor(tokens, 16, 480)
    whole = pl.BlockSpec((tokens, channel), lambda j: (0, 0))
    block = pl.BlockSpec((channel, width), lambda j: (0, j))
    line = pl.BlockSpec((1, width), lambda j: (0, j))
    part = lambda which: pl.BlockSpec((None, channel, width), lambda j: (which, 0, j))
    total = jax.ShapeDtypeStruct((tokens, channel), jnp.float32)
    grads = jax.ShapeDtypeStruct((channel, hidden), jnp.bfloat16)
    return pl.pallas_call(
        functools.partial(mlp_body, tile),
        grid=(hidden // width,),
        in_specs=[whole, whole, part(0), part(1), line],
        out_specs=[whole, whole, block, block, line],
        out_shape=[total, total, grads, grads, jax.ShapeDtypeStruct((1, hidden), jnp.float32)],
        scratch_shapes=[
            pltpu.VMEM((channel, tokens), jnp.bfloat16),
            pltpu.VMEM((channel, tokens), jnp.bfloat16),
            pltpu.VMEM((tokens, width), jnp.bfloat16),
            pltpu.VMEM((tokens, width), jnp.bfloat16),
        ],
        compiler_params=pltpu.CompilerParams(vmem_limit_bytes=56 * 1024 * 1024),
        cost_estimate=pl.CostEstimate(
            flops=12 * tokens * channel * hidden,
            bytes_accessed=8 * channel * hidden + 12 * tokens * channel,
            transcendentals=tokens * hidden,
        ),
        name="mlp_pass",
    )(normed, cot, weights, weights, bias)


def spectral_front(arrived, lat_fwd, first_pair, second_pair, bias_one, bias_two):
    spectrum = jnp.einsum(
        "pkqr,nrqmd->nkpmd", lat_fwd, arrived, preferred_element_type=jnp.float32
    ).astype(jnp.bfloat16)
    snap_local, lat_total, pair_count, mode_local, channel = spectrum.shape
    blocked = spectrum.reshape(
        snap_local, lat_total, pair_count, mode_local, BLOCKS, channel // BLOCKS
    )
    pre_one = (
        jnp.einsum("nkqmbi,pqbio->nkpmbo", blocked, first_pair, preferred_element_type=jnp.float32)
        + bias_one
    )
    act_one = jax.nn.gelu(pre_one).astype(jnp.bfloat16)
    pre_two = (
        jnp.einsum("nkqmbi,pqbio->nkpmbo", act_one, second_pair, preferred_element_type=jnp.float32)
        + bias_two
    )
    return (blocked, pre_one, act_one, pre_two)


def adamw(master, first_mom, second_mom, gradient, step_rate):
    first_next = beta_one * first_mom + (1.0 - beta_one) * gradient
    second_next = beta_two * second_mom + (1.0 - beta_two) * gradient * gradient
    fix_one = 1.0 - beta_one**STEP
    fix_two = 1.0 - beta_two**STEP
    direction = first_next / fix_one / (jnp.sqrt(second_next / fix_two) + adam_eps)
    master_next = master - step_rate * (direction + decay_rate * master)
    return (master_next, first_next, second_next, master_next.astype(jnp.bfloat16))


def per_device_modes(
    fields,
    cotangent,
    valid_mask,
    kept_modes,
    mlp_master,
    mlp_first,
    mlp_second,
    filter_master,
    filter_first,
    filter_second,
    small_master,
    small_first,
    small_second,
    run_stats,
):
    group_size = lax.axis_size("sp")
    snap_local, row_local, lon_total, channel = fields.shape
    lat_total = row_local * group_size
    mode_local = kept_modes.shape[1]
    mode_total = mode_local * group_size
    block_width = channel // BLOCKS
    lon_fwd, lon_inv = lon_tables(lon_total, mode_total)
    lat_fwd = lat_table(lat_total)
    mlp_w, filt_w, small_w = (
        lax.all_gather(mlp_master.astype(jnp.bfloat16), "sp", axis=1, tiled=True),
        lax.all_gather(filter_master.astype(jnp.bfloat16), "sp", axis=1, tiled=True),
        lax.all_gather(small_master.astype(jnp.bfloat16), "sp", axis=1, tiled=True),
    )
    small_f = small_w.astype(jnp.float32)
    weights = filt_w.reshape(4, BLOCKS, block_width, block_width)
    first_pair = complex_pair(weights[0], weights[1])
    second_pair = complex_pair(weights[2], weights[3])
    bias_one = small_f[4:6].reshape(2, 1, BLOCKS, block_width)
    bias_two = small_f[6:8].reshape(2, 1, BLOCKS, block_width)
    fields_float = fields.astype(jnp.float32)
    normed, norm_pull = jax.vjp(layer_norm, fields_float, small_f[0], small_f[1])
    normed_low = normed.astype(jnp.bfloat16)
    spec_lon = jnp.einsum(
        "nrld,lqm->nrqmd", normed_low, lon_fwd, preferred_element_type=jnp.float32
    ).astype(jnp.bfloat16)
    arrived = lax.all_to_all(spec_lon, "sp", split_axis=3, concat_axis=1, tiled=True)
    spectral = spectral_front(arrived, lat_fwd, first_pair, second_pair, bias_one, bias_two)
    keep_mask = kept_modes.astype(jnp.float32)[None, :, None, :, None, None]
    masked = (shrink(spectral[3]) * keep_mask).astype(jnp.bfloat16)
    masked = masked.reshape(snap_local, lat_total, 2, mode_local, channel)
    returned = jnp.einsum(
        "pkqr,nkpmd->nrqmd", lat_fwd, masked, preferred_element_type=jnp.float32
    ).astype(jnp.bfloat16)
    home_modes = lax.all_to_all(returned, "sp", split_axis=1, concat_axis=3, tiled=True)
    filtered = jnp.einsum(
        "nrqmd,qml->nrld", home_modes, lon_inv, preferred_element_type=jnp.float32
    )
    mixture = fields_float + normed + filtered
    normed_two, norm_two_pull = jax.vjp(layer_norm, mixture, small_f[2], small_f[3])
    normed_two_low = normed_two.astype(jnp.bfloat16)
    tokens = snap_local * row_local * lon_total
    passed = mlp_pass(
        normed_two_low.reshape(tokens, channel),
        cotangent.reshape(tokens, channel),
        mlp_w,
        small_f[9:].reshape(1, -1),
    )
    output = mixture + passed[0].reshape(mixture.shape) + small_f[8]
    weight_mask = valid_mask.astype(jnp.float32)[..., None]
    variables = output[..., :NVAR]
    local_sums = jnp.stack(
        [
            jnp.sum(weight_mask * variables, axis=(0, 1, 2)),
            jnp.sum(weight_mask * variables * variables, axis=(0, 1, 2)),
        ]
    )
    total_sums = lax.psum(local_sums, ("snap", "sp"))
    positions = snap_local * lax.axis_size("snap") * lat_total * lon_total
    stats_new = stat_decay * run_stats + (1.0 - stat_decay) * total_sums / positions
    cot_float = cotangent.astype(jnp.float32)
    grad_normed_two = passed[1].reshape(mixture.shape)
    grad_bias_hidden = passed[4]
    grad_mix_norm, grad_gain_two, grad_shift_two = norm_two_pull(grad_normed_two)
    grad_mixture = cot_float + grad_mix_norm
    grad_bias_out = jnp.sum(cot_float, axis=(0, 1, 2))
    grad_filtered = grad_mixture.astype(jnp.bfloat16)
    grad_home = jnp.einsum(
        "nrld,qml->nrqmd", grad_filtered, lon_inv, preferred_element_type=jnp.float32
    ).astype(jnp.bfloat16)
    grad_returned = lax.all_to_all(grad_home, "sp", split_axis=3, concat_axis=1, tiled=True)
    grad_masked = jnp.einsum(
        "pkqr,nrqmd->nkpmd", lat_fwd, grad_returned, preferred_element_type=jnp.float32
    )
    arrived_again = lax.all_to_all(spec_lon, "sp", split_axis=3, concat_axis=1, tiled=True)
    used_front = spectral_front(arrived_again, lat_fwd, first_pair, second_pair, bias_one, bias_two)
    blocked, pre_one, act_one, pre_two = used_front
    grad_two = jax.vjp(shrink, pre_two)[1](grad_masked.reshape(pre_two.shape) * keep_mask)[
        0
    ].astype(jnp.bfloat16)
    grad_bias_two = jnp.sum(grad_two.astype(jnp.float32), axis=(0, 1, 3))
    grad_second = jnp.einsum(
        "nkqmbi,nkpmbo->pqbio", act_one, grad_two, preferred_element_type=jnp.float32
    )
    grad_act = jnp.einsum(
        "nkpmbo,pqbio->nkqmbi", grad_two, second_pair, preferred_element_type=jnp.float32
    )
    grad_one = jax.vjp(jax.nn.gelu, pre_one)[1](grad_act)[0].astype(jnp.bfloat16)
    grad_bias_one = jnp.sum(grad_one.astype(jnp.float32), axis=(0, 1, 3))
    grad_first = jnp.einsum(
        "nkqmbi,nkpmbo->pqbio", blocked, grad_one, preferred_element_type=jnp.float32
    )
    grad_spectrum = jnp.einsum(
        "nkpmbo,pqbio->nkqmbi", grad_one, first_pair, preferred_element_type=jnp.float32
    ).astype(jnp.bfloat16)
    grad_spectrum = grad_spectrum.reshape(snap_local, lat_total, 2, mode_local, channel)
    grad_lon = jnp.einsum(
        "pkqr,nkpmd->nrqmd", lat_fwd, grad_spectrum, preferred_element_type=jnp.float32
    ).astype(jnp.bfloat16)
    grad_rows = lax.all_to_all(grad_lon, "sp", split_axis=1, concat_axis=3, tiled=True)
    grad_normed = grad_mixture + jnp.einsum(
        "nrqmd,lqm->nrld", grad_rows, lon_fwd, preferred_element_type=jnp.float32
    )
    grad_field_norm, grad_gain_one, grad_shift_one = norm_pull(grad_normed)
    input_grad = grad_mixture + grad_field_norm
    grad_filter = jnp.stack(
        [
            grad_first[0, 0] + grad_first[1, 1],
            grad_first[1, 0] - grad_first[0, 1],
            grad_second[0, 0] + grad_second[1, 1],
            grad_second[1, 0] - grad_second[0, 1],
        ]
    ).reshape(4, channel, block_width)
    grad_small = jnp.concatenate(
        [
            jnp.stack([grad_gain_one, grad_shift_one, grad_gain_two, grad_shift_two]),
            grad_bias_one.reshape(2, channel),
            grad_bias_two.reshape(2, channel),
            grad_bias_out[None, :],
            grad_bias_hidden.reshape(-1, channel),
        ],
        axis=0,
    )
    shares = (
        jnp.stack([
            lax.psum_scatter(part, "sp", scatter_dimension=0, tiled=True) for part in passed[2:4]
        ]),
        lax.psum_scatter(grad_filter, "sp", scatter_dimension=1, tiled=True),
        lax.psum_scatter(grad_small, "sp", scatter_dimension=1, tiled=True),
    )
    owned = (
        lax.psum(shares[0].astype(jnp.bfloat16), "snap").astype(jnp.float32),
        lax.psum(shares[1].astype(jnp.bfloat16), "snap").astype(jnp.float32),
        lax.psum(shares[2].astype(jnp.bfloat16), "snap").astype(jnp.float32),
    )
    mlp_new, mlp_first_new, mlp_second_new, mlp_copy = adamw(
        mlp_master, mlp_first, mlp_second, owned[0], rate_mlp
    )
    filter_new, filter_first_new, filter_second_new, filter_copy = adamw(
        filter_master, filter_first, filter_second, owned[1], rate_filter
    )
    small_new, small_first_new, small_second_new, small_copy = adamw(
        small_master, small_first, small_second, owned[2], rate_small
    )
    return (
        output.astype(jnp.bfloat16),
        input_grad,
        mlp_new,
        mlp_first_new,
        mlp_second_new,
        mlp_copy,
        filter_new,
        filter_first_new,
        filter_second_new,
        filter_copy,
        small_new,
        small_first_new,
        small_second_new,
        small_copy,
        stats_new,
    )


def lon_matrix(lon_total, mode_total, slabs):
    places = np.arange(lon_total)
    orders = np.arange(mode_total)
    angles = (places[:, None] * orders[None, :] % lon_total) * (2.0 * math.pi / lon_total)
    doubling = np.where(orders == 0, 1.0, 2.0)
    scaling = 1.0 / math.sqrt(lon_total)
    forward = np.stack([np.cos(angles), -np.sin(angles)], axis=1) * scaling
    inverse = forward * doubling
    each = np.eye(slabs)
    spread = lambda table: np.kron(each, table.reshape(lon_total, -1)).astype(ml_dtypes.bfloat16)
    return spread(forward), spread(inverse)


def lat_matrix(lat_total, mode_total):
    places = np.arange(lat_total)
    angles = (places[:, None] * places[None, :] % lat_total) * (2.0 * math.pi / lat_total)
    cosine, sine = np.cos(angles), np.sin(angles)
    table = np.stack([np.stack([cosine, sine], axis=1), np.stack([-sine, cosine], axis=1)])
    table = np.einsum("pkqr,ab->pakrqb", table / math.sqrt(lat_total), np.eye(mode_total))
    size = 2 * lat_total * mode_total
    return table.reshape(size, size).astype(ml_dtypes.bfloat16)


class Refs:
    pass


def block_body(names, sizes, *refs):
    g = Refs()
    for name, ref in zip(names, refs, strict=True):
        setattr(g, name, ref)
    snaps, group, parts, width = sizes
    levels = group // 2
    slabs, lon_total, channel = g.fields.shape
    tokens = slabs * lon_total
    owned = channel // group
    half = width // 2
    quarter = width // snaps
    tile = divisor(tokens, 16, 480)
    strip = divisor(tokens, 16, 240)
    low = jnp.bfloat16
    f32 = jnp.float32

    me_snap = lax.axis_index("snap")
    me_sp = lax.axis_index("sp")
    core = lax.rem(me_sp, 2)
    level = me_sp // 2

    def at(snap, sp):
        return {"snap": snap, "sp": sp}

    def sp_after(step):
        return lax.rem(me_sp + step, group)

    def sp_before(step):
        return lax.rem(me_sp + group - step, group)

    def snap_after(step):
        return lax.rem(me_snap + step, snaps)

    def snap_before(step):
        return lax.rem(me_snap + snaps - step, snaps)

    def level_after(step):
        return lax.rem(level + step, levels)

    def level_before(step):
        return lax.rem(level + levels - step, levels)

    other_core = at(me_snap, me_sp + 1 - 2 * core)

    def send(src, dst, sems, index, target):
        return pltpu.make_async_remote_copy(
            src_ref=src,
            dst_ref=dst,
            send_sem=sems[0].at[index],
            recv_sem=sems[1].at[index],
            device_id=target,
            device_id_type=pl.DeviceIdType.MESH,
        )

    def strips(body):
        @pl.loop(0, tokens // strip)
        def _(step):
            body(pl.ds(pl.multiple_of(step * strip, strip), strip))

    loads = {}

    def load(name, index):
        copy = pltpu.make_async_copy(getattr(g, name), getattr(g, name + "_in"), g.load_sem.at[index])
        copy.start()
        loads[name] = copy

    for index, name in enumerate(
        ["small", "kept", "fields", "filt", "cot", "valid", "lon_f", "lat_f", "lat_b", "lon_i", "lon_ft", "lon_it"]
    ):
        load(name, index)

    def master_load(part):
        return pltpu.make_async_copy(
            g.mlp.at[:, :, part * width : (part + 1) * width],
            g.mlp_part.at[part % 2],
            g.load_sem.at[len(loads) + part % 2],
        )

    master_load(0).start()
    master_load(1).start()

    barrier = pltpu.get_barrier_semaphore()
    peers = [at(me_snap, sp_after(step)) for step in range(1, group)]
    peers += [at(snap_after(step), me_sp) for step in range(1, snaps)]
    for peer in peers:
        pl.semaphore_signal(
            barrier, inc=1, device_id=peer, device_id_type=pl.DeviceIdType.MESH
        )

    loads["small"].wait()
    loads["kept"].wait()
    g.own_small[...] = jnp.zeros_like(g.own_small)
    rows_small = g.small.shape[0]
    g.own_small[0:rows_small, 0:owned] = g.small_in[...].astype(low).astype(f32)
    g.own_small[16:, :] = jnp.broadcast_to(
        g.kept_in[...].astype(f32), (g.kept.shape[0], g.own_small.shape[1])
    )
    pl.semaphore_wait(barrier, len(peers))

    def small_copy(step):
        return send(
            g.own_small, g.all_small.at[me_sp], (g.small_s, g.small_r), step, at(me_snap, sp_after(step))
        )

    for step in range(1, group):
        small_copy(step).start()
    g.all_small[me_sp] = g.own_small[...]

    def line_bit(part):
        which = 1 + part % 2
        return which, lax.rem(me_snap // which, 2)

    def half_cols(bit):
        return pl.ds(pl.multiple_of(bit * half, half), half)

    def own_rows(sp):
        return pl.ds(pl.multiple_of(sp * owned, owned), owned)

    def first_copy(part, step):
        target = sp_after(step)
        matrix = lax.rem(target, 2)
        cols = half_cols(line_bit(part)[1])
        return send(
            g.own_w.at[part, matrix, :, cols],
            g.all_w.at[part, matrix, own_rows(me_sp), cols],
            (g.first_s, g.first_r),
            (part, step),
            at(me_snap, target),
        )

    def first_local(part):
        cols = half_cols(line_bit(part)[1])
        return pltpu.make_async_copy(
            g.own_w.at[part, core, :, cols],
            g.all_w.at[part, core, own_rows(me_sp), cols],
            g.first_s.at[part, 0],
        )

    def second_copy(part):
        which, bit = line_bit(part)
        view = g.all_w.at[part, core, :, half_cols(bit)]
        target = at(me_snap + which * (1 - 2 * bit), me_sp)
        return send(view, view, (g.second_s, g.second_r), part, target)

    def third_copy(part):
        view = g.all_w.at[part, core]
        return send(view, view, (g.third_s, g.third_r), part, other_core)

    def start_first(part):
        for step in range(1, group):
            first_copy(part, step).start()
        first_local(part).start()

    def pass_second(part):
        for step in range(1, group):
            first_copy(part, step).wait_recv()
        first_local(part).wait()
        second_copy(part).start()

    def pass_third(part):
        second_copy(part).wait_recv()
        third_copy(part).start()

    for part in range(parts):
        master_load(part).wait()
        g.own_w[part] = g.mlp_part[part % 2].astype(low)
        if part + 2 < parts:
            master_load(part + 2).start()
        if part < 2:
            start_first(part)

    loads["fields"].wait()
    for slab in range(slabs):
        g.grid[slab * lon_total : (slab + 1) * lon_total, :] = g.fields_in[slab].astype(f32)
    for step in range(1, group):
        small_copy(step).wait_recv()
    for sp in range(group):
        g.gains[:, sp * owned : (sp + 1) * owned] = g.all_small[sp, 0:16, 0:owned]
        pairs = g.kept.shape[0]
        g.keep[sp * pairs : (sp + 1) * pairs, :] = g.all_small[sp, 16:, :]

    def first_norm(rows):
        values = g.grid[rows, :]
        centred = values - jnp.mean(values, axis=-1, keepdims=True)
        scale = lax.rsqrt(jnp.mean(centred * centred, axis=-1, keepdims=True) + eps_norm)
        centred = centred * scale
        normed = centred * g.gains[0:1, :] + g.gains[1:2, :]
        g.unit_one[rows, :] = centred.astype(low)
        g.scale_one[rows, :] = scale
        g.normed[rows, :] = normed.astype(low)
        g.grid[rows, :] = values + normed

    strips(first_norm)

    def to_blocks(table, which):
        modes = dot_nn(table, g.normed[...])
        for block in range(group):
            cut = modes[:, block * owned : (block + 1) * owned]
            cut = jnp.concatenate(
                [cut, jnp.zeros((cut.shape[0], 128 - owned), f32)], axis=1
            )
            g.modes[block] = cut.astype(low).reshape(g.modes.shape[1:])
        for step in range(1, group):
            block_copy(which, step).start()
        g.arrived[:, mode_rows(me_sp), :] = g.modes[me_sp]

    def mode_rows(sp):
        size = g.modes.shape[2]
        return pl.ds(pl.multiple_of(sp * size, size), size)

    def block_copy(which, step):
        target = sp_after(step)
        return send(
            g.modes.at[target],
            g.arrived.at[:, mode_rows(me_sp), :],
            (g.block_s, g.block_r),
            (which, step),
            at(me_snap, target),
        )

    def row_copy(which, step):
        target = sp_after(step)
        return send(
            g.turned.at[:, mode_rows(target), :],
            g.home.at[me_sp],
            (g.row_s, g.row_r),
            (which, step),
            at(me_snap, target),
        )

    def to_rows(which):
        for step in range(1, group):
            row_copy(which, step).start()
        g.home[me_sp] = g.turned[:, mode_rows(me_sp), :]

    def home_modes(which):
        for step in range(1, group):
            row_copy(which, step).wait_recv()
        for block in range(group):
            g.gathered[:, block * owned : (block + 1) * owned] = (
                g.home[block].reshape(g.gathered.shape[0], 128)[:, 0:owned].astype(f32)
            )
        return g.gathered[...].astype(low)

    loads["lon_f"].wait()
    to_blocks(g.lon_f_in[...], 0)
    for part in range(2, parts):
        start_first(part)

    loads["filt"].wait()
    for weight, first in ((g.weight_one, 0), (g.weight_two, 2)):
        weight[...] = jnp.zeros_like(weight)
        real = g.filt_in[first].astype(low)
        imag = g.filt_in[first + 1].astype(low)
        weight[0:owned, 0:owned] = real
        weight[128 : 128 + owned, 128 : 128 + owned] = real
        weight[0:owned, 128 : 128 + owned] = imag
        weight[128 : 128 + owned, 0:owned] = -imag

    def bias_row(first):
        return jnp.concatenate(
            [g.own_small[first : first + 1, :], g.own_small[first + 1 : first + 2, :]], axis=1
        )

    loads["cot"].wait()
    for slab in range(slabs):
        g.back[slab * lon_total : (slab + 1) * lon_total, :] = g.cot_in[slab].astype(f32)

    def flat_cot(rows):
        g.cot_flat[rows, :] = g.back[rows, :].astype(low)

    strips(flat_cot)

    loads["lat_f"].wait()
    loads["lat_b"].wait()
    for step in range(1, group):
        block_copy(0, step).wait_recv()
    snap_local = g.arrived.shape[0]
    pairs = g.arrived.shape[1] // 2

    def spectra(out, kind):
        for snap in range(snap_local):
            spectrum = dot_nn(g.lat_f_in[...], g.arrived[snap]).astype(kind)
            rows = slice(snap * pairs, (snap + 1) * pairs)
            out[rows, 0:128] = spectrum[0:pairs]
            out[rows, 128:256] = spectrum[pairs:]

    def grids(values):
        for snap in range(snap_local):
            rows = values[snap * pairs : (snap + 1) * pairs]
            rows = jnp.concatenate([rows[:, 0:128], rows[:, 128:256]], axis=0)
            g.turned[snap] = dot_nn(g.lat_b_in[...], rows).astype(low)

    def keep_all():
        keep = jnp.concatenate([g.keep[...], g.keep[...]], axis=1)
        return jnp.concatenate([keep] * snap_local, axis=0)

    spectra(g.spectrum, low)
    g.pre_one[...] = dot_nn(g.spectrum[...], g.weight_one[...]) + bias_row(4)
    g.act_one[...] = gelu_both(g.pre_one[...])[0].astype(low)
    g.pre_two[...] = dot_nn(g.act_one[...], g.weight_two[...]) + bias_row(6)
    grids((shrink(g.pre_two[...]) * keep_all()).astype(low))
    to_rows(0)

    pass_second(0)
    pass_second(1)
    g.cot_turned[...] = g.cot_flat[...].T
    pass_third(0)

    loads["lon_i"].wait()
    g.home_low[...] = home_modes(0)

    def add_filtered(rows):
        g.grid[rows, :] += dot_nn(g.lon_i_in[rows, :], g.home_low[...])

    def second_norm(rows):
        values = g.grid[rows, :]
        centred = values - jnp.mean(values, axis=-1, keepdims=True)
        scale = lax.rsqrt(jnp.mean(centred * centred, axis=-1, keepdims=True) + eps_norm)
        centred = centred * scale
        g.unit_two[rows, :] = centred.astype(low)
        g.scale_two[rows, :] = scale
        g.normed[rows, :] = (centred * g.gains[2:3, :] + g.gains[3:4, :]).astype(low)
        g.grid[rows, :] = values + g.gains[8:9, :]
        g.back[rows, :] = jnp.zeros((strip, channel), f32)

    add_filtered(slice(0, tokens))
    strips(second_norm)
    g.normed_turned[...] = g.normed[...].T
    for part in range(parts):
        flat = jnp.concatenate([g.gains[9 + row : 10 + row, :] for row in range(rows_small - 9)], axis=1)
        g.bias[part] = flat[:, part * width : (part + 1) * width]
    pass_third(1)
    for part in range(2, min(4, parts)):
        pass_second(part)

    def core_copy(part, matrix):
        slot = lax.rem(part, 2)
        return send(
            g.grads.at[slot, matrix, :, 1 - core],
            g.core_got.at[slot, matrix],
            (g.core_s, g.core_r),
            (slot, matrix),
            other_core,
        )

    def snap_copy(part, step):
        slot = lax.rem(part, 2)
        target = snap_after(step)
        return send(
            g.snap_out.at[slot, target],
            g.snap_got.at[slot, me_snap],
            (g.snap_s, g.snap_r),
            (slot, step),
            at(target, me_sp),
        )

    def level_copy(part, step):
        slot = lax.rem(part, 2)
        target = level_after(step)
        return send(
            g.level_out.at[slot, target],
            g.level_got.at[slot, level],
            (g.level_s, g.level_r),
            (slot, step),
            at(me_snap, 2 * target + core),
        )

    def last_copy(part, step):
        view = g.total.at[part, me_snap]
        return send(view, view, (g.last_s, g.last_r), (part, step), at(snap_after(step), me_sp))

    def snap_stage(part):
        slot = lax.rem(part, 2)

        @pl.when(part >= 2)
        def _():
            for step in range(1, snaps):
                snap_copy(part - 2, step).wait_send()

        for matrix in range(2):
            core_copy(part, matrix).wait_recv()
            for row in range(levels):
                both = g.grads[slot, matrix, row, core].astype(f32) + g.core_got[
                    slot, matrix, row
                ].astype(f32)
                both = both.astype(low)
                for snap in range(snaps):
                    g.snap_out[slot, snap, matrix, row] = both[:, snap * quarter : (snap + 1) * quarter]
        for step in range(1, snaps):
            snap_copy(part, step).start()

    def level_stage(part):
        slot = lax.rem(part, 2)

        @pl.when(part >= 2)
        def _():
            for step in range(1, levels):
                level_copy(part - 2, step).wait_send()

        for step in range(1, snaps):
            snap_copy(part, step).wait_recv()
        for matrix in range(2):
            for row in range(levels):
                sums = g.snap_out[slot, me_snap, matrix, row].astype(f32)
                for step in range(1, snaps):
                    sums += g.snap_got[slot, snap_before(step), matrix, row].astype(f32)
                g.level_out[slot, row, matrix] = sums.astype(low)
        for step in range(1, levels):
            level_copy(part, step).start()

    def last_stage(part):
        slot = lax.rem(part, 2)
        for step in range(1, levels):
            level_copy(part, step).wait_recv()
        sums = g.level_out[slot, level].astype(f32)
        for step in range(1, levels):
            sums += g.level_got[slot, level_before(step)].astype(f32)
        g.total[part, me_snap] = sums.astype(low)
        for step in range(1, snaps):
            last_copy(part, step).start()

    @pl.loop(0, parts)
    def _(part):
        slot = lax.rem(part, 2)
        third_copy(part).wait_recv()
        g.grad_bias[part] = jnp.zeros(g.grad_bias.shape[1:], f32)

        @pl.loop(0, tokens // tile)
        def _(step):
            rows = pl.ds(pl.multiple_of(step * tile, tile), tile)
            act, slope = gelu_both(dot_nn(g.normed[rows, :], g.all_w[part, 0]) + g.bias[part])
            act = act.astype(low)
            slope = (dot_nn(g.cot_flat[rows, :], g.all_w[part, 1]) * slope).astype(low)
            g.act[rows, :] = act
            g.slope[rows, :] = slope
            g.grad_bias[part] += jnp.sum(slope.astype(f32), axis=0, keepdims=True)
            g.grid[rows, :] += dot_nt(act, g.all_w[part, 1])
            g.back[rows, :] += dot_nt(slope, g.all_w[part, 0])

        @pl.when(part + 2 < parts)
        def _():
            pass_third(part + 2)

        @pl.when(part + 4 < parts)
        def _():
            pass_second(part + 4)

        @pl.when(part >= 3)
        def _():
            last_stage(part - 3)

        @pl.when(part >= 2)
        def _():
            level_stage(part - 2)

        @pl.when(part >= 1)
        def _():
            snap_stage(part - 1)

        @pl.when(part >= 2)
        def _():
            for matrix in range(2):
                core_copy(part - 2, matrix).wait_send()

        shape = g.grads.shape[2:]
        g.grads[slot, 0] = dot_nn(g.normed_turned[...], g.slope[...]).astype(low).reshape(shape)
        core_copy(part, 0).start()
        g.grads[slot, 1] = dot_nn(g.cot_turned[...], g.act[...]).astype(low).reshape(shape)
        core_copy(part, 1).start()

    for slab in range(slabs):
        g.fields_in[slab] = g.grid[slab * lon_total : (slab + 1) * lon_total, :].astype(low)
    out_copy = pltpu.make_async_copy(g.fields_in, g.out, g.load_sem.at[0])
    out_copy.start()
    loads["valid"].wait()
    g.weigh[...] = jnp.zeros_like(g.weigh)
    for slab in range(slabs):
        g.weigh[0:1, slab * lon_total : (slab + 1) * lon_total] = g.valid_in[
            slab : slab + 1, :
        ].astype(f32)
    variables = g.grid[:, 0:128]
    precise = lax.Precision.HIGHEST
    sums = [
        jnp.dot(g.weigh[...], v, precision=precise, preferred_element_type=f32)[0:1]
        for v in (variables, variables * variables)
    ]

    g.grad_rows[...] = jnp.zeros_like(g.grad_rows)

    def second_back(rows):
        grad = g.back[rows, :]
        unit = g.unit_two[rows, :].astype(f32)
        cot = g.cot_flat[rows, :].astype(f32)
        pulled = grad * g.gains[2:3, :]
        middle = jnp.mean(pulled, axis=-1, keepdims=True)
        slant = jnp.mean(pulled * unit, axis=-1, keepdims=True)
        total = cot + g.scale_two[rows, :] * (pulled - middle - unit * slant)
        g.back[rows, :] = total
        g.normed[rows, :] = total.astype(low)
        g.grad_rows[2:3, :] += jnp.sum(grad * unit, axis=0, keepdims=True)
        g.grad_rows[3:4, :] += jnp.sum(grad, axis=0, keepdims=True)
        g.grad_rows[8:9, :] += jnp.sum(cot, axis=0, keepdims=True)

    strips(second_back)
    loads["lon_it"].wait()
    for step in range(1, group):
        block_copy(0, step).wait_send()
    to_blocks(g.lon_it_in[...], 1)

    last_stage(parts - 3)
    level_stage(parts - 2)
    snap_stage(parts - 1)

    for step in range(1, group):
        block_copy(1, step).wait_recv()
    spectra(g.grad_two, f32)
    bend = jnp.tanh(g.pre_two[...] / shrink_level)
    grad_two = (g.grad_two[...] * keep_all() * (bend * bend)).astype(low)

    def dot_tn(left, right):
        return lax.dot_general(
            left, right, (((0,), (0,)), ((), ())), preferred_element_type=f32
        )

    def filter_rows(first, grad):
        g.pair_grad[...] = grad
        real = g.pair_grad[0:128, 0:128] + g.pair_grad[128:256, 128:256]
        imag = g.pair_grad[0:128, 128:256] - g.pair_grad[128:256, 0:128]
        g.filt_out[me_snap, first] = real[0:owned].astype(low)
        g.filt_out[me_snap, first + 1] = imag[0:owned].astype(low)

    bias_two = jnp.sum(grad_two.astype(f32), axis=0, keepdims=True)
    filter_rows(2, dot_tn(g.act_one[...], grad_two))
    grad_one = dot_nt(grad_two, g.weight_two[...])
    grad_one = (grad_one * gelu_both(g.pre_one[...])[1]).astype(low)
    bias_one = jnp.sum(grad_one.astype(f32), axis=0, keepdims=True)
    for step in range(1, group):
        row_copy(0, step).wait_send()
    grids(dot_nt(grad_one, g.weight_one[...]).astype(low))
    to_rows(1)
    filter_rows(0, dot_tn(g.spectrum[...], grad_one))

    def filter_copy(step):
        view = g.filt_out.at[me_snap]
        return send(view, view, (g.filt_s, g.filt_r), step, at(snap_after(step), me_sp))

    for step in range(1, snaps):
        filter_copy(step).start()

    last_stage(parts - 2)
    level_stage(parts - 1)

    loads["lon_ft"].wait()
    g.home_low[...] = home_modes(1)

    def add_modes(rows):
        g.grid[rows, :] = g.back[rows, :] + dot_nn(g.lon_ft_in[rows, :], g.home_low[...])

    def first_back(rows):
        grad = g.grid[rows, :]
        unit = g.unit_one[rows, :].astype(f32)
        pulled = grad * g.gains[0:1, :]
        middle = jnp.mean(pulled, axis=-1, keepdims=True)
        slant = jnp.mean(pulled * unit, axis=-1, keepdims=True)
        g.grid[rows, :] = g.back[rows, :] + g.scale_one[rows, :] * (
            pulled - middle - unit * slant
        )
        g.grad_rows[0:1, :] += jnp.sum(grad * unit, axis=0, keepdims=True)
        g.grad_rows[1:2, :] += jnp.sum(grad, axis=0, keepdims=True)

    add_modes(slice(0, tokens))
    strips(first_back)

    flat = jnp.concatenate([g.grad_bias[part] for part in range(parts)], axis=1)
    for row in range(rows_small - 9):
        g.grad_rows[9 + row : 10 + row, :] = flat[:, row * channel : (row + 1) * channel]
    for block in range(group):
        g.tiles[block] = jnp.zeros(g.tiles.shape[1:], f32)
        g.tiles[block, :, 0:owned] = g.grad_rows[:, block * owned : (block + 1) * owned]
        g.tiles[block, 13:14, :] = sums[0]
        g.tiles[block, 14:15, :] = sums[1]

    def tile_copy(step):
        target = sp_after(step)
        return send(
            g.tiles.at[target], g.tiles_got.at[me_sp], (g.tile_s, g.tile_r), step, at(me_snap, target)
        )

    def snap_tile_copy(step):
        view = g.snap_tiles.at[me_snap]
        return send(view, view, (g.snap_tile_s, g.snap_tile_r), step, at(snap_after(step), me_sp))

    for step in range(1, group):
        tile_copy(step).start()
    last_stage(parts - 1)

    stage = g.stage
    grad_copies = []
    for slab in range(slabs):
        if slab >= 2:
            grad_copies[slab - 2].wait()
        stage[slab % 2] = g.grid[slab * lon_total : (slab + 1) * lon_total, :]
        copy = pltpu.make_async_copy(stage.at[slab % 2], g.in_grad.at[slab], g.load_sem.at[1 + slab % 2])
        copy.start()
        grad_copies.append(copy)

    g.tiles_got[me_sp] = g.tiles[me_sp]
    for step in range(1, group):
        tile_copy(step).wait_recv()
    tile_sum = g.tiles_got[0]
    for sp in range(1, group):
        tile_sum += g.tiles_got[sp]
    g.snap_tiles[me_snap] = tile_sum
    g.snap_tiles[me_snap, 4:5, :] = bias_one[:, 0:128]
    g.snap_tiles[me_snap, 5:6, :] = bias_one[:, 128:256]
    g.snap_tiles[me_snap, 6:7, :] = bias_two[:, 0:128]
    g.snap_tiles[me_snap, 7:8, :] = bias_two[:, 128:256]
    for step in range(1, snaps):
        snap_tile_copy(step).start()

    for step in range(1, snaps):
        filter_copy(step).wait_recv()
    filter_sum = g.filt_out[0].astype(f32)
    for snap in range(1, snaps):
        filter_sum += g.filt_out[snap].astype(f32)
    g.grad_filt[...] = filter_sum
    for part in range(parts):
        for step in range(1, snaps):
            last_copy(part, step).wait_recv()
    grads_out = pltpu.make_async_copy(g.total, g.grad_mlp, g.load_sem.at[3])
    grads_out.start()
    for step in range(1, snaps):
        snap_tile_copy(step).wait_recv()
    tile_sum = g.snap_tiles[0]
    for snap in range(1, snaps):
        tile_sum += g.snap_tiles[snap]
    g.grad_small[...] = tile_sum

    out_copy.wait()
    grads_out.wait()
    for copy in grad_copies[-2:]:
        copy.wait()
    for step in range(1, group):
        small_copy(step).wait_send()
        block_copy(1, step).wait_send()
        row_copy(1, step).wait_send()
        tile_copy(step).wait_send()
        for part in range(parts):
            first_copy(part, step).wait_send()
    for part in range(parts):
        second_copy(part).wait_send()
        third_copy(part).wait_send()
    for part in (parts - 2, parts - 1):
        for matrix in range(2):
            core_copy(part, matrix).wait_send()
        for step in range(1, snaps):
            snap_copy(part, step).wait_send()
        for step in range(1, levels):
            level_copy(part, step).wait_send()
    for step in range(1, snaps):
        filter_copy(step).wait_send()
        snap_tile_copy(step).wait_send()
        for part in range(parts):
            last_copy(part, step).wait_send()


def block_pass(fields, cot, valid, kept, mlp, filt, small, snaps, group):
    snap_local, row_local, lon_total, channel = fields.shape
    slabs = snap_local * row_local
    tokens = slabs * lon_total
    hidden = mlp.shape[2]
    lat_total = row_local * group
    modes = kept.shape[1] * group
    owned = channel // group
    width = 512
    parts = hidden // width
    levels = group // 2
    quarter = width // snaps
    low, f32 = jnp.bfloat16, jnp.float32
    lon_f, lon_i = lon_matrix(lon_total, modes, slabs)
    lat_f = lat_matrix(lat_total, modes)
    pair = 2 * modes * row_local
    spread = slabs * 2 * modes
    inputs = dict(
        fields=fields.reshape(slabs, lon_total, channel),
        cot=cot.reshape(slabs, lon_total, channel),
        valid=valid.reshape(slabs, lon_total),
        kept=kept,
        mlp=mlp,
        filt=filt,
        small=small,
        lon_f=jnp.asarray(np.ascontiguousarray(lon_f.T)),
        lon_i=jnp.asarray(lon_i),
        lon_ft=jnp.asarray(lon_f),
        lon_it=jnp.asarray(np.ascontiguousarray(lon_i.T)),
        lat_f=jnp.asarray(lat_f),
        lat_b=jnp.asarray(np.ascontiguousarray(lat_f.T)),
    )
    outputs = dict(
        out=jax.ShapeDtypeStruct((slabs, lon_total, channel), low),
        in_grad=jax.ShapeDtypeStruct((slabs, lon_total, channel), f32),
        grad_mlp=jax.ShapeDtypeStruct((parts, snaps, 2, owned, quarter), low),
        grad_filt=jax.ShapeDtypeStruct((4, owned, 128), f32),
        grad_small=jax.ShapeDtypeStruct((16, 128), f32),
    )
    vmem = pltpu.VMEM
    dma = pltpu.SemaphoreType.DMA
    scratch = {
        name + "_in": vmem(value.shape, value.dtype)
        for name, value in inputs.items()
        if name != "mlp"
    }
    scratch |= dict(
        mlp_part=vmem((2, 2, owned, width), f32),
        grid=vmem((tokens, channel), f32),
        back=vmem((tokens, channel), f32),
        normed=vmem((tokens, channel), low),
        normed_turned=vmem((channel, tokens), low),
        cot_flat=vmem((tokens, channel), low),
        cot_turned=vmem((channel, tokens), low),
        unit_one=vmem((tokens, channel), low),
        unit_two=vmem((tokens, channel), low),
        scale_one=vmem((tokens, 1), f32),
        scale_two=vmem((tokens, 1), f32),
        own_small=vmem((16 + kept.shape[0], 128), f32),
        all_small=vmem((group, 16 + kept.shape[0], 128), f32),
        gains=vmem((16, channel), f32),
        keep=vmem((lat_total * modes, 128), f32),
        own_w=vmem((parts, 2, owned, width), low),
        all_w=vmem((parts, 2, channel, width), low),
        modes=vmem((group, snap_local, pair, 128), low),
        arrived=vmem((snap_local, pair * group, 128), low),
        turned=vmem((snap_local, pair * group, 128), low),
        home=vmem((group, snap_local, pair, 128), low),
        gathered=vmem((spread, channel), f32),
        home_low=vmem((spread, channel), low),
        weight_one=vmem((256, 256), low),
        weight_two=vmem((256, 256), low),
        spectrum=vmem((snap_local * lat_total * modes, 256), low),
        pre_one=vmem((snap_local * lat_total * modes, 256), f32),
        act_one=vmem((snap_local * lat_total * modes, 256), low),
        pre_two=vmem((snap_local * lat_total * modes, 256), f32),
        grad_two=vmem((snap_local * lat_total * modes, 256), f32),
        pair_grad=vmem((256, 256), f32),
        act=vmem((tokens, width), low),
        slope=vmem((tokens, width), low),
        bias=vmem((parts, 1, width), f32),
        grad_bias=vmem((parts, 1, width), f32),
        grad_rows=vmem((16, channel), f32),
        weigh=vmem((8, tokens), f32),
        stage=vmem((2, lon_total, channel), f32),
        grads=vmem((2, 2, levels, 2, owned, width), low),
        core_got=vmem((2, 2, levels, owned, width), low),
        snap_out=vmem((2, snaps, 2, levels, owned, quarter), low),
        snap_got=vmem((2, snaps, 2, levels, owned, quarter), low),
        level_out=vmem((2, levels, 2, owned, quarter), low),
        level_got=vmem((2, levels, 2, owned, quarter), low),
        total=vmem((parts, snaps, 2, owned, quarter), low),
        filt_out=vmem((snaps, 4, owned, 128), low),
        tiles=vmem((group, 16, 128), f32),
        tiles_got=vmem((group, 16, 128), f32),
        snap_tiles=vmem((snaps, 16, 128), f32),
        load_sem=dma((len(inputs) + 1,)),
    )
    for name, shape in dict(
        small=(group,),
        first=(parts, group),
        second=(parts,),
        third=(parts,),
        block=(2, group),
        row=(2, group),
        core=(2, 2),
        snap=(2, snaps),
        level=(2, levels),
        last=(parts, snaps),
        filt=(snaps,),
        tile=(group,),
        snap_tile=(snaps,),
    ).items():
        scratch[name + "_s"] = dma(shape)
        scratch[name + "_r"] = dma(shape)
    names = [*inputs, *outputs, *scratch]
    far = pl.BlockSpec(memory_space=pl.ANY)
    near = pl.BlockSpec(memory_space=pltpu.VMEM)
    results = pl.pallas_call(
        functools.partial(block_body, names, (snaps, group, parts, width)),
        in_specs=[far] * len(inputs),
        out_specs=[far, far, far, near, near],
        out_shape=list(outputs.values()),
        scratch_shapes=list(scratch.values()),
        compiler_params=pltpu.CompilerParams(
            collective_id=0, has_side_effects=True, vmem_limit_bytes=VMEM_LIMIT
        ),
        cost_estimate=pl.CostEstimate(
            flops=12 * tokens * channel * hidden,
            bytes_accessed=4 * hidden * channel,
            transcendentals=tokens * hidden,
        ),
        name="block_pass",
    )(*inputs.values())
    return results


def step_body(rates, *refs):
    (mlp_g, filt_g, small_g, mlp_w, mlp_m, mlp_v, filt_w, filt_m, filt_v, small_w, small_m, small_v, run) = refs[:13]
    (mlp_o, filt_o, small_o, stats_o) = refs[13:17], refs[17:21], refs[21:25], refs[25]
    snaps = mlp_g.shape[1]
    quarter = mlp_g.shape[4]

    def store(outs, where, results):
        for ref, value in zip(outs, results, strict=True):
            ref[where] = value

    for snap in range(snaps):
        cols = (slice(None), slice(None), slice(snap * quarter, (snap + 1) * quarter))
        grad = mlp_g[0, snap].astype(jnp.float32)
        store(mlp_o, cols, adamw(mlp_w[cols], mlp_m[cols], mlp_v[cols], grad, rate_mlp))

    @pl.when(pl.program_id(0) == 0)
    def _():
        owned = filt_w.shape[2]
        store(
            filt_o,
            ...,
            adamw(filt_w[...], filt_m[...], filt_v[...], filt_g[:, :, 0:owned], rate_filter),
        )
        rows = small_w.shape[0]
        store(
            small_o,
            ...,
            adamw(small_w[...], small_m[...], small_v[...], small_g[0:rows, 0:owned], rate_small),
        )
        count = run.shape[1]
        totals = small_g[rows : rows + 2, 0:count]
        stats_o[...] = stat_decay * run[...] + (1.0 - stat_decay) * totals / rates


def step_pass(grads, masters, run_stats, positions):
    grad_mlp, grad_filt, grad_small = grads
    mlp, filt, small = masters
    parts = grad_mlp.shape[0]
    width = mlp[0].shape[2] // parts
    f32, low = jnp.float32, jnp.bfloat16

    def whole(shape):
        return pl.BlockSpec(shape, lambda j: (0,) * len(shape))

    block = pl.BlockSpec((*mlp[0].shape[:2], width), lambda j: (0, 0, j))
    filt_block, small_block = whole(filt[0].shape), whole(small[0].shape)

    def four(array):
        return [jax.ShapeDtypeStruct(array.shape, kind) for kind in (f32, f32, f32, low)]

    return pl.pallas_call(
        functools.partial(step_body, positions),
        grid=(parts,),
        in_specs=[
            pl.BlockSpec((1, *grad_mlp.shape[1:]), lambda j: (j, 0, 0, 0, 0)),
            whole(grad_filt.shape),
            whole(grad_small.shape),
            *[block] * 3,
            *[filt_block] * 3,
            *[small_block] * 3,
            whole(run_stats.shape),
        ],
        out_specs=[*[block] * 4, *[filt_block] * 4, *[small_block] * 4, whole(run_stats.shape)],
        out_shape=[
            *four(mlp[0]),
            *four(filt[0]),
            *four(small[0]),
            jax.ShapeDtypeStruct(run_stats.shape, f32),
        ],
        compiler_params=pltpu.CompilerParams(vmem_limit_bytes=40 * 1024 * 1024),
        name="step_pass",
    )(grad_mlp, grad_filt, grad_small, *mlp, *filt, *small, run_stats)


def per_device_blocks(
    fields,
    cotangent,
    valid_mask,
    kept_modes,
    mlp_master,
    mlp_first,
    mlp_second,
    filter_master,
    filter_first,
    filter_second,
    small_master,
    small_first,
    small_second,
    run_stats,
):
    snaps, group = lax.axis_size("snap"), lax.axis_size("sp")
    out, in_grad, *grads = block_pass(
        fields, cotangent, valid_mask, kept_modes, mlp_master, filter_master, small_master, snaps, group
    )
    positions = fields.shape[0] * snaps * fields.shape[1] * group * fields.shape[2]
    stepped = step_pass(
        grads,
        (
            (mlp_master, mlp_first, mlp_second),
            (filter_master, filter_first, filter_second),
            (small_master, small_first, small_second),
        ),
        run_stats,
        positions,
    )
    return (out.reshape(fields.shape), in_grad.reshape(fields.shape), *stepped)


def per_device(*arrays):
    group, snaps = lax.axis_size("sp"), lax.axis_size("snap")
    channel, hidden = arrays[0].shape[3], arrays[4].shape[2]
    by_block = group == BLOCKS and snaps == 4 and arrays[3].shape[1] == 1
    if by_block and hidden % 512 == 0 and channel // group <= 128 and channel % (16 * group) == 0:
        return per_device_blocks(*arrays)
    return per_device_modes(*arrays)


def solution(mesh):
    return jax.shard_map(
        per_device,
        mesh=mesh,
        in_specs=(
            P("snap", "sp", None, None),
            P("snap", "sp", None, None),
            P("snap", "sp", None),
            P(None, "sp"),
            P(None, "sp", None),
            P(None, "sp", None),
            P(None, "sp", None),
            P(None, "sp", None),
            P(None, "sp", None),
            P(None, "sp", None),
            P(None, "sp"),
            P(None, "sp"),
            P(None, "sp"),
            P(),
        ),
        out_specs=(
            P("snap", "sp", None, None),
            P("snap", "sp", None, None),
            P(None, "sp", None),
            P(None, "sp", None),
            P(None, "sp", None),
            P(None, "sp", None),
            P(None, "sp", None),
            P(None, "sp", None),
            P(None, "sp", None),
            P(None, "sp", None),
            P(None, "sp"),
            P(None, "sp"),
            P(None, "sp"),
            P(None, "sp"),
            P(),
        ),
        check_vma=False,
    )
```

```python
import functools
import math

import jax
import jax.numpy as jnp
import ml_dtypes
import numpy as np
from jax import lax
from jax.experimental import pallas as pl
from jax.experimental.pallas import tpu as pltpu
from jax.sharding import PartitionSpec as P

BLOCKS = 8
NVAR = 20
STEP = 10
VMEM_LIMIT = 63 * 1024 * 1024


eps_norm = 1e-06
shrink_level = 0.01
beta_one = 0.5
beta_two = 0.5
adam_eps = 1e-08
decay_rate = 0.01
rate_mlp = 0.03
rate_filter = 0.1
rate_small = 0.2
stat_decay = 0.5


def layer_norm(values, gain_vec, shift_vec):
    centred = values - jnp.mean(values, axis=-1, keepdims=True)
    spread = jnp.mean(centred * centred, axis=-1, keepdims=True)
    return centred * lax.rsqrt(spread + eps_norm) * gain_vec + shift_vec


def shrink(values):
    return values - shrink_level * jnp.tanh(values / shrink_level)


def lon_tables(lon_total, mode_total):
    places = jnp.arange(lon_total, dtype=jnp.int32)
    orders = jnp.arange(mode_total, dtype=jnp.int32)
    angles = (places[:, None] * orders[None, :] % lon_total).astype(jnp.float32) * (
        2.0 * math.pi / lon_total
    )
    scaling = 1.0 / math.sqrt(lon_total)
    forward_tab = jnp.stack([jnp.cos(angles), -jnp.sin(angles)], axis=1) * scaling
    doubling = jnp.where(orders == 0, 1.0, 2.0).astype(jnp.float32)[:, None]
    inverse_tab = (
        jnp.stack([jnp.cos(angles).T * doubling, -jnp.sin(angles).T * doubling], axis=0) * scaling
    )
    return (forward_tab.astype(jnp.bfloat16), inverse_tab.astype(jnp.bfloat16))


def lat_table(lat_total):
    places = jnp.arange(lat_total, dtype=jnp.int32)
    angles = (places[:, None] * places[None, :] % lat_total).astype(jnp.float32) * (
        2.0 * math.pi / lat_total
    )
    cosine = jnp.cos(angles)
    sine_part = jnp.sin(angles)
    upper_rows = jnp.stack([cosine, sine_part], axis=1)
    bottom = jnp.stack([-sine_part, cosine], axis=1)
    return (jnp.stack([upper_rows, bottom], axis=0) / math.sqrt(lat_total)).astype(jnp.bfloat16)


def complex_pair(real_part, imag_part):
    return jnp.stack([jnp.stack([real_part, -imag_part]), jnp.stack([imag_part, real_part])])


gelu_scale = math.sqrt(2.0 / math.pi)
gelu_cubic = 0.044715


def gelu_both(value):
    square = value * value
    bent = jnp.tanh(gelu_scale * value * (1.0 + gelu_cubic * square))
    half = 0.5 + 0.5 * bent
    slope = half + (0.5 * gelu_scale) * value * (1.0 - bent * bent) * (
        1.0 + (3.0 * gelu_cubic) * square
    )
    return value * half, slope


def dot_nt(left, right):
    return lax.dot_general(
        left, right, (((1,), (1,)), ((), ())), preferred_element_type=jnp.float32
    )


def dot_nn(left, right):
    return jnp.dot(left, right, preferred_element_type=jnp.float32)


def divisor(total, unit, most):
    return max(size for size in range(unit, most + 1, unit) if total % size == 0)


def mlp_body(
    tile,
    normed_ref,
    cot_ref,
    up_ref,
    down_ref,
    bias_ref,
    out_ref,
    back_ref,
    grad_up_ref,
    grad_down_ref,
    grad_bias_ref,
    normed_turned,
    cot_turned,
    act_ref,
    slope_ref,
):
    tokens = normed_ref.shape[0]

    @pl.when(pl.program_id(0) == 0)
    def _():
        normed_turned[...] = normed_ref[...].T
        cot_turned[...] = cot_ref[...].T
        out_ref[...] = jnp.zeros_like(out_ref)
        back_ref[...] = jnp.zeros_like(back_ref)

    grad_bias_ref[...] = jnp.zeros_like(grad_bias_ref)

    @pl.loop(0, tokens // tile)
    def _(step):
        rows = pl.ds(pl.multiple_of(step * tile, tile), tile)
        act, slope = gelu_both(dot_nn(normed_ref[rows, :], up_ref[...]) + bias_ref[...])
        act = act.astype(jnp.bfloat16)
        slope = (dot_nn(cot_ref[rows, :], down_ref[...]) * slope).astype(jnp.bfloat16)
        act_ref[rows, :] = act
        slope_ref[rows, :] = slope
        grad_bias_ref[...] += jnp.sum(slope.astype(jnp.float32), axis=0, keepdims=True)
        out_ref[rows, :] += dot_nt(act, down_ref[...])
        back_ref[rows, :] += dot_nt(slope, up_ref[...])

    grad_up_ref[...] = dot_nn(normed_turned[...], slope_ref[...]).astype(grad_up_ref.dtype)
    grad_down_ref[...] = dot_nn(cot_turned[...], act_ref[...]).astype(grad_down_ref.dtype)


def mlp_pass(normed, cot, weights, bias):
    tokens, channel = normed.shape
    hidden = weights.shape[2]
    width = divisor(hidden, 128, 512)
    tile = divisor(tokens, 16, 480)
    whole = pl.BlockSpec((tokens, channel), lambda j: (0, 0))
    block = pl.BlockSpec((channel, width), lambda j: (0, j))
    line = pl.BlockSpec((1, width), lambda j: (0, j))
    part = lambda which: pl.BlockSpec((None, channel, width), lambda j: (which, 0, j))
    total = jax.ShapeDtypeStruct((tokens, channel), jnp.float32)
    grads = jax.ShapeDtypeStruct((channel, hidden), jnp.bfloat16)
    return pl.pallas_call(
        functools.partial(mlp_body, tile),
        grid=(hidden // width,),
        in_specs=[whole, whole, part(0), part(1), line],
        out_specs=[whole, whole, block, block, line],
        out_shape=[total, total, grads, grads, jax.ShapeDtypeStruct((1, hidden), jnp.float32)],
        scratch_shapes=[
            pltpu.VMEM((channel, tokens), jnp.bfloat16),
            pltpu.VMEM((channel, tokens), jnp.bfloat16),
            pltpu.VMEM((tokens, width), jnp.bfloat16),
            pltpu.VMEM((tokens, width), jnp.bfloat16),
        ],
        compiler_params=pltpu.CompilerParams(vmem_limit_bytes=56 * 1024 * 1024),
        cost_estimate=pl.CostEstimate(
            flops=12 * tokens * channel * hidden,
            bytes_accessed=8 * channel * hidden + 12 * tokens * channel,
            transcendentals=tokens * hidden,
        ),
        name="mlp_pass",
    )(normed, cot, weights, weights, bias)


def spectral_front(arrived, lat_fwd, first_pair, second_pair, bias_one, bias_two):
    spectrum = jnp.einsum(
        "pkqr,nrqmd->nkpmd", lat_fwd, arrived, preferred_element_type=jnp.float32
    ).astype(jnp.bfloat16)
    snap_local, lat_total, pair_count, mode_local, channel = spectrum.shape
    blocked = spectrum.reshape(
        snap_local, lat_total, pair_count, mode_local, BLOCKS, channel // BLOCKS
    )
    pre_one = (
        jnp.einsum("nkqmbi,pqbio->nkpmbo", blocked, first_pair, preferred_element_type=jnp.float32)
        + bias_one
    )
    act_one = jax.nn.gelu(pre_one).astype(jnp.bfloat16)
    pre_two = (
        jnp.einsum("nkqmbi,pqbio->nkpmbo", act_one, second_pair, preferred_element_type=jnp.float32)
        + bias_two
    )
    return (blocked, pre_one, act_one, pre_two)


def adamw(master, first_mom, second_mom, gradient, step_rate):
    first_next = beta_one * first_mom + (1.0 - beta_one) * gradient
    second_next = beta_two * second_mom + (1.0 - beta_two) * gradient * gradient
    fix_one = 1.0 - beta_one**STEP
    fix_two = 1.0 - beta_two**STEP
    direction = first_next / fix_one / (jnp.sqrt(second_next / fix_two) + adam_eps)
    master_next = master - step_rate * (direction + decay_rate * master)
    return (master_next, first_next, second_next, master_next.astype(jnp.bfloat16))


def per_device_modes(
    fields,
    cotangent,
    valid_mask,
    kept_modes,
    mlp_master,
    mlp_first,
    mlp_second,
    filter_master,
    filter_first,
    filter_second,
    small_master,
    small_first,
    small_second,
    run_stats,
):
    group_size = lax.axis_size("sp")
    snap_local, row_local, lon_total, channel = fields.shape
    lat_total = row_local * group_size
    mode_local = kept_modes.shape[1]
    mode_total = mode_local * group_size
    block_width = channel // BLOCKS
    lon_fwd, lon_inv = lon_tables(lon_total, mode_total)
    lat_fwd = lat_table(lat_total)
    mlp_w, filt_w, small_w = (
        lax.all_gather(mlp_master.astype(jnp.bfloat16), "sp", axis=1, tiled=True),
        lax.all_gather(filter_master.astype(jnp.bfloat16), "sp", axis=1, tiled=True),
        lax.all_gather(small_master.astype(jnp.bfloat16), "sp", axis=1, tiled=True),
    )
    small_f = small_w.astype(jnp.float32)
    weights = filt_w.reshape(4, BLOCKS, block_width, block_width)
    first_pair = complex_pair(weights[0], weights[1])
    second_pair = complex_pair(weights[2], weights[3])
    bias_one = small_f[4:6].reshape(2, 1, BLOCKS, block_width)
    bias_two = small_f[6:8].reshape(2, 1, BLOCKS, block_width)
    fields_float = fields.astype(jnp.float32)
    normed, norm_pull = jax.vjp(layer_norm, fields_float, small_f[0], small_f[1])
    normed_low = normed.astype(jnp.bfloat16)
    spec_lon = jnp.einsum(
        "nrld,lqm->nrqmd", normed_low, lon_fwd, preferred_element_type=jnp.float32
    ).astype(jnp.bfloat16)
    arrived = lax.all_to_all(spec_lon, "sp", split_axis=3, concat_axis=1, tiled=True)
    spectral = spectral_front(arrived, lat_fwd, first_pair, second_pair, bias_one, bias_two)
    keep_mask = kept_modes.astype(jnp.float32)[None, :, None, :, None, None]
    masked = (shrink(spectral[3]) * keep_mask).astype(jnp.bfloat16)
    masked = masked.reshape(snap_local, lat_total, 2, mode_local, channel)
    returned = jnp.einsum(
        "pkqr,nkpmd->nrqmd", lat_fwd, masked, preferred_element_type=jnp.float32
    ).astype(jnp.bfloat16)
    home_modes = lax.all_to_all(returned, "sp", split_axis=1, concat_axis=3, tiled=True)
    filtered = jnp.einsum(
        "nrqmd,qml->nrld", home_modes, lon_inv, preferred_element_type=jnp.float32
    )
    mixture = fields_float + normed + filtered
    normed_two, norm_two_pull = jax.vjp(layer_norm, mixture, small_f[2], small_f[3])
    normed_two_low = normed_two.astype(jnp.bfloat16)
    tokens = snap_local * row_local * lon_total
    passed = mlp_pass(
        normed_two_low.reshape(tokens, channel),
        cotangent.reshape(tokens, channel),
        mlp_w,
        small_f[9:].reshape(1, -1),
    )
    output = mixture + passed[0].reshape(mixture.shape) + small_f[8]
    weight_mask = valid_mask.astype(jnp.float32)[..., None]
    variables = output[..., :NVAR]
    local_sums = jnp.stack(
        [
            jnp.sum(weight_mask * variables, axis=(0, 1, 2)),
            jnp.sum(weight_mask * variables * variables, axis=(0, 1, 2)),
        ]
    )
    total_sums = lax.psum(local_sums, ("snap", "sp"))
    positions = snap_local * lax.axis_size("snap") * lat_total * lon_total
    stats_new = stat_decay * run_stats + (1.0 - stat_decay) * total_sums / positions
    cot_float = cotangent.astype(jnp.float32)
    grad_normed_two = passed[1].reshape(mixture.shape)
    grad_bias_hidden = passed[4]
    grad_mix_norm, grad_gain_two, grad_shift_two = norm_two_pull(grad_normed_two)
    grad_mixture = cot_float + grad_mix_norm
    grad_bias_out = jnp.sum(cot_float, axis=(0, 1, 2))
    grad_filtered = grad_mixture.astype(jnp.bfloat16)
    grad_home = jnp.einsum(
        "nrld,qml->nrqmd", grad_filtered, lon_inv, preferred_element_type=jnp.float32
    ).astype(jnp.bfloat16)
    grad_returned = lax.all_to_all(grad_home, "sp", split_axis=3, concat_axis=1, tiled=True)
    grad_masked = jnp.einsum(
        "pkqr,nrqmd->nkpmd", lat_fwd, grad_returned, preferred_element_type=jnp.float32
    )
    arrived_again = lax.all_to_all(spec_lon, "sp", split_axis=3, concat_axis=1, tiled=True)
    used_front = spectral_front(arrived_again, lat_fwd, first_pair, second_pair, bias_one, bias_two)
    blocked, pre_one, act_one, pre_two = used_front
    grad_two = jax.vjp(shrink, pre_two)[1](grad_masked.reshape(pre_two.shape) * keep_mask)[
        0
    ].astype(jnp.bfloat16)
    grad_bias_two = jnp.sum(grad_two.astype(jnp.float32), axis=(0, 1, 3))
    grad_second = jnp.einsum(
        "nkqmbi,nkpmbo->pqbio", act_one, grad_two, preferred_element_type=jnp.float32
    )
    grad_act = jnp.einsum(
        "nkpmbo,pqbio->nkqmbi", grad_two, second_pair, preferred_element_type=jnp.float32
    )
    grad_one = jax.vjp(jax.nn.gelu, pre_one)[1](grad_act)[0].astype(jnp.bfloat16)
    grad_bias_one = jnp.sum(grad_one.astype(jnp.float32), axis=(0, 1, 3))
    grad_first = jnp.einsum(
        "nkqmbi,nkpmbo->pqbio", blocked, grad_one, preferred_element_type=jnp.float32
    )
    grad_spectrum = jnp.einsum(
        "nkpmbo,pqbio->nkqmbi", grad_one, first_pair, preferred_element_type=jnp.float32
    ).astype(jnp.bfloat16)
    grad_spectrum = grad_spectrum.reshape(snap_local, lat_total, 2, mode_local, channel)
    grad_lon = jnp.einsum(
        "pkqr,nkpmd->nrqmd", lat_fwd, grad_spectrum, preferred_element_type=jnp.float32
    ).astype(jnp.bfloat16)
    grad_rows = lax.all_to_all(grad_lon, "sp", split_axis=1, concat_axis=3, tiled=True)
    grad_normed = grad_mixture + jnp.einsum(
        "nrqmd,lqm->nrld", grad_rows, lon_fwd, preferred_element_type=jnp.float32
    )
    grad_field_norm, grad_gain_one, grad_shift_one = norm_pull(grad_normed)
    input_grad = grad_mixture + grad_field_norm
    grad_filter = jnp.stack(
        [
            grad_first[0, 0] + grad_first[1, 1],
            grad_first[1, 0] - grad_first[0, 1],
            grad_second[0, 0] + grad_second[1, 1],
            grad_second[1, 0] - grad_second[0, 1],
        ]
    ).reshape(4, channel, block_width)
    grad_small = jnp.concatenate(
        [
            jnp.stack([grad_gain_one, grad_shift_one, grad_gain_two, grad_shift_two]),
            grad_bias_one.reshape(2, channel),
            grad_bias_two.reshape(2, channel),
            grad_bias_out[None, :],
            grad_bias_hidden.reshape(-1, channel),
        ],
        axis=0,
    )
    shares = (
        jnp.stack([
            lax.psum_scatter(part, "sp", scatter_dimension=0, tiled=True) for part in passed[2:4]
        ]),
        lax.psum_scatter(grad_filter, "sp", scatter_dimension=1, tiled=True),
        lax.psum_scatter(grad_small, "sp", scatter_dimension=1, tiled=True),
    )
    owned = (
        lax.psum(shares[0].astype(jnp.bfloat16), "snap").astype(jnp.float32),
        lax.psum(shares[1].astype(jnp.bfloat16), "snap").astype(jnp.float32),
        lax.psum(shares[2].astype(jnp.bfloat16), "snap").astype(jnp.float32),
    )
    mlp_new, mlp_first_new, mlp_second_new, mlp_copy = adamw(
        mlp_master, mlp_first, mlp_second, owned[0], rate_mlp
    )
    filter_new, filter_first_new, filter_second_new, filter_copy = adamw(
        filter_master, filter_first, filter_second, owned[1], rate_filter
    )
    small_new, small_first_new, small_second_new, small_copy = adamw(
        small_master, small_first, small_second, owned[2], rate_small
    )
    return (
        output.astype(jnp.bfloat16),
        input_grad,
        mlp_new,
        mlp_first_new,
        mlp_second_new,
        mlp_copy,
        filter_new,
        filter_first_new,
        filter_second_new,
        filter_copy,
        small_new,
        small_first_new,
        small_second_new,
        small_copy,
        stats_new,
    )


def lon_matrix(lon_total, mode_total, snaps, rows):
    places = np.arange(lon_total)
    orders = np.arange(mode_total)
    angles = (places[:, None] * orders[None, :] % lon_total) * (2.0 * math.pi / lon_total)
    doubling = np.where(orders == 0, 1.0, 2.0)
    scaling = 1.0 / math.sqrt(lon_total)
    forward = np.stack([np.cos(angles), -np.sin(angles)], axis=1) * scaling
    inverse = forward * doubling

    def spread(table):
        table = np.einsum(
            "ab,lx,rs->alrbsx", np.eye(snaps), table.reshape(lon_total, -1), np.eye(rows)
        )
        return table.reshape(snaps * lon_total * rows, -1).astype(ml_dtypes.bfloat16)

    return spread(forward), spread(inverse)


def lon_turn(lon_total, rows):
    turn = np.einsum("lk,rs->rlks", np.eye(lon_total), np.eye(rows))
    return turn.reshape(rows, lon_total, lon_total * rows).astype(ml_dtypes.bfloat16)


def lat_matrix(lat_total, mode_total):
    places = np.arange(lat_total)
    angles = (places[:, None] * places[None, :] % lat_total) * (2.0 * math.pi / lat_total)
    cosine, sine = np.cos(angles), np.sin(angles)
    table = np.stack([np.stack([cosine, sine], axis=1), np.stack([-sine, cosine], axis=1)])
    table = np.einsum("pkqr,ab->pakrqb", table / math.sqrt(lat_total), np.eye(mode_total))
    size = 2 * lat_total * mode_total
    return table.reshape(size, size).astype(ml_dtypes.bfloat16)


class Refs:
    pass


def block_body(names, sizes, *refs):
    g = Refs()
    for name, ref in zip(names, refs, strict=True):
        setattr(g, name, ref)
    snaps, group, parts, width = sizes
    levels = group // 2
    tokens, channel = g.fields.shape
    owned = channel // group
    half = width // 2
    quarter = width // snaps
    tile = divisor(tokens, 16, 480)
    strip = divisor(tokens, 16, 240)
    low = jnp.bfloat16
    f32 = jnp.float32

    me_snap = lax.axis_index("snap")
    me_sp = lax.axis_index("sp")
    core = lax.rem(me_sp, 2)
    level = me_sp // 2

    def at(snap, sp):
        return {"snap": snap, "sp": sp}

    def sp_after(step):
        return lax.rem(me_sp + step, group)

    def sp_before(step):
        return lax.rem(me_sp + group - step, group)

    def snap_after(step):
        return lax.rem(me_snap + step, snaps)

    def snap_before(step):
        return lax.rem(me_snap + snaps - step, snaps)

    def level_after(step):
        return lax.rem(level + step, levels)

    def level_before(step):
        return lax.rem(level + levels - step, levels)

    other_core = at(me_snap, me_sp + 1 - 2 * core)

    def send(src, dst, sems, index, target):
        return pltpu.make_async_remote_copy(
            src_ref=src,
            dst_ref=dst,
            send_sem=sems[0].at[index],
            recv_sem=sems[1].at[index],
            device_id=target,
            device_id_type=pl.DeviceIdType.MESH,
        )

    def strips(body):
        @pl.loop(0, tokens // strip)
        def _(step):
            body(pl.ds(pl.multiple_of(step * strip, strip), strip))

    loads = {}

    def load(name, index):
        copy = pltpu.make_async_copy(getattr(g, name), getattr(g, name + "_in"), g.load_sem.at[index])
        copy.start()
        loads[name] = copy

    for index, name in enumerate(
        [name for name in names[: names.index("out")] if name != "mlp"]
    ):
        load(name, index)

    def master_load(part):
        return pltpu.make_async_copy(
            g.mlp.at[:, :, part * width : (part + 1) * width],
            g.mlp_part.at[part % 2],
            g.load_sem.at[len(loads) + part % 2],
        )

    master_load(0).start()
    master_load(1).start()

    barrier = pltpu.get_barrier_semaphore()
    peers = [at(me_snap, sp_after(step)) for step in range(1, group)]
    peers += [at(snap_after(step), me_sp) for step in range(1, snaps)]
    for peer in peers:
        pl.semaphore_signal(
            barrier, inc=1, device_id=peer, device_id_type=pl.DeviceIdType.MESH
        )

    loads["small"].wait()
    loads["kept"].wait()
    g.own_small[...] = jnp.zeros_like(g.own_small)
    rows_small = g.small.shape[0]
    g.own_small[0:rows_small, 0:owned] = g.small_in[...].astype(low).astype(f32)
    pairs_kept = g.kept.shape[1]
    lines = lax.broadcasted_iota(jnp.int32, (pairs_kept, pairs_kept), 0)
    places = lax.broadcasted_iota(jnp.int32, (pairs_kept, pairs_kept), 1)
    kept = jnp.where(lines == places, g.kept_in[...].astype(f32), 0.0)
    g.own_small[16:, :] = jnp.broadcast_to(
        jnp.sum(kept, axis=1, keepdims=True), (pairs_kept, g.own_small.shape[1])
    )
    pl.semaphore_wait(barrier, len(peers))

    def small_copy(step):
        return send(
            g.own_small, g.all_small.at[me_sp], (g.small_s, g.small_r), step, at(me_snap, sp_after(step))
        )

    for step in range(1, group):
        small_copy(step).start()
    g.all_small[me_sp] = g.own_small[...]

    snap_low = lax.rem(me_snap, 2)
    snap_high = me_snap // 2
    beside_low = me_snap + 1 - 2 * snap_low
    beside_high = me_snap + 2 - 4 * snap_high

    def own_quarter(part):
        odd = lax.rem(part, 2)
        return (1 - odd) * me_snap + odd * (2 * snap_low + snap_high)

    def quarter_cols(part):
        return pl.ds(pl.multiple_of(own_quarter(part) * quarter, quarter), quarter)

    def half_cols(part):
        return pl.ds(pl.multiple_of((own_quarter(part) // 2) * half, half), half)

    def own_rows(sp):
        return pl.ds(pl.multiple_of(sp * owned, owned), owned)

    def first_copy(part, step):
        target = sp_after(step)
        matrix = lax.rem(target, 2)
        cols = quarter_cols(part)
        return send(
            g.own_w.at[part, matrix, :, cols],
            g.all_w.at[part, matrix, own_rows(me_sp), cols],
            (g.first_s, g.first_r),
            (part, step),
            at(me_snap, target),
        )

    def first_local(part):
        cols = quarter_cols(part)
        return pltpu.make_async_copy(
            g.own_w.at[part, core, :, cols],
            g.all_w.at[part, core, own_rows(me_sp), cols],
            g.first_s.at[part, 0],
        )

    def second_copy(part):
        odd = lax.rem(part, 2)
        view = g.all_w.at[part, core, :, quarter_cols(part)]
        target = at((1 - odd) * beside_low + odd * beside_high, me_sp)
        return send(view, view, (g.second_s, g.second_r), part, target)

    def third_copy(part):
        odd = lax.rem(part, 2)
        view = g.all_w.at[part, core, :, half_cols(part)]
        target = at((1 - odd) * beside_high + odd * beside_low, me_sp)
        return send(view, view, (g.third_s, g.third_r), part, target)

    def fourth_copy(part):
        view = g.all_w.at[part, core]
        return send(view, view, (g.fourth_s, g.fourth_r), part, other_core)

    def start_first(part):
        for step in range(1, group):
            first_copy(part, step).start()
        first_local(part).start()

    def pass_second(part):
        for step in range(1, group):
            first_copy(part, step).wait_recv()
        first_local(part).wait()
        second_copy(part).start()

    def pass_third(part):
        second_copy(part).wait_recv()
        third_copy(part).start()

    def pass_fourth(part):
        third_copy(part).wait_recv()
        fourth_copy(part).start()

    for part in range(parts):
        master_load(part).wait()
        g.own_w[part] = g.mlp_part[part % 2].astype(low)
        if part + 2 < parts:
            master_load(part + 2).start()
        if part < 2:
            start_first(part)

    loads["fields"].wait()
    for step in range(1, group):
        small_copy(step).wait_recv()
    for sp in range(group):
        g.gains[:, sp * owned : (sp + 1) * owned] = g.all_small[sp, 0:16, 0:owned]
        g.keep[sp * pairs_kept : (sp + 1) * pairs_kept, :] = g.all_small[sp, 16:, :]

    def first_norm(rows):
        values = g.fields_in[rows, :].astype(f32)
        centred = values - jnp.mean(values, axis=-1, keepdims=True)
        scale = lax.rsqrt(jnp.mean(centred * centred, axis=-1, keepdims=True) + eps_norm)
        centred = centred * scale
        normed = centred * g.gains[0:1, :] + g.gains[1:2, :]
        g.unit_one[rows, :] = centred.astype(low)
        g.scale_one[rows, :] = scale
        g.normed[rows, :] = normed.astype(low)
        g.grid[rows, :] = values + normed

    strips(first_norm)

    def to_blocks(table, which):
        modes = dot_nn(table, g.normed[...])
        for block in range(group):
            cut = modes[:, block * owned : (block + 1) * owned]
            cut = jnp.concatenate(
                [cut, jnp.zeros((cut.shape[0], 128 - owned), f32)], axis=1
            )
            g.modes[block] = cut.astype(low).reshape(g.modes.shape[1:])
        for step in range(1, group):
            block_copy(which, step).start()
        g.arrived[:, mode_rows(me_sp), :] = g.modes[me_sp]

    def mode_rows(sp):
        size = g.modes.shape[2]
        return pl.ds(pl.multiple_of(sp * size, size), size)

    def block_copy(which, step):
        target = sp_after(step)
        return send(
            g.modes.at[target],
            g.arrived.at[:, mode_rows(me_sp), :],
            (g.block_s, g.block_r),
            (which, step),
            at(me_snap, target),
        )

    def row_copy(which, step):
        target = sp_after(step)
        return send(
            g.turned.at[:, mode_rows(target), :],
            g.home.at[me_sp],
            (g.row_s, g.row_r),
            (which, step),
            at(me_snap, target),
        )

    def to_rows(which):
        for step in range(1, group):
            row_copy(which, step).start()
        g.home[me_sp] = g.turned[:, mode_rows(me_sp), :]

    def home_modes(which):
        for step in range(1, group):
            row_copy(which, step).wait_recv()
        for block in range(group):
            g.gathered[:, block * owned : (block + 1) * owned] = (
                g.home[block].reshape(g.gathered.shape[0], 128)[:, 0:owned].astype(f32)
            )
        return g.gathered[...].astype(low)

    loads["lon_f"].wait()
    to_blocks(g.lon_f_in[...], 0)
    for part in range(2, 4):
        start_first(part)

    loads["filt"].wait()
    for weight, first in ((g.weight_one, 0), (g.weight_two, 2)):
        weight[...] = jnp.zeros_like(weight)
        real = g.filt_in[first].astype(low)
        imag = g.filt_in[first + 1].astype(low)
        weight[0:owned, 0:owned] = real
        weight[128 : 128 + owned, 128 : 128 + owned] = real
        weight[0:owned, 128 : 128 + owned] = imag
        weight[128 : 128 + owned, 0:owned] = -imag

    def bias_row(first):
        return jnp.concatenate(
            [g.own_small[first : first + 1, :], g.own_small[first + 1 : first + 2, :]], axis=1
        )

    loads["lat_f"].wait()
    loads["lat_b"].wait()
    for step in range(1, group):
        block_copy(0, step).wait_recv()
    snap_local = g.arrived.shape[0]
    pairs = g.arrived.shape[1] // 2

    def spectra(out, kind):
        for snap in range(snap_local):
            spectrum = dot_nn(g.lat_f_in[...], g.arrived[snap]).astype(kind)
            rows = slice(snap * pairs, (snap + 1) * pairs)
            out[rows, 0:128] = spectrum[0:pairs]
            out[rows, 128:256] = spectrum[pairs:]

    def grids(values):
        for snap in range(snap_local):
            rows = values[snap * pairs : (snap + 1) * pairs]
            rows = jnp.concatenate([rows[:, 0:128], rows[:, 128:256]], axis=0)
            g.turned[snap] = dot_nn(g.lat_b_in[...], rows).astype(low)

    def keep_all():
        keep = jnp.concatenate([g.keep[...], g.keep[...]], axis=1)
        return jnp.concatenate([keep] * snap_local, axis=0)

    spectra(g.spectrum, low)
    g.pre_one[...] = dot_nn(g.spectrum[...], g.weight_one[...]) + bias_row(4)
    g.act_one[...] = gelu_both(g.pre_one[...])[0].astype(low)
    g.pre_two[...] = dot_nn(g.act_one[...], g.weight_two[...]) + bias_row(6)
    grids((shrink(g.pre_two[...]) * keep_all()).astype(low))
    to_rows(0)

    for part in range(2):
        pass_second(part)
    for part in range(4, parts):
        start_first(part)
    loads["cot"].wait()
    g.cot_turned[...] = g.cot_in[...].T
    for part in range(2):
        pass_third(part)

    loads["lon_i"].wait()
    g.home_low[...] = home_modes(0)

    def add_filtered(rows):
        g.grid[rows, :] += dot_nn(g.lon_i_in[rows, :], g.home_low[...])

    def second_norm(rows):
        values = g.grid[rows, :]
        centred = values - jnp.mean(values, axis=-1, keepdims=True)
        scale = lax.rsqrt(jnp.mean(centred * centred, axis=-1, keepdims=True) + eps_norm)
        centred = centred * scale
        g.unit_two[rows, :] = centred.astype(low)
        g.scale_two[rows, :] = scale
        g.normed[rows, :] = (centred * g.gains[2:3, :] + g.gains[3:4, :]).astype(low)
        g.grid[rows, :] = values + g.gains[8:9, :]
        g.back[rows, :] = jnp.zeros((strip, channel), f32)

    add_filtered(slice(0, tokens))
    for part in range(2, 4):
        pass_second(part)
    pass_fourth(0)
    strips(second_norm)
    pass_fourth(1)
    for part in range(2, 4):
        pass_third(part)
    g.normed_turned[...] = g.normed[...].T
    for part in range(parts):
        flat = jnp.concatenate([g.gains[9 + row : 10 + row, :] for row in range(rows_small - 9)], axis=1)
        g.bias[part] = flat[:, part * width : (part + 1) * width]

    def core_copy(part, matrix):
        slot = lax.rem(part, 2)
        return send(
            g.grads.at[slot, matrix, :, 1 - core],
            g.core_got.at[slot, matrix],
            (g.core_s, g.core_r),
            (slot, matrix),
            other_core,
        )

    places_one = (snap_low, snap_high)
    places_two = (snap_high, snap_low)
    beside_one = (beside_low, beside_high)
    beside_two = (beside_high, beside_low)
    place_last = (2 * snap_low + snap_high, me_snap)

    def half_copy(part, matrix):
        slot = lax.rem(part, 2)
        return send(
            g.half_out.at[slot, matrix, 1 - places_one[matrix]],
            g.half_got.at[slot, matrix],
            (g.half_s, g.half_r),
            (slot, matrix),
            at(beside_one[matrix], me_sp),
        )

    def quarter_copy(part, matrix):
        slot = lax.rem(part, 2)
        return send(
            g.quarter_out.at[slot, matrix, 1 - places_two[matrix]],
            g.quarter_got.at[slot, matrix],
            (g.quarter_s, g.quarter_r),
            (slot, matrix),
            at(beside_two[matrix], me_sp),
        )

    def level_copy(part, step):
        slot = lax.rem(part, 2)
        target = level_after(step)
        return send(
            g.level_out.at[slot, target],
            g.level_got.at[slot, level],
            (g.level_s, g.level_r),
            (slot, step),
            at(me_snap, 2 * target + core),
        )

    def last_copy(part, matrix, step):
        view = g.total.at[part, place_last[matrix], matrix]
        return send(
            view, view, (g.last_s, g.last_r), (part, matrix, step), at(snap_after(step), me_sp)
        )

    def half_stage(part):
        slot = lax.rem(part, 2)
        for matrix in range(2):

            @pl.when(part >= 2)
            def _(matrix=matrix):
                half_copy(part - 2, matrix).wait_send()

            core_copy(part, matrix).wait_recv()
            for row in range(levels):
                both = g.grads[slot, matrix, row, core].astype(f32) + g.core_got[
                    slot, matrix, row
                ].astype(f32)
                both = both.astype(low)
                g.half_out[slot, matrix, 0, row] = both[:, 0:half]
                g.half_out[slot, matrix, 1, row] = both[:, half:width]
            half_copy(part, matrix).start()

    def quarter_stage(part):
        slot = lax.rem(part, 2)
        for matrix in range(2):

            @pl.when(part >= 2)
            def _(matrix=matrix):
                quarter_copy(part - 2, matrix).wait_send()

            half_copy(part, matrix).wait_recv()
            for row in range(levels):
                both = g.half_out[slot, matrix, places_one[matrix], row].astype(f32) + g.half_got[
                    slot, matrix, row
                ].astype(f32)
                both = both.astype(low)
                g.quarter_out[slot, matrix, 0, row] = both[:, 0:quarter]
                g.quarter_out[slot, matrix, 1, row] = both[:, quarter:half]
            quarter_copy(part, matrix).start()

    def level_stage(part):
        slot = lax.rem(part, 2)

        @pl.when(part >= 2)
        def _():
            for step in range(1, levels):
                level_copy(part - 2, step).wait_send()

        for matrix in range(2):
            quarter_copy(part, matrix).wait_recv()
            for row in range(levels):
                both = g.quarter_out[slot, matrix, places_two[matrix], row].astype(
                    f32
                ) + g.quarter_got[slot, matrix, row].astype(f32)
                g.level_out[slot, row, matrix] = both.astype(low)
        for step in range(1, levels):
            level_copy(part, step).start()

    def last_stage(part):
        slot = lax.rem(part, 2)
        for step in range(1, levels):
            level_copy(part, step).wait_recv()
        for matrix in range(2):
            sums = g.level_out[slot, level, matrix].astype(f32)
            for step in range(1, levels):
                sums += g.level_got[slot, level_before(step), matrix].astype(f32)
            g.total[part, place_last[matrix], matrix] = sums.astype(low)
            for step in range(1, snaps):
                last_copy(part, matrix, step).start()

    @pl.loop(0, parts)
    def _(part):
        slot = lax.rem(part, 2)

        @pl.when(part >= 3)
        def _():
            level_stage(part - 3)

        @pl.when(part + 4 < parts)
        def _():
            pass_second(part + 4)

        fourth_copy(part).wait_recv()
        g.grad_bias[part] = jnp.zeros(g.grad_bias.shape[1:], f32)

        @pl.loop(0, tokens // tile)
        def _(step):
            rows = pl.ds(pl.multiple_of(step * tile, tile), tile)
            act, slope = gelu_both(dot_nn(g.normed[rows, :], g.all_w[part, 0]) + g.bias[part])
            act = act.astype(low)
            slope = (dot_nn(g.cot_in[rows, :], g.all_w[part, 1]) * slope).astype(low)
            g.act[rows, :] = act
            g.slope[rows, :] = slope
            g.grad_bias[part] += jnp.sum(slope.astype(f32), axis=0, keepdims=True)
            g.grid[rows, :] += dot_nt(act, g.all_w[part, 1])
            g.back[rows, :] += dot_nt(slope, g.all_w[part, 0])

        @pl.when(part + 2 < parts)
        def _():
            pass_fourth(part + 2)

        @pl.when(part + 4 < parts)
        def _():
            pass_third(part + 4)

        @pl.when(part >= 3)
        def _():
            last_stage(part - 3)

        @pl.when(part >= 2)
        def _():
            quarter_stage(part - 2)

        @pl.when(part >= 1)
        def _():
            half_stage(part - 1)

        @pl.when(part >= 2)
        def _():
            for matrix in range(2):
                core_copy(part - 2, matrix).wait_send()

        shape = g.grads.shape[2:]
        g.grads[slot, 0] = dot_nn(g.normed_turned[...], g.slope[...]).astype(low).reshape(shape)
        core_copy(part, 0).start()
        g.grads[slot, 1] = dot_nn(g.cot_turned[...], g.act[...]).astype(low).reshape(shape)
        core_copy(part, 1).start()

    level_stage(parts - 3)

    def low_out(rows):
        g.fields_in[rows, :] = g.grid[rows, :].astype(low)

    strips(low_out)
    out_copy = pltpu.make_async_copy(g.fields_in, g.out, g.load_sem.at[0])
    out_copy.start()
    loads["valid"].wait()
    loads["turn"].wait()
    weigh = sum(
        dot_nn(g.valid_in[:, row, :].astype(f32).astype(low), g.turn_in[row])
        for row in range(g.valid.shape[1])
    )
    places_each = weigh.shape[1]
    precise = lax.Precision.HIGHEST
    sums = [jnp.zeros((1, 128), f32), jnp.zeros((1, 128), f32)]
    for snap in range(g.valid.shape[0]):
        variables = g.grid[snap * places_each : (snap + 1) * places_each, 0:128]
        for index, value in enumerate((variables, variables * variables)):
            sums[index] += jnp.dot(
                weigh[snap : snap + 1, :], value, precision=precise, preferred_element_type=f32
            )

    g.grad_rows[...] = jnp.zeros_like(g.grad_rows)

    def second_back(rows):
        grad = g.back[rows, :]
        unit = g.unit_two[rows, :].astype(f32)
        cot = g.cot_in[rows, :].astype(f32)
        pulled = grad * g.gains[2:3, :]
        middle = jnp.mean(pulled, axis=-1, keepdims=True)
        slant = jnp.mean(pulled * unit, axis=-1, keepdims=True)
        total = cot + g.scale_two[rows, :] * (pulled - middle - unit * slant)
        g.back[rows, :] = total
        g.normed[rows, :] = total.astype(low)
        g.grad_rows[2:3, :] += jnp.sum(grad * unit, axis=0, keepdims=True)
        g.grad_rows[3:4, :] += jnp.sum(grad, axis=0, keepdims=True)
        g.grad_rows[8:9, :] += jnp.sum(cot, axis=0, keepdims=True)

    strips(second_back)
    loads["lon_it"].wait()
    for step in range(1, group):
        block_copy(0, step).wait_send()
    to_blocks(g.lon_it_in[...], 1)

    last_stage(parts - 3)
    quarter_stage(parts - 2)
    half_stage(parts - 1)

    for step in range(1, group):
        block_copy(1, step).wait_recv()
    spectra(g.grad_two, f32)
    bend = jnp.tanh(g.pre_two[...] / shrink_level)
    grad_two = (g.grad_two[...] * keep_all() * (bend * bend)).astype(low)

    def dot_tn(left, right):
        return lax.dot_general(
            left, right, (((0,), (0,)), ((), ())), preferred_element_type=f32
        )

    def filter_rows(first, grad):
        g.pair_grad[...] = grad
        real = g.pair_grad[0:128, 0:128] + g.pair_grad[128:256, 128:256]
        imag = g.pair_grad[0:128, 128:256] - g.pair_grad[128:256, 0:128]
        g.filt_out[me_snap, first] = real[0:owned].astype(low)
        g.filt_out[me_snap, first + 1] = imag[0:owned].astype(low)

    bias_two = jnp.sum(grad_two.astype(f32), axis=0, keepdims=True)
    filter_rows(2, dot_tn(g.act_one[...], grad_two))
    grad_one = dot_nt(grad_two, g.weight_two[...])
    grad_one = (grad_one * gelu_both(g.pre_one[...])[1]).astype(low)
    bias_one = jnp.sum(grad_one.astype(f32), axis=0, keepdims=True)
    for step in range(1, group):
        row_copy(0, step).wait_send()
    grids(dot_nt(grad_one, g.weight_one[...]).astype(low))
    to_rows(1)
    level_stage(parts - 2)
    quarter_stage(parts - 1)
    filter_rows(0, dot_tn(g.spectrum[...], grad_one))

    def filter_copy(step):
        view = g.filt_out.at[me_snap]
        return send(view, view, (g.filt_s, g.filt_r), step, at(snap_after(step), me_sp))

    for step in range(1, snaps):
        filter_copy(step).start()

    last_stage(parts - 2)
    level_stage(parts - 1)

    loads["lon_ft"].wait()
    g.home_low[...] = home_modes(1)
    grad_copy = pltpu.make_async_copy(g.grid, g.in_grad, g.load_sem.at[1])

    def add_modes(rows):
        g.grid[rows, :] = g.back[rows, :] + dot_nn(g.lon_ft_in[rows, :], g.home_low[...])

    def first_back(rows):
        grad = g.grid[rows, :]
        unit = g.unit_one[rows, :].astype(f32)
        pulled = grad * g.gains[0:1, :]
        middle = jnp.mean(pulled, axis=-1, keepdims=True)
        slant = jnp.mean(pulled * unit, axis=-1, keepdims=True)
        g.grid[rows, :] = g.back[rows, :] + g.scale_one[rows, :] * (
            pulled - middle - unit * slant
        )
        g.grad_rows[0:1, :] += jnp.sum(grad * unit, axis=0, keepdims=True)
        g.grad_rows[1:2, :] += jnp.sum(grad, axis=0, keepdims=True)

    add_modes(slice(0, tokens))
    strips(first_back)
    grad_copy.start()

    flat = jnp.concatenate([g.grad_bias[part] for part in range(parts)], axis=1)
    for row in range(rows_small - 9):
        g.grad_rows[9 + row : 10 + row, :] = flat[:, row * channel : (row + 1) * channel]
    for block in range(group):
        g.tiles[block] = jnp.zeros(g.tiles.shape[1:], f32)
        g.tiles[block, :, 0:owned] = g.grad_rows[:, block * owned : (block + 1) * owned]
        g.tiles[block, 13:14, :] = sums[0]
        g.tiles[block, 14:15, :] = sums[1]

    def tile_copy(step):
        target = sp_after(step)
        return send(
            g.tiles.at[target], g.tiles_got.at[me_sp], (g.tile_s, g.tile_r), step, at(me_snap, target)
        )

    def snap_tile_copy(step):
        view = g.snap_tiles.at[me_snap]
        return send(view, view, (g.snap_tile_s, g.snap_tile_r), step, at(snap_after(step), me_sp))

    for step in range(1, group):
        tile_copy(step).start()
    last_stage(parts - 1)

    g.tiles_got[me_sp] = g.tiles[me_sp]
    for step in range(1, group):
        tile_copy(step).wait_recv()
    tile_sum = g.tiles_got[0]
    for sp in range(1, group):
        tile_sum += g.tiles_got[sp]
    g.snap_tiles[me_snap] = tile_sum
    g.snap_tiles[me_snap, 4:5, :] = bias_one[:, 0:128]
    g.snap_tiles[me_snap, 5:6, :] = bias_one[:, 128:256]
    g.snap_tiles[me_snap, 6:7, :] = bias_two[:, 0:128]
    g.snap_tiles[me_snap, 7:8, :] = bias_two[:, 128:256]
    for step in range(1, snaps):
        snap_tile_copy(step).start()

    for step in range(1, snaps):
        filter_copy(step).wait_recv()
    filter_sum = g.filt_out[0].astype(f32)
    for snap in range(1, snaps):
        filter_sum += g.filt_out[snap].astype(f32)
    g.grad_filt[...] = filter_sum
    for part in range(parts):
        for matrix in range(2):
            for step in range(1, snaps):
                last_copy(part, matrix, step).wait_recv()
    grads_out = pltpu.make_async_copy(g.total, g.grad_mlp, g.load_sem.at[3])
    grads_out.start()
    for step in range(1, snaps):
        snap_tile_copy(step).wait_recv()
    tile_sum = g.snap_tiles[0]
    for snap in range(1, snaps):
        tile_sum += g.snap_tiles[snap]
    g.grad_small[...] = tile_sum

    out_copy.wait()
    grads_out.wait()
    grad_copy.wait()
    for step in range(1, group):
        small_copy(step).wait_send()
        block_copy(1, step).wait_send()
        row_copy(1, step).wait_send()
        tile_copy(step).wait_send()
        for part in range(parts):
            first_copy(part, step).wait_send()
    for part in range(parts):
        second_copy(part).wait_send()
        third_copy(part).wait_send()
        fourth_copy(part).wait_send()
    for part in (parts - 2, parts - 1):
        for matrix in range(2):
            core_copy(part, matrix).wait_send()
            half_copy(part, matrix).wait_send()
            quarter_copy(part, matrix).wait_send()
        for step in range(1, levels):
            level_copy(part, step).wait_send()
    for step in range(1, snaps):
        filter_copy(step).wait_send()
        snap_tile_copy(step).wait_send()
        for part in range(parts):
            for matrix in range(2):
                last_copy(part, matrix, step).wait_send()


def block_pass(fields, cot, valid, kept, mlp, filt, small, snaps, group):
    snap_local, row_local, lon_total, channel = fields.shape
    tokens = snap_local * row_local * lon_total
    hidden = mlp.shape[2]
    lat_total = row_local * group
    modes = kept.shape[1] * group
    owned = channel // group
    width = 512
    parts = hidden // width
    levels = group // 2
    quarter = width // snaps
    low, f32 = jnp.bfloat16, jnp.float32
    half = width // 2
    lon_f, lon_i = lon_matrix(lon_total, modes, snap_local, row_local)

    def flat(array):
        return jnp.transpose(array, (0, 2, 1, 3)).reshape(tokens, channel)

    lat_f = lat_matrix(lat_total, modes)
    pair = 2 * modes * row_local
    spread = snap_local * row_local * 2 * modes
    inputs = dict(
        small=small,
        kept=kept.T,
        fields=flat(fields),
        lon_f=jnp.asarray(np.ascontiguousarray(lon_f.T)),
        filt=filt,
        lat_f=jnp.asarray(lat_f),
        lat_b=jnp.asarray(np.ascontiguousarray(lat_f.T)),
        cot=flat(cot),
        lon_i=jnp.asarray(lon_i),
        valid=valid,
        turn=jnp.asarray(lon_turn(lon_total, row_local)),
        lon_it=jnp.asarray(np.ascontiguousarray(lon_i.T)),
        lon_ft=jnp.asarray(lon_f),
        mlp=mlp,
    )
    outputs = dict(
        out=jax.ShapeDtypeStruct((tokens, channel), low),
        in_grad=jax.ShapeDtypeStruct((tokens, channel), f32),
        grad_mlp=jax.ShapeDtypeStruct((parts, snaps, 2, owned, quarter), low),
        grad_filt=jax.ShapeDtypeStruct((4, owned, 128), f32),
        grad_small=jax.ShapeDtypeStruct((16, 128), f32),
    )
    vmem = pltpu.VMEM
    dma = pltpu.SemaphoreType.DMA
    scratch = {
        name + "_in": vmem(value.shape, value.dtype)
        for name, value in inputs.items()
        if name != "mlp"
    }
    scratch |= dict(
        mlp_part=vmem((2, 2, owned, width), f32),
        grid=vmem((tokens, channel), f32),
        back=vmem((tokens, channel), f32),
        normed=vmem((tokens, channel), low),
        normed_turned=vmem((channel, tokens), low),
        cot_turned=vmem((channel, tokens), low),
        unit_one=vmem((tokens, channel), low),
        unit_two=vmem((tokens, channel), low),
        scale_one=vmem((tokens, 1), f32),
        scale_two=vmem((tokens, 1), f32),
        own_small=vmem((16 + kept.shape[0], 128), f32),
        all_small=vmem((group, 16 + kept.shape[0], 128), f32),
        gains=vmem((16, channel), f32),
        keep=vmem((lat_total * modes, 128), f32),
        own_w=vmem((parts, 2, owned, width), low),
        all_w=vmem((parts, 2, channel, width), low),
        modes=vmem((group, snap_local, pair, 128), low),
        arrived=vmem((snap_local, pair * group, 128), low),
        turned=vmem((snap_local, pair * group, 128), low),
        home=vmem((group, snap_local, pair, 128), low),
        gathered=vmem((spread, channel), f32),
        home_low=vmem((spread, channel), low),
        weight_one=vmem((256, 256), low),
        weight_two=vmem((256, 256), low),
        spectrum=vmem((snap_local * lat_total * modes, 256), low),
        pre_one=vmem((snap_local * lat_total * modes, 256), f32),
        act_one=vmem((snap_local * lat_total * modes, 256), low),
        pre_two=vmem((snap_local * lat_total * modes, 256), f32),
        grad_two=vmem((snap_local * lat_total * modes, 256), f32),
        pair_grad=vmem((256, 256), f32),
        act=vmem((tokens, width), low),
        slope=vmem((tokens, width), low),
        bias=vmem((parts, 1, width), f32),
        grad_bias=vmem((parts, 1, width), f32),
        grad_rows=vmem((16, channel), f32),
        grads=vmem((2, 2, levels, 2, owned, width), low),
        core_got=vmem((2, 2, levels, owned, width), low),
        half_out=vmem((2, 2, 2, levels, owned, half), low),
        half_got=vmem((2, 2, levels, owned, half), low),
        quarter_out=vmem((2, 2, 2, levels, owned, quarter), low),
        quarter_got=vmem((2, 2, levels, owned, quarter), low),
        level_out=vmem((2, levels, 2, owned, quarter), low),
        level_got=vmem((2, levels, 2, owned, quarter), low),
        total=vmem((parts, snaps, 2, owned, quarter), low),
        filt_out=vmem((snaps, 4, owned, 128), low),
        tiles=vmem((group, 16, 128), f32),
        tiles_got=vmem((group, 16, 128), f32),
        snap_tiles=vmem((snaps, 16, 128), f32),
        load_sem=dma((len(inputs) + 1,)),
    )
    for name, shape in dict(
        small=(group,),
        first=(parts, group),
        second=(parts,),
        third=(parts,),
        fourth=(parts,),
        block=(2, group),
        row=(2, group),
        core=(2, 2),
        half=(2, 2),
        quarter=(2, 2),
        level=(2, levels),
        last=(parts, 2, snaps),
        filt=(snaps,),
        tile=(group,),
        snap_tile=(snaps,),
    ).items():
        scratch[name + "_s"] = dma(shape)
        scratch[name + "_r"] = dma(shape)
    names = [*inputs, *outputs, *scratch]
    far = pl.BlockSpec(memory_space=pl.ANY)
    near = pl.BlockSpec(memory_space=pltpu.VMEM)
    results = pl.pallas_call(
        functools.partial(block_body, names, (snaps, group, parts, width)),
        in_specs=[far] * len(inputs),
        out_specs=[far, far, far, near, near],
        out_shape=list(outputs.values()),
        scratch_shapes=list(scratch.values()),
        compiler_params=pltpu.CompilerParams(
            collective_id=0, has_side_effects=True, vmem_limit_bytes=VMEM_LIMIT
        ),
        cost_estimate=pl.CostEstimate(
            flops=12 * tokens * channel * hidden,
            bytes_accessed=4 * hidden * channel,
            transcendentals=tokens * hidden,
        ),
        name="block_pass",
    )(*inputs.values())
    rows_apart = (snap_local, lon_total, row_local, channel)
    return [jnp.transpose(array.reshape(rows_apart), (0, 2, 1, 3)) for array in results[:2]] + list(
        results[2:]
    )


def step_body(rates, *refs):
    (mlp_g, filt_g, small_g, mlp_w, mlp_m, mlp_v, filt_w, filt_m, filt_v, small_w, small_m, small_v, run) = refs[:13]
    (mlp_o, filt_o, small_o, stats_o) = refs[13:17], refs[17:21], refs[21:25], refs[25]
    snaps = mlp_g.shape[1]
    quarter = mlp_g.shape[4]

    def store(outs, where, results):
        for ref, value in zip(outs, results, strict=True):
            ref[where] = value

    for snap in range(snaps):
        cols = (slice(None), slice(None), slice(snap * quarter, (snap + 1) * quarter))
        grad = mlp_g[0, snap].astype(jnp.float32)
        store(mlp_o, cols, adamw(mlp_w[cols], mlp_m[cols], mlp_v[cols], grad, rate_mlp))

    @pl.when(pl.program_id(0) == 0)
    def _():
        owned = filt_w.shape[2]
        store(
            filt_o,
            ...,
            adamw(filt_w[...], filt_m[...], filt_v[...], filt_g[:, :, 0:owned], rate_filter),
        )
        rows = small_w.shape[0]
        store(
            small_o,
            ...,
            adamw(small_w[...], small_m[...], small_v[...], small_g[0:rows, 0:owned], rate_small),
        )
        count = run.shape[1]
        totals = small_g[rows : rows + 2, 0:count]
        stats_o[...] = stat_decay * run[...] + (1.0 - stat_decay) * totals / rates


def step_pass(grads, masters, run_stats, positions):
    grad_mlp, grad_filt, grad_small = grads
    mlp, filt, small = masters
    parts = grad_mlp.shape[0]
    width = mlp[0].shape[2] // parts
    f32, low = jnp.float32, jnp.bfloat16

    def whole(shape):
        return pl.BlockSpec(shape, lambda j: (0,) * len(shape))

    block = pl.BlockSpec((*mlp[0].shape[:2], width), lambda j: (0, 0, j))
    filt_block, small_block = whole(filt[0].shape), whole(small[0].shape)

    def four(array):
        return [jax.ShapeDtypeStruct(array.shape, kind) for kind in (f32, f32, f32, low)]

    return pl.pallas_call(
        functools.partial(step_body, positions),
        grid=(parts,),
        in_specs=[
            pl.BlockSpec((1, *grad_mlp.shape[1:]), lambda j: (j, 0, 0, 0, 0)),
            whole(grad_filt.shape),
            whole(grad_small.shape),
            *[block] * 3,
            *[filt_block] * 3,
            *[small_block] * 3,
            whole(run_stats.shape),
        ],
        out_specs=[*[block] * 4, *[filt_block] * 4, *[small_block] * 4, whole(run_stats.shape)],
        out_shape=[
            *four(mlp[0]),
            *four(filt[0]),
            *four(small[0]),
            jax.ShapeDtypeStruct(run_stats.shape, f32),
        ],
        compiler_params=pltpu.CompilerParams(vmem_limit_bytes=40 * 1024 * 1024),
        name="step_pass",
    )(grad_mlp, grad_filt, grad_small, *mlp, *filt, *small, run_stats)


def per_device_blocks(
    fields,
    cotangent,
    valid_mask,
    kept_modes,
    mlp_master,
    mlp_first,
    mlp_second,
    filter_master,
    filter_first,
    filter_second,
    small_master,
    small_first,
    small_second,
    run_stats,
):
    snaps, group = lax.axis_size("snap"), lax.axis_size("sp")
    out, in_grad, *grads = block_pass(
        fields, cotangent, valid_mask, kept_modes, mlp_master, filter_master, small_master, snaps, group
    )
    positions = fields.shape[0] * snaps * fields.shape[1] * group * fields.shape[2]
    stepped = step_pass(
        grads,
        (
            (mlp_master, mlp_first, mlp_second),
            (filter_master, filter_first, filter_second),
            (small_master, small_first, small_second),
        ),
        run_stats,
        positions,
    )
    return (out, in_grad, *stepped)


def per_device(*arrays):
    group, snaps = lax.axis_size("sp"), lax.axis_size("snap")
    channel, hidden = arrays[0].shape[3], arrays[4].shape[2]
    by_block = group == BLOCKS and snaps == 4 and arrays[3].shape[1] == 1
    if by_block and hidden % 512 == 0 and channel // group <= 128 and channel % (16 * group) == 0:
        return per_device_blocks(*arrays)
    return per_device_modes(*arrays)


def solution(mesh):
    return jax.shard_map(
        per_device,
        mesh=mesh,
        in_specs=(
            P("snap", "sp", None, None),
            P("snap", "sp", None, None),
            P("snap", "sp", None),
            P(None, "sp"),
            P(None, "sp", None),
            P(None, "sp", None),
            P(None, "sp", None),
            P(None, "sp", None),
            P(None, "sp", None),
            P(None, "sp", None),
            P(None, "sp"),
            P(None, "sp"),
            P(None, "sp"),
            P(),
        ),
        out_specs=(
            P("snap", "sp", None, None),
            P("snap", "sp", None, None),
            P(None, "sp", None),
            P(None, "sp", None),
            P(None, "sp", None),
            P(None, "sp", None),
            P(None, "sp", None),
            P(None, "sp", None),
            P(None, "sp", None),
            P(None, "sp", None),
            P(None, "sp"),
            P(None, "sp"),
            P(None, "sp"),
            P(None, "sp"),
            P(),
        ),
        check_vma=False,
    )
```

```python
import functools
import math

import jax
import jax.numpy as jnp
import ml_dtypes
import numpy as np
from jax import lax
from jax.experimental import pallas as pl
from jax.experimental.pallas import tpu as pltpu
from jax.sharding import PartitionSpec as P

BLOCKS = 8
NVAR = 20
STEP = 10
VMEM_LIMIT = 63 * 1024 * 1024


eps_norm = 1e-06
shrink_level = 0.01
beta_one = 0.5
beta_two = 0.5
adam_eps = 1e-08
decay_rate = 0.01
rate_mlp = 0.03
rate_filter = 0.1
rate_small = 0.2
stat_decay = 0.5


def layer_norm(values, gain_vec, shift_vec):
    centred = values - jnp.mean(values, axis=-1, keepdims=True)
    spread = jnp.mean(centred * centred, axis=-1, keepdims=True)
    return centred * lax.rsqrt(spread + eps_norm) * gain_vec + shift_vec


def shrink(values):
    return values - shrink_level * jnp.tanh(values / shrink_level)


def lon_tables(lon_total, mode_total):
    places = jnp.arange(lon_total, dtype=jnp.int32)
    orders = jnp.arange(mode_total, dtype=jnp.int32)
    angles = (places[:, None] * orders[None, :] % lon_total).astype(jnp.float32) * (
        2.0 * math.pi / lon_total
    )
    scaling = 1.0 / math.sqrt(lon_total)
    forward_tab = jnp.stack([jnp.cos(angles), -jnp.sin(angles)], axis=1) * scaling
    doubling = jnp.where(orders == 0, 1.0, 2.0).astype(jnp.float32)[:, None]
    inverse_tab = (
        jnp.stack([jnp.cos(angles).T * doubling, -jnp.sin(angles).T * doubling], axis=0) * scaling
    )
    return (forward_tab.astype(jnp.bfloat16), inverse_tab.astype(jnp.bfloat16))


def lat_table(lat_total):
    places = jnp.arange(lat_total, dtype=jnp.int32)
    angles = (places[:, None] * places[None, :] % lat_total).astype(jnp.float32) * (
        2.0 * math.pi / lat_total
    )
    cosine = jnp.cos(angles)
    sine_part = jnp.sin(angles)
    upper_rows = jnp.stack([cosine, sine_part], axis=1)
    bottom = jnp.stack([-sine_part, cosine], axis=1)
    return (jnp.stack([upper_rows, bottom], axis=0) / math.sqrt(lat_total)).astype(jnp.bfloat16)


def complex_pair(real_part, imag_part):
    return jnp.stack([jnp.stack([real_part, -imag_part]), jnp.stack([imag_part, real_part])])


gelu_scale = math.sqrt(2.0 / math.pi)
gelu_cubic = 0.044715


def gelu_both(value):
    square = value * value
    bent = jnp.tanh(gelu_scale * value * (1.0 + gelu_cubic * square))
    half = 0.5 + 0.5 * bent
    slope = half + (0.5 * gelu_scale) * value * (1.0 - bent * bent) * (
        1.0 + (3.0 * gelu_cubic) * square
    )
    return value * half, slope


def dot_nt(left, right):
    return lax.dot_general(
        left, right, (((1,), (1,)), ((), ())), preferred_element_type=jnp.float32
    )


def dot_nn(left, right):
    return jnp.dot(left, right, preferred_element_type=jnp.float32)


def divisor(total, unit, most):
    return max(size for size in range(unit, most + 1, unit) if total % size == 0)


def mlp_body(
    tile,
    normed_ref,
    cot_ref,
    up_ref,
    down_ref,
    bias_ref,
    out_ref,
    back_ref,
    grad_up_ref,
    grad_down_ref,
    grad_bias_ref,
    normed_turned,
    cot_turned,
    act_ref,
    slope_ref,
):
    tokens = normed_ref.shape[0]

    @pl.when(pl.program_id(0) == 0)
    def _():
        normed_turned[...] = normed_ref[...].T
        cot_turned[...] = cot_ref[...].T
        out_ref[...] = jnp.zeros_like(out_ref)
        back_ref[...] = jnp.zeros_like(back_ref)

    grad_bias_ref[...] = jnp.zeros_like(grad_bias_ref)

    @pl.loop(0, tokens // tile)
    def _(step):
        rows = pl.ds(pl.multiple_of(step * tile, tile), tile)
        act, slope = gelu_both(dot_nn(normed_ref[rows, :], up_ref[...]) + bias_ref[...])
        act = act.astype(jnp.bfloat16)
        slope = (dot_nn(cot_ref[rows, :], down_ref[...]) * slope).astype(jnp.bfloat16)
        act_ref[rows, :] = act
        slope_ref[rows, :] = slope
        grad_bias_ref[...] += jnp.sum(slope.astype(jnp.float32), axis=0, keepdims=True)
        out_ref[rows, :] += dot_nt(act, down_ref[...])
        back_ref[rows, :] += dot_nt(slope, up_ref[...])

    grad_up_ref[...] = dot_nn(normed_turned[...], slope_ref[...]).astype(grad_up_ref.dtype)
    grad_down_ref[...] = dot_nn(cot_turned[...], act_ref[...]).astype(grad_down_ref.dtype)


def mlp_pass(normed, cot, weights, bias):
    tokens, channel = normed.shape
    hidden = weights.shape[2]
    width = divisor(hidden, 128, 512)
    tile = divisor(tokens, 16, 480)
    whole = pl.BlockSpec((tokens, channel), lambda j: (0, 0))
    block = pl.BlockSpec((channel, width), lambda j: (0, j))
    line = pl.BlockSpec((1, width), lambda j: (0, j))
    part = lambda which: pl.BlockSpec((None, channel, width), lambda j: (which, 0, j))
    total = jax.ShapeDtypeStruct((tokens, channel), jnp.float32)
    grads = jax.ShapeDtypeStruct((channel, hidden), jnp.bfloat16)
    return pl.pallas_call(
        functools.partial(mlp_body, tile),
        grid=(hidden // width,),
        in_specs=[whole, whole, part(0), part(1), line],
        out_specs=[whole, whole, block, block, line],
        out_shape=[total, total, grads, grads, jax.ShapeDtypeStruct((1, hidden), jnp.float32)],
        scratch_shapes=[
            pltpu.VMEM((channel, tokens), jnp.bfloat16),
            pltpu.VMEM((channel, tokens), jnp.bfloat16),
            pltpu.VMEM((tokens, width), jnp.bfloat16),
            pltpu.VMEM((tokens, width), jnp.bfloat16),
        ],
        compiler_params=pltpu.CompilerParams(vmem_limit_bytes=56 * 1024 * 1024),
        cost_estimate=pl.CostEstimate(
            flops=12 * tokens * channel * hidden,
            bytes_accessed=8 * channel * hidden + 12 * tokens * channel,
            transcendentals=tokens * hidden,
        ),
        name="mlp_pass",
    )(normed, cot, weights, weights, bias)


def spectral_front(arrived, lat_fwd, first_pair, second_pair, bias_one, bias_two):
    spectrum = jnp.einsum(
        "pkqr,nrqmd->nkpmd", lat_fwd, arrived, preferred_element_type=jnp.float32
    ).astype(jnp.bfloat16)
    snap_local, lat_total, pair_count, mode_local, channel = spectrum.shape
    blocked = spectrum.reshape(
        snap_local, lat_total, pair_count, mode_local, BLOCKS, channel // BLOCKS
    )
    pre_one = (
        jnp.einsum("nkqmbi,pqbio->nkpmbo", blocked, first_pair, preferred_element_type=jnp.float32)
        + bias_one
    )
    act_one = jax.nn.gelu(pre_one).astype(jnp.bfloat16)
    pre_two = (
        jnp.einsum("nkqmbi,pqbio->nkpmbo", act_one, second_pair, preferred_element_type=jnp.float32)
        + bias_two
    )
    return (blocked, pre_one, act_one, pre_two)


def adamw(master, first_mom, second_mom, gradient, step_rate):
    first_next = beta_one * first_mom + (1.0 - beta_one) * gradient
    second_next = beta_two * second_mom + (1.0 - beta_two) * gradient * gradient
    fix_one = 1.0 - beta_one**STEP
    fix_two = 1.0 - beta_two**STEP
    direction = first_next / fix_one / (jnp.sqrt(second_next / fix_two) + adam_eps)
    master_next = master - step_rate * (direction + decay_rate * master)
    return (master_next, first_next, second_next, master_next.astype(jnp.bfloat16))


def per_device_modes(
    fields,
    cotangent,
    valid_mask,
    kept_modes,
    mlp_master,
    mlp_first,
    mlp_second,
    filter_master,
    filter_first,
    filter_second,
    small_master,
    small_first,
    small_second,
    run_stats,
):
    group_size = lax.axis_size("sp")
    snap_local, row_local, lon_total, channel = fields.shape
    lat_total = row_local * group_size
    mode_local = kept_modes.shape[1]
    mode_total = mode_local * group_size
    block_width = channel // BLOCKS
    lon_fwd, lon_inv = lon_tables(lon_total, mode_total)
    lat_fwd = lat_table(lat_total)
    mlp_w, filt_w, small_w = (
        lax.all_gather(mlp_master.astype(jnp.bfloat16), "sp", axis=1, tiled=True),
        lax.all_gather(filter_master.astype(jnp.bfloat16), "sp", axis=1, tiled=True),
        lax.all_gather(small_master.astype(jnp.bfloat16), "sp", axis=1, tiled=True),
    )
    small_f = small_w.astype(jnp.float32)
    weights = filt_w.reshape(4, BLOCKS, block_width, block_width)
    first_pair = complex_pair(weights[0], weights[1])
    second_pair = complex_pair(weights[2], weights[3])
    bias_one = small_f[4:6].reshape(2, 1, BLOCKS, block_width)
    bias_two = small_f[6:8].reshape(2, 1, BLOCKS, block_width)
    fields_float = fields.astype(jnp.float32)
    normed, norm_pull = jax.vjp(layer_norm, fields_float, small_f[0], small_f[1])
    normed_low = normed.astype(jnp.bfloat16)
    spec_lon = jnp.einsum(
        "nrld,lqm->nrqmd", normed_low, lon_fwd, preferred_element_type=jnp.float32
    ).astype(jnp.bfloat16)
    arrived = lax.all_to_all(spec_lon, "sp", split_axis=3, concat_axis=1, tiled=True)
    spectral = spectral_front(arrived, lat_fwd, first_pair, second_pair, bias_one, bias_two)
    keep_mask = kept_modes.astype(jnp.float32)[None, :, None, :, None, None]
    masked = (shrink(spectral[3]) * keep_mask).astype(jnp.bfloat16)
    masked = masked.reshape(snap_local, lat_total, 2, mode_local, channel)
    returned = jnp.einsum(
        "pkqr,nkpmd->nrqmd", lat_fwd, masked, preferred_element_type=jnp.float32
    ).astype(jnp.bfloat16)
    home_modes = lax.all_to_all(returned, "sp", split_axis=1, concat_axis=3, tiled=True)
    filtered = jnp.einsum(
        "nrqmd,qml->nrld", home_modes, lon_inv, preferred_element_type=jnp.float32
    )
    mixture = fields_float + normed + filtered
    normed_two, norm_two_pull = jax.vjp(layer_norm, mixture, small_f[2], small_f[3])
    normed_two_low = normed_two.astype(jnp.bfloat16)
    tokens = snap_local * row_local * lon_total
    passed = mlp_pass(
        normed_two_low.reshape(tokens, channel),
        cotangent.reshape(tokens, channel),
        mlp_w,
        small_f[9:].reshape(1, -1),
    )
    output = mixture + passed[0].reshape(mixture.shape) + small_f[8]
    weight_mask = valid_mask.astype(jnp.float32)[..., None]
    variables = output[..., :NVAR]
    local_sums = jnp.stack(
        [
            jnp.sum(weight_mask * variables, axis=(0, 1, 2)),
            jnp.sum(weight_mask * variables * variables, axis=(0, 1, 2)),
        ]
    )
    total_sums = lax.psum(local_sums, ("snap", "sp"))
    positions = snap_local * lax.axis_size("snap") * lat_total * lon_total
    stats_new = stat_decay * run_stats + (1.0 - stat_decay) * total_sums / positions
    cot_float = cotangent.astype(jnp.float32)
    grad_normed_two = passed[1].reshape(mixture.shape)
    grad_bias_hidden = passed[4]
    grad_mix_norm, grad_gain_two, grad_shift_two = norm_two_pull(grad_normed_two)
    grad_mixture = cot_float + grad_mix_norm
    grad_bias_out = jnp.sum(cot_float, axis=(0, 1, 2))
    grad_filtered = grad_mixture.astype(jnp.bfloat16)
    grad_home = jnp.einsum(
        "nrld,qml->nrqmd", grad_filtered, lon_inv, preferred_element_type=jnp.float32
    ).astype(jnp.bfloat16)
    grad_returned = lax.all_to_all(grad_home, "sp", split_axis=3, concat_axis=1, tiled=True)
    grad_masked = jnp.einsum(
        "pkqr,nrqmd->nkpmd", lat_fwd, grad_returned, preferred_element_type=jnp.float32
    )
    arrived_again = lax.all_to_all(spec_lon, "sp", split_axis=3, concat_axis=1, tiled=True)
    used_front = spectral_front(arrived_again, lat_fwd, first_pair, second_pair, bias_one, bias_two)
    blocked, pre_one, act_one, pre_two = used_front
    grad_two = jax.vjp(shrink, pre_two)[1](grad_masked.reshape(pre_two.shape) * keep_mask)[
        0
    ].astype(jnp.bfloat16)
    grad_bias_two = jnp.sum(grad_two.astype(jnp.float32), axis=(0, 1, 3))
    grad_second = jnp.einsum(
        "nkqmbi,nkpmbo->pqbio", act_one, grad_two, preferred_element_type=jnp.float32
    )
    grad_act = jnp.einsum(
        "nkpmbo,pqbio->nkqmbi", grad_two, second_pair, preferred_element_type=jnp.float32
    )
    grad_one = jax.vjp(jax.nn.gelu, pre_one)[1](grad_act)[0].astype(jnp.bfloat16)
    grad_bias_one = jnp.sum(grad_one.astype(jnp.float32), axis=(0, 1, 3))
    grad_first = jnp.einsum(
        "nkqmbi,nkpmbo->pqbio", blocked, grad_one, preferred_element_type=jnp.float32
    )
    grad_spectrum = jnp.einsum(
        "nkpmbo,pqbio->nkqmbi", grad_one, first_pair, preferred_element_type=jnp.float32
    ).astype(jnp.bfloat16)
    grad_spectrum = grad_spectrum.reshape(snap_local, lat_total, 2, mode_local, channel)
    grad_lon = jnp.einsum(
        "pkqr,nkpmd->nrqmd", lat_fwd, grad_spectrum, preferred_element_type=jnp.float32
    ).astype(jnp.bfloat16)
    grad_rows = lax.all_to_all(grad_lon, "sp", split_axis=1, concat_axis=3, tiled=True)
    grad_normed = grad_mixture + jnp.einsum(
        "nrqmd,lqm->nrld", grad_rows, lon_fwd, preferred_element_type=jnp.float32
    )
    grad_field_norm, grad_gain_one, grad_shift_one = norm_pull(grad_normed)
    input_grad = grad_mixture + grad_field_norm
    grad_filter = jnp.stack(
        [
            grad_first[0, 0] + grad_first[1, 1],
            grad_first[1, 0] - grad_first[0, 1],
            grad_second[0, 0] + grad_second[1, 1],
            grad_second[1, 0] - grad_second[0, 1],
        ]
    ).reshape(4, channel, block_width)
    grad_small = jnp.concatenate(
        [
            jnp.stack([grad_gain_one, grad_shift_one, grad_gain_two, grad_shift_two]),
            grad_bias_one.reshape(2, channel),
            grad_bias_two.reshape(2, channel),
            grad_bias_out[None, :],
            grad_bias_hidden.reshape(-1, channel),
        ],
        axis=0,
    )
    shares = (
        jnp.stack([
            lax.psum_scatter(part, "sp", scatter_dimension=0, tiled=True) for part in passed[2:4]
        ]),
        lax.psum_scatter(grad_filter, "sp", scatter_dimension=1, tiled=True),
        lax.psum_scatter(grad_small, "sp", scatter_dimension=1, tiled=True),
    )
    owned = (
        lax.psum(shares[0].astype(jnp.bfloat16), "snap").astype(jnp.float32),
        lax.psum(shares[1].astype(jnp.bfloat16), "snap").astype(jnp.float32),
        lax.psum(shares[2].astype(jnp.bfloat16), "snap").astype(jnp.float32),
    )
    mlp_new, mlp_first_new, mlp_second_new, mlp_copy = adamw(
        mlp_master, mlp_first, mlp_second, owned[0], rate_mlp
    )
    filter_new, filter_first_new, filter_second_new, filter_copy = adamw(
        filter_master, filter_first, filter_second, owned[1], rate_filter
    )
    small_new, small_first_new, small_second_new, small_copy = adamw(
        small_master, small_first, small_second, owned[2], rate_small
    )
    return (
        output.astype(jnp.bfloat16),
        input_grad,
        mlp_new,
        mlp_first_new,
        mlp_second_new,
        mlp_copy,
        filter_new,
        filter_first_new,
        filter_second_new,
        filter_copy,
        small_new,
        small_first_new,
        small_second_new,
        small_copy,
        stats_new,
    )


def lon_matrix(lon_total, mode_total, snaps, rows):
    places = np.arange(lon_total)
    orders = np.arange(mode_total)
    angles = (places[:, None] * orders[None, :] % lon_total) * (2.0 * math.pi / lon_total)
    doubling = np.where(orders == 0, 1.0, 2.0)
    scaling = 1.0 / math.sqrt(lon_total)
    forward = np.stack([np.cos(angles), -np.sin(angles)], axis=1) * scaling
    inverse = forward * doubling

    def spread(table):
        table = np.einsum(
            "ab,lx,rs->alrbsx", np.eye(snaps), table.reshape(lon_total, -1), np.eye(rows)
        )
        return table.reshape(snaps * lon_total * rows, -1).astype(ml_dtypes.bfloat16)

    return spread(forward), spread(inverse)


def lon_turn(lon_total, rows):
    turn = np.einsum("lk,rs->rlks", np.eye(lon_total), np.eye(rows))
    return turn.reshape(rows, lon_total, lon_total * rows).astype(ml_dtypes.bfloat16)


def lat_matrix(lat_total, mode_total):
    places = np.arange(lat_total)
    angles = (places[:, None] * places[None, :] % lat_total) * (2.0 * math.pi / lat_total)
    cosine, sine = np.cos(angles), np.sin(angles)
    table = np.stack([np.stack([cosine, sine], axis=1), np.stack([-sine, cosine], axis=1)])
    table = np.einsum("pkqr,ab->pakrqb", table / math.sqrt(lat_total), np.eye(mode_total))
    size = 2 * lat_total * mode_total
    return table.reshape(size, size).astype(ml_dtypes.bfloat16)


class Refs:
    pass


def block_body(names, sizes, *refs):
    g = Refs()
    for name, ref in zip(names, refs, strict=True):
        setattr(g, name, ref)
    snaps, group, parts, width = sizes
    levels = group // 2
    tokens = g.fields.shape[0] * g.fields.shape[1]
    channel = g.fields.shape[2]
    tiles = channel // 128
    owned = channel // group
    half = width // 2
    quarter = width // snaps
    tile = divisor(tokens, 16, 480)
    strip = divisor(tokens, 16, 96)
    low = jnp.bfloat16
    f32 = jnp.float32

    me_snap = lax.axis_index("snap")
    me_sp = lax.axis_index("sp")
    core = lax.rem(me_sp, 2)
    level = me_sp // 2

    def at(snap, sp):
        return {"snap": snap, "sp": sp}

    def sp_after(step):
        return lax.rem(me_sp + step, group)

    def sp_before(step):
        return lax.rem(me_sp + group - step, group)

    def snap_after(step):
        return lax.rem(me_snap + step, snaps)

    def snap_before(step):
        return lax.rem(me_snap + snaps - step, snaps)

    def level_after(step):
        return lax.rem(level + step, levels)

    def level_before(step):
        return lax.rem(level + levels - step, levels)

    other_core = at(me_snap, me_sp + 1 - 2 * core)

    def send(src, dst, sems, index, target):
        return pltpu.make_async_remote_copy(
            src_ref=src,
            dst_ref=dst,
            send_sem=sems[0].at[index],
            recv_sem=sems[1].at[index],
            device_id=target,
            device_id_type=pl.DeviceIdType.MESH,
        )

    def strips(body):
        @pl.loop(0, tokens // strip)
        def _(step):
            body(pl.ds(pl.multiple_of(step * strip, strip), strip))

    def columns(name):
        ref = getattr(g, name)
        return ref.reshape(tiles, ref.shape[1] * ref.shape[2], 128)

    def columns_of(name, rows):
        view = columns(name)
        return jnp.concatenate([view[tile_at, rows, :] for tile_at in range(tiles)], axis=1)

    def store_columns(name, rows, value):
        view = columns(name)
        for tile_at in range(tiles):
            view[tile_at, rows, :] = value[:, tile_at * 128 : (tile_at + 1) * 128]

    def column_copies(near, far, sems, out):
        copies = []
        for tile_at in range(tiles):
            ends = [near.at[tile_at], far.at[:, :, tile_at * 128 : (tile_at + 1) * 128]]
            if not out:
                ends.reverse()
            copies.append(pltpu.make_async_copy(*ends, sems.at[tile_at]))
        return copies

    loads = {}

    def load(name, index):
        copy = pltpu.make_async_copy(getattr(g, name), getattr(g, name + "_in"), g.load_sem.at[index])
        copy.start()
        loads[name] = copy

    for index, name in enumerate(
        [name for name in names[: names.index("out")] if name not in ("mlp", "fields", "cot")]
    ):
        load(name, index)
    fields_load = column_copies(g.fields_cols, g.fields, g.fields_sem, False)
    cot_load = column_copies(g.cot_cols, g.cot, g.cot_sem, False)
    for copy in fields_load + cot_load:
        copy.start()

    def master_load(part):
        return pltpu.make_async_copy(
            g.mlp.at[:, :, part * width : (part + 1) * width],
            g.mlp_part.at[part % 2],
            g.load_sem.at[len(loads) + part % 2],
        )

    master_load(0).start()
    master_load(1).start()

    barrier = pltpu.get_barrier_semaphore()
    peers = [at(me_snap, sp_after(step)) for step in range(1, group)]
    peers += [at(snap_after(step), me_sp) for step in range(1, snaps)]
    for peer in peers:
        pl.semaphore_signal(
            barrier, inc=1, device_id=peer, device_id_type=pl.DeviceIdType.MESH
        )

    loads["small"].wait()
    loads["kept"].wait()
    g.own_small[...] = jnp.zeros_like(g.own_small)
    rows_small = g.small.shape[0]
    g.own_small[0:rows_small, 0:owned] = g.small_in[...].astype(low).astype(f32)
    pairs_kept = g.kept.shape[1]
    lines = lax.broadcasted_iota(jnp.int32, (pairs_kept, pairs_kept), 0)
    places = lax.broadcasted_iota(jnp.int32, (pairs_kept, pairs_kept), 1)
    kept = jnp.where(lines == places, g.kept_in[...].astype(f32), 0.0)
    g.own_small[16:, :] = jnp.broadcast_to(
        jnp.sum(kept, axis=1, keepdims=True), (pairs_kept, g.own_small.shape[1])
    )
    pl.semaphore_wait(barrier, len(peers))

    def small_copy(step):
        return send(
            g.own_small, g.all_small.at[me_sp], (g.small_s, g.small_r), step, at(me_snap, sp_after(step))
        )

    for step in range(1, group):
        small_copy(step).start()
    g.all_small[me_sp] = g.own_small[...]

    snap_low = lax.rem(me_snap, 2)
    snap_high = me_snap // 2
    beside_low = me_snap + 1 - 2 * snap_low
    beside_high = me_snap + 2 - 4 * snap_high

    def own_quarter(part):
        odd = lax.rem(part, 2)
        return (1 - odd) * me_snap + odd * (2 * snap_low + snap_high)

    def quarter_cols(part):
        return pl.ds(pl.multiple_of(own_quarter(part) * quarter, quarter), quarter)

    def half_cols(part):
        return pl.ds(pl.multiple_of((own_quarter(part) // 2) * half, half), half)

    def own_rows(sp):
        return pl.ds(pl.multiple_of(sp * owned, owned), owned)

    def first_copy(part, step):
        target = sp_after(step)
        matrix = lax.rem(target, 2)
        cols = quarter_cols(part)
        return send(
            g.own_w.at[part, matrix, :, cols],
            g.all_w.at[part, matrix, own_rows(me_sp), cols],
            (g.first_s, g.first_r),
            (part, step),
            at(me_snap, target),
        )

    def first_local(part):
        cols = quarter_cols(part)
        return pltpu.make_async_copy(
            g.own_w.at[part, core, :, cols],
            g.all_w.at[part, core, own_rows(me_sp), cols],
            g.first_s.at[part, 0],
        )

    def second_copy(part):
        odd = lax.rem(part, 2)
        view = g.all_w.at[part, core, :, quarter_cols(part)]
        target = at((1 - odd) * beside_low + odd * beside_high, me_sp)
        return send(view, view, (g.second_s, g.second_r), part, target)

    def third_copy(part):
        odd = lax.rem(part, 2)
        view = g.all_w.at[part, core, :, half_cols(part)]
        target = at((1 - odd) * beside_high + odd * beside_low, me_sp)
        return send(view, view, (g.third_s, g.third_r), part, target)

    def fourth_copy(part):
        view = g.all_w.at[part, core]
        return send(view, view, (g.fourth_s, g.fourth_r), part, other_core)

    def start_first(part):
        for step in range(1, group):
            first_copy(part, step).start()
        first_local(part).start()

    def pass_second(part):
        for step in range(1, group):
            first_copy(part, step).wait_recv()
        first_local(part).wait()
        second_copy(part).start()

    def pass_third(part):
        second_copy(part).wait_recv()
        third_copy(part).start()

    def pass_fourth(part):
        third_copy(part).wait_recv()
        fourth_copy(part).start()

    for part in range(parts):
        master_load(part).wait()
        g.own_w[part] = g.mlp_part[part % 2].astype(low)
        if part + 2 < parts:
            master_load(part + 2).start()
        if part < 2:
            start_first(part)

    for copy in fields_load:
        copy.wait()

    def first_unit(rows):
        values = columns_of("fields_cols", rows).astype(f32)
        centred = values - jnp.mean(values, axis=-1, keepdims=True)
        scale = lax.rsqrt(jnp.mean(centred * centred, axis=-1, keepdims=True) + eps_norm)
        g.scale_one[rows, :] = scale
        g.grid[rows, :] = centred * scale

    strips(first_unit)
    for step in range(1, group):
        small_copy(step).wait_recv()
    for sp in range(group):
        g.gains[:, sp * owned : (sp + 1) * owned] = g.all_small[sp, 0:16, 0:owned]
        g.keep[sp * pairs_kept : (sp + 1) * pairs_kept, :] = g.all_small[sp, 16:, :]

    def first_norm(rows):
        unit = g.grid[rows, :]
        normed = unit * g.gains[0:1, :] + g.gains[1:2, :]
        g.unit_one[rows, :] = unit.astype(low)
        g.normed[rows, :] = normed.astype(low)
        g.grid[rows, :] = columns_of("fields_cols", rows).astype(f32) + normed

    strips(first_norm)

    def to_blocks(table, which):
        modes = dot_nn(table, g.normed[...])
        for block in range(group):
            cut = modes[:, block * owned : (block + 1) * owned]
            cut = jnp.concatenate(
                [cut, jnp.zeros((cut.shape[0], 128 - owned), f32)], axis=1
            )
            g.modes[block] = cut.astype(low).reshape(g.modes.shape[1:])
        for step in range(1, group):
            block_copy(which, step).start()
        g.arrived[:, mode_rows(me_sp), :] = g.modes[me_sp]

    def mode_rows(sp):
        size = g.modes.shape[2]
        return pl.ds(pl.multiple_of(sp * size, size), size)

    def block_copy(which, step):
        target = sp_after(step)
        return send(
            g.modes.at[target],
            g.arrived.at[:, mode_rows(me_sp), :],
            (g.block_s, g.block_r),
            (which, step),
            at(me_snap, target),
        )

    def row_copy(which, step):
        target = sp_after(step)
        return send(
            g.turned.at[:, mode_rows(target), :],
            g.home.at[me_sp],
            (g.row_s, g.row_r),
            (which, step),
            at(me_snap, target),
        )

    def to_rows(which):
        for step in range(1, group):
            row_copy(which, step).start()
        g.home[me_sp] = g.turned[:, mode_rows(me_sp), :]

    def home_modes(which):
        for step in range(1, group):
            row_copy(which, step).wait_recv()
        for block in range(group):
            g.gathered[:, block * owned : (block + 1) * owned] = (
                g.home[block].reshape(g.gathered.shape[0], 128)[:, 0:owned].astype(f32)
            )
        return g.gathered[...].astype(low)

    loads["lon_f"].wait()
    to_blocks(g.lon_f_in[...], 0)
    for part in range(2, 4):
        start_first(part)

    loads["filt"].wait()
    for weight, first in ((g.weight_one, 0), (g.weight_two, 2)):
        weight[...] = jnp.zeros_like(weight)
        real = g.filt_in[first].astype(low)
        imag = g.filt_in[first + 1].astype(low)
        weight[0:owned, 0:owned] = real
        weight[128 : 128 + owned, 128 : 128 + owned] = real
        weight[0:owned, 128 : 128 + owned] = imag
        weight[128 : 128 + owned, 0:owned] = -imag

    def bias_row(first):
        return jnp.concatenate(
            [g.own_small[first : first + 1, :], g.own_small[first + 1 : first + 2, :]], axis=1
        )

    loads["lat_f"].wait()
    loads["lat_b"].wait()
    for step in range(1, group):
        block_copy(0, step).wait_recv()
    snap_local = g.arrived.shape[0]
    pairs = g.arrived.shape[1] // 2

    def spectra(out, kind):
        for snap in range(snap_local):
            spectrum = dot_nn(g.lat_f_in[...], g.arrived[snap]).astype(kind)
            rows = slice(snap * pairs, (snap + 1) * pairs)
            out[rows, 0:128] = spectrum[0:pairs]
            out[rows, 128:256] = spectrum[pairs:]

    def grids(values):
        for snap in range(snap_local):
            rows = values[snap * pairs : (snap + 1) * pairs]
            rows = jnp.concatenate([rows[:, 0:128], rows[:, 128:256]], axis=0)
            g.turned[snap] = dot_nn(g.lat_b_in[...], rows).astype(low)

    def keep_all():
        keep = jnp.concatenate([g.keep[...], g.keep[...]], axis=1)
        return jnp.concatenate([keep] * snap_local, axis=0)

    spectra(g.spectrum, low)
    g.pre_one[...] = dot_nn(g.spectrum[...], g.weight_one[...]) + bias_row(4)
    g.act_one[...] = gelu_both(g.pre_one[...])[0].astype(low)
    g.pre_two[...] = dot_nn(g.act_one[...], g.weight_two[...]) + bias_row(6)
    grids((shrink(g.pre_two[...]) * keep_all()).astype(low))
    to_rows(0)

    for part in range(2):
        pass_second(part)
    for part in range(4, parts):
        start_first(part)
    for copy in cot_load:
        copy.wait()

    def flat_cot(rows):
        g.cot_in[rows, :] = columns_of("cot_cols", rows)

    strips(flat_cot)
    g.cot_turned[...] = g.cot_in[...].T
    for part in range(2):
        pass_third(part)

    loads["lon_i"].wait()
    g.home_low[...] = home_modes(0)

    def add_filtered(rows):
        g.grid[rows, :] += dot_nn(g.lon_i_in[rows, :], g.home_low[...])

    def second_norm(rows):
        values = g.grid[rows, :]
        centred = values - jnp.mean(values, axis=-1, keepdims=True)
        scale = lax.rsqrt(jnp.mean(centred * centred, axis=-1, keepdims=True) + eps_norm)
        centred = centred * scale
        g.unit_two[rows, :] = centred.astype(low)
        g.scale_two[rows, :] = scale
        g.normed[rows, :] = (centred * g.gains[2:3, :] + g.gains[3:4, :]).astype(low)
        g.grid[rows, :] = values + g.gains[8:9, :]
        g.back[rows, :] = jnp.zeros((strip, channel), f32)

    add_filtered(slice(0, tokens))
    for part in range(2, 4):
        pass_second(part)
    pass_fourth(0)
    strips(second_norm)
    pass_fourth(1)
    for part in range(2, 4):
        pass_third(part)
    g.normed_turned[...] = g.normed[...].T
    for part in range(parts):
        flat = jnp.concatenate([g.gains[9 + row : 10 + row, :] for row in range(rows_small - 9)], axis=1)
        g.bias[part] = flat[:, part * width : (part + 1) * width]

    def core_copy(part, matrix):
        slot = lax.rem(part, 2)
        return send(
            g.grads.at[slot, matrix, :, 1 - core],
            g.core_got.at[slot, matrix],
            (g.core_s, g.core_r),
            (slot, matrix),
            other_core,
        )

    places_one = (snap_low, snap_high)
    places_two = (snap_high, snap_low)
    beside_one = (beside_low, beside_high)
    beside_two = (beside_high, beside_low)
    place_last = (2 * snap_low + snap_high, me_snap)

    def half_copy(part, matrix):
        slot = lax.rem(part, 2)
        return send(
            g.half_out.at[slot, matrix, 1 - places_one[matrix]],
            g.half_got.at[slot, matrix],
            (g.half_s, g.half_r),
            (slot, matrix),
            at(beside_one[matrix], me_sp),
        )

    def quarter_copy(part, matrix):
        slot = lax.rem(part, 2)
        return send(
            g.quarter_out.at[slot, matrix, 1 - places_two[matrix]],
            g.quarter_got.at[slot, matrix],
            (g.quarter_s, g.quarter_r),
            (slot, matrix),
            at(beside_two[matrix], me_sp),
        )

    def level_copy(part, step):
        slot = lax.rem(part, 2)
        target = level_after(step)
        return send(
            g.level_out.at[slot, target],
            g.level_got.at[slot, level],
            (g.level_s, g.level_r),
            (slot, step),
            at(me_snap, 2 * target + core),
        )

    def last_copy(part, matrix, step):
        view = g.total.at[part, place_last[matrix], matrix]
        return send(
            view, view, (g.last_s, g.last_r), (part, matrix, step), at(snap_after(step), me_sp)
        )

    def half_stage(part):
        slot = lax.rem(part, 2)
        for matrix in range(2):

            @pl.when(part >= 2)
            def _(matrix=matrix):
                half_copy(part - 2, matrix).wait_send()

            core_copy(part, matrix).wait_recv()
            for row in range(levels):
                both = g.grads[slot, matrix, row, core].astype(f32) + g.core_got[
                    slot, matrix, row
                ].astype(f32)
                both = both.astype(low)
                g.half_out[slot, matrix, 0, row] = both[:, 0:half]
                g.half_out[slot, matrix, 1, row] = both[:, half:width]
            half_copy(part, matrix).start()

    def quarter_stage(part):
        slot = lax.rem(part, 2)
        for matrix in range(2):

            @pl.when(part >= 2)
            def _(matrix=matrix):
                quarter_copy(part - 2, matrix).wait_send()

            half_copy(part, matrix).wait_recv()
            for row in range(levels):
                both = g.half_out[slot, matrix, places_one[matrix], row].astype(f32) + g.half_got[
                    slot, matrix, row
                ].astype(f32)
                both = both.astype(low)
                g.quarter_out[slot, matrix, 0, row] = both[:, 0:quarter]
                g.quarter_out[slot, matrix, 1, row] = both[:, quarter:half]
            quarter_copy(part, matrix).start()

    def level_stage(part):
        slot = lax.rem(part, 2)

        @pl.when(part >= 2)
        def _():
            for step in range(1, levels):
                level_copy(part - 2, step).wait_send()

        for matrix in range(2):
            quarter_copy(part, matrix).wait_recv()
            for row in range(levels):
                both = g.quarter_out[slot, matrix, places_two[matrix], row].astype(
                    f32
                ) + g.quarter_got[slot, matrix, row].astype(f32)
                g.level_out[slot, row, matrix] = both.astype(low)
        for step in range(1, levels):
            level_copy(part, step).start()

    def last_stage(part):
        slot = lax.rem(part, 2)
        for step in range(1, levels):
            level_copy(part, step).wait_recv()
        for matrix in range(2):
            sums = g.level_out[slot, level, matrix].astype(f32)
            for step in range(1, levels):
                sums += g.level_got[slot, level_before(step), matrix].astype(f32)
            g.total[part, place_last[matrix], matrix] = sums.astype(low)
            for step in range(1, snaps):
                last_copy(part, matrix, step).start()

    @pl.loop(0, parts)
    def _(part):
        slot = lax.rem(part, 2)

        @pl.when(part >= 3)
        def _():
            level_stage(part - 3)

        @pl.when(part + 4 < parts)
        def _():
            pass_second(part + 4)

        fourth_copy(part).wait_recv()
        g.grad_bias[part] = jnp.zeros(g.grad_bias.shape[1:], f32)

        @pl.loop(0, tokens // tile)
        def _(step):
            rows = pl.ds(pl.multiple_of(step * tile, tile), tile)
            act, slope = gelu_both(dot_nn(g.normed[rows, :], g.all_w[part, 0]) + g.bias[part])
            act = act.astype(low)
            slope = (dot_nn(g.cot_in[rows, :], g.all_w[part, 1]) * slope).astype(low)
            g.act[rows, :] = act
            g.slope[rows, :] = slope
            g.grad_bias[part] += jnp.sum(slope.astype(f32), axis=0, keepdims=True)
            g.grid[rows, :] += dot_nt(act, g.all_w[part, 1])
            g.back[rows, :] += dot_nt(slope, g.all_w[part, 0])

        @pl.when(part + 2 < parts)
        def _():
            pass_fourth(part + 2)

        @pl.when(part + 4 < parts)
        def _():
            pass_third(part + 4)

        @pl.when(part >= 3)
        def _():
            last_stage(part - 3)

        @pl.when(part >= 2)
        def _():
            quarter_stage(part - 2)

        @pl.when(part >= 1)
        def _():
            half_stage(part - 1)

        @pl.when(part >= 2)
        def _():
            for matrix in range(2):
                core_copy(part - 2, matrix).wait_send()

        shape = g.grads.shape[2:]
        g.grads[slot, 0] = dot_nn(g.normed_turned[...], g.slope[...]).astype(low).reshape(shape)
        core_copy(part, 0).start()
        g.grads[slot, 1] = dot_nn(g.cot_turned[...], g.act[...]).astype(low).reshape(shape)
        core_copy(part, 1).start()

    level_stage(parts - 3)

    def low_out(rows):
        store_columns("fields_cols", rows, g.grid[rows, :].astype(low))

    strips(low_out)
    out_copies = column_copies(g.fields_cols, g.out, g.fields_sem, True)
    for copy in out_copies:
        copy.start()
    loads["valid"].wait()
    loads["turn"].wait()
    weigh = sum(
        dot_nn(g.valid_in[:, row, :].astype(f32).astype(low), g.turn_in[row])
        for row in range(g.valid.shape[1])
    )
    places_each = weigh.shape[1]
    precise = lax.Precision.HIGHEST
    sums = [jnp.zeros((1, 128), f32), jnp.zeros((1, 128), f32)]
    for snap in range(g.valid.shape[0]):
        variables = g.grid[snap * places_each : (snap + 1) * places_each, 0:128]
        for index, value in enumerate((variables, variables * variables)):
            sums[index] += jnp.dot(
                weigh[snap : snap + 1, :], value, precision=precise, preferred_element_type=f32
            )

    g.grad_rows[...] = jnp.zeros_like(g.grad_rows)

    def second_back(rows):
        grad = g.back[rows, :]
        unit = g.unit_two[rows, :].astype(f32)
        cot = g.cot_in[rows, :].astype(f32)
        pulled = grad * g.gains[2:3, :]
        middle = jnp.mean(pulled, axis=-1, keepdims=True)
        slant = jnp.mean(pulled * unit, axis=-1, keepdims=True)
        total = cot + g.scale_two[rows, :] * (pulled - middle - unit * slant)
        g.back[rows, :] = total
        g.normed[rows, :] = total.astype(low)
        g.grad_rows[2:3, :] += jnp.sum(grad * unit, axis=0, keepdims=True)
        g.grad_rows[3:4, :] += jnp.sum(grad, axis=0, keepdims=True)
        g.grad_rows[8:9, :] += jnp.sum(cot, axis=0, keepdims=True)

    strips(second_back)
    loads["lon_it"].wait()
    for step in range(1, group):
        block_copy(0, step).wait_send()
    to_blocks(g.lon_it_in[...], 1)

    last_stage(parts - 3)
    quarter_stage(parts - 2)
    half_stage(parts - 1)

    for step in range(1, group):
        block_copy(1, step).wait_recv()
    spectra(g.grad_two, f32)
    bend = jnp.tanh(g.pre_two[...] / shrink_level)
    grad_two = (g.grad_two[...] * keep_all() * (bend * bend)).astype(low)

    def dot_tn(left, right):
        return lax.dot_general(
            left, right, (((0,), (0,)), ((), ())), preferred_element_type=f32
        )

    def filter_rows(first, grad):
        g.pair_grad[...] = grad
        real = g.pair_grad[0:128, 0:128] + g.pair_grad[128:256, 128:256]
        imag = g.pair_grad[0:128, 128:256] - g.pair_grad[128:256, 0:128]
        g.filt_out[me_snap, first] = real[0:owned].astype(low)
        g.filt_out[me_snap, first + 1] = imag[0:owned].astype(low)

    bias_two = jnp.sum(grad_two.astype(f32), axis=0, keepdims=True)
    filter_rows(2, dot_tn(g.act_one[...], grad_two))
    grad_one = dot_nt(grad_two, g.weight_two[...])
    grad_one = (grad_one * gelu_both(g.pre_one[...])[1]).astype(low)
    bias_one = jnp.sum(grad_one.astype(f32), axis=0, keepdims=True)
    for step in range(1, group):
        row_copy(0, step).wait_send()
    grids(dot_nt(grad_one, g.weight_one[...]).astype(low))
    to_rows(1)
    level_stage(parts - 2)
    quarter_stage(parts - 1)
    filter_rows(0, dot_tn(g.spectrum[...], grad_one))

    def filter_copy(step):
        view = g.filt_out.at[me_snap]
        return send(view, view, (g.filt_s, g.filt_r), step, at(snap_after(step), me_sp))

    for step in range(1, snaps):
        filter_copy(step).start()

    last_stage(parts - 2)
    level_stage(parts - 1)

    loads["lon_ft"].wait()
    g.home_low[...] = home_modes(1)

    def add_modes(rows):
        g.grid[rows, :] = g.back[rows, :] + dot_nn(g.lon_ft_in[rows, :], g.home_low[...])

    add_modes(slice(0, tokens))
    piece = g.grad_cols_0.shape[1] * g.grad_cols_0.shape[2]
    grad_copies = []
    for index in range(tokens // piece):
        name = "grad_cols_" + str(index % 2)
        if index >= 2:
            for copy in grad_copies[index - 2]:
                copy.wait()

        @pl.loop(0, piece // strip)
        def _(step):
            near = pl.ds(pl.multiple_of(step * strip, strip), strip)
            rows = pl.ds(pl.multiple_of(index * piece + step * strip, strip), strip)
            grad = g.grid[rows, :]
            unit = g.unit_one[rows, :].astype(f32)
            pulled = grad * g.gains[0:1, :]
            middle = jnp.mean(pulled, axis=-1, keepdims=True)
            slant = jnp.mean(pulled * unit, axis=-1, keepdims=True)
            total = g.back[rows, :] + g.scale_one[rows, :] * (pulled - middle - unit * slant)
            store_columns(name, near, total)
            g.grad_rows[0:1, :] += jnp.sum(grad * unit, axis=0, keepdims=True)
            g.grad_rows[1:2, :] += jnp.sum(grad, axis=0, keepdims=True)

        pairs_out = pl.ds(index * (piece // g.fields.shape[1]), piece // g.fields.shape[1])
        grad_copies.append(
            column_copies(
                getattr(g, name), g.in_grad.at[pairs_out], g.grad_sem.at[index % 2], True
            )
        )
        for copy in grad_copies[index]:
            copy.start()

    flat = jnp.concatenate([g.grad_bias[part] for part in range(parts)], axis=1)
    for row in range(rows_small - 9):
        g.grad_rows[9 + row : 10 + row, :] = flat[:, row * channel : (row + 1) * channel]
    for block in range(group):
        g.tiles[block] = jnp.zeros(g.tiles.shape[1:], f32)
        g.tiles[block, :, 0:owned] = g.grad_rows[:, block * owned : (block + 1) * owned]
        g.tiles[block, 13:14, :] = sums[0]
        g.tiles[block, 14:15, :] = sums[1]

    def tile_copy(step):
        target = sp_after(step)
        return send(
            g.tiles.at[target], g.tiles_got.at[me_sp], (g.tile_s, g.tile_r), step, at(me_snap, target)
        )

    def snap_tile_copy(step):
        view = g.snap_tiles.at[me_snap]
        return send(view, view, (g.snap_tile_s, g.snap_tile_r), step, at(snap_after(step), me_sp))

    for step in range(1, group):
        tile_copy(step).start()
    last_stage(parts - 1)

    g.tiles_got[me_sp] = g.tiles[me_sp]
    for step in range(1, group):
        tile_copy(step).wait_recv()
    tile_sum = g.tiles_got[0]
    for sp in range(1, group):
        tile_sum += g.tiles_got[sp]
    g.snap_tiles[me_snap] = tile_sum
    g.snap_tiles[me_snap, 4:5, :] = bias_one[:, 0:128]
    g.snap_tiles[me_snap, 5:6, :] = bias_one[:, 128:256]
    g.snap_tiles[me_snap, 6:7, :] = bias_two[:, 0:128]
    g.snap_tiles[me_snap, 7:8, :] = bias_two[:, 128:256]
    for step in range(1, snaps):
        snap_tile_copy(step).start()

    for step in range(1, snaps):
        filter_copy(step).wait_recv()
    filter_sum = g.filt_out[0].astype(f32)
    for snap in range(1, snaps):
        filter_sum += g.filt_out[snap].astype(f32)
    g.grad_filt[...] = filter_sum
    for part in range(parts):
        for matrix in range(2):
            for step in range(1, snaps):
                last_copy(part, matrix, step).wait_recv()
    grads_out = pltpu.make_async_copy(g.total, g.grad_mlp, g.load_sem.at[3])
    grads_out.start()
    for step in range(1, snaps):
        snap_tile_copy(step).wait_recv()
    tile_sum = g.snap_tiles[0]
    for snap in range(1, snaps):
        tile_sum += g.snap_tiles[snap]
    g.grad_small[...] = tile_sum

    grads_out.wait()
    for copies in [out_copies, *grad_copies[-2:]]:
        for copy in copies:
            copy.wait()
    for step in range(1, group):
        small_copy(step).wait_send()
        block_copy(1, step).wait_send()
        row_copy(1, step).wait_send()
        tile_copy(step).wait_send()
        for part in range(parts):
            first_copy(part, step).wait_send()
    for part in range(parts):
        second_copy(part).wait_send()
        third_copy(part).wait_send()
        fourth_copy(part).wait_send()
    for part in (parts - 2, parts - 1):
        for matrix in range(2):
            core_copy(part, matrix).wait_send()
            half_copy(part, matrix).wait_send()
            quarter_copy(part, matrix).wait_send()
        for step in range(1, levels):
            level_copy(part, step).wait_send()
    for step in range(1, snaps):
        filter_copy(step).wait_send()
        snap_tile_copy(step).wait_send()
        for part in range(parts):
            for matrix in range(2):
                last_copy(part, matrix, step).wait_send()


def block_pass(fields, cot, valid, kept, mlp, filt, small, snaps, group):
    snap_local, row_local, lon_total, channel = fields.shape
    tokens = snap_local * row_local * lon_total
    hidden = mlp.shape[2]
    lat_total = row_local * group
    modes = kept.shape[1] * group
    owned = channel // group
    width = 512
    parts = hidden // width
    levels = group // 2
    quarter = width // snaps
    low, f32 = jnp.bfloat16, jnp.float32
    half = width // 2
    lon_f, lon_i = lon_matrix(lon_total, modes, snap_local, row_local)

    def paired(array):
        return jnp.transpose(array, (0, 2, 1, 3)).reshape(-1, row_local, channel)

    lat_f = lat_matrix(lat_total, modes)
    pair = 2 * modes * row_local
    spread = snap_local * row_local * 2 * modes
    inputs = dict(
        small=small,
        kept=kept.T,
        fields=paired(fields),
        lon_f=jnp.asarray(np.ascontiguousarray(lon_f.T)),
        filt=filt,
        lat_f=jnp.asarray(lat_f),
        lat_b=jnp.asarray(np.ascontiguousarray(lat_f.T)),
        cot=paired(cot),
        lon_i=jnp.asarray(lon_i),
        valid=valid,
        turn=jnp.asarray(lon_turn(lon_total, row_local)),
        lon_it=jnp.asarray(np.ascontiguousarray(lon_i.T)),
        lon_ft=jnp.asarray(lon_f),
        mlp=mlp,
    )
    outputs = dict(
        out=jax.ShapeDtypeStruct((tokens // row_local, row_local, channel), low),
        in_grad=jax.ShapeDtypeStruct((tokens // row_local, row_local, channel), f32),
        grad_mlp=jax.ShapeDtypeStruct((parts, snaps, 2, owned, quarter), low),
        grad_filt=jax.ShapeDtypeStruct((4, owned, 128), f32),
        grad_small=jax.ShapeDtypeStruct((16, 128), f32),
    )
    vmem = pltpu.VMEM
    dma = pltpu.SemaphoreType.DMA
    scratch = {
        name + "_in": vmem(value.shape, value.dtype)
        for name, value in inputs.items()
        if name not in ("mlp", "fields", "cot")
    }
    tiles = channel // 128
    cols = (tiles, tokens // row_local, row_local, 128)
    piece = divisor(tokens, 96, 288)
    scratch |= dict(
        mlp_part=vmem((2, 2, owned, width), f32),
        fields_cols=vmem(cols, low),
        cot_cols=vmem(cols, low),
        grad_cols_0=vmem((tiles, piece // row_local, row_local, 128), f32),
        grad_cols_1=vmem((tiles, piece // row_local, row_local, 128), f32),
        grad_sem=dma((2, tiles)),
        fields_sem=dma((tiles,)),
        cot_sem=dma((tiles,)),
        cot_in=vmem((tokens, channel), low),
        grid=vmem((tokens, channel), f32),
        back=vmem((tokens, channel), f32),
        normed=vmem((tokens, channel), low),
        normed_turned=vmem((channel, tokens), low),
        cot_turned=vmem((channel, tokens), low),
        unit_one=vmem((tokens, channel), low),
        unit_two=vmem((tokens, channel), low),
        scale_one=vmem((tokens, 1), f32),
        scale_two=vmem((tokens, 1), f32),
        own_small=vmem((16 + kept.shape[0], 128), f32),
        all_small=vmem((group, 16 + kept.shape[0], 128), f32),
        gains=vmem((16, channel), f32),
        keep=vmem((lat_total * modes, 128), f32),
        own_w=vmem((parts, 2, owned, width), low),
        all_w=vmem((parts, 2, channel, width), low),
        modes=vmem((group, snap_local, pair, 128), low),
        arrived=vmem((snap_local, pair * group, 128), low),
        turned=vmem((snap_local, pair * group, 128), low),
        home=vmem((group, snap_local, pair, 128), low),
        gathered=vmem((spread, channel), f32),
        home_low=vmem((spread, channel), low),
        weight_one=vmem((256, 256), low),
        weight_two=vmem((256, 256), low),
        spectrum=vmem((snap_local * lat_total * modes, 256), low),
        pre_one=vmem((snap_local * lat_total * modes, 256), f32),
        act_one=vmem((snap_local * lat_total * modes, 256), low),
        pre_two=vmem((snap_local * lat_total * modes, 256), f32),
        grad_two=vmem((snap_local * lat_total * modes, 256), f32),
        pair_grad=vmem((256, 256), f32),
        act=vmem((tokens, width), low),
        slope=vmem((tokens, width), low),
        bias=vmem((parts, 1, width), f32),
        grad_bias=vmem((parts, 1, width), f32),
        grad_rows=vmem((16, channel), f32),
        grads=vmem((2, 2, levels, 2, owned, width), low),
        core_got=vmem((2, 2, levels, owned, width), low),
        half_out=vmem((2, 2, 2, levels, owned, half), low),
        half_got=vmem((2, 2, levels, owned, half), low),
        quarter_out=vmem((2, 2, 2, levels, owned, quarter), low),
        quarter_got=vmem((2, 2, levels, owned, quarter), low),
        level_out=vmem((2, levels, 2, owned, quarter), low),
        level_got=vmem((2, levels, 2, owned, quarter), low),
        total=vmem((parts, snaps, 2, owned, quarter), low),
        filt_out=vmem((snaps, 4, owned, 128), low),
        tiles=vmem((group, 16, 128), f32),
        tiles_got=vmem((group, 16, 128), f32),
        snap_tiles=vmem((snaps, 16, 128), f32),
        load_sem=dma((len(inputs) + 1,)),
    )
    for name, shape in dict(
        small=(group,),
        first=(parts, group),
        second=(parts,),
        third=(parts,),
        fourth=(parts,),
        block=(2, group),
        row=(2, group),
        core=(2, 2),
        half=(2, 2),
        quarter=(2, 2),
        level=(2, levels),
        last=(parts, 2, snaps),
        filt=(snaps,),
        tile=(group,),
        snap_tile=(snaps,),
    ).items():
        scratch[name + "_s"] = dma(shape)
        scratch[name + "_r"] = dma(shape)
    names = [*inputs, *outputs, *scratch]
    far = pl.BlockSpec(memory_space=pl.ANY)
    near = pl.BlockSpec(memory_space=pltpu.VMEM)
    results = pl.pallas_call(
        functools.partial(block_body, names, (snaps, group, parts, width)),
        in_specs=[far] * len(inputs),
        out_specs=[far, far, far, near, near],
        out_shape=list(outputs.values()),
        scratch_shapes=list(scratch.values()),
        compiler_params=pltpu.CompilerParams(
            collective_id=0, has_side_effects=True, vmem_limit_bytes=VMEM_LIMIT
        ),
        cost_estimate=pl.CostEstimate(
            flops=12 * tokens * channel * hidden,
            bytes_accessed=4 * hidden * channel,
            transcendentals=tokens * hidden,
        ),
        name="block_pass",
    )(*inputs.values())
    return results


def step_body(names, positions, *refs):
    g = Refs()
    for name, ref in zip(names, refs, strict=True):
        setattr(g, name, ref)
    parts, snaps = g.grad_mlp.shape[:2]
    quarter = g.grad_mlp.shape[4]
    width = snaps * quarter
    moments = ("w", "m", "v")
    results = ("new", "first", "second", "copy")

    pieces = g.far_sem.shape[1]
    passing = []
    for kind, (source, target) in enumerate(((g.out, g.out_o), (g.in_grad, g.in_grad_o))):
        size = source.shape[0] // pieces
        for piece in range(pieces):
            rows = pl.ds(piece * size, size)
            passing.append(
                pltpu.make_async_copy(source.at[rows], target.at[rows], g.far_sem.at[kind, piece])
            )

    def part_cols(part):
        return pl.ds(part * width, width)

    def load(part):
        near = [
            pltpu.make_async_copy(
                getattr(g, "mlp_" + kind).at[:, :, part_cols(part)],
                g.near.at[index, part],
                g.near_sem.at[index, part],
            )
            for index, kind in enumerate(moments)
        ]
        near.append(
            pltpu.make_async_copy(g.grad_mlp.at[part], g.grad_near.at[part], g.near_sem.at[3, part])
        )
        return near

    def store(part):
        copies = [
            pltpu.make_async_copy(
                g.near.at[index, part],
                getattr(g, "mlp_" + kind).at[:, :, part_cols(part)],
                g.back_sem.at[index, part],
            )
            for index, kind in enumerate(results[:3])
        ]
        copies.append(
            pltpu.make_async_copy(
                g.low_near.at[part], g.mlp_copy.at[:, :, part_cols(part)], g.back_sem.at[3, part]
            )
        )
        return copies

    coming = [load(part) for part in range(parts)]
    going = [store(part) for part in range(parts)]
    for part in range(parts):
        for copy in coming[part]:
            copy.start()
    for copy in passing:
        copy.start()

    def put(prefix, values):
        for kind, value in zip(results, values, strict=True):
            getattr(g, prefix + kind)[...] = value

    owned = g.filt_w.shape[2]
    put(
        "filt_",
        adamw(g.filt_w[...], g.filt_m[...], g.filt_v[...], g.grad_filt[:, :, 0:owned], rate_filter),
    )
    rows = g.small_w.shape[0]
    put(
        "small_",
        adamw(
            g.small_w[...], g.small_m[...], g.small_v[...], g.grad_small[0:rows, 0:owned], rate_small
        ),
    )
    totals = g.grad_small[rows : rows + 2, 0 : g.run.shape[1]]
    g.stats[...] = stat_decay * g.run[...] + (1.0 - stat_decay) * totals / positions

    for part in range(parts):
        for copy in coming[part]:
            copy.wait()

        for snap in range(snaps):
            cols = slice(snap * quarter, (snap + 1) * quarter)
            where = (slice(None), slice(None), cols)
            now = [g.near[(index, part, *where)] for index in range(3)]
            grad = g.grad_near[part, snap].astype(jnp.float32)
            values = adamw(*now, grad, rate_mlp)
            for index in range(3):
                g.near[(index, part, *where)] = values[index]
            g.low_near[(part, *where)] = values[3]
        for copy in going[part]:
            copy.start()
    for copy in passing:
        copy.wait()
    for part in range(parts):
        for copy in going[part]:
            copy.wait()


def step_pass(shown, grads, masters, run_stats, positions):
    grad_mlp, grad_filt, grad_small = grads
    mlp, filt, small = masters
    parts = grad_mlp.shape[0]
    width = mlp[0].shape[2] // parts
    f32, low = jnp.float32, jnp.bfloat16
    far = pl.BlockSpec(memory_space=pltpu.HBM)
    near = pl.BlockSpec(memory_space=pltpu.VMEM)
    inputs = dict(out=shown[0], in_grad=shown[1], grad_mlp=grad_mlp)
    inputs |= dict(zip(("mlp_w", "mlp_m", "mlp_v"), mlp, strict=True))
    far_in = len(inputs)
    inputs |= dict(grad_filt=grad_filt, grad_small=grad_small)
    inputs |= dict(zip(("filt_w", "filt_m", "filt_v"), filt, strict=True))
    inputs |= dict(zip(("small_w", "small_m", "small_v"), small, strict=True))
    inputs |= dict(run=run_stats)
    results = (("new", f32), ("first", f32), ("second", f32), ("copy", low))
    outputs = {
        name + "_o": jax.ShapeDtypeStruct(array.shape, array.dtype)
        for name, array in zip(("out", "in_grad"), shown, strict=True)
    }
    outputs |= {"mlp_" + kind: jax.ShapeDtypeStruct(mlp[0].shape, dt) for kind, dt in results}
    far_out = len(outputs)
    outputs |= {"filt_" + kind: jax.ShapeDtypeStruct(filt[0].shape, dt) for kind, dt in results}
    outputs |= {"small_" + kind: jax.ShapeDtypeStruct(small[0].shape, dt) for kind, dt in results}
    outputs |= dict(stats=jax.ShapeDtypeStruct(run_stats.shape, f32))
    scratch = dict(
        near=pltpu.VMEM((3, parts, 2, mlp[0].shape[1], width), f32),
        grad_near=pltpu.VMEM(grad_mlp.shape, low),
        low_near=pltpu.VMEM((parts, 2, mlp[0].shape[1], width), low),
        near_sem=pltpu.SemaphoreType.DMA((4, parts)),
        back_sem=pltpu.SemaphoreType.DMA((4, parts)),
        far_sem=pltpu.SemaphoreType.DMA((2, divisor(shown[0].shape[0], 1, 8))),
    )
    return pl.pallas_call(
        functools.partial(step_body, [*inputs, *outputs, *scratch], positions),
        in_specs=[far] * far_in + [near] * (len(inputs) - far_in),
        out_specs=[far] * far_out + [near] * (len(outputs) - far_out),
        out_shape=list(outputs.values()),
        scratch_shapes=list(scratch.values()),
        compiler_params=pltpu.CompilerParams(vmem_limit_bytes=48 * 1024 * 1024),
        name="step_pass",
    )(*inputs.values())


def per_device_blocks(
    fields,
    cotangent,
    valid_mask,
    kept_modes,
    mlp_master,
    mlp_first,
    mlp_second,
    filter_master,
    filter_first,
    filter_second,
    small_master,
    small_first,
    small_second,
    run_stats,
):
    snaps, group = lax.axis_size("snap"), lax.axis_size("sp")
    out, in_grad, *grads = block_pass(
        fields, cotangent, valid_mask, kept_modes, mlp_master, filter_master, small_master, snaps, group
    )
    snap_local, row_local, lon_total, channel = fields.shape
    positions = snap_local * snaps * row_local * group * lon_total
    out, in_grad, *stepped = step_pass(
        (out, in_grad),
        grads,
        (
            (mlp_master, mlp_first, mlp_second),
            (filter_master, filter_first, filter_second),
            (small_master, small_first, small_second),
        ),
        run_stats,
        positions,
    )
    rows_apart = (snap_local, lon_total, row_local, channel)
    out, in_grad = [
        jnp.transpose(array.reshape(rows_apart), (0, 2, 1, 3)) for array in (out, in_grad)
    ]
    return (out, in_grad, *stepped)


def per_device(*arrays):
    group, snaps = lax.axis_size("sp"), lax.axis_size("snap")
    channel, hidden = arrays[0].shape[3], arrays[4].shape[2]
    by_block = group == BLOCKS and snaps == 4 and arrays[3].shape[1] == 1
    if by_block and hidden % 512 == 0 and channel // group <= 128 and channel % (16 * group) == 0:
        return per_device_blocks(*arrays)
    return per_device_modes(*arrays)


def solution(mesh):
    return jax.shard_map(
        per_device,
        mesh=mesh,
        in_specs=(
            P("snap", "sp", None, None),
            P("snap", "sp", None, None),
            P("snap", "sp", None),
            P(None, "sp"),
            P(None, "sp", None),
            P(None, "sp", None),
            P(None, "sp", None),
            P(None, "sp", None),
            P(None, "sp", None),
            P(None, "sp", None),
            P(None, "sp"),
            P(None, "sp"),
            P(None, "sp"),
            P(),
        ),
        out_specs=(
            P("snap", "sp", None, None),
            P("snap", "sp", None, None),
            P(None, "sp", None),
            P(None, "sp", None),
            P(None, "sp", None),
            P(None, "sp", None),
            P(None, "sp", None),
            P(None, "sp", None),
            P(None, "sp", None),
            P(None, "sp", None),
            P(None, "sp"),
            P(None, "sp"),
            P(None, "sp"),
            P(None, "sp"),
            P(),
        ),
        check_vma=False,
    )
```

```python
import functools
import math

import jax
import jax.numpy as jnp
import ml_dtypes
import numpy as np
from jax import lax
from jax.experimental import pallas as pl
from jax.experimental.pallas import tpu as pltpu
from jax.sharding import PartitionSpec as P

BLOCKS = 8
NVAR = 20
STEP = 10
VMEM_LIMIT = 63 * 1024 * 1024


eps_norm = 1e-06
shrink_level = 0.01
beta_one = 0.5
beta_two = 0.5
adam_eps = 1e-08
decay_rate = 0.01
rate_mlp = 0.03
rate_filter = 0.1
rate_small = 0.2
stat_decay = 0.5


def layer_norm(values, gain_vec, shift_vec):
    centred = values - jnp.mean(values, axis=-1, keepdims=True)
    spread = jnp.mean(centred * centred, axis=-1, keepdims=True)
    return centred * lax.rsqrt(spread + eps_norm) * gain_vec + shift_vec


def shrink(values):
    return values - shrink_level * jnp.tanh(values / shrink_level)


def lon_tables(lon_total, mode_total):
    places = jnp.arange(lon_total, dtype=jnp.int32)
    orders = jnp.arange(mode_total, dtype=jnp.int32)
    angles = (places[:, None] * orders[None, :] % lon_total).astype(jnp.float32) * (
        2.0 * math.pi / lon_total
    )
    scaling = 1.0 / math.sqrt(lon_total)
    forward_tab = jnp.stack([jnp.cos(angles), -jnp.sin(angles)], axis=1) * scaling
    doubling = jnp.where(orders == 0, 1.0, 2.0).astype(jnp.float32)[:, None]
    inverse_tab = (
        jnp.stack([jnp.cos(angles).T * doubling, -jnp.sin(angles).T * doubling], axis=0) * scaling
    )
    return (forward_tab.astype(jnp.bfloat16), inverse_tab.astype(jnp.bfloat16))


def lat_table(lat_total):
    places = jnp.arange(lat_total, dtype=jnp.int32)
    angles = (places[:, None] * places[None, :] % lat_total).astype(jnp.float32) * (
        2.0 * math.pi / lat_total
    )
    cosine = jnp.cos(angles)
    sine_part = jnp.sin(angles)
    upper_rows = jnp.stack([cosine, sine_part], axis=1)
    bottom = jnp.stack([-sine_part, cosine], axis=1)
    return (jnp.stack([upper_rows, bottom], axis=0) / math.sqrt(lat_total)).astype(jnp.bfloat16)


def complex_pair(real_part, imag_part):
    return jnp.stack([jnp.stack([real_part, -imag_part]), jnp.stack([imag_part, real_part])])


gelu_scale = math.sqrt(2.0 / math.pi)
gelu_cubic = 0.044715


def gelu_both(value):
    bend = (gelu_scale * gelu_cubic) * (value * value)
    turn = jnp.tanh(value * (gelu_scale + bend))
    half = 0.5 + 0.5 * turn
    slope = half * (1.0 + (value * (1.0 - turn)) * (gelu_scale + 3.0 * bend))
    return value * half, slope


def dot_nt(left, right):
    return lax.dot_general(
        left, right, (((1,), (1,)), ((), ())), preferred_element_type=jnp.float32
    )


def dot_nn(left, right):
    return jnp.dot(left, right, preferred_element_type=jnp.float32)


def divisor(total, unit, most):
    return max(size for size in range(unit, most + 1, unit) if total % size == 0)


def mlp_body(
    tile,
    normed_ref,
    cot_ref,
    up_ref,
    down_ref,
    bias_ref,
    out_ref,
    back_ref,
    grad_up_ref,
    grad_down_ref,
    grad_bias_ref,
    normed_turned,
    cot_turned,
    act_ref,
    slope_ref,
):
    tokens = normed_ref.shape[0]

    @pl.when(pl.program_id(0) == 0)
    def _():
        normed_turned[...] = normed_ref[...].T
        cot_turned[...] = cot_ref[...].T
        out_ref[...] = jnp.zeros_like(out_ref)
        back_ref[...] = jnp.zeros_like(back_ref)

    grad_bias_ref[...] = jnp.zeros_like(grad_bias_ref)

    @pl.loop(0, tokens // tile)
    def _(step):
        rows = pl.ds(pl.multiple_of(step * tile, tile), tile)
        act, slope = gelu_both(dot_nn(normed_ref[rows, :], up_ref[...]) + bias_ref[...])
        act = act.astype(jnp.bfloat16)
        slope = (dot_nn(cot_ref[rows, :], down_ref[...]) * slope).astype(jnp.bfloat16)
        act_ref[rows, :] = act
        slope_ref[rows, :] = slope
        grad_bias_ref[...] += jnp.sum(slope.astype(jnp.float32), axis=0, keepdims=True)
        out_ref[rows, :] += dot_nt(act, down_ref[...])
        back_ref[rows, :] += dot_nt(slope, up_ref[...])

    grad_up_ref[...] = dot_nn(normed_turned[...], slope_ref[...]).astype(grad_up_ref.dtype)
    grad_down_ref[...] = dot_nn(cot_turned[...], act_ref[...]).astype(grad_down_ref.dtype)


def mlp_pass(normed, cot, weights, bias):
    tokens, channel = normed.shape
    hidden = weights.shape[2]
    width = divisor(hidden, 128, 512)
    tile = divisor(tokens, 16, 480)
    whole = pl.BlockSpec((tokens, channel), lambda j: (0, 0))
    block = pl.BlockSpec((channel, width), lambda j: (0, j))
    line = pl.BlockSpec((1, width), lambda j: (0, j))
    part = lambda which: pl.BlockSpec((None, channel, width), lambda j: (which, 0, j))
    total = jax.ShapeDtypeStruct((tokens, channel), jnp.float32)
    grads = jax.ShapeDtypeStruct((channel, hidden), jnp.bfloat16)
    return pl.pallas_call(
        functools.partial(mlp_body, tile),
        grid=(hidden // width,),
        in_specs=[whole, whole, part(0), part(1), line],
        out_specs=[whole, whole, block, block, line],
        out_shape=[total, total, grads, grads, jax.ShapeDtypeStruct((1, hidden), jnp.float32)],
        scratch_shapes=[
            pltpu.VMEM((channel, tokens), jnp.bfloat16),
            pltpu.VMEM((channel, tokens), jnp.bfloat16),
            pltpu.VMEM((tokens, width), jnp.bfloat16),
            pltpu.VMEM((tokens, width), jnp.bfloat16),
        ],
        compiler_params=pltpu.CompilerParams(vmem_limit_bytes=56 * 1024 * 1024),
        cost_estimate=pl.CostEstimate(
            flops=12 * tokens * channel * hidden,
            bytes_accessed=8 * channel * hidden + 12 * tokens * channel,
            transcendentals=tokens * hidden,
        ),
        name="mlp_pass",
    )(normed, cot, weights, weights, bias)


def spectral_front(arrived, lat_fwd, first_pair, second_pair, bias_one, bias_two):
    spectrum = jnp.einsum(
        "pkqr,nrqmd->nkpmd", lat_fwd, arrived, preferred_element_type=jnp.float32
    ).astype(jnp.bfloat16)
    snap_local, lat_total, pair_count, mode_local, channel = spectrum.shape
    blocked = spectrum.reshape(
        snap_local, lat_total, pair_count, mode_local, BLOCKS, channel // BLOCKS
    )
    pre_one = (
        jnp.einsum("nkqmbi,pqbio->nkpmbo", blocked, first_pair, preferred_element_type=jnp.float32)
        + bias_one
    )
    act_one = jax.nn.gelu(pre_one).astype(jnp.bfloat16)
    pre_two = (
        jnp.einsum("nkqmbi,pqbio->nkpmbo", act_one, second_pair, preferred_element_type=jnp.float32)
        + bias_two
    )
    return (blocked, pre_one, act_one, pre_two)


def adamw(master, first_mom, second_mom, gradient, step_rate):
    first_next = beta_one * first_mom + (1.0 - beta_one) * gradient
    second_next = beta_two * second_mom + (1.0 - beta_two) * gradient * gradient
    fix_one = 1.0 - beta_one**STEP
    fix_two = 1.0 - beta_two**STEP
    direction = first_next / fix_one / (jnp.sqrt(second_next / fix_two) + adam_eps)
    master_next = master - step_rate * (direction + decay_rate * master)
    return (master_next, first_next, second_next, master_next.astype(jnp.bfloat16))


def per_device_modes(
    fields,
    cotangent,
    valid_mask,
    kept_modes,
    mlp_master,
    mlp_first,
    mlp_second,
    filter_master,
    filter_first,
    filter_second,
    small_master,
    small_first,
    small_second,
    run_stats,
):
    group_size = lax.axis_size("sp")
    snap_local, row_local, lon_total, channel = fields.shape
    lat_total = row_local * group_size
    mode_local = kept_modes.shape[1]
    mode_total = mode_local * group_size
    block_width = channel // BLOCKS
    lon_fwd, lon_inv = lon_tables(lon_total, mode_total)
    lat_fwd = lat_table(lat_total)
    mlp_w, filt_w, small_w = (
        lax.all_gather(mlp_master.astype(jnp.bfloat16), "sp", axis=1, tiled=True),
        lax.all_gather(filter_master.astype(jnp.bfloat16), "sp", axis=1, tiled=True),
        lax.all_gather(small_master.astype(jnp.bfloat16), "sp", axis=1, tiled=True),
    )
    small_f = small_w.astype(jnp.float32)
    weights = filt_w.reshape(4, BLOCKS, block_width, block_width)
    first_pair = complex_pair(weights[0], weights[1])
    second_pair = complex_pair(weights[2], weights[3])
    bias_one = small_f[4:6].reshape(2, 1, BLOCKS, block_width)
    bias_two = small_f[6:8].reshape(2, 1, BLOCKS, block_width)
    fields_float = fields.astype(jnp.float32)
    normed, norm_pull = jax.vjp(layer_norm, fields_float, small_f[0], small_f[1])
    normed_low = normed.astype(jnp.bfloat16)
    spec_lon = jnp.einsum(
        "nrld,lqm->nrqmd", normed_low, lon_fwd, preferred_element_type=jnp.float32
    ).astype(jnp.bfloat16)
    arrived = lax.all_to_all(spec_lon, "sp", split_axis=3, concat_axis=1, tiled=True)
    spectral = spectral_front(arrived, lat_fwd, first_pair, second_pair, bias_one, bias_two)
    keep_mask = kept_modes.astype(jnp.float32)[None, :, None, :, None, None]
    masked = (shrink(spectral[3]) * keep_mask).astype(jnp.bfloat16)
    masked = masked.reshape(snap_local, lat_total, 2, mode_local, channel)
    returned = jnp.einsum(
        "pkqr,nkpmd->nrqmd", lat_fwd, masked, preferred_element_type=jnp.float32
    ).astype(jnp.bfloat16)
    home_modes = lax.all_to_all(returned, "sp", split_axis=1, concat_axis=3, tiled=True)
    filtered = jnp.einsum(
        "nrqmd,qml->nrld", home_modes, lon_inv, preferred_element_type=jnp.float32
    )
    mixture = fields_float + normed + filtered
    normed_two, norm_two_pull = jax.vjp(layer_norm, mixture, small_f[2], small_f[3])
    normed_two_low = normed_two.astype(jnp.bfloat16)
    tokens = snap_local * row_local * lon_total
    passed = mlp_pass(
        normed_two_low.reshape(tokens, channel),
        cotangent.reshape(tokens, channel),
        mlp_w,
        small_f[9:].reshape(1, -1),
    )
    output = mixture + passed[0].reshape(mixture.shape) + small_f[8]
    weight_mask = valid_mask.astype(jnp.float32)[..., None]
    variables = output[..., :NVAR]
    local_sums = jnp.stack(
        [
            jnp.sum(weight_mask * variables, axis=(0, 1, 2)),
            jnp.sum(weight_mask * variables * variables, axis=(0, 1, 2)),
        ]
    )
    total_sums = lax.psum(local_sums, ("snap", "sp"))
    positions = snap_local * lax.axis_size("snap") * lat_total * lon_total
    stats_new = stat_decay * run_stats + (1.0 - stat_decay) * total_sums / positions
    cot_float = cotangent.astype(jnp.float32)
    grad_normed_two = passed[1].reshape(mixture.shape)
    grad_bias_hidden = passed[4]
    grad_mix_norm, grad_gain_two, grad_shift_two = norm_two_pull(grad_normed_two)
    grad_mixture = cot_float + grad_mix_norm
    grad_bias_out = jnp.sum(cot_float, axis=(0, 1, 2))
    grad_filtered = grad_mixture.astype(jnp.bfloat16)
    grad_home = jnp.einsum(
        "nrld,qml->nrqmd", grad_filtered, lon_inv, preferred_element_type=jnp.float32
    ).astype(jnp.bfloat16)
    grad_returned = lax.all_to_all(grad_home, "sp", split_axis=3, concat_axis=1, tiled=True)
    grad_masked = jnp.einsum(
        "pkqr,nrqmd->nkpmd", lat_fwd, grad_returned, preferred_element_type=jnp.float32
    )
    arrived_again = lax.all_to_all(spec_lon, "sp", split_axis=3, concat_axis=1, tiled=True)
    used_front = spectral_front(arrived_again, lat_fwd, first_pair, second_pair, bias_one, bias_two)
    blocked, pre_one, act_one, pre_two = used_front
    grad_two = jax.vjp(shrink, pre_two)[1](grad_masked.reshape(pre_two.shape) * keep_mask)[
        0
    ].astype(jnp.bfloat16)
    grad_bias_two = jnp.sum(grad_two.astype(jnp.float32), axis=(0, 1, 3))
    grad_second = jnp.einsum(
        "nkqmbi,nkpmbo->pqbio", act_one, grad_two, preferred_element_type=jnp.float32
    )
    grad_act = jnp.einsum(
        "nkpmbo,pqbio->nkqmbi", grad_two, second_pair, preferred_element_type=jnp.float32
    )
    grad_one = jax.vjp(jax.nn.gelu, pre_one)[1](grad_act)[0].astype(jnp.bfloat16)
    grad_bias_one = jnp.sum(grad_one.astype(jnp.float32), axis=(0, 1, 3))
    grad_first = jnp.einsum(
        "nkqmbi,nkpmbo->pqbio", blocked, grad_one, preferred_element_type=jnp.float32
    )
    grad_spectrum = jnp.einsum(
        "nkpmbo,pqbio->nkqmbi", grad_one, first_pair, preferred_element_type=jnp.float32
    ).astype(jnp.bfloat16)
    grad_spectrum = grad_spectrum.reshape(snap_local, lat_total, 2, mode_local, channel)
    grad_lon = jnp.einsum(
        "pkqr,nkpmd->nrqmd", lat_fwd, grad_spectrum, preferred_element_type=jnp.float32
    ).astype(jnp.bfloat16)
    grad_rows = lax.all_to_all(grad_lon, "sp", split_axis=1, concat_axis=3, tiled=True)
    grad_normed = grad_mixture + jnp.einsum(
        "nrqmd,lqm->nrld", grad_rows, lon_fwd, preferred_element_type=jnp.float32
    )
    grad_field_norm, grad_gain_one, grad_shift_one = norm_pull(grad_normed)
    input_grad = grad_mixture + grad_field_norm
    grad_filter = jnp.stack(
        [
            grad_first[0, 0] + grad_first[1, 1],
            grad_first[1, 0] - grad_first[0, 1],
            grad_second[0, 0] + grad_second[1, 1],
            grad_second[1, 0] - grad_second[0, 1],
        ]
    ).reshape(4, channel, block_width)
    grad_small = jnp.concatenate(
        [
            jnp.stack([grad_gain_one, grad_shift_one, grad_gain_two, grad_shift_two]),
            grad_bias_one.reshape(2, channel),
            grad_bias_two.reshape(2, channel),
            grad_bias_out[None, :],
            grad_bias_hidden.reshape(-1, channel),
        ],
        axis=0,
    )
    shares = (
        jnp.stack([
            lax.psum_scatter(part, "sp", scatter_dimension=0, tiled=True) for part in passed[2:4]
        ]),
        lax.psum_scatter(grad_filter, "sp", scatter_dimension=1, tiled=True),
        lax.psum_scatter(grad_small, "sp", scatter_dimension=1, tiled=True),
    )
    owned = (
        lax.psum(shares[0].astype(jnp.bfloat16), "snap").astype(jnp.float32),
        lax.psum(shares[1].astype(jnp.bfloat16), "snap").astype(jnp.float32),
        lax.psum(shares[2].astype(jnp.bfloat16), "snap").astype(jnp.float32),
    )
    mlp_new, mlp_first_new, mlp_second_new, mlp_copy = adamw(
        mlp_master, mlp_first, mlp_second, owned[0], rate_mlp
    )
    filter_new, filter_first_new, filter_second_new, filter_copy = adamw(
        filter_master, filter_first, filter_second, owned[1], rate_filter
    )
    small_new, small_first_new, small_second_new, small_copy = adamw(
        small_master, small_first, small_second, owned[2], rate_small
    )
    return (
        output.astype(jnp.bfloat16),
        input_grad,
        mlp_new,
        mlp_first_new,
        mlp_second_new,
        mlp_copy,
        filter_new,
        filter_first_new,
        filter_second_new,
        filter_copy,
        small_new,
        small_first_new,
        small_second_new,
        small_copy,
        stats_new,
    )


def lon_matrix(lon_total, mode_total, snaps, rows):
    places = np.arange(lon_total)
    orders = np.arange(mode_total)
    angles = (places[:, None] * orders[None, :] % lon_total) * (2.0 * math.pi / lon_total)
    doubling = np.where(orders == 0, 1.0, 2.0)
    scaling = 1.0 / math.sqrt(lon_total)
    forward = np.stack([np.cos(angles), -np.sin(angles)], axis=1) * scaling
    inverse = forward * doubling

    def spread(table):
        table = np.einsum(
            "ab,lx,rs->alrbsx", np.eye(snaps), table.reshape(lon_total, -1), np.eye(rows)
        )
        return table.reshape(snaps * lon_total * rows, -1).astype(ml_dtypes.bfloat16)

    return spread(forward), spread(inverse)


def lon_turn(lon_total, rows):
    turn = np.einsum("lk,rs->rlks", np.eye(lon_total), np.eye(rows))
    return turn.reshape(rows, lon_total, lon_total * rows).astype(ml_dtypes.bfloat16)


def lat_matrix(lat_total, mode_total):
    places = np.arange(lat_total)
    angles = (places[:, None] * places[None, :] % lat_total) * (2.0 * math.pi / lat_total)
    cosine, sine = np.cos(angles), np.sin(angles)
    table = np.stack([np.stack([cosine, sine], axis=1), np.stack([-sine, cosine], axis=1)])
    table = np.einsum("pkqr,ab->pakrqb", table / math.sqrt(lat_total), np.eye(mode_total))
    size = 2 * lat_total * mode_total
    return table.reshape(size, size).astype(ml_dtypes.bfloat16)


class Refs:
    pass


def block_body(names, sizes, *refs):
    g = Refs()
    for name, ref in zip(names, refs, strict=True):
        setattr(g, name, ref)
    snaps, group, parts, width = sizes
    levels = group // 2
    tokens = g.fields.shape[0] * g.fields.shape[1]
    channel = g.fields.shape[2]
    tiles = channel // 128
    owned = channel // group
    half = width // 2
    quarter = width // snaps
    tile = divisor(tokens, 16, 480)
    strip = divisor(tokens // 2, 48, 144)
    sub = divisor(strip, 16, 48)
    low = jnp.bfloat16
    f32 = jnp.float32

    me_snap = lax.axis_index("snap")
    me_sp = lax.axis_index("sp")
    core = lax.rem(me_sp, 2)
    level = me_sp // 2

    def at(snap, sp):
        return {"snap": snap, "sp": sp}

    def sp_after(step):
        return lax.rem(me_sp + step, group)

    def sp_before(step):
        return lax.rem(me_sp + group - step, group)

    def snap_after(step):
        return lax.rem(me_snap + step, snaps)

    def snap_before(step):
        return lax.rem(me_snap + snaps - step, snaps)

    def level_after(step):
        return lax.rem(level + step, levels)

    def level_before(step):
        return lax.rem(level + levels - step, levels)

    other_core = at(me_snap, me_sp + 1 - 2 * core)

    def send(src, dst, sems, index, target):
        return pltpu.make_async_remote_copy(
            src_ref=src,
            dst_ref=dst,
            send_sem=sems[0].at[index],
            recv_sem=sems[1].at[index],
            device_id=target,
            device_id_type=pl.DeviceIdType.MESH,
        )

    half_tokens = tokens // 2

    def strips(body, first=0, count=tokens):
        @pl.loop(0, count // strip)
        def _(step):
            for at_row in range(0, strip, sub):
                body(pl.ds(pl.multiple_of(first + step * strip + at_row, 16), sub))

    def half_strips(body, part):
        strips(body, part * half_tokens, half_tokens)

    def half_rows(part):
        return slice(part * half_tokens, (part + 1) * half_tokens)

    def fold(value):
        return jnp.sum(value.reshape(-1, 8, value.shape[1]), axis=0)

    def columns(name):
        ref = getattr(g, name)
        return ref.reshape(tiles, ref.shape[1] * ref.shape[2], 128)

    def columns_of(name, rows):
        view = columns(name)
        return jnp.concatenate([view[tile_at, rows, :] for tile_at in range(tiles)], axis=1)

    def store_columns(name, rows, value):
        view = columns(name)
        for tile_at in range(tiles):
            view[tile_at, rows, :] = value[:, tile_at * 128 : (tile_at + 1) * 128]

    def column_copies(near, far, sems, out):
        copies = []
        for tile_at in range(tiles):
            ends = [near.at[tile_at], far.at[:, :, tile_at * 128 : (tile_at + 1) * 128]]
            if not out:
                ends.reverse()
            copies.append(pltpu.make_async_copy(*ends, sems.at[tile_at]))
        return copies

    loads = {}

    def load(name, index):
        copy = pltpu.make_async_copy(getattr(g, name), getattr(g, name + "_in"), g.load_sem.at[index])
        copy.start()
        loads[name] = copy

    for index, name in enumerate(
        [name for name in names[: names.index("out")] if name not in ("mlp", "fields", "cot")]
    ):
        load(name, index)
    fields_load = column_copies(g.fields_cols, g.fields, g.fields_sem, False)
    cot_load = column_copies(g.cot_cols, g.cot, g.cot_sem, False)
    for copy in fields_load + cot_load:
        copy.start()

    def master_load(part):
        return pltpu.make_async_copy(
            g.mlp.at[:, :, part * width : (part + 1) * width],
            g.mlp_part.at[part % 2],
            g.load_sem.at[len(loads) + part % 2],
        )

    master_load(0).start()
    master_load(1).start()

    barrier = pltpu.get_barrier_semaphore()
    peers = [at(me_snap, sp_after(step)) for step in range(1, group)]
    peers += [at(snap_after(step), me_sp) for step in range(1, snaps)]
    for peer in peers:
        pl.semaphore_signal(
            barrier, inc=1, device_id=peer, device_id_type=pl.DeviceIdType.MESH
        )

    loads["small"].wait()
    loads["kept"].wait()
    g.own_small[...] = jnp.zeros_like(g.own_small)
    rows_small = g.small.shape[0]
    g.own_small[0:rows_small, 0:owned] = g.small_in[...].astype(low).astype(f32)
    pairs_kept = g.kept.shape[1]
    lines = lax.broadcasted_iota(jnp.int32, (pairs_kept, pairs_kept), 0)
    places = lax.broadcasted_iota(jnp.int32, (pairs_kept, pairs_kept), 1)
    kept = jnp.where(lines == places, g.kept_in[...].astype(f32), 0.0)
    g.own_small[16:, :] = jnp.broadcast_to(
        jnp.sum(kept, axis=1, keepdims=True), (pairs_kept, g.own_small.shape[1])
    )
    pl.semaphore_wait(barrier, len(peers))

    def small_copy(step):
        return send(
            g.own_small, g.all_small.at[me_sp], (g.small_s, g.small_r), step, at(me_snap, sp_after(step))
        )

    for step in range(1, group):
        small_copy(step).start()
    g.all_small[me_sp] = g.own_small[...]

    snap_low = lax.rem(me_snap, 2)
    snap_high = me_snap // 2
    beside_low = me_snap + 1 - 2 * snap_low
    beside_high = me_snap + 2 - 4 * snap_high

    def own_quarter(part):
        odd = lax.rem(part, 2)
        return (1 - odd) * me_snap + odd * (2 * snap_low + snap_high)

    def half_quarters(part):
        return pl.ds(2 * (own_quarter(part) // 2), 2)

    def own_rows(sp):
        return pl.ds(pl.multiple_of(sp * owned, owned), owned)

    def first_copy(part, step):
        target = sp_after(step)
        matrix = lax.rem(target, 2)
        place = own_quarter(part)
        return send(
            g.own_w.at[part, matrix, place],
            g.all_w.at[part, matrix, place, own_rows(me_sp)],
            (g.first_s, g.first_r),
            (part, step),
            at(me_snap, target),
        )

    def first_local(part):
        place = own_quarter(part)
        return pltpu.make_async_copy(
            g.own_w.at[part, core, place],
            g.all_w.at[part, core, place, own_rows(me_sp)],
            g.first_s.at[part, 0],
        )

    def second_copy(part):
        odd = lax.rem(part, 2)
        view = g.all_w.at[part, core, own_quarter(part)]
        target = at((1 - odd) * beside_low + odd * beside_high, me_sp)
        return send(view, view, (g.second_s, g.second_r), part, target)

    def third_copy(part):
        odd = lax.rem(part, 2)
        view = g.all_w.at[part, core, half_quarters(part)]
        target = at((1 - odd) * beside_high + odd * beside_low, me_sp)
        return send(view, view, (g.third_s, g.third_r), part, target)

    def fourth_copy(part):
        view = g.all_w.at[part, core]
        return send(view, view, (g.fourth_s, g.fourth_r), part, other_core)

    def start_first(part):
        for step in range(1, group):
            first_copy(part, step).start()
        first_local(part).start()

    def pass_second(part):
        for step in range(1, group):
            first_copy(part, step).wait_recv()
        first_local(part).wait()
        second_copy(part).start()

    def pass_third(part):
        second_copy(part).wait_recv()
        third_copy(part).start()

    def pass_fourth(part):
        third_copy(part).wait_recv()
        fourth_copy(part).start()

    for part in range(parts):
        master_load(part).wait()
        for place in range(snaps):
            cols = slice(place * quarter, (place + 1) * quarter)
            g.own_w[part, :, place] = g.mlp_part[part % 2, :, :, cols].astype(low)
        if part + 2 < parts:
            master_load(part + 2).start()
        if part < 2:
            start_first(part)

    for copy in fields_load:
        copy.wait()

    def first_unit(rows):
        values = columns_of("fields_cols", rows).astype(f32)
        centred = values - jnp.mean(values, axis=-1, keepdims=True)
        scale = lax.rsqrt(jnp.mean(centred * centred, axis=-1, keepdims=True) + eps_norm)
        g.scale_one[rows, :] = scale
        g.grid[rows, :] = centred * scale

    strips(first_unit)
    for step in range(1, group):
        small_copy(step).wait_recv()
    for sp in range(group):
        g.gains[:, sp * owned : (sp + 1) * owned] = g.all_small[sp, 0:16, 0:owned]
        g.keep[sp * pairs_kept : (sp + 1) * pairs_kept, :] = g.all_small[sp, 16:, :]

    def first_norm(rows):
        unit = g.grid[rows, :]
        normed = unit * g.gains[0:1, :] + g.gains[1:2, :]
        g.unit_one[rows, :] = unit.astype(low)
        g.normed[rows, :] = normed.astype(low)
        g.grid[rows, :] = columns_of("fields_cols", rows).astype(f32) + normed

    half_snaps = g.arrived.shape[0] // 2

    def some_snaps(part):
        return pl.ds(part * half_snaps, half_snaps)

    def to_blocks(table, which, part):
        modes = dot_nn(table, g.normed[half_rows(part), :])
        for block in range(group):
            cut = modes[:, block * owned : (block + 1) * owned]
            cut = jnp.concatenate([cut, jnp.zeros((cut.shape[0], 128 - owned), f32)], axis=1)
            g.modes[part, block] = cut.astype(low).reshape(g.modes.shape[2:])
        for step in range(1, group):
            block_copy(which, part, step).start()
        g.arrived[some_snaps(part), mode_rows(me_sp), :] = g.modes[part, me_sp]

    def mode_rows(sp):
        size = g.modes.shape[3]
        return pl.ds(pl.multiple_of(sp * size, size), size)

    def block_copy(which, part, step):
        target = sp_after(step)
        return send(
            g.modes.at[part, target],
            g.arrived.at[some_snaps(part), mode_rows(me_sp), :],
            (g.block_s, g.block_r),
            (which, part, step),
            at(me_snap, target),
        )

    def row_copy(which, part, step):
        target = sp_after(step)
        return send(
            g.turned.at[some_snaps(part), mode_rows(target), :],
            g.home.at[part, me_sp],
            (g.row_s, g.row_r),
            (which, part, step),
            at(me_snap, target),
        )

    def to_rows(which, part):
        for step in range(1, group):
            row_copy(which, part, step).start()
        g.home[part, me_sp] = g.turned[some_snaps(part), mode_rows(me_sp), :]

    def home_modes(which, part):
        for step in range(1, group):
            row_copy(which, part, step).wait_recv()
        count = g.gathered.shape[1]
        for block in range(group):
            g.gathered[part, :, block * owned : (block + 1) * owned] = (
                g.home[part, block].reshape(count, 128)[:, 0:owned].astype(f32)
            )
        g.home_low[part] = g.gathered[part].astype(low)

    loads["lon_f"].wait()
    for part in range(2):
        half_strips(first_norm, part)
        to_blocks(g.lon_f_in[...], 0, part)
    for part in range(2, 4):
        start_first(part)

    loads["filt"].wait()
    for weight, first in ((g.weight_one, 0), (g.weight_two, 2)):
        weight[...] = jnp.zeros_like(weight)
        real = g.filt_in[first].astype(low)
        imag = g.filt_in[first + 1].astype(low)
        weight[0:owned, 0:owned] = real
        weight[128 : 128 + owned, 128 : 128 + owned] = real
        weight[0:owned, 128 : 128 + owned] = imag
        weight[128 : 128 + owned, 0:owned] = -imag

    def bias_row(first):
        return jnp.concatenate(
            [g.own_small[first : first + 1, :], g.own_small[first + 1 : first + 2, :]], axis=1
        )

    for copy in cot_load:
        copy.wait()

    def flat_cot(rows):
        g.cot_in[rows, :] = columns_of("cot_cols", rows)

    strips(flat_cot)
    loads["lat_f"].wait()
    loads["lat_b"].wait()
    pairs = g.arrived.shape[1] // 2
    half_modes = half_snaps * pairs

    def mode_half(part):
        return slice(part * half_modes, (part + 1) * half_modes)

    def spectra(out, kind, part):
        for snap in range(part * half_snaps, (part + 1) * half_snaps):
            spectrum = dot_nn(g.lat_f_in[...], g.arrived[snap]).astype(kind)
            rows = slice(snap * pairs, (snap + 1) * pairs)
            out[rows, 0:128] = spectrum[0:pairs]
            out[rows, 128:256] = spectrum[pairs:]

    def grids(values, part):
        for index in range(half_snaps):
            rows = values[index * pairs : (index + 1) * pairs]
            rows = jnp.concatenate([rows[:, 0:128], rows[:, 128:256]], axis=0)
            g.turned[part * half_snaps + index] = dot_nn(g.lat_b_in[...], rows).astype(low)

    def keep_half():
        keep = jnp.concatenate([g.keep[...], g.keep[...]], axis=1)
        return jnp.concatenate([keep] * half_snaps, axis=0)

    for part in range(2):
        for step in range(1, group):
            block_copy(0, part, step).wait_recv()
        rows = mode_half(part)
        spectra(g.spectrum, low, part)
        g.pre_one[rows, :] = dot_nn(g.spectrum[rows, :], g.weight_one[...]) + bias_row(4)
        g.act_one[rows, :] = gelu_both(g.pre_one[rows, :])[0].astype(low)
        g.pre_two[rows, :] = dot_nn(g.act_one[rows, :], g.weight_two[...]) + bias_row(6)
        grids((shrink(g.pre_two[rows, :]) * keep_half()).astype(low), part)
        to_rows(0, part)
        pass_second(part)
    for part in range(4, parts):
        start_first(part)
    g.cot_turned[...] = g.cot_in[...].T
    for part in range(2):
        pass_third(part)

    loads["lon_i"].wait()

    def second_norm(rows):
        values = g.grid[rows, :]
        centred = values - jnp.mean(values, axis=-1, keepdims=True)
        scale = lax.rsqrt(jnp.mean(centred * centred, axis=-1, keepdims=True) + eps_norm)
        centred = centred * scale
        g.unit_two[rows, :] = centred.astype(low)
        g.scale_two[rows, :] = scale
        g.normed[rows, :] = (centred * g.gains[2:3, :] + g.gains[3:4, :]).astype(low)
        g.grid[rows, :] = values + g.gains[8:9, :]
        g.back[rows, :] = jnp.zeros((sub, channel), f32)

    for part in range(2):
        home_modes(0, part)
        g.grid[half_rows(part), :] += dot_nn(g.lon_i_in[...], g.home_low[part])
        half_strips(second_norm, part)
        pass_second(2 + part)
        pass_fourth(part)
    g.normed_turned[...] = g.normed[...].T
    for part in range(2, 4):
        pass_third(part)
    flat = jnp.concatenate([g.gains[9 + row : 10 + row, :] for row in range(rows_small - 9)], axis=1)
    for part in range(parts):
        g.bias[part] = flat[:, part * width : (part + 1) * width]

    def core_copy(part, matrix):
        slot = lax.rem(part, 2)
        return send(
            g.grads.at[slot, matrix, :, 1 - core],
            g.core_got.at[slot, matrix],
            (g.core_s, g.core_r),
            (slot, matrix),
            other_core,
        )

    places_one = (snap_low, snap_high)
    places_two = (snap_high, snap_low)
    beside_one = (beside_low, beside_high)
    beside_two = (beside_high, beside_low)
    place_last = (2 * snap_low + snap_high, me_snap)

    def half_copy(part, matrix):
        slot = lax.rem(part, 2)
        return send(
            g.half_out.at[slot, matrix, 1 - places_one[matrix]],
            g.half_got.at[slot, matrix],
            (g.half_s, g.half_r),
            (slot, matrix),
            at(beside_one[matrix], me_sp),
        )

    def quarter_copy(part, matrix):
        slot = lax.rem(part, 2)
        return send(
            g.quarter_out.at[slot, matrix, 1 - places_two[matrix]],
            g.quarter_got.at[slot, matrix],
            (g.quarter_s, g.quarter_r),
            (slot, matrix),
            at(beside_two[matrix], me_sp),
        )

    def level_copy(part, step):
        slot = lax.rem(part, 2)
        target = level_after(step)
        return send(
            g.level_out.at[slot, target],
            g.level_got.at[slot, level],
            (g.level_s, g.level_r),
            (slot, step),
            at(me_snap, 2 * target + core),
        )

    def last_copy(part, matrix, step):
        view = g.total.at[part, place_last[matrix], matrix]
        return send(
            view, view, (g.last_s, g.last_r), (part, matrix, step), at(snap_after(step), me_sp)
        )

    def half_stage(part):
        slot = lax.rem(part, 2)
        for matrix in range(2):

            @pl.when(part >= 2)
            def _(matrix=matrix):
                half_copy(part - 2, matrix).wait_send()

            core_copy(part, matrix).wait_recv()
            for row in range(levels):
                both = g.grads[slot, matrix, row, core].astype(f32) + g.core_got[
                    slot, matrix, row
                ].astype(f32)
                both = both.astype(low)
                g.half_out[slot, matrix, 0, row] = both[:, 0:half]
                g.half_out[slot, matrix, 1, row] = both[:, half:width]
            half_copy(part, matrix).start()

    def quarter_stage(part):
        slot = lax.rem(part, 2)
        for matrix in range(2):

            @pl.when(part >= 2)
            def _(matrix=matrix):
                quarter_copy(part - 2, matrix).wait_send()

            half_copy(part, matrix).wait_recv()
            for row in range(levels):
                both = g.half_out[slot, matrix, places_one[matrix], row].astype(f32) + g.half_got[
                    slot, matrix, row
                ].astype(f32)
                both = both.astype(low)
                g.quarter_out[slot, matrix, 0, row] = both[:, 0:quarter]
                g.quarter_out[slot, matrix, 1, row] = both[:, quarter:half]
            quarter_copy(part, matrix).start()

    def level_stage(part):
        slot = lax.rem(part, 2)

        @pl.when(part >= 2)
        def _():
            for step in range(1, levels):
                level_copy(part - 2, step).wait_send()

        for matrix in range(2):
            quarter_copy(part, matrix).wait_recv()
            for row in range(levels):
                both = g.quarter_out[slot, matrix, places_two[matrix], row].astype(
                    f32
                ) + g.quarter_got[slot, matrix, row].astype(f32)
                g.level_out[slot, row, matrix] = both.astype(low)
        for step in range(1, levels):
            level_copy(part, step).start()

    def last_stage(part):
        slot = lax.rem(part, 2)
        for step in range(1, levels):
            level_copy(part, step).wait_recv()
        for matrix in range(2):
            sums = g.level_out[slot, level, matrix].astype(f32)
            for step in range(1, levels):
                sums += g.level_got[slot, level_before(step), matrix].astype(f32)
            g.total[part, place_last[matrix], matrix] = sums.astype(low)
            for step in range(1, snaps):
                last_copy(part, matrix, step).start()

    def weight(part, matrix):
        return jnp.concatenate([g.all_w[part, matrix, place] for place in range(snaps)], axis=1)

    @pl.loop(0, parts)
    def _(part):
        slot = lax.rem(part, 2)

        @pl.when(part >= 3)
        def _():
            level_stage(part - 3)

        @pl.when(part + 4 < parts)
        def _():
            pass_second(part + 4)

        fourth_copy(part).wait_recv()
        g.grad_bias[part] = jnp.zeros(g.grad_bias.shape[1:], f32)

        @pl.loop(0, tokens // tile)
        def _(step):
            rows = pl.ds(pl.multiple_of(step * tile, tile), tile)
            act, slope = gelu_both(dot_nn(g.normed[rows, :], weight(part, 0)) + g.bias[part])
            act = act.astype(low)
            slope = (dot_nn(g.cot_in[rows, :], weight(part, 1)) * slope).astype(low)
            g.act[rows, :] = act
            g.slope[rows, :] = slope
            g.grad_bias[part] += fold(slope.astype(f32))
            g.grid[rows, :] += dot_nt(act, weight(part, 1))
            g.back[rows, :] += dot_nt(slope, weight(part, 0))

        @pl.when(part + 2 < parts)
        def _():
            pass_fourth(part + 2)

        @pl.when(part + 4 < parts)
        def _():
            pass_third(part + 4)

        @pl.when(part >= 3)
        def _():
            last_stage(part - 3)

        @pl.when(part >= 2)
        def _():
            quarter_stage(part - 2)

        @pl.when(part >= 1)
        def _():
            half_stage(part - 1)

        @pl.when(part >= 2)
        def _():
            for matrix in range(2):
                core_copy(part - 2, matrix).wait_send()

        shape = g.grads.shape[2:]
        g.grads[slot, 0] = dot_nn(g.normed_turned[...], g.slope[...]).astype(low).reshape(shape)
        core_copy(part, 0).start()
        g.grads[slot, 1] = dot_nn(g.cot_turned[...], g.act[...]).astype(low).reshape(shape)
        core_copy(part, 1).start()

    level_stage(parts - 3)

    g.folds[...] = jnp.zeros_like(g.folds)

    def second_back(rows):
        grad = g.back[rows, :]
        unit = g.unit_two[rows, :].astype(f32)
        cot = g.cot_in[rows, :].astype(f32)
        pulled = grad * g.gains[2:3, :]
        middle = jnp.mean(pulled, axis=-1, keepdims=True)
        slant = jnp.mean(pulled * unit, axis=-1, keepdims=True)
        total = cot + g.scale_two[rows, :] * (pulled - middle - unit * slant)
        g.back[rows, :] = total
        g.normed[rows, :] = total.astype(low)
        g.folds[2] += fold(grad * unit)
        g.folds[3] += fold(grad)
        g.folds[4] += fold(cot)

    loads["lon_it"].wait()
    for part in range(2):
        half_strips(second_back, part)
        for step in range(1, group):
            block_copy(0, part, step).wait_send()
        to_blocks(g.lon_it_in[...], 1, part)

    last_stage(parts - 3)
    quarter_stage(parts - 2)

    def low_out(rows):
        store_columns("fields_cols", rows, g.grid[rows, :].astype(low))

    strips(low_out)
    out_copies = column_copies(g.fields_cols, g.out, g.fields_sem, True)
    for copy in out_copies:
        copy.start()
    half_stage(parts - 1)
    loads["valid"].wait()
    loads["turn"].wait()
    weigh = sum(
        dot_nn(g.valid_in[:, row, :].astype(f32).astype(low), g.turn_in[row])
        for row in range(g.valid.shape[1])
    )
    places_each = weigh.shape[1]
    precise = lax.Precision.HIGHEST
    sums = [jnp.zeros((1, 128), f32), jnp.zeros((1, 128), f32)]
    for snap in range(g.valid.shape[0]):
        variables = g.grid[snap * places_each : (snap + 1) * places_each, 0:128]
        for index, value in enumerate((variables, variables * variables)):
            sums[index] += jnp.dot(
                weigh[snap : snap + 1, :], value, precision=precise, preferred_element_type=f32
            )

    def dot_tn(left, right):
        return lax.dot_general(
            left, right, (((0,), (0,)), ((), ())), preferred_element_type=f32
        )

    def filter_rows(first, grad):
        g.pair_grad[...] = grad
        real = g.pair_grad[0:128, 0:128] + g.pair_grad[128:256, 128:256]
        imag = g.pair_grad[0:128, 128:256] - g.pair_grad[128:256, 0:128]
        g.filt_out[me_snap, first] = real[0:owned].astype(low)
        g.filt_out[me_snap, first + 1] = imag[0:owned].astype(low)

    for part in range(2):
        for step in range(1, group):
            block_copy(1, part, step).wait_recv()
        rows = mode_half(part)
        spectra(g.grad_pre, f32, part)
        bend = jnp.tanh(g.pre_two[rows, :] / shrink_level)
        grad = (g.grad_pre[rows, :] * keep_half() * (bend * bend)).astype(low)
        g.grad_two[rows, :] = grad
        grad = dot_nt(grad, g.weight_two[...]) * gelu_both(g.pre_one[rows, :])[1]
        grad = grad.astype(low)
        g.grad_one[rows, :] = grad
        for step in range(1, group):
            row_copy(0, part, step).wait_send()
        grids(dot_nt(grad, g.weight_one[...]).astype(low), part)
        to_rows(1, part)
    level_stage(parts - 2)
    quarter_stage(parts - 1)
    bias_one = jnp.sum(g.grad_one[...].astype(f32), axis=0, keepdims=True)
    bias_two = jnp.sum(g.grad_two[...].astype(f32), axis=0, keepdims=True)
    filter_rows(2, dot_tn(g.act_one[...], g.grad_two[...]))
    filter_rows(0, dot_tn(g.spectrum[...], g.grad_one[...]))

    def filter_copy(step):
        view = g.filt_out.at[me_snap]
        return send(view, view, (g.filt_s, g.filt_r), step, at(snap_after(step), me_sp))

    for step in range(1, snaps):
        filter_copy(step).start()

    last_stage(parts - 2)
    level_stage(parts - 1)

    loads["lon_ft"].wait()
    strip_pairs = strip // g.fields.shape[1]
    grad_view = g.grad_cols.reshape(2, tiles, strip, 128)

    def grad_copies(place, slot):
        pairs_out = pl.ds(place * strip_pairs, strip_pairs)
        return column_copies(
            g.grad_cols.at[slot], g.in_grad.at[pairs_out], g.grad_sem.at[slot], True
        )

    steps = half_tokens // strip
    for part in range(2):
        home_modes(1, part)
        g.grid[half_rows(part), :] = g.back[half_rows(part), :] + dot_nn(
            g.lon_ft_in[...], g.home_low[part]
        )

        @pl.loop(0, steps)
        def _(step):
            place = part * steps + step
            slot = lax.rem(place, 2)

            @pl.when(place >= 2)
            def _():
                for copy in grad_copies(place, slot):
                    copy.wait()

            for at_row in range(0, strip, sub):
                rows = pl.ds(pl.multiple_of(place * strip + at_row, 16), sub)
                grad = g.grid[rows, :]
                unit = g.unit_one[rows, :].astype(f32)
                pulled = grad * g.gains[0:1, :]
                middle = jnp.mean(pulled, axis=-1, keepdims=True)
                slant = jnp.mean(pulled * unit, axis=-1, keepdims=True)
                total = g.back[rows, :] + g.scale_one[rows, :] * (pulled - middle - unit * slant)
                for tile_at in range(tiles):
                    grad_view[slot, tile_at, at_row : at_row + sub, :] = total[
                        :, tile_at * 128 : (tile_at + 1) * 128
                    ]
                g.folds[0] += fold(grad * unit)
                g.folds[1] += fold(grad)
            for copy in grad_copies(place, slot):
                copy.start()

    g.grad_rows[...] = jnp.zeros_like(g.grad_rows)
    for index, row in enumerate((0, 1, 2, 3, 8)):
        g.grad_rows[row : row + 1, :] = jnp.sum(g.folds[index], axis=0, keepdims=True)
    flat = jnp.concatenate(
        [jnp.sum(g.grad_bias[part], axis=0, keepdims=True) for part in range(parts)], axis=1
    )
    for row in range(rows_small - 9):
        g.grad_rows[9 + row : 10 + row, :] = flat[:, row * channel : (row + 1) * channel]
    for block in range(group):
        g.tiles[block] = jnp.zeros(g.tiles.shape[1:], f32)
        g.tiles[block, :, 0:owned] = g.grad_rows[:, block * owned : (block + 1) * owned]
        g.tiles[block, 13:14, :] = sums[0]
        g.tiles[block, 14:15, :] = sums[1]

    def tile_copy(step):
        target = sp_after(step)
        return send(
            g.tiles.at[target], g.tiles_got.at[me_sp], (g.tile_s, g.tile_r), step, at(me_snap, target)
        )

    def snap_tile_copy(step):
        view = g.snap_tiles.at[me_snap]
        return send(view, view, (g.snap_tile_s, g.snap_tile_r), step, at(snap_after(step), me_sp))

    for step in range(1, group):
        tile_copy(step).start()
    last_stage(parts - 1)

    g.tiles_got[me_sp] = g.tiles[me_sp]
    for step in range(1, group):
        tile_copy(step).wait_recv()
    tile_sum = g.tiles_got[0]
    for sp in range(1, group):
        tile_sum += g.tiles_got[sp]
    g.snap_tiles[me_snap] = tile_sum
    g.snap_tiles[me_snap, 4:5, :] = bias_one[:, 0:128]
    g.snap_tiles[me_snap, 5:6, :] = bias_one[:, 128:256]
    g.snap_tiles[me_snap, 6:7, :] = bias_two[:, 0:128]
    g.snap_tiles[me_snap, 7:8, :] = bias_two[:, 128:256]
    for step in range(1, snaps):
        snap_tile_copy(step).start()

    for step in range(1, snaps):
        filter_copy(step).wait_recv()
    filter_sum = g.filt_out[0].astype(f32)
    for snap in range(1, snaps):
        filter_sum += g.filt_out[snap].astype(f32)
    g.grad_filt[...] = filter_sum
    for part in range(parts):
        for matrix in range(2):
            for step in range(1, snaps):
                last_copy(part, matrix, step).wait_recv()
    grads_out = pltpu.make_async_copy(g.total, g.grad_mlp, g.load_sem.at[3])
    grads_out.start()
    for step in range(1, snaps):
        snap_tile_copy(step).wait_recv()
    tile_sum = g.snap_tiles[0]
    for snap in range(1, snaps):
        tile_sum += g.snap_tiles[snap]
    g.grad_small[...] = tile_sum

    grads_out.wait()
    for copy in out_copies:
        copy.wait()
    for slot in range(2):
        for copy in grad_copies(0, slot):
            copy.wait()
    for step in range(1, group):
        small_copy(step).wait_send()
        for part in range(2):
            block_copy(1, part, step).wait_send()
            row_copy(1, part, step).wait_send()
        tile_copy(step).wait_send()
        for part in range(parts):
            first_copy(part, step).wait_send()
    for part in range(parts):
        second_copy(part).wait_send()
        third_copy(part).wait_send()
        fourth_copy(part).wait_send()
    for part in (parts - 2, parts - 1):
        for matrix in range(2):
            core_copy(part, matrix).wait_send()
            half_copy(part, matrix).wait_send()
            quarter_copy(part, matrix).wait_send()
        for step in range(1, levels):
            level_copy(part, step).wait_send()
    for step in range(1, snaps):
        filter_copy(step).wait_send()
        snap_tile_copy(step).wait_send()
        for part in range(parts):
            for matrix in range(2):
                last_copy(part, matrix, step).wait_send()


def block_pass(fields, cot, valid, kept, mlp, filt, small, snaps, group):
    snap_local, row_local, lon_total, channel = fields.shape
    tokens = snap_local * row_local * lon_total
    hidden = mlp.shape[2]
    lat_total = row_local * group
    modes = kept.shape[1] * group
    owned = channel // group
    width = 512
    parts = hidden // width
    levels = group // 2
    quarter = width // snaps
    low, f32 = jnp.bfloat16, jnp.float32
    half = width // 2
    half_snaps = snap_local // 2
    lon_f, lon_i = lon_matrix(lon_total, modes, half_snaps, row_local)

    def paired(array):
        return jnp.transpose(array, (0, 2, 1, 3)).reshape(-1, row_local, channel)

    lat_f = lat_matrix(lat_total, modes)
    pair = 2 * modes * row_local
    spread = half_snaps * row_local * 2 * modes
    inputs = dict(
        small=small,
        kept=kept.T,
        fields=paired(fields),
        lon_f=jnp.asarray(np.ascontiguousarray(lon_f.T)),
        filt=filt,
        lat_f=jnp.asarray(lat_f),
        lat_b=jnp.asarray(np.ascontiguousarray(lat_f.T)),
        cot=paired(cot),
        lon_i=jnp.asarray(lon_i),
        valid=valid,
        turn=jnp.asarray(lon_turn(lon_total, row_local)),
        lon_it=jnp.asarray(np.ascontiguousarray(lon_i.T)),
        lon_ft=jnp.asarray(lon_f),
        mlp=mlp,
    )
    outputs = dict(
        out=jax.ShapeDtypeStruct((tokens // row_local, row_local, channel), low),
        in_grad=jax.ShapeDtypeStruct((tokens // row_local, row_local, channel), f32),
        grad_mlp=jax.ShapeDtypeStruct((parts, snaps, 2, owned, quarter), low),
        grad_filt=jax.ShapeDtypeStruct((4, owned, 128), f32),
        grad_small=jax.ShapeDtypeStruct((16, 128), f32),
    )
    vmem = pltpu.VMEM
    dma = pltpu.SemaphoreType.DMA
    scratch = {
        name + "_in": vmem(value.shape, value.dtype)
        for name, value in inputs.items()
        if name not in ("mlp", "fields", "cot")
    }
    tiles = channel // 128
    cols = (tiles, tokens // row_local, row_local, 128)
    strip = divisor(tokens // 2, 48, 144)
    scratch |= dict(
        mlp_part=vmem((2, 2, owned, width), f32),
        fields_cols=vmem(cols, low),
        cot_cols=vmem(cols, low),
        grad_cols=vmem((2, tiles, strip // row_local, row_local, 128), f32),
        grad_sem=dma((2, tiles)),
        fields_sem=dma((tiles,)),
        cot_sem=dma((tiles,)),
        cot_in=vmem((tokens, channel), low),
        grid=vmem((tokens, channel), f32),
        back=vmem((tokens, channel), f32),
        normed=vmem((tokens, channel), low),
        normed_turned=vmem((channel, tokens), low),
        cot_turned=vmem((channel, tokens), low),
        unit_one=vmem((tokens, channel), low),
        unit_two=vmem((tokens, channel), low),
        scale_one=vmem((tokens, 1), f32),
        scale_two=vmem((tokens, 1), f32),
        own_small=vmem((16 + kept.shape[0], 128), f32),
        all_small=vmem((group, 16 + kept.shape[0], 128), f32),
        gains=vmem((16, channel), f32),
        keep=vmem((lat_total * modes, 128), f32),
        own_w=vmem((parts, 2, snaps, owned, quarter), low),
        all_w=vmem((parts, 2, snaps, channel, quarter), low),
        modes=vmem((2, group, half_snaps, pair, 128), low),
        arrived=vmem((snap_local, pair * group, 128), low),
        turned=vmem((snap_local, pair * group, 128), low),
        home=vmem((2, group, half_snaps, pair, 128), low),
        gathered=vmem((2, spread, channel), f32),
        home_low=vmem((2, spread, channel), low),
        weight_one=vmem((256, 256), low),
        weight_two=vmem((256, 256), low),
        spectrum=vmem((snap_local * lat_total * modes, 256), low),
        pre_one=vmem((snap_local * lat_total * modes, 256), f32),
        act_one=vmem((snap_local * lat_total * modes, 256), low),
        pre_two=vmem((snap_local * lat_total * modes, 256), f32),
        grad_pre=vmem((snap_local * lat_total * modes, 256), f32),
        grad_two=vmem((snap_local * lat_total * modes, 256), low),
        grad_one=vmem((snap_local * lat_total * modes, 256), low),
        folds=vmem((5, 8, channel), f32),
        pair_grad=vmem((256, 256), f32),
        act=vmem((tokens, width), low),
        slope=vmem((tokens, width), low),
        bias=vmem((parts, 1, width), f32),
        grad_bias=vmem((parts, 8, width), f32),
        grad_rows=vmem((16, channel), f32),
        grads=vmem((2, 2, levels, 2, owned, width), low),
        core_got=vmem((2, 2, levels, owned, width), low),
        half_out=vmem((2, 2, 2, levels, owned, half), low),
        half_got=vmem((2, 2, levels, owned, half), low),
        quarter_out=vmem((2, 2, 2, levels, owned, quarter), low),
        quarter_got=vmem((2, 2, levels, owned, quarter), low),
        level_out=vmem((2, levels, 2, owned, quarter), low),
        level_got=vmem((2, levels, 2, owned, quarter), low),
        total=vmem((parts, snaps, 2, owned, quarter), low),
        filt_out=vmem((snaps, 4, owned, 128), low),
        tiles=vmem((group, 16, 128), f32),
        tiles_got=vmem((group, 16, 128), f32),
        snap_tiles=vmem((snaps, 16, 128), f32),
        load_sem=dma((len(inputs) + 1,)),
    )
    for name, shape in dict(
        small=(group,),
        first=(parts, group),
        second=(parts,),
        third=(parts,),
        fourth=(parts,),
        block=(2, 2, group),
        row=(2, 2, group),
        core=(2, 2),
        half=(2, 2),
        quarter=(2, 2),
        level=(2, levels),
        last=(parts, 2, snaps),
        filt=(snaps,),
        tile=(group,),
        snap_tile=(snaps,),
    ).items():
        scratch[name + "_s"] = dma(shape)
        scratch[name + "_r"] = dma(shape)
    names = [*inputs, *outputs, *scratch]
    far = pl.BlockSpec(memory_space=pl.ANY)
    near = pl.BlockSpec(memory_space=pltpu.VMEM)
    results = pl.pallas_call(
        functools.partial(block_body, names, (snaps, group, parts, width)),
        in_specs=[far] * len(inputs),
        out_specs=[far, far, far, near, near],
        out_shape=list(outputs.values()),
        scratch_shapes=list(scratch.values()),
        compiler_params=pltpu.CompilerParams(
            collective_id=0, has_side_effects=True, vmem_limit_bytes=VMEM_LIMIT
        ),
        cost_estimate=pl.CostEstimate(
            flops=12 * tokens * channel * hidden,
            bytes_accessed=4 * hidden * channel,
            transcendentals=tokens * hidden,
        ),
        name="block_pass",
    )(*inputs.values())
    return results


def step_body(names, positions, *refs):
    g = Refs()
    for name, ref in zip(names, refs, strict=True):
        setattr(g, name, ref)
    parts, snaps = g.grad_mlp.shape[:2]
    quarter = g.grad_mlp.shape[4]
    width = snaps * quarter
    moments = ("w", "m", "v")
    results = ("new", "first", "second", "copy")

    pieces = g.far_sem.shape[2]
    ends = ((g.out, g.out_near, g.out_o), (g.in_grad, g.in_grad_near, g.in_grad_o))

    def passing(kind, piece, leg):
        size = ends[kind][0].shape[0] // pieces
        rows = pl.ds(piece * size, size)
        return pltpu.make_async_copy(
            ends[kind][leg].at[rows], ends[kind][leg + 1].at[rows], g.far_sem.at[leg, kind, piece]
        )

    through = [(kind, piece) for kind in range(2) for piece in range(pieces)]

    def part_cols(part):
        return pl.ds(part * width, width)

    def load(part):
        near = [
            pltpu.make_async_copy(
                getattr(g, "mlp_" + kind).at[:, :, part_cols(part)],
                g.near.at[index, part],
                g.near_sem.at[index, part],
            )
            for index, kind in enumerate(moments)
        ]
        near.append(
            pltpu.make_async_copy(g.grad_mlp.at[part], g.grad_near.at[part], g.near_sem.at[3, part])
        )
        return near

    def store(part):
        copies = [
            pltpu.make_async_copy(
                g.near.at[index, part],
                getattr(g, "mlp_" + kind).at[:, :, part_cols(part)],
                g.back_sem.at[index, part],
            )
            for index, kind in enumerate(results[:3])
        ]
        copies.append(
            pltpu.make_async_copy(
                g.low_near.at[part], g.mlp_copy.at[:, :, part_cols(part)], g.back_sem.at[3, part]
            )
        )
        return copies

    coming = [load(part) for part in range(parts)]
    going = [store(part) for part in range(parts)]
    for part in range(parts):
        for copy in coming[part]:
            copy.start()
    for each in through:
        passing(*each, 0).start()

    def put(prefix, values):
        for kind, value in zip(results, values, strict=True):
            getattr(g, prefix + kind)[...] = value

    owned = g.filt_w.shape[2]
    put(
        "filt_",
        adamw(g.filt_w[...], g.filt_m[...], g.filt_v[...], g.grad_filt[:, :, 0:owned], rate_filter),
    )
    rows = g.small_w.shape[0]
    put(
        "small_",
        adamw(
            g.small_w[...], g.small_m[...], g.small_v[...], g.grad_small[0:rows, 0:owned], rate_small
        ),
    )
    totals = g.grad_small[rows : rows + 2, 0 : g.run.shape[1]]
    g.stats[...] = stat_decay * g.run[...] + (1.0 - stat_decay) * totals / positions

    for part in range(parts):
        for copy in coming[part]:
            copy.wait()

        for snap in range(snaps):
            cols = slice(snap * quarter, (snap + 1) * quarter)
            where = (slice(None), slice(None), cols)
            now = [g.near[(index, part, *where)] for index in range(3)]
            grad = g.grad_near[part, snap].astype(jnp.float32)
            values = adamw(*now, grad, rate_mlp)
            for index in range(3):
                g.near[(index, part, *where)] = values[index]
            g.low_near[(part, *where)] = values[3]
        for copy in going[part]:
            copy.start()
    for each in through:
        passing(*each, 0).wait()
        passing(*each, 1).start()
    for each in through:
        passing(*each, 1).wait()
    for part in range(parts):
        for copy in going[part]:
            copy.wait()


def step_pass(shown, grads, masters, run_stats, positions):
    grad_mlp, grad_filt, grad_small = grads
    mlp, filt, small = masters
    parts = grad_mlp.shape[0]
    width = mlp[0].shape[2] // parts
    f32, low = jnp.float32, jnp.bfloat16
    far = pl.BlockSpec(memory_space=pltpu.HBM)
    near = pl.BlockSpec(memory_space=pltpu.VMEM)
    inputs = dict(out=shown[0], in_grad=shown[1], grad_mlp=grad_mlp)
    inputs |= dict(zip(("mlp_w", "mlp_m", "mlp_v"), mlp, strict=True))
    far_in = len(inputs)
    inputs |= dict(grad_filt=grad_filt, grad_small=grad_small)
    inputs |= dict(zip(("filt_w", "filt_m", "filt_v"), filt, strict=True))
    inputs |= dict(zip(("small_w", "small_m", "small_v"), small, strict=True))
    inputs |= dict(run=run_stats)
    results = (("new", f32), ("first", f32), ("second", f32), ("copy", low))
    outputs = {
        name + "_o": jax.ShapeDtypeStruct(array.shape, array.dtype)
        for name, array in zip(("out", "in_grad"), shown, strict=True)
    }
    outputs |= {"mlp_" + kind: jax.ShapeDtypeStruct(mlp[0].shape, dt) for kind, dt in results}
    far_out = len(outputs)
    outputs |= {"filt_" + kind: jax.ShapeDtypeStruct(filt[0].shape, dt) for kind, dt in results}
    outputs |= {"small_" + kind: jax.ShapeDtypeStruct(small[0].shape, dt) for kind, dt in results}
    outputs |= dict(stats=jax.ShapeDtypeStruct(run_stats.shape, f32))
    scratch = dict(
        near=pltpu.VMEM((3, parts, 2, mlp[0].shape[1], width), f32),
        grad_near=pltpu.VMEM(grad_mlp.shape, low),
        low_near=pltpu.VMEM((parts, 2, mlp[0].shape[1], width), low),
        near_sem=pltpu.SemaphoreType.DMA((4, parts)),
        back_sem=pltpu.SemaphoreType.DMA((4, parts)),
        out_near=pltpu.VMEM(shown[0].shape, low),
        in_grad_near=pltpu.VMEM(shown[1].shape, f32),
        far_sem=pltpu.SemaphoreType.DMA((2, 2, divisor(shown[0].shape[0], 1, 4))),
    )
    return pl.pallas_call(
        functools.partial(step_body, [*inputs, *outputs, *scratch], positions),
        in_specs=[far] * far_in + [near] * (len(inputs) - far_in),
        out_specs=[far] * far_out + [near] * (len(outputs) - far_out),
        out_shape=list(outputs.values()),
        scratch_shapes=list(scratch.values()),
        compiler_params=pltpu.CompilerParams(vmem_limit_bytes=VMEM_LIMIT),
        name="step_pass",
    )(*inputs.values())


def per_device_blocks(
    fields,
    cotangent,
    valid_mask,
    kept_modes,
    mlp_master,
    mlp_first,
    mlp_second,
    filter_master,
    filter_first,
    filter_second,
    small_master,
    small_first,
    small_second,
    run_stats,
):
    snaps, group = lax.axis_size("snap"), lax.axis_size("sp")
    out, in_grad, *grads = block_pass(
        fields, cotangent, valid_mask, kept_modes, mlp_master, filter_master, small_master, snaps, group
    )
    snap_local, row_local, lon_total, channel = fields.shape
    positions = snap_local * snaps * row_local * group * lon_total
    out, in_grad, *stepped = step_pass(
        (out, in_grad),
        grads,
        (
            (mlp_master, mlp_first, mlp_second),
            (filter_master, filter_first, filter_second),
            (small_master, small_first, small_second),
        ),
        run_stats,
        positions,
    )
    rows_apart = (snap_local, lon_total, row_local, channel)
    out, in_grad = [
        jnp.transpose(array.reshape(rows_apart), (0, 2, 1, 3)) for array in (out, in_grad)
    ]
    return (out, in_grad, *stepped)


def per_device(*arrays):
    group, snaps = lax.axis_size("sp"), lax.axis_size("snap")
    channel, hidden = arrays[0].shape[3], arrays[4].shape[2]
    by_block = group == BLOCKS and snaps == 4 and arrays[3].shape[1] == 1
    if by_block and hidden % 512 == 0 and channel // group <= 128 and channel % (16 * group) == 0:
        return per_device_blocks(*arrays)
    return per_device_modes(*arrays)


def solution(mesh):
    return jax.shard_map(
        per_device,
        mesh=mesh,
        in_specs=(
            P("snap", "sp", None, None),
            P("snap", "sp", None, None),
            P("snap", "sp", None),
            P(None, "sp"),
            P(None, "sp", None),
            P(None, "sp", None),
            P(None, "sp", None),
            P(None, "sp", None),
            P(None, "sp", None),
            P(None, "sp", None),
            P(None, "sp"),
            P(None, "sp"),
            P(None, "sp"),
            P(),
        ),
        out_specs=(
            P("snap", "sp", None, None),
            P("snap", "sp", None, None),
            P(None, "sp", None),
            P(None, "sp", None),
            P(None, "sp", None),
            P(None, "sp", None),
            P(None, "sp", None),
            P(None, "sp", None),
            P(None, "sp", None),
            P(None, "sp", None),
            P(None, "sp"),
            P(None, "sp"),
            P(None, "sp"),
            P(None, "sp"),
            P(),
        ),
        check_vma=False,
    )
```

```python
import functools
import math

import jax
import jax.numpy as jnp
import ml_dtypes
import numpy as np
from jax import lax
from jax.experimental import pallas as pl
from jax.experimental.pallas import tpu as pltpu
from jax.sharding import PartitionSpec as P

BLOCKS = 8
NVAR = 20
STEP = 10
VMEM_LIMIT = 63 * 1024 * 1024


eps_norm = 1e-06
shrink_level = 0.01
beta_one = 0.5
beta_two = 0.5
adam_eps = 1e-08
decay_rate = 0.01
rate_mlp = 0.03
rate_filter = 0.1
rate_small = 0.2
stat_decay = 0.5


def layer_norm(values, gain_vec, shift_vec):
    centred = values - jnp.mean(values, axis=-1, keepdims=True)
    spread = jnp.mean(centred * centred, axis=-1, keepdims=True)
    return centred * lax.rsqrt(spread + eps_norm) * gain_vec + shift_vec


def shrink(values):
    return values - shrink_level * jnp.tanh(values / shrink_level)


def lon_tables(lon_total, mode_total):
    places = jnp.arange(lon_total, dtype=jnp.int32)
    orders = jnp.arange(mode_total, dtype=jnp.int32)
    angles = (places[:, None] * orders[None, :] % lon_total).astype(jnp.float32) * (
        2.0 * math.pi / lon_total
    )
    scaling = 1.0 / math.sqrt(lon_total)
    forward_tab = jnp.stack([jnp.cos(angles), -jnp.sin(angles)], axis=1) * scaling
    doubling = jnp.where(orders == 0, 1.0, 2.0).astype(jnp.float32)[:, None]
    inverse_tab = (
        jnp.stack([jnp.cos(angles).T * doubling, -jnp.sin(angles).T * doubling], axis=0) * scaling
    )
    return (forward_tab.astype(jnp.bfloat16), inverse_tab.astype(jnp.bfloat16))


def lat_table(lat_total):
    places = jnp.arange(lat_total, dtype=jnp.int32)
    angles = (places[:, None] * places[None, :] % lat_total).astype(jnp.float32) * (
        2.0 * math.pi / lat_total
    )
    cosine = jnp.cos(angles)
    sine_part = jnp.sin(angles)
    upper_rows = jnp.stack([cosine, sine_part], axis=1)
    bottom = jnp.stack([-sine_part, cosine], axis=1)
    return (jnp.stack([upper_rows, bottom], axis=0) / math.sqrt(lat_total)).astype(jnp.bfloat16)


def complex_pair(real_part, imag_part):
    return jnp.stack([jnp.stack([real_part, -imag_part]), jnp.stack([imag_part, real_part])])


gelu_scale = math.sqrt(2.0 / math.pi)
gelu_cubic = 0.044715


def gelu_both(value):
    bend = (gelu_scale * gelu_cubic) * (value * value)
    turn = jnp.tanh(value * (gelu_scale + bend))
    half = 0.5 + 0.5 * turn
    slope = half * (1.0 + (value * (1.0 - turn)) * (gelu_scale + 3.0 * bend))
    return value * half, slope


def dot_nt(left, right):
    return lax.dot_general(
        left, right, (((1,), (1,)), ((), ())), preferred_element_type=jnp.float32
    )


def dot_nn(left, right):
    return jnp.dot(left, right, preferred_element_type=jnp.float32)


def divisor(total, unit, most):
    return max(size for size in range(unit, most + 1, unit) if total % size == 0)


def mlp_body(
    tile,
    normed_ref,
    cot_ref,
    up_ref,
    down_ref,
    bias_ref,
    out_ref,
    back_ref,
    grad_up_ref,
    grad_down_ref,
    grad_bias_ref,
    normed_turned,
    cot_turned,
    act_ref,
    slope_ref,
):
    tokens = normed_ref.shape[0]

    @pl.when(pl.program_id(0) == 0)
    def _():
        normed_turned[...] = normed_ref[...].T
        cot_turned[...] = cot_ref[...].T
        out_ref[...] = jnp.zeros_like(out_ref)
        back_ref[...] = jnp.zeros_like(back_ref)

    grad_bias_ref[...] = jnp.zeros_like(grad_bias_ref)

    @pl.loop(0, tokens // tile)
    def _(step):
        rows = pl.ds(pl.multiple_of(step * tile, tile), tile)
        act, slope = gelu_both(dot_nn(normed_ref[rows, :], up_ref[...]) + bias_ref[...])
        act = act.astype(jnp.bfloat16)
        slope = (dot_nn(cot_ref[rows, :], down_ref[...]) * slope).astype(jnp.bfloat16)
        act_ref[rows, :] = act
        slope_ref[rows, :] = slope
        grad_bias_ref[...] += jnp.sum(slope.astype(jnp.float32), axis=0, keepdims=True)
        out_ref[rows, :] += dot_nt(act, down_ref[...])
        back_ref[rows, :] += dot_nt(slope, up_ref[...])

    grad_up_ref[...] = dot_nn(normed_turned[...], slope_ref[...]).astype(grad_up_ref.dtype)
    grad_down_ref[...] = dot_nn(cot_turned[...], act_ref[...]).astype(grad_down_ref.dtype)


def mlp_pass(normed, cot, weights, bias):
    tokens, channel = normed.shape
    hidden = weights.shape[2]
    width = divisor(hidden, 128, 512)
    tile = divisor(tokens, 16, 480)
    whole = pl.BlockSpec((tokens, channel), lambda j: (0, 0))
    block = pl.BlockSpec((channel, width), lambda j: (0, j))
    line = pl.BlockSpec((1, width), lambda j: (0, j))
    part = lambda which: pl.BlockSpec((None, channel, width), lambda j: (which, 0, j))
    total = jax.ShapeDtypeStruct((tokens, channel), jnp.float32)
    grads = jax.ShapeDtypeStruct((channel, hidden), jnp.bfloat16)
    return pl.pallas_call(
        functools.partial(mlp_body, tile),
        grid=(hidden // width,),
        in_specs=[whole, whole, part(0), part(1), line],
        out_specs=[whole, whole, block, block, line],
        out_shape=[total, total, grads, grads, jax.ShapeDtypeStruct((1, hidden), jnp.float32)],
        scratch_shapes=[
            pltpu.VMEM((channel, tokens), jnp.bfloat16),
            pltpu.VMEM((channel, tokens), jnp.bfloat16),
            pltpu.VMEM((tokens, width), jnp.bfloat16),
            pltpu.VMEM((tokens, width), jnp.bfloat16),
        ],
        compiler_params=pltpu.CompilerParams(vmem_limit_bytes=56 * 1024 * 1024),
        cost_estimate=pl.CostEstimate(
            flops=12 * tokens * channel * hidden,
            bytes_accessed=8 * channel * hidden + 12 * tokens * channel,
            transcendentals=tokens * hidden,
        ),
        name="mlp_pass",
    )(normed, cot, weights, weights, bias)


def spectral_front(arrived, lat_fwd, first_pair, second_pair, bias_one, bias_two):
    spectrum = jnp.einsum(
        "pkqr,nrqmd->nkpmd", lat_fwd, arrived, preferred_element_type=jnp.float32
    ).astype(jnp.bfloat16)
    snap_local, lat_total, pair_count, mode_local, channel = spectrum.shape
    blocked = spectrum.reshape(
        snap_local, lat_total, pair_count, mode_local, BLOCKS, channel // BLOCKS
    )
    pre_one = (
        jnp.einsum("nkqmbi,pqbio->nkpmbo", blocked, first_pair, preferred_element_type=jnp.float32)
        + bias_one
    )
    act_one = jax.nn.gelu(pre_one).astype(jnp.bfloat16)
    pre_two = (
        jnp.einsum("nkqmbi,pqbio->nkpmbo", act_one, second_pair, preferred_element_type=jnp.float32)
        + bias_two
    )
    return (blocked, pre_one, act_one, pre_two)


def adamw(master, first_mom, second_mom, gradient, step_rate):
    first_next = beta_one * first_mom + (1.0 - beta_one) * gradient
    second_next = beta_two * second_mom + (1.0 - beta_two) * gradient * gradient
    fix_one = 1.0 - beta_one**STEP
    fix_two = 1.0 - beta_two**STEP
    direction = first_next / fix_one / (jnp.sqrt(second_next / fix_two) + adam_eps)
    master_next = master - step_rate * (direction + decay_rate * master)
    return (master_next, first_next, second_next, master_next.astype(jnp.bfloat16))


def per_device_modes(
    fields,
    cotangent,
    valid_mask,
    kept_modes,
    mlp_master,
    mlp_first,
    mlp_second,
    filter_master,
    filter_first,
    filter_second,
    small_master,
    small_first,
    small_second,
    run_stats,
):
    group_size = lax.axis_size("sp")
    snap_local, row_local, lon_total, channel = fields.shape
    lat_total = row_local * group_size
    mode_local = kept_modes.shape[1]
    mode_total = mode_local * group_size
    block_width = channel // BLOCKS
    lon_fwd, lon_inv = lon_tables(lon_total, mode_total)
    lat_fwd = lat_table(lat_total)
    mlp_w, filt_w, small_w = (
        lax.all_gather(mlp_master.astype(jnp.bfloat16), "sp", axis=1, tiled=True),
        lax.all_gather(filter_master.astype(jnp.bfloat16), "sp", axis=1, tiled=True),
        lax.all_gather(small_master.astype(jnp.bfloat16), "sp", axis=1, tiled=True),
    )
    small_f = small_w.astype(jnp.float32)
    weights = filt_w.reshape(4, BLOCKS, block_width, block_width)
    first_pair = complex_pair(weights[0], weights[1])
    second_pair = complex_pair(weights[2], weights[3])
    bias_one = small_f[4:6].reshape(2, 1, BLOCKS, block_width)
    bias_two = small_f[6:8].reshape(2, 1, BLOCKS, block_width)
    fields_float = fields.astype(jnp.float32)
    normed, norm_pull = jax.vjp(layer_norm, fields_float, small_f[0], small_f[1])
    normed_low = normed.astype(jnp.bfloat16)
    spec_lon = jnp.einsum(
        "nrld,lqm->nrqmd", normed_low, lon_fwd, preferred_element_type=jnp.float32
    ).astype(jnp.bfloat16)
    arrived = lax.all_to_all(spec_lon, "sp", split_axis=3, concat_axis=1, tiled=True)
    spectral = spectral_front(arrived, lat_fwd, first_pair, second_pair, bias_one, bias_two)
    keep_mask = kept_modes.astype(jnp.float32)[None, :, None, :, None, None]
    masked = (shrink(spectral[3]) * keep_mask).astype(jnp.bfloat16)
    masked = masked.reshape(snap_local, lat_total, 2, mode_local, channel)
    returned = jnp.einsum(
        "pkqr,nkpmd->nrqmd", lat_fwd, masked, preferred_element_type=jnp.float32
    ).astype(jnp.bfloat16)
    home_modes = lax.all_to_all(returned, "sp", split_axis=1, concat_axis=3, tiled=True)
    filtered = jnp.einsum(
        "nrqmd,qml->nrld", home_modes, lon_inv, preferred_element_type=jnp.float32
    )
    mixture = fields_float + normed + filtered
    normed_two, norm_two_pull = jax.vjp(layer_norm, mixture, small_f[2], small_f[3])
    normed_two_low = normed_two.astype(jnp.bfloat16)
    tokens = snap_local * row_local * lon_total
    passed = mlp_pass(
        normed_two_low.reshape(tokens, channel),
        cotangent.reshape(tokens, channel),
        mlp_w,
        small_f[9:].reshape(1, -1),
    )
    output = mixture + passed[0].reshape(mixture.shape) + small_f[8]
    weight_mask = valid_mask.astype(jnp.float32)[..., None]
    variables = output[..., :NVAR]
    local_sums = jnp.stack(
        [
            jnp.sum(weight_mask * variables, axis=(0, 1, 2)),
            jnp.sum(weight_mask * variables * variables, axis=(0, 1, 2)),
        ]
    )
    total_sums = lax.psum(local_sums, ("snap", "sp"))
    positions = snap_local * lax.axis_size("snap") * lat_total * lon_total
    stats_new = stat_decay * run_stats + (1.0 - stat_decay) * total_sums / positions
    cot_float = cotangent.astype(jnp.float32)
    grad_normed_two = passed[1].reshape(mixture.shape)
    grad_bias_hidden = passed[4]
    grad_mix_norm, grad_gain_two, grad_shift_two = norm_two_pull(grad_normed_two)
    grad_mixture = cot_float + grad_mix_norm
    grad_bias_out = jnp.sum(cot_float, axis=(0, 1, 2))
    grad_filtered = grad_mixture.astype(jnp.bfloat16)
    grad_home = jnp.einsum(
        "nrld,qml->nrqmd", grad_filtered, lon_inv, preferred_element_type=jnp.float32
    ).astype(jnp.bfloat16)
    grad_returned = lax.all_to_all(grad_home, "sp", split_axis=3, concat_axis=1, tiled=True)
    grad_masked = jnp.einsum(
        "pkqr,nrqmd->nkpmd", lat_fwd, grad_returned, preferred_element_type=jnp.float32
    )
    arrived_again = lax.all_to_all(spec_lon, "sp", split_axis=3, concat_axis=1, tiled=True)
    used_front = spectral_front(arrived_again, lat_fwd, first_pair, second_pair, bias_one, bias_two)
    blocked, pre_one, act_one, pre_two = used_front
    grad_two = jax.vjp(shrink, pre_two)[1](grad_masked.reshape(pre_two.shape) * keep_mask)[
        0
    ].astype(jnp.bfloat16)
    grad_bias_two = jnp.sum(grad_two.astype(jnp.float32), axis=(0, 1, 3))
    grad_second = jnp.einsum(
        "nkqmbi,nkpmbo->pqbio", act_one, grad_two, preferred_element_type=jnp.float32
    )
    grad_act = jnp.einsum(
        "nkpmbo,pqbio->nkqmbi", grad_two, second_pair, preferred_element_type=jnp.float32
    )
    grad_one = jax.vjp(jax.nn.gelu, pre_one)[1](grad_act)[0].astype(jnp.bfloat16)
    grad_bias_one = jnp.sum(grad_one.astype(jnp.float32), axis=(0, 1, 3))
    grad_first = jnp.einsum(
        "nkqmbi,nkpmbo->pqbio", blocked, grad_one, preferred_element_type=jnp.float32
    )
    grad_spectrum = jnp.einsum(
        "nkpmbo,pqbio->nkqmbi", grad_one, first_pair, preferred_element_type=jnp.float32
    ).astype(jnp.bfloat16)
    grad_spectrum = grad_spectrum.reshape(snap_local, lat_total, 2, mode_local, channel)
    grad_lon = jnp.einsum(
        "pkqr,nkpmd->nrqmd", lat_fwd, grad_spectrum, preferred_element_type=jnp.float32
    ).astype(jnp.bfloat16)
    grad_rows = lax.all_to_all(grad_lon, "sp", split_axis=1, concat_axis=3, tiled=True)
    grad_normed = grad_mixture + jnp.einsum(
        "nrqmd,lqm->nrld", grad_rows, lon_fwd, preferred_element_type=jnp.float32
    )
    grad_field_norm, grad_gain_one, grad_shift_one = norm_pull(grad_normed)
    input_grad = grad_mixture + grad_field_norm
    grad_filter = jnp.stack(
        [
            grad_first[0, 0] + grad_first[1, 1],
            grad_first[1, 0] - grad_first[0, 1],
            grad_second[0, 0] + grad_second[1, 1],
            grad_second[1, 0] - grad_second[0, 1],
        ]
    ).reshape(4, channel, block_width)
    grad_small = jnp.concatenate(
        [
            jnp.stack([grad_gain_one, grad_shift_one, grad_gain_two, grad_shift_two]),
            grad_bias_one.reshape(2, channel),
            grad_bias_two.reshape(2, channel),
            grad_bias_out[None, :],
            grad_bias_hidden.reshape(-1, channel),
        ],
        axis=0,
    )
    shares = (
        jnp.stack([
            lax.psum_scatter(part, "sp", scatter_dimension=0, tiled=True) for part in passed[2:4]
        ]),
        lax.psum_scatter(grad_filter, "sp", scatter_dimension=1, tiled=True),
        lax.psum_scatter(grad_small, "sp", scatter_dimension=1, tiled=True),
    )
    owned = (
        lax.psum(shares[0].astype(jnp.bfloat16), "snap").astype(jnp.float32),
        lax.psum(shares[1].astype(jnp.bfloat16), "snap").astype(jnp.float32),
        lax.psum(shares[2].astype(jnp.bfloat16), "snap").astype(jnp.float32),
    )
    mlp_new, mlp_first_new, mlp_second_new, mlp_copy = adamw(
        mlp_master, mlp_first, mlp_second, owned[0], rate_mlp
    )
    filter_new, filter_first_new, filter_second_new, filter_copy = adamw(
        filter_master, filter_first, filter_second, owned[1], rate_filter
    )
    small_new, small_first_new, small_second_new, small_copy = adamw(
        small_master, small_first, small_second, owned[2], rate_small
    )
    return (
        output.astype(jnp.bfloat16),
        input_grad,
        mlp_new,
        mlp_first_new,
        mlp_second_new,
        mlp_copy,
        filter_new,
        filter_first_new,
        filter_second_new,
        filter_copy,
        small_new,
        small_first_new,
        small_second_new,
        small_copy,
        stats_new,
    )


def lon_matrix(lon_total, mode_total, snaps, rows):
    places = np.arange(lon_total)
    orders = np.arange(mode_total)
    angles = (places[:, None] * orders[None, :] % lon_total) * (2.0 * math.pi / lon_total)
    doubling = np.where(orders == 0, 1.0, 2.0)
    scaling = 1.0 / math.sqrt(lon_total)
    forward = np.stack([np.cos(angles), -np.sin(angles)], axis=1) * scaling
    inverse = forward * doubling

    def spread(table):
        table = np.einsum(
            "ab,lx,rs->alrbsx", np.eye(snaps), table.reshape(lon_total, -1), np.eye(rows)
        )
        return table.reshape(snaps * lon_total * rows, -1).astype(ml_dtypes.bfloat16)

    return spread(forward), spread(inverse)


def lon_turn(lon_total, rows):
    turn = np.einsum("lk,rs->rlks", np.eye(lon_total), np.eye(rows))
    return turn.reshape(rows, lon_total, lon_total * rows).astype(ml_dtypes.bfloat16)


def lat_matrix(lat_total, mode_total):
    places = np.arange(lat_total)
    angles = (places[:, None] * places[None, :] % lat_total) * (2.0 * math.pi / lat_total)
    cosine, sine = np.cos(angles), np.sin(angles)
    table = np.stack([np.stack([cosine, sine], axis=1), np.stack([-sine, cosine], axis=1)])
    table = np.einsum("pkqr,ab->pakrqb", table / math.sqrt(lat_total), np.eye(mode_total))
    size = 2 * lat_total * mode_total
    return table.reshape(size, size).astype(ml_dtypes.bfloat16)


class Refs:
    pass


def block_body(names, sizes, *refs):
    g = Refs()
    for name, ref in zip(names, refs, strict=True):
        setattr(g, name, ref)
    snaps, group, parts, width = sizes
    levels = group // 2
    tokens = g.fields.shape[0] * g.fields.shape[1]
    channel = g.fields.shape[2]
    tiles = channel // 128
    owned = channel // group
    half = width // 2
    quarter = width // snaps
    tile = divisor(tokens, 16, 480)
    strip = divisor(tokens // 2, 48, 144)
    sub = divisor(strip, 16, 48)
    low = jnp.bfloat16
    f32 = jnp.float32

    me_snap = lax.axis_index("snap")
    me_sp = lax.axis_index("sp")
    core = lax.rem(me_sp, 2)
    level = me_sp // 2

    def at(snap, sp):
        return {"snap": snap, "sp": sp}

    def sp_after(step):
        return lax.rem(me_sp + step, group)

    def sp_before(step):
        return lax.rem(me_sp + group - step, group)

    def snap_after(step):
        return lax.rem(me_snap + step, snaps)

    def snap_before(step):
        return lax.rem(me_snap + snaps - step, snaps)

    def level_after(step):
        return lax.rem(level + step, levels)

    def level_before(step):
        return lax.rem(level + levels - step, levels)

    other_core = at(me_snap, me_sp + 1 - 2 * core)

    def send(src, dst, sems, index, target):
        return pltpu.make_async_remote_copy(
            src_ref=src,
            dst_ref=dst,
            send_sem=sems[0].at[index],
            recv_sem=sems[1].at[index],
            device_id=target,
            device_id_type=pl.DeviceIdType.MESH,
        )

    half_tokens = tokens // 2

    def strips(body, first=0, count=tokens):
        @pl.loop(0, count // strip)
        def _(step):
            for at_row in range(0, strip, sub):
                body(pl.ds(pl.multiple_of(first + step * strip + at_row, 16), sub))

    def half_strips(body, part):
        strips(body, part * half_tokens, half_tokens)

    def half_rows(part):
        return slice(part * half_tokens, (part + 1) * half_tokens)

    def fold(value):
        return jnp.sum(value.reshape(-1, 8, value.shape[1]), axis=0)

    def columns(name):
        ref = getattr(g, name)
        return ref.reshape(tiles, ref.shape[1] * ref.shape[2], 128)

    def columns_of(name, rows):
        view = columns(name)
        return jnp.concatenate([view[tile_at, rows, :] for tile_at in range(tiles)], axis=1)

    def store_columns(name, rows, value):
        view = columns(name)
        for tile_at in range(tiles):
            view[tile_at, rows, :] = value[:, tile_at * 128 : (tile_at + 1) * 128]

    def column_copies(near, far, sems, out):
        copies = []
        for tile_at in range(tiles):
            ends = [near.at[tile_at], far.at[:, :, tile_at * 128 : (tile_at + 1) * 128]]
            if not out:
                ends.reverse()
            copies.append(pltpu.make_async_copy(*ends, sems.at[tile_at]))
        return copies

    loads = {}

    def load(name, index):
        copy = pltpu.make_async_copy(getattr(g, name), getattr(g, name + "_in"), g.load_sem.at[index])
        copy.start()
        loads[name] = copy

    for index, name in enumerate(
        [name for name in names[: names.index("out")] if name not in ("mlp", "fields", "cot")]
    ):
        load(name, index)
    fields_load = column_copies(g.fields_cols, g.fields, g.fields_sem, False)
    cot_load = column_copies(g.cot_cols, g.cot, g.cot_sem, False)
    for copy in fields_load + cot_load:
        copy.start()

    def master_load(part):
        return pltpu.make_async_copy(
            g.mlp.at[:, :, part * width : (part + 1) * width],
            g.mlp_part.at[part % 2],
            g.load_sem.at[len(loads) + part % 2],
        )

    master_load(0).start()
    master_load(1).start()

    barrier = pltpu.get_barrier_semaphore()
    peers = [at(me_snap, sp_after(step)) for step in range(1, group)]
    peers += [at(snap_after(step), me_sp) for step in range(1, snaps)]
    for peer in peers:
        pl.semaphore_signal(
            barrier, inc=1, device_id=peer, device_id_type=pl.DeviceIdType.MESH
        )

    loads["small"].wait()
    loads["kept"].wait()
    g.own_small[...] = jnp.zeros_like(g.own_small)
    rows_small = g.small.shape[0]
    g.own_small[0:rows_small, 0:owned] = g.small_in[...].astype(low).astype(f32)
    pairs_kept = g.kept.shape[1]
    lines = lax.broadcasted_iota(jnp.int32, (pairs_kept, pairs_kept), 0)
    places = lax.broadcasted_iota(jnp.int32, (pairs_kept, pairs_kept), 1)
    kept = jnp.where(lines == places, g.kept_in[...].astype(f32), 0.0)
    g.own_small[16:, :] = jnp.broadcast_to(
        jnp.sum(kept, axis=1, keepdims=True), (pairs_kept, g.own_small.shape[1])
    )
    pl.semaphore_wait(barrier, len(peers))

    def small_copy(step):
        return send(
            g.own_small, g.all_small.at[me_sp], (g.small_s, g.small_r), step, at(me_snap, sp_after(step))
        )

    for step in range(1, group):
        small_copy(step).start()
    g.all_small[me_sp] = g.own_small[...]

    snap_low = lax.rem(me_snap, 2)
    snap_high = me_snap // 2
    beside_low = me_snap + 1 - 2 * snap_low
    beside_high = me_snap + 2 - 4 * snap_high

    def own_quarter(part):
        odd = lax.rem(part, 2)
        return (1 - odd) * me_snap + odd * (2 * snap_low + snap_high)

    def half_quarters(part):
        return pl.ds(2 * (own_quarter(part) // 2), 2)

    def own_rows(sp):
        return pl.ds(pl.multiple_of(sp * owned, owned), owned)

    def first_copy(part, step):
        target = sp_after(step)
        matrix = lax.rem(target, 2)
        place = own_quarter(part)
        return send(
            g.own_w.at[part, matrix, place],
            g.all_w.at[part, matrix, place, own_rows(me_sp)],
            (g.first_s, g.first_r),
            (part, step),
            at(me_snap, target),
        )

    def first_local(part):
        place = own_quarter(part)
        return pltpu.make_async_copy(
            g.own_w.at[part, core, place],
            g.all_w.at[part, core, place, own_rows(me_sp)],
            g.first_s.at[part, 0],
        )

    def second_copy(part):
        odd = lax.rem(part, 2)
        view = g.all_w.at[part, core, own_quarter(part)]
        target = at((1 - odd) * beside_low + odd * beside_high, me_sp)
        return send(view, view, (g.second_s, g.second_r), part, target)

    def third_copy(part):
        odd = lax.rem(part, 2)
        view = g.all_w.at[part, core, half_quarters(part)]
        target = at((1 - odd) * beside_high + odd * beside_low, me_sp)
        return send(view, view, (g.third_s, g.third_r), part, target)

    def fourth_copy(part):
        view = g.all_w.at[part, core]
        return send(view, view, (g.fourth_s, g.fourth_r), part, other_core)

    def start_first(part):
        for step in range(1, group):
            first_copy(part, step).start()
        first_local(part).start()

    def pass_second(part):
        for step in range(1, group):
            first_copy(part, step).wait_recv()
        first_local(part).wait()
        second_copy(part).start()

    def pass_third(part):
        second_copy(part).wait_recv()
        third_copy(part).start()

    def pass_fourth(part):
        third_copy(part).wait_recv()
        fourth_copy(part).start()

    for part in range(parts):
        master_load(part).wait()
        for place in range(snaps):
            cols = slice(place * quarter, (place + 1) * quarter)
            g.own_w[part, :, place] = g.mlp_part[part % 2, :, :, cols].astype(low)
        if part + 2 < parts:
            master_load(part + 2).start()
        if part < 2:
            start_first(part)

    for copy in fields_load:
        copy.wait()

    def first_unit(rows):
        values = columns_of("fields_cols", rows).astype(f32)
        centred = values - jnp.mean(values, axis=-1, keepdims=True)
        scale = lax.rsqrt(jnp.mean(centred * centred, axis=-1, keepdims=True) + eps_norm)
        g.scale_one[rows, :] = scale
        g.grid[rows, :] = centred * scale

    strips(first_unit)
    for step in range(1, group):
        small_copy(step).wait_recv()
    for sp in range(group):
        g.gains[:, sp * owned : (sp + 1) * owned] = g.all_small[sp, 0:16, 0:owned]
        g.keep[sp * pairs_kept : (sp + 1) * pairs_kept, :] = g.all_small[sp, 16:, :]

    def first_norm(rows):
        unit = g.grid[rows, :]
        normed = unit * g.gains[0:1, :] + g.gains[1:2, :]
        g.unit_one[rows, :] = unit.astype(low)
        g.normed[rows, :] = normed.astype(low)
        g.grid[rows, :] = columns_of("fields_cols", rows).astype(f32) + normed

    half_snaps = g.arrived.shape[0] // 2

    def some_snaps(part):
        return pl.ds(part * half_snaps, half_snaps)

    def to_blocks(table, which, part):
        modes = dot_nn(table, g.normed[half_rows(part), :])
        for block in range(group):
            cut = modes[:, block * owned : (block + 1) * owned]
            cut = jnp.concatenate([cut, jnp.zeros((cut.shape[0], 128 - owned), f32)], axis=1)
            g.modes[part, block] = cut.astype(low).reshape(g.modes.shape[2:])
        for step in range(1, group):
            block_copy(which, part, step).start()
        g.arrived[some_snaps(part), mode_rows(me_sp), :] = g.modes[part, me_sp]

    def mode_rows(sp):
        size = g.modes.shape[3]
        return pl.ds(pl.multiple_of(sp * size, size), size)

    def block_copy(which, part, step):
        target = sp_after(step)
        return send(
            g.modes.at[part, target],
            g.arrived.at[some_snaps(part), mode_rows(me_sp), :],
            (g.block_s, g.block_r),
            (which, part, step),
            at(me_snap, target),
        )

    def row_copy(which, part, step):
        target = sp_after(step)
        return send(
            g.turned.at[some_snaps(part), mode_rows(target), :],
            g.home.at[part, me_sp],
            (g.row_s, g.row_r),
            (which, part, step),
            at(me_snap, target),
        )

    def to_rows(which, part):
        for step in range(1, group):
            row_copy(which, part, step).start()
        g.home[part, me_sp] = g.turned[some_snaps(part), mode_rows(me_sp), :]

    def home_modes(which, part):
        for step in range(1, group):
            row_copy(which, part, step).wait_recv()
        count = g.gathered.shape[1]
        for block in range(group):
            g.gathered[part, :, block * owned : (block + 1) * owned] = (
                g.home[part, block].reshape(count, 128)[:, 0:owned].astype(f32)
            )
        g.home_low[part] = g.gathered[part].astype(low)

    loads["lon_f"].wait()
    for part in range(2):
        half_strips(first_norm, part)
        to_blocks(g.lon_f_in[...], 0, part)
        pass_second(part)
    for part in range(2, 4):
        start_first(part)

    loads["filt"].wait()
    for weight, first in ((g.weight_one, 0), (g.weight_two, 2)):
        weight[...] = jnp.zeros_like(weight)
        real = g.filt_in[first].astype(low)
        imag = g.filt_in[first + 1].astype(low)
        weight[0:owned, 0:owned] = real
        weight[128 : 128 + owned, 128 : 128 + owned] = real
        weight[0:owned, 128 : 128 + owned] = imag
        weight[128 : 128 + owned, 0:owned] = -imag

    def bias_row(first):
        return jnp.concatenate(
            [g.own_small[first : first + 1, :], g.own_small[first + 1 : first + 2, :]], axis=1
        )

    for copy in cot_load:
        copy.wait()

    def flat_cot(rows):
        g.cot_in[rows, :] = columns_of("cot_cols", rows)

    strips(flat_cot)
    pass_third(0)
    loads["lat_f"].wait()
    loads["lat_b"].wait()
    pairs = g.arrived.shape[1] // 2
    half_modes = half_snaps * pairs

    def mode_half(part):
        return slice(part * half_modes, (part + 1) * half_modes)

    def spectra(out, kind, part):
        for snap in range(part * half_snaps, (part + 1) * half_snaps):
            spectrum = dot_nn(g.lat_f_in[...], g.arrived[snap]).astype(kind)
            rows = slice(snap * pairs, (snap + 1) * pairs)
            out[rows, 0:128] = spectrum[0:pairs]
            out[rows, 128:256] = spectrum[pairs:]

    def grids(values, part):
        for index in range(half_snaps):
            rows = values[index * pairs : (index + 1) * pairs]
            rows = jnp.concatenate([rows[:, 0:128], rows[:, 128:256]], axis=0)
            g.turned[part * half_snaps + index] = dot_nn(g.lat_b_in[...], rows).astype(low)

    def keep_half():
        keep = jnp.concatenate([g.keep[...], g.keep[...]], axis=1)
        return jnp.concatenate([keep] * half_snaps, axis=0)

    for part in range(2):
        for step in range(1, group):
            block_copy(0, part, step).wait_recv()
        rows = mode_half(part)
        spectra(g.spectrum, low, part)
        g.pre_one[rows, :] = dot_nn(g.spectrum[rows, :], g.weight_one[...]) + bias_row(4)
        g.act_one[rows, :] = gelu_both(g.pre_one[rows, :])[0].astype(low)
        g.pre_two[rows, :] = dot_nn(g.act_one[rows, :], g.weight_two[...]) + bias_row(6)
        grids((shrink(g.pre_two[rows, :]) * keep_half()).astype(low), part)
        to_rows(0, part)
        if part == 0:
            pass_third(1)
    for part in range(4, parts):
        start_first(part)
    pass_second(2)
    g.cot_turned[...] = g.cot_in[...].T
    pass_second(3)

    loads["lon_i"].wait()

    def second_norm(rows):
        values = g.grid[rows, :]
        centred = values - jnp.mean(values, axis=-1, keepdims=True)
        scale = lax.rsqrt(jnp.mean(centred * centred, axis=-1, keepdims=True) + eps_norm)
        centred = centred * scale
        g.unit_two[rows, :] = centred.astype(low)
        g.scale_two[rows, :] = scale
        g.normed[rows, :] = (centred * g.gains[2:3, :] + g.gains[3:4, :]).astype(low)
        g.grid[rows, :] = values + g.gains[8:9, :]
        g.back[rows, :] = jnp.zeros((sub, channel), f32)

    for part in range(2):
        home_modes(0, part)
        g.grid[half_rows(part), :] += dot_nn(g.lon_i_in[...], g.home_low[part])
        half_strips(second_norm, part)
        pass_fourth(part)
        pass_third(2 + part)
    g.normed_turned[...] = g.normed[...].T
    for part in range(4, parts):
        pass_second(part)
    flat = jnp.concatenate([g.gains[9 + row : 10 + row, :] for row in range(rows_small - 9)], axis=1)
    for part in range(parts):
        g.bias[part] = flat[:, part * width : (part + 1) * width]

    def core_copy(part, matrix):
        slot = lax.rem(part, 2)
        return send(
            g.grads.at[slot, matrix, :, 1 - core],
            g.core_got.at[slot, matrix],
            (g.core_s, g.core_r),
            (slot, matrix),
            other_core,
        )

    places_one = (snap_low, snap_high)
    places_two = (snap_high, snap_low)
    beside_one = (beside_low, beside_high)
    beside_two = (beside_high, beside_low)
    place_last = (2 * snap_low + snap_high, me_snap)

    def half_copy(part, matrix):
        slot = lax.rem(part, 2)
        return send(
            g.half_out.at[slot, matrix, 1 - places_one[matrix]],
            g.half_got.at[slot, matrix],
            (g.half_s, g.half_r),
            (slot, matrix),
            at(beside_one[matrix], me_sp),
        )

    def quarter_copy(part, matrix):
        slot = lax.rem(part, 2)
        return send(
            g.quarter_out.at[slot, matrix, 1 - places_two[matrix]],
            g.quarter_got.at[slot, matrix],
            (g.quarter_s, g.quarter_r),
            (slot, matrix),
            at(beside_two[matrix], me_sp),
        )

    def level_copy(part, step):
        slot = lax.rem(part, 2)
        target = level_after(step)
        return send(
            g.level_out.at[slot, target],
            g.level_got.at[slot, level],
            (g.level_s, g.level_r),
            (slot, step),
            at(me_snap, 2 * target + core),
        )

    def last_copy(part, matrix, step):
        view = g.total.at[part, place_last[matrix], matrix]
        return send(
            view, view, (g.last_s, g.last_r), (part, matrix, step), at(snap_after(step), me_sp)
        )

    def half_stage(part):
        slot = lax.rem(part, 2)
        for matrix in range(2):

            @pl.when(part >= 2)
            def _(matrix=matrix):
                half_copy(part - 2, matrix).wait_send()

            core_copy(part, matrix).wait_recv()
            for row in range(levels):
                both = g.grads[slot, matrix, row, core].astype(f32) + g.core_got[
                    slot, matrix, row
                ].astype(f32)
                both = both.astype(low)
                g.half_out[slot, matrix, 0, row] = both[:, 0:half]
                g.half_out[slot, matrix, 1, row] = both[:, half:width]
            half_copy(part, matrix).start()

    def quarter_stage(part):
        slot = lax.rem(part, 2)
        for matrix in range(2):

            @pl.when(part >= 2)
            def _(matrix=matrix):
                quarter_copy(part - 2, matrix).wait_send()

            half_copy(part, matrix).wait_recv()
            for row in range(levels):
                both = g.half_out[slot, matrix, places_one[matrix], row].astype(f32) + g.half_got[
                    slot, matrix, row
                ].astype(f32)
                both = both.astype(low)
                g.quarter_out[slot, matrix, 0, row] = both[:, 0:quarter]
                g.quarter_out[slot, matrix, 1, row] = both[:, quarter:half]
            quarter_copy(part, matrix).start()

    def level_stage(part):
        slot = lax.rem(part, 2)

        @pl.when(part >= 2)
        def _():
            for step in range(1, levels):
                level_copy(part - 2, step).wait_send()

        for matrix in range(2):
            quarter_copy(part, matrix).wait_recv()
            for row in range(levels):
                both = g.quarter_out[slot, matrix, places_two[matrix], row].astype(
                    f32
                ) + g.quarter_got[slot, matrix, row].astype(f32)
                g.level_out[slot, row, matrix] = both.astype(low)
        for step in range(1, levels):
            level_copy(part, step).start()

    def last_stage(part):
        slot = lax.rem(part, 2)
        for step in range(1, levels):
            level_copy(part, step).wait_recv()
        for matrix in range(2):
            sums = g.level_out[slot, level, matrix].astype(f32)
            for step in range(1, levels):
                sums += g.level_got[slot, level_before(step), matrix].astype(f32)
            g.total[part, place_last[matrix], matrix] = sums.astype(low)
            for step in range(1, snaps):
                last_copy(part, matrix, step).start()

    def weight(part, matrix):
        return jnp.concatenate([g.all_w[part, matrix, place] for place in range(snaps)], axis=1)

    @pl.loop(0, parts)
    def _(part):
        slot = lax.rem(part, 2)
        fourth_copy(part).wait_recv()
        g.grad_bias[part] = jnp.zeros(g.grad_bias.shape[1:], f32)

        @pl.loop(0, tokens // tile)
        def _(step):
            rows = pl.ds(pl.multiple_of(step * tile, tile), tile)
            act, slope = gelu_both(dot_nn(g.normed[rows, :], weight(part, 0)) + g.bias[part])
            act = act.astype(low)
            slope = (dot_nn(g.cot_in[rows, :], weight(part, 1)) * slope).astype(low)
            g.act[rows, :] = act
            g.slope[rows, :] = slope
            g.grad_bias[part] += fold(slope.astype(f32))
            g.grid[rows, :] += dot_nt(act, weight(part, 1))
            g.back[rows, :] += dot_nt(slope, weight(part, 0))

        @pl.when(part + 2 < parts)
        def _():
            pass_fourth(part + 2)

        @pl.when(part + 4 < parts)
        def _():
            pass_third(part + 4)

        @pl.when(part >= 4)
        def _():
            last_stage(part - 4)

        @pl.when(part >= 3)
        def _():
            level_stage(part - 3)

        @pl.when(part >= 2)
        def _():
            quarter_stage(part - 2)

        @pl.when(part >= 1)
        def _():
            half_stage(part - 1)

        @pl.when(part >= 2)
        def _():
            for matrix in range(2):
                core_copy(part - 2, matrix).wait_send()

        shape = g.grads.shape[2:]
        g.grads[slot, 0] = dot_nn(g.normed_turned[...], g.slope[...]).astype(low).reshape(shape)
        core_copy(part, 0).start()
        g.grads[slot, 1] = dot_nn(g.cot_turned[...], g.act[...]).astype(low).reshape(shape)
        core_copy(part, 1).start()

    g.folds[...] = jnp.zeros_like(g.folds)

    def second_back(rows):
        grad = g.back[rows, :]
        unit = g.unit_two[rows, :].astype(f32)
        cot = g.cot_in[rows, :].astype(f32)
        pulled = grad * g.gains[2:3, :]
        middle = jnp.mean(pulled, axis=-1, keepdims=True)
        slant = jnp.mean(pulled * unit, axis=-1, keepdims=True)
        total = cot + g.scale_two[rows, :] * (pulled - middle - unit * slant)
        g.back[rows, :] = total
        g.normed[rows, :] = total.astype(low)
        g.folds[2] += fold(grad * unit)
        g.folds[3] += fold(grad)
        g.folds[4] += fold(cot)

    loads["lon_it"].wait()
    for part in range(2):
        half_strips(second_back, part)
        for step in range(1, group):
            block_copy(0, part, step).wait_send()
        to_blocks(g.lon_it_in[...], 1, part)

    last_stage(parts - 4)
    level_stage(parts - 3)
    quarter_stage(parts - 2)
    half_stage(parts - 1)

    def low_out(rows):
        store_columns("fields_cols", rows, g.grid[rows, :].astype(low))

    strips(low_out)
    out_copies = column_copies(g.fields_cols, g.out, g.fields_sem, True)
    for copy in out_copies:
        copy.start()
    loads["valid"].wait()
    loads["turn"].wait()
    weigh = sum(
        dot_nn(g.valid_in[:, row, :].astype(f32).astype(low), g.turn_in[row])
        for row in range(g.valid.shape[1])
    )
    places_each = weigh.shape[1]
    precise = lax.Precision.HIGHEST
    sums = [jnp.zeros((1, 128), f32), jnp.zeros((1, 128), f32)]
    for snap in range(g.valid.shape[0]):
        variables = g.grid[snap * places_each : (snap + 1) * places_each, 0:128]
        for index, value in enumerate((variables, variables * variables)):
            sums[index] += jnp.dot(
                weigh[snap : snap + 1, :], value, precision=precise, preferred_element_type=f32
            )

    def dot_tn(left, right):
        return lax.dot_general(
            left, right, (((0,), (0,)), ((), ())), preferred_element_type=f32
        )

    def filter_rows(first, grad):
        g.pair_grad[...] = grad
        real = g.pair_grad[0:128, 0:128] + g.pair_grad[128:256, 128:256]
        imag = g.pair_grad[0:128, 128:256] - g.pair_grad[128:256, 0:128]
        g.filt_out[me_snap, first] = real[0:owned].astype(low)
        g.filt_out[me_snap, first + 1] = imag[0:owned].astype(low)

    for part in range(2):
        for step in range(1, group):
            block_copy(1, part, step).wait_recv()
        rows = mode_half(part)
        spectra(g.grad_pre, f32, part)
        bend = jnp.tanh(g.pre_two[rows, :] / shrink_level)
        grad = (g.grad_pre[rows, :] * keep_half() * (bend * bend)).astype(low)
        g.grad_two[rows, :] = grad
        grad = dot_nt(grad, g.weight_two[...]) * gelu_both(g.pre_one[rows, :])[1]
        grad = grad.astype(low)
        g.grad_one[rows, :] = grad
        for step in range(1, group):
            row_copy(0, part, step).wait_send()
        grids(dot_nt(grad, g.weight_one[...]).astype(low), part)
        to_rows(1, part)
    last_stage(parts - 3)
    level_stage(parts - 2)
    quarter_stage(parts - 1)
    bias_one = jnp.sum(g.grad_one[...].astype(f32), axis=0, keepdims=True)
    bias_two = jnp.sum(g.grad_two[...].astype(f32), axis=0, keepdims=True)
    filter_rows(2, dot_tn(g.act_one[...], g.grad_two[...]))
    filter_rows(0, dot_tn(g.spectrum[...], g.grad_one[...]))

    def filter_copy(step):
        view = g.filt_out.at[me_snap]
        return send(view, view, (g.filt_s, g.filt_r), step, at(snap_after(step), me_sp))

    for step in range(1, snaps):
        filter_copy(step).start()


    loads["lon_ft"].wait()
    strip_pairs = strip // g.fields.shape[1]
    grad_view = g.grad_cols.reshape(2, tiles, strip, 128)

    def grad_copies(place, slot):
        pairs_out = pl.ds(place * strip_pairs, strip_pairs)
        return column_copies(
            g.grad_cols.at[slot], g.in_grad.at[pairs_out], g.grad_sem.at[slot], True
        )

    steps = half_tokens // strip
    for part in range(2):
        home_modes(1, part)
        if part == 1:
            last_stage(parts - 2)
            level_stage(parts - 1)
        g.grid[half_rows(part), :] = g.back[half_rows(part), :] + dot_nn(
            g.lon_ft_in[...], g.home_low[part]
        )

        @pl.loop(0, steps)
        def _(step):
            place = part * steps + step
            slot = lax.rem(place, 2)

            @pl.when(place >= 2)
            def _():
                for copy in grad_copies(place, slot):
                    copy.wait()

            for at_row in range(0, strip, sub):
                rows = pl.ds(pl.multiple_of(place * strip + at_row, 16), sub)
                grad = g.grid[rows, :]
                unit = g.unit_one[rows, :].astype(f32)
                pulled = grad * g.gains[0:1, :]
                middle = jnp.mean(pulled, axis=-1, keepdims=True)
                slant = jnp.mean(pulled * unit, axis=-1, keepdims=True)
                total = g.back[rows, :] + g.scale_one[rows, :] * (pulled - middle - unit * slant)
                for tile_at in range(tiles):
                    grad_view[slot, tile_at, at_row : at_row + sub, :] = total[
                        :, tile_at * 128 : (tile_at + 1) * 128
                    ]
                g.folds[0] += fold(grad * unit)
                g.folds[1] += fold(grad)
            for copy in grad_copies(place, slot):
                copy.start()

    g.grad_rows[...] = jnp.zeros_like(g.grad_rows)
    for index, row in enumerate((0, 1, 2, 3, 8)):
        g.grad_rows[row : row + 1, :] = jnp.sum(g.folds[index], axis=0, keepdims=True)
    flat = jnp.concatenate(
        [jnp.sum(g.grad_bias[part], axis=0, keepdims=True) for part in range(parts)], axis=1
    )
    for row in range(rows_small - 9):
        g.grad_rows[9 + row : 10 + row, :] = flat[:, row * channel : (row + 1) * channel]
    for block in range(group):
        g.tiles[block] = jnp.zeros(g.tiles.shape[1:], f32)
        g.tiles[block, :, 0:owned] = g.grad_rows[:, block * owned : (block + 1) * owned]
        g.tiles[block, 13:14, :] = sums[0]
        g.tiles[block, 14:15, :] = sums[1]

    def tile_copy(step):
        target = sp_after(step)
        return send(
            g.tiles.at[target], g.tiles_got.at[me_sp], (g.tile_s, g.tile_r), step, at(me_snap, target)
        )

    def snap_tile_copy(step):
        view = g.snap_tiles.at[me_snap]
        return send(view, view, (g.snap_tile_s, g.snap_tile_r), step, at(snap_after(step), me_sp))

    for step in range(1, group):
        tile_copy(step).start()
    last_stage(parts - 1)

    g.tiles_got[me_sp] = g.tiles[me_sp]
    for step in range(1, group):
        tile_copy(step).wait_recv()
    tile_sum = g.tiles_got[0]
    for sp in range(1, group):
        tile_sum += g.tiles_got[sp]
    g.snap_tiles[me_snap] = tile_sum
    g.snap_tiles[me_snap, 4:5, :] = bias_one[:, 0:128]
    g.snap_tiles[me_snap, 5:6, :] = bias_one[:, 128:256]
    g.snap_tiles[me_snap, 6:7, :] = bias_two[:, 0:128]
    g.snap_tiles[me_snap, 7:8, :] = bias_two[:, 128:256]
    for step in range(1, snaps):
        snap_tile_copy(step).start()

    for step in range(1, snaps):
        filter_copy(step).wait_recv()
    filter_sum = g.filt_out[0].astype(f32)
    for snap in range(1, snaps):
        filter_sum += g.filt_out[snap].astype(f32)
    g.grad_filt[...] = filter_sum
    for part in range(parts):
        for matrix in range(2):
            for step in range(1, snaps):
                last_copy(part, matrix, step).wait_recv()
    grads_out = pltpu.make_async_copy(g.total, g.grad_mlp, g.load_sem.at[3])
    grads_out.start()
    for step in range(1, snaps):
        snap_tile_copy(step).wait_recv()
    tile_sum = g.snap_tiles[0]
    for snap in range(1, snaps):
        tile_sum += g.snap_tiles[snap]
    g.grad_small[...] = tile_sum

    grads_out.wait()
    for copy in out_copies:
        copy.wait()
    for slot in range(2):
        for copy in grad_copies(0, slot):
            copy.wait()
    for step in range(1, group):
        small_copy(step).wait_send()
        for part in range(2):
            block_copy(1, part, step).wait_send()
            row_copy(1, part, step).wait_send()
        tile_copy(step).wait_send()
        for part in range(parts):
            first_copy(part, step).wait_send()
    for part in range(parts):
        second_copy(part).wait_send()
        third_copy(part).wait_send()
        fourth_copy(part).wait_send()
    for part in (parts - 2, parts - 1):
        for matrix in range(2):
            core_copy(part, matrix).wait_send()
            half_copy(part, matrix).wait_send()
            quarter_copy(part, matrix).wait_send()
        for step in range(1, levels):
            level_copy(part, step).wait_send()
    for step in range(1, snaps):
        filter_copy(step).wait_send()
        snap_tile_copy(step).wait_send()
        for part in range(parts):
            for matrix in range(2):
                last_copy(part, matrix, step).wait_send()


def block_pass(fields, cot, valid, kept, mlp, filt, small, snaps, group):
    snap_local, row_local, lon_total, channel = fields.shape
    tokens = snap_local * row_local * lon_total
    hidden = mlp.shape[2]
    lat_total = row_local * group
    modes = kept.shape[1] * group
    owned = channel // group
    width = 512
    parts = hidden // width
    levels = group // 2
    quarter = width // snaps
    low, f32 = jnp.bfloat16, jnp.float32
    half = width // 2
    half_snaps = snap_local // 2
    lon_f, lon_i = lon_matrix(lon_total, modes, half_snaps, row_local)

    def paired(array):
        return jnp.transpose(array, (0, 2, 1, 3)).reshape(-1, row_local, channel)

    lat_f = lat_matrix(lat_total, modes)
    pair = 2 * modes * row_local
    spread = half_snaps * row_local * 2 * modes
    inputs = dict(
        small=small,
        kept=kept.T,
        fields=paired(fields),
        lon_f=jnp.asarray(np.ascontiguousarray(lon_f.T)),
        filt=filt,
        lat_f=jnp.asarray(lat_f),
        lat_b=jnp.asarray(np.ascontiguousarray(lat_f.T)),
        cot=paired(cot),
        lon_i=jnp.asarray(lon_i),
        valid=valid,
        turn=jnp.asarray(lon_turn(lon_total, row_local)),
        lon_it=jnp.asarray(np.ascontiguousarray(lon_i.T)),
        lon_ft=jnp.asarray(lon_f),
        mlp=mlp,
    )
    outputs = dict(
        out=jax.ShapeDtypeStruct((tokens // row_local, row_local, channel), low),
        in_grad=jax.ShapeDtypeStruct((tokens // row_local, row_local, channel), f32),
        grad_mlp=jax.ShapeDtypeStruct((parts, snaps, 2, owned, quarter), low),
        grad_filt=jax.ShapeDtypeStruct((4, owned, 128), f32),
        grad_small=jax.ShapeDtypeStruct((16, 128), f32),
    )
    vmem = pltpu.VMEM
    dma = pltpu.SemaphoreType.DMA
    scratch = {
        name + "_in": vmem(value.shape, value.dtype)
        for name, value in inputs.items()
        if name not in ("mlp", "fields", "cot")
    }
    tiles = channel // 128
    cols = (tiles, tokens // row_local, row_local, 128)
    strip = divisor(tokens // 2, 48, 144)
    scratch |= dict(
        mlp_part=vmem((2, 2, owned, width), f32),
        fields_cols=vmem(cols, low),
        cot_cols=vmem(cols, low),
        grad_cols=vmem((2, tiles, strip // row_local, row_local, 128), f32),
        grad_sem=dma((2, tiles)),
        fields_sem=dma((tiles,)),
        cot_sem=dma((tiles,)),
        cot_in=vmem((tokens, channel), low),
        grid=vmem((tokens, channel), f32),
        back=vmem((tokens, channel), f32),
        normed=vmem((tokens, channel), low),
        normed_turned=vmem((channel, tokens), low),
        cot_turned=vmem((channel, tokens), low),
        unit_one=vmem((tokens, channel), low),
        unit_two=vmem((tokens, channel), low),
        scale_one=vmem((tokens, 1), f32),
        scale_two=vmem((tokens, 1), f32),
        own_small=vmem((16 + kept.shape[0], 128), f32),
        all_small=vmem((group, 16 + kept.shape[0], 128), f32),
        gains=vmem((16, channel), f32),
        keep=vmem((lat_total * modes, 128), f32),
        own_w=vmem((parts, 2, snaps, owned, quarter), low),
        all_w=vmem((parts, 2, snaps, channel, quarter), low),
        modes=vmem((2, group, half_snaps, pair, 128), low),
        arrived=vmem((snap_local, pair * group, 128), low),
        turned=vmem((snap_local, pair * group, 128), low),
        home=vmem((2, group, half_snaps, pair, 128), low),
        gathered=vmem((2, spread, channel), f32),
        home_low=vmem((2, spread, channel), low),
        weight_one=vmem((256, 256), low),
        weight_two=vmem((256, 256), low),
        spectrum=vmem((snap_local * lat_total * modes, 256), low),
        pre_one=vmem((snap_local * lat_total * modes, 256), f32),
        act_one=vmem((snap_local * lat_total * modes, 256), low),
        pre_two=vmem((snap_local * lat_total * modes, 256), f32),
        grad_pre=vmem((snap_local * lat_total * modes, 256), f32),
        grad_two=vmem((snap_local * lat_total * modes, 256), low),
        grad_one=vmem((snap_local * lat_total * modes, 256), low),
        folds=vmem((5, 8, channel), f32),
        pair_grad=vmem((256, 256), f32),
        act=vmem((tokens, width), low),
        slope=vmem((tokens, width), low),
        bias=vmem((parts, 1, width), f32),
        grad_bias=vmem((parts, 8, width), f32),
        grad_rows=vmem((16, channel), f32),
        grads=vmem((2, 2, levels, 2, owned, width), low),
        core_got=vmem((2, 2, levels, owned, width), low),
        half_out=vmem((2, 2, 2, levels, owned, half), low),
        half_got=vmem((2, 2, levels, owned, half), low),
        quarter_out=vmem((2, 2, 2, levels, owned, quarter), low),
        quarter_got=vmem((2, 2, levels, owned, quarter), low),
        level_out=vmem((2, levels, 2, owned, quarter), low),
        level_got=vmem((2, levels, 2, owned, quarter), low),
        total=vmem((parts, snaps, 2, owned, quarter), low),
        filt_out=vmem((snaps, 4, owned, 128), low),
        tiles=vmem((group, 16, 128), f32),
        tiles_got=vmem((group, 16, 128), f32),
        snap_tiles=vmem((snaps, 16, 128), f32),
        load_sem=dma((len(inputs) + 1,)),
    )
    for name, shape in dict(
        small=(group,),
        first=(parts, group),
        second=(parts,),
        third=(parts,),
        fourth=(parts,),
        block=(2, 2, group),
        row=(2, 2, group),
        core=(2, 2),
        half=(2, 2),
        quarter=(2, 2),
        level=(2, levels),
        last=(parts, 2, snaps),
        filt=(snaps,),
        tile=(group,),
        snap_tile=(snaps,),
    ).items():
        scratch[name + "_s"] = dma(shape)
        scratch[name + "_r"] = dma(shape)
    names = [*inputs, *outputs, *scratch]
    far = pl.BlockSpec(memory_space=pl.ANY)
    near = pl.BlockSpec(memory_space=pltpu.VMEM)
    results = pl.pallas_call(
        functools.partial(block_body, names, (snaps, group, parts, width)),
        in_specs=[far] * len(inputs),
        out_specs=[far, far, far, near, near],
        out_shape=list(outputs.values()),
        scratch_shapes=list(scratch.values()),
        compiler_params=pltpu.CompilerParams(
            collective_id=0, has_side_effects=True, vmem_limit_bytes=VMEM_LIMIT
        ),
        cost_estimate=pl.CostEstimate(
            flops=12 * tokens * channel * hidden,
            bytes_accessed=4 * hidden * channel,
            transcendentals=tokens * hidden,
        ),
        name="block_pass",
    )(*inputs.values())
    return results


def step_body(names, positions, *refs):
    g = Refs()
    for name, ref in zip(names, refs, strict=True):
        setattr(g, name, ref)
    parts, snaps = g.grad_mlp.shape[:2]
    quarter = g.grad_mlp.shape[4]
    width = snaps * quarter
    moments = ("w", "m", "v")
    results = ("new", "first", "second", "copy")

    pieces = g.far_sem.shape[2]
    ends = ((g.out, g.out_near, g.out_o), (g.in_grad, g.in_grad_near, g.in_grad_o))

    def passing(kind, piece, leg):
        size = ends[kind][0].shape[0] // pieces
        rows = pl.ds(piece * size, size)
        return pltpu.make_async_copy(
            ends[kind][leg].at[rows], ends[kind][leg + 1].at[rows], g.far_sem.at[leg, kind, piece]
        )

    through = [(kind, piece) for kind in range(2) for piece in range(pieces)]

    def part_cols(part):
        return pl.ds(part * width, width)

    def load(part):
        near = [
            pltpu.make_async_copy(
                getattr(g, "mlp_" + kind).at[:, :, part_cols(part)],
                g.near.at[index, part],
                g.near_sem.at[index, part],
            )
            for index, kind in enumerate(moments)
        ]
        near.append(
            pltpu.make_async_copy(g.grad_mlp.at[part], g.grad_near.at[part], g.near_sem.at[3, part])
        )
        return near

    def store(part):
        copies = [
            pltpu.make_async_copy(
                g.near.at[index, part],
                getattr(g, "mlp_" + kind).at[:, :, part_cols(part)],
                g.back_sem.at[index, part],
            )
            for index, kind in enumerate(results[:3])
        ]
        copies.append(
            pltpu.make_async_copy(
                g.low_near.at[part], g.mlp_copy.at[:, :, part_cols(part)], g.back_sem.at[3, part]
            )
        )
        return copies

    coming = [load(part) for part in range(parts)]
    going = [store(part) for part in range(parts)]
    shares = [through[part::parts] for part in range(parts)]
    for part in range(parts):
        for copy in coming[part]:
            copy.start()
        for each in shares[part]:
            passing(*each, 0).start()

    def put(prefix, values):
        for kind, value in zip(results, values, strict=True):
            getattr(g, prefix + kind)[...] = value

    owned = g.filt_w.shape[2]
    put(
        "filt_",
        adamw(g.filt_w[...], g.filt_m[...], g.filt_v[...], g.grad_filt[:, :, 0:owned], rate_filter),
    )
    rows = g.small_w.shape[0]
    put(
        "small_",
        adamw(
            g.small_w[...], g.small_m[...], g.small_v[...], g.grad_small[0:rows, 0:owned], rate_small
        ),
    )
    totals = g.grad_small[rows : rows + 2, 0 : g.run.shape[1]]
    g.stats[...] = stat_decay * g.run[...] + (1.0 - stat_decay) * totals / positions

    for part in range(parts):
        for copy in coming[part]:
            copy.wait()

        for snap in range(snaps):
            cols = slice(snap * quarter, (snap + 1) * quarter)
            where = (slice(None), slice(None), cols)
            now = [g.near[(index, part, *where)] for index in range(3)]
            grad = g.grad_near[part, snap].astype(jnp.float32)
            values = adamw(*now, grad, rate_mlp)
            for index in range(3):
                g.near[(index, part, *where)] = values[index]
            g.low_near[(part, *where)] = values[3]
        for copy in going[part]:
            copy.start()
        for each in shares[part]:
            passing(*each, 0).wait()
            passing(*each, 1).start()
    for each in through:
        passing(*each, 1).wait()
    for part in range(parts):
        for copy in going[part]:
            copy.wait()


def step_pass(shown, grads, masters, run_stats, positions):
    grad_mlp, grad_filt, grad_small = grads
    mlp, filt, small = masters
    parts = grad_mlp.shape[0]
    width = mlp[0].shape[2] // parts
    f32, low = jnp.float32, jnp.bfloat16
    far = pl.BlockSpec(memory_space=pltpu.HBM)
    near = pl.BlockSpec(memory_space=pltpu.VMEM)
    inputs = dict(out=shown[0], in_grad=shown[1], grad_mlp=grad_mlp)
    inputs |= dict(zip(("mlp_w", "mlp_m", "mlp_v"), mlp, strict=True))
    far_in = len(inputs)
    inputs |= dict(grad_filt=grad_filt, grad_small=grad_small)
    inputs |= dict(zip(("filt_w", "filt_m", "filt_v"), filt, strict=True))
    inputs |= dict(zip(("small_w", "small_m", "small_v"), small, strict=True))
    inputs |= dict(run=run_stats)
    results = (("new", f32), ("first", f32), ("second", f32), ("copy", low))
    outputs = {
        name + "_o": jax.ShapeDtypeStruct(array.shape, array.dtype)
        for name, array in zip(("out", "in_grad"), shown, strict=True)
    }
    outputs |= {"mlp_" + kind: jax.ShapeDtypeStruct(mlp[0].shape, dt) for kind, dt in results}
    far_out = len(outputs)
    outputs |= {"filt_" + kind: jax.ShapeDtypeStruct(filt[0].shape, dt) for kind, dt in results}
    outputs |= {"small_" + kind: jax.ShapeDtypeStruct(small[0].shape, dt) for kind, dt in results}
    outputs |= dict(stats=jax.ShapeDtypeStruct(run_stats.shape, f32))
    scratch = dict(
        near=pltpu.VMEM((3, parts, 2, mlp[0].shape[1], width), f32),
        grad_near=pltpu.VMEM(grad_mlp.shape, low),
        low_near=pltpu.VMEM((parts, 2, mlp[0].shape[1], width), low),
        near_sem=pltpu.SemaphoreType.DMA((4, parts)),
        back_sem=pltpu.SemaphoreType.DMA((4, parts)),
        out_near=pltpu.VMEM(shown[0].shape, low),
        in_grad_near=pltpu.VMEM(shown[1].shape, f32),
        far_sem=pltpu.SemaphoreType.DMA((2, 2, divisor(shown[0].shape[0], 1, 4))),
    )
    return pl.pallas_call(
        functools.partial(step_body, [*inputs, *outputs, *scratch], positions),
        in_specs=[far] * far_in + [near] * (len(inputs) - far_in),
        out_specs=[far] * far_out + [near] * (len(outputs) - far_out),
        out_shape=list(outputs.values()),
        scratch_shapes=list(scratch.values()),
        compiler_params=pltpu.CompilerParams(vmem_limit_bytes=VMEM_LIMIT),
        name="step_pass",
    )(*inputs.values())


def per_device_blocks(
    fields,
    cotangent,
    valid_mask,
    kept_modes,
    mlp_master,
    mlp_first,
    mlp_second,
    filter_master,
    filter_first,
    filter_second,
    small_master,
    small_first,
    small_second,
    run_stats,
):
    snaps, group = lax.axis_size("snap"), lax.axis_size("sp")
    out, in_grad, *grads = block_pass(
        fields, cotangent, valid_mask, kept_modes, mlp_master, filter_master, small_master, snaps, group
    )
    snap_local, row_local, lon_total, channel = fields.shape
    positions = snap_local * snaps * row_local * group * lon_total
    out, in_grad, *stepped = step_pass(
        (out, in_grad),
        grads,
        (
            (mlp_master, mlp_first, mlp_second),
            (filter_master, filter_first, filter_second),
            (small_master, small_first, small_second),
        ),
        run_stats,
        positions,
    )
    rows_apart = (snap_local, lon_total, row_local, channel)
    out, in_grad = [
        jnp.transpose(array.reshape(rows_apart), (0, 2, 1, 3)) for array in (out, in_grad)
    ]
    return (out, in_grad, *stepped)


def per_device(*arrays):
    group, snaps = lax.axis_size("sp"), lax.axis_size("snap")
    channel, hidden = arrays[0].shape[3], arrays[4].shape[2]
    by_block = group == BLOCKS and snaps == 4 and arrays[3].shape[1] == 1
    if by_block and hidden % 512 == 0 and channel // group <= 128 and channel % (16 * group) == 0:
        return per_device_blocks(*arrays)
    return per_device_modes(*arrays)


def solution(mesh):
    return jax.shard_map(
        per_device,
        mesh=mesh,
        in_specs=(
            P("snap", "sp", None, None),
            P("snap", "sp", None, None),
            P("snap", "sp", None),
            P(None, "sp"),
            P(None, "sp", None),
            P(None, "sp", None),
            P(None, "sp", None),
            P(None, "sp", None),
            P(None, "sp", None),
            P(None, "sp", None),
            P(None, "sp"),
            P(None, "sp"),
            P(None, "sp"),
            P(),
        ),
        out_specs=(
            P("snap", "sp", None, None),
            P("snap", "sp", None, None),
            P(None, "sp", None),
            P(None, "sp", None),
            P(None, "sp", None),
            P(None, "sp", None),
            P(None, "sp", None),
            P(None, "sp", None),
            P(None, "sp", None),
            P(None, "sp", None),
            P(None, "sp"),
            P(None, "sp"),
            P(None, "sp"),
            P(None, "sp"),
            P(),
        ),
        check_vma=False,
    )
```

```python
import functools
import math

import jax
import jax.numpy as jnp
import ml_dtypes
import numpy as np
from jax import lax
from jax.experimental import pallas as pl
from jax.experimental.pallas import tpu as pltpu
from jax.sharding import PartitionSpec as P

BLOCKS = 8
NVAR = 20
STEP = 10
VMEM_LIMIT = 63 * 1024 * 1024


eps_norm = 1e-06
shrink_level = 0.01
beta_one = 0.5
beta_two = 0.5
adam_eps = 1e-08
decay_rate = 0.01
rate_mlp = 0.03
rate_filter = 0.1
rate_small = 0.2
stat_decay = 0.5


def layer_norm(values, gain_vec, shift_vec):
    centred = values - jnp.mean(values, axis=-1, keepdims=True)
    spread = jnp.mean(centred * centred, axis=-1, keepdims=True)
    return centred * lax.rsqrt(spread + eps_norm) * gain_vec + shift_vec


def shrink(values):
    return values - shrink_level * jnp.tanh(values / shrink_level)


def lon_tables(lon_total, mode_total):
    places = jnp.arange(lon_total, dtype=jnp.int32)
    orders = jnp.arange(mode_total, dtype=jnp.int32)
    angles = (places[:, None] * orders[None, :] % lon_total).astype(jnp.float32) * (
        2.0 * math.pi / lon_total
    )
    scaling = 1.0 / math.sqrt(lon_total)
    forward_tab = jnp.stack([jnp.cos(angles), -jnp.sin(angles)], axis=1) * scaling
    doubling = jnp.where(orders == 0, 1.0, 2.0).astype(jnp.float32)[:, None]
    inverse_tab = (
        jnp.stack([jnp.cos(angles).T * doubling, -jnp.sin(angles).T * doubling], axis=0) * scaling
    )
    return (forward_tab.astype(jnp.bfloat16), inverse_tab.astype(jnp.bfloat16))


def lat_table(lat_total):
    places = jnp.arange(lat_total, dtype=jnp.int32)
    angles = (places[:, None] * places[None, :] % lat_total).astype(jnp.float32) * (
        2.0 * math.pi / lat_total
    )
    cosine = jnp.cos(angles)
    sine_part = jnp.sin(angles)
    upper_rows = jnp.stack([cosine, sine_part], axis=1)
    bottom = jnp.stack([-sine_part, cosine], axis=1)
    return (jnp.stack([upper_rows, bottom], axis=0) / math.sqrt(lat_total)).astype(jnp.bfloat16)


def complex_pair(real_part, imag_part):
    return jnp.stack([jnp.stack([real_part, -imag_part]), jnp.stack([imag_part, real_part])])


gelu_scale = math.sqrt(2.0 / math.pi)
gelu_cubic = 0.044715


def gelu_both(value):
    bend = (gelu_scale * gelu_cubic) * (value * value)
    turn = jnp.tanh(value * (gelu_scale + bend))
    half = 0.5 + 0.5 * turn
    slope = half * (1.0 + (value * (1.0 - turn)) * (gelu_scale + 3.0 * bend))
    return value * half, slope


def dot_nt(left, right):
    return lax.dot_general(
        left, right, (((1,), (1,)), ((), ())), preferred_element_type=jnp.float32
    )


def dot_nn(left, right):
    return jnp.dot(left, right, preferred_element_type=jnp.float32)


def divisor(total, unit, most):
    return max(size for size in range(unit, most + 1, unit) if total % size == 0)


def mlp_body(
    tile,
    normed_ref,
    cot_ref,
    up_ref,
    down_ref,
    bias_ref,
    out_ref,
    back_ref,
    grad_up_ref,
    grad_down_ref,
    grad_bias_ref,
    normed_turned,
    cot_turned,
    act_ref,
    slope_ref,
):
    tokens = normed_ref.shape[0]

    @pl.when(pl.program_id(0) == 0)
    def _():
        normed_turned[...] = normed_ref[...].T
        cot_turned[...] = cot_ref[...].T
        out_ref[...] = jnp.zeros_like(out_ref)
        back_ref[...] = jnp.zeros_like(back_ref)

    grad_bias_ref[...] = jnp.zeros_like(grad_bias_ref)

    @pl.loop(0, tokens // tile)
    def _(step):
        rows = pl.ds(pl.multiple_of(step * tile, tile), tile)
        act, slope = gelu_both(dot_nn(normed_ref[rows, :], up_ref[...]) + bias_ref[...])
        act = act.astype(jnp.bfloat16)
        slope = (dot_nn(cot_ref[rows, :], down_ref[...]) * slope).astype(jnp.bfloat16)
        act_ref[rows, :] = act
        slope_ref[rows, :] = slope
        grad_bias_ref[...] += jnp.sum(slope.astype(jnp.float32), axis=0, keepdims=True)
        out_ref[rows, :] += dot_nt(act, down_ref[...])
        back_ref[rows, :] += dot_nt(slope, up_ref[...])

    grad_up_ref[...] = dot_nn(normed_turned[...], slope_ref[...]).astype(grad_up_ref.dtype)
    grad_down_ref[...] = dot_nn(cot_turned[...], act_ref[...]).astype(grad_down_ref.dtype)


def mlp_pass(normed, cot, weights, bias):
    tokens, channel = normed.shape
    hidden = weights.shape[2]
    width = divisor(hidden, 128, 512)
    tile = divisor(tokens, 16, 480)
    whole = pl.BlockSpec((tokens, channel), lambda j: (0, 0))
    block = pl.BlockSpec((channel, width), lambda j: (0, j))
    line = pl.BlockSpec((1, width), lambda j: (0, j))
    part = lambda which: pl.BlockSpec((None, channel, width), lambda j: (which, 0, j))
    total = jax.ShapeDtypeStruct((tokens, channel), jnp.float32)
    grads = jax.ShapeDtypeStruct((channel, hidden), jnp.bfloat16)
    return pl.pallas_call(
        functools.partial(mlp_body, tile),
        grid=(hidden // width,),
        in_specs=[whole, whole, part(0), part(1), line],
        out_specs=[whole, whole, block, block, line],
        out_shape=[total, total, grads, grads, jax.ShapeDtypeStruct((1, hidden), jnp.float32)],
        scratch_shapes=[
            pltpu.VMEM((channel, tokens), jnp.bfloat16),
            pltpu.VMEM((channel, tokens), jnp.bfloat16),
            pltpu.VMEM((tokens, width), jnp.bfloat16),
            pltpu.VMEM((tokens, width), jnp.bfloat16),
        ],
        compiler_params=pltpu.CompilerParams(vmem_limit_bytes=56 * 1024 * 1024),
        cost_estimate=pl.CostEstimate(
            flops=12 * tokens * channel * hidden,
            bytes_accessed=8 * channel * hidden + 12 * tokens * channel,
            transcendentals=tokens * hidden,
        ),
        name="mlp_pass",
    )(normed, cot, weights, weights, bias)


def spectral_front(arrived, lat_fwd, first_pair, second_pair, bias_one, bias_two):
    spectrum = jnp.einsum(
        "pkqr,nrqmd->nkpmd", lat_fwd, arrived, preferred_element_type=jnp.float32
    ).astype(jnp.bfloat16)
    snap_local, lat_total, pair_count, mode_local, channel = spectrum.shape
    blocked = spectrum.reshape(
        snap_local, lat_total, pair_count, mode_local, BLOCKS, channel // BLOCKS
    )
    pre_one = (
        jnp.einsum("nkqmbi,pqbio->nkpmbo", blocked, first_pair, preferred_element_type=jnp.float32)
        + bias_one
    )
    act_one = jax.nn.gelu(pre_one).astype(jnp.bfloat16)
    pre_two = (
        jnp.einsum("nkqmbi,pqbio->nkpmbo", act_one, second_pair, preferred_element_type=jnp.float32)
        + bias_two
    )
    return (blocked, pre_one, act_one, pre_two)


def adamw(master, first_mom, second_mom, gradient, step_rate):
    first_next = beta_one * first_mom + (1.0 - beta_one) * gradient
    second_next = beta_two * second_mom + (1.0 - beta_two) * gradient * gradient
    fix_one = 1.0 - beta_one**STEP
    fix_two = 1.0 - beta_two**STEP
    direction = first_next / fix_one / (jnp.sqrt(second_next / fix_two) + adam_eps)
    master_next = master - step_rate * (direction + decay_rate * master)
    return (master_next, first_next, second_next, master_next.astype(jnp.bfloat16))


def per_device_modes(
    fields,
    cotangent,
    valid_mask,
    kept_modes,
    mlp_master,
    mlp_first,
    mlp_second,
    filter_master,
    filter_first,
    filter_second,
    small_master,
    small_first,
    small_second,
    run_stats,
):
    group_size = lax.axis_size("sp")
    snap_local, row_local, lon_total, channel = fields.shape
    lat_total = row_local * group_size
    mode_local = kept_modes.shape[1]
    mode_total = mode_local * group_size
    block_width = channel // BLOCKS
    lon_fwd, lon_inv = lon_tables(lon_total, mode_total)
    lat_fwd = lat_table(lat_total)
    mlp_w, filt_w, small_w = (
        lax.all_gather(mlp_master.astype(jnp.bfloat16), "sp", axis=1, tiled=True),
        lax.all_gather(filter_master.astype(jnp.bfloat16), "sp", axis=1, tiled=True),
        lax.all_gather(small_master.astype(jnp.bfloat16), "sp", axis=1, tiled=True),
    )
    small_f = small_w.astype(jnp.float32)
    weights = filt_w.reshape(4, BLOCKS, block_width, block_width)
    first_pair = complex_pair(weights[0], weights[1])
    second_pair = complex_pair(weights[2], weights[3])
    bias_one = small_f[4:6].reshape(2, 1, BLOCKS, block_width)
    bias_two = small_f[6:8].reshape(2, 1, BLOCKS, block_width)
    fields_float = fields.astype(jnp.float32)
    normed, norm_pull = jax.vjp(layer_norm, fields_float, small_f[0], small_f[1])
    normed_low = normed.astype(jnp.bfloat16)
    spec_lon = jnp.einsum(
        "nrld,lqm->nrqmd", normed_low, lon_fwd, preferred_element_type=jnp.float32
    ).astype(jnp.bfloat16)
    arrived = lax.all_to_all(spec_lon, "sp", split_axis=3, concat_axis=1, tiled=True)
    spectral = spectral_front(arrived, lat_fwd, first_pair, second_pair, bias_one, bias_two)
    keep_mask = kept_modes.astype(jnp.float32)[None, :, None, :, None, None]
    masked = (shrink(spectral[3]) * keep_mask).astype(jnp.bfloat16)
    masked = masked.reshape(snap_local, lat_total, 2, mode_local, channel)
    returned = jnp.einsum(
        "pkqr,nkpmd->nrqmd", lat_fwd, masked, preferred_element_type=jnp.float32
    ).astype(jnp.bfloat16)
    home_modes = lax.all_to_all(returned, "sp", split_axis=1, concat_axis=3, tiled=True)
    filtered = jnp.einsum(
        "nrqmd,qml->nrld", home_modes, lon_inv, preferred_element_type=jnp.float32
    )
    mixture = fields_float + normed + filtered
    normed_two, norm_two_pull = jax.vjp(layer_norm, mixture, small_f[2], small_f[3])
    normed_two_low = normed_two.astype(jnp.bfloat16)
    tokens = snap_local * row_local * lon_total
    passed = mlp_pass(
        normed_two_low.reshape(tokens, channel),
        cotangent.reshape(tokens, channel),
        mlp_w,
        small_f[9:].reshape(1, -1),
    )
    output = mixture + passed[0].reshape(mixture.shape) + small_f[8]
    weight_mask = valid_mask.astype(jnp.float32)[..., None]
    variables = output[..., :NVAR]
    local_sums = jnp.stack(
        [
            jnp.sum(weight_mask * variables, axis=(0, 1, 2)),
            jnp.sum(weight_mask * variables * variables, axis=(0, 1, 2)),
        ]
    )
    total_sums = lax.psum(local_sums, ("snap", "sp"))
    positions = snap_local * lax.axis_size("snap") * lat_total * lon_total
    stats_new = stat_decay * run_stats + (1.0 - stat_decay) * total_sums / positions
    cot_float = cotangent.astype(jnp.float32)
    grad_normed_two = passed[1].reshape(mixture.shape)
    grad_bias_hidden = passed[4]
    grad_mix_norm, grad_gain_two, grad_shift_two = norm_two_pull(grad_normed_two)
    grad_mixture = cot_float + grad_mix_norm
    grad_bias_out = jnp.sum(cot_float, axis=(0, 1, 2))
    grad_filtered = grad_mixture.astype(jnp.bfloat16)
    grad_home = jnp.einsum(
        "nrld,qml->nrqmd", grad_filtered, lon_inv, preferred_element_type=jnp.float32
    ).astype(jnp.bfloat16)
    grad_returned = lax.all_to_all(grad_home, "sp", split_axis=3, concat_axis=1, tiled=True)
    grad_masked = jnp.einsum(
        "pkqr,nrqmd->nkpmd", lat_fwd, grad_returned, preferred_element_type=jnp.float32
    )
    arrived_again = lax.all_to_all(spec_lon, "sp", split_axis=3, concat_axis=1, tiled=True)
    used_front = spectral_front(arrived_again, lat_fwd, first_pair, second_pair, bias_one, bias_two)
    blocked, pre_one, act_one, pre_two = used_front
    grad_two = jax.vjp(shrink, pre_two)[1](grad_masked.reshape(pre_two.shape) * keep_mask)[
        0
    ].astype(jnp.bfloat16)
    grad_bias_two = jnp.sum(grad_two.astype(jnp.float32), axis=(0, 1, 3))
    grad_second = jnp.einsum(
        "nkqmbi,nkpmbo->pqbio", act_one, grad_two, preferred_element_type=jnp.float32
    )
    grad_act = jnp.einsum(
        "nkpmbo,pqbio->nkqmbi", grad_two, second_pair, preferred_element_type=jnp.float32
    )
    grad_one = jax.vjp(jax.nn.gelu, pre_one)[1](grad_act)[0].astype(jnp.bfloat16)
    grad_bias_one = jnp.sum(grad_one.astype(jnp.float32), axis=(0, 1, 3))
    grad_first = jnp.einsum(
        "nkqmbi,nkpmbo->pqbio", blocked, grad_one, preferred_element_type=jnp.float32
    )
    grad_spectrum = jnp.einsum(
        "nkpmbo,pqbio->nkqmbi", grad_one, first_pair, preferred_element_type=jnp.float32
    ).astype(jnp.bfloat16)
    grad_spectrum = grad_spectrum.reshape(snap_local, lat_total, 2, mode_local, channel)
    grad_lon = jnp.einsum(
        "pkqr,nkpmd->nrqmd", lat_fwd, grad_spectrum, preferred_element_type=jnp.float32
    ).astype(jnp.bfloat16)
    grad_rows = lax.all_to_all(grad_lon, "sp", split_axis=1, concat_axis=3, tiled=True)
    grad_normed = grad_mixture + jnp.einsum(
        "nrqmd,lqm->nrld", grad_rows, lon_fwd, preferred_element_type=jnp.float32
    )
    grad_field_norm, grad_gain_one, grad_shift_one = norm_pull(grad_normed)
    input_grad = grad_mixture + grad_field_norm
    grad_filter = jnp.stack(
        [
            grad_first[0, 0] + grad_first[1, 1],
            grad_first[1, 0] - grad_first[0, 1],
            grad_second[0, 0] + grad_second[1, 1],
            grad_second[1, 0] - grad_second[0, 1],
        ]
    ).reshape(4, channel, block_width)
    grad_small = jnp.concatenate(
        [
            jnp.stack([grad_gain_one, grad_shift_one, grad_gain_two, grad_shift_two]),
            grad_bias_one.reshape(2, channel),
            grad_bias_two.reshape(2, channel),
            grad_bias_out[None, :],
            grad_bias_hidden.reshape(-1, channel),
        ],
        axis=0,
    )
    shares = (
        jnp.stack([
            lax.psum_scatter(part, "sp", scatter_dimension=0, tiled=True) for part in passed[2:4]
        ]),
        lax.psum_scatter(grad_filter, "sp", scatter_dimension=1, tiled=True),
        lax.psum_scatter(grad_small, "sp", scatter_dimension=1, tiled=True),
    )
    owned = (
        lax.psum(shares[0].astype(jnp.bfloat16), "snap").astype(jnp.float32),
        lax.psum(shares[1].astype(jnp.bfloat16), "snap").astype(jnp.float32),
        lax.psum(shares[2].astype(jnp.bfloat16), "snap").astype(jnp.float32),
    )
    mlp_new, mlp_first_new, mlp_second_new, mlp_copy = adamw(
        mlp_master, mlp_first, mlp_second, owned[0], rate_mlp
    )
    filter_new, filter_first_new, filter_second_new, filter_copy = adamw(
        filter_master, filter_first, filter_second, owned[1], rate_filter
    )
    small_new, small_first_new, small_second_new, small_copy = adamw(
        small_master, small_first, small_second, owned[2], rate_small
    )
    return (
        output.astype(jnp.bfloat16),
        input_grad,
        mlp_new,
        mlp_first_new,
        mlp_second_new,
        mlp_copy,
        filter_new,
        filter_first_new,
        filter_second_new,
        filter_copy,
        small_new,
        small_first_new,
        small_second_new,
        small_copy,
        stats_new,
    )


def lon_matrix(lon_total, mode_total, snaps, rows):
    places = np.arange(lon_total)
    orders = np.arange(mode_total)
    angles = (places[:, None] * orders[None, :] % lon_total) * (2.0 * math.pi / lon_total)
    doubling = np.where(orders == 0, 1.0, 2.0)
    scaling = 1.0 / math.sqrt(lon_total)
    forward = np.stack([np.cos(angles), -np.sin(angles)], axis=1) * scaling
    inverse = forward * doubling

    def spread(table):
        table = np.einsum(
            "ab,lx,rs->alrbsx", np.eye(snaps), table.reshape(lon_total, -1), np.eye(rows)
        )
        return table.reshape(snaps * lon_total * rows, -1).astype(ml_dtypes.bfloat16)

    return spread(forward), spread(inverse)


def lon_turn(lon_total, rows):
    turn = np.einsum("lk,rs->rlks", np.eye(lon_total), np.eye(rows))
    return turn.reshape(rows, lon_total, lon_total * rows).astype(ml_dtypes.bfloat16)


def lat_matrix(lat_total, mode_total):
    places = np.arange(lat_total)
    angles = (places[:, None] * places[None, :] % lat_total) * (2.0 * math.pi / lat_total)
    cosine, sine = np.cos(angles), np.sin(angles)
    table = np.stack([np.stack([cosine, sine], axis=1), np.stack([-sine, cosine], axis=1)])
    table = np.einsum("pkqr,ab->pakrqb", table / math.sqrt(lat_total), np.eye(mode_total))
    size = 2 * lat_total * mode_total
    return table.reshape(size, size).astype(ml_dtypes.bfloat16)


class Refs:
    pass


def block_body(names, sizes, *refs):
    g = Refs()
    for name, ref in zip(names, refs, strict=True):
        setattr(g, name, ref)
    snaps, group, parts, width = sizes
    levels = group // 2
    tokens = g.fields.shape[0] * g.fields.shape[1]
    channel = g.fields.shape[2]
    tiles = channel // 128
    owned = channel // group
    half = width // 2
    quarter = width // snaps
    tile = divisor(tokens, 16, 480)
    strip = divisor(tokens // 2, 48, 144)
    sub = divisor(strip, 16, 48)
    low = jnp.bfloat16
    f32 = jnp.float32

    me_snap = lax.axis_index("snap")
    me_sp = lax.axis_index("sp")
    core = lax.rem(me_sp, 2)
    level = me_sp // 2

    def at(snap, sp):
        return {"snap": snap, "sp": sp}

    def sp_after(step):
        return lax.rem(me_sp + step, group)

    def sp_before(step):
        return lax.rem(me_sp + group - step, group)

    def snap_after(step):
        return lax.rem(me_snap + step, snaps)

    def snap_before(step):
        return lax.rem(me_snap + snaps - step, snaps)

    def level_after(step):
        return lax.rem(level + step, levels)

    def level_before(step):
        return lax.rem(level + levels - step, levels)

    other_core = at(me_snap, me_sp + 1 - 2 * core)

    def send(src, dst, sems, index, target):
        return pltpu.make_async_remote_copy(
            src_ref=src,
            dst_ref=dst,
            send_sem=sems[0].at[index],
            recv_sem=sems[1].at[index],
            device_id=target,
            device_id_type=pl.DeviceIdType.MESH,
        )

    half_tokens = tokens // 2

    def strips(body, first=0, count=tokens):
        @pl.loop(0, count // strip)
        def _(step):
            for at_row in range(0, strip, sub):
                body(pl.ds(pl.multiple_of(first + step * strip + at_row, 16), sub))

    def half_strips(body, part):
        strips(body, part * half_tokens, half_tokens)

    def half_rows(part):
        return slice(part * half_tokens, (part + 1) * half_tokens)

    def fold(value):
        return jnp.sum(value.reshape(-1, 8, value.shape[1]), axis=0)

    def columns(name):
        ref = getattr(g, name)
        return ref.reshape(tiles, ref.shape[1] * ref.shape[2], 128)

    def columns_of(name, rows):
        view = columns(name)
        return jnp.concatenate([view[tile_at, rows, :] for tile_at in range(tiles)], axis=1)

    def store_columns(name, rows, value):
        view = columns(name)
        for tile_at in range(tiles):
            view[tile_at, rows, :] = value[:, tile_at * 128 : (tile_at + 1) * 128]

    def column_copies(near, far, sems, out):
        copies = []
        for tile_at in range(tiles):
            ends = [near.at[tile_at], far.at[:, :, tile_at * 128 : (tile_at + 1) * 128]]
            if not out:
                ends.reverse()
            copies.append(pltpu.make_async_copy(*ends, sems.at[tile_at]))
        return copies

    loads = {}

    def load(name, index):
        copy = pltpu.make_async_copy(getattr(g, name), getattr(g, name + "_in"), g.load_sem.at[index])
        copy.start()
        loads[name] = copy

    for index, name in enumerate(
        [name for name in names[: names.index("out")] if name not in ("mlp", "fields", "cot")]
    ):
        load(name, index)
    fields_load = column_copies(g.fields_cols, g.fields, g.fields_sem, False)
    cot_load = column_copies(g.cot_cols, g.cot, g.cot_sem, False)
    for copy in fields_load + cot_load:
        copy.start()

    def master_load(part):
        return pltpu.make_async_copy(
            g.mlp.at[:, :, part * width : (part + 1) * width],
            g.mlp_part.at[part % 2],
            g.load_sem.at[len(loads) + part % 2],
        )

    master_load(0).start()
    master_load(1).start()

    barrier = pltpu.get_barrier_semaphore()
    peers = [at(me_snap, sp_after(step)) for step in range(1, group)]
    peers += [at(snap_after(step), me_sp) for step in range(1, snaps)]
    for peer in peers:
        pl.semaphore_signal(
            barrier, inc=1, device_id=peer, device_id_type=pl.DeviceIdType.MESH
        )

    loads["small"].wait()
    loads["kept"].wait()
    g.own_small[...] = jnp.zeros_like(g.own_small)
    rows_small = g.small.shape[0]
    g.own_small[0:rows_small, 0:owned] = g.small_in[...].astype(low).astype(f32)
    pairs_kept = g.kept.shape[1]
    lines = lax.broadcasted_iota(jnp.int32, (pairs_kept, pairs_kept), 0)
    places = lax.broadcasted_iota(jnp.int32, (pairs_kept, pairs_kept), 1)
    kept = jnp.where(lines == places, g.kept_in[...].astype(f32), 0.0)
    g.own_small[16:, :] = jnp.broadcast_to(
        jnp.sum(kept, axis=1, keepdims=True), (pairs_kept, g.own_small.shape[1])
    )
    pl.semaphore_wait(barrier, len(peers))

    def small_copy(step):
        return send(
            g.own_small, g.all_small.at[me_sp], (g.small_s, g.small_r), step, at(me_snap, sp_after(step))
        )

    for step in range(1, group):
        small_copy(step).start()
    g.all_small[me_sp] = g.own_small[...]

    snap_low = lax.rem(me_snap, 2)
    snap_high = me_snap // 2
    beside_low = me_snap + 1 - 2 * snap_low
    beside_high = me_snap + 2 - 4 * snap_high

    def own_quarter(part):
        odd = lax.rem(part, 2)
        return (1 - odd) * me_snap + odd * (2 * snap_low + snap_high)

    def half_quarters(part):
        return pl.ds(2 * (own_quarter(part) // 2), 2)

    def own_rows(sp):
        return pl.ds(pl.multiple_of(sp * owned, owned), owned)

    def first_copy(part, step):
        target = sp_after(step)
        matrix = lax.rem(target, 2)
        place = own_quarter(part)
        return send(
            g.own_w.at[part, matrix, place],
            g.all_w.at[part, matrix, place, own_rows(me_sp)],
            (g.first_s, g.first_r),
            (part, step),
            at(me_snap, target),
        )

    def first_local(part):
        place = own_quarter(part)
        return pltpu.make_async_copy(
            g.own_w.at[part, core, place],
            g.all_w.at[part, core, place, own_rows(me_sp)],
            g.first_s.at[part, 0],
        )

    def second_copy(part):
        odd = lax.rem(part, 2)
        view = g.all_w.at[part, core, own_quarter(part)]
        target = at((1 - odd) * beside_low + odd * beside_high, me_sp)
        return send(view, view, (g.second_s, g.second_r), part, target)

    def third_copy(part):
        odd = lax.rem(part, 2)
        view = g.all_w.at[part, core, half_quarters(part)]
        target = at((1 - odd) * beside_high + odd * beside_low, me_sp)
        return send(view, view, (g.third_s, g.third_r), part, target)

    def fourth_copy(part):
        view = g.all_w.at[part, core]
        return send(view, view, (g.fourth_s, g.fourth_r), part, other_core)

    def start_first(part):
        for step in range(1, group):
            first_copy(part, step).start()
        first_local(part).start()

    def pass_second(part):
        for step in range(1, group):
            first_copy(part, step).wait_recv()
        first_local(part).wait()
        second_copy(part).start()

    def pass_third(part):
        second_copy(part).wait_recv()
        third_copy(part).start()

    def pass_fourth(part):
        third_copy(part).wait_recv()
        fourth_copy(part).start()

    for part in range(parts):
        master_load(part).wait()
        for place in range(snaps):
            cols = slice(place * quarter, (place + 1) * quarter)
            g.own_w[part, :, place] = g.mlp_part[part % 2, :, :, cols].astype(low)
        if part + 2 < parts:
            master_load(part + 2).start()
        if part < 2:
            start_first(part)

    for copy in fields_load:
        copy.wait()

    def first_unit(rows):
        values = columns_of("fields_cols", rows).astype(f32)
        centred = values - jnp.mean(values, axis=-1, keepdims=True)
        scale = lax.rsqrt(jnp.mean(centred * centred, axis=-1, keepdims=True) + eps_norm)
        g.scale_one[rows, :] = scale
        g.grid[rows, :] = centred * scale

    strips(first_unit)
    for step in range(1, group):
        small_copy(step).wait_recv()
    for sp in range(group):
        g.gains[:, sp * owned : (sp + 1) * owned] = g.all_small[sp, 0:16, 0:owned]
        g.keep[sp * pairs_kept : (sp + 1) * pairs_kept, :] = g.all_small[sp, 16:, :]

    def first_norm(rows):
        unit = g.grid[rows, :]
        normed = unit * g.gains[0:1, :] + g.gains[1:2, :]
        g.unit_one[rows, :] = unit.astype(low)
        g.normed[rows, :] = normed.astype(low)
        g.grid[rows, :] = columns_of("fields_cols", rows).astype(f32) + normed

    half_snaps = g.arrived.shape[0] // 2

    def some_snaps(part):
        return pl.ds(part * half_snaps, half_snaps)

    def to_blocks(table, which, part):
        modes = dot_nn(table, g.normed[half_rows(part), :])
        for block in range(group):
            cut = modes[:, block * owned : (block + 1) * owned]
            cut = jnp.concatenate([cut, jnp.zeros((cut.shape[0], 128 - owned), f32)], axis=1)
            g.modes[part, block] = cut.astype(low).reshape(g.modes.shape[2:])
        for step in range(1, group):
            block_copy(which, part, step).start()
        g.arrived[some_snaps(part), mode_rows(me_sp), :] = g.modes[part, me_sp]

    def mode_rows(sp):
        size = g.modes.shape[3]
        return pl.ds(pl.multiple_of(sp * size, size), size)

    def block_copy(which, part, step):
        target = sp_after(step)
        return send(
            g.modes.at[part, target],
            g.arrived.at[some_snaps(part), mode_rows(me_sp), :],
            (g.block_s, g.block_r),
            (which, part, step),
            at(me_snap, target),
        )

    def row_copy(which, part, step):
        target = sp_after(step)
        return send(
            g.turned.at[some_snaps(part), mode_rows(target), :],
            g.home.at[part, me_sp],
            (g.row_s, g.row_r),
            (which, part, step),
            at(me_snap, target),
        )

    def to_rows(which, part):
        for step in range(1, group):
            row_copy(which, part, step).start()
        g.home[part, me_sp] = g.turned[some_snaps(part), mode_rows(me_sp), :]

    def home_modes(which, part):
        for step in range(1, group):
            row_copy(which, part, step).wait_recv()
        count = g.gathered.shape[1]
        for block in range(group):
            g.gathered[part, :, block * owned : (block + 1) * owned] = (
                g.home[part, block].reshape(count, 128)[:, 0:owned].astype(f32)
            )
        g.home_low[part] = g.gathered[part].astype(low)

    loads["lon_f"].wait()
    for part in range(2):
        half_strips(first_norm, part)
        to_blocks(g.lon_f_in[...], 0, part)
        pass_second(part)

    loads["filt"].wait()
    for weight, first in ((g.weight_one, 0), (g.weight_two, 2)):
        weight[...] = jnp.zeros_like(weight)
        real = g.filt_in[first].astype(low)
        imag = g.filt_in[first + 1].astype(low)
        weight[0:owned, 0:owned] = real
        weight[128 : 128 + owned, 128 : 128 + owned] = real
        weight[0:owned, 128 : 128 + owned] = imag
        weight[128 : 128 + owned, 0:owned] = -imag

    def bias_row(first):
        return jnp.concatenate(
            [g.own_small[first : first + 1, :], g.own_small[first + 1 : first + 2, :]], axis=1
        )

    for copy in cot_load:
        copy.wait()

    def flat_cot(rows):
        g.cot_in[rows, :] = columns_of("cot_cols", rows)

    strips(flat_cot)
    pass_third(0)
    loads["lat_f"].wait()
    loads["lat_b"].wait()
    pairs = g.arrived.shape[1] // 2
    half_modes = half_snaps * pairs

    def mode_half(part):
        return slice(part * half_modes, (part + 1) * half_modes)

    def spectra(out, kind, part):
        for snap in range(part * half_snaps, (part + 1) * half_snaps):
            spectrum = dot_nn(g.lat_f_in[...], g.arrived[snap]).astype(kind)
            rows = slice(snap * pairs, (snap + 1) * pairs)
            out[rows, 0:128] = spectrum[0:pairs]
            out[rows, 128:256] = spectrum[pairs:]

    def grids(values, part):
        for index in range(half_snaps):
            rows = values[index * pairs : (index + 1) * pairs]
            rows = jnp.concatenate([rows[:, 0:128], rows[:, 128:256]], axis=0)
            g.turned[part * half_snaps + index] = dot_nn(g.lat_b_in[...], rows).astype(low)

    def keep_half():
        keep = jnp.concatenate([g.keep[...], g.keep[...]], axis=1)
        return jnp.concatenate([keep] * half_snaps, axis=0)

    for part in range(2):
        for step in range(1, group):
            block_copy(0, part, step).wait_recv()
        rows = mode_half(part)
        spectra(g.spectrum, low, part)
        g.pre_one[rows, :] = dot_nn(g.spectrum[rows, :], g.weight_one[...]) + bias_row(4)
        g.act_one[rows, :] = gelu_both(g.pre_one[rows, :])[0].astype(low)
        g.pre_two[rows, :] = dot_nn(g.act_one[rows, :], g.weight_two[...]) + bias_row(6)
        grids((shrink(g.pre_two[rows, :]) * keep_half()).astype(low), part)
        to_rows(0, part)
        if part == 0:
            pass_third(1)
    for part in range(2, 4):
        start_first(part)
    g.cot_turned[...] = g.cot_in[...].T

    loads["lon_i"].wait()

    def second_norm(rows):
        values = g.grid[rows, :]
        centred = values - jnp.mean(values, axis=-1, keepdims=True)
        scale = lax.rsqrt(jnp.mean(centred * centred, axis=-1, keepdims=True) + eps_norm)
        centred = centred * scale
        g.unit_two[rows, :] = centred.astype(low)
        g.scale_two[rows, :] = scale
        g.normed[rows, :] = (centred * g.gains[2:3, :] + g.gains[3:4, :]).astype(low)
        g.grid[rows, :] = values + g.gains[8:9, :]
        g.back[rows, :] = jnp.zeros((sub, channel), f32)

    for part in range(2):
        home_modes(0, part)
        g.grid[half_rows(part), :] += dot_nn(g.lon_i_in[...], g.home_low[part])
        half_strips(second_norm, part)
        pass_fourth(part)
        pass_second(2 + part)
    g.normed_turned[...] = g.normed[...].T
    for part in range(2, 4):
        pass_third(part)
    for part in range(4, parts):
        start_first(part)
    flat = jnp.concatenate([g.gains[9 + row : 10 + row, :] for row in range(rows_small - 9)], axis=1)
    for part in range(parts):
        g.bias[part] = flat[:, part * width : (part + 1) * width]

    def core_copy(part, matrix):
        slot = lax.rem(part, 2)
        return send(
            g.grads.at[slot, matrix, :, 1 - core],
            g.core_got.at[slot, matrix],
            (g.core_s, g.core_r),
            (slot, matrix),
            other_core,
        )

    places_one = (snap_low, snap_high)
    places_two = (snap_high, snap_low)
    beside_one = (beside_low, beside_high)
    beside_two = (beside_high, beside_low)
    place_last = (2 * snap_low + snap_high, me_snap)

    def half_copy(part, matrix):
        slot = lax.rem(part, 2)
        return send(
            g.half_out.at[slot, matrix, 1 - places_one[matrix]],
            g.half_got.at[slot, matrix],
            (g.half_s, g.half_r),
            (slot, matrix),
            at(beside_one[matrix], me_sp),
        )

    def quarter_copy(part, matrix):
        slot = lax.rem(part, 2)
        return send(
            g.quarter_out.at[slot, matrix, 1 - places_two[matrix]],
            g.quarter_got.at[slot, matrix],
            (g.quarter_s, g.quarter_r),
            (slot, matrix),
            at(beside_two[matrix], me_sp),
        )

    def level_copy(part, step):
        slot = lax.rem(part, 2)
        target = level_after(step)
        return send(
            g.level_out.at[slot, target],
            g.level_got.at[slot, level],
            (g.level_s, g.level_r),
            (slot, step),
            at(me_snap, 2 * target + core),
        )

    def last_copy(part, matrix, step):
        view = g.total.at[part, place_last[matrix], matrix]
        return send(
            view, view, (g.last_s, g.last_r), (part, matrix, step), at(snap_after(step), me_sp)
        )

    def half_stage(part):
        slot = lax.rem(part, 2)
        for matrix in range(2):

            @pl.when(part >= 2)
            def _(matrix=matrix):
                half_copy(part - 2, matrix).wait_send()

            core_copy(part, matrix).wait_recv()
            for row in range(levels):
                both = g.grads[slot, matrix, row, core].astype(f32) + g.core_got[
                    slot, matrix, row
                ].astype(f32)
                both = both.astype(low)
                g.half_out[slot, matrix, 0, row] = both[:, 0:half]
                g.half_out[slot, matrix, 1, row] = both[:, half:width]
            half_copy(part, matrix).start()

    def quarter_stage(part):
        slot = lax.rem(part, 2)
        for matrix in range(2):

            @pl.when(part >= 2)
            def _(matrix=matrix):
                quarter_copy(part - 2, matrix).wait_send()

            half_copy(part, matrix).wait_recv()
            for row in range(levels):
                both = g.half_out[slot, matrix, places_one[matrix], row].astype(f32) + g.half_got[
                    slot, matrix, row
                ].astype(f32)
                both = both.astype(low)
                g.quarter_out[slot, matrix, 0, row] = both[:, 0:quarter]
                g.quarter_out[slot, matrix, 1, row] = both[:, quarter:half]
            quarter_copy(part, matrix).start()

    def level_stage(part):
        slot = lax.rem(part, 2)

        @pl.when(part >= 2)
        def _():
            for step in range(1, levels):
                level_copy(part - 2, step).wait_send()

        for matrix in range(2):
            quarter_copy(part, matrix).wait_recv()
            for row in range(levels):
                both = g.quarter_out[slot, matrix, places_two[matrix], row].astype(
                    f32
                ) + g.quarter_got[slot, matrix, row].astype(f32)
                g.level_out[slot, row, matrix] = both.astype(low)
        for step in range(1, levels):
            level_copy(part, step).start()

    def last_stage(part):
        slot = lax.rem(part, 2)
        for step in range(1, levels):
            level_copy(part, step).wait_recv()
        for matrix in range(2):
            sums = g.level_out[slot, level, matrix].astype(f32)
            for step in range(1, levels):
                sums += g.level_got[slot, level_before(step), matrix].astype(f32)
            g.total[part, place_last[matrix], matrix] = sums.astype(low)
            for step in range(1, snaps):
                last_copy(part, matrix, step).start()

    def weight(part, matrix):
        return jnp.concatenate([g.all_w[part, matrix, place] for place in range(snaps)], axis=1)

    @pl.loop(0, parts)
    def _(part):
        slot = lax.rem(part, 2)
        fourth_copy(part).wait_recv()

        @pl.when((part >= 1) & (part + 1 < parts))
        def _():
            pass_fourth(part + 1)

        g.grad_bias[part] = jnp.zeros(g.grad_bias.shape[1:], f32)

        @pl.loop(0, tokens // tile)
        def _(step):
            rows = pl.ds(pl.multiple_of(step * tile, tile), tile)
            act, slope = gelu_both(dot_nn(g.normed[rows, :], weight(part, 0)) + g.bias[part])
            act = act.astype(low)
            slope = (dot_nn(g.cot_in[rows, :], weight(part, 1)) * slope).astype(low)
            g.act[rows, :] = act
            g.slope[rows, :] = slope
            g.grad_bias[part] += fold(slope.astype(f32))
            g.grid[rows, :] += dot_nt(act, weight(part, 1))
            g.back[rows, :] += dot_nt(slope, weight(part, 0))

        @pl.when(part == 0)
        def _():
            for later in range(4, parts):
                pass_second(later)

        @pl.when(part == 1)
        def _():
            for later in range(4, parts):
                pass_third(later)

        @pl.when(part >= 4)
        def _():
            last_stage(part - 4)

        @pl.when(part >= 3)
        def _():
            level_stage(part - 3)

        @pl.when(part >= 2)
        def _():
            quarter_stage(part - 2)

        @pl.when(part >= 1)
        def _():
            half_stage(part - 1)

        @pl.when(part >= 2)
        def _():
            for matrix in range(2):
                core_copy(part - 2, matrix).wait_send()

        shape = g.grads.shape[2:]
        g.grads[slot, 0] = dot_nn(g.normed_turned[...], g.slope[...]).astype(low).reshape(shape)
        core_copy(part, 0).start()
        g.grads[slot, 1] = dot_nn(g.cot_turned[...], g.act[...]).astype(low).reshape(shape)
        core_copy(part, 1).start()

    g.folds[...] = jnp.zeros_like(g.folds)

    def second_back(rows):
        grad = g.back[rows, :]
        unit = g.unit_two[rows, :].astype(f32)
        cot = g.cot_in[rows, :].astype(f32)
        pulled = grad * g.gains[2:3, :]
        middle = jnp.mean(pulled, axis=-1, keepdims=True)
        slant = jnp.mean(pulled * unit, axis=-1, keepdims=True)
        total = cot + g.scale_two[rows, :] * (pulled - middle - unit * slant)
        g.back[rows, :] = total
        g.normed[rows, :] = total.astype(low)
        g.folds[2] += fold(grad * unit)
        g.folds[3] += fold(grad)
        g.folds[4] += fold(cot)

    loads["lon_it"].wait()
    for part in range(2):
        half_strips(second_back, part)
        for step in range(1, group):
            block_copy(0, part, step).wait_send()
        to_blocks(g.lon_it_in[...], 1, part)

    last_stage(parts - 4)
    level_stage(parts - 3)
    quarter_stage(parts - 2)
    half_stage(parts - 1)

    def low_out(rows):
        store_columns("fields_cols", rows, g.grid[rows, :].astype(low))

    strips(low_out)
    out_copies = column_copies(g.fields_cols, g.out, g.fields_sem, True)
    for copy in out_copies:
        copy.start()
    loads["valid"].wait()
    loads["turn"].wait()
    weigh = sum(
        dot_nn(g.valid_in[:, row, :].astype(f32).astype(low), g.turn_in[row])
        for row in range(g.valid.shape[1])
    )
    places_each = weigh.shape[1]
    precise = lax.Precision.HIGHEST
    sums = [jnp.zeros((1, 128), f32), jnp.zeros((1, 128), f32)]
    for snap in range(g.valid.shape[0]):
        variables = g.grid[snap * places_each : (snap + 1) * places_each, 0:128]
        for index, value in enumerate((variables, variables * variables)):
            sums[index] += jnp.dot(
                weigh[snap : snap + 1, :], value, precision=precise, preferred_element_type=f32
            )

    def dot_tn(left, right):
        return lax.dot_general(
            left, right, (((0,), (0,)), ((), ())), preferred_element_type=f32
        )

    def filter_rows(first, grad):
        g.pair_grad[...] = grad
        real = g.pair_grad[0:128, 0:128] + g.pair_grad[128:256, 128:256]
        imag = g.pair_grad[0:128, 128:256] - g.pair_grad[128:256, 0:128]
        g.filt_out[me_snap, first] = real[0:owned].astype(low)
        g.filt_out[me_snap, first + 1] = imag[0:owned].astype(low)

    for part in range(2):
        for step in range(1, group):
            block_copy(1, part, step).wait_recv()
        rows = mode_half(part)
        spectra(g.grad_pre, f32, part)
        bend = jnp.tanh(g.pre_two[rows, :] / shrink_level)
        grad = (g.grad_pre[rows, :] * keep_half() * (bend * bend)).astype(low)
        g.grad_two[rows, :] = grad
        grad = dot_nt(grad, g.weight_two[...]) * gelu_both(g.pre_one[rows, :])[1]
        grad = grad.astype(low)
        g.grad_one[rows, :] = grad
        for step in range(1, group):
            row_copy(0, part, step).wait_send()
        grids(dot_nt(grad, g.weight_one[...]).astype(low), part)
        to_rows(1, part)
    last_stage(parts - 3)
    level_stage(parts - 2)
    quarter_stage(parts - 1)
    bias_one = jnp.sum(g.grad_one[...].astype(f32), axis=0, keepdims=True)
    bias_two = jnp.sum(g.grad_two[...].astype(f32), axis=0, keepdims=True)
    filter_rows(2, dot_tn(g.act_one[...], g.grad_two[...]))
    filter_rows(0, dot_tn(g.spectrum[...], g.grad_one[...]))

    def filter_copy(step):
        view = g.filt_out.at[me_snap]
        return send(view, view, (g.filt_s, g.filt_r), step, at(snap_after(step), me_sp))

    for step in range(1, snaps):
        filter_copy(step).start()


    loads["lon_ft"].wait()
    strip_pairs = strip // g.fields.shape[1]
    grad_view = g.grad_cols.reshape(2, tiles, strip, 128)

    def grad_copies(place, slot):
        pairs_out = pl.ds(place * strip_pairs, strip_pairs)
        return column_copies(
            g.grad_cols.at[slot], g.in_grad.at[pairs_out], g.grad_sem.at[slot], True
        )

    steps = half_tokens // strip
    for part in range(2):
        home_modes(1, part)
        if part == 1:
            last_stage(parts - 2)
            level_stage(parts - 1)
        g.grid[half_rows(part), :] = g.back[half_rows(part), :] + dot_nn(
            g.lon_ft_in[...], g.home_low[part]
        )

        @pl.loop(0, steps)
        def _(step):
            place = part * steps + step
            slot = lax.rem(place, 2)

            @pl.when(place >= 2)
            def _():
                for copy in grad_copies(place, slot):
                    copy.wait()

            for at_row in range(0, strip, sub):
                rows = pl.ds(pl.multiple_of(place * strip + at_row, 16), sub)
                grad = g.grid[rows, :]
                unit = g.unit_one[rows, :].astype(f32)
                pulled = grad * g.gains[0:1, :]
                middle = jnp.mean(pulled, axis=-1, keepdims=True)
                slant = jnp.mean(pulled * unit, axis=-1, keepdims=True)
                total = g.back[rows, :] + g.scale_one[rows, :] * (pulled - middle - unit * slant)
                for tile_at in range(tiles):
                    grad_view[slot, tile_at, at_row : at_row + sub, :] = total[
                        :, tile_at * 128 : (tile_at + 1) * 128
                    ]
                g.folds[0] += fold(grad * unit)
                g.folds[1] += fold(grad)
            for copy in grad_copies(place, slot):
                copy.start()

    g.grad_rows[...] = jnp.zeros_like(g.grad_rows)
    for index, row in enumerate((0, 1, 2, 3, 8)):
        g.grad_rows[row : row + 1, :] = jnp.sum(g.folds[index], axis=0, keepdims=True)
    flat = jnp.concatenate(
        [jnp.sum(g.grad_bias[part], axis=0, keepdims=True) for part in range(parts)], axis=1
    )
    for row in range(rows_small - 9):
        g.grad_rows[9 + row : 10 + row, :] = flat[:, row * channel : (row + 1) * channel]
    for block in range(group):
        g.tiles[block] = jnp.zeros(g.tiles.shape[1:], f32)
        g.tiles[block, :, 0:owned] = g.grad_rows[:, block * owned : (block + 1) * owned]
        g.tiles[block, 13:14, :] = sums[0]
        g.tiles[block, 14:15, :] = sums[1]

    def tile_copy(step):
        target = sp_after(step)
        return send(
            g.tiles.at[target], g.tiles_got.at[me_sp], (g.tile_s, g.tile_r), step, at(me_snap, target)
        )

    def snap_tile_copy(step):
        view = g.snap_tiles.at[me_snap]
        return send(view, view, (g.snap_tile_s, g.snap_tile_r), step, at(snap_after(step), me_sp))

    for step in range(1, group):
        tile_copy(step).start()
    last_stage(parts - 1)

    g.tiles_got[me_sp] = g.tiles[me_sp]
    for step in range(1, group):
        tile_copy(step).wait_recv()
    tile_sum = g.tiles_got[0]
    for sp in range(1, group):
        tile_sum += g.tiles_got[sp]
    g.snap_tiles[me_snap] = tile_sum
    g.snap_tiles[me_snap, 4:5, :] = bias_one[:, 0:128]
    g.snap_tiles[me_snap, 5:6, :] = bias_one[:, 128:256]
    g.snap_tiles[me_snap, 6:7, :] = bias_two[:, 0:128]
    g.snap_tiles[me_snap, 7:8, :] = bias_two[:, 128:256]
    for step in range(1, snaps):
        snap_tile_copy(step).start()

    for step in range(1, snaps):
        filter_copy(step).wait_recv()
    filter_sum = g.filt_out[0].astype(f32)
    for snap in range(1, snaps):
        filter_sum += g.filt_out[snap].astype(f32)
    g.grad_filt[...] = filter_sum
    for part in range(parts):
        for matrix in range(2):
            for step in range(1, snaps):
                last_copy(part, matrix, step).wait_recv()
    grads_out = pltpu.make_async_copy(g.total, g.grad_mlp, g.load_sem.at[3])
    grads_out.start()
    for step in range(1, snaps):
        snap_tile_copy(step).wait_recv()
    tile_sum = g.snap_tiles[0]
    for snap in range(1, snaps):
        tile_sum += g.snap_tiles[snap]
    g.grad_small[...] = tile_sum

    grads_out.wait()
    for copy in out_copies:
        copy.wait()
    for slot in range(2):
        for copy in grad_copies(0, slot):
            copy.wait()
    for step in range(1, group):
        small_copy(step).wait_send()
        for part in range(2):
            block_copy(1, part, step).wait_send()
            row_copy(1, part, step).wait_send()
        tile_copy(step).wait_send()
        for part in range(parts):
            first_copy(part, step).wait_send()
    for part in range(parts):
        second_copy(part).wait_send()
        third_copy(part).wait_send()
        fourth_copy(part).wait_send()
    for part in (parts - 2, parts - 1):
        for matrix in range(2):
            core_copy(part, matrix).wait_send()
            half_copy(part, matrix).wait_send()
            quarter_copy(part, matrix).wait_send()
        for step in range(1, levels):
            level_copy(part, step).wait_send()
    for step in range(1, snaps):
        filter_copy(step).wait_send()
        snap_tile_copy(step).wait_send()
        for part in range(parts):
            for matrix in range(2):
                last_copy(part, matrix, step).wait_send()


def block_pass(fields, cot, valid, kept, mlp, filt, small, snaps, group):
    snap_local, row_local, lon_total, channel = fields.shape
    tokens = snap_local * row_local * lon_total
    hidden = mlp.shape[2]
    lat_total = row_local * group
    modes = kept.shape[1] * group
    owned = channel // group
    width = 512
    parts = hidden // width
    levels = group // 2
    quarter = width // snaps
    low, f32 = jnp.bfloat16, jnp.float32
    half = width // 2
    half_snaps = snap_local // 2
    lon_f, lon_i = lon_matrix(lon_total, modes, half_snaps, row_local)

    def paired(array):
        return jnp.transpose(array, (0, 2, 1, 3)).reshape(-1, row_local, channel)

    lat_f = lat_matrix(lat_total, modes)
    pair = 2 * modes * row_local
    spread = half_snaps * row_local * 2 * modes
    inputs = dict(
        small=small,
        kept=kept.T,
        fields=paired(fields),
        lon_f=jnp.asarray(np.ascontiguousarray(lon_f.T)),
        filt=filt,
        lat_f=jnp.asarray(lat_f),
        lat_b=jnp.asarray(np.ascontiguousarray(lat_f.T)),
        cot=paired(cot),
        lon_i=jnp.asarray(lon_i),
        valid=valid,
        turn=jnp.asarray(lon_turn(lon_total, row_local)),
        lon_it=jnp.asarray(np.ascontiguousarray(lon_i.T)),
        lon_ft=jnp.asarray(lon_f),
        mlp=mlp,
    )
    outputs = dict(
        out=jax.ShapeDtypeStruct((tokens // row_local, row_local, channel), low),
        in_grad=jax.ShapeDtypeStruct((tokens // row_local, row_local, channel), f32),
        grad_mlp=jax.ShapeDtypeStruct((parts, snaps, 2, owned, quarter), low),
        grad_filt=jax.ShapeDtypeStruct((4, owned, 128), f32),
        grad_small=jax.ShapeDtypeStruct((16, 128), f32),
    )
    vmem = pltpu.VMEM
    dma = pltpu.SemaphoreType.DMA
    scratch = {
        name + "_in": vmem(value.shape, value.dtype)
        for name, value in inputs.items()
        if name not in ("mlp", "fields", "cot")
    }
    tiles = channel // 128
    cols = (tiles, tokens // row_local, row_local, 128)
    strip = divisor(tokens // 2, 48, 144)
    scratch |= dict(
        mlp_part=vmem((2, 2, owned, width), f32),
        fields_cols=vmem(cols, low),
        cot_cols=vmem(cols, low),
        grad_cols=vmem((2, tiles, strip // row_local, row_local, 128), f32),
        grad_sem=dma((2, tiles)),
        fields_sem=dma((tiles,)),
        cot_sem=dma((tiles,)),
        cot_in=vmem((tokens, channel), low),
        grid=vmem((tokens, channel), f32),
        back=vmem((tokens, channel), f32),
        normed=vmem((tokens, channel), low),
        normed_turned=vmem((channel, tokens), low),
        cot_turned=vmem((channel, tokens), low),
        unit_one=vmem((tokens, channel), low),
        unit_two=vmem((tokens, channel), low),
        scale_one=vmem((tokens, 1), f32),
        scale_two=vmem((tokens, 1), f32),
        own_small=vmem((16 + kept.shape[0], 128), f32),
        all_small=vmem((group, 16 + kept.shape[0], 128), f32),
        gains=vmem((16, channel), f32),
        keep=vmem((lat_total * modes, 128), f32),
        own_w=vmem((parts, 2, snaps, owned, quarter), low),
        all_w=vmem((parts, 2, snaps, channel, quarter), low),
        modes=vmem((2, group, half_snaps, pair, 128), low),
        arrived=vmem((snap_local, pair * group, 128), low),
        turned=vmem((snap_local, pair * group, 128), low),
        home=vmem((2, group, half_snaps, pair, 128), low),
        gathered=vmem((2, spread, channel), f32),
        home_low=vmem((2, spread, channel), low),
        weight_one=vmem((256, 256), low),
        weight_two=vmem((256, 256), low),
        spectrum=vmem((snap_local * lat_total * modes, 256), low),
        pre_one=vmem((snap_local * lat_total * modes, 256), f32),
        act_one=vmem((snap_local * lat_total * modes, 256), low),
        pre_two=vmem((snap_local * lat_total * modes, 256), f32),
        grad_pre=vmem((snap_local * lat_total * modes, 256), f32),
        grad_two=vmem((snap_local * lat_total * modes, 256), low),
        grad_one=vmem((snap_local * lat_total * modes, 256), low),
        folds=vmem((5, 8, channel), f32),
        pair_grad=vmem((256, 256), f32),
        act=vmem((tokens, width), low),
        slope=vmem((tokens, width), low),
        bias=vmem((parts, 1, width), f32),
        grad_bias=vmem((parts, 8, width), f32),
        grad_rows=vmem((16, channel), f32),
        grads=vmem((2, 2, levels, 2, owned, width), low),
        core_got=vmem((2, 2, levels, owned, width), low),
        half_out=vmem((2, 2, 2, levels, owned, half), low),
        half_got=vmem((2, 2, levels, owned, half), low),
        quarter_out=vmem((2, 2, 2, levels, owned, quarter), low),
        quarter_got=vmem((2, 2, levels, owned, quarter), low),
        level_out=vmem((2, levels, 2, owned, quarter), low),
        level_got=vmem((2, levels, 2, owned, quarter), low),
        total=vmem((parts, snaps, 2, owned, quarter), low),
        filt_out=vmem((snaps, 4, owned, 128), low),
        tiles=vmem((group, 16, 128), f32),
        tiles_got=vmem((group, 16, 128), f32),
        snap_tiles=vmem((snaps, 16, 128), f32),
        load_sem=dma((len(inputs) + 1,)),
    )
    for name, shape in dict(
        small=(group,),
        first=(parts, group),
        second=(parts,),
        third=(parts,),
        fourth=(parts,),
        block=(2, 2, group),
        row=(2, 2, group),
        core=(2, 2),
        half=(2, 2),
        quarter=(2, 2),
        level=(2, levels),
        last=(parts, 2, snaps),
        filt=(snaps,),
        tile=(group,),
        snap_tile=(snaps,),
    ).items():
        scratch[name + "_s"] = dma(shape)
        scratch[name + "_r"] = dma(shape)
    names = [*inputs, *outputs, *scratch]
    far = pl.BlockSpec(memory_space=pl.ANY)
    near = pl.BlockSpec(memory_space=pltpu.VMEM)
    results = pl.pallas_call(
        functools.partial(block_body, names, (snaps, group, parts, width)),
        in_specs=[far] * len(inputs),
        out_specs=[far, far, far, near, near],
        out_shape=list(outputs.values()),
        scratch_shapes=list(scratch.values()),
        compiler_params=pltpu.CompilerParams(
            collective_id=0, has_side_effects=True, vmem_limit_bytes=VMEM_LIMIT
        ),
        cost_estimate=pl.CostEstimate(
            flops=12 * tokens * channel * hidden,
            bytes_accessed=4 * hidden * channel,
            transcendentals=tokens * hidden,
        ),
        name="block_pass",
    )(*inputs.values())
    return results


def step_body(names, positions, *refs):
    g = Refs()
    for name, ref in zip(names, refs, strict=True):
        setattr(g, name, ref)
    parts, snaps = g.grad_mlp.shape[:2]
    quarter = g.grad_mlp.shape[4]
    width = snaps * quarter
    moments = ("w", "m", "v")
    results = ("new", "first", "second", "copy")

    pieces = g.far_sem.shape[2]
    ends = ((g.out, g.out_near, g.out_o), (g.in_grad, g.in_grad_near, g.in_grad_o))

    def passing(kind, piece, leg):
        size = ends[kind][0].shape[0] // pieces
        rows = pl.ds(piece * size, size)
        return pltpu.make_async_copy(
            ends[kind][leg].at[rows], ends[kind][leg + 1].at[rows], g.far_sem.at[leg, kind, piece]
        )

    through = [(kind, piece) for kind in range(2) for piece in range(pieces)]

    def part_cols(part):
        return pl.ds(part * width, width)

    def load(part):
        near = [
            pltpu.make_async_copy(
                getattr(g, "mlp_" + kind).at[:, :, part_cols(part)],
                g.near.at[index, part],
                g.near_sem.at[index, part],
            )
            for index, kind in enumerate(moments)
        ]
        near.append(
            pltpu.make_async_copy(g.grad_mlp.at[part], g.grad_near.at[part], g.near_sem.at[3, part])
        )
        return near

    def store(part):
        copies = [
            pltpu.make_async_copy(
                g.near.at[index, part],
                getattr(g, "mlp_" + kind).at[:, :, part_cols(part)],
                g.back_sem.at[index, part],
            )
            for index, kind in enumerate(results[:3])
        ]
        copies.append(
            pltpu.make_async_copy(
                g.low_near.at[part], g.mlp_copy.at[:, :, part_cols(part)], g.back_sem.at[3, part]
            )
        )
        return copies

    coming = [load(part) for part in range(parts)]
    going = [store(part) for part in range(parts)]
    shares = [through[part::parts] for part in range(parts)]
    for part in range(parts):
        for copy in coming[part]:
            copy.start()
        for each in shares[part]:
            passing(*each, 0).start()

    def put(prefix, values):
        for kind, value in zip(results, values, strict=True):
            getattr(g, prefix + kind)[...] = value

    owned = g.filt_w.shape[2]
    put(
        "filt_",
        adamw(g.filt_w[...], g.filt_m[...], g.filt_v[...], g.grad_filt[:, :, 0:owned], rate_filter),
    )
    rows = g.small_w.shape[0]
    put(
        "small_",
        adamw(
            g.small_w[...], g.small_m[...], g.small_v[...], g.grad_small[0:rows, 0:owned], rate_small
        ),
    )
    totals = g.grad_small[rows : rows + 2, 0 : g.run.shape[1]]
    g.stats[...] = stat_decay * g.run[...] + (1.0 - stat_decay) * totals / positions

    for part in range(parts):
        for copy in coming[part]:
            copy.wait()

        for snap in range(snaps):
            cols = slice(snap * quarter, (snap + 1) * quarter)
            where = (slice(None), slice(None), cols)
            now = [g.near[(index, part, *where)] for index in range(3)]
            grad = g.grad_near[part, snap].astype(jnp.float32)
            values = adamw(*now, grad, rate_mlp)
            for index in range(3):
                g.near[(index, part, *where)] = values[index]
            g.low_near[(part, *where)] = values[3]
        for copy in going[part]:
            copy.start()
        for each in shares[part]:
            passing(*each, 0).wait()
            passing(*each, 1).start()
    for each in through:
        passing(*each, 1).wait()
    for part in range(parts):
        for copy in going[part]:
            copy.wait()


def step_pass(shown, grads, masters, run_stats, positions):
    grad_mlp, grad_filt, grad_small = grads
    mlp, filt, small = masters
    parts = grad_mlp.shape[0]
    width = mlp[0].shape[2] // parts
    f32, low = jnp.float32, jnp.bfloat16
    far = pl.BlockSpec(memory_space=pltpu.HBM)
    near = pl.BlockSpec(memory_space=pltpu.VMEM)
    inputs = dict(out=shown[0], in_grad=shown[1], grad_mlp=grad_mlp)
    inputs |= dict(zip(("mlp_w", "mlp_m", "mlp_v"), mlp, strict=True))
    far_in = len(inputs)
    inputs |= dict(grad_filt=grad_filt, grad_small=grad_small)
    inputs |= dict(zip(("filt_w", "filt_m", "filt_v"), filt, strict=True))
    inputs |= dict(zip(("small_w", "small_m", "small_v"), small, strict=True))
    inputs |= dict(run=run_stats)
    results = (("new", f32), ("first", f32), ("second", f32), ("copy", low))
    outputs = {
        name + "_o": jax.ShapeDtypeStruct(array.shape, array.dtype)
        for name, array in zip(("out", "in_grad"), shown, strict=True)
    }
    outputs |= {"mlp_" + kind: jax.ShapeDtypeStruct(mlp[0].shape, dt) for kind, dt in results}
    far_out = len(outputs)
    outputs |= {"filt_" + kind: jax.ShapeDtypeStruct(filt[0].shape, dt) for kind, dt in results}
    outputs |= {"small_" + kind: jax.ShapeDtypeStruct(small[0].shape, dt) for kind, dt in results}
    outputs |= dict(stats=jax.ShapeDtypeStruct(run_stats.shape, f32))
    scratch = dict(
        near=pltpu.VMEM((3, parts, 2, mlp[0].shape[1], width), f32),
        grad_near=pltpu.VMEM(grad_mlp.shape, low),
        low_near=pltpu.VMEM((parts, 2, mlp[0].shape[1], width), low),
        near_sem=pltpu.SemaphoreType.DMA((4, parts)),
        back_sem=pltpu.SemaphoreType.DMA((4, parts)),
        out_near=pltpu.VMEM(shown[0].shape, low),
        in_grad_near=pltpu.VMEM(shown[1].shape, f32),
        far_sem=pltpu.SemaphoreType.DMA((2, 2, divisor(shown[0].shape[0], 1, 4))),
    )
    return pl.pallas_call(
        functools.partial(step_body, [*inputs, *outputs, *scratch], positions),
        in_specs=[far] * far_in + [near] * (len(inputs) - far_in),
        out_specs=[far] * far_out + [near] * (len(outputs) - far_out),
        out_shape=list(outputs.values()),
        scratch_shapes=list(scratch.values()),
        compiler_params=pltpu.CompilerParams(vmem_limit_bytes=VMEM_LIMIT),
        name="step_pass",
    )(*inputs.values())


def per_device_blocks(
    fields,
    cotangent,
    valid_mask,
    kept_modes,
    mlp_master,
    mlp_first,
    mlp_second,
    filter_master,
    filter_first,
    filter_second,
    small_master,
    small_first,
    small_second,
    run_stats,
):
    snaps, group = lax.axis_size("snap"), lax.axis_size("sp")
    out, in_grad, *grads = block_pass(
        fields, cotangent, valid_mask, kept_modes, mlp_master, filter_master, small_master, snaps, group
    )
    snap_local, row_local, lon_total, channel = fields.shape
    positions = snap_local * snaps * row_local * group * lon_total
    out, in_grad, *stepped = step_pass(
        (out, in_grad),
        grads,
        (
            (mlp_master, mlp_first, mlp_second),
            (filter_master, filter_first, filter_second),
            (small_master, small_first, small_second),
        ),
        run_stats,
        positions,
    )
    rows_apart = (snap_local, lon_total, row_local, channel)
    out, in_grad = [
        jnp.transpose(array.reshape(rows_apart), (0, 2, 1, 3)) for array in (out, in_grad)
    ]
    return (out, in_grad, *stepped)


def per_device(*arrays):
    group, snaps = lax.axis_size("sp"), lax.axis_size("snap")
    channel, hidden = arrays[0].shape[3], arrays[4].shape[2]
    by_block = group == BLOCKS and snaps == 4 and arrays[3].shape[1] == 1
    if by_block and hidden % 512 == 0 and channel // group <= 128 and channel % (16 * group) == 0:
        return per_device_blocks(*arrays)
    return per_device_modes(*arrays)


def solution(mesh):
    return jax.shard_map(
        per_device,
        mesh=mesh,
        in_specs=(
            P("snap", "sp", None, None),
            P("snap", "sp", None, None),
            P("snap", "sp", None),
            P(None, "sp"),
            P(None, "sp", None),
            P(None, "sp", None),
            P(None, "sp", None),
            P(None, "sp", None),
            P(None, "sp", None),
            P(None, "sp", None),
            P(None, "sp"),
            P(None, "sp"),
            P(None, "sp"),
            P(),
        ),
        out_specs=(
            P("snap", "sp", None, None),
            P("snap", "sp", None, None),
            P(None, "sp", None),
            P(None, "sp", None),
            P(None, "sp", None),
            P(None, "sp", None),
            P(None, "sp", None),
            P(None, "sp", None),
            P(None, "sp", None),
            P(None, "sp", None),
            P(None, "sp"),
            P(None, "sp"),
            P(None, "sp"),
            P(None, "sp"),
            P(),
        ),
        check_vma=False,
    )
```

```python
import functools
import math

import jax
import jax.numpy as jnp
import ml_dtypes
import numpy as np
from jax import lax
from jax.experimental import pallas as pl
from jax.experimental.pallas import tpu as pltpu
from jax.sharding import PartitionSpec as P

BLOCKS = 8
NVAR = 20
STEP = 10
VMEM_LIMIT = 63 * 1024 * 1024


eps_norm = 1e-06
shrink_level = 0.01
beta_one = 0.5
beta_two = 0.5
adam_eps = 1e-08
decay_rate = 0.01
rate_mlp = 0.03
rate_filter = 0.1
rate_small = 0.2
stat_decay = 0.5


def layer_norm(values, gain_vec, shift_vec):
    centred = values - jnp.mean(values, axis=-1, keepdims=True)
    spread = jnp.mean(centred * centred, axis=-1, keepdims=True)
    return centred * lax.rsqrt(spread + eps_norm) * gain_vec + shift_vec


def shrink(values):
    return values - shrink_level * jnp.tanh(values / shrink_level)


def lon_tables(lon_total, mode_total):
    places = jnp.arange(lon_total, dtype=jnp.int32)
    orders = jnp.arange(mode_total, dtype=jnp.int32)
    angles = (places[:, None] * orders[None, :] % lon_total).astype(jnp.float32) * (
        2.0 * math.pi / lon_total
    )
    scaling = 1.0 / math.sqrt(lon_total)
    forward_tab = jnp.stack([jnp.cos(angles), -jnp.sin(angles)], axis=1) * scaling
    doubling = jnp.where(orders == 0, 1.0, 2.0).astype(jnp.float32)[:, None]
    inverse_tab = (
        jnp.stack([jnp.cos(angles).T * doubling, -jnp.sin(angles).T * doubling], axis=0) * scaling
    )
    return (forward_tab.astype(jnp.bfloat16), inverse_tab.astype(jnp.bfloat16))


def lat_table(lat_total):
    places = jnp.arange(lat_total, dtype=jnp.int32)
    angles = (places[:, None] * places[None, :] % lat_total).astype(jnp.float32) * (
        2.0 * math.pi / lat_total
    )
    cosine = jnp.cos(angles)
    sine_part = jnp.sin(angles)
    upper_rows = jnp.stack([cosine, sine_part], axis=1)
    bottom = jnp.stack([-sine_part, cosine], axis=1)
    return (jnp.stack([upper_rows, bottom], axis=0) / math.sqrt(lat_total)).astype(jnp.bfloat16)


def complex_pair(real_part, imag_part):
    return jnp.stack([jnp.stack([real_part, -imag_part]), jnp.stack([imag_part, real_part])])


gelu_scale = math.sqrt(2.0 / math.pi)
gelu_cubic = 0.044715


def gelu_both(value):
    bend = (gelu_scale * gelu_cubic) * (value * value)
    turn = jnp.tanh(value * (gelu_scale + bend))
    half = 0.5 + 0.5 * turn
    slope = half * (1.0 + (value * (1.0 - turn)) * (gelu_scale + 3.0 * bend))
    return value * half, slope


def dot_nt(left, right):
    return lax.dot_general(
        left, right, (((1,), (1,)), ((), ())), preferred_element_type=jnp.float32
    )


def dot_nn(left, right):
    return jnp.dot(left, right, preferred_element_type=jnp.float32)


def divisor(total, unit, most):
    return max(size for size in range(unit, most + 1, unit) if total % size == 0)


def mlp_body(
    tile,
    normed_ref,
    cot_ref,
    up_ref,
    down_ref,
    bias_ref,
    out_ref,
    back_ref,
    grad_up_ref,
    grad_down_ref,
    grad_bias_ref,
    normed_turned,
    cot_turned,
    act_ref,
    slope_ref,
):
    tokens = normed_ref.shape[0]

    @pl.when(pl.program_id(0) == 0)
    def _():
        normed_turned[...] = normed_ref[...].T
        cot_turned[...] = cot_ref[...].T
        out_ref[...] = jnp.zeros_like(out_ref)
        back_ref[...] = jnp.zeros_like(back_ref)

    grad_bias_ref[...] = jnp.zeros_like(grad_bias_ref)

    @pl.loop(0, tokens // tile)
    def _(step):
        rows = pl.ds(pl.multiple_of(step * tile, tile), tile)
        act, slope = gelu_both(dot_nn(normed_ref[rows, :], up_ref[...]) + bias_ref[...])
        act = act.astype(jnp.bfloat16)
        slope = (dot_nn(cot_ref[rows, :], down_ref[...]) * slope).astype(jnp.bfloat16)
        act_ref[rows, :] = act
        slope_ref[rows, :] = slope
        grad_bias_ref[...] += jnp.sum(slope.astype(jnp.float32), axis=0, keepdims=True)
        out_ref[rows, :] += dot_nt(act, down_ref[...])
        back_ref[rows, :] += dot_nt(slope, up_ref[...])

    grad_up_ref[...] = dot_nn(normed_turned[...], slope_ref[...]).astype(grad_up_ref.dtype)
    grad_down_ref[...] = dot_nn(cot_turned[...], act_ref[...]).astype(grad_down_ref.dtype)


def mlp_pass(normed, cot, weights, bias):
    tokens, channel = normed.shape
    hidden = weights.shape[2]
    width = divisor(hidden, 128, 512)
    tile = divisor(tokens, 16, 480)
    whole = pl.BlockSpec((tokens, channel), lambda j: (0, 0))
    block = pl.BlockSpec((channel, width), lambda j: (0, j))
    line = pl.BlockSpec((1, width), lambda j: (0, j))
    part = lambda which: pl.BlockSpec((None, channel, width), lambda j: (which, 0, j))
    total = jax.ShapeDtypeStruct((tokens, channel), jnp.float32)
    grads = jax.ShapeDtypeStruct((channel, hidden), jnp.bfloat16)
    return pl.pallas_call(
        functools.partial(mlp_body, tile),
        grid=(hidden // width,),
        in_specs=[whole, whole, part(0), part(1), line],
        out_specs=[whole, whole, block, block, line],
        out_shape=[total, total, grads, grads, jax.ShapeDtypeStruct((1, hidden), jnp.float32)],
        scratch_shapes=[
            pltpu.VMEM((channel, tokens), jnp.bfloat16),
            pltpu.VMEM((channel, tokens), jnp.bfloat16),
            pltpu.VMEM((tokens, width), jnp.bfloat16),
            pltpu.VMEM((tokens, width), jnp.bfloat16),
        ],
        compiler_params=pltpu.CompilerParams(vmem_limit_bytes=56 * 1024 * 1024),
        cost_estimate=pl.CostEstimate(
            flops=12 * tokens * channel * hidden,
            bytes_accessed=8 * channel * hidden + 12 * tokens * channel,
            transcendentals=tokens * hidden,
        ),
        name="mlp_pass",
    )(normed, cot, weights, weights, bias)


def spectral_front(arrived, lat_fwd, first_pair, second_pair, bias_one, bias_two):
    spectrum = jnp.einsum(
        "pkqr,nrqmd->nkpmd", lat_fwd, arrived, preferred_element_type=jnp.float32
    ).astype(jnp.bfloat16)
    snap_local, lat_total, pair_count, mode_local, channel = spectrum.shape
    blocked = spectrum.reshape(
        snap_local, lat_total, pair_count, mode_local, BLOCKS, channel // BLOCKS
    )
    pre_one = (
        jnp.einsum("nkqmbi,pqbio->nkpmbo", blocked, first_pair, preferred_element_type=jnp.float32)
        + bias_one
    )
    act_one = jax.nn.gelu(pre_one).astype(jnp.bfloat16)
    pre_two = (
        jnp.einsum("nkqmbi,pqbio->nkpmbo", act_one, second_pair, preferred_element_type=jnp.float32)
        + bias_two
    )
    return (blocked, pre_one, act_one, pre_two)


def adamw(master, first_mom, second_mom, gradient, step_rate):
    first_next = beta_one * first_mom + (1.0 - beta_one) * gradient
    second_next = beta_two * second_mom + (1.0 - beta_two) * gradient * gradient
    fix_one = 1.0 - beta_one**STEP
    fix_two = 1.0 - beta_two**STEP
    direction = first_next / fix_one / (jnp.sqrt(second_next / fix_two) + adam_eps)
    master_next = master - step_rate * (direction + decay_rate * master)
    return (master_next, first_next, second_next, master_next.astype(jnp.bfloat16))


def per_device_modes(
    fields,
    cotangent,
    valid_mask,
    kept_modes,
    mlp_master,
    mlp_first,
    mlp_second,
    filter_master,
    filter_first,
    filter_second,
    small_master,
    small_first,
    small_second,
    run_stats,
):
    group_size = lax.axis_size("sp")
    snap_local, row_local, lon_total, channel = fields.shape
    lat_total = row_local * group_size
    mode_local = kept_modes.shape[1]
    mode_total = mode_local * group_size
    block_width = channel // BLOCKS
    lon_fwd, lon_inv = lon_tables(lon_total, mode_total)
    lat_fwd = lat_table(lat_total)
    mlp_w, filt_w, small_w = (
        lax.all_gather(mlp_master.astype(jnp.bfloat16), "sp", axis=1, tiled=True),
        lax.all_gather(filter_master.astype(jnp.bfloat16), "sp", axis=1, tiled=True),
        lax.all_gather(small_master.astype(jnp.bfloat16), "sp", axis=1, tiled=True),
    )
    small_f = small_w.astype(jnp.float32)
    weights = filt_w.reshape(4, BLOCKS, block_width, block_width)
    first_pair = complex_pair(weights[0], weights[1])
    second_pair = complex_pair(weights[2], weights[3])
    bias_one = small_f[4:6].reshape(2, 1, BLOCKS, block_width)
    bias_two = small_f[6:8].reshape(2, 1, BLOCKS, block_width)
    fields_float = fields.astype(jnp.float32)
    normed, norm_pull = jax.vjp(layer_norm, fields_float, small_f[0], small_f[1])
    normed_low = normed.astype(jnp.bfloat16)
    spec_lon = jnp.einsum(
        "nrld,lqm->nrqmd", normed_low, lon_fwd, preferred_element_type=jnp.float32
    ).astype(jnp.bfloat16)
    arrived = lax.all_to_all(spec_lon, "sp", split_axis=3, concat_axis=1, tiled=True)
    spectral = spectral_front(arrived, lat_fwd, first_pair, second_pair, bias_one, bias_two)
    keep_mask = kept_modes.astype(jnp.float32)[None, :, None, :, None, None]
    masked = (shrink(spectral[3]) * keep_mask).astype(jnp.bfloat16)
    masked = masked.reshape(snap_local, lat_total, 2, mode_local, channel)
    returned = jnp.einsum(
        "pkqr,nkpmd->nrqmd", lat_fwd, masked, preferred_element_type=jnp.float32
    ).astype(jnp.bfloat16)
    home_modes = lax.all_to_all(returned, "sp", split_axis=1, concat_axis=3, tiled=True)
    filtered = jnp.einsum(
        "nrqmd,qml->nrld", home_modes, lon_inv, preferred_element_type=jnp.float32
    )
    mixture = fields_float + normed + filtered
    normed_two, norm_two_pull = jax.vjp(layer_norm, mixture, small_f[2], small_f[3])
    normed_two_low = normed_two.astype(jnp.bfloat16)
    tokens = snap_local * row_local * lon_total
    passed = mlp_pass(
        normed_two_low.reshape(tokens, channel),
        cotangent.reshape(tokens, channel),
        mlp_w,
        small_f[9:].reshape(1, -1),
    )
    output = mixture + passed[0].reshape(mixture.shape) + small_f[8]
    weight_mask = valid_mask.astype(jnp.float32)[..., None]
    variables = output[..., :NVAR]
    local_sums = jnp.stack(
        [
            jnp.sum(weight_mask * variables, axis=(0, 1, 2)),
            jnp.sum(weight_mask * variables * variables, axis=(0, 1, 2)),
        ]
    )
    total_sums = lax.psum(local_sums, ("snap", "sp"))
    positions = snap_local * lax.axis_size("snap") * lat_total * lon_total
    stats_new = stat_decay * run_stats + (1.0 - stat_decay) * total_sums / positions
    cot_float = cotangent.astype(jnp.float32)
    grad_normed_two = passed[1].reshape(mixture.shape)
    grad_bias_hidden = passed[4]
    grad_mix_norm, grad_gain_two, grad_shift_two = norm_two_pull(grad_normed_two)
    grad_mixture = cot_float + grad_mix_norm
    grad_bias_out = jnp.sum(cot_float, axis=(0, 1, 2))
    grad_filtered = grad_mixture.astype(jnp.bfloat16)
    grad_home = jnp.einsum(
        "nrld,qml->nrqmd", grad_filtered, lon_inv, preferred_element_type=jnp.float32
    ).astype(jnp.bfloat16)
    grad_returned = lax.all_to_all(grad_home, "sp", split_axis=3, concat_axis=1, tiled=True)
    grad_masked = jnp.einsum(
        "pkqr,nrqmd->nkpmd", lat_fwd, grad_returned, preferred_element_type=jnp.float32
    )
    arrived_again = lax.all_to_all(spec_lon, "sp", split_axis=3, concat_axis=1, tiled=True)
    used_front = spectral_front(arrived_again, lat_fwd, first_pair, second_pair, bias_one, bias_two)
    blocked, pre_one, act_one, pre_two = used_front
    grad_two = jax.vjp(shrink, pre_two)[1](grad_masked.reshape(pre_two.shape) * keep_mask)[
        0
    ].astype(jnp.bfloat16)
    grad_bias_two = jnp.sum(grad_two.astype(jnp.float32), axis=(0, 1, 3))
    grad_second = jnp.einsum(
        "nkqmbi,nkpmbo->pqbio", act_one, grad_two, preferred_element_type=jnp.float32
    )
    grad_act = jnp.einsum(
        "nkpmbo,pqbio->nkqmbi", grad_two, second_pair, preferred_element_type=jnp.float32
    )
    grad_one = jax.vjp(jax.nn.gelu, pre_one)[1](grad_act)[0].astype(jnp.bfloat16)
    grad_bias_one = jnp.sum(grad_one.astype(jnp.float32), axis=(0, 1, 3))
    grad_first = jnp.einsum(
        "nkqmbi,nkpmbo->pqbio", blocked, grad_one, preferred_element_type=jnp.float32
    )
    grad_spectrum = jnp.einsum(
        "nkpmbo,pqbio->nkqmbi", grad_one, first_pair, preferred_element_type=jnp.float32
    ).astype(jnp.bfloat16)
    grad_spectrum = grad_spectrum.reshape(snap_local, lat_total, 2, mode_local, channel)
    grad_lon = jnp.einsum(
        "pkqr,nkpmd->nrqmd", lat_fwd, grad_spectrum, preferred_element_type=jnp.float32
    ).astype(jnp.bfloat16)
    grad_rows = lax.all_to_all(grad_lon, "sp", split_axis=1, concat_axis=3, tiled=True)
    grad_normed = grad_mixture + jnp.einsum(
        "nrqmd,lqm->nrld", grad_rows, lon_fwd, preferred_element_type=jnp.float32
    )
    grad_field_norm, grad_gain_one, grad_shift_one = norm_pull(grad_normed)
    input_grad = grad_mixture + grad_field_norm
    grad_filter = jnp.stack(
        [
            grad_first[0, 0] + grad_first[1, 1],
            grad_first[1, 0] - grad_first[0, 1],
            grad_second[0, 0] + grad_second[1, 1],
            grad_second[1, 0] - grad_second[0, 1],
        ]
    ).reshape(4, channel, block_width)
    grad_small = jnp.concatenate(
        [
            jnp.stack([grad_gain_one, grad_shift_one, grad_gain_two, grad_shift_two]),
            grad_bias_one.reshape(2, channel),
            grad_bias_two.reshape(2, channel),
            grad_bias_out[None, :],
            grad_bias_hidden.reshape(-1, channel),
        ],
        axis=0,
    )
    shares = (
        jnp.stack([
            lax.psum_scatter(part, "sp", scatter_dimension=0, tiled=True) for part in passed[2:4]
        ]),
        lax.psum_scatter(grad_filter, "sp", scatter_dimension=1, tiled=True),
        lax.psum_scatter(grad_small, "sp", scatter_dimension=1, tiled=True),
    )
    owned = (
        lax.psum(shares[0].astype(jnp.bfloat16), "snap").astype(jnp.float32),
        lax.psum(shares[1].astype(jnp.bfloat16), "snap").astype(jnp.float32),
        lax.psum(shares[2].astype(jnp.bfloat16), "snap").astype(jnp.float32),
    )
    mlp_new, mlp_first_new, mlp_second_new, mlp_copy = adamw(
        mlp_master, mlp_first, mlp_second, owned[0], rate_mlp
    )
    filter_new, filter_first_new, filter_second_new, filter_copy = adamw(
        filter_master, filter_first, filter_second, owned[1], rate_filter
    )
    small_new, small_first_new, small_second_new, small_copy = adamw(
        small_master, small_first, small_second, owned[2], rate_small
    )
    return (
        output.astype(jnp.bfloat16),
        input_grad,
        mlp_new,
        mlp_first_new,
        mlp_second_new,
        mlp_copy,
        filter_new,
        filter_first_new,
        filter_second_new,
        filter_copy,
        small_new,
        small_first_new,
        small_second_new,
        small_copy,
        stats_new,
    )


def lon_matrix(lon_total, mode_total, snaps, rows):
    places = np.arange(lon_total)
    orders = np.arange(mode_total)
    angles = (places[:, None] * orders[None, :] % lon_total) * (2.0 * math.pi / lon_total)
    doubling = np.where(orders == 0, 1.0, 2.0)
    scaling = 1.0 / math.sqrt(lon_total)
    forward = np.stack([np.cos(angles), -np.sin(angles)], axis=1) * scaling
    inverse = forward * doubling

    def spread(table):
        table = np.einsum(
            "ab,lx,rs->alrbsx", np.eye(snaps), table.reshape(lon_total, -1), np.eye(rows)
        )
        return table.reshape(snaps * lon_total * rows, -1).astype(ml_dtypes.bfloat16)

    return spread(forward), spread(inverse)


def lon_turn(lon_total, rows):
    turn = np.einsum("lk,rs->rlks", np.eye(lon_total), np.eye(rows))
    return turn.reshape(rows, lon_total, lon_total * rows).astype(ml_dtypes.bfloat16)


def lat_matrix(lat_total, mode_total):
    places = np.arange(lat_total)
    angles = (places[:, None] * places[None, :] % lat_total) * (2.0 * math.pi / lat_total)
    cosine, sine = np.cos(angles), np.sin(angles)
    table = np.stack([np.stack([cosine, sine], axis=1), np.stack([-sine, cosine], axis=1)])
    table = np.einsum("pkqr,ab->pakrqb", table / math.sqrt(lat_total), np.eye(mode_total))
    size = 2 * lat_total * mode_total
    return table.reshape(size, size).astype(ml_dtypes.bfloat16)


class Refs:
    pass


def block_body(names, sizes, *refs):
    g = Refs()
    for name, ref in zip(names, refs, strict=True):
        setattr(g, name, ref)
    snaps, group, parts, width = sizes
    levels = group // 2
    tokens = g.fields.shape[0] * g.fields.shape[1]
    channel = g.fields.shape[2]
    tiles = channel // 128
    owned = channel // group
    half = width // 2
    quarter = width // snaps
    tile = divisor(tokens // 2, 16, 240)
    strip = divisor(tokens // 2, 48, 144)
    sub = divisor(strip, 16, 48)
    low = jnp.bfloat16
    f32 = jnp.float32

    me_snap = lax.axis_index("snap")
    me_sp = lax.axis_index("sp")
    core = lax.rem(me_sp, 2)
    level = me_sp // 2

    def at(snap, sp):
        return {"snap": snap, "sp": sp}

    def sp_after(step):
        return lax.rem(me_sp + step, group)

    def sp_before(step):
        return lax.rem(me_sp + group - step, group)

    def snap_after(step):
        return lax.rem(me_snap + step, snaps)

    def snap_before(step):
        return lax.rem(me_snap + snaps - step, snaps)

    def level_after(step):
        return lax.rem(level + step, levels)

    def level_before(step):
        return lax.rem(level + levels - step, levels)

    other_core = at(me_snap, me_sp + 1 - 2 * core)

    def send(src, dst, sems, index, target):
        return pltpu.make_async_remote_copy(
            src_ref=src,
            dst_ref=dst,
            send_sem=sems[0].at[index],
            recv_sem=sems[1].at[index],
            device_id=target,
            device_id_type=pl.DeviceIdType.MESH,
        )

    half_tokens = tokens // 2

    def strips(body, first=0, count=tokens):
        @pl.loop(0, count // strip)
        def _(step):
            for at_row in range(0, strip, sub):
                body(pl.ds(pl.multiple_of(first + step * strip + at_row, 16), sub))

    def half_strips(body, part):
        strips(body, part * half_tokens, half_tokens)

    def half_rows(part):
        return slice(part * half_tokens, (part + 1) * half_tokens)

    def fold(value):
        return jnp.sum(value.reshape(-1, 8, value.shape[1]), axis=0)

    def columns(name):
        ref = getattr(g, name)
        return ref.reshape(tiles, ref.shape[1] * ref.shape[2], 128)

    def columns_of(name, rows):
        view = columns(name)
        return jnp.concatenate([view[tile_at, rows, :] for tile_at in range(tiles)], axis=1)

    def store_columns(name, rows, value):
        view = columns(name)
        for tile_at in range(tiles):
            view[tile_at, rows, :] = value[:, tile_at * 128 : (tile_at + 1) * 128]

    def column_copies(near, far, sems, out):
        copies = []
        for tile_at in range(tiles):
            ends = [near.at[tile_at], far.at[:, :, tile_at * 128 : (tile_at + 1) * 128]]
            if not out:
                ends.reverse()
            copies.append(pltpu.make_async_copy(*ends, sems.at[tile_at]))
        return copies

    loads = {}

    def load(name, index):
        copy = pltpu.make_async_copy(getattr(g, name), getattr(g, name + "_in"), g.load_sem.at[index])
        copy.start()
        loads[name] = copy

    for index, name in enumerate(
        [name for name in names[: names.index("out")] if name not in ("mlp", "fields", "cot")]
    ):
        load(name, index)
    fields_load = column_copies(g.fields_cols, g.fields, g.fields_sem, False)
    cot_load = column_copies(g.cot_cols, g.cot, g.cot_sem, False)
    for copy in fields_load + cot_load:
        copy.start()

    def master_load(part):
        return pltpu.make_async_copy(
            g.mlp.at[:, :, part * width : (part + 1) * width],
            g.mlp_part.at[part % 2],
            g.load_sem.at[len(loads) + part % 2],
        )

    master_load(0).start()
    master_load(1).start()

    barrier = pltpu.get_barrier_semaphore()
    peers = [at(me_snap, sp_after(step)) for step in range(1, group)]
    peers += [at(snap_after(step), me_sp) for step in range(1, snaps)]
    for peer in peers:
        pl.semaphore_signal(
            barrier, inc=1, device_id=peer, device_id_type=pl.DeviceIdType.MESH
        )

    loads["small"].wait()
    loads["kept"].wait()
    g.own_small[...] = jnp.zeros_like(g.own_small)
    rows_small = g.small.shape[0]
    g.own_small[0:rows_small, 0:owned] = g.small_in[...].astype(low).astype(f32)
    pairs_kept = g.kept.shape[1]
    lines = lax.broadcasted_iota(jnp.int32, (pairs_kept, pairs_kept), 0)
    places = lax.broadcasted_iota(jnp.int32, (pairs_kept, pairs_kept), 1)
    kept = jnp.where(lines == places, g.kept_in[...].astype(f32), 0.0)
    g.own_small[16:, :] = jnp.broadcast_to(
        jnp.sum(kept, axis=1, keepdims=True), (pairs_kept, g.own_small.shape[1])
    )
    pl.semaphore_wait(barrier, len(peers))

    def small_copy(step):
        return send(
            g.own_small, g.all_small.at[me_sp], (g.small_s, g.small_r), step, at(me_snap, sp_after(step))
        )

    for step in range(1, group):
        small_copy(step).start()
    g.all_small[me_sp] = g.own_small[...]

    snap_low = lax.rem(me_snap, 2)
    snap_high = me_snap // 2
    beside_low = me_snap + 1 - 2 * snap_low
    beside_high = me_snap + 2 - 4 * snap_high

    def own_quarter(part):
        odd = lax.rem(part, 2)
        return (1 - odd) * me_snap + odd * (2 * snap_low + snap_high)

    def half_quarters(part):
        return pl.ds(2 * (own_quarter(part) // 2), 2)

    def own_rows(sp):
        return pl.ds(pl.multiple_of(sp * owned, owned), owned)

    def first_copy(part, step):
        target = sp_after(step)
        matrix = lax.rem(target, 2)
        place = own_quarter(part)
        return send(
            g.own_w.at[part, matrix, place],
            g.all_w.at[part, matrix, place, own_rows(me_sp)],
            (g.first_s, g.first_r),
            (part, step),
            at(me_snap, target),
        )

    def first_local(part):
        place = own_quarter(part)
        return pltpu.make_async_copy(
            g.own_w.at[part, core, place],
            g.all_w.at[part, core, place, own_rows(me_sp)],
            g.first_s.at[part, 0],
        )

    def second_copy(part):
        odd = lax.rem(part, 2)
        view = g.all_w.at[part, core, own_quarter(part)]
        target = at((1 - odd) * beside_low + odd * beside_high, me_sp)
        return send(view, view, (g.second_s, g.second_r), part, target)

    def third_copy(part):
        odd = lax.rem(part, 2)
        view = g.all_w.at[part, core, half_quarters(part)]
        target = at((1 - odd) * beside_high + odd * beside_low, me_sp)
        return send(view, view, (g.third_s, g.third_r), part, target)

    def fourth_copy(part):
        view = g.all_w.at[part, core]
        return send(view, view, (g.fourth_s, g.fourth_r), part, other_core)

    def start_first(part):
        for step in range(1, group):
            first_copy(part, step).start()
        first_local(part).start()

    def pass_second(part):
        for step in range(1, group):
            first_copy(part, step).wait_recv()
        first_local(part).wait()
        second_copy(part).start()

    def pass_third(part):
        second_copy(part).wait_recv()
        third_copy(part).start()

    def pass_fourth(part):
        third_copy(part).wait_recv()
        fourth_copy(part).start()

    for part in range(parts):
        master_load(part).wait()
        for place in range(snaps):
            cols = slice(place * quarter, (place + 1) * quarter)
            g.own_w[part, :, place] = g.mlp_part[part % 2, :, :, cols].astype(low)
        if part + 2 < parts:
            master_load(part + 2).start()
        if part < 2:
            start_first(part)

    for copy in fields_load:
        copy.wait()

    def first_unit(rows):
        values = columns_of("fields_cols", rows).astype(f32)
        centred = values - jnp.mean(values, axis=-1, keepdims=True)
        scale = lax.rsqrt(jnp.mean(centred * centred, axis=-1, keepdims=True) + eps_norm)
        g.scale_one[rows, :] = scale
        g.grid[rows, :] = centred * scale

    strips(first_unit)
    for step in range(1, group):
        small_copy(step).wait_recv()
    for sp in range(group):
        g.gains[:, sp * owned : (sp + 1) * owned] = g.all_small[sp, 0:16, 0:owned]
        g.keep[sp * pairs_kept : (sp + 1) * pairs_kept, :] = g.all_small[sp, 16:, :]

    def first_norm(rows):
        unit = g.grid[rows, :]
        normed = unit * g.gains[0:1, :] + g.gains[1:2, :]
        g.unit_one[rows, :] = unit.astype(low)
        g.normed[rows, :] = normed.astype(low)
        g.grid[rows, :] = columns_of("fields_cols", rows).astype(f32) + normed

    half_snaps = g.arrived.shape[0] // 2

    def some_snaps(part):
        return pl.ds(part * half_snaps, half_snaps)

    def to_blocks(table, which, part):
        modes = dot_nn(table, g.normed[half_rows(part), :])
        for block in range(group):
            cut = modes[:, block * owned : (block + 1) * owned]
            cut = jnp.concatenate([cut, jnp.zeros((cut.shape[0], 128 - owned), f32)], axis=1)
            g.modes[part, block] = cut.astype(low).reshape(g.modes.shape[2:])
        for step in range(1, group):
            block_copy(which, part, step).start()
        g.arrived[some_snaps(part), mode_rows(me_sp), :] = g.modes[part, me_sp]

    def mode_rows(sp):
        size = g.modes.shape[3]
        return pl.ds(pl.multiple_of(sp * size, size), size)

    def block_copy(which, part, step):
        target = sp_after(step)
        return send(
            g.modes.at[part, target],
            g.arrived.at[some_snaps(part), mode_rows(me_sp), :],
            (g.block_s, g.block_r),
            (which, part, step),
            at(me_snap, target),
        )

    def row_copy(which, part, step):
        target = sp_after(step)
        return send(
            g.turned.at[some_snaps(part), mode_rows(target), :],
            g.home.at[part, me_sp],
            (g.row_s, g.row_r),
            (which, part, step),
            at(me_snap, target),
        )

    def to_rows(which, part):
        for step in range(1, group):
            row_copy(which, part, step).start()
        g.home[part, me_sp] = g.turned[some_snaps(part), mode_rows(me_sp), :]

    def home_modes(which, part):
        for step in range(1, group):
            row_copy(which, part, step).wait_recv()
        count = g.gathered.shape[1]
        for block in range(group):
            g.gathered[part, :, block * owned : (block + 1) * owned] = (
                g.home[part, block].reshape(count, 128)[:, 0:owned].astype(f32)
            )
        g.home_low[part] = g.gathered[part].astype(low)

    loads["lon_f"].wait()
    for part in range(2):
        half_strips(first_norm, part)
        to_blocks(g.lon_f_in[...], 0, part)
        pass_second(part)

    loads["filt"].wait()
    for weight, first in ((g.weight_one, 0), (g.weight_two, 2)):
        weight[...] = jnp.zeros_like(weight)
        real = g.filt_in[first].astype(low)
        imag = g.filt_in[first + 1].astype(low)
        weight[0:owned, 0:owned] = real
        weight[128 : 128 + owned, 128 : 128 + owned] = real
        weight[0:owned, 128 : 128 + owned] = imag
        weight[128 : 128 + owned, 0:owned] = -imag

    def bias_row(first):
        return jnp.concatenate(
            [g.own_small[first : first + 1, :], g.own_small[first + 1 : first + 2, :]], axis=1
        )

    for copy in cot_load:
        copy.wait()

    def flat_cot(rows):
        g.cot_in[rows, :] = columns_of("cot_cols", rows)

    strips(flat_cot)
    pass_third(0)
    loads["lat_f"].wait()
    loads["lat_b"].wait()
    pairs = g.arrived.shape[1] // 2
    half_modes = half_snaps * pairs

    def mode_half(part):
        return slice(part * half_modes, (part + 1) * half_modes)

    def spectra(out, kind, part):
        for snap in range(part * half_snaps, (part + 1) * half_snaps):
            spectrum = dot_nn(g.lat_f_in[...], g.arrived[snap]).astype(kind)
            rows = slice(snap * pairs, (snap + 1) * pairs)
            out[rows, 0:128] = spectrum[0:pairs]
            out[rows, 128:256] = spectrum[pairs:]

    def grids(values, part):
        for index in range(half_snaps):
            rows = values[index * pairs : (index + 1) * pairs]
            rows = jnp.concatenate([rows[:, 0:128], rows[:, 128:256]], axis=0)
            g.turned[part * half_snaps + index] = dot_nn(g.lat_b_in[...], rows).astype(low)

    def keep_half():
        keep = jnp.concatenate([g.keep[...], g.keep[...]], axis=1)
        return jnp.concatenate([keep] * half_snaps, axis=0)

    for part in range(2):
        for step in range(1, group):
            block_copy(0, part, step).wait_recv()
        rows = mode_half(part)
        spectra(g.spectrum, low, part)
        g.pre_one[rows, :] = dot_nn(g.spectrum[rows, :], g.weight_one[...]) + bias_row(4)
        g.act_one[rows, :] = gelu_both(g.pre_one[rows, :])[0].astype(low)
        g.pre_two[rows, :] = dot_nn(g.act_one[rows, :], g.weight_two[...]) + bias_row(6)
        grids((shrink(g.pre_two[rows, :]) * keep_half()).astype(low), part)
        to_rows(0, part)
        if part == 0:
            pass_third(1)
    for part in range(2, 4):
        start_first(part)
    g.cot_turned[...] = g.cot_in[...].T

    loads["lon_i"].wait()

    def second_norm(rows):
        values = g.grid[rows, :]
        centred = values - jnp.mean(values, axis=-1, keepdims=True)
        scale = lax.rsqrt(jnp.mean(centred * centred, axis=-1, keepdims=True) + eps_norm)
        centred = centred * scale
        g.unit_two[rows, :] = centred.astype(low)
        g.scale_two[rows, :] = scale
        g.normed[rows, :] = (centred * g.gains[2:3, :] + g.gains[3:4, :]).astype(low)
        g.grid[rows, :] = values + g.gains[8:9, :]
        g.back[rows, :] = jnp.zeros((sub, channel), f32)

    for part in range(2):
        home_modes(0, part)
        g.grid[half_rows(part), :] += dot_nn(g.lon_i_in[...], g.home_low[part])
        half_strips(second_norm, part)
        pass_fourth(part)
        pass_second(2 + part)
    g.normed_turned[...] = g.normed[...].T
    for part in range(2, 4):
        pass_third(part)
    for part in range(4, parts):
        start_first(part)
    flat = jnp.concatenate([g.gains[9 + row : 10 + row, :] for row in range(rows_small - 9)], axis=1)
    for part in range(parts):
        g.bias[part] = flat[:, part * width : (part + 1) * width]

    def core_copy(part, matrix):
        slot = lax.rem(part, 2)
        return send(
            g.grads.at[matrix, :, 1 - core],
            g.core_got.at[slot, matrix],
            (g.core_s, g.core_r),
            (slot, matrix),
            other_core,
        )

    places_one = (snap_low, snap_high)
    places_two = (snap_high, snap_low)
    beside_one = (beside_low, beside_high)
    beside_two = (beside_high, beside_low)
    place_last = (2 * snap_low + snap_high, me_snap)

    def half_copy(part, matrix):
        slot = lax.rem(part, 2)
        return send(
            g.half_out.at[slot, matrix, 1 - places_one[matrix]],
            g.half_got.at[slot, matrix],
            (g.half_s, g.half_r),
            (slot, matrix),
            at(beside_one[matrix], me_sp),
        )

    def quarter_copy(part, matrix):
        slot = lax.rem(part, 2)
        return send(
            g.quarter_out.at[slot, matrix, 1 - places_two[matrix]],
            g.quarter_got.at[slot, matrix],
            (g.quarter_s, g.quarter_r),
            (slot, matrix),
            at(beside_two[matrix], me_sp),
        )

    def level_copy(part, step):
        slot = lax.rem(part, 2)
        target = level_after(step)
        return send(
            g.level_out.at[slot, target],
            g.level_got.at[slot, level],
            (g.level_s, g.level_r),
            (slot, step),
            at(me_snap, 2 * target + core),
        )

    def last_copy(part, matrix, step):
        view = g.total.at[part, place_last[matrix], matrix]
        return send(
            view, view, (g.last_s, g.last_r), (part, matrix, step), at(snap_after(step), me_sp)
        )

    def half_stage(part):
        slot = lax.rem(part, 2)
        for matrix in range(2):

            @pl.when(part >= 2)
            def _(matrix=matrix):
                half_copy(part - 2, matrix).wait_send()

            core_copy(part, matrix).wait_recv()
            for row in range(levels):
                both = g.grads[matrix, row, core].astype(f32) + g.core_got[
                    slot, matrix, row
                ].astype(f32)
                both = both.astype(low)
                g.half_out[slot, matrix, 0, row] = both[:, 0:half]
                g.half_out[slot, matrix, 1, row] = both[:, half:width]
            half_copy(part, matrix).start()

    def quarter_stage(part):
        slot = lax.rem(part, 2)
        for matrix in range(2):

            @pl.when(part >= 2)
            def _(matrix=matrix):
                quarter_copy(part - 2, matrix).wait_send()

            half_copy(part, matrix).wait_recv()
            for row in range(levels):
                both = g.half_out[slot, matrix, places_one[matrix], row].astype(f32) + g.half_got[
                    slot, matrix, row
                ].astype(f32)
                both = both.astype(low)
                g.quarter_out[slot, matrix, 0, row] = both[:, 0:quarter]
                g.quarter_out[slot, matrix, 1, row] = both[:, quarter:half]
            quarter_copy(part, matrix).start()

    def level_stage(part):
        slot = lax.rem(part, 2)

        @pl.when(part >= 2)
        def _():
            for step in range(1, levels):
                level_copy(part - 2, step).wait_send()

        for matrix in range(2):
            quarter_copy(part, matrix).wait_recv()
            for row in range(levels):
                both = g.quarter_out[slot, matrix, places_two[matrix], row].astype(
                    f32
                ) + g.quarter_got[slot, matrix, row].astype(f32)
                g.level_out[slot, row, matrix] = both.astype(low)
        for step in range(1, levels):
            level_copy(part, step).start()

    def last_stage(part):
        slot = lax.rem(part, 2)
        for step in range(1, levels):
            level_copy(part, step).wait_recv()
        for matrix in range(2):
            sums = g.level_out[slot, level, matrix].astype(f32)
            for step in range(1, levels):
                sums += g.level_got[slot, level_before(step), matrix].astype(f32)
            g.total[part, place_last[matrix], matrix] = sums.astype(low)
            for step in range(1, snaps):
                last_copy(part, matrix, step).start()

    def weight(part, matrix):
        return jnp.concatenate([g.all_w[part, matrix, place] for place in range(snaps)], axis=1)

    @pl.loop(0, parts)
    def _(part):
        slot = lax.rem(part, 2)
        fourth_copy(part).wait_recv()

        @pl.when((part >= 1) & (part + 1 < parts))
        def _():
            pass_fourth(part + 1)

        g.grad_bias[part] = jnp.zeros(g.grad_bias.shape[1:], f32)

        def tile_rows(place):
            return pl.ds(pl.multiple_of(place * tile, tile), tile)

        def enter(place, pre, grad):
            rows = tile_rows(place)
            pre[...] = dot_nn(g.normed[rows, :], weight(part, 0)) + g.bias[part]
            grad[...] = dot_nn(g.cot_in[rows, :], weight(part, 1))

        def leave(place, pre, grad):
            rows = tile_rows(place)
            act, slope = gelu_both(pre[...])
            act = act.astype(low)
            slope = (grad[...] * slope).astype(low)
            g.act[rows, :] = act
            g.slope[rows, :] = slope
            g.grad_bias[part] += fold(slope.astype(f32))
            g.grid[rows, :] += dot_nt(act, weight(part, 1))
            g.back[rows, :] += dot_nt(slope, weight(part, 0))

        count = tokens // tile
        enter(0, g.pre_even, g.grad_even)

        @pl.loop(0, count // 2)
        def _(step):
            enter(2 * step + 1, g.pre_odd, g.grad_odd)
            leave(2 * step, g.pre_even, g.grad_even)
            enter(lax.rem(2 * step + 2, count), g.pre_even, g.grad_even)
            leave(2 * step + 1, g.pre_odd, g.grad_odd)

        @pl.when(part == 0)
        def _():
            for later in range(4, parts):
                pass_second(later)

        @pl.when(part == 1)
        def _():
            for later in range(4, parts):
                pass_third(later)

        @pl.when(part >= 4)
        def _():
            last_stage(part - 4)

        @pl.when(part >= 3)
        def _():
            level_stage(part - 3)

        @pl.when(part >= 2)
        def _():
            quarter_stage(part - 2)

        @pl.when(part >= 1)
        def _():
            half_stage(part - 1)

        @pl.when(part >= 1)
        def _():
            for matrix in range(2):
                core_copy(part - 1, matrix).wait_send()

        shape = g.grads.shape[1:]
        g.grads[0] = dot_nn(g.normed_turned[...], g.slope[...]).astype(low).reshape(shape)
        core_copy(part, 0).start()
        g.grads[1] = dot_nn(g.cot_turned[...], g.act[...]).astype(low).reshape(shape)
        core_copy(part, 1).start()

    g.folds[...] = jnp.zeros_like(g.folds)

    def second_back(rows):
        grad = g.back[rows, :]
        unit = g.unit_two[rows, :].astype(f32)
        cot = g.cot_in[rows, :].astype(f32)
        pulled = grad * g.gains[2:3, :]
        middle = jnp.mean(pulled, axis=-1, keepdims=True)
        slant = jnp.mean(pulled * unit, axis=-1, keepdims=True)
        total = cot + g.scale_two[rows, :] * (pulled - middle - unit * slant)
        g.back[rows, :] = total
        g.normed[rows, :] = total.astype(low)
        g.folds[2] += fold(grad * unit)
        g.folds[3] += fold(grad)
        g.folds[4] += fold(cot)

    loads["lon_it"].wait()
    for part in range(2):
        half_strips(second_back, part)
        for step in range(1, group):
            block_copy(0, part, step).wait_send()
        to_blocks(g.lon_it_in[...], 1, part)

    last_stage(parts - 4)
    level_stage(parts - 3)
    quarter_stage(parts - 2)
    half_stage(parts - 1)

    def low_out(rows):
        store_columns("fields_cols", rows, g.grid[rows, :].astype(low))

    strips(low_out)
    out_copies = column_copies(g.fields_cols, g.out, g.fields_sem, True)
    for copy in out_copies:
        copy.start()
    loads["valid"].wait()
    loads["turn"].wait()
    weigh = sum(
        dot_nn(g.valid_in[:, row, :].astype(f32).astype(low), g.turn_in[row])
        for row in range(g.valid.shape[1])
    )
    places_each = weigh.shape[1]
    precise = lax.Precision.HIGHEST
    sums = [jnp.zeros((1, 128), f32), jnp.zeros((1, 128), f32)]
    for snap in range(g.valid.shape[0]):
        variables = g.grid[snap * places_each : (snap + 1) * places_each, 0:128]
        for index, value in enumerate((variables, variables * variables)):
            sums[index] += jnp.dot(
                weigh[snap : snap + 1, :], value, precision=precise, preferred_element_type=f32
            )

    def dot_tn(left, right):
        return lax.dot_general(
            left, right, (((0,), (0,)), ((), ())), preferred_element_type=f32
        )

    def filter_rows(first, grad):
        g.pair_grad[...] = grad
        real = g.pair_grad[0:128, 0:128] + g.pair_grad[128:256, 128:256]
        imag = g.pair_grad[0:128, 128:256] - g.pair_grad[128:256, 0:128]
        g.filt_out[me_snap, first] = real[0:owned].astype(low)
        g.filt_out[me_snap, first + 1] = imag[0:owned].astype(low)

    for part in range(2):
        for step in range(1, group):
            block_copy(1, part, step).wait_recv()
        rows = mode_half(part)
        spectra(g.grad_pre, f32, part)
        bend = jnp.tanh(g.pre_two[rows, :] / shrink_level)
        grad = (g.grad_pre[rows, :] * keep_half() * (bend * bend)).astype(low)
        g.grad_two[rows, :] = grad
        grad = dot_nt(grad, g.weight_two[...]) * gelu_both(g.pre_one[rows, :])[1]
        grad = grad.astype(low)
        g.grad_one[rows, :] = grad
        for step in range(1, group):
            row_copy(0, part, step).wait_send()
        grids(dot_nt(grad, g.weight_one[...]).astype(low), part)
        to_rows(1, part)
    last_stage(parts - 3)
    level_stage(parts - 2)
    quarter_stage(parts - 1)
    bias_one = jnp.sum(g.grad_one[...].astype(f32), axis=0, keepdims=True)
    bias_two = jnp.sum(g.grad_two[...].astype(f32), axis=0, keepdims=True)
    filter_rows(2, dot_tn(g.act_one[...], g.grad_two[...]))
    filter_rows(0, dot_tn(g.spectrum[...], g.grad_one[...]))

    def filter_copy(step):
        view = g.filt_out.at[me_snap]
        return send(view, view, (g.filt_s, g.filt_r), step, at(snap_after(step), me_sp))

    for step in range(1, snaps):
        filter_copy(step).start()


    loads["lon_ft"].wait()
    strip_pairs = strip // g.fields.shape[1]
    grad_view = g.grad_cols.reshape(2, tiles, strip, 128)

    def grad_copies(place, slot):
        pairs_out = pl.ds(place * strip_pairs, strip_pairs)
        return column_copies(
            g.grad_cols.at[slot], g.in_grad.at[pairs_out], g.grad_sem.at[slot], True
        )

    steps = half_tokens // strip
    for part in range(2):
        home_modes(1, part)
        if part == 1:
            last_stage(parts - 2)
            level_stage(parts - 1)
        g.grid[half_rows(part), :] = g.back[half_rows(part), :] + dot_nn(
            g.lon_ft_in[...], g.home_low[part]
        )

        @pl.loop(0, steps)
        def _(step):
            place = part * steps + step
            slot = lax.rem(place, 2)

            @pl.when(place >= 2)
            def _():
                for copy in grad_copies(place, slot):
                    copy.wait()

            for at_row in range(0, strip, sub):
                rows = pl.ds(pl.multiple_of(place * strip + at_row, 16), sub)
                grad = g.grid[rows, :]
                unit = g.unit_one[rows, :].astype(f32)
                pulled = grad * g.gains[0:1, :]
                middle = jnp.mean(pulled, axis=-1, keepdims=True)
                slant = jnp.mean(pulled * unit, axis=-1, keepdims=True)
                total = g.back[rows, :] + g.scale_one[rows, :] * (pulled - middle - unit * slant)
                for tile_at in range(tiles):
                    grad_view[slot, tile_at, at_row : at_row + sub, :] = total[
                        :, tile_at * 128 : (tile_at + 1) * 128
                    ]
                g.folds[0] += fold(grad * unit)
                g.folds[1] += fold(grad)
            for copy in grad_copies(place, slot):
                copy.start()

    g.grad_rows[...] = jnp.zeros_like(g.grad_rows)
    for index, row in enumerate((0, 1, 2, 3, 8)):
        g.grad_rows[row : row + 1, :] = jnp.sum(g.folds[index], axis=0, keepdims=True)
    flat = jnp.concatenate(
        [jnp.sum(g.grad_bias[part], axis=0, keepdims=True) for part in range(parts)], axis=1
    )
    for row in range(rows_small - 9):
        g.grad_rows[9 + row : 10 + row, :] = flat[:, row * channel : (row + 1) * channel]
    for block in range(group):
        g.tiles[block] = jnp.zeros(g.tiles.shape[1:], f32)
        g.tiles[block, :, 0:owned] = g.grad_rows[:, block * owned : (block + 1) * owned]
        g.tiles[block, 13:14, :] = sums[0]
        g.tiles[block, 14:15, :] = sums[1]

    def tile_copy(step):
        target = sp_after(step)
        return send(
            g.tiles.at[target], g.tiles_got.at[me_sp], (g.tile_s, g.tile_r), step, at(me_snap, target)
        )

    def snap_tile_copy(step):
        view = g.snap_tiles.at[me_snap]
        return send(view, view, (g.snap_tile_s, g.snap_tile_r), step, at(snap_after(step), me_sp))

    for step in range(1, group):
        tile_copy(step).start()
    last_stage(parts - 1)

    g.tiles_got[me_sp] = g.tiles[me_sp]
    for step in range(1, group):
        tile_copy(step).wait_recv()
    tile_sum = g.tiles_got[0]
    for sp in range(1, group):
        tile_sum += g.tiles_got[sp]
    g.snap_tiles[me_snap] = tile_sum
    g.snap_tiles[me_snap, 4:5, :] = bias_one[:, 0:128]
    g.snap_tiles[me_snap, 5:6, :] = bias_one[:, 128:256]
    g.snap_tiles[me_snap, 6:7, :] = bias_two[:, 0:128]
    g.snap_tiles[me_snap, 7:8, :] = bias_two[:, 128:256]
    for step in range(1, snaps):
        snap_tile_copy(step).start()

    for step in range(1, snaps):
        filter_copy(step).wait_recv()
    filter_sum = g.filt_out[0].astype(f32)
    for snap in range(1, snaps):
        filter_sum += g.filt_out[snap].astype(f32)
    g.grad_filt[...] = filter_sum
    for part in range(parts):
        for matrix in range(2):
            for step in range(1, snaps):
                last_copy(part, matrix, step).wait_recv()
    grads_out = pltpu.make_async_copy(g.total, g.grad_mlp, g.load_sem.at[3])
    grads_out.start()
    for step in range(1, snaps):
        snap_tile_copy(step).wait_recv()
    tile_sum = g.snap_tiles[0]
    for snap in range(1, snaps):
        tile_sum += g.snap_tiles[snap]
    g.grad_small[...] = tile_sum

    grads_out.wait()
    for copy in out_copies:
        copy.wait()
    for slot in range(2):
        for copy in grad_copies(0, slot):
            copy.wait()
    for step in range(1, group):
        small_copy(step).wait_send()
        for part in range(2):
            block_copy(1, part, step).wait_send()
            row_copy(1, part, step).wait_send()
        tile_copy(step).wait_send()
        for part in range(parts):
            first_copy(part, step).wait_send()
    for part in range(parts):
        second_copy(part).wait_send()
        third_copy(part).wait_send()
        fourth_copy(part).wait_send()
    for matrix in range(2):
        core_copy(parts - 1, matrix).wait_send()
    for part in (parts - 2, parts - 1):
        for matrix in range(2):
            half_copy(part, matrix).wait_send()
            quarter_copy(part, matrix).wait_send()
        for step in range(1, levels):
            level_copy(part, step).wait_send()
    for step in range(1, snaps):
        filter_copy(step).wait_send()
        snap_tile_copy(step).wait_send()
        for part in range(parts):
            for matrix in range(2):
                last_copy(part, matrix, step).wait_send()


def block_pass(fields, cot, valid, kept, mlp, filt, small, snaps, group):
    snap_local, row_local, lon_total, channel = fields.shape
    tokens = snap_local * row_local * lon_total
    hidden = mlp.shape[2]
    lat_total = row_local * group
    modes = kept.shape[1] * group
    owned = channel // group
    width = 512
    parts = hidden // width
    levels = group // 2
    quarter = width // snaps
    low, f32 = jnp.bfloat16, jnp.float32
    half = width // 2
    half_snaps = snap_local // 2
    lon_f, lon_i = lon_matrix(lon_total, modes, half_snaps, row_local)

    def paired(array):
        return jnp.transpose(array, (0, 2, 1, 3)).reshape(-1, row_local, channel)

    lat_f = lat_matrix(lat_total, modes)
    pair = 2 * modes * row_local
    spread = half_snaps * row_local * 2 * modes
    inputs = dict(
        small=small,
        kept=kept.T,
        fields=paired(fields),
        lon_f=jnp.asarray(np.ascontiguousarray(lon_f.T)),
        filt=filt,
        lat_f=jnp.asarray(lat_f),
        lat_b=jnp.asarray(np.ascontiguousarray(lat_f.T)),
        cot=paired(cot),
        lon_i=jnp.asarray(lon_i),
        valid=valid,
        turn=jnp.asarray(lon_turn(lon_total, row_local)),
        lon_it=jnp.asarray(np.ascontiguousarray(lon_i.T)),
        lon_ft=jnp.asarray(lon_f),
        mlp=mlp,
    )
    outputs = dict(
        out=jax.ShapeDtypeStruct((tokens // row_local, row_local, channel), low),
        in_grad=jax.ShapeDtypeStruct((tokens // row_local, row_local, channel), f32),
        grad_mlp=jax.ShapeDtypeStruct((parts, snaps, 2, owned, quarter), low),
        grad_filt=jax.ShapeDtypeStruct((4, owned, 128), f32),
        grad_small=jax.ShapeDtypeStruct((16, 128), f32),
    )
    vmem = pltpu.VMEM
    dma = pltpu.SemaphoreType.DMA
    scratch = {
        name + "_in": vmem(value.shape, value.dtype)
        for name, value in inputs.items()
        if name not in ("mlp", "fields", "cot")
    }
    tiles = channel // 128
    cols = (tiles, tokens // row_local, row_local, 128)
    tile = divisor(tokens // 2, 16, 240)
    strip = divisor(tokens // 2, 48, 144)
    scratch |= dict(
        mlp_part=vmem((2, 2, owned, width), f32),
        fields_cols=vmem(cols, low),
        cot_cols=vmem(cols, low),
        grad_cols=vmem((2, tiles, strip // row_local, row_local, 128), f32),
        grad_sem=dma((2, tiles)),
        fields_sem=dma((tiles,)),
        cot_sem=dma((tiles,)),
        cot_in=vmem((tokens, channel), low),
        grid=vmem((tokens, channel), f32),
        back=vmem((tokens, channel), f32),
        normed=vmem((tokens, channel), low),
        normed_turned=vmem((channel, tokens), low),
        cot_turned=vmem((channel, tokens), low),
        unit_one=vmem((tokens, channel), low),
        unit_two=vmem((tokens, channel), low),
        scale_one=vmem((tokens, 1), f32),
        scale_two=vmem((tokens, 1), f32),
        own_small=vmem((16 + kept.shape[0], 128), f32),
        all_small=vmem((group, 16 + kept.shape[0], 128), f32),
        gains=vmem((16, channel), f32),
        keep=vmem((lat_total * modes, 128), f32),
        own_w=vmem((parts, 2, snaps, owned, quarter), low),
        all_w=vmem((parts, 2, snaps, channel, quarter), low),
        modes=vmem((2, group, half_snaps, pair, 128), low),
        arrived=vmem((snap_local, pair * group, 128), low),
        turned=vmem((snap_local, pair * group, 128), low),
        home=vmem((2, group, half_snaps, pair, 128), low),
        gathered=vmem((2, spread, channel), f32),
        home_low=vmem((2, spread, channel), low),
        weight_one=vmem((256, 256), low),
        weight_two=vmem((256, 256), low),
        spectrum=vmem((snap_local * lat_total * modes, 256), low),
        pre_one=vmem((snap_local * lat_total * modes, 256), f32),
        act_one=vmem((snap_local * lat_total * modes, 256), low),
        pre_two=vmem((snap_local * lat_total * modes, 256), f32),
        grad_pre=vmem((snap_local * lat_total * modes, 256), f32),
        grad_two=vmem((snap_local * lat_total * modes, 256), low),
        grad_one=vmem((snap_local * lat_total * modes, 256), low),
        folds=vmem((5, 8, channel), f32),
        pair_grad=vmem((256, 256), f32),
        pre_even=vmem((tile, width), f32),
        pre_odd=vmem((tile, width), f32),
        grad_even=vmem((tile, width), f32),
        grad_odd=vmem((tile, width), f32),
        act=vmem((tokens, width), low),
        slope=vmem((tokens, width), low),
        bias=vmem((parts, 1, width), f32),
        grad_bias=vmem((parts, 8, width), f32),
        grad_rows=vmem((16, channel), f32),
        grads=vmem((2, levels, 2, owned, width), low),
        core_got=vmem((2, 2, levels, owned, width), low),
        half_out=vmem((2, 2, 2, levels, owned, half), low),
        half_got=vmem((2, 2, levels, owned, half), low),
        quarter_out=vmem((2, 2, 2, levels, owned, quarter), low),
        quarter_got=vmem((2, 2, levels, owned, quarter), low),
        level_out=vmem((2, levels, 2, owned, quarter), low),
        level_got=vmem((2, levels, 2, owned, quarter), low),
        total=vmem((parts, snaps, 2, owned, quarter), low),
        filt_out=vmem((snaps, 4, owned, 128), low),
        tiles=vmem((group, 16, 128), f32),
        tiles_got=vmem((group, 16, 128), f32),
        snap_tiles=vmem((snaps, 16, 128), f32),
        load_sem=dma((len(inputs) + 1,)),
    )
    for name, shape in dict(
        small=(group,),
        first=(parts, group),
        second=(parts,),
        third=(parts,),
        fourth=(parts,),
        block=(2, 2, group),
        row=(2, 2, group),
        core=(2, 2),
        half=(2, 2),
        quarter=(2, 2),
        level=(2, levels),
        last=(parts, 2, snaps),
        filt=(snaps,),
        tile=(group,),
        snap_tile=(snaps,),
    ).items():
        scratch[name + "_s"] = dma(shape)
        scratch[name + "_r"] = dma(shape)
    names = [*inputs, *outputs, *scratch]
    far = pl.BlockSpec(memory_space=pl.ANY)
    near = pl.BlockSpec(memory_space=pltpu.VMEM)
    results = pl.pallas_call(
        functools.partial(block_body, names, (snaps, group, parts, width)),
        in_specs=[far] * len(inputs),
        out_specs=[far, far, far, near, near],
        out_shape=list(outputs.values()),
        scratch_shapes=list(scratch.values()),
        compiler_params=pltpu.CompilerParams(
            collective_id=0, has_side_effects=True, vmem_limit_bytes=VMEM_LIMIT
        ),
        cost_estimate=pl.CostEstimate(
            flops=12 * tokens * channel * hidden,
            bytes_accessed=4 * hidden * channel,
            transcendentals=tokens * hidden,
        ),
        name="block_pass",
    )(*inputs.values())
    return results


def step_body(names, positions, *refs):
    g = Refs()
    for name, ref in zip(names, refs, strict=True):
        setattr(g, name, ref)
    parts, snaps = g.grad_mlp.shape[:2]
    quarter = g.grad_mlp.shape[4]
    width = snaps * quarter
    moments = ("w", "m", "v")
    results = ("new", "first", "second", "copy")

    pieces = g.far_sem.shape[2]
    ends = ((g.out, g.out_near, g.out_o), (g.in_grad, g.in_grad_near, g.in_grad_o))

    def passing(kind, piece, leg):
        size = ends[kind][0].shape[0] // pieces
        rows = pl.ds(piece * size, size)
        return pltpu.make_async_copy(
            ends[kind][leg].at[rows], ends[kind][leg + 1].at[rows], g.far_sem.at[leg, kind, piece]
        )

    through = [(kind, piece) for kind in range(2) for piece in range(pieces)]

    def part_cols(part):
        return pl.ds(part * width, width)

    def load(part):
        near = [
            pltpu.make_async_copy(
                getattr(g, "mlp_" + kind).at[:, :, part_cols(part)],
                g.near.at[index, part],
                g.near_sem.at[index, part],
            )
            for index, kind in enumerate(moments)
        ]
        near.append(
            pltpu.make_async_copy(g.grad_mlp.at[part], g.grad_near.at[part], g.near_sem.at[3, part])
        )
        return near

    def store(part):
        copies = [
            pltpu.make_async_copy(
                g.near.at[index, part],
                getattr(g, "mlp_" + kind).at[:, :, part_cols(part)],
                g.back_sem.at[index, part],
            )
            for index, kind in enumerate(results[:3])
        ]
        copies.append(
            pltpu.make_async_copy(
                g.low_near.at[part], g.mlp_copy.at[:, :, part_cols(part)], g.back_sem.at[3, part]
            )
        )
        return copies

    coming = [load(part) for part in range(parts)]
    going = [store(part) for part in range(parts)]
    shares = [through[part::parts] for part in range(parts)]
    for part in range(parts):
        for copy in coming[part]:
            copy.start()
        for each in shares[part]:
            passing(*each, 0).start()

    def put(prefix, values):
        for kind, value in zip(results, values, strict=True):
            getattr(g, prefix + kind)[...] = value

    owned = g.filt_w.shape[2]
    put(
        "filt_",
        adamw(g.filt_w[...], g.filt_m[...], g.filt_v[...], g.grad_filt[:, :, 0:owned], rate_filter),
    )
    rows = g.small_w.shape[0]
    put(
        "small_",
        adamw(
            g.small_w[...], g.small_m[...], g.small_v[...], g.grad_small[0:rows, 0:owned], rate_small
        ),
    )
    totals = g.grad_small[rows : rows + 2, 0 : g.run.shape[1]]
    g.stats[...] = stat_decay * g.run[...] + (1.0 - stat_decay) * totals / positions

    for part in range(parts):
        for copy in coming[part]:
            copy.wait()

        for snap in range(snaps):
            cols = slice(snap * quarter, (snap + 1) * quarter)
            where = (slice(None), slice(None), cols)
            now = [g.near[(index, part, *where)] for index in range(3)]
            grad = g.grad_near[part, snap].astype(jnp.float32)
            values = adamw(*now, grad, rate_mlp)
            for index in range(3):
                g.near[(index, part, *where)] = values[index]
            g.low_near[(part, *where)] = values[3]
        for copy in going[part]:
            copy.start()
        for each in shares[part]:
            passing(*each, 0).wait()
            passing(*each, 1).start()
    for each in through:
        passing(*each, 1).wait()
    for part in range(parts):
        for copy in going[part]:
            copy.wait()


def step_pass(shown, grads, masters, run_stats, positions):
    grad_mlp, grad_filt, grad_small = grads
    mlp, filt, small = masters
    parts = grad_mlp.shape[0]
    width = mlp[0].shape[2] // parts
    f32, low = jnp.float32, jnp.bfloat16
    far = pl.BlockSpec(memory_space=pltpu.HBM)
    near = pl.BlockSpec(memory_space=pltpu.VMEM)
    inputs = dict(out=shown[0], in_grad=shown[1], grad_mlp=grad_mlp)
    inputs |= dict(zip(("mlp_w", "mlp_m", "mlp_v"), mlp, strict=True))
    far_in = len(inputs)
    inputs |= dict(grad_filt=grad_filt, grad_small=grad_small)
    inputs |= dict(zip(("filt_w", "filt_m", "filt_v"), filt, strict=True))
    inputs |= dict(zip(("small_w", "small_m", "small_v"), small, strict=True))
    inputs |= dict(run=run_stats)
    results = (("new", f32), ("first", f32), ("second", f32), ("copy", low))
    outputs = {
        name + "_o": jax.ShapeDtypeStruct(array.shape, array.dtype)
        for name, array in zip(("out", "in_grad"), shown, strict=True)
    }
    outputs |= {"mlp_" + kind: jax.ShapeDtypeStruct(mlp[0].shape, dt) for kind, dt in results}
    far_out = len(outputs)
    outputs |= {"filt_" + kind: jax.ShapeDtypeStruct(filt[0].shape, dt) for kind, dt in results}
    outputs |= {"small_" + kind: jax.ShapeDtypeStruct(small[0].shape, dt) for kind, dt in results}
    outputs |= dict(stats=jax.ShapeDtypeStruct(run_stats.shape, f32))
    scratch = dict(
        near=pltpu.VMEM((3, parts, 2, mlp[0].shape[1], width), f32),
        grad_near=pltpu.VMEM(grad_mlp.shape, low),
        low_near=pltpu.VMEM((parts, 2, mlp[0].shape[1], width), low),
        near_sem=pltpu.SemaphoreType.DMA((4, parts)),
        back_sem=pltpu.SemaphoreType.DMA((4, parts)),
        out_near=pltpu.VMEM(shown[0].shape, low),
        in_grad_near=pltpu.VMEM(shown[1].shape, f32),
        far_sem=pltpu.SemaphoreType.DMA((2, 2, divisor(shown[0].shape[0], 1, 4))),
    )
    return pl.pallas_call(
        functools.partial(step_body, [*inputs, *outputs, *scratch], positions),
        in_specs=[far] * far_in + [near] * (len(inputs) - far_in),
        out_specs=[far] * far_out + [near] * (len(outputs) - far_out),
        out_shape=list(outputs.values()),
        scratch_shapes=list(scratch.values()),
        compiler_params=pltpu.CompilerParams(vmem_limit_bytes=VMEM_LIMIT),
        name="step_pass",
    )(*inputs.values())


def per_device_blocks(
    fields,
    cotangent,
    valid_mask,
    kept_modes,
    mlp_master,
    mlp_first,
    mlp_second,
    filter_master,
    filter_first,
    filter_second,
    small_master,
    small_first,
    small_second,
    run_stats,
):
    snaps, group = lax.axis_size("snap"), lax.axis_size("sp")
    out, in_grad, *grads = block_pass(
        fields, cotangent, valid_mask, kept_modes, mlp_master, filter_master, small_master, snaps, group
    )
    snap_local, row_local, lon_total, channel = fields.shape
    positions = snap_local * snaps * row_local * group * lon_total
    out, in_grad, *stepped = step_pass(
        (out, in_grad),
        grads,
        (
            (mlp_master, mlp_first, mlp_second),
            (filter_master, filter_first, filter_second),
            (small_master, small_first, small_second),
        ),
        run_stats,
        positions,
    )
    rows_apart = (snap_local, lon_total, row_local, channel)
    out, in_grad = [
        jnp.transpose(array.reshape(rows_apart), (0, 2, 1, 3)) for array in (out, in_grad)
    ]
    return (out, in_grad, *stepped)


def per_device(*arrays):
    group, snaps = lax.axis_size("sp"), lax.axis_size("snap")
    channel, hidden = arrays[0].shape[3], arrays[4].shape[2]
    by_block = group == BLOCKS and snaps == 4 and arrays[3].shape[1] == 1
    if by_block and hidden % 512 == 0 and channel // group <= 128 and channel % (16 * group) == 0:
        return per_device_blocks(*arrays)
    return per_device_modes(*arrays)


def solution(mesh):
    return jax.shard_map(
        per_device,
        mesh=mesh,
        in_specs=(
            P("snap", "sp", None, None),
            P("snap", "sp", None, None),
            P("snap", "sp", None),
            P(None, "sp"),
            P(None, "sp", None),
            P(None, "sp", None),
            P(None, "sp", None),
            P(None, "sp", None),
            P(None, "sp", None),
            P(None, "sp", None),
            P(None, "sp"),
            P(None, "sp"),
            P(None, "sp"),
            P(),
        ),
        out_specs=(
            P("snap", "sp", None, None),
            P("snap", "sp", None, None),
            P(None, "sp", None),
            P(None, "sp", None),
            P(None, "sp", None),
            P(None, "sp", None),
            P(None, "sp", None),
            P(None, "sp", None),
            P(None, "sp", None),
            P(None, "sp", None),
            P(None, "sp"),
            P(None, "sp"),
            P(None, "sp"),
            P(None, "sp"),
            P(),
        ),
        check_vma=False,
    )
```

```python
import functools
import math

import jax
import jax.numpy as jnp
import ml_dtypes
import numpy as np
from jax import lax
from jax.experimental import pallas as pl
from jax.experimental.pallas import tpu as pltpu
from jax.sharding import PartitionSpec as P

BLOCKS = 8
NVAR = 20
STEP = 10
VMEM_LIMIT = 63 * 1024 * 1024


eps_norm = 1e-06
shrink_level = 0.01
beta_one = 0.5
beta_two = 0.5
adam_eps = 1e-08
decay_rate = 0.01
rate_mlp = 0.03
rate_filter = 0.1
rate_small = 0.2
stat_decay = 0.5


def layer_norm(values, gain_vec, shift_vec):
    centred = values - jnp.mean(values, axis=-1, keepdims=True)
    spread = jnp.mean(centred * centred, axis=-1, keepdims=True)
    return centred * lax.rsqrt(spread + eps_norm) * gain_vec + shift_vec


def shrink(values):
    return values - shrink_level * jnp.tanh(values / shrink_level)


def lon_tables(lon_total, mode_total):
    places = jnp.arange(lon_total, dtype=jnp.int32)
    orders = jnp.arange(mode_total, dtype=jnp.int32)
    angles = (places[:, None] * orders[None, :] % lon_total).astype(jnp.float32) * (
        2.0 * math.pi / lon_total
    )
    scaling = 1.0 / math.sqrt(lon_total)
    forward_tab = jnp.stack([jnp.cos(angles), -jnp.sin(angles)], axis=1) * scaling
    doubling = jnp.where(orders == 0, 1.0, 2.0).astype(jnp.float32)[:, None]
    inverse_tab = (
        jnp.stack([jnp.cos(angles).T * doubling, -jnp.sin(angles).T * doubling], axis=0) * scaling
    )
    return (forward_tab.astype(jnp.bfloat16), inverse_tab.astype(jnp.bfloat16))


def lat_table(lat_total):
    places = jnp.arange(lat_total, dtype=jnp.int32)
    angles = (places[:, None] * places[None, :] % lat_total).astype(jnp.float32) * (
        2.0 * math.pi / lat_total
    )
    cosine = jnp.cos(angles)
    sine_part = jnp.sin(angles)
    upper_rows = jnp.stack([cosine, sine_part], axis=1)
    bottom = jnp.stack([-sine_part, cosine], axis=1)
    return (jnp.stack([upper_rows, bottom], axis=0) / math.sqrt(lat_total)).astype(jnp.bfloat16)


def complex_pair(real_part, imag_part):
    return jnp.stack([jnp.stack([real_part, -imag_part]), jnp.stack([imag_part, real_part])])


gelu_scale = math.sqrt(2.0 / math.pi)
gelu_cubic = 0.044715


def gelu_both(value):
    bend = (gelu_scale * gelu_cubic) * (value * value)
    turn = jnp.tanh(value * (gelu_scale + bend))
    half = 0.5 + 0.5 * turn
    slope = half * (1.0 + (value * (1.0 - turn)) * (gelu_scale + 3.0 * bend))
    return value * half, slope


def dot_nt(left, right):
    return lax.dot_general(
        left, right, (((1,), (1,)), ((), ())), preferred_element_type=jnp.float32
    )


def dot_nn(left, right):
    return jnp.dot(left, right, preferred_element_type=jnp.float32)


def divisor(total, unit, most):
    return max(size for size in range(unit, most + 1, unit) if total % size == 0)


def mlp_body(
    tile,
    normed_ref,
    cot_ref,
    up_ref,
    down_ref,
    bias_ref,
    out_ref,
    back_ref,
    grad_up_ref,
    grad_down_ref,
    grad_bias_ref,
    normed_turned,
    cot_turned,
    act_ref,
    slope_ref,
):
    tokens = normed_ref.shape[0]

    @pl.when(pl.program_id(0) == 0)
    def _():
        normed_turned[...] = normed_ref[...].T
        cot_turned[...] = cot_ref[...].T
        out_ref[...] = jnp.zeros_like(out_ref)
        back_ref[...] = jnp.zeros_like(back_ref)

    grad_bias_ref[...] = jnp.zeros_like(grad_bias_ref)

    @pl.loop(0, tokens // tile)
    def _(step):
        rows = pl.ds(pl.multiple_of(step * tile, tile), tile)
        act, slope = gelu_both(dot_nn(normed_ref[rows, :], up_ref[...]) + bias_ref[...])
        act = act.astype(jnp.bfloat16)
        slope = (dot_nn(cot_ref[rows, :], down_ref[...]) * slope).astype(jnp.bfloat16)
        act_ref[rows, :] = act
        slope_ref[rows, :] = slope
        grad_bias_ref[...] += jnp.sum(slope.astype(jnp.float32), axis=0, keepdims=True)
        out_ref[rows, :] += dot_nt(act, down_ref[...])
        back_ref[rows, :] += dot_nt(slope, up_ref[...])

    grad_up_ref[...] = dot_nn(normed_turned[...], slope_ref[...]).astype(grad_up_ref.dtype)
    grad_down_ref[...] = dot_nn(cot_turned[...], act_ref[...]).astype(grad_down_ref.dtype)


def mlp_pass(normed, cot, weights, bias):
    tokens, channel = normed.shape
    hidden = weights.shape[2]
    width = divisor(hidden, 128, 512)
    tile = divisor(tokens, 16, 480)
    whole = pl.BlockSpec((tokens, channel), lambda j: (0, 0))
    block = pl.BlockSpec((channel, width), lambda j: (0, j))
    line = pl.BlockSpec((1, width), lambda j: (0, j))
    part = lambda which: pl.BlockSpec((None, channel, width), lambda j: (which, 0, j))
    total = jax.ShapeDtypeStruct((tokens, channel), jnp.float32)
    grads = jax.ShapeDtypeStruct((channel, hidden), jnp.bfloat16)
    return pl.pallas_call(
        functools.partial(mlp_body, tile),
        grid=(hidden // width,),
        in_specs=[whole, whole, part(0), part(1), line],
        out_specs=[whole, whole, block, block, line],
        out_shape=[total, total, grads, grads, jax.ShapeDtypeStruct((1, hidden), jnp.float32)],
        scratch_shapes=[
            pltpu.VMEM((channel, tokens), jnp.bfloat16),
            pltpu.VMEM((channel, tokens), jnp.bfloat16),
            pltpu.VMEM((tokens, width), jnp.bfloat16),
            pltpu.VMEM((tokens, width), jnp.bfloat16),
        ],
        compiler_params=pltpu.CompilerParams(vmem_limit_bytes=56 * 1024 * 1024),
        cost_estimate=pl.CostEstimate(
            flops=12 * tokens * channel * hidden,
            bytes_accessed=8 * channel * hidden + 12 * tokens * channel,
            transcendentals=tokens * hidden,
        ),
        name="mlp_pass",
    )(normed, cot, weights, weights, bias)


def spectral_front(arrived, lat_fwd, first_pair, second_pair, bias_one, bias_two):
    spectrum = jnp.einsum(
        "pkqr,nrqmd->nkpmd", lat_fwd, arrived, preferred_element_type=jnp.float32
    ).astype(jnp.bfloat16)
    snap_local, lat_total, pair_count, mode_local, channel = spectrum.shape
    blocked = spectrum.reshape(
        snap_local, lat_total, pair_count, mode_local, BLOCKS, channel // BLOCKS
    )
    pre_one = (
        jnp.einsum("nkqmbi,pqbio->nkpmbo", blocked, first_pair, preferred_element_type=jnp.float32)
        + bias_one
    )
    act_one = jax.nn.gelu(pre_one).astype(jnp.bfloat16)
    pre_two = (
        jnp.einsum("nkqmbi,pqbio->nkpmbo", act_one, second_pair, preferred_element_type=jnp.float32)
        + bias_two
    )
    return (blocked, pre_one, act_one, pre_two)


def adamw(master, first_mom, second_mom, gradient, step_rate):
    first_next = beta_one * first_mom + (1.0 - beta_one) * gradient
    second_next = beta_two * second_mom + (1.0 - beta_two) * gradient * gradient
    fix_one = 1.0 - beta_one**STEP
    fix_two = 1.0 - beta_two**STEP
    direction = first_next / fix_one / (jnp.sqrt(second_next / fix_two) + adam_eps)
    master_next = master - step_rate * (direction + decay_rate * master)
    return (master_next, first_next, second_next, master_next.astype(jnp.bfloat16))


def per_device_modes(
    fields,
    cotangent,
    valid_mask,
    kept_modes,
    mlp_master,
    mlp_first,
    mlp_second,
    filter_master,
    filter_first,
    filter_second,
    small_master,
    small_first,
    small_second,
    run_stats,
):
    group_size = lax.axis_size("sp")
    snap_local, row_local, lon_total, channel = fields.shape
    lat_total = row_local * group_size
    mode_local = kept_modes.shape[1]
    mode_total = mode_local * group_size
    block_width = channel // BLOCKS
    lon_fwd, lon_inv = lon_tables(lon_total, mode_total)
    lat_fwd = lat_table(lat_total)
    mlp_w, filt_w, small_w = (
        lax.all_gather(mlp_master.astype(jnp.bfloat16), "sp", axis=1, tiled=True),
        lax.all_gather(filter_master.astype(jnp.bfloat16), "sp", axis=1, tiled=True),
        lax.all_gather(small_master.astype(jnp.bfloat16), "sp", axis=1, tiled=True),
    )
    small_f = small_w.astype(jnp.float32)
    weights = filt_w.reshape(4, BLOCKS, block_width, block_width)
    first_pair = complex_pair(weights[0], weights[1])
    second_pair = complex_pair(weights[2], weights[3])
    bias_one = small_f[4:6].reshape(2, 1, BLOCKS, block_width)
    bias_two = small_f[6:8].reshape(2, 1, BLOCKS, block_width)
    fields_float = fields.astype(jnp.float32)
    normed, norm_pull = jax.vjp(layer_norm, fields_float, small_f[0], small_f[1])
    normed_low = normed.astype(jnp.bfloat16)
    spec_lon = jnp.einsum(
        "nrld,lqm->nrqmd", normed_low, lon_fwd, preferred_element_type=jnp.float32
    ).astype(jnp.bfloat16)
    arrived = lax.all_to_all(spec_lon, "sp", split_axis=3, concat_axis=1, tiled=True)
    spectral = spectral_front(arrived, lat_fwd, first_pair, second_pair, bias_one, bias_two)
    keep_mask = kept_modes.astype(jnp.float32)[None, :, None, :, None, None]
    masked = (shrink(spectral[3]) * keep_mask).astype(jnp.bfloat16)
    masked = masked.reshape(snap_local, lat_total, 2, mode_local, channel)
    returned = jnp.einsum(
        "pkqr,nkpmd->nrqmd", lat_fwd, masked, preferred_element_type=jnp.float32
    ).astype(jnp.bfloat16)
    home_modes = lax.all_to_all(returned, "sp", split_axis=1, concat_axis=3, tiled=True)
    filtered = jnp.einsum(
        "nrqmd,qml->nrld", home_modes, lon_inv, preferred_element_type=jnp.float32
    )
    mixture = fields_float + normed + filtered
    normed_two, norm_two_pull = jax.vjp(layer_norm, mixture, small_f[2], small_f[3])
    normed_two_low = normed_two.astype(jnp.bfloat16)
    tokens = snap_local * row_local * lon_total
    passed = mlp_pass(
        normed_two_low.reshape(tokens, channel),
        cotangent.reshape(tokens, channel),
        mlp_w,
        small_f[9:].reshape(1, -1),
    )
    output = mixture + passed[0].reshape(mixture.shape) + small_f[8]
    weight_mask = valid_mask.astype(jnp.float32)[..., None]
    variables = output[..., :NVAR]
    local_sums = jnp.stack(
        [
            jnp.sum(weight_mask * variables, axis=(0, 1, 2)),
            jnp.sum(weight_mask * variables * variables, axis=(0, 1, 2)),
        ]
    )
    total_sums = lax.psum(local_sums, ("snap", "sp"))
    positions = snap_local * lax.axis_size("snap") * lat_total * lon_total
    stats_new = stat_decay * run_stats + (1.0 - stat_decay) * total_sums / positions
    cot_float = cotangent.astype(jnp.float32)
    grad_normed_two = passed[1].reshape(mixture.shape)
    grad_bias_hidden = passed[4]
    grad_mix_norm, grad_gain_two, grad_shift_two = norm_two_pull(grad_normed_two)
    grad_mixture = cot_float + grad_mix_norm
    grad_bias_out = jnp.sum(cot_float, axis=(0, 1, 2))
    grad_filtered = grad_mixture.astype(jnp.bfloat16)
    grad_home = jnp.einsum(
        "nrld,qml->nrqmd", grad_filtered, lon_inv, preferred_element_type=jnp.float32
    ).astype(jnp.bfloat16)
    grad_returned = lax.all_to_all(grad_home, "sp", split_axis=3, concat_axis=1, tiled=True)
    grad_masked = jnp.einsum(
        "pkqr,nrqmd->nkpmd", lat_fwd, grad_returned, preferred_element_type=jnp.float32
    )
    arrived_again = lax.all_to_all(spec_lon, "sp", split_axis=3, concat_axis=1, tiled=True)
    used_front = spectral_front(arrived_again, lat_fwd, first_pair, second_pair, bias_one, bias_two)
    blocked, pre_one, act_one, pre_two = used_front
    grad_two = jax.vjp(shrink, pre_two)[1](grad_masked.reshape(pre_two.shape) * keep_mask)[
        0
    ].astype(jnp.bfloat16)
    grad_bias_two = jnp.sum(grad_two.astype(jnp.float32), axis=(0, 1, 3))
    grad_second = jnp.einsum(
        "nkqmbi,nkpmbo->pqbio", act_one, grad_two, preferred_element_type=jnp.float32
    )
    grad_act = jnp.einsum(
        "nkpmbo,pqbio->nkqmbi", grad_two, second_pair, preferred_element_type=jnp.float32
    )
    grad_one = jax.vjp(jax.nn.gelu, pre_one)[1](grad_act)[0].astype(jnp.bfloat16)
    grad_bias_one = jnp.sum(grad_one.astype(jnp.float32), axis=(0, 1, 3))
    grad_first = jnp.einsum(
        "nkqmbi,nkpmbo->pqbio", blocked, grad_one, preferred_element_type=jnp.float32
    )
    grad_spectrum = jnp.einsum(
        "nkpmbo,pqbio->nkqmbi", grad_one, first_pair, preferred_element_type=jnp.float32
    ).astype(jnp.bfloat16)
    grad_spectrum = grad_spectrum.reshape(snap_local, lat_total, 2, mode_local, channel)
    grad_lon = jnp.einsum(
        "pkqr,nkpmd->nrqmd", lat_fwd, grad_spectrum, preferred_element_type=jnp.float32
    ).astype(jnp.bfloat16)
    grad_rows = lax.all_to_all(grad_lon, "sp", split_axis=1, concat_axis=3, tiled=True)
    grad_normed = grad_mixture + jnp.einsum(
        "nrqmd,lqm->nrld", grad_rows, lon_fwd, preferred_element_type=jnp.float32
    )
    grad_field_norm, grad_gain_one, grad_shift_one = norm_pull(grad_normed)
    input_grad = grad_mixture + grad_field_norm
    grad_filter = jnp.stack(
        [
            grad_first[0, 0] + grad_first[1, 1],
            grad_first[1, 0] - grad_first[0, 1],
            grad_second[0, 0] + grad_second[1, 1],
            grad_second[1, 0] - grad_second[0, 1],
        ]
    ).reshape(4, channel, block_width)
    grad_small = jnp.concatenate(
        [
            jnp.stack([grad_gain_one, grad_shift_one, grad_gain_two, grad_shift_two]),
            grad_bias_one.reshape(2, channel),
            grad_bias_two.reshape(2, channel),
            grad_bias_out[None, :],
            grad_bias_hidden.reshape(-1, channel),
        ],
        axis=0,
    )
    shares = (
        jnp.stack([
            lax.psum_scatter(part, "sp", scatter_dimension=0, tiled=True) for part in passed[2:4]
        ]),
        lax.psum_scatter(grad_filter, "sp", scatter_dimension=1, tiled=True),
        lax.psum_scatter(grad_small, "sp", scatter_dimension=1, tiled=True),
    )
    owned = (
        lax.psum(shares[0].astype(jnp.bfloat16), "snap").astype(jnp.float32),
        lax.psum(shares[1].astype(jnp.bfloat16), "snap").astype(jnp.float32),
        lax.psum(shares[2].astype(jnp.bfloat16), "snap").astype(jnp.float32),
    )
    mlp_new, mlp_first_new, mlp_second_new, mlp_copy = adamw(
        mlp_master, mlp_first, mlp_second, owned[0], rate_mlp
    )
    filter_new, filter_first_new, filter_second_new, filter_copy = adamw(
        filter_master, filter_first, filter_second, owned[1], rate_filter
    )
    small_new, small_first_new, small_second_new, small_copy = adamw(
        small_master, small_first, small_second, owned[2], rate_small
    )
    return (
        output.astype(jnp.bfloat16),
        input_grad,
        mlp_new,
        mlp_first_new,
        mlp_second_new,
        mlp_copy,
        filter_new,
        filter_first_new,
        filter_second_new,
        filter_copy,
        small_new,
        small_first_new,
        small_second_new,
        small_copy,
        stats_new,
    )


def lon_matrix(lon_total, mode_total, snaps, rows):
    places = np.arange(lon_total)
    orders = np.arange(mode_total)
    angles = (places[:, None] * orders[None, :] % lon_total) * (2.0 * math.pi / lon_total)
    doubling = np.where(orders == 0, 1.0, 2.0)
    scaling = 1.0 / math.sqrt(lon_total)
    forward = np.stack([np.cos(angles), -np.sin(angles)], axis=1) * scaling
    inverse = forward * doubling

    def spread(table):
        table = np.einsum(
            "ab,lx,rs->alrbsx", np.eye(snaps), table.reshape(lon_total, -1), np.eye(rows)
        )
        return table.reshape(snaps * lon_total * rows, -1).astype(ml_dtypes.bfloat16)

    return spread(forward), spread(inverse)


def lon_turn(lon_total, rows):
    turn = np.einsum("lk,rs->rlks", np.eye(lon_total), np.eye(rows))
    return turn.reshape(rows, lon_total, lon_total * rows).astype(ml_dtypes.bfloat16)


def lat_matrix(lat_total, mode_total):
    places = np.arange(lat_total)
    angles = (places[:, None] * places[None, :] % lat_total) * (2.0 * math.pi / lat_total)
    cosine, sine = np.cos(angles), np.sin(angles)
    table = np.stack([np.stack([cosine, sine], axis=1), np.stack([-sine, cosine], axis=1)])
    table = np.einsum("pkqr,ab->pakrqb", table / math.sqrt(lat_total), np.eye(mode_total))
    size = 2 * lat_total * mode_total
    return table.reshape(size, size).astype(ml_dtypes.bfloat16)


class Refs:
    pass


def block_body(names, sizes, *refs):
    g = Refs()
    for name, ref in zip(names, refs, strict=True):
        setattr(g, name, ref)
    snaps, group, parts, width = sizes
    levels = group // 2
    tokens = g.fields.shape[0] * g.fields.shape[1]
    channel = g.fields.shape[2]
    tiles = channel // 128
    owned = channel // group
    half = width // 2
    quarter = width // snaps
    tile = tokens // 3
    strip = divisor(tokens // 2, 48, 144)
    sub = divisor(strip, 16, 48)
    low = jnp.bfloat16
    f32 = jnp.float32

    me_snap = lax.axis_index("snap")
    me_sp = lax.axis_index("sp")
    core = lax.rem(me_sp, 2)
    level = me_sp // 2

    def at(snap, sp):
        return {"snap": snap, "sp": sp}

    def sp_after(step):
        return lax.rem(me_sp + step, group)

    def sp_before(step):
        return lax.rem(me_sp + group - step, group)

    def snap_after(step):
        return lax.rem(me_snap + step, snaps)

    def snap_before(step):
        return lax.rem(me_snap + snaps - step, snaps)

    def level_after(step):
        return lax.rem(level + step, levels)

    def level_before(step):
        return lax.rem(level + levels - step, levels)

    other_core = at(me_snap, me_sp + 1 - 2 * core)

    def send(src, dst, sems, index, target):
        return pltpu.make_async_remote_copy(
            src_ref=src,
            dst_ref=dst,
            send_sem=sems[0].at[index],
            recv_sem=sems[1].at[index],
            device_id=target,
            device_id_type=pl.DeviceIdType.MESH,
        )

    half_tokens = tokens // 2

    def strips(body, first=0, count=tokens):
        @pl.loop(0, count // strip)
        def _(step):
            for at_row in range(0, strip, sub):
                body(pl.ds(pl.multiple_of(first + step * strip + at_row, 16), sub))

    def half_strips(body, part):
        strips(body, part * half_tokens, half_tokens)

    def half_rows(part):
        return slice(part * half_tokens, (part + 1) * half_tokens)

    def fold(value):
        return jnp.sum(value.reshape(-1, 8, value.shape[1]), axis=0)

    def columns(name):
        ref = getattr(g, name)
        return ref.reshape(tiles, ref.shape[1] * ref.shape[2], 128)

    def columns_of(name, rows):
        view = columns(name)
        return jnp.concatenate([view[tile_at, rows, :] for tile_at in range(tiles)], axis=1)

    def store_columns(name, rows, value):
        view = columns(name)
        for tile_at in range(tiles):
            view[tile_at, rows, :] = value[:, tile_at * 128 : (tile_at + 1) * 128]

    def column_copies(near, far, sems, out):
        copies = []
        for tile_at in range(tiles):
            ends = [near.at[tile_at], far.at[:, :, tile_at * 128 : (tile_at + 1) * 128]]
            if not out:
                ends.reverse()
            copies.append(pltpu.make_async_copy(*ends, sems.at[tile_at]))
        return copies

    loads = {}

    def load(name, index):
        copy = pltpu.make_async_copy(getattr(g, name), getattr(g, name + "_in"), g.load_sem.at[index])
        copy.start()
        loads[name] = copy

    for index, name in enumerate(
        [name for name in names[: names.index("out")] if name not in ("mlp", "fields", "cot")]
    ):
        load(name, index)
    fields_load = column_copies(g.fields_cols, g.fields, g.fields_sem, False)
    cot_load = column_copies(g.cot_cols, g.cot, g.cot_sem, False)
    for copy in fields_load + cot_load:
        copy.start()

    def master_load(part):
        return pltpu.make_async_copy(
            g.mlp.at[:, :, part * width : (part + 1) * width],
            g.mlp_part.at[part % 2],
            g.load_sem.at[len(loads) + part % 2],
        )

    master_load(0).start()
    master_load(1).start()

    barrier = pltpu.get_barrier_semaphore()
    peers = [at(me_snap, sp_after(step)) for step in range(1, group)]
    peers += [at(snap_after(step), me_sp) for step in range(1, snaps)]
    for peer in peers:
        pl.semaphore_signal(
            barrier, inc=1, device_id=peer, device_id_type=pl.DeviceIdType.MESH
        )

    loads["small"].wait()
    loads["kept"].wait()
    g.own_small[...] = jnp.zeros_like(g.own_small)
    rows_small = g.small.shape[0]
    g.own_small[0:rows_small, 0:owned] = g.small_in[...].astype(low).astype(f32)
    pairs_kept = g.kept.shape[1]
    lines = lax.broadcasted_iota(jnp.int32, (pairs_kept, pairs_kept), 0)
    places = lax.broadcasted_iota(jnp.int32, (pairs_kept, pairs_kept), 1)
    kept = jnp.where(lines == places, g.kept_in[...].astype(f32), 0.0)
    g.own_small[16:, :] = jnp.broadcast_to(
        jnp.sum(kept, axis=1, keepdims=True), (pairs_kept, g.own_small.shape[1])
    )
    pl.semaphore_wait(barrier, len(peers))

    def small_copy(step):
        return send(
            g.own_small, g.all_small.at[me_sp], (g.small_s, g.small_r), step, at(me_snap, sp_after(step))
        )

    for step in range(1, group):
        small_copy(step).start()
    g.all_small[me_sp] = g.own_small[...]

    snap_low = lax.rem(me_snap, 2)
    snap_high = me_snap // 2
    beside_low = me_snap + 1 - 2 * snap_low
    beside_high = me_snap + 2 - 4 * snap_high

    def own_quarter(part):
        odd = lax.rem(part, 2)
        return (1 - odd) * me_snap + odd * (2 * snap_low + snap_high)

    def half_quarters(part):
        return pl.ds(2 * (own_quarter(part) // 2), 2)

    def own_rows(sp):
        return pl.ds(pl.multiple_of(sp * owned, owned), owned)

    def first_copy(part, step):
        target = sp_after(step)
        matrix = lax.rem(target, 2)
        place = own_quarter(part)
        return send(
            g.own_w.at[part, matrix, place],
            g.all_w.at[part, matrix, place, own_rows(me_sp)],
            (g.first_s, g.first_r),
            (part, step),
            at(me_snap, target),
        )

    def first_local(part):
        place = own_quarter(part)
        return pltpu.make_async_copy(
            g.own_w.at[part, core, place],
            g.all_w.at[part, core, place, own_rows(me_sp)],
            g.first_s.at[part, 0],
        )

    def second_copy(part):
        odd = lax.rem(part, 2)
        view = g.all_w.at[part, core, own_quarter(part)]
        target = at((1 - odd) * beside_low + odd * beside_high, me_sp)
        return send(view, view, (g.second_s, g.second_r), part, target)

    def third_copy(part):
        odd = lax.rem(part, 2)
        view = g.all_w.at[part, core, half_quarters(part)]
        target = at((1 - odd) * beside_high + odd * beside_low, me_sp)
        return send(view, view, (g.third_s, g.third_r), part, target)

    def fourth_copy(part):
        view = g.all_w.at[part, core]
        return send(view, view, (g.fourth_s, g.fourth_r), part, other_core)

    def start_first(part):
        for step in range(1, group):
            first_copy(part, step).start()
        first_local(part).start()

    def pass_second(part):
        for step in range(1, group):
            first_copy(part, step).wait_recv()
        first_local(part).wait()
        second_copy(part).start()

    def pass_third(part):
        second_copy(part).wait_recv()
        third_copy(part).start()

    def pass_fourth(part):
        third_copy(part).wait_recv()
        fourth_copy(part).start()

    for part in range(parts):
        master_load(part).wait()
        for place in range(snaps):
            cols = slice(place * quarter, (place + 1) * quarter)
            g.own_w[part, :, place] = g.mlp_part[part % 2, :, :, cols].astype(low)
        if part + 2 < parts:
            master_load(part + 2).start()
        if part < 2:
            start_first(part)

    for copy in fields_load:
        copy.wait()

    def first_unit(rows):
        values = columns_of("fields_cols", rows).astype(f32)
        centred = values - jnp.mean(values, axis=-1, keepdims=True)
        scale = lax.rsqrt(jnp.mean(centred * centred, axis=-1, keepdims=True) + eps_norm)
        g.scale_one[rows, :] = scale
        g.grid[rows, :] = centred * scale

    strips(first_unit)
    for step in range(1, group):
        small_copy(step).wait_recv()
    for sp in range(group):
        g.gains[:, sp * owned : (sp + 1) * owned] = g.all_small[sp, 0:16, 0:owned]
        g.keep[sp * pairs_kept : (sp + 1) * pairs_kept, :] = g.all_small[sp, 16:, :]

    def first_norm(rows):
        unit = g.grid[rows, :]
        normed = unit * g.gains[0:1, :] + g.gains[1:2, :]
        g.unit_one[rows, :] = unit.astype(low)
        g.normed[rows, :] = normed.astype(low)
        g.grid[rows, :] = columns_of("fields_cols", rows).astype(f32) + normed

    half_snaps = g.arrived.shape[0] // 2

    def some_snaps(part):
        return pl.ds(part * half_snaps, half_snaps)

    def to_blocks(table, which, part):
        modes = dot_nn(table, g.normed[half_rows(part), :])
        for block in range(group):
            cut = modes[:, block * owned : (block + 1) * owned]
            cut = jnp.concatenate([cut, jnp.zeros((cut.shape[0], 128 - owned), f32)], axis=1)
            g.modes[part, block] = cut.astype(low).reshape(g.modes.shape[2:])
        for step in range(1, group):
            block_copy(which, part, step).start()
        g.arrived[some_snaps(part), mode_rows(me_sp), :] = g.modes[part, me_sp]

    def mode_rows(sp):
        size = g.modes.shape[3]
        return pl.ds(pl.multiple_of(sp * size, size), size)

    def block_copy(which, part, step):
        target = sp_after(step)
        return send(
            g.modes.at[part, target],
            g.arrived.at[some_snaps(part), mode_rows(me_sp), :],
            (g.block_s, g.block_r),
            (which, part, step),
            at(me_snap, target),
        )

    def row_copy(which, part, step):
        target = sp_after(step)
        return send(
            g.turned.at[some_snaps(part), mode_rows(target), :],
            g.home.at[part, me_sp],
            (g.row_s, g.row_r),
            (which, part, step),
            at(me_snap, target),
        )

    def to_rows(which, part):
        for step in range(1, group):
            row_copy(which, part, step).start()
        g.home[part, me_sp] = g.turned[some_snaps(part), mode_rows(me_sp), :]

    def home_modes(which, part):
        for step in range(1, group):
            row_copy(which, part, step).wait_recv()
        count = g.gathered.shape[1]
        for block in range(group):
            g.gathered[part, :, block * owned : (block + 1) * owned] = (
                g.home[part, block].reshape(count, 128)[:, 0:owned].astype(f32)
            )
        g.home_low[part] = g.gathered[part].astype(low)

    loads["lon_f"].wait()
    for part in range(2):
        half_strips(first_norm, part)
        to_blocks(g.lon_f_in[...], 0, part)
        pass_second(part)

    loads["filt"].wait()
    for weight, first in ((g.weight_one, 0), (g.weight_two, 2)):
        weight[...] = jnp.zeros_like(weight)
        real = g.filt_in[first].astype(low)
        imag = g.filt_in[first + 1].astype(low)
        weight[0:owned, 0:owned] = real
        weight[128 : 128 + owned, 128 : 128 + owned] = real
        weight[0:owned, 128 : 128 + owned] = imag
        weight[128 : 128 + owned, 0:owned] = -imag

    def bias_row(first):
        return jnp.concatenate(
            [g.own_small[first : first + 1, :], g.own_small[first + 1 : first + 2, :]], axis=1
        )

    for copy in cot_load:
        copy.wait()

    def flat_cot(rows):
        g.cot_in[rows, :] = columns_of("cot_cols", rows)

    strips(flat_cot)
    pass_third(0)
    loads["lat_f"].wait()
    loads["lat_b"].wait()
    pairs = g.arrived.shape[1] // 2
    half_modes = half_snaps * pairs

    def mode_half(part):
        return slice(part * half_modes, (part + 1) * half_modes)

    def spectra(out, kind, part):
        for snap in range(part * half_snaps, (part + 1) * half_snaps):
            spectrum = dot_nn(g.lat_f_in[...], g.arrived[snap]).astype(kind)
            rows = slice(snap * pairs, (snap + 1) * pairs)
            out[rows, 0:128] = spectrum[0:pairs]
            out[rows, 128:256] = spectrum[pairs:]

    def grids(values, part):
        for index in range(half_snaps):
            rows = values[index * pairs : (index + 1) * pairs]
            rows = jnp.concatenate([rows[:, 0:128], rows[:, 128:256]], axis=0)
            g.turned[part * half_snaps + index] = dot_nn(g.lat_b_in[...], rows).astype(low)

    def keep_half():
        keep = jnp.concatenate([g.keep[...], g.keep[...]], axis=1)
        return jnp.concatenate([keep] * half_snaps, axis=0)

    for part in range(2):
        for step in range(1, group):
            block_copy(0, part, step).wait_recv()
        rows = mode_half(part)
        spectra(g.spectrum, low, part)
        g.pre_one[rows, :] = dot_nn(g.spectrum[rows, :], g.weight_one[...]) + bias_row(4)
        g.act_one[rows, :] = gelu_both(g.pre_one[rows, :])[0].astype(low)
        g.pre_two[rows, :] = dot_nn(g.act_one[rows, :], g.weight_two[...]) + bias_row(6)
        grids((shrink(g.pre_two[rows, :]) * keep_half()).astype(low), part)
        to_rows(0, part)
    pass_third(1)
    for part in range(2, 4):
        start_first(part)
    g.cot_turned[...] = g.cot_in[...].T

    loads["lon_i"].wait()

    def second_norm(rows):
        values = g.grid[rows, :]
        centred = values - jnp.mean(values, axis=-1, keepdims=True)
        scale = lax.rsqrt(jnp.mean(centred * centred, axis=-1, keepdims=True) + eps_norm)
        centred = centred * scale
        g.unit_two[rows, :] = centred.astype(low)
        g.scale_two[rows, :] = scale
        g.normed[rows, :] = (centred * g.gains[2:3, :] + g.gains[3:4, :]).astype(low)
        g.grid[rows, :] = values + g.gains[8:9, :]
        g.back[rows, :] = jnp.zeros((sub, channel), f32)

    for part in range(2):
        home_modes(0, part)
        g.grid[half_rows(part), :] += dot_nn(g.lon_i_in[...], g.home_low[part])
        half_strips(second_norm, part)
    pass_fourth(0)
    for part in range(4, parts):
        start_first(part)
    g.normed_turned[...] = g.normed[...].T
    pass_fourth(1)
    pass_second(2)
    flat = jnp.concatenate([g.gains[9 + row : 10 + row, :] for row in range(rows_small - 9)], axis=1)
    for part in range(parts):
        g.bias[part] = flat[:, part * width : (part + 1) * width]

    def core_copy(part, matrix):
        slot = lax.rem(part, 2)
        return send(
            g.grads.at[matrix, :, 1 - core],
            g.core_got.at[slot, matrix],
            (g.core_s, g.core_r),
            (slot, matrix),
            other_core,
        )

    places_one = (snap_low, snap_high)
    places_two = (snap_high, snap_low)
    beside_one = (beside_low, beside_high)
    beside_two = (beside_high, beside_low)
    place_last = (2 * snap_low + snap_high, me_snap)

    def half_copy(part, matrix):
        slot = lax.rem(part, 2)
        place = lax.rem(part, 4)
        return send(
            g.half_out.at[slot, matrix, 1 - places_one[matrix]],
            g.half_got.at[place, matrix],
            (g.half_s, g.half_r),
            (place, matrix),
            at(beside_one[matrix], me_sp),
        )

    def quarter_copy(part, matrix):
        slot = lax.rem(part, 2)
        return send(
            g.quarter_out.at[slot, matrix, 1 - places_two[matrix]],
            g.quarter_got.at[slot, matrix],
            (g.quarter_s, g.quarter_r),
            (slot, matrix),
            at(beside_two[matrix], me_sp),
        )

    def level_copy(part, step):
        slot = lax.rem(part, 2)
        place = lax.rem(part, 4)
        target = level_after(step)
        return send(
            g.level_out.at[slot, target],
            g.level_got.at[place, level],
            (g.level_s, g.level_r),
            (place, step),
            at(me_snap, 2 * target + core),
        )

    def last_copy(part, matrix, step):
        view = g.total.at[part, place_last[matrix], matrix]
        return send(
            view, view, (g.last_s, g.last_r), (part, matrix, step), at(snap_after(step), me_sp)
        )

    def half_stage(part):
        slot = lax.rem(part, 2)
        for matrix in range(2):

            @pl.when(part >= 2)
            def _(matrix=matrix):
                half_copy(part - 2, matrix).wait_send()

            core_copy(part, matrix).wait_recv()
            for row in range(levels):
                both = g.grads[matrix, row, core].astype(f32) + g.core_got[
                    slot, matrix, row
                ].astype(f32)
                both = both.astype(low)
                g.half_out[slot, matrix, 0, row] = both[:, 0:half]
                g.half_out[slot, matrix, 1, row] = both[:, half:width]
            half_copy(part, matrix).start()

    def quarter_stage(part):
        slot = lax.rem(part, 2)
        for matrix in range(2):

            @pl.when(part >= 2)
            def _(matrix=matrix):
                quarter_copy(part - 2, matrix).wait_send()

            half_copy(part, matrix).wait_recv()
            for row in range(levels):
                both = g.half_out[slot, matrix, places_one[matrix], row].astype(f32) + g.half_got[
                    lax.rem(part, 4), matrix, row
                ].astype(f32)
                both = both.astype(low)
                g.quarter_out[slot, matrix, 0, row] = both[:, 0:quarter]
                g.quarter_out[slot, matrix, 1, row] = both[:, quarter:half]
            quarter_copy(part, matrix).start()

    def level_stage(part):
        slot = lax.rem(part, 2)

        @pl.when(part >= 2)
        def _():
            for step in range(1, levels):
                level_copy(part - 2, step).wait_send()

        for matrix in range(2):
            quarter_copy(part, matrix).wait_recv()
            for row in range(levels):
                both = g.quarter_out[slot, matrix, places_two[matrix], row].astype(
                    f32
                ) + g.quarter_got[slot, matrix, row].astype(f32)
                g.level_out[slot, row, matrix] = both.astype(low)
        for step in range(1, levels):
            level_copy(part, step).start()

    def last_stage(part):
        slot = lax.rem(part, 2)
        for step in range(1, levels):
            level_copy(part, step).wait_recv()
        for matrix in range(2):
            sums = g.level_out[slot, level, matrix].astype(f32)
            for step in range(1, levels):
                sums += g.level_got[lax.rem(part, 4), level_before(step), matrix].astype(f32)
            g.total[part, place_last[matrix], matrix] = sums.astype(low)
            for step in range(1, snaps):
                last_copy(part, matrix, step).start()

    def weight(part, matrix):
        return jnp.concatenate([g.all_w[part, matrix, place] for place in range(snaps)], axis=1)

    @pl.loop(0, parts)
    def _(part):
        slot = lax.rem(part, 2)
        def when(condition, stage, *arguments):
            pl.when(condition)(functools.partial(stage, *arguments))

        fourth_copy(part).wait_recv()
        when(part >= 3, quarter_stage, part - 3)
        when(part == 4, pass_fourth, 5)
        when(part == 1, pass_third, 3)
        when(part == 1, pass_second, 5)
        g.grad_bias[part] = jnp.zeros(g.grad_bias.shape[1:], f32)

        @pl.loop(0, tokens // tile)
        def _(step):
            rows = pl.ds(pl.multiple_of(step * tile, tile), tile)
            act, slope = gelu_both(dot_nn(g.normed[rows, :], weight(part, 0)) + g.bias[part])
            act = act.astype(low)
            slope = (dot_nn(g.cot_in[rows, :], weight(part, 1)) * slope).astype(low)
            g.act[rows, :] = act
            g.slope[rows, :] = slope
            g.grad_bias[part] += fold(slope.astype(f32))
            g.grid[rows, :] += dot_nt(act, weight(part, 1))
            g.back[rows, :] += dot_nt(slope, weight(part, 0))

            @pl.when(step == 0)
            def _():
                when(part == 0, pass_second, 3)
                when(part == 1, pass_third, 4)
                when(part == 2, pass_fourth, 3)
                when(part == 2, pass_third, 5)
                when(part == 3, pass_fourth, 4)

            @pl.when(step == 1)
            def _():
                when(part >= 1, half_stage, part - 1)

            @pl.when(step == 2)
            def _():
                when(part == 0, pass_third, 2)

        when(part == 5, last_stage, 0)
        when(part >= 3, level_stage, part - 3)
        when(part == 5, quarter_stage, 3)
        when(part == 0, pass_second, 4)
        when(part == 1, pass_fourth, 2)

        @pl.when(part >= 1)
        def _():
            for matrix in range(2):
                core_copy(part - 1, matrix).wait_send()

        shape = g.grads.shape[1:]
        g.grads[0] = dot_nn(g.normed_turned[...], g.slope[...]).astype(low).reshape(shape)
        core_copy(part, 0).start()
        g.grads[1] = dot_nn(g.cot_turned[...], g.act[...]).astype(low).reshape(shape)
        core_copy(part, 1).start()

    g.folds[...] = jnp.zeros_like(g.folds)

    def second_back(rows):
        grad = g.back[rows, :]
        unit = g.unit_two[rows, :].astype(f32)
        cot = g.cot_in[rows, :].astype(f32)
        pulled = grad * g.gains[2:3, :]
        middle = jnp.mean(pulled, axis=-1, keepdims=True)
        slant = jnp.mean(pulled * unit, axis=-1, keepdims=True)
        total = cot + g.scale_two[rows, :] * (pulled - middle - unit * slant)
        g.back[rows, :] = total
        g.normed[rows, :] = total.astype(low)
        g.folds[2] += fold(grad * unit)
        g.folds[3] += fold(grad)
        g.folds[4] += fold(cot)

    loads["lon_it"].wait()
    for part in range(2):
        half_strips(second_back, part)
        for step in range(1, group):
            block_copy(0, part, step).wait_send()
        to_blocks(g.lon_it_in[...], 1, part)
        if part == 0:
            half_stage(parts - 1)
    last_stage(parts - 5)
    level_stage(parts - 3)
    quarter_stage(parts - 2)

    def low_out(rows):
        store_columns("fields_cols", rows, g.grid[rows, :].astype(low))

    strips(low_out)
    out_copies = column_copies(g.fields_cols, g.out, g.fields_sem, True)
    for copy in out_copies:
        copy.start()
    loads["valid"].wait()
    loads["turn"].wait()
    weigh = sum(
        dot_nn(g.valid_in[:, row, :].astype(f32).astype(low), g.turn_in[row])
        for row in range(g.valid.shape[1])
    )
    places_each = weigh.shape[1]
    precise = lax.Precision.HIGHEST
    sums = [jnp.zeros((1, 128), f32), jnp.zeros((1, 128), f32)]
    for snap in range(g.valid.shape[0]):
        variables = g.grid[snap * places_each : (snap + 1) * places_each, 0:128]
        for index, value in enumerate((variables, variables * variables)):
            sums[index] += jnp.dot(
                weigh[snap : snap + 1, :], value, precision=precise, preferred_element_type=f32
            )

    last_stage(parts - 4)

    def dot_tn(left, right):
        return lax.dot_general(
            left, right, (((0,), (0,)), ((), ())), preferred_element_type=f32
        )

    def filter_rows(first, grad):
        g.pair_grad[...] = grad
        real = g.pair_grad[0:128, 0:128] + g.pair_grad[128:256, 128:256]
        imag = g.pair_grad[0:128, 128:256] - g.pair_grad[128:256, 0:128]
        g.filt_out[me_snap, first] = real[0:owned].astype(low)
        g.filt_out[me_snap, first + 1] = imag[0:owned].astype(low)

    for part in range(2):
        for step in range(1, group):
            block_copy(1, part, step).wait_recv()
        rows = mode_half(part)
        spectra(g.grad_pre, f32, part)
        bend = jnp.tanh(g.pre_two[rows, :] / shrink_level)
        grad = (g.grad_pre[rows, :] * keep_half() * (bend * bend)).astype(low)
        g.grad_two[rows, :] = grad
        grad = dot_nt(grad, g.weight_two[...]) * gelu_both(g.pre_one[rows, :])[1]
        grad = grad.astype(low)
        g.grad_one[rows, :] = grad
        for step in range(1, group):
            row_copy(0, part, step).wait_send()
        grids(dot_nt(grad, g.weight_one[...]).astype(low), part)
        to_rows(1, part)
        if part == 0:
            level_stage(parts - 2)
            quarter_stage(parts - 1)
    last_stage(parts - 3)
    bias_one = jnp.sum(g.grad_one[...].astype(f32), axis=0, keepdims=True)
    bias_two = jnp.sum(g.grad_two[...].astype(f32), axis=0, keepdims=True)
    filter_rows(2, dot_tn(g.act_one[...], g.grad_two[...]))
    filter_rows(0, dot_tn(g.spectrum[...], g.grad_one[...]))

    def filter_copy(step):
        view = g.filt_out.at[me_snap]
        return send(view, view, (g.filt_s, g.filt_r), step, at(snap_after(step), me_sp))

    for step in range(1, snaps):
        filter_copy(step).start()


    loads["lon_ft"].wait()
    strip_pairs = strip // g.fields.shape[1]
    grad_view = g.grad_cols.reshape(2, tiles, strip, 128)

    def grad_copies(place, slot):
        pairs_out = pl.ds(place * strip_pairs, strip_pairs)
        return column_copies(
            g.grad_cols.at[slot], g.in_grad.at[pairs_out], g.grad_sem.at[slot], True
        )

    steps = half_tokens // strip
    for part in range(2):
        home_modes(1, part)
        if part == 0:
            level_stage(parts - 1)
        else:
            last_stage(parts - 2)
        g.grid[half_rows(part), :] = g.back[half_rows(part), :] + dot_nn(
            g.lon_ft_in[...], g.home_low[part]
        )

        @pl.loop(0, steps)
        def _(step):
            place = part * steps + step
            slot = lax.rem(place, 2)

            @pl.when(place >= 2)
            def _():
                for copy in grad_copies(place, slot):
                    copy.wait()

            for at_row in range(0, strip, sub):
                rows = pl.ds(pl.multiple_of(place * strip + at_row, 16), sub)
                grad = g.grid[rows, :]
                unit = g.unit_one[rows, :].astype(f32)
                pulled = grad * g.gains[0:1, :]
                middle = jnp.mean(pulled, axis=-1, keepdims=True)
                slant = jnp.mean(pulled * unit, axis=-1, keepdims=True)
                total = g.back[rows, :] + g.scale_one[rows, :] * (pulled - middle - unit * slant)
                for tile_at in range(tiles):
                    grad_view[slot, tile_at, at_row : at_row + sub, :] = total[
                        :, tile_at * 128 : (tile_at + 1) * 128
                    ]
                g.folds[0] += fold(grad * unit)
                g.folds[1] += fold(grad)
            for copy in grad_copies(place, slot):
                copy.start()

    g.grad_rows[...] = jnp.zeros_like(g.grad_rows)
    for index, row in enumerate((0, 1, 2, 3, 8)):
        g.grad_rows[row : row + 1, :] = jnp.sum(g.folds[index], axis=0, keepdims=True)
    flat = jnp.concatenate(
        [jnp.sum(g.grad_bias[part], axis=0, keepdims=True) for part in range(parts)], axis=1
    )
    for row in range(rows_small - 9):
        g.grad_rows[9 + row : 10 + row, :] = flat[:, row * channel : (row + 1) * channel]
    for block in range(group):
        g.tiles[block] = jnp.zeros(g.tiles.shape[1:], f32)
        g.tiles[block, :, 0:owned] = g.grad_rows[:, block * owned : (block + 1) * owned]
        g.tiles[block, 13:14, :] = sums[0]
        g.tiles[block, 14:15, :] = sums[1]

    def tile_copy(step):
        target = sp_after(step)
        return send(
            g.tiles.at[target], g.tiles_got.at[me_sp], (g.tile_s, g.tile_r), step, at(me_snap, target)
        )

    def snap_tile_copy(step):
        view = g.snap_tiles.at[me_snap]
        return send(view, view, (g.snap_tile_s, g.snap_tile_r), step, at(snap_after(step), me_sp))

    for step in range(1, group):
        tile_copy(step).start()
    last_stage(parts - 1)

    g.tiles_got[me_sp] = g.tiles[me_sp]
    for step in range(1, group):
        tile_copy(step).wait_recv()
    tile_sum = g.tiles_got[0]
    for sp in range(1, group):
        tile_sum += g.tiles_got[sp]
    g.snap_tiles[me_snap] = tile_sum
    g.snap_tiles[me_snap, 4:5, :] = bias_one[:, 0:128]
    g.snap_tiles[me_snap, 5:6, :] = bias_one[:, 128:256]
    g.snap_tiles[me_snap, 6:7, :] = bias_two[:, 0:128]
    g.snap_tiles[me_snap, 7:8, :] = bias_two[:, 128:256]
    for step in range(1, snaps):
        snap_tile_copy(step).start()

    for step in range(1, snaps):
        filter_copy(step).wait_recv()
    filter_sum = g.filt_out[0].astype(f32)
    for snap in range(1, snaps):
        filter_sum += g.filt_out[snap].astype(f32)
    g.grad_filt[...] = filter_sum
    for part in range(parts):
        for matrix in range(2):
            for step in range(1, snaps):
                last_copy(part, matrix, step).wait_recv()
    grads_out = pltpu.make_async_copy(g.total, g.grad_mlp, g.load_sem.at[3])
    grads_out.start()
    for step in range(1, snaps):
        snap_tile_copy(step).wait_recv()
    tile_sum = g.snap_tiles[0]
    for snap in range(1, snaps):
        tile_sum += g.snap_tiles[snap]
    g.grad_small[...] = tile_sum

    grads_out.wait()
    for copy in out_copies:
        copy.wait()
    for slot in range(2):
        for copy in grad_copies(0, slot):
            copy.wait()
    for step in range(1, group):
        small_copy(step).wait_send()
        for part in range(2):
            block_copy(1, part, step).wait_send()
            row_copy(1, part, step).wait_send()
        tile_copy(step).wait_send()
        for part in range(parts):
            first_copy(part, step).wait_send()
    for part in range(parts):
        second_copy(part).wait_send()
        third_copy(part).wait_send()
        fourth_copy(part).wait_send()
    for matrix in range(2):
        core_copy(parts - 1, matrix).wait_send()
    for part in (parts - 2, parts - 1):
        for matrix in range(2):
            half_copy(part, matrix).wait_send()
            quarter_copy(part, matrix).wait_send()
        for step in range(1, levels):
            level_copy(part, step).wait_send()
    for step in range(1, snaps):
        filter_copy(step).wait_send()
        snap_tile_copy(step).wait_send()
        for part in range(parts):
            for matrix in range(2):
                last_copy(part, matrix, step).wait_send()


def block_pass(fields, cot, valid, kept, mlp, filt, small, snaps, group):
    snap_local, row_local, lon_total, channel = fields.shape
    tokens = snap_local * row_local * lon_total
    hidden = mlp.shape[2]
    lat_total = row_local * group
    modes = kept.shape[1] * group
    owned = channel // group
    width = 512
    parts = hidden // width
    levels = group // 2
    quarter = width // snaps
    low, f32 = jnp.bfloat16, jnp.float32
    half = width // 2
    half_snaps = snap_local // 2
    lon_f, lon_i = lon_matrix(lon_total, modes, half_snaps, row_local)

    def paired(array):
        return jnp.transpose(array, (0, 2, 1, 3)).reshape(-1, row_local, channel)

    lat_f = lat_matrix(lat_total, modes)
    pair = 2 * modes * row_local
    spread = half_snaps * row_local * 2 * modes
    inputs = dict(
        small=small,
        kept=kept.T,
        fields=paired(fields),
        lon_f=jnp.asarray(np.ascontiguousarray(lon_f.T)),
        filt=filt,
        lat_f=jnp.asarray(lat_f),
        lat_b=jnp.asarray(np.ascontiguousarray(lat_f.T)),
        cot=paired(cot),
        lon_i=jnp.asarray(lon_i),
        valid=valid,
        turn=jnp.asarray(lon_turn(lon_total, row_local)),
        lon_it=jnp.asarray(np.ascontiguousarray(lon_i.T)),
        lon_ft=jnp.asarray(lon_f),
        mlp=mlp,
    )
    outputs = dict(
        out=jax.ShapeDtypeStruct((tokens // row_local, row_local, channel), low),
        in_grad=jax.ShapeDtypeStruct((tokens // row_local, row_local, channel), f32),
        grad_mlp=jax.ShapeDtypeStruct((parts, snaps, 2, owned, quarter), low),
        grad_filt=jax.ShapeDtypeStruct((4, owned, 128), f32),
        grad_small=jax.ShapeDtypeStruct((16, 128), f32),
    )
    vmem = pltpu.VMEM
    dma = pltpu.SemaphoreType.DMA
    scratch = {
        name + "_in": vmem(value.shape, value.dtype)
        for name, value in inputs.items()
        if name not in ("mlp", "fields", "cot")
    }
    tiles = channel // 128
    cols = (tiles, tokens // row_local, row_local, 128)
    strip = divisor(tokens // 2, 48, 144)
    scratch |= dict(
        mlp_part=vmem((2, 2, owned, width), f32),
        fields_cols=vmem(cols, low),
        cot_cols=vmem(cols, low),
        grad_cols=vmem((2, tiles, strip // row_local, row_local, 128), f32),
        grad_sem=dma((2, tiles)),
        fields_sem=dma((tiles,)),
        cot_sem=dma((tiles,)),
        cot_in=vmem((tokens, channel), low),
        grid=vmem((tokens, channel), f32),
        back=vmem((tokens, channel), f32),
        normed=vmem((tokens, channel), low),
        normed_turned=vmem((channel, tokens), low),
        cot_turned=vmem((channel, tokens), low),
        unit_one=vmem((tokens, channel), low),
        unit_two=vmem((tokens, channel), low),
        scale_one=vmem((tokens, 1), f32),
        scale_two=vmem((tokens, 1), f32),
        own_small=vmem((16 + kept.shape[0], 128), f32),
        all_small=vmem((group, 16 + kept.shape[0], 128), f32),
        gains=vmem((16, channel), f32),
        keep=vmem((lat_total * modes, 128), f32),
        own_w=vmem((parts, 2, snaps, owned, quarter), low),
        all_w=vmem((parts, 2, snaps, channel, quarter), low),
        modes=vmem((2, group, half_snaps, pair, 128), low),
        arrived=vmem((snap_local, pair * group, 128), low),
        turned=vmem((snap_local, pair * group, 128), low),
        home=vmem((2, group, half_snaps, pair, 128), low),
        gathered=vmem((2, spread, channel), f32),
        home_low=vmem((2, spread, channel), low),
        weight_one=vmem((256, 256), low),
        weight_two=vmem((256, 256), low),
        spectrum=vmem((snap_local * lat_total * modes, 256), low),
        pre_one=vmem((snap_local * lat_total * modes, 256), f32),
        act_one=vmem((snap_local * lat_total * modes, 256), low),
        pre_two=vmem((snap_local * lat_total * modes, 256), f32),
        grad_pre=vmem((snap_local * lat_total * modes, 256), f32),
        grad_two=vmem((snap_local * lat_total * modes, 256), low),
        grad_one=vmem((snap_local * lat_total * modes, 256), low),
        folds=vmem((5, 8, channel), f32),
        pair_grad=vmem((256, 256), f32),
        act=vmem((tokens, width), low),
        slope=vmem((tokens, width), low),
        bias=vmem((parts, 1, width), f32),
        grad_bias=vmem((parts, 8, width), f32),
        grad_rows=vmem((16, channel), f32),
        grads=vmem((2, levels, 2, owned, width), low),
        core_got=vmem((2, 2, levels, owned, width), low),
        half_out=vmem((2, 2, 2, levels, owned, half), low),
        half_got=vmem((4, 2, levels, owned, half), low),
        quarter_out=vmem((2, 2, 2, levels, owned, quarter), low),
        quarter_got=vmem((2, 2, levels, owned, quarter), low),
        level_out=vmem((2, levels, 2, owned, quarter), low),
        level_got=vmem((4, levels, 2, owned, quarter), low),
        total=vmem((parts, snaps, 2, owned, quarter), low),
        filt_out=vmem((snaps, 4, owned, 128), low),
        tiles=vmem((group, 16, 128), f32),
        tiles_got=vmem((group, 16, 128), f32),
        snap_tiles=vmem((snaps, 16, 128), f32),
        load_sem=dma((len(inputs) + 1,)),
    )
    for name, shape in dict(
        small=(group,),
        first=(parts, group),
        second=(parts,),
        third=(parts,),
        fourth=(parts,),
        block=(2, 2, group),
        row=(2, 2, group),
        core=(2, 2),
        half=(4, 2),
        quarter=(2, 2),
        level=(4, levels),
        last=(parts, 2, snaps),
        filt=(snaps,),
        tile=(group,),
        snap_tile=(snaps,),
    ).items():
        scratch[name + "_s"] = dma(shape)
        scratch[name + "_r"] = dma(shape)
    names = [*inputs, *outputs, *scratch]
    far = pl.BlockSpec(memory_space=pl.ANY)
    near = pl.BlockSpec(memory_space=pltpu.VMEM)
    results = pl.pallas_call(
        functools.partial(block_body, names, (snaps, group, parts, width)),
        in_specs=[far] * len(inputs),
        out_specs=[far, far, far, near, near],
        out_shape=list(outputs.values()),
        scratch_shapes=list(scratch.values()),
        compiler_params=pltpu.CompilerParams(
            collective_id=0, has_side_effects=True, vmem_limit_bytes=VMEM_LIMIT
        ),
        cost_estimate=pl.CostEstimate(
            flops=12 * tokens * channel * hidden,
            bytes_accessed=4 * hidden * channel,
            transcendentals=tokens * hidden,
        ),
        name="block_pass",
    )(*inputs.values())
    return results


def step_body(names, positions, *refs):
    g = Refs()
    for name, ref in zip(names, refs, strict=True):
        setattr(g, name, ref)
    parts, snaps = g.grad_mlp.shape[:2]
    quarter = g.grad_mlp.shape[4]
    width = snaps * quarter
    moments = ("w", "m", "v")
    results = ("new", "first", "second", "copy")

    pieces = g.far_sem.shape[2]
    ends = ((g.out, g.out_near, g.out_o), (g.in_grad, g.in_grad_near, g.in_grad_o))

    def passing(kind, piece, leg):
        size = ends[kind][0].shape[0] // pieces
        rows = pl.ds(piece * size, size)
        return pltpu.make_async_copy(
            ends[kind][leg].at[rows], ends[kind][leg + 1].at[rows], g.far_sem.at[leg, kind, piece]
        )

    through = [(kind, piece) for kind in range(2) for piece in range(pieces)]

    def part_cols(part):
        return pl.ds(part * width, width)

    def load(part):
        near = [
            pltpu.make_async_copy(
                getattr(g, "mlp_" + kind).at[:, :, part_cols(part)],
                g.near.at[index, part],
                g.near_sem.at[index, part],
            )
            for index, kind in enumerate(moments)
        ]
        near.append(
            pltpu.make_async_copy(g.grad_mlp.at[part], g.grad_near.at[part], g.near_sem.at[3, part])
        )
        return near

    def store(part):
        copies = [
            pltpu.make_async_copy(
                g.near.at[index, part],
                getattr(g, "mlp_" + kind).at[:, :, part_cols(part)],
                g.back_sem.at[index, part],
            )
            for index, kind in enumerate(results[:3])
        ]
        copies.append(
            pltpu.make_async_copy(
                g.low_near.at[part], g.mlp_copy.at[:, :, part_cols(part)], g.back_sem.at[3, part]
            )
        )
        return copies

    coming = [load(part) for part in range(parts)]
    going = [store(part) for part in range(parts)]
    shares = [through[part::parts] for part in range(parts)]
    for part in range(parts):
        for copy in coming[part]:
            copy.start()
        for each in shares[part]:
            passing(*each, 0).start()

    def put(prefix, values):
        for kind, value in zip(results, values, strict=True):
            getattr(g, prefix + kind)[...] = value

    owned = g.filt_w.shape[2]
    put(
        "filt_",
        adamw(g.filt_w[...], g.filt_m[...], g.filt_v[...], g.grad_filt[:, :, 0:owned], rate_filter),
    )
    rows = g.small_w.shape[0]
    put(
        "small_",
        adamw(
            g.small_w[...], g.small_m[...], g.small_v[...], g.grad_small[0:rows, 0:owned], rate_small
        ),
    )
    totals = g.grad_small[rows : rows + 2, 0 : g.run.shape[1]]
    g.stats[...] = stat_decay * g.run[...] + (1.0 - stat_decay) * totals / positions

    for part in range(parts):
        for copy in coming[part]:
            copy.wait()

        for snap in range(snaps):
            cols = slice(snap * quarter, (snap + 1) * quarter)
            where = (slice(None), slice(None), cols)
            now = [g.near[(index, part, *where)] for index in range(3)]
            grad = g.grad_near[part, snap].astype(jnp.float32)
            values = adamw(*now, grad, rate_mlp)
            for index in range(3):
                g.near[(index, part, *where)] = values[index]
            g.low_near[(part, *where)] = values[3]
        for copy in going[part]:
            copy.start()
        for each in shares[part]:
            passing(*each, 0).wait()
            passing(*each, 1).start()
    for each in through:
        passing(*each, 1).wait()
    for part in range(parts):
        for copy in going[part]:
            copy.wait()


def step_pass(shown, grads, masters, run_stats, positions):
    grad_mlp, grad_filt, grad_small = grads
    mlp, filt, small = masters
    parts = grad_mlp.shape[0]
    width = mlp[0].shape[2] // parts
    f32, low = jnp.float32, jnp.bfloat16
    far = pl.BlockSpec(memory_space=pltpu.HBM)
    near = pl.BlockSpec(memory_space=pltpu.VMEM)
    inputs = dict(out=shown[0], in_grad=shown[1], grad_mlp=grad_mlp)
    inputs |= dict(zip(("mlp_w", "mlp_m", "mlp_v"), mlp, strict=True))
    far_in = len(inputs)
    inputs |= dict(grad_filt=grad_filt, grad_small=grad_small)
    inputs |= dict(zip(("filt_w", "filt_m", "filt_v"), filt, strict=True))
    inputs |= dict(zip(("small_w", "small_m", "small_v"), small, strict=True))
    inputs |= dict(run=run_stats)
    results = (("new", f32), ("first", f32), ("second", f32), ("copy", low))
    outputs = {
        name + "_o": jax.ShapeDtypeStruct(array.shape, array.dtype)
        for name, array in zip(("out", "in_grad"), shown, strict=True)
    }
    outputs |= {"mlp_" + kind: jax.ShapeDtypeStruct(mlp[0].shape, dt) for kind, dt in results}
    far_out = len(outputs)
    outputs |= {"filt_" + kind: jax.ShapeDtypeStruct(filt[0].shape, dt) for kind, dt in results}
    outputs |= {"small_" + kind: jax.ShapeDtypeStruct(small[0].shape, dt) for kind, dt in results}
    outputs |= dict(stats=jax.ShapeDtypeStruct(run_stats.shape, f32))
    scratch = dict(
        near=pltpu.VMEM((3, parts, 2, mlp[0].shape[1], width), f32),
        grad_near=pltpu.VMEM(grad_mlp.shape, low),
        low_near=pltpu.VMEM((parts, 2, mlp[0].shape[1], width), low),
        near_sem=pltpu.SemaphoreType.DMA((4, parts)),
        back_sem=pltpu.SemaphoreType.DMA((4, parts)),
        out_near=pltpu.VMEM(shown[0].shape, low),
        in_grad_near=pltpu.VMEM(shown[1].shape, f32),
        far_sem=pltpu.SemaphoreType.DMA((2, 2, divisor(shown[0].shape[0], 1, 4))),
    )
    return pl.pallas_call(
        functools.partial(step_body, [*inputs, *outputs, *scratch], positions),
        in_specs=[far] * far_in + [near] * (len(inputs) - far_in),
        out_specs=[far] * far_out + [near] * (len(outputs) - far_out),
        out_shape=list(outputs.values()),
        scratch_shapes=list(scratch.values()),
        compiler_params=pltpu.CompilerParams(vmem_limit_bytes=VMEM_LIMIT),
        name="step_pass",
    )(*inputs.values())


def per_device_blocks(
    fields,
    cotangent,
    valid_mask,
    kept_modes,
    mlp_master,
    mlp_first,
    mlp_second,
    filter_master,
    filter_first,
    filter_second,
    small_master,
    small_first,
    small_second,
    run_stats,
):
    snaps, group = lax.axis_size("snap"), lax.axis_size("sp")
    out, in_grad, *grads = block_pass(
        fields, cotangent, valid_mask, kept_modes, mlp_master, filter_master, small_master, snaps, group
    )
    snap_local, row_local, lon_total, channel = fields.shape
    positions = snap_local * snaps * row_local * group * lon_total
    out, in_grad, *stepped = step_pass(
        (out, in_grad),
        grads,
        (
            (mlp_master, mlp_first, mlp_second),
            (filter_master, filter_first, filter_second),
            (small_master, small_first, small_second),
        ),
        run_stats,
        positions,
    )
    rows_apart = (snap_local, lon_total, row_local, channel)
    out, in_grad = [
        jnp.transpose(array.reshape(rows_apart), (0, 2, 1, 3)) for array in (out, in_grad)
    ]
    return (out, in_grad, *stepped)


def per_device(*arrays):
    group, snaps = lax.axis_size("sp"), lax.axis_size("snap")
    channel, hidden = arrays[0].shape[3], arrays[4].shape[2]
    by_block = group == BLOCKS and snaps == 4 and arrays[3].shape[1] == 1
    if by_block and hidden == 6 * 512 and channel // group <= 128 and channel % (16 * group) == 0:
        return per_device_blocks(*arrays)
    return per_device_modes(*arrays)


def solution(mesh):
    return jax.shard_map(
        per_device,
        mesh=mesh,
        in_specs=(
            P("snap", "sp", None, None),
            P("snap", "sp", None, None),
            P("snap", "sp", None),
            P(None, "sp"),
            P(None, "sp", None),
            P(None, "sp", None),
            P(None, "sp", None),
            P(None, "sp", None),
            P(None, "sp", None),
            P(None, "sp", None),
            P(None, "sp"),
            P(None, "sp"),
            P(None, "sp"),
            P(),
        ),
        out_specs=(
            P("snap", "sp", None, None),
            P("snap", "sp", None, None),
            P(None, "sp", None),
            P(None, "sp", None),
            P(None, "sp", None),
            P(None, "sp", None),
            P(None, "sp", None),
            P(None, "sp", None),
            P(None, "sp", None),
            P(None, "sp", None),
            P(None, "sp"),
            P(None, "sp"),
            P(None, "sp"),
            P(None, "sp"),
            P(),
        ),
        check_vma=False,
    )
```

```python
import functools
import math

import jax
import jax.numpy as jnp
import ml_dtypes
import numpy as np
from jax import lax
from jax.experimental import pallas as pl
from jax.experimental.pallas import tpu as pltpu
from jax.sharding import PartitionSpec as P

BLOCKS = 8
NVAR = 20
STEP = 10
VMEM_LIMIT = 63 * 1024 * 1024


eps_norm = 1e-06
shrink_level = 0.01
beta_one = 0.5
beta_two = 0.5
adam_eps = 1e-08
decay_rate = 0.01
rate_mlp = 0.03
rate_filter = 0.1
rate_small = 0.2
stat_decay = 0.5


def layer_norm(values, gain_vec, shift_vec):
    centred = values - jnp.mean(values, axis=-1, keepdims=True)
    spread = jnp.mean(centred * centred, axis=-1, keepdims=True)
    return centred * lax.rsqrt(spread + eps_norm) * gain_vec + shift_vec


def shrink(values):
    return values - shrink_level * jnp.tanh(values / shrink_level)


def lon_tables(lon_total, mode_total):
    places = jnp.arange(lon_total, dtype=jnp.int32)
    orders = jnp.arange(mode_total, dtype=jnp.int32)
    angles = (places[:, None] * orders[None, :] % lon_total).astype(jnp.float32) * (
        2.0 * math.pi / lon_total
    )
    scaling = 1.0 / math.sqrt(lon_total)
    forward_tab = jnp.stack([jnp.cos(angles), -jnp.sin(angles)], axis=1) * scaling
    doubling = jnp.where(orders == 0, 1.0, 2.0).astype(jnp.float32)[:, None]
    inverse_tab = (
        jnp.stack([jnp.cos(angles).T * doubling, -jnp.sin(angles).T * doubling], axis=0) * scaling
    )
    return (forward_tab.astype(jnp.bfloat16), inverse_tab.astype(jnp.bfloat16))


def lat_table(lat_total):
    places = jnp.arange(lat_total, dtype=jnp.int32)
    angles = (places[:, None] * places[None, :] % lat_total).astype(jnp.float32) * (
        2.0 * math.pi / lat_total
    )
    cosine = jnp.cos(angles)
    sine_part = jnp.sin(angles)
    upper_rows = jnp.stack([cosine, sine_part], axis=1)
    bottom = jnp.stack([-sine_part, cosine], axis=1)
    return (jnp.stack([upper_rows, bottom], axis=0) / math.sqrt(lat_total)).astype(jnp.bfloat16)


def complex_pair(real_part, imag_part):
    return jnp.stack([jnp.stack([real_part, -imag_part]), jnp.stack([imag_part, real_part])])


gelu_scale = math.sqrt(2.0 / math.pi)
gelu_cubic = 0.044715


def gelu_both(value):
    bend = (gelu_scale * gelu_cubic) * (value * value)
    turn = jnp.tanh(value * (gelu_scale + bend))
    half = 0.5 + 0.5 * turn
    slope = half * (1.0 + (value * (1.0 - turn)) * (gelu_scale + 3.0 * bend))
    return value * half, slope


def dot_nt(left, right):
    return lax.dot_general(
        left, right, (((1,), (1,)), ((), ())), preferred_element_type=jnp.float32
    )


def dot_nn(left, right):
    return jnp.dot(left, right, preferred_element_type=jnp.float32)


def divisor(total, unit, most):
    return max(size for size in range(unit, most + 1, unit) if total % size == 0)


def mlp_body(
    tile,
    normed_ref,
    cot_ref,
    up_ref,
    down_ref,
    bias_ref,
    out_ref,
    back_ref,
    grad_up_ref,
    grad_down_ref,
    grad_bias_ref,
    normed_turned,
    cot_turned,
    act_ref,
    slope_ref,
):
    tokens = normed_ref.shape[0]

    @pl.when(pl.program_id(0) == 0)
    def _():
        normed_turned[...] = normed_ref[...].T
        cot_turned[...] = cot_ref[...].T
        out_ref[...] = jnp.zeros_like(out_ref)
        back_ref[...] = jnp.zeros_like(back_ref)

    grad_bias_ref[...] = jnp.zeros_like(grad_bias_ref)

    @pl.loop(0, tokens // tile)
    def _(step):
        rows = pl.ds(pl.multiple_of(step * tile, tile), tile)
        act, slope = gelu_both(dot_nn(normed_ref[rows, :], up_ref[...]) + bias_ref[...])
        act = act.astype(jnp.bfloat16)
        slope = (dot_nn(cot_ref[rows, :], down_ref[...]) * slope).astype(jnp.bfloat16)
        act_ref[rows, :] = act
        slope_ref[rows, :] = slope
        grad_bias_ref[...] += jnp.sum(slope.astype(jnp.float32), axis=0, keepdims=True)
        out_ref[rows, :] += dot_nt(act, down_ref[...])
        back_ref[rows, :] += dot_nt(slope, up_ref[...])

    grad_up_ref[...] = dot_nn(normed_turned[...], slope_ref[...]).astype(grad_up_ref.dtype)
    grad_down_ref[...] = dot_nn(cot_turned[...], act_ref[...]).astype(grad_down_ref.dtype)


def mlp_pass(normed, cot, weights, bias):
    tokens, channel = normed.shape
    hidden = weights.shape[2]
    width = divisor(hidden, 128, 512)
    tile = divisor(tokens, 16, 480)
    whole = pl.BlockSpec((tokens, channel), lambda j: (0, 0))
    block = pl.BlockSpec((channel, width), lambda j: (0, j))
    line = pl.BlockSpec((1, width), lambda j: (0, j))
    part = lambda which: pl.BlockSpec((None, channel, width), lambda j: (which, 0, j))
    total = jax.ShapeDtypeStruct((tokens, channel), jnp.float32)
    grads = jax.ShapeDtypeStruct((channel, hidden), jnp.bfloat16)
    return pl.pallas_call(
        functools.partial(mlp_body, tile),
        grid=(hidden // width,),
        in_specs=[whole, whole, part(0), part(1), line],
        out_specs=[whole, whole, block, block, line],
        out_shape=[total, total, grads, grads, jax.ShapeDtypeStruct((1, hidden), jnp.float32)],
        scratch_shapes=[
            pltpu.VMEM((channel, tokens), jnp.bfloat16),
            pltpu.VMEM((channel, tokens), jnp.bfloat16),
            pltpu.VMEM((tokens, width), jnp.bfloat16),
            pltpu.VMEM((tokens, width), jnp.bfloat16),
        ],
        compiler_params=pltpu.CompilerParams(vmem_limit_bytes=56 * 1024 * 1024),
        cost_estimate=pl.CostEstimate(
            flops=12 * tokens * channel * hidden,
            bytes_accessed=8 * channel * hidden + 12 * tokens * channel,
            transcendentals=tokens * hidden,
        ),
        name="mlp_pass",
    )(normed, cot, weights, weights, bias)


def spectral_front(arrived, lat_fwd, first_pair, second_pair, bias_one, bias_two):
    spectrum = jnp.einsum(
        "pkqr,nrqmd->nkpmd", lat_fwd, arrived, preferred_element_type=jnp.float32
    ).astype(jnp.bfloat16)
    snap_local, lat_total, pair_count, mode_local, channel = spectrum.shape
    blocked = spectrum.reshape(
        snap_local, lat_total, pair_count, mode_local, BLOCKS, channel // BLOCKS
    )
    pre_one = (
        jnp.einsum("nkqmbi,pqbio->nkpmbo", blocked, first_pair, preferred_element_type=jnp.float32)
        + bias_one
    )
    act_one = jax.nn.gelu(pre_one).astype(jnp.bfloat16)
    pre_two = (
        jnp.einsum("nkqmbi,pqbio->nkpmbo", act_one, second_pair, preferred_element_type=jnp.float32)
        + bias_two
    )
    return (blocked, pre_one, act_one, pre_two)


def adamw(master, first_mom, second_mom, gradient, step_rate):
    first_next = beta_one * first_mom + (1.0 - beta_one) * gradient
    second_next = beta_two * second_mom + (1.0 - beta_two) * gradient * gradient
    fix_one = 1.0 / (1.0 - beta_one**STEP)
    fix_two = 1.0 / (1.0 - beta_two**STEP)
    direction = first_next * fix_one / (jnp.sqrt(second_next * fix_two) + adam_eps)
    master_next = master - step_rate * (direction + decay_rate * master)
    return (master_next, first_next, second_next, master_next.astype(jnp.bfloat16))


def per_device_modes(
    fields,
    cotangent,
    valid_mask,
    kept_modes,
    mlp_master,
    mlp_first,
    mlp_second,
    filter_master,
    filter_first,
    filter_second,
    small_master,
    small_first,
    small_second,
    run_stats,
):
    group_size = lax.axis_size("sp")
    snap_local, row_local, lon_total, channel = fields.shape
    lat_total = row_local * group_size
    mode_local = kept_modes.shape[1]
    mode_total = mode_local * group_size
    block_width = channel // BLOCKS
    lon_fwd, lon_inv = lon_tables(lon_total, mode_total)
    lat_fwd = lat_table(lat_total)
    mlp_w, filt_w, small_w = (
        lax.all_gather(mlp_master.astype(jnp.bfloat16), "sp", axis=1, tiled=True),
        lax.all_gather(filter_master.astype(jnp.bfloat16), "sp", axis=1, tiled=True),
        lax.all_gather(small_master.astype(jnp.bfloat16), "sp", axis=1, tiled=True),
    )
    small_f = small_w.astype(jnp.float32)
    weights = filt_w.reshape(4, BLOCKS, block_width, block_width)
    first_pair = complex_pair(weights[0], weights[1])
    second_pair = complex_pair(weights[2], weights[3])
    bias_one = small_f[4:6].reshape(2, 1, BLOCKS, block_width)
    bias_two = small_f[6:8].reshape(2, 1, BLOCKS, block_width)
    fields_float = fields.astype(jnp.float32)
    normed, norm_pull = jax.vjp(layer_norm, fields_float, small_f[0], small_f[1])
    normed_low = normed.astype(jnp.bfloat16)
    spec_lon = jnp.einsum(
        "nrld,lqm->nrqmd", normed_low, lon_fwd, preferred_element_type=jnp.float32
    ).astype(jnp.bfloat16)
    arrived = lax.all_to_all(spec_lon, "sp", split_axis=3, concat_axis=1, tiled=True)
    spectral = spectral_front(arrived, lat_fwd, first_pair, second_pair, bias_one, bias_two)
    keep_mask = kept_modes.astype(jnp.float32)[None, :, None, :, None, None]
    masked = (shrink(spectral[3]) * keep_mask).astype(jnp.bfloat16)
    masked = masked.reshape(snap_local, lat_total, 2, mode_local, channel)
    returned = jnp.einsum(
        "pkqr,nkpmd->nrqmd", lat_fwd, masked, preferred_element_type=jnp.float32
    ).astype(jnp.bfloat16)
    home_modes = lax.all_to_all(returned, "sp", split_axis=1, concat_axis=3, tiled=True)
    filtered = jnp.einsum(
        "nrqmd,qml->nrld", home_modes, lon_inv, preferred_element_type=jnp.float32
    )
    mixture = fields_float + normed + filtered
    normed_two, norm_two_pull = jax.vjp(layer_norm, mixture, small_f[2], small_f[3])
    normed_two_low = normed_two.astype(jnp.bfloat16)
    tokens = snap_local * row_local * lon_total
    passed = mlp_pass(
        normed_two_low.reshape(tokens, channel),
        cotangent.reshape(tokens, channel),
        mlp_w,
        small_f[9:].reshape(1, -1),
    )
    output = mixture + passed[0].reshape(mixture.shape) + small_f[8]
    weight_mask = valid_mask.astype(jnp.float32)[..., None]
    variables = output[..., :NVAR]
    local_sums = jnp.stack(
        [
            jnp.sum(weight_mask * variables, axis=(0, 1, 2)),
            jnp.sum(weight_mask * variables * variables, axis=(0, 1, 2)),
        ]
    )
    total_sums = lax.psum(local_sums, ("snap", "sp"))
    positions = snap_local * lax.axis_size("snap") * lat_total * lon_total
    stats_new = stat_decay * run_stats + (1.0 - stat_decay) * total_sums / positions
    cot_float = cotangent.astype(jnp.float32)
    grad_normed_two = passed[1].reshape(mixture.shape)
    grad_bias_hidden = passed[4]
    grad_mix_norm, grad_gain_two, grad_shift_two = norm_two_pull(grad_normed_two)
    grad_mixture = cot_float + grad_mix_norm
    grad_bias_out = jnp.sum(cot_float, axis=(0, 1, 2))
    grad_filtered = grad_mixture.astype(jnp.bfloat16)
    grad_home = jnp.einsum(
        "nrld,qml->nrqmd", grad_filtered, lon_inv, preferred_element_type=jnp.float32
    ).astype(jnp.bfloat16)
    grad_returned = lax.all_to_all(grad_home, "sp", split_axis=3, concat_axis=1, tiled=True)
    grad_masked = jnp.einsum(
        "pkqr,nrqmd->nkpmd", lat_fwd, grad_returned, preferred_element_type=jnp.float32
    )
    arrived_again = lax.all_to_all(spec_lon, "sp", split_axis=3, concat_axis=1, tiled=True)
    used_front = spectral_front(arrived_again, lat_fwd, first_pair, second_pair, bias_one, bias_two)
    blocked, pre_one, act_one, pre_two = used_front
    grad_two = jax.vjp(shrink, pre_two)[1](grad_masked.reshape(pre_two.shape) * keep_mask)[
        0
    ].astype(jnp.bfloat16)
    grad_bias_two = jnp.sum(grad_two.astype(jnp.float32), axis=(0, 1, 3))
    grad_second = jnp.einsum(
        "nkqmbi,nkpmbo->pqbio", act_one, grad_two, preferred_element_type=jnp.float32
    )
    grad_act = jnp.einsum(
        "nkpmbo,pqbio->nkqmbi", grad_two, second_pair, preferred_element_type=jnp.float32
    )
    grad_one = jax.vjp(jax.nn.gelu, pre_one)[1](grad_act)[0].astype(jnp.bfloat16)
    grad_bias_one = jnp.sum(grad_one.astype(jnp.float32), axis=(0, 1, 3))
    grad_first = jnp.einsum(
        "nkqmbi,nkpmbo->pqbio", blocked, grad_one, preferred_element_type=jnp.float32
    )
    grad_spectrum = jnp.einsum(
        "nkpmbo,pqbio->nkqmbi", grad_one, first_pair, preferred_element_type=jnp.float32
    ).astype(jnp.bfloat16)
    grad_spectrum = grad_spectrum.reshape(snap_local, lat_total, 2, mode_local, channel)
    grad_lon = jnp.einsum(
        "pkqr,nkpmd->nrqmd", lat_fwd, grad_spectrum, preferred_element_type=jnp.float32
    ).astype(jnp.bfloat16)
    grad_rows = lax.all_to_all(grad_lon, "sp", split_axis=1, concat_axis=3, tiled=True)
    grad_normed = grad_mixture + jnp.einsum(
        "nrqmd,lqm->nrld", grad_rows, lon_fwd, preferred_element_type=jnp.float32
    )
    grad_field_norm, grad_gain_one, grad_shift_one = norm_pull(grad_normed)
    input_grad = grad_mixture + grad_field_norm
    grad_filter = jnp.stack(
        [
            grad_first[0, 0] + grad_first[1, 1],
            grad_first[1, 0] - grad_first[0, 1],
            grad_second[0, 0] + grad_second[1, 1],
            grad_second[1, 0] - grad_second[0, 1],
        ]
    ).reshape(4, channel, block_width)
    grad_small = jnp.concatenate(
        [
            jnp.stack([grad_gain_one, grad_shift_one, grad_gain_two, grad_shift_two]),
            grad_bias_one.reshape(2, channel),
            grad_bias_two.reshape(2, channel),
            grad_bias_out[None, :],
            grad_bias_hidden.reshape(-1, channel),
        ],
        axis=0,
    )
    shares = (
        jnp.stack([
            lax.psum_scatter(part, "sp", scatter_dimension=0, tiled=True) for part in passed[2:4]
        ]),
        lax.psum_scatter(grad_filter, "sp", scatter_dimension=1, tiled=True),
        lax.psum_scatter(grad_small, "sp", scatter_dimension=1, tiled=True),
    )
    owned = (
        lax.psum(shares[0].astype(jnp.bfloat16), "snap").astype(jnp.float32),
        lax.psum(shares[1].astype(jnp.bfloat16), "snap").astype(jnp.float32),
        lax.psum(shares[2].astype(jnp.bfloat16), "snap").astype(jnp.float32),
    )
    mlp_new, mlp_first_new, mlp_second_new, mlp_copy = adamw(
        mlp_master, mlp_first, mlp_second, owned[0], rate_mlp
    )
    filter_new, filter_first_new, filter_second_new, filter_copy = adamw(
        filter_master, filter_first, filter_second, owned[1], rate_filter
    )
    small_new, small_first_new, small_second_new, small_copy = adamw(
        small_master, small_first, small_second, owned[2], rate_small
    )
    return (
        output.astype(jnp.bfloat16),
        input_grad,
        mlp_new,
        mlp_first_new,
        mlp_second_new,
        mlp_copy,
        filter_new,
        filter_first_new,
        filter_second_new,
        filter_copy,
        small_new,
        small_first_new,
        small_second_new,
        small_copy,
        stats_new,
    )


SCHEDULE = {
    "cast": [("first", 0), ("first", 1)],
    "norm_one_0": [("second", 0)],
    "sent_one_1": [("second", 1), ("first", 2)],
    "sent_two_0": [("third", 0)],
    "sent_two_1": [("second", 2), ("first", 3)],
    "turned_cot": [("third", 1)],
    "added_0": [("first", 4)],
    "added_1": [("fourth", 0), ("third", 2)],
    ("row_2", 0): [("second", 3), ("second", 4)],
    ("grads", 0): [("fourth", 1), ("first", 5)],
    ("sum_0", 0): [("fourth", 2)],
    ("sum_1", 0): [("half", 0)],
    ("row_1", 1): [("third", 3)],
    ("row_2", 1): [("third", 4)],
    ("row_0", 2): [("half", 1)],
    ("grads", 2): [("fourth", 3)],
    ("sum_1", 2): [("quarter", 0)],
    ("sum_2", 2): [("half", 2), ("fourth", 4)],
    ("row_0", 3): [("fourth", 5)],
    ("grads", 3): [("level", 0), ("quarter", 1)],
    ("begin", 4): [("half", 3)],
    ("row_2", 4): [("level", 1)],
    ("rows", 4): [("quarter", 2)],
    ("begin", 5): [("last", 0)],
    ("row_0", 5): [("level", 2)],
    ("row_1", 5): [("quarter", 3)],
    ("row_2", 5): [("half", 4)],
    ("grads", 5): [("last", 1), ("level", 3)],
    "summed_1": [("quarter", 4)],
    "sent_three_1": [("half", 5)],
    "shown": [("last", 2), ("level", 4)],
    "got_three_1": [("quarter", 5)],
    "sent_four_1": [("last", 3), ("last", 4)],
    "got_four_0": [("level", 5)],
    "tiles": [("last", 5)],
}


def lon_matrix(lon_total, mode_total, snaps, rows):
    places = np.arange(lon_total)
    orders = np.arange(mode_total)
    angles = (places[:, None] * orders[None, :] % lon_total) * (2.0 * math.pi / lon_total)
    doubling = np.where(orders == 0, 1.0, 2.0)
    scaling = 1.0 / math.sqrt(lon_total)
    forward = np.stack([np.cos(angles), -np.sin(angles)], axis=1) * scaling
    inverse = forward * doubling

    def spread(table):
        table = np.einsum(
            "ab,lx,rs->alrbsx", np.eye(snaps), table.reshape(lon_total, -1), np.eye(rows)
        )
        return table.reshape(snaps * lon_total * rows, -1).astype(ml_dtypes.bfloat16)

    return spread(forward), spread(inverse)


def lon_turn(lon_total, rows):
    turn = np.einsum("lk,rs->rlks", np.eye(lon_total), np.eye(rows))
    return turn.reshape(rows, lon_total, lon_total * rows).astype(ml_dtypes.bfloat16)


def lat_matrix(lat_total, mode_total):
    places = np.arange(lat_total)
    angles = (places[:, None] * places[None, :] % lat_total) * (2.0 * math.pi / lat_total)
    cosine, sine = np.cos(angles), np.sin(angles)
    table = np.stack([np.stack([cosine, sine], axis=1), np.stack([-sine, cosine], axis=1)])
    table = np.einsum("pkqr,ab->pakrqb", table / math.sqrt(lat_total), np.eye(mode_total))
    size = 2 * lat_total * mode_total
    return table.reshape(size, size).astype(ml_dtypes.bfloat16)


class Refs:
    pass


def block_body(names, sizes, *refs):
    g = Refs()
    for name, ref in zip(names, refs, strict=True):
        setattr(g, name, ref)
    snaps, group, parts, width = sizes
    levels = group // 2
    tokens = g.fields.shape[0] * g.fields.shape[1]
    channel = g.fields.shape[2]
    tiles = channel // 128
    owned = channel // group
    half = width // 2
    quarter = width // snaps
    tile = tokens // 3
    short = divisor(tokens // 2, 16, 240)
    packed = g.modes.shape[2]
    strip = divisor(tokens // 2, 48, 144)
    sub = divisor(strip, 16, 48)
    low = jnp.bfloat16
    f32 = jnp.float32

    me_snap = lax.axis_index("snap")
    me_sp = lax.axis_index("sp")
    core = lax.rem(me_sp, 2)
    level = me_sp // 2

    def at(snap, sp):
        return {"snap": snap, "sp": sp}

    def sp_after(step):
        return lax.rem(me_sp + step, group)

    def sp_before(step):
        return lax.rem(me_sp + group - step, group)

    def snap_after(step):
        return lax.rem(me_snap + step, snaps)

    def snap_before(step):
        return lax.rem(me_snap + snaps - step, snaps)

    def level_after(step):
        return lax.rem(level + step, levels)

    def level_before(step):
        return lax.rem(level + levels - step, levels)

    other_core = at(me_snap, me_sp + 1 - 2 * core)

    def send(src, dst, sems, index, target):
        return pltpu.make_async_remote_copy(
            src_ref=src,
            dst_ref=dst,
            send_sem=sems[0].at[index],
            recv_sem=sems[1].at[index],
            device_id=target,
            device_id_type=pl.DeviceIdType.MESH,
        )

    half_tokens = tokens // 2

    def strips(body, first=0, count=tokens):
        @pl.loop(0, count // strip)
        def _(step):
            for at_row in range(0, strip, sub):
                body(pl.ds(pl.multiple_of(first + step * strip + at_row, 16), sub))

    def half_strips(body, part):
        strips(body, part * half_tokens, half_tokens)

    def half_rows(part):
        return slice(part * half_tokens, (part + 1) * half_tokens)

    def fold(value):
        return jnp.sum(value.reshape(-1, 8, value.shape[1]), axis=0)

    def columns(name):
        ref = getattr(g, name)
        return ref.reshape(tiles, ref.shape[1] * ref.shape[2], 128)

    def columns_of(name, rows):
        view = columns(name)
        return jnp.concatenate([view[tile_at, rows, :] for tile_at in range(tiles)], axis=1)

    def store_columns(name, rows, value):
        view = columns(name)
        for tile_at in range(tiles):
            view[tile_at, rows, :] = value[:, tile_at * 128 : (tile_at + 1) * 128]

    def column_copies(near, far, sems, out):
        copies = []
        for tile_at in range(tiles):
            ends = [near.at[tile_at], far.at[:, :, tile_at * 128 : (tile_at + 1) * 128]]
            if not out:
                ends.reverse()
            copies.append(pltpu.make_async_copy(*ends, sems.at[tile_at]))
        return copies

    loads = {}

    def load(name, index):
        copy = pltpu.make_async_copy(getattr(g, name), getattr(g, name + "_in"), g.load_sem.at[index])
        copy.start()
        loads[name] = copy

    for index, name in enumerate(
        [name for name in names[: names.index("out")] if name not in ("mlp", "fields", "cot")]
    ):
        load(name, index)
    fields_load = column_copies(g.fields_cols, g.fields, g.fields_sem, False)
    cot_load = column_copies(g.cot_cols, g.cot, g.cot_sem, False)
    for copy in fields_load + cot_load:
        copy.start()

    def master_load(part):
        return pltpu.make_async_copy(
            g.mlp.at[:, :, part * width : (part + 1) * width],
            g.mlp_part.at[part % 2],
            g.load_sem.at[len(loads) + part % 2],
        )

    master_load(0).start()
    master_load(1).start()

    barrier = pltpu.get_barrier_semaphore()
    peers = [at(me_snap, sp_after(step)) for step in range(1, group)]
    peers += [at(snap_after(step), me_sp) for step in range(1, snaps)]
    for peer in peers:
        pl.semaphore_signal(
            barrier, inc=1, device_id=peer, device_id_type=pl.DeviceIdType.MESH
        )

    loads["small"].wait()
    loads["kept"].wait()
    g.own_small[...] = jnp.zeros_like(g.own_small)
    rows_small = g.small.shape[0]
    g.own_small[0:rows_small, 0:owned] = g.small_in[...].astype(low).astype(f32)
    pairs_kept = g.kept.shape[1]
    lines = lax.broadcasted_iota(jnp.int32, (pairs_kept, pairs_kept), 0)
    places = lax.broadcasted_iota(jnp.int32, (pairs_kept, pairs_kept), 1)
    kept = jnp.where(lines == places, g.kept_in[...].astype(f32), 0.0)
    g.own_small[16:, :] = jnp.broadcast_to(
        jnp.sum(kept, axis=1, keepdims=True), (pairs_kept, g.own_small.shape[1])
    )
    pl.semaphore_wait(barrier, len(peers))

    def small_copy(step):
        return send(
            g.own_small, g.all_small.at[me_sp], (g.small_s, g.small_r), step, at(me_snap, sp_after(step))
        )

    for step in range(1, group):
        small_copy(step).start()
    g.all_small[me_sp] = g.own_small[...]

    snap_low = lax.rem(me_snap, 2)
    snap_high = me_snap // 2
    beside_low = me_snap + 1 - 2 * snap_low
    beside_high = me_snap + 2 - 4 * snap_high

    def own_quarter(part):
        odd = lax.rem(part, 2)
        return (1 - odd) * me_snap + odd * (2 * snap_low + snap_high)

    def own_place(part):
        return pl.ds(0, snaps) if part == parts - 1 else own_quarter(part)

    def half_quarters(part):
        return pl.ds(2 * (own_quarter(part) // 2), 2)

    def own_rows(sp):
        return pl.ds(pl.multiple_of(sp * owned, owned), owned)

    def first_copy(part, step):
        target = sp_after(step)
        matrix = lax.rem(target, 2)
        place = own_place(part)
        return send(
            g.own_w.at[part, matrix, place],
            g.all_w.at[part, matrix, place, own_rows(me_sp)],
            (g.first_s, g.first_r),
            (part, step),
            at(me_snap, target),
        )

    def first_local(part):
        place = own_place(part)
        return pltpu.make_async_copy(
            g.own_w.at[part, core, place],
            g.all_w.at[part, core, place, own_rows(me_sp)],
            g.first_s.at[part, 0],
        )

    def second_copy(part):
        odd = lax.rem(part, 2)
        view = g.all_w.at[part, core, own_quarter(part)]
        target = at((1 - odd) * beside_low + odd * beside_high, me_sp)
        return send(view, view, (g.second_s, g.second_r), part, target)

    def third_copy(part):
        odd = lax.rem(part, 2)
        view = g.all_w.at[part, core, half_quarters(part)]
        target = at((1 - odd) * beside_high + odd * beside_low, me_sp)
        return send(view, view, (g.third_s, g.third_r), part, target)

    def fourth_copy(part):
        view = g.all_w.at[part, core]
        return send(view, view, (g.fourth_s, g.fourth_r), part, other_core)

    def start_first(part):
        for step in range(1, group):
            first_copy(part, step).start()
        first_local(part).start()

    def wait_first(part):
        for step in range(1, group):
            first_copy(part, step).wait_recv()
        first_local(part).wait()

    def pass_second(part):
        wait_first(part)
        second_copy(part).start()

    def pass_third(part):
        second_copy(part).wait_recv()
        third_copy(part).start()

    def pass_fourth(part):
        if part == parts - 1:
            wait_first(part)
        else:
            third_copy(part).wait_recv()
        fourth_copy(part).start()

    stages = dict(first=start_first, second=pass_second, third=pass_third, fourth=pass_fourth)

    def reach(point):
        for stage, part in SCHEDULE.get(point, ()):
            stages[stage](part)

    for part in range(parts):
        master_load(part).wait()
        for place in range(snaps):
            cols = slice(place * quarter, (place + 1) * quarter)
            g.own_w[part, :, place] = g.mlp_part[part % 2, :, :, cols].astype(low)
        if part + 2 < parts:
            master_load(part + 2).start()
        if ("first", part) in SCHEDULE["cast"]:
            start_first(part)

    for copy in fields_load:
        copy.wait()

    def first_unit(rows):
        values = columns_of("fields_cols", rows).astype(f32)
        centred = values - jnp.mean(values, axis=-1, keepdims=True)
        scale = lax.rsqrt(jnp.mean(centred * centred, axis=-1, keepdims=True) + eps_norm)
        g.scale_one[rows, :] = scale
        g.grid[rows, :] = centred * scale

    strips(first_unit)
    reach("unit")
    for step in range(1, group):
        small_copy(step).wait_recv()
    for sp in range(group):
        g.gains[:, sp * owned : (sp + 1) * owned] = g.all_small[sp, 0:16, 0:owned]
        g.keep[sp * pairs_kept : (sp + 1) * pairs_kept, :] = g.all_small[sp, 16:, :]

    def first_norm(rows):
        unit = g.grid[rows, :]
        normed = unit * g.gains[0:1, :] + g.gains[1:2, :]
        g.unit_one[rows, :] = unit.astype(low)
        g.normed[rows, :] = normed.astype(low)
        g.grid[rows, :] = columns_of("fields_cols", rows).astype(f32) + normed

    half_snaps = g.arrived.shape[0] // 2

    third_rows = packed // 3
    spare = 128 - owned

    def pack(value):
        return jnp.concatenate(
            [
                jnp.concatenate(
                    [
                        value[at_row * third_rows : (at_row + 1) * third_rows],
                        value[packed:, at_row * spare : (at_row + 1) * spare],
                    ],
                    axis=1,
                )
                for at_row in range(3)
            ],
            axis=0,
        ).astype(low)

    def unpack(value):
        value = value.astype(f32)
        rest = [
            value[at_row * third_rows : (at_row + 1) * third_rows, owned:] for at_row in range(3)
        ]
        return jnp.concatenate([value[:, 0:owned], jnp.concatenate(rest, axis=1)], axis=0)

    def block_copy(which, part, step):
        target = sp_after(step)
        return send(
            g.modes.at[part, target],
            g.modes_got.at[part, me_sp],
            (g.block_s, g.block_r),
            (which, part, step),
            at(me_snap, target),
        )

    def row_copy(which, part, step):
        target = sp_after(step)
        return send(
            g.rows_out.at[part, target],
            g.rows_got.at[part, me_sp],
            (g.row_s, g.row_r),
            (which, part, step),
            at(me_snap, target),
        )

    def to_blocks(table, which, part):
        modes = dot_nn(table, g.normed[half_rows(part), :])
        for block in range(group):
            g.modes[part, block] = pack(modes[:, block * owned : (block + 1) * owned])
        for step in range(1, group):
            block_copy(which, part, step).start()
        g.modes_got[part, me_sp] = g.modes[part, me_sp]

    def take_blocks(which, part):
        for step in range(1, group):
            block_copy(which, part, step).wait_recv()
        each = g.arrived.shape[1] // group
        for sp in range(group):
            value = unpack(g.modes_got[part, sp])
            value = jnp.concatenate([value, jnp.zeros((value.shape[0], spare), f32)], axis=1)
            for index in range(half_snaps):
                g.arrived[part * half_snaps + index, sp * each : (sp + 1) * each, :] = value[
                    index * each : (index + 1) * each
                ].astype(low)

    def to_rows(which, part, tables):
        each = tables[0].shape[0] // group
        for sp in range(group):
            value = [table[sp * each : (sp + 1) * each, 0:owned] for table in tables]
            g.rows_out[part, sp] = pack(jnp.concatenate(value, axis=0))
        for step in range(1, group):
            row_copy(which, part, step).start()
        g.rows_got[part, me_sp] = g.rows_out[part, me_sp]

    def home_modes(which, part):
        for step in range(1, group):
            row_copy(which, part, step).wait_recv()
        for block in range(group):
            g.gathered[part, :, block * owned : (block + 1) * owned] = unpack(
                g.rows_got[part, block]
            )
        g.home_low[part] = g.gathered[part].astype(low)

    loads["lon_f"].wait()
    for part in range(2):
        half_strips(first_norm, part)
        reach("norm_one_" + str(part))
        to_blocks(g.lon_f_in[...], 0, part)
        reach("sent_one_" + str(part))

    loads["filt"].wait()
    for weight, first in ((g.weight_one, 0), (g.weight_two, 2)):
        weight[...] = jnp.zeros_like(weight)
        real = g.filt_in[first].astype(low)
        imag = g.filt_in[first + 1].astype(low)
        weight[0:owned, 0:owned] = real
        weight[128 : 128 + owned, 128 : 128 + owned] = real
        weight[0:owned, 128 : 128 + owned] = imag
        weight[128 : 128 + owned, 0:owned] = -imag

    def bias_row(first):
        return jnp.concatenate(
            [g.own_small[first : first + 1, :], g.own_small[first + 1 : first + 2, :]], axis=1
        )

    for copy in cot_load:
        copy.wait()

    def flat_cot(rows):
        g.cot_in[rows, :] = columns_of("cot_cols", rows)

    strips(flat_cot)
    reach("flat")
    loads["lat_f"].wait()
    loads["lat_b"].wait()
    pairs = g.arrived.shape[1] // 2
    half_modes = half_snaps * pairs

    def mode_half(part):
        return slice(part * half_modes, (part + 1) * half_modes)

    def spectra(out, kind, part):
        for snap in range(part * half_snaps, (part + 1) * half_snaps):
            spectrum = dot_nn(g.lat_f_in[...], g.arrived[snap]).astype(kind)
            rows = slice(snap * pairs, (snap + 1) * pairs)
            out[rows, 0:128] = spectrum[0:pairs]
            out[rows, 128:256] = spectrum[pairs:]

    def grids(values):
        tables = []
        for index in range(half_snaps):
            rows = values[index * pairs : (index + 1) * pairs]
            rows = jnp.concatenate([rows[:, 0:128], rows[:, 128:256]], axis=0)
            tables.append(dot_nn(g.lat_b_in[...], rows))
        return tables

    def keep_half():
        keep = jnp.concatenate([g.keep[...], g.keep[...]], axis=1)
        return jnp.concatenate([keep] * half_snaps, axis=0)

    for part in range(2):
        take_blocks(0, part)
        rows = mode_half(part)
        spectra(g.spectrum, low, part)
        g.pre_one[rows, :] = dot_nn(g.spectrum[rows, :], g.weight_one[...]) + bias_row(4)
        g.act_one[rows, :] = gelu_both(g.pre_one[rows, :])[0].astype(low)
        g.pre_two[rows, :] = dot_nn(g.act_one[rows, :], g.weight_two[...]) + bias_row(6)
        to_rows(0, part, grids((shrink(g.pre_two[rows, :]) * keep_half()).astype(low)))
        reach("sent_two_" + str(part))
    g.cot_turned[...] = g.cot_in[...].T
    reach("turned_cot")

    loads["lon_i"].wait()

    def second_norm(rows):
        values = g.grid[rows, :]
        centred = values - jnp.mean(values, axis=-1, keepdims=True)
        scale = lax.rsqrt(jnp.mean(centred * centred, axis=-1, keepdims=True) + eps_norm)
        centred = centred * scale
        g.unit_two[rows, :] = centred.astype(low)
        g.scale_two[rows, :] = scale
        g.normed[rows, :] = (centred * g.gains[2:3, :] + g.gains[3:4, :]).astype(low)
        g.grid[rows, :] = values + g.gains[8:9, :]
        g.back[rows, :] = jnp.zeros((sub, channel), f32)

    for part in range(2):
        home_modes(0, part)
        g.grid[half_rows(part), :] += dot_nn(g.lon_i_in[...], g.home_low[part])
        reach("added_" + str(part))
        half_strips(second_norm, part)
        reach("norm_two_" + str(part))
    g.normed_turned[...] = g.normed[...].T
    reach("turned_normed")
    flat = jnp.concatenate([g.gains[9 + row : 10 + row, :] for row in range(rows_small - 9)], axis=1)
    for part in range(parts):
        g.bias[part] = flat[:, part * width : (part + 1) * width]

    def core_copy(part, matrix):
        slot = lax.rem(part, 2)
        return send(
            g.grads.at[matrix, :, 1 - core],
            g.core_got.at[slot, matrix],
            (g.core_s, g.core_r),
            (slot, matrix),
            other_core,
        )

    places_one = (snap_low, snap_high)
    places_two = (snap_high, snap_low)
    beside_one = (beside_low, beside_high)
    beside_two = (beside_high, beside_low)
    place_last = (2 * snap_low + snap_high, me_snap)

    def half_copy(part, matrix):
        slot = lax.rem(part, 2)
        place = lax.rem(part, 4)
        return send(
            g.half_out.at[slot, matrix, 1 - places_one[matrix]],
            g.half_got.at[place, matrix],
            (g.half_s, g.half_r),
            (place, matrix),
            at(beside_one[matrix], me_sp),
        )

    def quarter_copy(part, matrix):
        slot = lax.rem(part, 2)
        return send(
            g.quarter_out.at[slot, matrix, 1 - places_two[matrix]],
            g.quarter_got.at[slot, matrix],
            (g.quarter_s, g.quarter_r),
            (slot, matrix),
            at(beside_two[matrix], me_sp),
        )

    def level_copy(part, step):
        slot = lax.rem(part, 2)
        place = lax.rem(part, 4)
        target = level_after(step)
        return send(
            g.level_out.at[slot, target],
            g.level_got.at[place, level],
            (g.level_s, g.level_r),
            (place, step),
            at(me_snap, 2 * target + core),
        )

    def last_copy(part, matrix, step):
        view = g.total.at[part, place_last[matrix], matrix]
        return send(
            view, view, (g.last_s, g.last_r), (part, matrix, step), at(snap_after(step), me_sp)
        )

    def half_stage(part):
        slot = lax.rem(part, 2)
        for matrix in range(2):

            if part >= 2:
                half_copy(part - 2, matrix).wait_send()

            core_copy(part, matrix).wait_recv()

            @pl.loop(0, levels)
            def _(row, matrix=matrix):
                both = g.grads[matrix, row, core].astype(f32) + g.core_got[
                    slot, matrix, row
                ].astype(f32)
                both = both.astype(low)
                g.half_out[slot, matrix, 0, row] = both[:, 0:half]
                g.half_out[slot, matrix, 1, row] = both[:, half:width]

            half_copy(part, matrix).start()

    def quarter_stage(part):
        slot = lax.rem(part, 2)
        for matrix in range(2):

            if part >= 2:
                quarter_copy(part - 2, matrix).wait_send()

            half_copy(part, matrix).wait_recv()
            for row in range(levels):
                both = g.half_out[slot, matrix, places_one[matrix], row].astype(f32) + g.half_got[
                    lax.rem(part, 4), matrix, row
                ].astype(f32)
                both = both.astype(low)
                g.quarter_out[slot, matrix, 0, row] = both[:, 0:quarter]
                g.quarter_out[slot, matrix, 1, row] = both[:, quarter:half]
            quarter_copy(part, matrix).start()

    def level_stage(part):
        slot = lax.rem(part, 2)

        if part >= 2:
            for step in range(1, levels):
                level_copy(part - 2, step).wait_send()

        for matrix in range(2):
            quarter_copy(part, matrix).wait_recv()
            for row in range(levels):
                both = g.quarter_out[slot, matrix, places_two[matrix], row].astype(
                    f32
                ) + g.quarter_got[slot, matrix, row].astype(f32)
                g.level_out[slot, row, matrix] = both.astype(low)
        for step in range(1, levels):
            level_copy(part, step).start()

    def last_stage(part):
        slot = lax.rem(part, 2)
        for step in range(1, levels):
            level_copy(part, step).wait_recv()
        for matrix in range(2):
            sums = g.level_out[slot, level, matrix].astype(f32)
            for step in range(1, levels):
                sums += g.level_got[lax.rem(part, 4), level_before(step), matrix].astype(f32)
            g.total[part, place_last[matrix], matrix] = sums.astype(low)
            for step in range(1, snaps):
                last_copy(part, matrix, step).start()

    stages |= dict(half=half_stage, quarter=quarter_stage, level=level_stage, last=last_stage)

    def weight(part, matrix):
        return jnp.concatenate([g.all_w[part, matrix, place] for place in range(snaps)], axis=1)

    def add_products(part, rows):
        g.grid[rows, :] += dot_nt(g.act[rows, :], weight(part, 1))
        g.back[rows, :] += dot_nt(g.slope[rows, :], weight(part, 0))

    @pl.loop(0, parts)
    def _(part):
        def reach_in(point, also=True):
            for at_part in range(parts):
                if (point, at_part) in SCHEDULE:
                    pl.when((part == at_part) & also)(functools.partial(reach, (point, at_part)))

        def tile_rows(step):
            return pl.ds(pl.multiple_of(step * tile, tile), tile)

        fourth_copy(part).wait_recv()
        reach_in("begin")
        g.grad_bias[part] = jnp.zeros(g.grad_bias.shape[1:], f32)

        @pl.loop(0, tokens // tile)
        def _(step):
            rows = tile_rows(step)
            act, slope = gelu_both(dot_nn(g.normed[rows, :], weight(part, 0)) + g.bias[part])
            g.act[rows, :] = act.astype(low)
            slope = (dot_nn(g.cot_in[rows, :], weight(part, 1)) * slope).astype(low)
            g.slope[rows, :] = slope
            g.grad_bias[part] += fold(slope.astype(f32))
            for at_step in range(tokens // tile):
                reach_in("row_" + str(at_step), step == at_step)

        reach_in("rows")

        @pl.when(part >= 1)
        def _():
            for matrix in range(2):
                core_copy(part - 1, matrix).wait_send()

        shape = g.grads.shape[1:]
        g.grads[0] = dot_nn(g.normed_turned[...], g.slope[...]).astype(low).reshape(shape)
        core_copy(part, 0).start()
        g.grads[1] = dot_nn(g.cot_turned[...], g.act[...]).astype(low).reshape(shape)
        core_copy(part, 1).start()
        reach_in("grads")

        @pl.when(part < parts - 1)
        def _():
            @pl.loop(0, tokens // tile)
            def _(step):
                add_products(part, tile_rows(step))
                for at_step in range(tokens // tile):
                    reach_in("sum_" + str(at_step), step == at_step)

    g.folds[...] = jnp.zeros_like(g.folds)

    def second_back(rows):
        grad = g.back[rows, :]
        unit = g.unit_two[rows, :].astype(f32)
        cot = g.cot_in[rows, :].astype(f32)
        pulled = grad * g.gains[2:3, :]
        middle = jnp.mean(pulled, axis=-1, keepdims=True)
        slant = jnp.mean(pulled * unit, axis=-1, keepdims=True)
        total = cot + g.scale_two[rows, :] * (pulled - middle - unit * slant)
        g.back[rows, :] = total
        g.normed[rows, :] = total.astype(low)
        g.folds[2] += fold(grad * unit)
        g.folds[3] += fold(grad)
        g.folds[4] += fold(cot)

    loads["lon_it"].wait()
    for part in range(2):

        @pl.loop(0, half_tokens // short)
        def _(step, part=part):
            first_row = part * half_tokens + step * short
            add_products(parts - 1, pl.ds(pl.multiple_of(first_row, 16), short))

        reach("summed_" + str(part))
        half_strips(second_back, part)
        for step in range(1, group):
            block_copy(0, part, step).wait_send()
        to_blocks(g.lon_it_in[...], 1, part)
        reach("sent_three_" + str(part))
    reach("sent_three")

    def low_out(rows):
        store_columns("fields_cols", rows, g.grid[rows, :].astype(low))

    strips(low_out)
    out_copies = column_copies(g.fields_cols, g.out, g.fields_sem, True)
    for copy in out_copies:
        copy.start()
    reach("shown")
    loads["valid"].wait()
    loads["turn"].wait()
    weigh = sum(
        dot_nn(g.valid_in[:, row, :].astype(f32).astype(low), g.turn_in[row])
        for row in range(g.valid.shape[1])
    )
    places_each = weigh.shape[1]
    precise = lax.Precision.HIGHEST
    sums = [jnp.zeros((1, 128), f32), jnp.zeros((1, 128), f32)]
    for snap in range(g.valid.shape[0]):
        variables = g.grid[snap * places_each : (snap + 1) * places_each, 0:128]
        for index, value in enumerate((variables, variables * variables)):
            sums[index] += jnp.dot(
                weigh[snap : snap + 1, :], value, precision=precise, preferred_element_type=f32
            )

    reach("weighed")

    def dot_tn(left, right):
        return lax.dot_general(
            left, right, (((0,), (0,)), ((), ())), preferred_element_type=f32
        )

    def filter_rows(first, grad):
        g.pair_grad[...] = grad
        real = g.pair_grad[0:128, 0:128] + g.pair_grad[128:256, 128:256]
        imag = g.pair_grad[0:128, 128:256] - g.pair_grad[128:256, 0:128]
        g.filt_out[me_snap, first] = real[0:owned].astype(low)
        g.filt_out[me_snap, first + 1] = imag[0:owned].astype(low)

    for part in range(2):
        take_blocks(1, part)
        reach("got_three_" + str(part))
        rows = mode_half(part)
        spectra(g.grad_pre, f32, part)
        bend = jnp.tanh(g.pre_two[rows, :] / shrink_level)
        grad = (g.grad_pre[rows, :] * keep_half() * (bend * bend)).astype(low)
        g.grad_two[rows, :] = grad
        grad = dot_nt(grad, g.weight_two[...]) * gelu_both(g.pre_one[rows, :])[1]
        grad = grad.astype(low)
        g.grad_one[rows, :] = grad
        for step in range(1, group):
            row_copy(0, part, step).wait_send()
        to_rows(1, part, grids(dot_nt(grad, g.weight_one[...]).astype(low)))
        reach("sent_four_" + str(part))
    reach("sent_four")
    bias_one = jnp.sum(g.grad_one[...].astype(f32), axis=0, keepdims=True)
    bias_two = jnp.sum(g.grad_two[...].astype(f32), axis=0, keepdims=True)
    filter_rows(2, dot_tn(g.act_one[...], g.grad_two[...]))
    filter_rows(0, dot_tn(g.spectrum[...], g.grad_one[...]))

    def filter_copy(step):
        view = g.filt_out.at[me_snap]
        return send(view, view, (g.filt_s, g.filt_r), step, at(snap_after(step), me_sp))

    for step in range(1, snaps):
        filter_copy(step).start()


    reach("filters")

    loads["lon_ft"].wait()
    strip_pairs = strip // g.fields.shape[1]
    grad_view = g.grad_cols.reshape(2, tiles, strip, 128)

    def grad_copies(place, slot):
        pairs_out = pl.ds(place * strip_pairs, strip_pairs)
        return column_copies(
            g.grad_cols.at[slot], g.in_grad.at[pairs_out], g.grad_sem.at[slot], True
        )

    steps = half_tokens // strip
    for part in range(2):
        home_modes(1, part)
        reach("got_four_" + str(part))
        g.grid[half_rows(part), :] = g.back[half_rows(part), :] + dot_nn(
            g.lon_ft_in[...], g.home_low[part]
        )

        @pl.loop(0, steps)
        def _(step):
            place = part * steps + step
            slot = lax.rem(place, 2)

            @pl.when(place >= 2)
            def _():
                for copy in grad_copies(place, slot):
                    copy.wait()

            for at_row in range(0, strip, sub):
                rows = pl.ds(pl.multiple_of(place * strip + at_row, 16), sub)
                grad = g.grid[rows, :]
                unit = g.unit_one[rows, :].astype(f32)
                pulled = grad * g.gains[0:1, :]
                middle = jnp.mean(pulled, axis=-1, keepdims=True)
                slant = jnp.mean(pulled * unit, axis=-1, keepdims=True)
                total = g.back[rows, :] + g.scale_one[rows, :] * (pulled - middle - unit * slant)
                for tile_at in range(tiles):
                    grad_view[slot, tile_at, at_row : at_row + sub, :] = total[
                        :, tile_at * 128 : (tile_at + 1) * 128
                    ]
                g.folds[0] += fold(grad * unit)
                g.folds[1] += fold(grad)
            for copy in grad_copies(place, slot):
                copy.start()

        reach("done_" + str(part))

    g.grad_rows[...] = jnp.zeros_like(g.grad_rows)
    for index, row in enumerate((0, 1, 2, 3, 8)):
        g.grad_rows[row : row + 1, :] = jnp.sum(g.folds[index], axis=0, keepdims=True)
    flat = jnp.concatenate(
        [jnp.sum(g.grad_bias[part], axis=0, keepdims=True) for part in range(parts)], axis=1
    )
    for row in range(rows_small - 9):
        g.grad_rows[9 + row : 10 + row, :] = flat[:, row * channel : (row + 1) * channel]
    for block in range(group):
        g.tiles[block] = jnp.zeros(g.tiles.shape[1:], f32)
        g.tiles[block, :, 0:owned] = g.grad_rows[:, block * owned : (block + 1) * owned]
        g.tiles[block, 13:14, :] = sums[0]
        g.tiles[block, 14:15, :] = sums[1]

    def tile_copy(step):
        target = sp_after(step)
        return send(
            g.tiles.at[target], g.tiles_got.at[me_sp], (g.tile_s, g.tile_r), step, at(me_snap, target)
        )

    def snap_tile_copy(step):
        view = g.snap_tiles.at[me_snap]
        return send(view, view, (g.snap_tile_s, g.snap_tile_r), step, at(snap_after(step), me_sp))

    for step in range(1, group):
        tile_copy(step).start()
    reach("tiles")

    g.tiles_got[me_sp] = g.tiles[me_sp]
    for step in range(1, group):
        tile_copy(step).wait_recv()
    tile_sum = g.tiles_got[0]
    for sp in range(1, group):
        tile_sum += g.tiles_got[sp]
    g.snap_tiles[me_snap] = tile_sum
    g.snap_tiles[me_snap, 4:5, :] = bias_one[:, 0:128]
    g.snap_tiles[me_snap, 5:6, :] = bias_one[:, 128:256]
    g.snap_tiles[me_snap, 6:7, :] = bias_two[:, 0:128]
    g.snap_tiles[me_snap, 7:8, :] = bias_two[:, 128:256]
    for step in range(1, snaps):
        snap_tile_copy(step).start()

    for step in range(1, snaps):
        filter_copy(step).wait_recv()
    filter_sum = g.filt_out[0].astype(f32)
    for snap in range(1, snaps):
        filter_sum += g.filt_out[snap].astype(f32)
    g.grad_filt[...] = filter_sum
    for part in range(parts):
        for matrix in range(2):
            for step in range(1, snaps):
                last_copy(part, matrix, step).wait_recv()
    grads_out = pltpu.make_async_copy(g.total, g.grad_mlp, g.load_sem.at[3])
    grads_out.start()
    for step in range(1, snaps):
        snap_tile_copy(step).wait_recv()
    tile_sum = g.snap_tiles[0]
    for snap in range(1, snaps):
        tile_sum += g.snap_tiles[snap]
    g.grad_small[...] = tile_sum

    grads_out.wait()
    for copy in out_copies:
        copy.wait()
    for slot in range(2):
        for copy in grad_copies(0, slot):
            copy.wait()
    for step in range(1, group):
        small_copy(step).wait_send()
        for part in range(2):
            block_copy(1, part, step).wait_send()
            row_copy(1, part, step).wait_send()
        tile_copy(step).wait_send()
        for part in range(parts):
            first_copy(part, step).wait_send()
    for part in range(parts):
        if part < parts - 1:
            second_copy(part).wait_send()
            third_copy(part).wait_send()
        fourth_copy(part).wait_send()
    for matrix in range(2):
        core_copy(parts - 1, matrix).wait_send()
    for part in (parts - 2, parts - 1):
        for matrix in range(2):
            half_copy(part, matrix).wait_send()
            quarter_copy(part, matrix).wait_send()
        for step in range(1, levels):
            level_copy(part, step).wait_send()
    for step in range(1, snaps):
        filter_copy(step).wait_send()
        snap_tile_copy(step).wait_send()
        for part in range(parts):
            for matrix in range(2):
                last_copy(part, matrix, step).wait_send()


def block_pass(fields, cot, valid, kept, mlp, filt, small, snaps, group):
    snap_local, row_local, lon_total, channel = fields.shape
    tokens = snap_local * row_local * lon_total
    hidden = mlp.shape[2]
    lat_total = row_local * group
    modes = kept.shape[1] * group
    owned = channel // group
    width = 512
    parts = hidden // width
    levels = group // 2
    quarter = width // snaps
    low, f32 = jnp.bfloat16, jnp.float32
    half = width // 2
    half_snaps = snap_local // 2
    lon_f, lon_i = lon_matrix(lon_total, modes, half_snaps, row_local)

    def paired(array):
        return jnp.transpose(array, (0, 2, 1, 3)).reshape(-1, row_local, channel)

    lat_f = lat_matrix(lat_total, modes)
    pair = 2 * modes * row_local
    spread = half_snaps * row_local * 2 * modes
    inputs = dict(
        small=small,
        kept=kept.T,
        fields=paired(fields),
        lon_f=jnp.asarray(np.ascontiguousarray(lon_f.T)),
        filt=filt,
        lat_f=jnp.asarray(lat_f),
        lat_b=jnp.asarray(np.ascontiguousarray(lat_f.T)),
        cot=paired(cot),
        lon_i=jnp.asarray(lon_i),
        valid=valid,
        turn=jnp.asarray(lon_turn(lon_total, row_local)),
        lon_it=jnp.asarray(np.ascontiguousarray(lon_i.T)),
        lon_ft=jnp.asarray(lon_f),
        mlp=mlp,
    )
    outputs = dict(
        out=jax.ShapeDtypeStruct((tokens // row_local, row_local, channel), low),
        in_grad=jax.ShapeDtypeStruct((tokens // row_local, row_local, channel), f32),
        grad_mlp=jax.ShapeDtypeStruct((parts, snaps, 2, owned, quarter), low),
        grad_filt=jax.ShapeDtypeStruct((4, owned, 128), f32),
        grad_small=jax.ShapeDtypeStruct((16, 128), f32),
    )
    vmem = pltpu.VMEM
    dma = pltpu.SemaphoreType.DMA
    scratch = {
        name + "_in": vmem(value.shape, value.dtype)
        for name, value in inputs.items()
        if name not in ("mlp", "fields", "cot")
    }
    tiles = channel // 128
    cols = (tiles, tokens // row_local, row_local, 128)
    strip = divisor(tokens // 2, 48, 144)
    scratch |= dict(
        mlp_part=vmem((2, 2, owned, width), f32),
        fields_cols=vmem(cols, low),
        cot_cols=vmem(cols, low),
        grad_cols=vmem((2, tiles, strip // row_local, row_local, 128), f32),
        grad_sem=dma((2, tiles)),
        fields_sem=dma((tiles,)),
        cot_sem=dma((tiles,)),
        cot_in=vmem((tokens, channel), low),
        grid=vmem((tokens, channel), f32),
        back=vmem((tokens, channel), f32),
        normed=vmem((tokens, channel), low),
        normed_turned=vmem((channel, tokens), low),
        cot_turned=vmem((channel, tokens), low),
        unit_one=vmem((tokens, channel), low),
        unit_two=vmem((tokens, channel), low),
        scale_one=vmem((tokens, 1), f32),
        scale_two=vmem((tokens, 1), f32),
        own_small=vmem((16 + kept.shape[0], 128), f32),
        all_small=vmem((group, 16 + kept.shape[0], 128), f32),
        gains=vmem((16, channel), f32),
        keep=vmem((lat_total * modes, 128), f32),
        own_w=vmem((parts, 2, snaps, owned, quarter), low),
        all_w=vmem((parts, 2, snaps, channel, quarter), low),
        modes=vmem((2, group, half_snaps * pair * 3 // 4, 128), low),
        modes_got=vmem((2, group, half_snaps * pair * 3 // 4, 128), low),
        rows_out=vmem((2, group, half_snaps * pair * 3 // 4, 128), low),
        rows_got=vmem((2, group, half_snaps * pair * 3 // 4, 128), low),
        arrived=vmem((snap_local, pair * group, 128), low),
        gathered=vmem((2, spread, channel), f32),
        home_low=vmem((2, spread, channel), low),
        weight_one=vmem((256, 256), low),
        weight_two=vmem((256, 256), low),
        spectrum=vmem((snap_local * lat_total * modes, 256), low),
        pre_one=vmem((snap_local * lat_total * modes, 256), f32),
        act_one=vmem((snap_local * lat_total * modes, 256), low),
        pre_two=vmem((snap_local * lat_total * modes, 256), f32),
        grad_pre=vmem((snap_local * lat_total * modes, 256), f32),
        grad_two=vmem((snap_local * lat_total * modes, 256), low),
        grad_one=vmem((snap_local * lat_total * modes, 256), low),
        folds=vmem((5, 8, channel), f32),
        pair_grad=vmem((256, 256), f32),
        act=vmem((tokens, width), low),
        slope=vmem((tokens, width), low),
        bias=vmem((parts, 1, width), f32),
        grad_bias=vmem((parts, 8, width), f32),
        grad_rows=vmem((16, channel), f32),
        grads=vmem((2, levels, 2, owned, width), low),
        core_got=vmem((2, 2, levels, owned, width), low),
        half_out=vmem((2, 2, 2, levels, owned, half), low),
        half_got=vmem((4, 2, levels, owned, half), low),
        quarter_out=vmem((2, 2, 2, levels, owned, quarter), low),
        quarter_got=vmem((2, 2, levels, owned, quarter), low),
        level_out=vmem((2, levels, 2, owned, quarter), low),
        level_got=vmem((4, levels, 2, owned, quarter), low),
        total=vmem((parts, snaps, 2, owned, quarter), low),
        filt_out=vmem((snaps, 4, owned, 128), low),
        tiles=vmem((group, 16, 128), f32),
        tiles_got=vmem((group, 16, 128), f32),
        snap_tiles=vmem((snaps, 16, 128), f32),
        load_sem=dma((len(inputs) + 1,)),
    )
    for name, shape in dict(
        small=(group,),
        first=(parts, group),
        second=(parts,),
        third=(parts,),
        fourth=(parts,),
        block=(2, 2, group),
        row=(2, 2, group),
        core=(2, 2),
        half=(4, 2),
        quarter=(2, 2),
        level=(4, levels),
        last=(parts, 2, snaps),
        filt=(snaps,),
        tile=(group,),
        snap_tile=(snaps,),
    ).items():
        scratch[name + "_s"] = dma(shape)
        scratch[name + "_r"] = dma(shape)
    names = [*inputs, *outputs, *scratch]
    far = pl.BlockSpec(memory_space=pl.ANY)
    near = pl.BlockSpec(memory_space=pltpu.VMEM)
    results = pl.pallas_call(
        functools.partial(block_body, names, (snaps, group, parts, width)),
        in_specs=[far] * len(inputs),
        out_specs=[far, far, far, near, near],
        out_shape=list(outputs.values()),
        scratch_shapes=list(scratch.values()),
        compiler_params=pltpu.CompilerParams(
            collective_id=0, has_side_effects=True, vmem_limit_bytes=VMEM_LIMIT
        ),
        cost_estimate=pl.CostEstimate(
            flops=12 * tokens * channel * hidden,
            bytes_accessed=4 * hidden * channel,
            transcendentals=tokens * hidden,
        ),
        name="block_pass",
    )(*inputs.values())
    return results


def step_body(names, positions, *refs):
    g = Refs()
    for name, ref in zip(names, refs, strict=True):
        setattr(g, name, ref)
    parts, snaps = g.grad_mlp.shape[:2]
    quarter = g.grad_mlp.shape[4]
    width = snaps * quarter
    moments = ("w", "m", "v")
    results = ("new", "first", "second", "copy")

    pieces = g.far_sem.shape[2]
    ends = ((g.out, g.out_near, g.out_o), (g.in_grad, g.in_grad_near, g.in_grad_o))

    def passing(kind, piece, leg):
        size = ends[kind][0].shape[0] // pieces
        rows = pl.ds(piece * size, size)
        return pltpu.make_async_copy(
            ends[kind][leg].at[rows], ends[kind][leg + 1].at[rows], g.far_sem.at[leg, kind, piece]
        )

    through = [(kind, piece) for kind in range(2) for piece in range(pieces)]

    def part_cols(part):
        return pl.ds(part * width, width)

    def load(part):
        near = [
            pltpu.make_async_copy(
                getattr(g, "mlp_" + kind).at[:, :, part_cols(part)],
                g.near.at[index, part],
                g.near_sem.at[index, part],
            )
            for index, kind in enumerate(moments)
        ]
        near.append(
            pltpu.make_async_copy(g.grad_mlp.at[part], g.grad_near.at[part], g.near_sem.at[3, part])
        )
        return near

    def store(part):
        copies = [
            pltpu.make_async_copy(
                g.near.at[index, part],
                getattr(g, "mlp_" + kind).at[:, :, part_cols(part)],
                g.back_sem.at[index, part],
            )
            for index, kind in enumerate(results[:3])
        ]
        copies.append(
            pltpu.make_async_copy(
                g.low_near.at[part], g.mlp_copy.at[:, :, part_cols(part)], g.back_sem.at[3, part]
            )
        )
        return copies

    coming = [load(part) for part in range(parts)]
    going = [store(part) for part in range(parts)]
    shares = [through[part::parts] for part in range(parts)]
    for part in range(parts):
        for copy in coming[part]:
            copy.start()
        for each in shares[part]:
            passing(*each, 0).start()

    def put(prefix, values):
        for kind, value in zip(results, values, strict=True):
            getattr(g, prefix + kind)[...] = value

    owned = g.filt_w.shape[2]
    put(
        "filt_",
        adamw(g.filt_w[...], g.filt_m[...], g.filt_v[...], g.grad_filt[:, :, 0:owned], rate_filter),
    )
    rows = g.small_w.shape[0]
    put(
        "small_",
        adamw(
            g.small_w[...], g.small_m[...], g.small_v[...], g.grad_small[0:rows, 0:owned], rate_small
        ),
    )
    totals = g.grad_small[rows : rows + 2, 0 : g.run.shape[1]]
    g.stats[...] = stat_decay * g.run[...] + (1.0 - stat_decay) * totals / positions

    for part in range(parts):
        for copy in coming[part]:
            copy.wait()

        for snap in range(snaps):
            cols = slice(snap * quarter, (snap + 1) * quarter)
            where = (slice(None), slice(None), cols)
            now = [g.near[(index, part, *where)] for index in range(3)]
            grad = g.grad_near[part, snap].astype(jnp.float32)
            values = adamw(*now, grad, rate_mlp)
            for index in range(3):
                g.near[(index, part, *where)] = values[index]
            g.low_near[(part, *where)] = values[3]
        for copy in going[part]:
            copy.start()
        for each in shares[part]:
            passing(*each, 0).wait()
            passing(*each, 1).start()
    for each in through:
        passing(*each, 1).wait()
    for part in range(parts):
        for copy in going[part]:
            copy.wait()


def step_pass(shown, grads, masters, run_stats, positions):
    grad_mlp, grad_filt, grad_small = grads
    mlp, filt, small = masters
    parts = grad_mlp.shape[0]
    width = mlp[0].shape[2] // parts
    f32, low = jnp.float32, jnp.bfloat16
    far = pl.BlockSpec(memory_space=pltpu.HBM)
    near = pl.BlockSpec(memory_space=pltpu.VMEM)
    inputs = dict(out=shown[0], in_grad=shown[1], grad_mlp=grad_mlp)
    inputs |= dict(zip(("mlp_w", "mlp_m", "mlp_v"), mlp, strict=True))
    far_in = len(inputs)
    inputs |= dict(grad_filt=grad_filt, grad_small=grad_small)
    inputs |= dict(zip(("filt_w", "filt_m", "filt_v"), filt, strict=True))
    inputs |= dict(zip(("small_w", "small_m", "small_v"), small, strict=True))
    inputs |= dict(run=run_stats)
    results = (("new", f32), ("first", f32), ("second", f32), ("copy", low))
    outputs = {
        name + "_o": jax.ShapeDtypeStruct(array.shape, array.dtype)
        for name, array in zip(("out", "in_grad"), shown, strict=True)
    }
    outputs |= {"mlp_" + kind: jax.ShapeDtypeStruct(mlp[0].shape, dt) for kind, dt in results}
    far_out = len(outputs)
    outputs |= {"filt_" + kind: jax.ShapeDtypeStruct(filt[0].shape, dt) for kind, dt in results}
    outputs |= {"small_" + kind: jax.ShapeDtypeStruct(small[0].shape, dt) for kind, dt in results}
    outputs |= dict(stats=jax.ShapeDtypeStruct(run_stats.shape, f32))
    scratch = dict(
        near=pltpu.VMEM((3, parts, 2, mlp[0].shape[1], width), f32),
        grad_near=pltpu.VMEM(grad_mlp.shape, low),
        low_near=pltpu.VMEM((parts, 2, mlp[0].shape[1], width), low),
        near_sem=pltpu.SemaphoreType.DMA((4, parts)),
        back_sem=pltpu.SemaphoreType.DMA((4, parts)),
        out_near=pltpu.VMEM(shown[0].shape, low),
        in_grad_near=pltpu.VMEM(shown[1].shape, f32),
        far_sem=pltpu.SemaphoreType.DMA((2, 2, divisor(shown[0].shape[0], 1, 4))),
    )
    return pl.pallas_call(
        functools.partial(step_body, [*inputs, *outputs, *scratch], positions),
        in_specs=[far] * far_in + [near] * (len(inputs) - far_in),
        out_specs=[far] * far_out + [near] * (len(outputs) - far_out),
        out_shape=list(outputs.values()),
        scratch_shapes=list(scratch.values()),
        compiler_params=pltpu.CompilerParams(vmem_limit_bytes=VMEM_LIMIT),
        name="step_pass",
    )(*inputs.values())


def per_device_blocks(
    fields,
    cotangent,
    valid_mask,
    kept_modes,
    mlp_master,
    mlp_first,
    mlp_second,
    filter_master,
    filter_first,
    filter_second,
    small_master,
    small_first,
    small_second,
    run_stats,
):
    snaps, group = lax.axis_size("snap"), lax.axis_size("sp")
    out, in_grad, *grads = block_pass(
        fields, cotangent, valid_mask, kept_modes, mlp_master, filter_master, small_master, snaps, group
    )
    snap_local, row_local, lon_total, channel = fields.shape
    positions = snap_local * snaps * row_local * group * lon_total
    out, in_grad, *stepped = step_pass(
        (out, in_grad),
        grads,
        (
            (mlp_master, mlp_first, mlp_second),
            (filter_master, filter_first, filter_second),
            (small_master, small_first, small_second),
        ),
        run_stats,
        positions,
    )
    rows_apart = (snap_local, lon_total, row_local, channel)
    out, in_grad = [
        jnp.transpose(array.reshape(rows_apart), (0, 2, 1, 3)) for array in (out, in_grad)
    ]
    return (out, in_grad, *stepped)


def per_device(*arrays):
    group, snaps = lax.axis_size("sp"), lax.axis_size("snap")
    channel, hidden = arrays[0].shape[3], arrays[4].shape[2]
    by_block = group == BLOCKS and snaps == 4 and arrays[3].shape[1] == 1
    if by_block and hidden == 6 * 512 and channel // group <= 128 and channel % (16 * group) == 0:
        return per_device_blocks(*arrays)
    return per_device_modes(*arrays)


def solution(mesh):
    return jax.shard_map(
        per_device,
        mesh=mesh,
        in_specs=(
            P("snap", "sp", None, None),
            P("snap", "sp", None, None),
            P("snap", "sp", None),
            P(None, "sp"),
            P(None, "sp", None),
            P(None, "sp", None),
            P(None, "sp", None),
            P(None, "sp", None),
            P(None, "sp", None),
            P(None, "sp", None),
            P(None, "sp"),
            P(None, "sp"),
            P(None, "sp"),
            P(),
        ),
        out_specs=(
            P("snap", "sp", None, None),
            P("snap", "sp", None, None),
            P(None, "sp", None),
            P(None, "sp", None),
            P(None, "sp", None),
            P(None, "sp", None),
            P(None, "sp", None),
            P(None, "sp", None),
            P(None, "sp", None),
            P(None, "sp", None),
            P(None, "sp"),
            P(None, "sp"),
            P(None, "sp"),
            P(None, "sp"),
            P(),
        ),
        check_vma=False,
    )
```

```python
import functools
import math

import jax
import jax.numpy as jnp
import ml_dtypes
import numpy as np
from jax import lax
from jax.experimental import pallas as pl
from jax.experimental.pallas import tpu as pltpu
from jax.sharding import PartitionSpec as P

BLOCKS = 8
NVAR = 20
STEP = 10
VMEM_LIMIT = 63 * 1024 * 1024


eps_norm = 1e-06
shrink_level = 0.01
beta_one = 0.5
beta_two = 0.5
adam_eps = 1e-08
decay_rate = 0.01
rate_mlp = 0.03
rate_filter = 0.1
rate_small = 0.2
stat_decay = 0.5


def layer_norm(values, gain_vec, shift_vec):
    centred = values - jnp.mean(values, axis=-1, keepdims=True)
    spread = jnp.mean(centred * centred, axis=-1, keepdims=True)
    return centred * lax.rsqrt(spread + eps_norm) * gain_vec + shift_vec


def shrink(values):
    return values - shrink_level * jnp.tanh(values / shrink_level)


def lon_tables(lon_total, mode_total):
    places = jnp.arange(lon_total, dtype=jnp.int32)
    orders = jnp.arange(mode_total, dtype=jnp.int32)
    angles = (places[:, None] * orders[None, :] % lon_total).astype(jnp.float32) * (
        2.0 * math.pi / lon_total
    )
    scaling = 1.0 / math.sqrt(lon_total)
    forward_tab = jnp.stack([jnp.cos(angles), -jnp.sin(angles)], axis=1) * scaling
    doubling = jnp.where(orders == 0, 1.0, 2.0).astype(jnp.float32)[:, None]
    inverse_tab = (
        jnp.stack([jnp.cos(angles).T * doubling, -jnp.sin(angles).T * doubling], axis=0) * scaling
    )
    return (forward_tab.astype(jnp.bfloat16), inverse_tab.astype(jnp.bfloat16))


def lat_table(lat_total):
    places = jnp.arange(lat_total, dtype=jnp.int32)
    angles = (places[:, None] * places[None, :] % lat_total).astype(jnp.float32) * (
        2.0 * math.pi / lat_total
    )
    cosine = jnp.cos(angles)
    sine_part = jnp.sin(angles)
    upper_rows = jnp.stack([cosine, sine_part], axis=1)
    bottom = jnp.stack([-sine_part, cosine], axis=1)
    return (jnp.stack([upper_rows, bottom], axis=0) / math.sqrt(lat_total)).astype(jnp.bfloat16)


def complex_pair(real_part, imag_part):
    return jnp.stack([jnp.stack([real_part, -imag_part]), jnp.stack([imag_part, real_part])])


gelu_scale = math.sqrt(2.0 / math.pi)
gelu_cubic = 0.044715


def gelu_both(value):
    bend = (gelu_scale * gelu_cubic) * (value * value)
    turn = jnp.tanh(value * (gelu_scale + bend))
    half = 0.5 + 0.5 * turn
    slope = half * (1.0 + (value * (1.0 - turn)) * (gelu_scale + 3.0 * bend))
    return value * half, slope


def dot_nt(left, right):
    return lax.dot_general(
        left, right, (((1,), (1,)), ((), ())), preferred_element_type=jnp.float32
    )


def dot_nn(left, right):
    return jnp.dot(left, right, preferred_element_type=jnp.float32)


def divisor(total, unit, most):
    return max(size for size in range(unit, most + 1, unit) if total % size == 0)


def mlp_body(
    tile,
    normed_ref,
    cot_ref,
    up_ref,
    down_ref,
    bias_ref,
    out_ref,
    back_ref,
    grad_up_ref,
    grad_down_ref,
    grad_bias_ref,
    normed_turned,
    cot_turned,
    act_ref,
    slope_ref,
):
    tokens = normed_ref.shape[0]

    @pl.when(pl.program_id(0) == 0)
    def _():
        normed_turned[...] = normed_ref[...].T
        cot_turned[...] = cot_ref[...].T
        out_ref[...] = jnp.zeros_like(out_ref)
        back_ref[...] = jnp.zeros_like(back_ref)

    grad_bias_ref[...] = jnp.zeros_like(grad_bias_ref)

    @pl.loop(0, tokens // tile)
    def _(step):
        rows = pl.ds(pl.multiple_of(step * tile, tile), tile)
        act, slope = gelu_both(dot_nn(normed_ref[rows, :], up_ref[...]) + bias_ref[...])
        act = act.astype(jnp.bfloat16)
        slope = (dot_nn(cot_ref[rows, :], down_ref[...]) * slope).astype(jnp.bfloat16)
        act_ref[rows, :] = act
        slope_ref[rows, :] = slope
        grad_bias_ref[...] += jnp.sum(slope.astype(jnp.float32), axis=0, keepdims=True)
        out_ref[rows, :] += dot_nt(act, down_ref[...])
        back_ref[rows, :] += dot_nt(slope, up_ref[...])

    grad_up_ref[...] = dot_nn(normed_turned[...], slope_ref[...]).astype(grad_up_ref.dtype)
    grad_down_ref[...] = dot_nn(cot_turned[...], act_ref[...]).astype(grad_down_ref.dtype)


def mlp_pass(normed, cot, weights, bias):
    tokens, channel = normed.shape
    hidden = weights.shape[2]
    width = divisor(hidden, 128, 512)
    tile = divisor(tokens, 16, 480)
    whole = pl.BlockSpec((tokens, channel), lambda j: (0, 0))
    block = pl.BlockSpec((channel, width), lambda j: (0, j))
    line = pl.BlockSpec((1, width), lambda j: (0, j))
    part = lambda which: pl.BlockSpec((None, channel, width), lambda j: (which, 0, j))
    total = jax.ShapeDtypeStruct((tokens, channel), jnp.float32)
    grads = jax.ShapeDtypeStruct((channel, hidden), jnp.bfloat16)
    return pl.pallas_call(
        functools.partial(mlp_body, tile),
        grid=(hidden // width,),
        in_specs=[whole, whole, part(0), part(1), line],
        out_specs=[whole, whole, block, block, line],
        out_shape=[total, total, grads, grads, jax.ShapeDtypeStruct((1, hidden), jnp.float32)],
        scratch_shapes=[
            pltpu.VMEM((channel, tokens), jnp.bfloat16),
            pltpu.VMEM((channel, tokens), jnp.bfloat16),
            pltpu.VMEM((tokens, width), jnp.bfloat16),
            pltpu.VMEM((tokens, width), jnp.bfloat16),
        ],
        compiler_params=pltpu.CompilerParams(vmem_limit_bytes=56 * 1024 * 1024),
        cost_estimate=pl.CostEstimate(
            flops=12 * tokens * channel * hidden,
            bytes_accessed=8 * channel * hidden + 12 * tokens * channel,
            transcendentals=tokens * hidden,
        ),
        name="mlp_pass",
    )(normed, cot, weights, weights, bias)


def spectral_front(arrived, lat_fwd, first_pair, second_pair, bias_one, bias_two):
    spectrum = jnp.einsum(
        "pkqr,nrqmd->nkpmd", lat_fwd, arrived, preferred_element_type=jnp.float32
    ).astype(jnp.bfloat16)
    snap_local, lat_total, pair_count, mode_local, channel = spectrum.shape
    blocked = spectrum.reshape(
        snap_local, lat_total, pair_count, mode_local, BLOCKS, channel // BLOCKS
    )
    pre_one = (
        jnp.einsum("nkqmbi,pqbio->nkpmbo", blocked, first_pair, preferred_element_type=jnp.float32)
        + bias_one
    )
    act_one = jax.nn.gelu(pre_one).astype(jnp.bfloat16)
    pre_two = (
        jnp.einsum("nkqmbi,pqbio->nkpmbo", act_one, second_pair, preferred_element_type=jnp.float32)
        + bias_two
    )
    return (blocked, pre_one, act_one, pre_two)


def adamw(master, first_mom, second_mom, gradient, step_rate):
    first_next = beta_one * first_mom + (1.0 - beta_one) * gradient
    second_next = beta_two * second_mom + (1.0 - beta_two) * gradient * gradient
    fix_one = 1.0 / (1.0 - beta_one**STEP)
    fix_two = 1.0 / (1.0 - beta_two**STEP)
    direction = first_next * fix_one / (jnp.sqrt(second_next * fix_two) + adam_eps)
    master_next = master - step_rate * (direction + decay_rate * master)
    return (master_next, first_next, second_next, master_next.astype(jnp.bfloat16))


def per_device_modes(
    fields,
    cotangent,
    valid_mask,
    kept_modes,
    mlp_master,
    mlp_first,
    mlp_second,
    filter_master,
    filter_first,
    filter_second,
    small_master,
    small_first,
    small_second,
    run_stats,
):
    group_size = lax.axis_size("sp")
    snap_local, row_local, lon_total, channel = fields.shape
    lat_total = row_local * group_size
    mode_local = kept_modes.shape[1]
    mode_total = mode_local * group_size
    block_width = channel // BLOCKS
    lon_fwd, lon_inv = lon_tables(lon_total, mode_total)
    lat_fwd = lat_table(lat_total)
    mlp_w, filt_w, small_w = (
        lax.all_gather(mlp_master.astype(jnp.bfloat16), "sp", axis=1, tiled=True),
        lax.all_gather(filter_master.astype(jnp.bfloat16), "sp", axis=1, tiled=True),
        lax.all_gather(small_master.astype(jnp.bfloat16), "sp", axis=1, tiled=True),
    )
    small_f = small_w.astype(jnp.float32)
    weights = filt_w.reshape(4, BLOCKS, block_width, block_width)
    first_pair = complex_pair(weights[0], weights[1])
    second_pair = complex_pair(weights[2], weights[3])
    bias_one = small_f[4:6].reshape(2, 1, BLOCKS, block_width)
    bias_two = small_f[6:8].reshape(2, 1, BLOCKS, block_width)
    fields_float = fields.astype(jnp.float32)
    normed, norm_pull = jax.vjp(layer_norm, fields_float, small_f[0], small_f[1])
    normed_low = normed.astype(jnp.bfloat16)
    spec_lon = jnp.einsum(
        "nrld,lqm->nrqmd", normed_low, lon_fwd, preferred_element_type=jnp.float32
    ).astype(jnp.bfloat16)
    arrived = lax.all_to_all(spec_lon, "sp", split_axis=3, concat_axis=1, tiled=True)
    spectral = spectral_front(arrived, lat_fwd, first_pair, second_pair, bias_one, bias_two)
    keep_mask = kept_modes.astype(jnp.float32)[None, :, None, :, None, None]
    masked = (shrink(spectral[3]) * keep_mask).astype(jnp.bfloat16)
    masked = masked.reshape(snap_local, lat_total, 2, mode_local, channel)
    returned = jnp.einsum(
        "pkqr,nkpmd->nrqmd", lat_fwd, masked, preferred_element_type=jnp.float32
    ).astype(jnp.bfloat16)
    home_modes = lax.all_to_all(returned, "sp", split_axis=1, concat_axis=3, tiled=True)
    filtered = jnp.einsum(
        "nrqmd,qml->nrld", home_modes, lon_inv, preferred_element_type=jnp.float32
    )
    mixture = fields_float + normed + filtered
    normed_two, norm_two_pull = jax.vjp(layer_norm, mixture, small_f[2], small_f[3])
    normed_two_low = normed_two.astype(jnp.bfloat16)
    tokens = snap_local * row_local * lon_total
    passed = mlp_pass(
        normed_two_low.reshape(tokens, channel),
        cotangent.reshape(tokens, channel),
        mlp_w,
        small_f[9:].reshape(1, -1),
    )
    output = mixture + passed[0].reshape(mixture.shape) + small_f[8]
    weight_mask = valid_mask.astype(jnp.float32)[..., None]
    variables = output[..., :NVAR]
    local_sums = jnp.stack(
        [
            jnp.sum(weight_mask * variables, axis=(0, 1, 2)),
            jnp.sum(weight_mask * variables * variables, axis=(0, 1, 2)),
        ]
    )
    total_sums = lax.psum(local_sums, ("snap", "sp"))
    positions = snap_local * lax.axis_size("snap") * lat_total * lon_total
    stats_new = stat_decay * run_stats + (1.0 - stat_decay) * total_sums / positions
    cot_float = cotangent.astype(jnp.float32)
    grad_normed_two = passed[1].reshape(mixture.shape)
    grad_bias_hidden = passed[4]
    grad_mix_norm, grad_gain_two, grad_shift_two = norm_two_pull(grad_normed_two)
    grad_mixture = cot_float + grad_mix_norm
    grad_bias_out = jnp.sum(cot_float, axis=(0, 1, 2))
    grad_filtered = grad_mixture.astype(jnp.bfloat16)
    grad_home = jnp.einsum(
        "nrld,qml->nrqmd", grad_filtered, lon_inv, preferred_element_type=jnp.float32
    ).astype(jnp.bfloat16)
    grad_returned = lax.all_to_all(grad_home, "sp", split_axis=3, concat_axis=1, tiled=True)
    grad_masked = jnp.einsum(
        "pkqr,nrqmd->nkpmd", lat_fwd, grad_returned, preferred_element_type=jnp.float32
    )
    arrived_again = lax.all_to_all(spec_lon, "sp", split_axis=3, concat_axis=1, tiled=True)
    used_front = spectral_front(arrived_again, lat_fwd, first_pair, second_pair, bias_one, bias_two)
    blocked, pre_one, act_one, pre_two = used_front
    grad_two = jax.vjp(shrink, pre_two)[1](grad_masked.reshape(pre_two.shape) * keep_mask)[
        0
    ].astype(jnp.bfloat16)
    grad_bias_two = jnp.sum(grad_two.astype(jnp.float32), axis=(0, 1, 3))
    grad_second = jnp.einsum(
        "nkqmbi,nkpmbo->pqbio", act_one, grad_two, preferred_element_type=jnp.float32
    )
    grad_act = jnp.einsum(
        "nkpmbo,pqbio->nkqmbi", grad_two, second_pair, preferred_element_type=jnp.float32
    )
    grad_one = jax.vjp(jax.nn.gelu, pre_one)[1](grad_act)[0].astype(jnp.bfloat16)
    grad_bias_one = jnp.sum(grad_one.astype(jnp.float32), axis=(0, 1, 3))
    grad_first = jnp.einsum(
        "nkqmbi,nkpmbo->pqbio", blocked, grad_one, preferred_element_type=jnp.float32
    )
    grad_spectrum = jnp.einsum(
        "nkpmbo,pqbio->nkqmbi", grad_one, first_pair, preferred_element_type=jnp.float32
    ).astype(jnp.bfloat16)
    grad_spectrum = grad_spectrum.reshape(snap_local, lat_total, 2, mode_local, channel)
    grad_lon = jnp.einsum(
        "pkqr,nkpmd->nrqmd", lat_fwd, grad_spectrum, preferred_element_type=jnp.float32
    ).astype(jnp.bfloat16)
    grad_rows = lax.all_to_all(grad_lon, "sp", split_axis=1, concat_axis=3, tiled=True)
    grad_normed = grad_mixture + jnp.einsum(
        "nrqmd,lqm->nrld", grad_rows, lon_fwd, preferred_element_type=jnp.float32
    )
    grad_field_norm, grad_gain_one, grad_shift_one = norm_pull(grad_normed)
    input_grad = grad_mixture + grad_field_norm
    grad_filter = jnp.stack(
        [
            grad_first[0, 0] + grad_first[1, 1],
            grad_first[1, 0] - grad_first[0, 1],
            grad_second[0, 0] + grad_second[1, 1],
            grad_second[1, 0] - grad_second[0, 1],
        ]
    ).reshape(4, channel, block_width)
    grad_small = jnp.concatenate(
        [
            jnp.stack([grad_gain_one, grad_shift_one, grad_gain_two, grad_shift_two]),
            grad_bias_one.reshape(2, channel),
            grad_bias_two.reshape(2, channel),
            grad_bias_out[None, :],
            grad_bias_hidden.reshape(-1, channel),
        ],
        axis=0,
    )
    shares = (
        jnp.stack([
            lax.psum_scatter(part, "sp", scatter_dimension=0, tiled=True) for part in passed[2:4]
        ]),
        lax.psum_scatter(grad_filter, "sp", scatter_dimension=1, tiled=True),
        lax.psum_scatter(grad_small, "sp", scatter_dimension=1, tiled=True),
    )
    owned = (
        lax.psum(shares[0].astype(jnp.bfloat16), "snap").astype(jnp.float32),
        lax.psum(shares[1].astype(jnp.bfloat16), "snap").astype(jnp.float32),
        lax.psum(shares[2].astype(jnp.bfloat16), "snap").astype(jnp.float32),
    )
    mlp_new, mlp_first_new, mlp_second_new, mlp_copy = adamw(
        mlp_master, mlp_first, mlp_second, owned[0], rate_mlp
    )
    filter_new, filter_first_new, filter_second_new, filter_copy = adamw(
        filter_master, filter_first, filter_second, owned[1], rate_filter
    )
    small_new, small_first_new, small_second_new, small_copy = adamw(
        small_master, small_first, small_second, owned[2], rate_small
    )
    return (
        output.astype(jnp.bfloat16),
        input_grad,
        mlp_new,
        mlp_first_new,
        mlp_second_new,
        mlp_copy,
        filter_new,
        filter_first_new,
        filter_second_new,
        filter_copy,
        small_new,
        small_first_new,
        small_second_new,
        small_copy,
        stats_new,
    )


FIRST, SECOND, THIRD, FOURTH, HALF, QUARTER, LEVEL, LAST = range(8)
SCHEDULE = {
    "a": [(FIRST, 0), (FIRST, 1)],
    "c1": [(SECOND, 0)],
    "e": [(SECOND, 1), (FIRST, 2)],
    "f0": [(THIRD, 0)],
    "f1": [(THIRD, 1), (FIRST, 3)],
    "g": [(FIRST, 4), (FIRST, 5)],
    "i1": [(FOURTH, 0), (SECOND, 2)],
    "j": [(SECOND, 3)],
    ("k", 0): [(FOURTH, 1)],
    ("l", 0): [(THIRD, 2), (SECOND, 4)],
    ("m", 0): [(THIRD, 3)],
    ("n", 0): [(HALF, 0), (THIRD, 4)],
    ("l", 1): [(FOURTH, 2)],
    ("n", 1): [(FOURTH, 3)],
    ("l", 2): [(QUARTER, 0), (HALF, 1)],
    ("k", 3): [(LEVEL, 0), (HALF, 2), (FOURTH, 4), (FOURTH, 5)],
    ("l", 3): [(QUARTER, 1)],
    ("n", 3): [(LAST, 0), (LEVEL, 1)],
    ("k", 4): [(QUARTER, 2)],
    ("l", 4): [(HALF, 3)],
    ("m", 4): [(LEVEL, 2)],
    ("k", 5): [(QUARTER, 3), (HALF, 4)],
    ("l", 5): [(LAST, 1)],
    ("m", 5): [(LEVEL, 3)],
    "o0": [(QUARTER, 4)],
    "p0": [(HALF, 5)],
    "p1": [(LAST, 2), (LEVEL, 4)],
    "s": [(QUARTER, 5)],
    "u1": [(LAST, 3)],
    "w": [(LAST, 4), (LEVEL, 5)],
    "z": [(LAST, 5)],
}


def lon_matrix(lon_total, mode_total, snaps, rows):
    places = np.arange(lon_total)
    orders = np.arange(mode_total)
    angles = (places[:, None] * orders[None, :] % lon_total) * (2.0 * math.pi / lon_total)
    doubling = np.where(orders == 0, 1.0, 2.0)
    scaling = 1.0 / math.sqrt(lon_total)
    forward = np.stack([np.cos(angles), -np.sin(angles)], axis=1) * scaling
    inverse = forward * doubling

    def spread(table):
        table = np.einsum(
            "ab,lx,rs->alrbsx", np.eye(snaps), table.reshape(lon_total, -1), np.eye(rows)
        )
        return table.reshape(snaps * lon_total * rows, -1).astype(ml_dtypes.bfloat16)

    return spread(forward), spread(inverse)


def lon_turn(lon_total, rows):
    turn = np.einsum("lk,rs->rlks", np.eye(lon_total), np.eye(rows))
    return turn.reshape(rows, lon_total, lon_total * rows).astype(ml_dtypes.bfloat16)


def lat_matrix(lat_total, mode_total):
    places = np.arange(lat_total)
    angles = (places[:, None] * places[None, :] % lat_total) * (2.0 * math.pi / lat_total)
    cosine, sine = np.cos(angles), np.sin(angles)
    table = np.stack([np.stack([cosine, sine], axis=1), np.stack([-sine, cosine], axis=1)])
    table = np.einsum("pkqr,ab->pakrqb", table / math.sqrt(lat_total), np.eye(mode_total))
    size = 2 * lat_total * mode_total
    return table.reshape(size, size).astype(ml_dtypes.bfloat16)


class Refs:
    pass


def block_body(names, sizes, *refs):
    g = Refs()
    for name, ref in zip(names, refs, strict=True):
        setattr(g, name, ref)
    snaps, group, parts, width = sizes
    levels = group // 2
    tokens = g.fields.shape[0] * g.fields.shape[1]
    channel = g.fields.shape[2]
    owned = channel // group
    half = width // 2
    quarter = width // snaps
    tile = tokens // 3
    short = divisor(tokens // 2, 16, 240)
    packed = g.modes.shape[2]
    strip = divisor(tokens // 2, 48, 144)
    sub = divisor(strip, 16, 48)
    low = jnp.bfloat16
    f32 = jnp.float32

    me_snap = lax.axis_index("snap")
    me_sp = lax.axis_index("sp")
    core = lax.rem(me_sp, 2)
    level = me_sp // 2

    def at(snap, sp):
        return {"snap": snap, "sp": sp}

    def sp_after(step):
        return lax.rem(me_sp + step, group)

    def sp_before(step):
        return lax.rem(me_sp + group - step, group)

    def snap_after(step):
        return lax.rem(me_snap + step, snaps)

    def snap_before(step):
        return lax.rem(me_snap + snaps - step, snaps)

    def level_after(step):
        return lax.rem(level + step, levels)

    def level_before(step):
        return lax.rem(level + levels - step, levels)

    other_core = at(me_snap, me_sp + 1 - 2 * core)

    def send(src, dst, sems, index, target):
        return pltpu.make_async_remote_copy(
            src_ref=src,
            dst_ref=dst,
            send_sem=sems[0].at[index],
            recv_sem=sems[1].at[index],
            device_id=target,
            device_id_type=pl.DeviceIdType.MESH,
        )

    half_tokens = tokens // 2

    def strips(body, first=0, count=tokens):
        @pl.loop(0, count // strip)
        def _(step):
            for at_row in range(0, strip, sub):
                body(pl.ds(pl.multiple_of(first + step * strip + at_row, 16), sub))

    def half_strips(body, part):
        strips(body, part * half_tokens, half_tokens)

    def half_rows(part):
        return slice(part * half_tokens, (part + 1) * half_tokens)

    def fold(value):
        return jnp.sum(value.reshape(-1, 8, value.shape[1]), axis=0)

    loads = {}

    def load(name, index):
        source, near = getattr(g, name), getattr(g, name + "_in")
        if source.shape != near.shape:
            source = source.reshape(near.shape)
        copy = pltpu.make_async_copy(source, near, g.load_sem.at[index])
        copy.start()
        loads[name] = copy

    for index, name in enumerate(
        [name for name in names[: names.index("out")] if name != "mlp"]
    ):
        load(name, index)

    def master_load(part):
        return pltpu.make_async_copy(
            g.mlp.at[:, :, part * width : (part + 1) * width],
            g.mlp_part.at[part % 2],
            g.load_sem.at[len(loads) + part % 2],
        )

    master_load(0).start()
    master_load(1).start()

    barrier = pltpu.get_barrier_semaphore()
    peers = [at(me_snap, sp_after(step)) for step in range(1, group)]
    peers += [at(snap_after(step), me_sp) for step in range(1, snaps)]
    for peer in peers:
        pl.semaphore_signal(
            barrier, inc=1, device_id=peer, device_id_type=pl.DeviceIdType.MESH
        )

    loads["small"].wait()
    loads["kept"].wait()
    g.own_small[...] = jnp.zeros_like(g.own_small)
    rows_small = g.small.shape[0]
    g.own_small[0:rows_small, 0:owned] = g.small_in[...].astype(low).astype(f32)
    pairs_kept = g.kept.shape[1]
    lines = lax.broadcasted_iota(jnp.int32, (pairs_kept, pairs_kept), 0)
    places = lax.broadcasted_iota(jnp.int32, (pairs_kept, pairs_kept), 1)
    kept = jnp.where(lines == places, g.kept_in[...].astype(f32), 0.0)
    g.own_small[16:, :] = jnp.broadcast_to(
        jnp.sum(kept, axis=1, keepdims=True), (pairs_kept, g.own_small.shape[1])
    )
    pl.semaphore_wait(barrier, len(peers))

    def small_copy(step):
        return send(
            g.own_small, g.all_small.at[me_sp], (g.small_s, g.small_r), step, at(me_snap, sp_after(step))
        )

    for step in range(1, group):
        small_copy(step).start()
    g.all_small[me_sp] = g.own_small[...]

    snap_low = lax.rem(me_snap, 2)
    snap_high = me_snap // 2
    beside_low = me_snap + 1 - 2 * snap_low
    beside_high = me_snap + 2 - 4 * snap_high

    def own_quarter(part):
        odd = lax.rem(part, 2)
        return (1 - odd) * me_snap + odd * (2 * snap_low + snap_high)

    def own_place(part):
        return pl.ds(0, snaps) if part == parts - 1 else own_quarter(part)

    def half_quarters(part):
        return pl.ds(2 * (own_quarter(part) // 2), 2)

    def own_rows(sp):
        return pl.ds(pl.multiple_of(sp * owned, owned), owned)

    def first_copy(part, step):
        target = sp_after(step)
        matrix = lax.rem(target, 2)
        place = own_place(part)
        return send(
            g.own_w.at[part, matrix, place],
            g.all_w.at[part, matrix, place, own_rows(me_sp)],
            (g.first_s, g.first_r),
            (part, step),
            at(me_snap, target),
        )

    def first_local(part):
        place = own_place(part)
        return pltpu.make_async_copy(
            g.own_w.at[part, core, place],
            g.all_w.at[part, core, place, own_rows(me_sp)],
            g.first_s.at[part, 0],
        )

    def second_copy(part):
        odd = lax.rem(part, 2)
        view = g.all_w.at[part, core, own_quarter(part)]
        target = at((1 - odd) * beside_low + odd * beside_high, me_sp)
        return send(view, view, (g.second_s, g.second_r), part, target)

    def third_copy(part):
        odd = lax.rem(part, 2)
        view = g.all_w.at[part, core, half_quarters(part)]
        target = at((1 - odd) * beside_high + odd * beside_low, me_sp)
        return send(view, view, (g.third_s, g.third_r), part, target)

    def fourth_copy(part):
        view = g.all_w.at[part, core]
        return send(view, view, (g.fourth_s, g.fourth_r), part, other_core)

    def start_first(part):
        for step in range(1, group):
            first_copy(part, step).start()
        first_local(part).start()

    def wait_first(part):
        for step in range(1, group):
            first_copy(part, step).wait_recv()
        first_local(part).wait()

    def pass_second(part):
        wait_first(part)
        second_copy(part).start()

    def pass_third(part):
        second_copy(part).wait_recv()
        third_copy(part).start()

    def pass_fourth(part):
        if part == parts - 1:
            wait_first(part)
        else:
            third_copy(part).wait_recv()
        fourth_copy(part).start()

    stages = {FIRST: start_first, SECOND: pass_second, THIRD: pass_third, FOURTH: pass_fourth}

    def reach(point):
        for stage, part in SCHEDULE.get(point, ()):
            stages[stage](part)

    for part in range(parts):
        master_load(part).wait()
        for place in range(snaps):
            cols = slice(place * quarter, (place + 1) * quarter)
            g.own_w[part, :, place] = g.mlp_part[part % 2, :, :, cols].astype(low)
        if part + 2 < parts:
            master_load(part + 2).start()
        if (FIRST, part) in SCHEDULE["a"]:
            start_first(part)

    loads["fields"].wait()

    def first_unit(rows):
        values = g.fields_in[rows, :].astype(f32)
        centred = values - jnp.mean(values, axis=-1, keepdims=True)
        scale = lax.rsqrt(jnp.mean(centred * centred, axis=-1, keepdims=True) + eps_norm)
        g.scale_one[rows, :] = scale
        g.grid[rows, :] = centred * scale

    strips(first_unit)
    reach("b")
    for step in range(1, group):
        small_copy(step).wait_recv()
    for sp in range(group):
        g.gains[:, sp * owned : (sp + 1) * owned] = g.all_small[sp, 0:16, 0:owned]
        g.keep[sp * pairs_kept : (sp + 1) * pairs_kept, :] = g.all_small[sp, 16:, :]

    def first_norm(rows):
        unit = g.grid[rows, :]
        normed = unit * g.gains[0:1, :] + g.gains[1:2, :]
        g.unit_one[rows, :] = unit.astype(low)
        g.normed[rows, :] = normed.astype(low)
        g.grid[rows, :] = g.fields_in[rows, :].astype(f32) + normed

    half_snaps = g.arrived.shape[0] // 2

    third_rows = packed // 3
    spare = 128 - owned

    def pack(value):
        return jnp.concatenate(
            [
                jnp.concatenate(
                    [
                        value[at_row * third_rows : (at_row + 1) * third_rows],
                        value[packed:, at_row * spare : (at_row + 1) * spare],
                    ],
                    axis=1,
                )
                for at_row in range(3)
            ],
            axis=0,
        ).astype(low)

    def unpack(value):
        value = value.astype(f32)
        rest = [
            value[at_row * third_rows : (at_row + 1) * third_rows, owned:] for at_row in range(3)
        ]
        return jnp.concatenate([value[:, 0:owned], jnp.concatenate(rest, axis=1)], axis=0)

    def block_copy(which, part, step):
        target = sp_after(step)
        return send(
            g.modes.at[part, target],
            g.modes_got.at[part, me_sp],
            (g.block_s, g.block_r),
            (which, part, step),
            at(me_snap, target),
        )

    def row_copy(which, part, step):
        target = sp_after(step)
        return send(
            g.rows_out.at[part, target],
            g.rows_got.at[part, me_sp],
            (g.row_s, g.row_r),
            (which, part, step),
            at(me_snap, target),
        )

    def to_blocks(table, which, part):
        modes = dot_nn(table, g.normed[half_rows(part), :])
        for block in range(group):
            g.modes[part, block] = pack(modes[:, block * owned : (block + 1) * owned])
        for step in range(1, group):
            block_copy(which, part, step).start()
        g.modes_got[part, me_sp] = g.modes[part, me_sp]

    def take_blocks(which, part):
        for step in range(1, group):
            block_copy(which, part, step).wait_recv()
        each = g.arrived.shape[1] // group
        for sp in range(group):
            value = unpack(g.modes_got[part, sp])
            value = jnp.concatenate([value, jnp.zeros((value.shape[0], spare), f32)], axis=1)
            for index in range(half_snaps):
                g.arrived[part * half_snaps + index, sp * each : (sp + 1) * each, :] = value[
                    index * each : (index + 1) * each
                ].astype(low)

    def to_rows(which, part, tables):
        each = tables[0].shape[0] // group
        for sp in range(group):
            value = [table[sp * each : (sp + 1) * each, 0:owned] for table in tables]
            g.rows_out[part, sp] = pack(jnp.concatenate(value, axis=0))
        for step in range(1, group):
            row_copy(which, part, step).start()
        g.rows_got[part, me_sp] = g.rows_out[part, me_sp]

    def home_modes(which, part):
        for step in range(1, group):
            row_copy(which, part, step).wait_recv()
        for block in range(group):
            g.gathered[part, :, block * owned : (block + 1) * owned] = unpack(
                g.rows_got[part, block]
            )
        g.home_low[part] = g.gathered[part].astype(low)

    loads["lon_f"].wait()
    for part in range(2):
        half_strips(first_norm, part)
        reach("c" + str(part))
        to_blocks(g.lon_f_in[...], 0, part)
        reach("d" + str(part))

    loads["filt"].wait()
    for weight, first in ((g.weight_one, 0), (g.weight_two, 2)):
        weight[...] = jnp.zeros_like(weight)
        real = g.filt_in[first].astype(low)
        imag = g.filt_in[first + 1].astype(low)
        weight[0:owned, 0:owned] = real
        weight[128 : 128 + owned, 128 : 128 + owned] = real
        weight[0:owned, 128 : 128 + owned] = imag
        weight[128 : 128 + owned, 0:owned] = -imag

    def bias_row(first):
        return jnp.concatenate(
            [g.own_small[first : first + 1, :], g.own_small[first + 1 : first + 2, :]], axis=1
        )

    loads["cot"].wait()
    reach("e")
    loads["lat_f"].wait()
    loads["lat_b"].wait()
    pairs = g.arrived.shape[1] // 2
    half_modes = half_snaps * pairs

    def mode_half(part):
        return slice(part * half_modes, (part + 1) * half_modes)

    def spectra(out, kind, part):
        for snap in range(part * half_snaps, (part + 1) * half_snaps):
            spectrum = dot_nn(g.lat_f_in[...], g.arrived[snap]).astype(kind)
            rows = slice(snap * pairs, (snap + 1) * pairs)
            out[rows, 0:128] = spectrum[0:pairs]
            out[rows, 128:256] = spectrum[pairs:]

    def grids(values):
        tables = []
        for index in range(half_snaps):
            rows = values[index * pairs : (index + 1) * pairs]
            rows = jnp.concatenate([rows[:, 0:128], rows[:, 128:256]], axis=0)
            tables.append(dot_nn(g.lat_b_in[...], rows))
        return tables

    def keep_half():
        keep = jnp.concatenate([g.keep[...], g.keep[...]], axis=1)
        return jnp.concatenate([keep] * half_snaps, axis=0)

    for part in range(2):
        take_blocks(0, part)
        rows = mode_half(part)
        spectra(g.spectrum, low, part)
        g.pre_one[rows, :] = dot_nn(g.spectrum[rows, :], g.weight_one[...]) + bias_row(4)
        g.act_one[rows, :] = gelu_both(g.pre_one[rows, :])[0].astype(low)
        g.pre_two[rows, :] = dot_nn(g.act_one[rows, :], g.weight_two[...]) + bias_row(6)
        to_rows(0, part, grids((shrink(g.pre_two[rows, :]) * keep_half()).astype(low)))
        reach("f" + str(part))
    g.cot_turned[...] = g.cot_in[...].T
    reach("g")

    loads["lon_i"].wait()

    def second_norm(rows):
        values = g.grid[rows, :]
        centred = values - jnp.mean(values, axis=-1, keepdims=True)
        scale = lax.rsqrt(jnp.mean(centred * centred, axis=-1, keepdims=True) + eps_norm)
        centred = centred * scale
        g.unit_two[rows, :] = centred.astype(low)
        g.scale_two[rows, :] = scale
        g.normed[rows, :] = (centred * g.gains[2:3, :] + g.gains[3:4, :]).astype(low)
        g.grid[rows, :] = values + g.gains[8:9, :]
        g.back[rows, :] = jnp.zeros((sub, channel), f32)

    for part in range(2):
        home_modes(0, part)
        g.grid[half_rows(part), :] += dot_nn(g.lon_i_in[...], g.home_low[part])
        reach("h" + str(part))
        half_strips(second_norm, part)
        reach("i" + str(part))
    g.normed_turned[...] = g.normed[...].T
    reach("j")
    flat = jnp.concatenate([g.gains[9 + row : 10 + row, :] for row in range(rows_small - 9)], axis=1)
    for part in range(parts):
        g.bias[part] = flat[:, part * width : (part + 1) * width]

    def core_copy(part, matrix):
        slot = lax.rem(part, 2)
        return send(
            g.grads.at[matrix, :, 1 - core],
            g.core_got.at[slot, matrix],
            (g.core_s, g.core_r),
            (slot, matrix),
            other_core,
        )

    places_one = (snap_low, snap_high)
    places_two = (snap_high, snap_low)
    beside_one = (beside_low, beside_high)
    beside_two = (beside_high, beside_low)

    def half_copy(part, matrix):
        slot = lax.rem(part, 2)
        place = lax.rem(part, 4)
        return send(
            g.half_out.at[slot, matrix, 1 - places_one[matrix]],
            g.half_got.at[place, matrix],
            (g.half_s, g.half_r),
            (place, matrix),
            at(beside_one[matrix], me_sp),
        )

    def quarter_copy(part, matrix):
        slot = lax.rem(part, 2)
        return send(
            g.quarter_out.at[slot, matrix, 1 - places_two[matrix]],
            g.quarter_got.at[slot, matrix],
            (g.quarter_s, g.quarter_r),
            (slot, matrix),
            at(beside_two[matrix], me_sp),
        )

    def level_copy(part, step):
        slot = lax.rem(part, 2)
        place = lax.rem(part, 4)
        target = level_after(step)
        return send(
            g.level_out.at[slot, target],
            g.level_got.at[place, level],
            (g.level_s, g.level_r),
            (place, step),
            at(me_snap, 2 * target + core),
        )

    def last_copy(part, step):
        view = g.total.at[part, me_snap]
        return send(view, view, (g.last_s, g.last_r), (part, step), at(snap_after(step), me_sp))

    def half_stage(part):
        slot = lax.rem(part, 2)
        for matrix in range(2):

            if part >= 2:
                half_copy(part - 2, matrix).wait_send()

            core_copy(part, matrix).wait_recv()

            @pl.loop(0, levels)
            def _(row, matrix=matrix):
                both = g.grads[matrix, row, core].astype(f32) + g.core_got[
                    slot, matrix, row
                ].astype(f32)
                both = both.astype(low)
                g.half_out[slot, matrix, 0, row] = both[:, 0:half]
                g.half_out[slot, matrix, 1, row] = both[:, half:width]

            half_copy(part, matrix).start()

    def quarter_stage(part):
        slot = lax.rem(part, 2)
        for matrix in range(2):

            if part >= 2:
                quarter_copy(part - 2, matrix).wait_send()

            half_copy(part, matrix).wait_recv()
            for row in range(levels):
                both = g.half_out[slot, matrix, places_one[matrix], row].astype(f32) + g.half_got[
                    lax.rem(part, 4), matrix, row
                ].astype(f32)
                both = both.astype(low)
                g.quarter_out[slot, matrix, 0, row] = both[:, 0:quarter]
                g.quarter_out[slot, matrix, 1, row] = both[:, quarter:half]
            quarter_copy(part, matrix).start()

    def level_stage(part):
        slot = lax.rem(part, 2)

        if part >= 2:
            for step in range(1, levels):
                level_copy(part - 2, step).wait_send()

        for matrix in range(2):
            quarter_copy(part, matrix).wait_recv()
            for row in range(levels):
                both = g.quarter_out[slot, matrix, places_two[matrix], row].astype(
                    f32
                ) + g.quarter_got[slot, matrix, row].astype(f32)
                g.level_out[slot, row, matrix] = both.astype(low)
        for step in range(1, levels):
            level_copy(part, step).start()

    def last_stage(part):
        slot = lax.rem(part, 2)
        for step in range(1, levels):
            level_copy(part, step).wait_recv()
        for matrix in range(2):
            sums = g.level_out[slot, level, matrix].astype(f32)
            for step in range(1, levels):
                sums += g.level_got[lax.rem(part, 4), level_before(step), matrix].astype(f32)
            g.total[part, me_snap, matrix] = sums.astype(low)
        for step in range(1, snaps):
            last_copy(part, step).start()

    stages |= {HALF: half_stage, QUARTER: quarter_stage, LEVEL: level_stage, LAST: last_stage}

    def weight(part, matrix):
        return jnp.concatenate([g.all_w[part, matrix, place] for place in range(snaps)], axis=1)

    def add_products(part, rows):
        g.grid[rows, :] += dot_nt(g.act[rows, :], weight(part, 1))
        g.back[rows, :] += dot_nt(g.slope[rows, :], weight(part, 0))

    @pl.loop(0, parts)
    def _(part):
        def reach_in(point):
            for at_part in range(parts):
                if (point, at_part) in SCHEDULE:
                    pl.when(part == at_part)(functools.partial(reach, (point, at_part)))

        def tile_rows(step):
            return pl.ds(pl.multiple_of(step * tile, tile), tile)

        fourth_copy(part).wait_recv()
        reach_in("k")
        g.grad_bias[part] = jnp.zeros(g.grad_bias.shape[1:], f32)

        @pl.loop(0, tokens // tile)
        def _(step):
            rows = tile_rows(step)
            act, slope = gelu_both(dot_nn(g.normed[rows, :], weight(part, 0)) + g.bias[part])
            g.act[rows, :] = act.astype(low)
            slope = (dot_nn(g.cot_in[rows, :], weight(part, 1)) * slope).astype(low)
            g.slope[rows, :] = slope
            g.grad_bias[part] += fold(slope.astype(f32))

        reach_in("l")

        @pl.when(part >= 1)
        def _():
            for matrix in range(2):
                core_copy(part - 1, matrix).wait_send()

        shape = g.grads.shape[1:]
        g.grads[0] = dot_nn(g.normed_turned[...], g.slope[...]).astype(low).reshape(shape)
        core_copy(part, 0).start()
        g.grads[1] = dot_nn(g.cot_turned[...], g.act[...]).astype(low).reshape(shape)
        core_copy(part, 1).start()
        reach_in("m")

        @pl.when(part < parts - 1)
        def _():
            @pl.loop(0, tokens // tile)
            def _(step):
                add_products(part, tile_rows(step))

            reach_in("n")

    g.folds[...] = jnp.zeros_like(g.folds)

    def second_back(rows):
        grad = g.back[rows, :]
        unit = g.unit_two[rows, :].astype(f32)
        cot = g.cot_in[rows, :].astype(f32)
        pulled = grad * g.gains[2:3, :]
        middle = jnp.mean(pulled, axis=-1, keepdims=True)
        slant = jnp.mean(pulled * unit, axis=-1, keepdims=True)
        total = cot + g.scale_two[rows, :] * (pulled - middle - unit * slant)
        g.back[rows, :] = total
        g.normed[rows, :] = total.astype(low)
        g.folds[2] += fold(grad * unit)
        g.folds[3] += fold(grad)
        g.folds[4] += fold(cot)

    loads["lon_it"].wait()
    for part in range(2):

        @pl.loop(0, half_tokens // short)
        def _(step, part=part):
            first_row = part * half_tokens + step * short
            add_products(parts - 1, pl.ds(pl.multiple_of(first_row, 16), short))

        reach("o" + str(part))
        half_strips(second_back, part)
        for step in range(1, group):
            block_copy(0, part, step).wait_send()
        to_blocks(g.lon_it_in[...], 1, part)
        reach("p" + str(part))
    reach("q")

    def low_out(rows):
        g.fields_in[rows, :] = g.grid[rows, :].astype(low)

    strips(low_out)
    out_copy = pltpu.make_async_copy(
        g.fields_in, g.out.reshape(tokens, channel), g.load_sem.at[0]
    )
    out_copy.start()
    reach("r")
    loads["valid"].wait()
    loads["turn"].wait()
    weigh = sum(
        dot_nn(g.valid_in[:, row, :].astype(f32).astype(low), g.turn_in[row])
        for row in range(g.valid.shape[1])
    )
    places_each = weigh.shape[1]
    precise = lax.Precision.HIGHEST
    sums = [jnp.zeros((1, 128), f32), jnp.zeros((1, 128), f32)]
    for snap in range(g.valid.shape[0]):
        variables = g.grid[snap * places_each : (snap + 1) * places_each, 0:128]
        for index, value in enumerate((variables, variables * variables)):
            sums[index] += jnp.dot(
                weigh[snap : snap + 1, :], value, precision=precise, preferred_element_type=f32
            )

    reach("s")

    def dot_tn(left, right):
        return lax.dot_general(
            left, right, (((0,), (0,)), ((), ())), preferred_element_type=f32
        )

    def filter_rows(first, grad):
        g.pair_grad[...] = grad
        real = g.pair_grad[0:128, 0:128] + g.pair_grad[128:256, 128:256]
        imag = g.pair_grad[0:128, 128:256] - g.pair_grad[128:256, 0:128]
        g.filt_out[me_snap, first] = real[0:owned].astype(low)
        g.filt_out[me_snap, first + 1] = imag[0:owned].astype(low)

    for part in range(2):
        take_blocks(1, part)
        reach("t" + str(part))
        rows = mode_half(part)
        spectra(g.grad_pre, f32, part)
        bend = jnp.tanh(g.pre_two[rows, :] / shrink_level)
        grad = (g.grad_pre[rows, :] * keep_half() * (bend * bend)).astype(low)
        g.grad_two[rows, :] = grad
        grad = dot_nt(grad, g.weight_two[...]) * gelu_both(g.pre_one[rows, :])[1]
        grad = grad.astype(low)
        g.grad_one[rows, :] = grad
        for step in range(1, group):
            row_copy(0, part, step).wait_send()
        to_rows(1, part, grids(dot_nt(grad, g.weight_one[...]).astype(low)))
        reach("u" + str(part))
    reach("v")
    bias_one = jnp.sum(g.grad_one[...].astype(f32), axis=0, keepdims=True)
    bias_two = jnp.sum(g.grad_two[...].astype(f32), axis=0, keepdims=True)
    filter_rows(2, dot_tn(g.act_one[...], g.grad_two[...]))
    filter_rows(0, dot_tn(g.spectrum[...], g.grad_one[...]))

    def filter_copy(step):
        view = g.filt_out.at[me_snap]
        return send(view, view, (g.filt_s, g.filt_r), step, at(snap_after(step), me_sp))

    for step in range(1, snaps):
        filter_copy(step).start()


    reach("w")

    loads["lon_ft"].wait()

    def first_back(rows):
        grad = g.grid[rows, :]
        unit = g.unit_one[rows, :].astype(f32)
        pulled = grad * g.gains[0:1, :]
        middle = jnp.mean(pulled, axis=-1, keepdims=True)
        slant = jnp.mean(pulled * unit, axis=-1, keepdims=True)
        g.grid[rows, :] = g.back[rows, :] + g.scale_one[rows, :] * (
            pulled - middle - unit * slant
        )
        g.folds[0] += fold(grad * unit)
        g.folds[1] += fold(grad)

    grad_copies = [
        pltpu.make_async_copy(
            g.grid.at[rows], g.in_grad.reshape(tokens, channel).at[rows], g.load_sem.at[1 + part]
        )
        for part, rows in enumerate(pl.ds(part * half_tokens, half_tokens) for part in range(2))
    ]
    for part in range(2):
        home_modes(1, part)
        reach("x" + str(part))
        g.grid[half_rows(part), :] = g.back[half_rows(part), :] + dot_nn(
            g.lon_ft_in[...], g.home_low[part]
        )
        half_strips(first_back, part)
        grad_copies[part].start()
        reach("y" + str(part))

    g.grad_rows[...] = jnp.zeros_like(g.grad_rows)
    for index, row in enumerate((0, 1, 2, 3, 8)):
        g.grad_rows[row : row + 1, :] = jnp.sum(g.folds[index], axis=0, keepdims=True)
    flat = jnp.concatenate(
        [jnp.sum(g.grad_bias[part], axis=0, keepdims=True) for part in range(parts)], axis=1
    )
    for row in range(rows_small - 9):
        g.grad_rows[9 + row : 10 + row, :] = flat[:, row * channel : (row + 1) * channel]
    for block in range(group):
        g.tiles[block] = jnp.zeros(g.tiles.shape[1:], f32)
        g.tiles[block, :, 0:owned] = g.grad_rows[:, block * owned : (block + 1) * owned]
        g.tiles[block, 13:14, :] = sums[0]
        g.tiles[block, 14:15, :] = sums[1]

    def tile_copy(step):
        target = sp_after(step)
        return send(
            g.tiles.at[target], g.tiles_got.at[me_sp], (g.tile_s, g.tile_r), step, at(me_snap, target)
        )

    def snap_tile_copy(step):
        view = g.snap_tiles.at[me_snap]
        return send(view, view, (g.snap_tile_s, g.snap_tile_r), step, at(snap_after(step), me_sp))

    for step in range(1, group):
        tile_copy(step).start()
    reach("z")

    g.tiles_got[me_sp] = g.tiles[me_sp]
    for step in range(1, group):
        tile_copy(step).wait_recv()
    tile_sum = g.tiles_got[0]
    for sp in range(1, group):
        tile_sum += g.tiles_got[sp]
    g.snap_tiles[me_snap] = tile_sum
    g.snap_tiles[me_snap, 4:5, :] = bias_one[:, 0:128]
    g.snap_tiles[me_snap, 5:6, :] = bias_one[:, 128:256]
    g.snap_tiles[me_snap, 6:7, :] = bias_two[:, 0:128]
    g.snap_tiles[me_snap, 7:8, :] = bias_two[:, 128:256]
    for step in range(1, snaps):
        snap_tile_copy(step).start()

    for step in range(1, snaps):
        filter_copy(step).wait_recv()
    filter_sum = g.filt_out[0].astype(f32)
    for snap in range(1, snaps):
        filter_sum += g.filt_out[snap].astype(f32)
    g.grad_filt[...] = filter_sum
    for part in range(parts):
        for step in range(1, snaps):
            last_copy(part, step).wait_recv()
    grads_out = pltpu.make_async_copy(g.total, g.grad_mlp, g.load_sem.at[3])
    grads_out.start()
    for step in range(1, snaps):
        snap_tile_copy(step).wait_recv()
    tile_sum = g.snap_tiles[0]
    for snap in range(1, snaps):
        tile_sum += g.snap_tiles[snap]
    g.grad_small[...] = tile_sum

    grads_out.wait()
    for copy in [out_copy, *grad_copies]:
        copy.wait()
    for step in range(1, group):
        small_copy(step).wait_send()
        for part in range(2):
            block_copy(1, part, step).wait_send()
            row_copy(1, part, step).wait_send()
        tile_copy(step).wait_send()
        for part in range(parts):
            first_copy(part, step).wait_send()
    for part in range(parts):
        if part < parts - 1:
            second_copy(part).wait_send()
            third_copy(part).wait_send()
        fourth_copy(part).wait_send()
    for matrix in range(2):
        core_copy(parts - 1, matrix).wait_send()
    for part in (parts - 2, parts - 1):
        for matrix in range(2):
            half_copy(part, matrix).wait_send()
            quarter_copy(part, matrix).wait_send()
        for step in range(1, levels):
            level_copy(part, step).wait_send()
    for step in range(1, snaps):
        filter_copy(step).wait_send()
        snap_tile_copy(step).wait_send()
        for part in range(parts):
            last_copy(part, step).wait_send()


def block_pass(fields, cot, valid, kept, mlp, filt, small, snaps, group):
    snap_local, row_local, lon_total, channel = fields.shape
    tokens = snap_local * row_local * lon_total
    hidden = mlp.shape[2]
    lat_total = row_local * group
    modes = kept.shape[1] * group
    owned = channel // group
    width = 512
    parts = hidden // width
    levels = group // 2
    quarter = width // snaps
    low, f32 = jnp.bfloat16, jnp.float32
    half = width // 2
    half_snaps = snap_local // 2
    lon_f, lon_i = lon_matrix(lon_total, modes, half_snaps, row_local)

    def paired(array):
        return jnp.transpose(array, (0, 2, 1, 3)).reshape(-1, row_local, channel)

    lat_f = lat_matrix(lat_total, modes)
    pair = 2 * modes * row_local
    spread = half_snaps * row_local * 2 * modes
    inputs = dict(
        small=small,
        kept=kept.T,
        fields=paired(fields),
        lon_f=jnp.asarray(np.ascontiguousarray(lon_f.T)),
        filt=filt,
        lat_f=jnp.asarray(lat_f),
        lat_b=jnp.asarray(np.ascontiguousarray(lat_f.T)),
        cot=paired(cot),
        lon_i=jnp.asarray(lon_i),
        valid=valid,
        turn=jnp.asarray(lon_turn(lon_total, row_local)),
        lon_it=jnp.asarray(np.ascontiguousarray(lon_i.T)),
        lon_ft=jnp.asarray(lon_f),
        mlp=mlp,
    )
    outputs = dict(
        out=jax.ShapeDtypeStruct((tokens // row_local, row_local, channel), low),
        in_grad=jax.ShapeDtypeStruct((tokens // row_local, row_local, channel), f32),
        grad_mlp=jax.ShapeDtypeStruct((parts, snaps, 2, owned, quarter), low),
        grad_filt=jax.ShapeDtypeStruct((4, owned, 128), f32),
        grad_small=jax.ShapeDtypeStruct((16, 128), f32),
    )
    vmem = pltpu.VMEM
    dma = pltpu.SemaphoreType.DMA
    scratch = {
        name + "_in": vmem(value.shape, value.dtype)
        for name, value in inputs.items()
        if name not in ("mlp", "fields", "cot")
    }
    scratch |= dict(
        mlp_part=vmem((2, 2, owned, width), f32),
        fields_in=vmem((tokens, channel), low),
        cot_in=vmem((tokens, channel), low),
        grid=vmem((tokens, channel), f32),
        back=vmem((tokens, channel), f32),
        normed=vmem((tokens, channel), low),
        normed_turned=vmem((channel, tokens), low),
        cot_turned=vmem((channel, tokens), low),
        unit_one=vmem((tokens, channel), low),
        unit_two=vmem((tokens, channel), low),
        scale_one=vmem((tokens, 1), f32),
        scale_two=vmem((tokens, 1), f32),
        own_small=vmem((16 + kept.shape[0], 128), f32),
        all_small=vmem((group, 16 + kept.shape[0], 128), f32),
        gains=vmem((16, channel), f32),
        keep=vmem((lat_total * modes, 128), f32),
        own_w=vmem((parts, 2, snaps, owned, quarter), low),
        all_w=vmem((parts, 2, snaps, channel, quarter), low),
        modes=vmem((2, group, half_snaps * pair * 3 // 4, 128), low),
        modes_got=vmem((2, group, half_snaps * pair * 3 // 4, 128), low),
        rows_out=vmem((2, group, half_snaps * pair * 3 // 4, 128), low),
        rows_got=vmem((2, group, half_snaps * pair * 3 // 4, 128), low),
        arrived=vmem((snap_local, pair * group, 128), low),
        gathered=vmem((2, spread, channel), f32),
        home_low=vmem((2, spread, channel), low),
        weight_one=vmem((256, 256), low),
        weight_two=vmem((256, 256), low),
        spectrum=vmem((snap_local * lat_total * modes, 256), low),
        pre_one=vmem((snap_local * lat_total * modes, 256), f32),
        act_one=vmem((snap_local * lat_total * modes, 256), low),
        pre_two=vmem((snap_local * lat_total * modes, 256), f32),
        grad_pre=vmem((snap_local * lat_total * modes, 256), f32),
        grad_two=vmem((snap_local * lat_total * modes, 256), low),
        grad_one=vmem((snap_local * lat_total * modes, 256), low),
        folds=vmem((5, 8, channel), f32),
        pair_grad=vmem((256, 256), f32),
        act=vmem((tokens, width), low),
        slope=vmem((tokens, width), low),
        bias=vmem((parts, 1, width), f32),
        grad_bias=vmem((parts, 8, width), f32),
        grad_rows=vmem((16, channel), f32),
        grads=vmem((2, levels, 2, owned, width), low),
        core_got=vmem((2, 2, levels, owned, width), low),
        half_out=vmem((2, 2, 2, levels, owned, half), low),
        half_got=vmem((4, 2, levels, owned, half), low),
        quarter_out=vmem((2, 2, 2, levels, owned, quarter), low),
        quarter_got=vmem((2, 2, levels, owned, quarter), low),
        level_out=vmem((2, levels, 2, owned, quarter), low),
        level_got=vmem((4, levels, 2, owned, quarter), low),
        total=vmem((parts, snaps, 2, owned, quarter), low),
        filt_out=vmem((snaps, 4, owned, 128), low),
        tiles=vmem((group, 16, 128), f32),
        tiles_got=vmem((group, 16, 128), f32),
        snap_tiles=vmem((snaps, 16, 128), f32),
        load_sem=dma((len(inputs) + 1,)),
    )
    for name, shape in dict(
        small=(group,),
        first=(parts, group),
        second=(parts,),
        third=(parts,),
        fourth=(parts,),
        block=(2, 2, group),
        row=(2, 2, group),
        core=(2, 2),
        half=(4, 2),
        quarter=(2, 2),
        level=(4, levels),
        last=(parts, snaps),
        filt=(snaps,),
        tile=(group,),
        snap_tile=(snaps,),
    ).items():
        scratch[name + "_s"] = dma(shape)
        scratch[name + "_r"] = dma(shape)
    names = [*inputs, *outputs, *scratch]
    far = pl.BlockSpec(memory_space=pl.ANY)
    near = pl.BlockSpec(memory_space=pltpu.VMEM)
    results = pl.pallas_call(
        functools.partial(block_body, names, (snaps, group, parts, width)),
        in_specs=[far] * len(inputs),
        out_specs=[far, far, far, near, near],
        out_shape=list(outputs.values()),
        scratch_shapes=list(scratch.values()),
        compiler_params=pltpu.CompilerParams(
            collective_id=0, has_side_effects=True, vmem_limit_bytes=VMEM_LIMIT
        ),
        cost_estimate=pl.CostEstimate(
            flops=12 * tokens * channel * hidden,
            bytes_accessed=4 * hidden * channel,
            transcendentals=tokens * hidden,
        ),
        name="block_pass",
    )(*inputs.values())
    return results


def step_body(names, positions, *refs):
    g = Refs()
    for name, ref in zip(names, refs, strict=True):
        setattr(g, name, ref)
    parts, snaps = g.grad_mlp.shape[:2]
    quarter = g.grad_mlp.shape[4]
    width = snaps * quarter
    moments = ("w", "m", "v")
    results = ("new", "first", "second", "copy")

    pieces = g.far_sem.shape[2]
    ends = ((g.out, g.out_near, g.out_o), (g.in_grad, g.in_grad_near, g.in_grad_o))

    def passing(kind, piece, leg):
        size = ends[kind][0].shape[0] // pieces
        rows = pl.ds(piece * size, size)
        return pltpu.make_async_copy(
            ends[kind][leg].at[rows], ends[kind][leg + 1].at[rows], g.far_sem.at[leg, kind, piece]
        )

    through = [(kind, piece) for kind in range(2) for piece in range(pieces)]

    def part_cols(part):
        return pl.ds(part * width, width)

    def load(part):
        near = [
            pltpu.make_async_copy(
                getattr(g, "mlp_" + kind).at[:, :, part_cols(part)],
                g.near.at[index, part],
                g.near_sem.at[index, part],
            )
            for index, kind in enumerate(moments)
        ]
        near.append(
            pltpu.make_async_copy(g.grad_mlp.at[part], g.grad_near.at[part], g.near_sem.at[3, part])
        )
        return near

    def store(part):
        copies = [
            pltpu.make_async_copy(
                g.near.at[index, part],
                getattr(g, "mlp_" + kind).at[:, :, part_cols(part)],
                g.back_sem.at[index, part],
            )
            for index, kind in enumerate(results[:3])
        ]
        copies.append(
            pltpu.make_async_copy(
                g.low_near.at[part], g.mlp_copy.at[:, :, part_cols(part)], g.back_sem.at[3, part]
            )
        )
        return copies

    coming = [load(part) for part in range(parts)]
    going = [store(part) for part in range(parts)]
    shares = [through[part::parts] for part in range(parts)]
    for part in range(parts):
        for copy in coming[part]:
            copy.start()
        for each in shares[part]:
            passing(*each, 0).start()

    def put(prefix, values):
        for kind, value in zip(results, values, strict=True):
            getattr(g, prefix + kind)[...] = value

    owned = g.filt_w.shape[2]
    put(
        "filt_",
        adamw(g.filt_w[...], g.filt_m[...], g.filt_v[...], g.grad_filt[:, :, 0:owned], rate_filter),
    )
    rows = g.small_w.shape[0]
    put(
        "small_",
        adamw(
            g.small_w[...], g.small_m[...], g.small_v[...], g.grad_small[0:rows, 0:owned], rate_small
        ),
    )
    totals = g.grad_small[rows : rows + 2, 0 : g.run.shape[1]]
    g.stats[...] = stat_decay * g.run[...] + (1.0 - stat_decay) * totals / positions

    for part in range(parts):
        for copy in coming[part]:
            copy.wait()

        for matrix, snap in [(matrix, snap) for matrix in range(2) for snap in range(snaps)]:
            place = snap if matrix else 2 * (snap % 2) + snap // 2
            where = (matrix, slice(None), slice(place * quarter, (place + 1) * quarter))
            now = [g.near[(index, part, *where)] for index in range(3)]
            grad = g.grad_near[part, snap, matrix].astype(jnp.float32)
            values = adamw(*now, grad, rate_mlp)
            for index in range(3):
                g.near[(index, part, *where)] = values[index]
            g.low_near[(part, *where)] = values[3]
        for copy in going[part]:
            copy.start()
        for each in shares[part]:
            passing(*each, 0).wait()
            passing(*each, 1).start()
    for each in through:
        passing(*each, 1).wait()
    for part in range(parts):
        for copy in going[part]:
            copy.wait()


def step_pass(shown, grads, masters, run_stats, positions):
    grad_mlp, grad_filt, grad_small = grads
    mlp, filt, small = masters
    parts = grad_mlp.shape[0]
    width = mlp[0].shape[2] // parts
    f32, low = jnp.float32, jnp.bfloat16
    far = pl.BlockSpec(memory_space=pltpu.HBM)
    near = pl.BlockSpec(memory_space=pltpu.VMEM)
    inputs = dict(out=shown[0], in_grad=shown[1], grad_mlp=grad_mlp)
    inputs |= dict(zip(("mlp_w", "mlp_m", "mlp_v"), mlp, strict=True))
    far_in = len(inputs)
    inputs |= dict(grad_filt=grad_filt, grad_small=grad_small)
    inputs |= dict(zip(("filt_w", "filt_m", "filt_v"), filt, strict=True))
    inputs |= dict(zip(("small_w", "small_m", "small_v"), small, strict=True))
    inputs |= dict(run=run_stats)
    results = (("new", f32), ("first", f32), ("second", f32), ("copy", low))
    outputs = {
        name + "_o": jax.ShapeDtypeStruct(array.shape, array.dtype)
        for name, array in zip(("out", "in_grad"), shown, strict=True)
    }
    outputs |= {"mlp_" + kind: jax.ShapeDtypeStruct(mlp[0].shape, dt) for kind, dt in results}
    far_out = len(outputs)
    outputs |= {"filt_" + kind: jax.ShapeDtypeStruct(filt[0].shape, dt) for kind, dt in results}
    outputs |= {"small_" + kind: jax.ShapeDtypeStruct(small[0].shape, dt) for kind, dt in results}
    outputs |= dict(stats=jax.ShapeDtypeStruct(run_stats.shape, f32))
    scratch = dict(
        near=pltpu.VMEM((3, parts, 2, mlp[0].shape[1], width), f32),
        grad_near=pltpu.VMEM(grad_mlp.shape, low),
        low_near=pltpu.VMEM((parts, 2, mlp[0].shape[1], width), low),
        near_sem=pltpu.SemaphoreType.DMA((4, parts)),
        back_sem=pltpu.SemaphoreType.DMA((4, parts)),
        out_near=pltpu.VMEM(shown[0].shape, low),
        in_grad_near=pltpu.VMEM(shown[1].shape, f32),
        far_sem=pltpu.SemaphoreType.DMA((2, 2, divisor(shown[0].shape[0], 1, 4))),
    )
    return pl.pallas_call(
        functools.partial(step_body, [*inputs, *outputs, *scratch], positions),
        in_specs=[far] * far_in + [near] * (len(inputs) - far_in),
        out_specs=[far] * far_out + [near] * (len(outputs) - far_out),
        out_shape=list(outputs.values()),
        scratch_shapes=list(scratch.values()),
        compiler_params=pltpu.CompilerParams(vmem_limit_bytes=VMEM_LIMIT),
        name="step_pass",
    )(*inputs.values())


def per_device_blocks(
    fields,
    cotangent,
    valid_mask,
    kept_modes,
    mlp_master,
    mlp_first,
    mlp_second,
    filter_master,
    filter_first,
    filter_second,
    small_master,
    small_first,
    small_second,
    run_stats,
):
    snaps, group = lax.axis_size("snap"), lax.axis_size("sp")
    out, in_grad, *grads = block_pass(
        fields, cotangent, valid_mask, kept_modes, mlp_master, filter_master, small_master, snaps, group
    )
    snap_local, row_local, lon_total, channel = fields.shape
    positions = snap_local * snaps * row_local * group * lon_total
    out, in_grad, *stepped = step_pass(
        (out, in_grad),
        grads,
        (
            (mlp_master, mlp_first, mlp_second),
            (filter_master, filter_first, filter_second),
            (small_master, small_first, small_second),
        ),
        run_stats,
        positions,
    )
    rows_apart = (snap_local, lon_total, row_local, channel)
    out, in_grad = [
        jnp.transpose(array.reshape(rows_apart), (0, 2, 1, 3)) for array in (out, in_grad)
    ]
    return (out, in_grad, *stepped)


def per_device(*arrays):
    group, snaps = lax.axis_size("sp"), lax.axis_size("snap")
    channel, hidden = arrays[0].shape[3], arrays[4].shape[2]
    by_block = group == BLOCKS and snaps == 4 and arrays[3].shape[1] == 1
    if by_block and hidden == 6 * 512 and channel // group <= 128 and channel % (16 * group) == 0:
        return per_device_blocks(*arrays)
    return per_device_modes(*arrays)


def solution(mesh):
    return jax.shard_map(
        per_device,
        mesh=mesh,
        in_specs=(
            P("snap", "sp", None, None),
            P("snap", "sp", None, None),
            P("snap", "sp", None),
            P(None, "sp"),
            P(None, "sp", None),
            P(None, "sp", None),
            P(None, "sp", None),
            P(None, "sp", None),
            P(None, "sp", None),
            P(None, "sp", None),
            P(None, "sp"),
            P(None, "sp"),
            P(None, "sp"),
            P(),
        ),
        out_specs=(
            P("snap", "sp", None, None),
            P("snap", "sp", None, None),
            P(None, "sp", None),
            P(None, "sp", None),
            P(None, "sp", None),
            P(None, "sp", None),
            P(None, "sp", None),
            P(None, "sp", None),
            P(None, "sp", None),
            P(None, "sp", None),
            P(None, "sp"),
            P(None, "sp"),
            P(None, "sp"),
            P(None, "sp"),
            P(),
        ),
        check_vma=False,
    )
```

```python
import functools
import math

import jax
import jax.numpy as jnp
import ml_dtypes
import numpy as np
from jax import lax
from jax.experimental import pallas as pl
from jax.experimental.pallas import tpu as pltpu
from jax.sharding import PartitionSpec as P

BLOCKS = 8
NVAR = 20
STEP = 10
VMEM_LIMIT = 63 * 1024 * 1024


eps_norm = 1e-06
shrink_level = 0.01
beta_one = 0.5
beta_two = 0.5
adam_eps = 1e-08
decay_rate = 0.01
rate_mlp = 0.03
rate_filter = 0.1
rate_small = 0.2
stat_decay = 0.5


def layer_norm(values, gain_vec, shift_vec):
    centred = values - jnp.mean(values, axis=-1, keepdims=True)
    spread = jnp.mean(centred * centred, axis=-1, keepdims=True)
    return centred * lax.rsqrt(spread + eps_norm) * gain_vec + shift_vec


def shrink(values):
    return values - shrink_level * jnp.tanh(values / shrink_level)


def lon_tables(lon_total, mode_total):
    places = jnp.arange(lon_total, dtype=jnp.int32)
    orders = jnp.arange(mode_total, dtype=jnp.int32)
    angles = (places[:, None] * orders[None, :] % lon_total).astype(jnp.float32) * (
        2.0 * math.pi / lon_total
    )
    scaling = 1.0 / math.sqrt(lon_total)
    forward_tab = jnp.stack([jnp.cos(angles), -jnp.sin(angles)], axis=1) * scaling
    doubling = jnp.where(orders == 0, 1.0, 2.0).astype(jnp.float32)[:, None]
    inverse_tab = (
        jnp.stack([jnp.cos(angles).T * doubling, -jnp.sin(angles).T * doubling], axis=0) * scaling
    )
    return (forward_tab.astype(jnp.bfloat16), inverse_tab.astype(jnp.bfloat16))


def lat_table(lat_total):
    places = jnp.arange(lat_total, dtype=jnp.int32)
    angles = (places[:, None] * places[None, :] % lat_total).astype(jnp.float32) * (
        2.0 * math.pi / lat_total
    )
    cosine = jnp.cos(angles)
    sine_part = jnp.sin(angles)
    upper_rows = jnp.stack([cosine, sine_part], axis=1)
    bottom = jnp.stack([-sine_part, cosine], axis=1)
    return (jnp.stack([upper_rows, bottom], axis=0) / math.sqrt(lat_total)).astype(jnp.bfloat16)


def complex_pair(real_part, imag_part):
    return jnp.stack([jnp.stack([real_part, -imag_part]), jnp.stack([imag_part, real_part])])


gelu_scale = math.sqrt(2.0 / math.pi)
gelu_cubic = 0.044715


def gelu_both(value):
    bend = (gelu_scale * gelu_cubic) * (value * value)
    turn = jnp.tanh(value * (gelu_scale + bend))
    half = 0.5 + 0.5 * turn
    slope = half * (1.0 + (value * (1.0 - turn)) * (gelu_scale + 3.0 * bend))
    return value * half, slope


def dot_nt(left, right):
    return lax.dot_general(
        left, right, (((1,), (1,)), ((), ())), preferred_element_type=jnp.float32
    )


def dot_nn(left, right):
    return jnp.dot(left, right, preferred_element_type=jnp.float32)


def divisor(total, unit, most):
    return max(size for size in range(unit, most + 1, unit) if total % size == 0)


def mlp_body(
    tile,
    normed_ref,
    cot_ref,
    up_ref,
    down_ref,
    bias_ref,
    out_ref,
    back_ref,
    grad_up_ref,
    grad_down_ref,
    grad_bias_ref,
    normed_turned,
    cot_turned,
    act_ref,
    slope_ref,
):
    tokens = normed_ref.shape[0]

    @pl.when(pl.program_id(0) == 0)
    def _():
        normed_turned[...] = normed_ref[...].T
        cot_turned[...] = cot_ref[...].T
        out_ref[...] = jnp.zeros_like(out_ref)
        back_ref[...] = jnp.zeros_like(back_ref)

    grad_bias_ref[...] = jnp.zeros_like(grad_bias_ref)

    @pl.loop(0, tokens // tile)
    def _(step):
        rows = pl.ds(pl.multiple_of(step * tile, tile), tile)
        act, slope = gelu_both(dot_nn(normed_ref[rows, :], up_ref[...]) + bias_ref[...])
        act = act.astype(jnp.bfloat16)
        slope = (dot_nn(cot_ref[rows, :], down_ref[...]) * slope).astype(jnp.bfloat16)
        act_ref[rows, :] = act
        slope_ref[rows, :] = slope
        grad_bias_ref[...] += jnp.sum(slope.astype(jnp.float32), axis=0, keepdims=True)
        out_ref[rows, :] += dot_nt(act, down_ref[...])
        back_ref[rows, :] += dot_nt(slope, up_ref[...])

    grad_up_ref[...] = dot_nn(normed_turned[...], slope_ref[...]).astype(grad_up_ref.dtype)
    grad_down_ref[...] = dot_nn(cot_turned[...], act_ref[...]).astype(grad_down_ref.dtype)


def mlp_pass(normed, cot, weights, bias):
    tokens, channel = normed.shape
    hidden = weights.shape[2]
    width = divisor(hidden, 128, 512)
    tile = divisor(tokens, 16, 480)
    whole = pl.BlockSpec((tokens, channel), lambda j: (0, 0))
    block = pl.BlockSpec((channel, width), lambda j: (0, j))
    line = pl.BlockSpec((1, width), lambda j: (0, j))
    part = lambda which: pl.BlockSpec((None, channel, width), lambda j: (which, 0, j))
    total = jax.ShapeDtypeStruct((tokens, channel), jnp.float32)
    grads = jax.ShapeDtypeStruct((channel, hidden), jnp.bfloat16)
    return pl.pallas_call(
        functools.partial(mlp_body, tile),
        grid=(hidden // width,),
        in_specs=[whole, whole, part(0), part(1), line],
        out_specs=[whole, whole, block, block, line],
        out_shape=[total, total, grads, grads, jax.ShapeDtypeStruct((1, hidden), jnp.float32)],
        scratch_shapes=[
            pltpu.VMEM((channel, tokens), jnp.bfloat16),
            pltpu.VMEM((channel, tokens), jnp.bfloat16),
            pltpu.VMEM((tokens, width), jnp.bfloat16),
            pltpu.VMEM((tokens, width), jnp.bfloat16),
        ],
        compiler_params=pltpu.CompilerParams(vmem_limit_bytes=56 * 1024 * 1024),
        cost_estimate=pl.CostEstimate(
            flops=12 * tokens * channel * hidden,
            bytes_accessed=8 * channel * hidden + 12 * tokens * channel,
            transcendentals=tokens * hidden,
        ),
        name="mlp_pass",
    )(normed, cot, weights, weights, bias)


def spectral_front(arrived, lat_fwd, first_pair, second_pair, bias_one, bias_two):
    spectrum = jnp.einsum(
        "pkqr,nrqmd->nkpmd", lat_fwd, arrived, preferred_element_type=jnp.float32
    ).astype(jnp.bfloat16)
    snap_local, lat_total, pair_count, mode_local, channel = spectrum.shape
    blocked = spectrum.reshape(
        snap_local, lat_total, pair_count, mode_local, BLOCKS, channel // BLOCKS
    )
    pre_one = (
        jnp.einsum("nkqmbi,pqbio->nkpmbo", blocked, first_pair, preferred_element_type=jnp.float32)
        + bias_one
    )
    act_one = jax.nn.gelu(pre_one).astype(jnp.bfloat16)
    pre_two = (
        jnp.einsum("nkqmbi,pqbio->nkpmbo", act_one, second_pair, preferred_element_type=jnp.float32)
        + bias_two
    )
    return (blocked, pre_one, act_one, pre_two)


def adamw(master, first_mom, second_mom, gradient, step_rate):
    first_next = beta_one * first_mom + (1.0 - beta_one) * gradient
    second_next = beta_two * second_mom + (1.0 - beta_two) * gradient * gradient
    fix_one = 1.0 / (1.0 - beta_one**STEP)
    fix_two = 1.0 / (1.0 - beta_two**STEP)
    direction = first_next * fix_one / (jnp.sqrt(second_next * fix_two) + adam_eps)
    master_next = master - step_rate * (direction + decay_rate * master)
    return (master_next, first_next, second_next, master_next.astype(jnp.bfloat16))


def per_device_modes(
    fields,
    cotangent,
    valid_mask,
    kept_modes,
    mlp_master,
    mlp_first,
    mlp_second,
    filter_master,
    filter_first,
    filter_second,
    small_master,
    small_first,
    small_second,
    run_stats,
):
    group_size = lax.axis_size("sp")
    snap_local, row_local, lon_total, channel = fields.shape
    lat_total = row_local * group_size
    mode_local = kept_modes.shape[1]
    mode_total = mode_local * group_size
    block_width = channel // BLOCKS
    lon_fwd, lon_inv = lon_tables(lon_total, mode_total)
    lat_fwd = lat_table(lat_total)
    mlp_w, filt_w, small_w = (
        lax.all_gather(mlp_master.astype(jnp.bfloat16), "sp", axis=1, tiled=True),
        lax.all_gather(filter_master.astype(jnp.bfloat16), "sp", axis=1, tiled=True),
        lax.all_gather(small_master.astype(jnp.bfloat16), "sp", axis=1, tiled=True),
    )
    small_f = small_w.astype(jnp.float32)
    weights = filt_w.reshape(4, BLOCKS, block_width, block_width)
    first_pair = complex_pair(weights[0], weights[1])
    second_pair = complex_pair(weights[2], weights[3])
    bias_one = small_f[4:6].reshape(2, 1, BLOCKS, block_width)
    bias_two = small_f[6:8].reshape(2, 1, BLOCKS, block_width)
    fields_float = fields.astype(jnp.float32)
    normed, norm_pull = jax.vjp(layer_norm, fields_float, small_f[0], small_f[1])
    normed_low = normed.astype(jnp.bfloat16)
    spec_lon = jnp.einsum(
        "nrld,lqm->nrqmd", normed_low, lon_fwd, preferred_element_type=jnp.float32
    ).astype(jnp.bfloat16)
    arrived = lax.all_to_all(spec_lon, "sp", split_axis=3, concat_axis=1, tiled=True)
    spectral = spectral_front(arrived, lat_fwd, first_pair, second_pair, bias_one, bias_two)
    keep_mask = kept_modes.astype(jnp.float32)[None, :, None, :, None, None]
    masked = (shrink(spectral[3]) * keep_mask).astype(jnp.bfloat16)
    masked = masked.reshape(snap_local, lat_total, 2, mode_local, channel)
    returned = jnp.einsum(
        "pkqr,nkpmd->nrqmd", lat_fwd, masked, preferred_element_type=jnp.float32
    ).astype(jnp.bfloat16)
    home_modes = lax.all_to_all(returned, "sp", split_axis=1, concat_axis=3, tiled=True)
    filtered = jnp.einsum(
        "nrqmd,qml->nrld", home_modes, lon_inv, preferred_element_type=jnp.float32
    )
    mixture = fields_float + normed + filtered
    normed_two, norm_two_pull = jax.vjp(layer_norm, mixture, small_f[2], small_f[3])
    normed_two_low = normed_two.astype(jnp.bfloat16)
    tokens = snap_local * row_local * lon_total
    passed = mlp_pass(
        normed_two_low.reshape(tokens, channel),
        cotangent.reshape(tokens, channel),
        mlp_w,
        small_f[9:].reshape(1, -1),
    )
    output = mixture + passed[0].reshape(mixture.shape) + small_f[8]
    weight_mask = valid_mask.astype(jnp.float32)[..., None]
    variables = output[..., :NVAR]
    local_sums = jnp.stack(
        [
            jnp.sum(weight_mask * variables, axis=(0, 1, 2)),
            jnp.sum(weight_mask * variables * variables, axis=(0, 1, 2)),
        ]
    )
    total_sums = lax.psum(local_sums, ("snap", "sp"))
    positions = snap_local * lax.axis_size("snap") * lat_total * lon_total
    stats_new = stat_decay * run_stats + (1.0 - stat_decay) * total_sums / positions
    cot_float = cotangent.astype(jnp.float32)
    grad_normed_two = passed[1].reshape(mixture.shape)
    grad_bias_hidden = passed[4]
    grad_mix_norm, grad_gain_two, grad_shift_two = norm_two_pull(grad_normed_two)
    grad_mixture = cot_float + grad_mix_norm
    grad_bias_out = jnp.sum(cot_float, axis=(0, 1, 2))
    grad_filtered = grad_mixture.astype(jnp.bfloat16)
    grad_home = jnp.einsum(
        "nrld,qml->nrqmd", grad_filtered, lon_inv, preferred_element_type=jnp.float32
    ).astype(jnp.bfloat16)
    grad_returned = lax.all_to_all(grad_home, "sp", split_axis=3, concat_axis=1, tiled=True)
    grad_masked = jnp.einsum(
        "pkqr,nrqmd->nkpmd", lat_fwd, grad_returned, preferred_element_type=jnp.float32
    )
    arrived_again = lax.all_to_all(spec_lon, "sp", split_axis=3, concat_axis=1, tiled=True)
    used_front = spectral_front(arrived_again, lat_fwd, first_pair, second_pair, bias_one, bias_two)
    blocked, pre_one, act_one, pre_two = used_front
    grad_two = jax.vjp(shrink, pre_two)[1](grad_masked.reshape(pre_two.shape) * keep_mask)[
        0
    ].astype(jnp.bfloat16)
    grad_bias_two = jnp.sum(grad_two.astype(jnp.float32), axis=(0, 1, 3))
    grad_second = jnp.einsum(
        "nkqmbi,nkpmbo->pqbio", act_one, grad_two, preferred_element_type=jnp.float32
    )
    grad_act = jnp.einsum(
        "nkpmbo,pqbio->nkqmbi", grad_two, second_pair, preferred_element_type=jnp.float32
    )
    grad_one = jax.vjp(jax.nn.gelu, pre_one)[1](grad_act)[0].astype(jnp.bfloat16)
    grad_bias_one = jnp.sum(grad_one.astype(jnp.float32), axis=(0, 1, 3))
    grad_first = jnp.einsum(
        "nkqmbi,nkpmbo->pqbio", blocked, grad_one, preferred_element_type=jnp.float32
    )
    grad_spectrum = jnp.einsum(
        "nkpmbo,pqbio->nkqmbi", grad_one, first_pair, preferred_element_type=jnp.float32
    ).astype(jnp.bfloat16)
    grad_spectrum = grad_spectrum.reshape(snap_local, lat_total, 2, mode_local, channel)
    grad_lon = jnp.einsum(
        "pkqr,nkpmd->nrqmd", lat_fwd, grad_spectrum, preferred_element_type=jnp.float32
    ).astype(jnp.bfloat16)
    grad_rows = lax.all_to_all(grad_lon, "sp", split_axis=1, concat_axis=3, tiled=True)
    grad_normed = grad_mixture + jnp.einsum(
        "nrqmd,lqm->nrld", grad_rows, lon_fwd, preferred_element_type=jnp.float32
    )
    grad_field_norm, grad_gain_one, grad_shift_one = norm_pull(grad_normed)
    input_grad = grad_mixture + grad_field_norm
    grad_filter = jnp.stack(
        [
            grad_first[0, 0] + grad_first[1, 1],
            grad_first[1, 0] - grad_first[0, 1],
            grad_second[0, 0] + grad_second[1, 1],
            grad_second[1, 0] - grad_second[0, 1],
        ]
    ).reshape(4, channel, block_width)
    grad_small = jnp.concatenate(
        [
            jnp.stack([grad_gain_one, grad_shift_one, grad_gain_two, grad_shift_two]),
            grad_bias_one.reshape(2, channel),
            grad_bias_two.reshape(2, channel),
            grad_bias_out[None, :],
            grad_bias_hidden.reshape(-1, channel),
        ],
        axis=0,
    )
    shares = (
        jnp.stack([
            lax.psum_scatter(part, "sp", scatter_dimension=0, tiled=True) for part in passed[2:4]
        ]),
        lax.psum_scatter(grad_filter, "sp", scatter_dimension=1, tiled=True),
        lax.psum_scatter(grad_small, "sp", scatter_dimension=1, tiled=True),
    )
    owned = (
        lax.psum(shares[0].astype(jnp.bfloat16), "snap").astype(jnp.float32),
        lax.psum(shares[1].astype(jnp.bfloat16), "snap").astype(jnp.float32),
        lax.psum(shares[2].astype(jnp.bfloat16), "snap").astype(jnp.float32),
    )
    mlp_new, mlp_first_new, mlp_second_new, mlp_copy = adamw(
        mlp_master, mlp_first, mlp_second, owned[0], rate_mlp
    )
    filter_new, filter_first_new, filter_second_new, filter_copy = adamw(
        filter_master, filter_first, filter_second, owned[1], rate_filter
    )
    small_new, small_first_new, small_second_new, small_copy = adamw(
        small_master, small_first, small_second, owned[2], rate_small
    )
    return (
        output.astype(jnp.bfloat16),
        input_grad,
        mlp_new,
        mlp_first_new,
        mlp_second_new,
        mlp_copy,
        filter_new,
        filter_first_new,
        filter_second_new,
        filter_copy,
        small_new,
        small_first_new,
        small_second_new,
        small_copy,
        stats_new,
    )


FIRST, SECOND, THIRD, FOURTH, HALF, QUARTER, LEVEL, LAST = range(8)
SCHEDULE = {
    "a": [(FIRST, 0), (FIRST, 1)],
    "c1": [(SECOND, 0)],
    "e": [(SECOND, 1), (FIRST, 2)],
    "f0": [(THIRD, 0)],
    "f1": [(THIRD, 1), (FIRST, 3)],
    "g": [(FIRST, 4), (FIRST, 5)],
    "i1": [(FOURTH, 0), (SECOND, 2)],
    "j": [(SECOND, 3)],
    ("k", 0): [(FOURTH, 1)],
    ("l", 0): [(THIRD, 2), (SECOND, 4)],
    ("m", 0): [(THIRD, 3)],
    ("n", 0): [(HALF, 0), (THIRD, 4)],
    ("l", 1): [(FOURTH, 2)],
    ("n", 1): [(FOURTH, 3)],
    ("l", 2): [(QUARTER, 0), (HALF, 1)],
    ("k", 3): [(LEVEL, 0), (HALF, 2), (FOURTH, 4), (FOURTH, 5)],
    ("l", 3): [(QUARTER, 1)],
    ("n", 3): [(LAST, 0), (LEVEL, 1)],
    ("k", 4): [(QUARTER, 2)],
    ("l", 4): [(HALF, 3)],
    ("m", 4): [(LEVEL, 2)],
    ("k", 5): [(QUARTER, 3), (HALF, 4)],
    ("l", 5): [(LAST, 1)],
    ("m", 5): [(LEVEL, 3)],
    "o0": [(QUARTER, 4)],
    "p0": [(HALF, 5)],
    "p1": [(LAST, 2), (LEVEL, 4)],
    "s": [(QUARTER, 5)],
    "u1": [(LAST, 3)],
    "w": [(LAST, 4), (LEVEL, 5)],
    "z": [(LAST, 5)],
}


def lon_matrix(lon_total, mode_total, snaps, rows):
    places = np.arange(lon_total)
    orders = np.arange(mode_total)
    angles = (places[:, None] * orders[None, :] % lon_total) * (2.0 * math.pi / lon_total)
    doubling = np.where(orders == 0, 1.0, 2.0)
    scaling = 1.0 / math.sqrt(lon_total)
    forward = np.stack([np.cos(angles), -np.sin(angles)], axis=1) * scaling
    inverse = forward * doubling

    def spread(table):
        table = np.einsum(
            "ab,lx,rs->alrbsx", np.eye(snaps), table.reshape(lon_total, -1), np.eye(rows)
        )
        return table.reshape(snaps * lon_total * rows, -1).astype(ml_dtypes.bfloat16)

    return spread(forward), spread(inverse)


def lon_turn(lon_total, rows):
    turn = np.einsum("lk,rs->rlks", np.eye(lon_total), np.eye(rows))
    return turn.reshape(rows, lon_total, lon_total * rows).astype(ml_dtypes.bfloat16)


def lat_matrix(lat_total, mode_total):
    places = np.arange(lat_total)
    angles = (places[:, None] * places[None, :] % lat_total) * (2.0 * math.pi / lat_total)
    cosine, sine = np.cos(angles), np.sin(angles)
    table = np.stack([np.stack([cosine, sine], axis=1), np.stack([-sine, cosine], axis=1)])
    table = np.einsum("pkqr,ab->pakrqb", table / math.sqrt(lat_total), np.eye(mode_total))
    size = 2 * lat_total * mode_total
    return table.reshape(size, size).astype(ml_dtypes.bfloat16)


class Refs:
    pass


def block_body(names, sizes, *refs):
    g = Refs()
    for name, ref in zip(names, refs, strict=True):
        setattr(g, name, ref)
    snaps, group, parts, width = sizes
    levels = group // 2
    tokens = g.fields.shape[0] * g.fields.shape[1]
    channel = g.fields.shape[2]
    owned = channel // group
    half = width // 2
    quarter = width // snaps
    tile = tokens // 3
    short = divisor(tokens // 2, 16, 240)
    packed = g.modes.shape[2]
    strip = divisor(tokens // 2, 48, 144)
    sub = divisor(strip, 16, 48)
    low = jnp.bfloat16
    f32 = jnp.float32

    me_snap = lax.axis_index("snap")
    me_sp = lax.axis_index("sp")
    core = lax.rem(me_sp, 2)
    level = me_sp // 2

    def at(snap, sp):
        return {"snap": snap, "sp": sp}

    def sp_after(step):
        return lax.rem(me_sp + step, group)

    def sp_before(step):
        return lax.rem(me_sp + group - step, group)

    def snap_after(step):
        return lax.rem(me_snap + step, snaps)

    def snap_before(step):
        return lax.rem(me_snap + snaps - step, snaps)

    def level_after(step):
        return lax.rem(level + step, levels)

    def level_before(step):
        return lax.rem(level + levels - step, levels)

    other_core = at(me_snap, me_sp + 1 - 2 * core)

    def send(src, dst, sems, index, target):
        return pltpu.make_async_remote_copy(
            src_ref=src,
            dst_ref=dst,
            send_sem=sems[0].at[index],
            recv_sem=sems[1].at[index],
            device_id=target,
            device_id_type=pl.DeviceIdType.MESH,
        )

    half_tokens = tokens // 2

    def strips(body, first=0, count=tokens, before=None, after=None):
        @pl.loop(0, count // strip)
        def _(step):
            if before is not None:
                before(first // strip + step)
            for at_row in range(0, strip, sub):
                body(pl.ds(pl.multiple_of(first + step * strip + at_row, 16), sub))
            if after is not None:
                after(first // strip + step)

    def half_strips(body, part, **around):
        strips(body, part * half_tokens, half_tokens, **around)

    def strip_copy(near, far, sems, place, out):
        rows = pl.ds(pl.multiple_of(place * strip, strip), strip)
        ends = [near.at[rows], far.reshape(tokens, channel).at[rows]]
        if not out:
            ends.reverse()
        return pltpu.make_async_copy(*ends, sems.at[place])

    def fields_load(place):
        return strip_copy(g.fields_in, g.fields, g.fields_sem, place, False)

    def cot_load(place):
        return strip_copy(g.cot_in, g.cot, g.cot_sem, place, False)

    def out_copy(place):
        return strip_copy(g.fields_in, g.out, g.fields_sem, place, True)

    def grad_copy(place):
        return strip_copy(g.grid, g.in_grad, g.cot_sem, place, True)

    def half_rows(part):
        return slice(part * half_tokens, (part + 1) * half_tokens)

    def fold(value):
        return jnp.sum(value.reshape(-1, 8, value.shape[1]), axis=0)

    loads = {}

    def load(name, index):
        copy = pltpu.make_async_copy(getattr(g, name), getattr(g, name + "_in"), g.load_sem.at[index])
        copy.start()
        loads[name] = copy

    for index, name in enumerate(
        [name for name in names[: names.index("out")] if name not in ("mlp", "fields", "cot")]
    ):
        load(name, index)
    for copy in (fields_load, cot_load):
        for place in range(tokens // strip):
            copy(place).start()

    def master_load(part):
        return pltpu.make_async_copy(
            g.mlp.at[:, :, part * width : (part + 1) * width],
            g.mlp_part.at[part % 2],
            g.load_sem.at[len(loads) + part % 2],
        )

    master_load(0).start()
    master_load(1).start()

    barrier = pltpu.get_barrier_semaphore()
    peers = [at(me_snap, sp_after(step)) for step in range(1, group)]
    peers += [at(snap_after(step), me_sp) for step in range(1, snaps)]
    for peer in peers:
        pl.semaphore_signal(
            barrier, inc=1, device_id=peer, device_id_type=pl.DeviceIdType.MESH
        )

    loads["small"].wait()
    loads["kept"].wait()
    g.own_small[...] = jnp.zeros_like(g.own_small)
    rows_small = g.small.shape[0]
    g.own_small[0:rows_small, 0:owned] = g.small_in[...].astype(low).astype(f32)
    pairs_kept = g.kept.shape[1]
    lines = lax.broadcasted_iota(jnp.int32, (pairs_kept, pairs_kept), 0)
    places = lax.broadcasted_iota(jnp.int32, (pairs_kept, pairs_kept), 1)
    kept = jnp.where(lines == places, g.kept_in[...].astype(f32), 0.0)
    g.own_small[16:, :] = jnp.broadcast_to(
        jnp.sum(kept, axis=1, keepdims=True), (pairs_kept, g.own_small.shape[1])
    )
    pl.semaphore_wait(barrier, len(peers))

    def small_copy(step):
        return send(
            g.own_small, g.all_small.at[me_sp], (g.small_s, g.small_r), step, at(me_snap, sp_after(step))
        )

    for step in range(1, group):
        small_copy(step).start()
    g.all_small[me_sp] = g.own_small[...]

    snap_low = lax.rem(me_snap, 2)
    snap_high = me_snap // 2
    beside_low = me_snap + 1 - 2 * snap_low
    beside_high = me_snap + 2 - 4 * snap_high

    def own_quarter(part):
        odd = lax.rem(part, 2)
        return (1 - odd) * me_snap + odd * (2 * snap_low + snap_high)

    def own_place(part):
        return pl.ds(0, snaps) if part == parts - 1 else own_quarter(part)

    def half_quarters(part):
        return pl.ds(2 * (own_quarter(part) // 2), 2)

    def own_rows(sp):
        return pl.ds(pl.multiple_of(sp * owned, owned), owned)

    def first_copy(part, step):
        target = sp_after(step)
        matrix = lax.rem(target, 2)
        place = own_place(part)
        return send(
            g.own_w.at[part, matrix, place],
            g.all_w.at[part, matrix, place, own_rows(me_sp)],
            (g.first_s, g.first_r),
            (part, step),
            at(me_snap, target),
        )

    def first_local(part):
        place = own_place(part)
        return pltpu.make_async_copy(
            g.own_w.at[part, core, place],
            g.all_w.at[part, core, place, own_rows(me_sp)],
            g.first_s.at[part, 0],
        )

    def second_copy(part):
        odd = lax.rem(part, 2)
        view = g.all_w.at[part, core, own_quarter(part)]
        target = at((1 - odd) * beside_low + odd * beside_high, me_sp)
        return send(view, view, (g.second_s, g.second_r), part, target)

    def third_copy(part):
        odd = lax.rem(part, 2)
        view = g.all_w.at[part, core, half_quarters(part)]
        target = at((1 - odd) * beside_high + odd * beside_low, me_sp)
        return send(view, view, (g.third_s, g.third_r), part, target)

    def fourth_copy(part):
        view = g.all_w.at[part, core]
        return send(view, view, (g.fourth_s, g.fourth_r), part, other_core)

    def start_first(part):
        for step in range(1, group):
            first_copy(part, step).start()
        first_local(part).start()

    def wait_first(part):
        for step in range(1, group):
            first_copy(part, step).wait_recv()
        first_local(part).wait()

    def pass_second(part):
        wait_first(part)
        second_copy(part).start()

    def pass_third(part):
        second_copy(part).wait_recv()
        third_copy(part).start()

    def pass_fourth(part):
        if part == parts - 1:
            wait_first(part)
        else:
            third_copy(part).wait_recv()
        fourth_copy(part).start()

    stages = {FIRST: start_first, SECOND: pass_second, THIRD: pass_third, FOURTH: pass_fourth}

    def reach(point):
        for stage, part in SCHEDULE.get(point, ()):
            stages[stage](part)

    for part in range(parts):
        master_load(part).wait()
        for place in range(snaps):
            cols = slice(place * quarter, (place + 1) * quarter)
            g.own_w[part, :, place] = g.mlp_part[part % 2, :, :, cols].astype(low)
        if part + 2 < parts:
            master_load(part + 2).start()
        if (FIRST, part) in SCHEDULE["a"]:
            start_first(part)

    def first_unit(rows):
        values = g.fields_in[rows, :].astype(f32)
        centred = values - jnp.mean(values, axis=-1, keepdims=True)
        scale = lax.rsqrt(jnp.mean(centred * centred, axis=-1, keepdims=True) + eps_norm)
        g.scale_one[rows, :] = scale
        g.grid[rows, :] = centred * scale

    strips(first_unit, before=lambda place: fields_load(place).wait())
    reach("b")
    for step in range(1, group):
        small_copy(step).wait_recv()
    for sp in range(group):
        g.gains[:, sp * owned : (sp + 1) * owned] = g.all_small[sp, 0:16, 0:owned]
        g.keep[sp * pairs_kept : (sp + 1) * pairs_kept, :] = g.all_small[sp, 16:, :]

    def first_norm(rows):
        unit = g.grid[rows, :]
        normed = unit * g.gains[0:1, :] + g.gains[1:2, :]
        g.unit_one[rows, :] = unit.astype(low)
        g.normed[rows, :] = normed.astype(low)
        g.grid[rows, :] = g.fields_in[rows, :].astype(f32) + normed

    half_snaps = g.arrived.shape[0] // 2

    third_rows = packed // 3
    spare = 128 - owned

    def pack(value):
        return jnp.concatenate(
            [
                jnp.concatenate(
                    [
                        value[at_row * third_rows : (at_row + 1) * third_rows],
                        value[packed:, at_row * spare : (at_row + 1) * spare],
                    ],
                    axis=1,
                )
                for at_row in range(3)
            ],
            axis=0,
        ).astype(low)

    def unpack(value):
        value = value.astype(f32)
        rest = [
            value[at_row * third_rows : (at_row + 1) * third_rows, owned:] for at_row in range(3)
        ]
        return jnp.concatenate([value[:, 0:owned], jnp.concatenate(rest, axis=1)], axis=0)

    def block_copy(which, part, step):
        target = sp_after(step)
        return send(
            g.modes.at[part, target],
            g.modes_got.at[part, me_sp],
            (g.block_s, g.block_r),
            (which, part, step),
            at(me_snap, target),
        )

    def row_copy(which, part, step):
        target = sp_after(step)
        return send(
            g.rows_out.at[part, target],
            g.rows_got.at[part, me_sp],
            (g.row_s, g.row_r),
            (which, part, step),
            at(me_snap, target),
        )

    def to_blocks(table, which, part):
        modes = dot_nn(table, g.normed[half_rows(part), :])
        for block in range(group):
            g.modes[part, block] = pack(modes[:, block * owned : (block + 1) * owned])
        for step in range(1, group):
            block_copy(which, part, step).start()
        g.modes_got[part, me_sp] = g.modes[part, me_sp]

    def take_blocks(which, part):
        for step in range(1, group):
            block_copy(which, part, step).wait_recv()
        each = g.arrived.shape[1] // group
        for sp in range(group):
            value = unpack(g.modes_got[part, sp])
            value = jnp.concatenate([value, jnp.zeros((value.shape[0], spare), f32)], axis=1)
            for index in range(half_snaps):
                g.arrived[part * half_snaps + index, sp * each : (sp + 1) * each, :] = value[
                    index * each : (index + 1) * each
                ].astype(low)

    def to_rows(which, part, tables):
        each = tables[0].shape[0] // group
        for sp in range(group):
            value = [table[sp * each : (sp + 1) * each, 0:owned] for table in tables]
            g.rows_out[part, sp] = pack(jnp.concatenate(value, axis=0))
        for step in range(1, group):
            row_copy(which, part, step).start()
        g.rows_got[part, me_sp] = g.rows_out[part, me_sp]

    def home_modes(which, part):
        for step in range(1, group):
            row_copy(which, part, step).wait_recv()
        for block in range(group):
            g.gathered[part, :, block * owned : (block + 1) * owned] = unpack(
                g.rows_got[part, block]
            )
        g.home_low[part] = g.gathered[part].astype(low)

    loads["lon_f"].wait()
    for part in range(2):
        half_strips(first_norm, part)
        reach("c" + str(part))
        to_blocks(g.lon_f_in[...], 0, part)
        reach("d" + str(part))

    loads["filt"].wait()
    for weight, first in ((g.weight_one, 0), (g.weight_two, 2)):
        weight[...] = jnp.zeros_like(weight)
        real = g.filt_in[first].astype(low)
        imag = g.filt_in[first + 1].astype(low)
        weight[0:owned, 0:owned] = real
        weight[128 : 128 + owned, 128 : 128 + owned] = real
        weight[0:owned, 128 : 128 + owned] = imag
        weight[128 : 128 + owned, 0:owned] = -imag

    def bias_row(first):
        return jnp.concatenate(
            [g.own_small[first : first + 1, :], g.own_small[first + 1 : first + 2, :]], axis=1
        )

    for place in range(tokens // strip):
        cot_load(place).wait()
    reach("e")
    loads["lat_f"].wait()
    loads["lat_b"].wait()
    pairs = g.arrived.shape[1] // 2
    half_modes = half_snaps * pairs

    def mode_half(part):
        return slice(part * half_modes, (part + 1) * half_modes)

    def spectra(out, kind, part):
        for snap in range(part * half_snaps, (part + 1) * half_snaps):
            spectrum = dot_nn(g.lat_f_in[...], g.arrived[snap]).astype(kind)
            rows = slice(snap * pairs, (snap + 1) * pairs)
            out[rows, 0:128] = spectrum[0:pairs]
            out[rows, 128:256] = spectrum[pairs:]

    def grids(values):
        tables = []
        for index in range(half_snaps):
            rows = values[index * pairs : (index + 1) * pairs]
            rows = jnp.concatenate([rows[:, 0:128], rows[:, 128:256]], axis=0)
            tables.append(dot_nn(g.lat_b_in[...], rows))
        return tables

    def keep_half():
        keep = jnp.concatenate([g.keep[...], g.keep[...]], axis=1)
        return jnp.concatenate([keep] * half_snaps, axis=0)

    for part in range(2):
        take_blocks(0, part)
        rows = mode_half(part)
        spectra(g.spectrum, low, part)
        g.pre_one[rows, :] = dot_nn(g.spectrum[rows, :], g.weight_one[...]) + bias_row(4)
        g.act_one[rows, :] = gelu_both(g.pre_one[rows, :])[0].astype(low)
        g.pre_two[rows, :] = dot_nn(g.act_one[rows, :], g.weight_two[...]) + bias_row(6)
        to_rows(0, part, grids((shrink(g.pre_two[rows, :]) * keep_half()).astype(low)))
        reach("f" + str(part))
    g.cot_turned[...] = g.cot_in[...].T
    reach("g")

    loads["lon_i"].wait()

    def second_norm(rows):
        values = g.grid[rows, :]
        centred = values - jnp.mean(values, axis=-1, keepdims=True)
        scale = lax.rsqrt(jnp.mean(centred * centred, axis=-1, keepdims=True) + eps_norm)
        centred = centred * scale
        g.unit_two[rows, :] = centred.astype(low)
        g.scale_two[rows, :] = scale
        g.normed[rows, :] = (centred * g.gains[2:3, :] + g.gains[3:4, :]).astype(low)
        g.grid[rows, :] = values + g.gains[8:9, :]
        g.back[rows, :] = jnp.zeros((sub, channel), f32)

    for part in range(2):
        home_modes(0, part)
        g.grid[half_rows(part), :] += dot_nn(g.lon_i_in[...], g.home_low[part])
        reach("h" + str(part))
        half_strips(second_norm, part)
        reach("i" + str(part))
    g.normed_turned[...] = g.normed[...].T
    reach("j")
    flat = jnp.concatenate([g.gains[9 + row : 10 + row, :] for row in range(rows_small - 9)], axis=1)
    for part in range(parts):
        g.bias[part] = flat[:, part * width : (part + 1) * width]

    def core_copy(part, matrix):
        slot = lax.rem(part, 2)
        return send(
            g.grads.at[matrix, :, 1 - core],
            g.core_got.at[slot, matrix],
            (g.core_s, g.core_r),
            (slot, matrix),
            other_core,
        )

    places_one = (snap_low, snap_high)
    places_two = (snap_high, snap_low)
    beside_one = (beside_low, beside_high)
    beside_two = (beside_high, beside_low)

    def half_copy(part, matrix):
        slot = lax.rem(part, 2)
        place = lax.rem(part, 4)
        return send(
            g.half_out.at[slot, matrix, 1 - places_one[matrix]],
            g.half_got.at[place, matrix],
            (g.half_s, g.half_r),
            (place, matrix),
            at(beside_one[matrix], me_sp),
        )

    def quarter_copy(part, matrix):
        slot = lax.rem(part, 2)
        return send(
            g.quarter_out.at[slot, matrix, 1 - places_two[matrix]],
            g.quarter_got.at[slot, matrix],
            (g.quarter_s, g.quarter_r),
            (slot, matrix),
            at(beside_two[matrix], me_sp),
        )

    def level_copy(part, step):
        slot = lax.rem(part, 2)
        place = lax.rem(part, 4)
        target = level_after(step)
        return send(
            g.level_out.at[slot, target],
            g.level_got.at[place, level],
            (g.level_s, g.level_r),
            (place, step),
            at(me_snap, 2 * target + core),
        )

    def last_copy(part, step):
        view = g.total.at[part, me_snap]
        return send(view, view, (g.last_s, g.last_r), (part, step), at(snap_after(step), me_sp))

    def half_stage(part):
        slot = lax.rem(part, 2)
        for matrix in range(2):

            if part >= 2:
                half_copy(part - 2, matrix).wait_send()

            core_copy(part, matrix).wait_recv()

            @pl.loop(0, levels)
            def _(row, matrix=matrix):
                both = g.grads[matrix, row, core].astype(f32) + g.core_got[
                    slot, matrix, row
                ].astype(f32)
                both = both.astype(low)
                g.half_out[slot, matrix, 0, row] = both[:, 0:half]
                g.half_out[slot, matrix, 1, row] = both[:, half:width]

            half_copy(part, matrix).start()

    def quarter_stage(part):
        slot = lax.rem(part, 2)
        for matrix in range(2):

            if part >= 2:
                quarter_copy(part - 2, matrix).wait_send()

            half_copy(part, matrix).wait_recv()
            for row in range(levels):
                both = g.half_out[slot, matrix, places_one[matrix], row].astype(f32) + g.half_got[
                    lax.rem(part, 4), matrix, row
                ].astype(f32)
                both = both.astype(low)
                g.quarter_out[slot, matrix, 0, row] = both[:, 0:quarter]
                g.quarter_out[slot, matrix, 1, row] = both[:, quarter:half]
            quarter_copy(part, matrix).start()

    def level_stage(part):
        slot = lax.rem(part, 2)

        if part >= 2:
            for step in range(1, levels):
                level_copy(part - 2, step).wait_send()

        for matrix in range(2):
            quarter_copy(part, matrix).wait_recv()
            for row in range(levels):
                both = g.quarter_out[slot, matrix, places_two[matrix], row].astype(
                    f32
                ) + g.quarter_got[slot, matrix, row].astype(f32)
                g.level_out[slot, row, matrix] = both.astype(low)
        for step in range(1, levels):
            level_copy(part, step).start()

    def last_stage(part):
        slot = lax.rem(part, 2)
        for step in range(1, levels):
            level_copy(part, step).wait_recv()
        for matrix in range(2):
            sums = g.level_out[slot, level, matrix].astype(f32)
            for step in range(1, levels):
                sums += g.level_got[lax.rem(part, 4), level_before(step), matrix].astype(f32)
            g.total[part, me_snap, matrix] = sums.astype(low)
        for step in range(1, snaps):
            last_copy(part, step).start()

    stages |= {HALF: half_stage, QUARTER: quarter_stage, LEVEL: level_stage, LAST: last_stage}

    def weight(part, matrix):
        return jnp.concatenate([g.all_w[part, matrix, place] for place in range(snaps)], axis=1)

    def add_products(part, rows):
        g.grid[rows, :] += dot_nt(g.act[rows, :], weight(part, 1))
        g.back[rows, :] += dot_nt(g.slope[rows, :], weight(part, 0))

    @pl.loop(0, parts)
    def _(part):
        def reach_in(point):
            for at_part in range(parts):
                if (point, at_part) in SCHEDULE:
                    pl.when(part == at_part)(functools.partial(reach, (point, at_part)))

        def tile_rows(step):
            return pl.ds(pl.multiple_of(step * tile, tile), tile)

        fourth_copy(part).wait_recv()
        reach_in("k")
        g.grad_bias[part] = jnp.zeros(g.grad_bias.shape[1:], f32)

        @pl.loop(0, tokens // tile)
        def _(step):
            rows = tile_rows(step)
            act, slope = gelu_both(dot_nn(g.normed[rows, :], weight(part, 0)) + g.bias[part])
            g.act[rows, :] = act.astype(low)
            slope = (dot_nn(g.cot_in[rows, :], weight(part, 1)) * slope).astype(low)
            g.slope[rows, :] = slope
            g.grad_bias[part] += fold(slope.astype(f32))

        reach_in("l")

        @pl.when(part >= 1)
        def _():
            for matrix in range(2):
                core_copy(part - 1, matrix).wait_send()

        shape = g.grads.shape[1:]
        g.grads[0] = dot_nn(g.normed_turned[...], g.slope[...]).astype(low).reshape(shape)
        core_copy(part, 0).start()
        g.grads[1] = dot_nn(g.cot_turned[...], g.act[...]).astype(low).reshape(shape)
        core_copy(part, 1).start()
        reach_in("m")

        @pl.when(part < parts - 1)
        def _():
            @pl.loop(0, tokens // tile)
            def _(step):
                add_products(part, tile_rows(step))

            reach_in("n")

    g.folds[...] = jnp.zeros_like(g.folds)

    def second_back(rows):
        grad = g.back[rows, :]
        unit = g.unit_two[rows, :].astype(f32)
        cot = g.cot_in[rows, :].astype(f32)
        pulled = grad * g.gains[2:3, :]
        middle = jnp.mean(pulled, axis=-1, keepdims=True)
        slant = jnp.mean(pulled * unit, axis=-1, keepdims=True)
        total = cot + g.scale_two[rows, :] * (pulled - middle - unit * slant)
        g.back[rows, :] = total
        g.normed[rows, :] = total.astype(low)
        g.folds[2] += fold(grad * unit)
        g.folds[3] += fold(grad)
        g.folds[4] += fold(cot)

    loads["lon_it"].wait()
    for part in range(2):

        @pl.loop(0, half_tokens // short)
        def _(step, part=part):
            first_row = part * half_tokens + step * short
            add_products(parts - 1, pl.ds(pl.multiple_of(first_row, 16), short))

        reach("o" + str(part))
        half_strips(second_back, part)
        for step in range(1, group):
            block_copy(0, part, step).wait_send()
        to_blocks(g.lon_it_in[...], 1, part)
        reach("p" + str(part))
    reach("q")

    def low_out(rows):
        g.fields_in[rows, :] = g.grid[rows, :].astype(low)

    strips(low_out, after=lambda place: out_copy(place).start())
    reach("r")
    loads["valid"].wait()
    loads["turn"].wait()
    weigh = sum(
        dot_nn(g.valid_in[:, row, :].astype(f32).astype(low), g.turn_in[row])
        for row in range(g.valid.shape[1])
    )
    places_each = weigh.shape[1]
    precise = lax.Precision.HIGHEST
    sums = [jnp.zeros((1, 128), f32), jnp.zeros((1, 128), f32)]
    for snap in range(g.valid.shape[0]):
        variables = g.grid[snap * places_each : (snap + 1) * places_each, 0:128]
        for index, value in enumerate((variables, variables * variables)):
            sums[index] += jnp.dot(
                weigh[snap : snap + 1, :], value, precision=precise, preferred_element_type=f32
            )

    reach("s")

    def dot_tn(left, right):
        return lax.dot_general(
            left, right, (((0,), (0,)), ((), ())), preferred_element_type=f32
        )

    def filter_rows(first, grad):
        g.pair_grad[...] = grad
        real = g.pair_grad[0:128, 0:128] + g.pair_grad[128:256, 128:256]
        imag = g.pair_grad[0:128, 128:256] - g.pair_grad[128:256, 0:128]
        g.filt_out[me_snap, first] = real[0:owned].astype(low)
        g.filt_out[me_snap, first + 1] = imag[0:owned].astype(low)

    for part in range(2):
        take_blocks(1, part)
        reach("t" + str(part))
        rows = mode_half(part)
        spectra(g.grad_pre, f32, part)
        bend = jnp.tanh(g.pre_two[rows, :] / shrink_level)
        grad = (g.grad_pre[rows, :] * keep_half() * (bend * bend)).astype(low)
        g.grad_two[rows, :] = grad
        grad = dot_nt(grad, g.weight_two[...]) * gelu_both(g.pre_one[rows, :])[1]
        grad = grad.astype(low)
        g.grad_one[rows, :] = grad
        for step in range(1, group):
            row_copy(0, part, step).wait_send()
        to_rows(1, part, grids(dot_nt(grad, g.weight_one[...]).astype(low)))
        reach("u" + str(part))
    reach("v")
    bias_one = jnp.sum(g.grad_one[...].astype(f32), axis=0, keepdims=True)
    bias_two = jnp.sum(g.grad_two[...].astype(f32), axis=0, keepdims=True)
    filter_rows(2, dot_tn(g.act_one[...], g.grad_two[...]))
    filter_rows(0, dot_tn(g.spectrum[...], g.grad_one[...]))

    def filter_copy(step):
        view = g.filt_out.at[me_snap]
        return send(view, view, (g.filt_s, g.filt_r), step, at(snap_after(step), me_sp))

    for step in range(1, snaps):
        filter_copy(step).start()


    reach("w")

    loads["lon_ft"].wait()

    def first_back(rows):
        grad = g.grid[rows, :]
        unit = g.unit_one[rows, :].astype(f32)
        pulled = grad * g.gains[0:1, :]
        middle = jnp.mean(pulled, axis=-1, keepdims=True)
        slant = jnp.mean(pulled * unit, axis=-1, keepdims=True)
        g.grid[rows, :] = g.back[rows, :] + g.scale_one[rows, :] * (
            pulled - middle - unit * slant
        )
        g.folds[0] += fold(grad * unit)
        g.folds[1] += fold(grad)

    for part in range(2):
        home_modes(1, part)
        reach("x" + str(part))
        g.grid[half_rows(part), :] = g.back[half_rows(part), :] + dot_nn(
            g.lon_ft_in[...], g.home_low[part]
        )
        half_strips(first_back, part, after=lambda place: grad_copy(place).start())
        reach("y" + str(part))

    g.grad_rows[...] = jnp.zeros_like(g.grad_rows)
    for index, row in enumerate((0, 1, 2, 3, 8)):
        g.grad_rows[row : row + 1, :] = jnp.sum(g.folds[index], axis=0, keepdims=True)
    flat = jnp.concatenate(
        [jnp.sum(g.grad_bias[part], axis=0, keepdims=True) for part in range(parts)], axis=1
    )
    for row in range(rows_small - 9):
        g.grad_rows[9 + row : 10 + row, :] = flat[:, row * channel : (row + 1) * channel]
    for block in range(group):
        g.tiles[block] = jnp.zeros(g.tiles.shape[1:], f32)
        g.tiles[block, :, 0:owned] = g.grad_rows[:, block * owned : (block + 1) * owned]
        g.tiles[block, 13:14, :] = sums[0]
        g.tiles[block, 14:15, :] = sums[1]

    def tile_copy(step):
        target = sp_after(step)
        return send(
            g.tiles.at[target], g.tiles_got.at[me_sp], (g.tile_s, g.tile_r), step, at(me_snap, target)
        )

    def snap_tile_copy(step):
        view = g.snap_tiles.at[me_snap]
        return send(view, view, (g.snap_tile_s, g.snap_tile_r), step, at(snap_after(step), me_sp))

    for step in range(1, group):
        tile_copy(step).start()
    reach("z")

    g.tiles_got[me_sp] = g.tiles[me_sp]
    for step in range(1, group):
        tile_copy(step).wait_recv()
    tile_sum = g.tiles_got[0]
    for sp in range(1, group):
        tile_sum += g.tiles_got[sp]
    g.snap_tiles[me_snap] = tile_sum
    g.snap_tiles[me_snap, 4:5, :] = bias_one[:, 0:128]
    g.snap_tiles[me_snap, 5:6, :] = bias_one[:, 128:256]
    g.snap_tiles[me_snap, 6:7, :] = bias_two[:, 0:128]
    g.snap_tiles[me_snap, 7:8, :] = bias_two[:, 128:256]
    for step in range(1, snaps):
        snap_tile_copy(step).start()

    for step in range(1, snaps):
        filter_copy(step).wait_recv()
    filter_sum = g.filt_out[0].astype(f32)
    for snap in range(1, snaps):
        filter_sum += g.filt_out[snap].astype(f32)
    g.grad_filt[...] = filter_sum
    for part in range(parts):
        for step in range(1, snaps):
            last_copy(part, step).wait_recv()
    grads_out = pltpu.make_async_copy(g.total, g.grad_mlp, g.load_sem.at[3])
    grads_out.start()
    for step in range(1, snaps):
        snap_tile_copy(step).wait_recv()
    tile_sum = g.snap_tiles[0]
    for snap in range(1, snaps):
        tile_sum += g.snap_tiles[snap]
    g.grad_small[...] = tile_sum

    grads_out.wait()
    for place in range(tokens // strip):
        out_copy(place).wait()
        grad_copy(place).wait()
    for step in range(1, group):
        small_copy(step).wait_send()
        for part in range(2):
            block_copy(1, part, step).wait_send()
            row_copy(1, part, step).wait_send()
        tile_copy(step).wait_send()
        for part in range(parts):
            first_copy(part, step).wait_send()
    for part in range(parts):
        if part < parts - 1:
            second_copy(part).wait_send()
            third_copy(part).wait_send()
        fourth_copy(part).wait_send()
    for matrix in range(2):
        core_copy(parts - 1, matrix).wait_send()
    for part in (parts - 2, parts - 1):
        for matrix in range(2):
            half_copy(part, matrix).wait_send()
            quarter_copy(part, matrix).wait_send()
        for step in range(1, levels):
            level_copy(part, step).wait_send()
    for step in range(1, snaps):
        filter_copy(step).wait_send()
        snap_tile_copy(step).wait_send()
        for part in range(parts):
            last_copy(part, step).wait_send()


def block_pass(fields, cot, valid, kept, mlp, filt, small, snaps, group):
    snap_local, row_local, lon_total, channel = fields.shape
    tokens = snap_local * row_local * lon_total
    hidden = mlp.shape[2]
    lat_total = row_local * group
    modes = kept.shape[1] * group
    owned = channel // group
    width = 512
    parts = hidden // width
    levels = group // 2
    quarter = width // snaps
    low, f32 = jnp.bfloat16, jnp.float32
    half = width // 2
    half_snaps = snap_local // 2
    lon_f, lon_i = lon_matrix(lon_total, modes, half_snaps, row_local)

    def paired(array):
        return jnp.transpose(array, (0, 2, 1, 3)).reshape(-1, row_local, channel)

    lat_f = lat_matrix(lat_total, modes)
    pair = 2 * modes * row_local
    spread = half_snaps * row_local * 2 * modes
    inputs = dict(
        small=small,
        kept=kept.T,
        fields=paired(fields),
        lon_f=jnp.asarray(np.ascontiguousarray(lon_f.T)),
        filt=filt,
        lat_f=jnp.asarray(lat_f),
        lat_b=jnp.asarray(np.ascontiguousarray(lat_f.T)),
        cot=paired(cot),
        lon_i=jnp.asarray(lon_i),
        valid=valid,
        turn=jnp.asarray(lon_turn(lon_total, row_local)),
        lon_it=jnp.asarray(np.ascontiguousarray(lon_i.T)),
        lon_ft=jnp.asarray(lon_f),
        mlp=mlp,
    )
    outputs = dict(
        out=jax.ShapeDtypeStruct((tokens // row_local, row_local, channel), low),
        in_grad=jax.ShapeDtypeStruct((tokens // row_local, row_local, channel), f32),
        grad_mlp=jax.ShapeDtypeStruct((parts, snaps, 2, owned, quarter), low),
        grad_filt=jax.ShapeDtypeStruct((4, owned, 128), f32),
        grad_small=jax.ShapeDtypeStruct((16, 128), f32),
    )
    vmem = pltpu.VMEM
    dma = pltpu.SemaphoreType.DMA
    scratch = {
        name + "_in": vmem(value.shape, value.dtype)
        for name, value in inputs.items()
        if name not in ("mlp", "fields", "cot")
    }
    strip = divisor(tokens // 2, 48, 144)
    scratch |= dict(
        mlp_part=vmem((2, 2, owned, width), f32),
        fields_in=vmem((tokens, channel), low),
        fields_sem=dma((tokens // strip,)),
        cot_sem=dma((tokens // strip,)),
        cot_in=vmem((tokens, channel), low),
        grid=vmem((tokens, channel), f32),
        back=vmem((tokens, channel), f32),
        normed=vmem((tokens, channel), low),
        normed_turned=vmem((channel, tokens), low),
        cot_turned=vmem((channel, tokens), low),
        unit_one=vmem((tokens, channel), low),
        unit_two=vmem((tokens, channel), low),
        scale_one=vmem((tokens, 1), f32),
        scale_two=vmem((tokens, 1), f32),
        own_small=vmem((16 + kept.shape[0], 128), f32),
        all_small=vmem((group, 16 + kept.shape[0], 128), f32),
        gains=vmem((16, channel), f32),
        keep=vmem((lat_total * modes, 128), f32),
        own_w=vmem((parts, 2, snaps, owned, quarter), low),
        all_w=vmem((parts, 2, snaps, channel, quarter), low),
        modes=vmem((2, group, half_snaps * pair * 3 // 4, 128), low),
        modes_got=vmem((2, group, half_snaps * pair * 3 // 4, 128), low),
        rows_out=vmem((2, group, half_snaps * pair * 3 // 4, 128), low),
        rows_got=vmem((2, group, half_snaps * pair * 3 // 4, 128), low),
        arrived=vmem((snap_local, pair * group, 128), low),
        gathered=vmem((2, spread, channel), f32),
        home_low=vmem((2, spread, channel), low),
        weight_one=vmem((256, 256), low),
        weight_two=vmem((256, 256), low),
        spectrum=vmem((snap_local * lat_total * modes, 256), low),
        pre_one=vmem((snap_local * lat_total * modes, 256), f32),
        act_one=vmem((snap_local * lat_total * modes, 256), low),
        pre_two=vmem((snap_local * lat_total * modes, 256), f32),
        grad_pre=vmem((snap_local * lat_total * modes, 256), f32),
        grad_two=vmem((snap_local * lat_total * modes, 256), low),
        grad_one=vmem((snap_local * lat_total * modes, 256), low),
        folds=vmem((5, 8, channel), f32),
        pair_grad=vmem((256, 256), f32),
        act=vmem((tokens, width), low),
        slope=vmem((tokens, width), low),
        bias=vmem((parts, 1, width), f32),
        grad_bias=vmem((parts, 8, width), f32),
        grad_rows=vmem((16, channel), f32),
        grads=vmem((2, levels, 2, owned, width), low),
        core_got=vmem((2, 2, levels, owned, width), low),
        half_out=vmem((2, 2, 2, levels, owned, half), low),
        half_got=vmem((4, 2, levels, owned, half), low),
        quarter_out=vmem((2, 2, 2, levels, owned, quarter), low),
        quarter_got=vmem((2, 2, levels, owned, quarter), low),
        level_out=vmem((2, levels, 2, owned, quarter), low),
        level_got=vmem((4, levels, 2, owned, quarter), low),
        total=vmem((parts, snaps, 2, owned, quarter), low),
        filt_out=vmem((snaps, 4, owned, 128), low),
        tiles=vmem((group, 16, 128), f32),
        tiles_got=vmem((group, 16, 128), f32),
        snap_tiles=vmem((snaps, 16, 128), f32),
        load_sem=dma((len(inputs) + 1,)),
    )
    for name, shape in dict(
        small=(group,),
        first=(parts, group),
        second=(parts,),
        third=(parts,),
        fourth=(parts,),
        block=(2, 2, group),
        row=(2, 2, group),
        core=(2, 2),
        half=(4, 2),
        quarter=(2, 2),
        level=(4, levels),
        last=(parts, snaps),
        filt=(snaps,),
        tile=(group,),
        snap_tile=(snaps,),
    ).items():
        scratch[name + "_s"] = dma(shape)
        scratch[name + "_r"] = dma(shape)
    names = [*inputs, *outputs, *scratch]
    far = pl.BlockSpec(memory_space=pl.ANY)
    near = pl.BlockSpec(memory_space=pltpu.VMEM)
    results = pl.pallas_call(
        functools.partial(block_body, names, (snaps, group, parts, width)),
        in_specs=[far] * len(inputs),
        out_specs=[far, far, far, near, near],
        out_shape=list(outputs.values()),
        scratch_shapes=list(scratch.values()),
        compiler_params=pltpu.CompilerParams(
            collective_id=0, has_side_effects=True, vmem_limit_bytes=VMEM_LIMIT
        ),
        cost_estimate=pl.CostEstimate(
            flops=12 * tokens * channel * hidden,
            bytes_accessed=4 * hidden * channel,
            transcendentals=tokens * hidden,
        ),
        name="block_pass",
    )(*inputs.values())
    return results


def step_body(names, positions, *refs):
    g = Refs()
    for name, ref in zip(names, refs, strict=True):
        setattr(g, name, ref)
    parts, snaps = g.grad_mlp.shape[:2]
    quarter = g.grad_mlp.shape[4]
    width = snaps * quarter
    moments = ("w", "m", "v")
    results = ("new", "first", "second", "copy")

    pieces = g.far_sem.shape[2]
    ends = ((g.out, g.out_near, g.out_o), (g.in_grad, g.in_grad_near, g.in_grad_o))

    def passing(kind, piece, leg):
        size = ends[kind][0].shape[0] // pieces
        rows = pl.ds(piece * size, size)
        return pltpu.make_async_copy(
            ends[kind][leg].at[rows], ends[kind][leg + 1].at[rows], g.far_sem.at[leg, kind, piece]
        )

    through = [(kind, piece) for kind in range(2) for piece in range(pieces)]

    def part_cols(part):
        return pl.ds(part * width, width)

    def load(part):
        near = [
            pltpu.make_async_copy(
                getattr(g, "mlp_" + kind).at[:, :, part_cols(part)],
                g.near.at[index, part],
                g.near_sem.at[index, part],
            )
            for index, kind in enumerate(moments)
        ]
        near.append(
            pltpu.make_async_copy(g.grad_mlp.at[part], g.grad_near.at[part], g.near_sem.at[3, part])
        )
        return near

    def store(part):
        copies = [
            pltpu.make_async_copy(
                g.near.at[index, part],
                getattr(g, "mlp_" + kind).at[:, :, part_cols(part)],
                g.back_sem.at[index, part],
            )
            for index, kind in enumerate(results[:3])
        ]
        copies.append(
            pltpu.make_async_copy(
                g.low_near.at[part], g.mlp_copy.at[:, :, part_cols(part)], g.back_sem.at[3, part]
            )
        )
        return copies

    coming = [load(part) for part in range(parts)]
    going = [store(part) for part in range(parts)]
    shares = [through[part::parts] for part in range(parts)]
    for part in range(parts):
        for copy in coming[part]:
            copy.start()
        for each in shares[part]:
            passing(*each, 0).start()

    def put(prefix, values):
        for kind, value in zip(results, values, strict=True):
            getattr(g, prefix + kind)[...] = value

    owned = g.filt_w.shape[2]
    put(
        "filt_",
        adamw(g.filt_w[...], g.filt_m[...], g.filt_v[...], g.grad_filt[:, :, 0:owned], rate_filter),
    )
    rows = g.small_w.shape[0]
    put(
        "small_",
        adamw(
            g.small_w[...], g.small_m[...], g.small_v[...], g.grad_small[0:rows, 0:owned], rate_small
        ),
    )
    totals = g.grad_small[rows : rows + 2, 0 : g.run.shape[1]]
    g.stats[...] = stat_decay * g.run[...] + (1.0 - stat_decay) * totals / positions

    for part in range(parts):
        for copy in coming[part]:
            copy.wait()

        for matrix, snap in [(matrix, snap) for matrix in range(2) for snap in range(snaps)]:
            place = snap if matrix else 2 * (snap % 2) + snap // 2
            where = (matrix, slice(None), slice(place * quarter, (place + 1) * quarter))
            now = [g.near[(index, part, *where)] for index in range(3)]
            grad = g.grad_near[part, snap, matrix].astype(jnp.float32)
            values = adamw(*now, grad, rate_mlp)
            for index in range(3):
                g.near[(index, part, *where)] = values[index]
            g.low_near[(part, *where)] = values[3]
        for copy in going[part]:
            copy.start()
        for each in shares[part]:
            passing(*each, 0).wait()
            passing(*each, 1).start()
    for each in through:
        passing(*each, 1).wait()
    for part in range(parts):
        for copy in going[part]:
            copy.wait()


def step_pass(shown, grads, masters, run_stats, positions):
    grad_mlp, grad_filt, grad_small = grads
    mlp, filt, small = masters
    parts = grad_mlp.shape[0]
    width = mlp[0].shape[2] // parts
    f32, low = jnp.float32, jnp.bfloat16
    far = pl.BlockSpec(memory_space=pltpu.HBM)
    near = pl.BlockSpec(memory_space=pltpu.VMEM)
    inputs = dict(out=shown[0], in_grad=shown[1], grad_mlp=grad_mlp)
    inputs |= dict(zip(("mlp_w", "mlp_m", "mlp_v"), mlp, strict=True))
    far_in = len(inputs)
    inputs |= dict(grad_filt=grad_filt, grad_small=grad_small)
    inputs |= dict(zip(("filt_w", "filt_m", "filt_v"), filt, strict=True))
    inputs |= dict(zip(("small_w", "small_m", "small_v"), small, strict=True))
    inputs |= dict(run=run_stats)
    results = (("new", f32), ("first", f32), ("second", f32), ("copy", low))
    outputs = {
        name + "_o": jax.ShapeDtypeStruct(array.shape, array.dtype)
        for name, array in zip(("out", "in_grad"), shown, strict=True)
    }
    outputs |= {"mlp_" + kind: jax.ShapeDtypeStruct(mlp[0].shape, dt) for kind, dt in results}
    far_out = len(outputs)
    outputs |= {"filt_" + kind: jax.ShapeDtypeStruct(filt[0].shape, dt) for kind, dt in results}
    outputs |= {"small_" + kind: jax.ShapeDtypeStruct(small[0].shape, dt) for kind, dt in results}
    outputs |= dict(stats=jax.ShapeDtypeStruct(run_stats.shape, f32))
    scratch = dict(
        near=pltpu.VMEM((3, parts, 2, mlp[0].shape[1], width), f32),
        grad_near=pltpu.VMEM(grad_mlp.shape, low),
        low_near=pltpu.VMEM((parts, 2, mlp[0].shape[1], width), low),
        near_sem=pltpu.SemaphoreType.DMA((4, parts)),
        back_sem=pltpu.SemaphoreType.DMA((4, parts)),
        out_near=pltpu.VMEM(shown[0].shape, low),
        in_grad_near=pltpu.VMEM(shown[1].shape, f32),
        far_sem=pltpu.SemaphoreType.DMA((2, 2, divisor(shown[0].shape[0], 1, 4))),
    )
    return pl.pallas_call(
        functools.partial(step_body, [*inputs, *outputs, *scratch], positions),
        in_specs=[far] * far_in + [near] * (len(inputs) - far_in),
        out_specs=[far] * far_out + [near] * (len(outputs) - far_out),
        out_shape=list(outputs.values()),
        scratch_shapes=list(scratch.values()),
        compiler_params=pltpu.CompilerParams(vmem_limit_bytes=VMEM_LIMIT),
        name="step_pass",
    )(*inputs.values())


def per_device_blocks(
    fields,
    cotangent,
    valid_mask,
    kept_modes,
    mlp_master,
    mlp_first,
    mlp_second,
    filter_master,
    filter_first,
    filter_second,
    small_master,
    small_first,
    small_second,
    run_stats,
):
    snaps, group = lax.axis_size("snap"), lax.axis_size("sp")
    out, in_grad, *grads = block_pass(
        fields, cotangent, valid_mask, kept_modes, mlp_master, filter_master, small_master, snaps, group
    )
    snap_local, row_local, lon_total, channel = fields.shape
    positions = snap_local * snaps * row_local * group * lon_total
    out, in_grad, *stepped = step_pass(
        (out, in_grad),
        grads,
        (
            (mlp_master, mlp_first, mlp_second),
            (filter_master, filter_first, filter_second),
            (small_master, small_first, small_second),
        ),
        run_stats,
        positions,
    )
    rows_apart = (snap_local, lon_total, row_local, channel)
    out, in_grad = [
        jnp.transpose(array.reshape(rows_apart), (0, 2, 1, 3)) for array in (out, in_grad)
    ]
    return (out, in_grad, *stepped)


def per_device(*arrays):
    group, snaps = lax.axis_size("sp"), lax.axis_size("snap")
    channel, hidden = arrays[0].shape[3], arrays[4].shape[2]
    by_block = group == BLOCKS and snaps == 4 and arrays[3].shape[1] == 1
    if by_block and hidden == 6 * 512 and channel // group <= 128 and channel % (16 * group) == 0:
        return per_device_blocks(*arrays)
    return per_device_modes(*arrays)


def solution(mesh):
    return jax.shard_map(
        per_device,
        mesh=mesh,
        in_specs=(
            P("snap", "sp", None, None),
            P("snap", "sp", None, None),
            P("snap", "sp", None),
            P(None, "sp"),
            P(None, "sp", None),
            P(None, "sp", None),
            P(None, "sp", None),
            P(None, "sp", None),
            P(None, "sp", None),
            P(None, "sp", None),
            P(None, "sp"),
            P(None, "sp"),
            P(None, "sp"),
            P(),
        ),
        out_specs=(
            P("snap", "sp", None, None),
            P("snap", "sp", None, None),
            P(None, "sp", None),
            P(None, "sp", None),
            P(None, "sp", None),
            P(None, "sp", None),
            P(None, "sp", None),
            P(None, "sp", None),
            P(None, "sp", None),
            P(None, "sp", None),
            P(None, "sp"),
            P(None, "sp"),
            P(None, "sp"),
            P(None, "sp"),
            P(),
        ),
        check_vma=False,
    )
```

```python
import functools
import math

import jax
import jax.numpy as jnp
import ml_dtypes
import numpy as np
from jax import lax
from jax.experimental import pallas as pl
from jax.experimental.pallas import tpu as pltpu
from jax.sharding import PartitionSpec as P

BLOCKS = 8
NVAR = 20
STEP = 10
VMEM_LIMIT = 63 * 1024 * 1024


eps_norm = 1e-06
shrink_level = 0.01
beta_one = 0.5
beta_two = 0.5
adam_eps = 1e-08
decay_rate = 0.01
rate_mlp = 0.03
rate_filter = 0.1
rate_small = 0.2
stat_decay = 0.5


def layer_norm(values, gain_vec, shift_vec):
    centred = values - jnp.mean(values, axis=-1, keepdims=True)
    spread = jnp.mean(centred * centred, axis=-1, keepdims=True)
    return centred * lax.rsqrt(spread + eps_norm) * gain_vec + shift_vec


def shrink(values):
    return values - shrink_level * jnp.tanh(values / shrink_level)


def lon_tables(lon_total, mode_total):
    places = jnp.arange(lon_total, dtype=jnp.int32)
    orders = jnp.arange(mode_total, dtype=jnp.int32)
    angles = (places[:, None] * orders[None, :] % lon_total).astype(jnp.float32) * (
        2.0 * math.pi / lon_total
    )
    scaling = 1.0 / math.sqrt(lon_total)
    forward_tab = jnp.stack([jnp.cos(angles), -jnp.sin(angles)], axis=1) * scaling
    doubling = jnp.where(orders == 0, 1.0, 2.0).astype(jnp.float32)[:, None]
    inverse_tab = (
        jnp.stack([jnp.cos(angles).T * doubling, -jnp.sin(angles).T * doubling], axis=0) * scaling
    )
    return (forward_tab.astype(jnp.bfloat16), inverse_tab.astype(jnp.bfloat16))


def lat_table(lat_total):
    places = jnp.arange(lat_total, dtype=jnp.int32)
    angles = (places[:, None] * places[None, :] % lat_total).astype(jnp.float32) * (
        2.0 * math.pi / lat_total
    )
    cosine = jnp.cos(angles)
    sine_part = jnp.sin(angles)
    upper_rows = jnp.stack([cosine, sine_part], axis=1)
    bottom = jnp.stack([-sine_part, cosine], axis=1)
    return (jnp.stack([upper_rows, bottom], axis=0) / math.sqrt(lat_total)).astype(jnp.bfloat16)


def complex_pair(real_part, imag_part):
    return jnp.stack([jnp.stack([real_part, -imag_part]), jnp.stack([imag_part, real_part])])


gelu_scale = math.sqrt(2.0 / math.pi)
gelu_cubic = 0.044715


def gelu_both(value):
    bend = (gelu_scale * gelu_cubic) * (value * value)
    turn = jnp.tanh(value * (gelu_scale + bend))
    half = 0.5 + 0.5 * turn
    slope = half * (1.0 + (value * (1.0 - turn)) * (gelu_scale + 3.0 * bend))
    return value * half, slope


def dot_nt(left, right):
    return lax.dot_general(
        left, right, (((1,), (1,)), ((), ())), preferred_element_type=jnp.float32
    )


def dot_nn(left, right):
    return jnp.dot(left, right, preferred_element_type=jnp.float32)


def divisor(total, unit, most):
    return max(size for size in range(unit, most + 1, unit) if total % size == 0)


def mlp_body(
    tile,
    normed_ref,
    cot_ref,
    up_ref,
    down_ref,
    bias_ref,
    out_ref,
    back_ref,
    grad_up_ref,
    grad_down_ref,
    grad_bias_ref,
    normed_turned,
    cot_turned,
    act_ref,
    slope_ref,
):
    tokens = normed_ref.shape[0]

    @pl.when(pl.program_id(0) == 0)
    def _():
        normed_turned[...] = normed_ref[...].T
        cot_turned[...] = cot_ref[...].T
        out_ref[...] = jnp.zeros_like(out_ref)
        back_ref[...] = jnp.zeros_like(back_ref)

    grad_bias_ref[...] = jnp.zeros_like(grad_bias_ref)

    @pl.loop(0, tokens // tile)
    def _(step):
        rows = pl.ds(pl.multiple_of(step * tile, tile), tile)
        act, slope = gelu_both(dot_nn(normed_ref[rows, :], up_ref[...]) + bias_ref[...])
        act = act.astype(jnp.bfloat16)
        slope = (dot_nn(cot_ref[rows, :], down_ref[...]) * slope).astype(jnp.bfloat16)
        act_ref[rows, :] = act
        slope_ref[rows, :] = slope
        grad_bias_ref[...] += jnp.sum(slope.astype(jnp.float32), axis=0, keepdims=True)
        out_ref[rows, :] += dot_nt(act, down_ref[...])
        back_ref[rows, :] += dot_nt(slope, up_ref[...])

    grad_up_ref[...] = dot_nn(normed_turned[...], slope_ref[...]).astype(grad_up_ref.dtype)
    grad_down_ref[...] = dot_nn(cot_turned[...], act_ref[...]).astype(grad_down_ref.dtype)


def mlp_pass(normed, cot, weights, bias):
    tokens, channel = normed.shape
    hidden = weights.shape[2]
    width = divisor(hidden, 128, 512)
    tile = divisor(tokens, 16, 480)
    whole = pl.BlockSpec((tokens, channel), lambda j: (0, 0))
    block = pl.BlockSpec((channel, width), lambda j: (0, j))
    line = pl.BlockSpec((1, width), lambda j: (0, j))
    part = lambda which: pl.BlockSpec((None, channel, width), lambda j: (which, 0, j))
    total = jax.ShapeDtypeStruct((tokens, channel), jnp.float32)
    grads = jax.ShapeDtypeStruct((channel, hidden), jnp.bfloat16)
    return pl.pallas_call(
        functools.partial(mlp_body, tile),
        grid=(hidden // width,),
        in_specs=[whole, whole, part(0), part(1), line],
        out_specs=[whole, whole, block, block, line],
        out_shape=[total, total, grads, grads, jax.ShapeDtypeStruct((1, hidden), jnp.float32)],
        scratch_shapes=[
            pltpu.VMEM((channel, tokens), jnp.bfloat16),
            pltpu.VMEM((channel, tokens), jnp.bfloat16),
            pltpu.VMEM((tokens, width), jnp.bfloat16),
            pltpu.VMEM((tokens, width), jnp.bfloat16),
        ],
        compiler_params=pltpu.CompilerParams(vmem_limit_bytes=56 * 1024 * 1024),
        cost_estimate=pl.CostEstimate(
            flops=12 * tokens * channel * hidden,
            bytes_accessed=8 * channel * hidden + 12 * tokens * channel,
            transcendentals=tokens * hidden,
        ),
        name="mlp_pass",
    )(normed, cot, weights, weights, bias)


def spectral_front(arrived, lat_fwd, first_pair, second_pair, bias_one, bias_two):
    spectrum = jnp.einsum(
        "pkqr,nrqmd->nkpmd", lat_fwd, arrived, preferred_element_type=jnp.float32
    ).astype(jnp.bfloat16)
    snap_local, lat_total, pair_count, mode_local, channel = spectrum.shape
    blocked = spectrum.reshape(
        snap_local, lat_total, pair_count, mode_local, BLOCKS, channel // BLOCKS
    )
    pre_one = (
        jnp.einsum("nkqmbi,pqbio->nkpmbo", blocked, first_pair, preferred_element_type=jnp.float32)
        + bias_one
    )
    act_one = jax.nn.gelu(pre_one).astype(jnp.bfloat16)
    pre_two = (
        jnp.einsum("nkqmbi,pqbio->nkpmbo", act_one, second_pair, preferred_element_type=jnp.float32)
        + bias_two
    )
    return (blocked, pre_one, act_one, pre_two)


def adamw(master, first_mom, second_mom, gradient, step_rate):
    first_next = beta_one * first_mom + (1.0 - beta_one) * gradient
    second_next = beta_two * second_mom + (1.0 - beta_two) * gradient * gradient
    fix_one = 1.0 / (1.0 - beta_one**STEP)
    fix_two = 1.0 / (1.0 - beta_two**STEP)
    direction = first_next * fix_one / (jnp.sqrt(second_next * fix_two) + adam_eps)
    master_next = master - step_rate * (direction + decay_rate * master)
    return (master_next, first_next, second_next, master_next.astype(jnp.bfloat16))


def per_device_modes(
    fields,
    cotangent,
    valid_mask,
    kept_modes,
    mlp_master,
    mlp_first,
    mlp_second,
    filter_master,
    filter_first,
    filter_second,
    small_master,
    small_first,
    small_second,
    run_stats,
):
    group_size = lax.axis_size("sp")
    snap_local, row_local, lon_total, channel = fields.shape
    lat_total = row_local * group_size
    mode_local = kept_modes.shape[1]
    mode_total = mode_local * group_size
    block_width = channel // BLOCKS
    lon_fwd, lon_inv = lon_tables(lon_total, mode_total)
    lat_fwd = lat_table(lat_total)
    mlp_w, filt_w, small_w = (
        lax.all_gather(mlp_master.astype(jnp.bfloat16), "sp", axis=1, tiled=True),
        lax.all_gather(filter_master.astype(jnp.bfloat16), "sp", axis=1, tiled=True),
        lax.all_gather(small_master.astype(jnp.bfloat16), "sp", axis=1, tiled=True),
    )
    small_f = small_w.astype(jnp.float32)
    weights = filt_w.reshape(4, BLOCKS, block_width, block_width)
    first_pair = complex_pair(weights[0], weights[1])
    second_pair = complex_pair(weights[2], weights[3])
    bias_one = small_f[4:6].reshape(2, 1, BLOCKS, block_width)
    bias_two = small_f[6:8].reshape(2, 1, BLOCKS, block_width)
    fields_float = fields.astype(jnp.float32)
    normed, norm_pull = jax.vjp(layer_norm, fields_float, small_f[0], small_f[1])
    normed_low = normed.astype(jnp.bfloat16)
    spec_lon = jnp.einsum(
        "nrld,lqm->nrqmd", normed_low, lon_fwd, preferred_element_type=jnp.float32
    ).astype(jnp.bfloat16)
    arrived = lax.all_to_all(spec_lon, "sp", split_axis=3, concat_axis=1, tiled=True)
    spectral = spectral_front(arrived, lat_fwd, first_pair, second_pair, bias_one, bias_two)
    keep_mask = kept_modes.astype(jnp.float32)[None, :, None, :, None, None]
    masked = (shrink(spectral[3]) * keep_mask).astype(jnp.bfloat16)
    masked = masked.reshape(snap_local, lat_total, 2, mode_local, channel)
    returned = jnp.einsum(
        "pkqr,nkpmd->nrqmd", lat_fwd, masked, preferred_element_type=jnp.float32
    ).astype(jnp.bfloat16)
    home_modes = lax.all_to_all(returned, "sp", split_axis=1, concat_axis=3, tiled=True)
    filtered = jnp.einsum(
        "nrqmd,qml->nrld", home_modes, lon_inv, preferred_element_type=jnp.float32
    )
    mixture = fields_float + normed + filtered
    normed_two, norm_two_pull = jax.vjp(layer_norm, mixture, small_f[2], small_f[3])
    normed_two_low = normed_two.astype(jnp.bfloat16)
    tokens = snap_local * row_local * lon_total
    passed = mlp_pass(
        normed_two_low.reshape(tokens, channel),
        cotangent.reshape(tokens, channel),
        mlp_w,
        small_f[9:].reshape(1, -1),
    )
    output = mixture + passed[0].reshape(mixture.shape) + small_f[8]
    weight_mask = valid_mask.astype(jnp.float32)[..., None]
    variables = output[..., :NVAR]
    local_sums = jnp.stack(
        [
            jnp.sum(weight_mask * variables, axis=(0, 1, 2)),
            jnp.sum(weight_mask * variables * variables, axis=(0, 1, 2)),
        ]
    )
    total_sums = lax.psum(local_sums, ("snap", "sp"))
    positions = snap_local * lax.axis_size("snap") * lat_total * lon_total
    stats_new = stat_decay * run_stats + (1.0 - stat_decay) * total_sums / positions
    cot_float = cotangent.astype(jnp.float32)
    grad_normed_two = passed[1].reshape(mixture.shape)
    grad_bias_hidden = passed[4]
    grad_mix_norm, grad_gain_two, grad_shift_two = norm_two_pull(grad_normed_two)
    grad_mixture = cot_float + grad_mix_norm
    grad_bias_out = jnp.sum(cot_float, axis=(0, 1, 2))
    grad_filtered = grad_mixture.astype(jnp.bfloat16)
    grad_home = jnp.einsum(
        "nrld,qml->nrqmd", grad_filtered, lon_inv, preferred_element_type=jnp.float32
    ).astype(jnp.bfloat16)
    grad_returned = lax.all_to_all(grad_home, "sp", split_axis=3, concat_axis=1, tiled=True)
    grad_masked = jnp.einsum(
        "pkqr,nrqmd->nkpmd", lat_fwd, grad_returned, preferred_element_type=jnp.float32
    )
    arrived_again = lax.all_to_all(spec_lon, "sp", split_axis=3, concat_axis=1, tiled=True)
    used_front = spectral_front(arrived_again, lat_fwd, first_pair, second_pair, bias_one, bias_two)
    blocked, pre_one, act_one, pre_two = used_front
    grad_two = jax.vjp(shrink, pre_two)[1](grad_masked.reshape(pre_two.shape) * keep_mask)[
        0
    ].astype(jnp.bfloat16)
    grad_bias_two = jnp.sum(grad_two.astype(jnp.float32), axis=(0, 1, 3))
    grad_second = jnp.einsum(
        "nkqmbi,nkpmbo->pqbio", act_one, grad_two, preferred_element_type=jnp.float32
    )
    grad_act = jnp.einsum(
        "nkpmbo,pqbio->nkqmbi", grad_two, second_pair, preferred_element_type=jnp.float32
    )
    grad_one = jax.vjp(jax.nn.gelu, pre_one)[1](grad_act)[0].astype(jnp.bfloat16)
    grad_bias_one = jnp.sum(grad_one.astype(jnp.float32), axis=(0, 1, 3))
    grad_first = jnp.einsum(
        "nkqmbi,nkpmbo->pqbio", blocked, grad_one, preferred_element_type=jnp.float32
    )
    grad_spectrum = jnp.einsum(
        "nkpmbo,pqbio->nkqmbi", grad_one, first_pair, preferred_element_type=jnp.float32
    ).astype(jnp.bfloat16)
    grad_spectrum = grad_spectrum.reshape(snap_local, lat_total, 2, mode_local, channel)
    grad_lon = jnp.einsum(
        "pkqr,nkpmd->nrqmd", lat_fwd, grad_spectrum, preferred_element_type=jnp.float32
    ).astype(jnp.bfloat16)
    grad_rows = lax.all_to_all(grad_lon, "sp", split_axis=1, concat_axis=3, tiled=True)
    grad_normed = grad_mixture + jnp.einsum(
        "nrqmd,lqm->nrld", grad_rows, lon_fwd, preferred_element_type=jnp.float32
    )
    grad_field_norm, grad_gain_one, grad_shift_one = norm_pull(grad_normed)
    input_grad = grad_mixture + grad_field_norm
    grad_filter = jnp.stack(
        [
            grad_first[0, 0] + grad_first[1, 1],
            grad_first[1, 0] - grad_first[0, 1],
            grad_second[0, 0] + grad_second[1, 1],
            grad_second[1, 0] - grad_second[0, 1],
        ]
    ).reshape(4, channel, block_width)
    grad_small = jnp.concatenate(
        [
            jnp.stack([grad_gain_one, grad_shift_one, grad_gain_two, grad_shift_two]),
            grad_bias_one.reshape(2, channel),
            grad_bias_two.reshape(2, channel),
            grad_bias_out[None, :],
            grad_bias_hidden.reshape(-1, channel),
        ],
        axis=0,
    )
    shares = (
        jnp.stack([
            lax.psum_scatter(part, "sp", scatter_dimension=0, tiled=True) for part in passed[2:4]
        ]),
        lax.psum_scatter(grad_filter, "sp", scatter_dimension=1, tiled=True),
        lax.psum_scatter(grad_small, "sp", scatter_dimension=1, tiled=True),
    )
    owned = (
        lax.psum(shares[0].astype(jnp.bfloat16), "snap").astype(jnp.float32),
        lax.psum(shares[1].astype(jnp.bfloat16), "snap").astype(jnp.float32),
        lax.psum(shares[2].astype(jnp.bfloat16), "snap").astype(jnp.float32),
    )
    mlp_new, mlp_first_new, mlp_second_new, mlp_copy = adamw(
        mlp_master, mlp_first, mlp_second, owned[0], rate_mlp
    )
    filter_new, filter_first_new, filter_second_new, filter_copy = adamw(
        filter_master, filter_first, filter_second, owned[1], rate_filter
    )
    small_new, small_first_new, small_second_new, small_copy = adamw(
        small_master, small_first, small_second, owned[2], rate_small
    )
    return (
        output.astype(jnp.bfloat16),
        input_grad,
        mlp_new,
        mlp_first_new,
        mlp_second_new,
        mlp_copy,
        filter_new,
        filter_first_new,
        filter_second_new,
        filter_copy,
        small_new,
        small_first_new,
        small_second_new,
        small_copy,
        stats_new,
    )


FIRST, SECOND, THIRD, FOURTH, HALF, QUARTER, LEVEL, LAST = range(8)
SCHEDULE = {
    "a": [(FIRST, 0), (FIRST, 1)],
    "c0": [(SECOND, 0)],
    "d1": [(SECOND, 1), (FIRST, 2)],
    "f0": [(THIRD, 0)],
    "f1": [(SECOND, 2), (FIRST, 3)],
    "g": [(THIRD, 1)],
    "h0": [(FIRST, 4)],
    "h1": [(FOURTH, 0), (THIRD, 2)],
    ("k2", 0): [(SECOND, 3), (SECOND, 4)],
    ("m", 0): [(FOURTH, 1), (FIRST, 5)],
    ("m0", 0): [(FOURTH, 2)],
    ("m1", 0): [(HALF, 0)],
    ("k1", 1): [(THIRD, 3)],
    ("k2", 1): [(THIRD, 4)],
    ("k0", 2): [(HALF, 1)],
    ("m", 2): [(FOURTH, 3)],
    ("m1", 2): [(QUARTER, 0)],
    ("m2", 2): [(HALF, 2), (FOURTH, 4)],
    ("k0", 3): [(FOURTH, 5)],
    ("m", 3): [(LEVEL, 0), (QUARTER, 1)],
    ("k", 4): [(HALF, 3)],
    ("k2", 4): [(LEVEL, 1)],
    ("l", 4): [(QUARTER, 2)],
    ("k", 5): [(LAST, 0)],
    ("k0", 5): [(LEVEL, 2)],
    ("k1", 5): [(QUARTER, 3)],
    ("k2", 5): [(HALF, 4)],
    ("m", 5): [(LAST, 1), (LEVEL, 3)],
    "o1": [(QUARTER, 4)],
    "p1": [(HALF, 5)],
    "r": [(LAST, 2), (LEVEL, 4)],
    "t1": [(QUARTER, 5)],
    "u1": [(LAST, 3), (LAST, 4)],
    "x0": [(LEVEL, 5)],
    "z": [(LAST, 5)],
}


def lon_matrix(lon_total, mode_total, snaps, rows):
    places = np.arange(lon_total)
    orders = np.arange(mode_total)
    angles = (places[:, None] * orders[None, :] % lon_total) * (2.0 * math.pi / lon_total)
    doubling = np.where(orders == 0, 1.0, 2.0)
    scaling = 1.0 / math.sqrt(lon_total)
    forward = np.stack([np.cos(angles), -np.sin(angles)], axis=1) * scaling
    inverse = forward * doubling

    def spread(table):
        table = np.einsum(
            "ab,lx,rs->alrbsx", np.eye(snaps), table.reshape(lon_total, -1), np.eye(rows)
        )
        return table.reshape(snaps * lon_total * rows, -1).astype(ml_dtypes.bfloat16)

    return spread(forward), spread(inverse)


def lon_turn(lon_total, rows):
    turn = np.einsum("lk,rs->rlks", np.eye(lon_total), np.eye(rows))
    return turn.reshape(rows, lon_total, lon_total * rows).astype(ml_dtypes.bfloat16)


def lat_matrix(lat_total, mode_total):
    places = np.arange(lat_total)
    angles = (places[:, None] * places[None, :] % lat_total) * (2.0 * math.pi / lat_total)
    cosine, sine = np.cos(angles), np.sin(angles)
    table = np.stack([np.stack([cosine, sine], axis=1), np.stack([-sine, cosine], axis=1)])
    table = np.einsum("pkqr,ab->pakrqb", table / math.sqrt(lat_total), np.eye(mode_total))
    size = 2 * lat_total * mode_total
    return table.reshape(size, size).astype(ml_dtypes.bfloat16)


class Refs:
    pass


def block_body(names, sizes, *refs):
    g = Refs()
    for name, ref in zip(names, refs, strict=True):
        setattr(g, name, ref)
    snaps, group, parts, width = sizes
    levels = group // 2
    tokens = g.fields.shape[0] * g.fields.shape[1]
    channel = g.fields.shape[2]
    owned = channel // group
    half = width // 2
    quarter = width // snaps
    tile = tokens // 3
    short = divisor(tokens // 2, 16, 240)
    packed = g.modes.shape[2]
    strip = divisor(tokens // 2, 48, 144)
    sub = divisor(strip, 16, 48)
    low = jnp.bfloat16
    f32 = jnp.float32

    me_snap = lax.axis_index("snap")
    me_sp = lax.axis_index("sp")
    core = lax.rem(me_sp, 2)
    level = me_sp // 2

    def at(snap, sp):
        return {"snap": snap, "sp": sp}

    def sp_after(step):
        return lax.rem(me_sp + step, group)

    def sp_before(step):
        return lax.rem(me_sp + group - step, group)

    def snap_after(step):
        return lax.rem(me_snap + step, snaps)

    def snap_before(step):
        return lax.rem(me_snap + snaps - step, snaps)

    def level_after(step):
        return lax.rem(level + step, levels)

    def level_before(step):
        return lax.rem(level + levels - step, levels)

    other_core = at(me_snap, me_sp + 1 - 2 * core)

    def send(src, dst, sems, index, target):
        return pltpu.make_async_remote_copy(
            src_ref=src,
            dst_ref=dst,
            send_sem=sems[0].at[index],
            recv_sem=sems[1].at[index],
            device_id=target,
            device_id_type=pl.DeviceIdType.MESH,
        )

    half_tokens = tokens // 2

    def strips(body, first=0, count=tokens, before=None, after=None):
        @pl.loop(0, count // strip)
        def _(step):
            if before is not None:
                before(first // strip + step)
            for at_row in range(0, strip, sub):
                body(pl.ds(pl.multiple_of(first + step * strip + at_row, 16), sub))
            if after is not None:
                after(first // strip + step)

    def half_strips(body, part, **around):
        strips(body, part * half_tokens, half_tokens, **around)

    def strip_copy(near, far, sems, place, out):
        rows = pl.ds(pl.multiple_of(place * strip, strip), strip)
        ends = [near.at[rows], far.reshape(tokens, channel).at[rows]]
        if not out:
            ends.reverse()
        return pltpu.make_async_copy(*ends, sems.at[place])

    def fields_load(place):
        return strip_copy(g.fields_in, g.fields, g.fields_sem, place, False)

    def cot_load(place):
        return strip_copy(g.cot_in, g.cot, g.cot_sem, place, False)

    def out_copy(place):
        return strip_copy(g.fields_in, g.out, g.fields_sem, place, True)

    def grad_copy(place):
        return strip_copy(g.grid, g.in_grad, g.cot_sem, place, True)

    def half_rows(part):
        return slice(part * half_tokens, (part + 1) * half_tokens)

    def fold(value):
        return jnp.sum(value.reshape(-1, 8, value.shape[1]), axis=0)

    loads = {}

    def load(name, index):
        copy = pltpu.make_async_copy(getattr(g, name), getattr(g, name + "_in"), g.load_sem.at[index])
        copy.start()
        loads[name] = copy

    for index, name in enumerate(
        [name for name in names[: names.index("out")] if name not in ("mlp", "fields", "cot")]
    ):
        load(name, index)
    for copy in (fields_load, cot_load):
        for place in range(tokens // strip):
            copy(place).start()

    def master_load(part):
        return pltpu.make_async_copy(
            g.mlp.at[:, :, part * width : (part + 1) * width],
            g.mlp_part.at[part % 2],
            g.load_sem.at[len(loads) + part % 2],
        )

    master_load(0).start()
    master_load(1).start()

    barrier = pltpu.get_barrier_semaphore()
    peers = [at(me_snap, sp_after(step)) for step in range(1, group)]
    peers += [at(snap_after(step), me_sp) for step in range(1, snaps)]
    for peer in peers:
        pl.semaphore_signal(
            barrier, inc=1, device_id=peer, device_id_type=pl.DeviceIdType.MESH
        )

    loads["small"].wait()
    loads["kept"].wait()
    g.own_small[...] = jnp.zeros_like(g.own_small)
    rows_small = g.small.shape[0]
    g.own_small[0:rows_small, 0:owned] = g.small_in[...].astype(low).astype(f32)
    pairs_kept = g.kept.shape[1]
    lines = lax.broadcasted_iota(jnp.int32, (pairs_kept, pairs_kept), 0)
    places = lax.broadcasted_iota(jnp.int32, (pairs_kept, pairs_kept), 1)
    kept = jnp.where(lines == places, g.kept_in[...].astype(f32), 0.0)
    g.own_small[16:, :] = jnp.broadcast_to(
        jnp.sum(kept, axis=1, keepdims=True), (pairs_kept, g.own_small.shape[1])
    )
    pl.semaphore_wait(barrier, len(peers))

    def small_copy(step):
        return send(
            g.own_small, g.all_small.at[me_sp], (g.small_s, g.small_r), step, at(me_snap, sp_after(step))
        )

    for step in range(1, group):
        small_copy(step).start()
    g.all_small[me_sp] = g.own_small[...]

    snap_low = lax.rem(me_snap, 2)
    snap_high = me_snap // 2
    beside_low = me_snap + 1 - 2 * snap_low
    beside_high = me_snap + 2 - 4 * snap_high

    def own_quarter(part):
        odd = lax.rem(part, 2)
        return (1 - odd) * me_snap + odd * (2 * snap_low + snap_high)

    def own_place(part):
        return pl.ds(0, snaps) if part == parts - 1 else own_quarter(part)

    def half_quarters(part):
        return pl.ds(2 * (own_quarter(part) // 2), 2)

    def own_rows(sp):
        return pl.ds(pl.multiple_of(sp * owned, owned), owned)

    def first_copy(part, step):
        target = sp_after(step)
        matrix = lax.rem(target, 2)
        place = own_place(part)
        return send(
            g.own_w.at[part, matrix, place],
            g.all_w.at[part, matrix, place, own_rows(me_sp)],
            (g.first_s, g.first_r),
            (part, step),
            at(me_snap, target),
        )

    def first_local(part):
        place = own_place(part)
        return pltpu.make_async_copy(
            g.own_w.at[part, core, place],
            g.all_w.at[part, core, place, own_rows(me_sp)],
            g.first_s.at[part, 0],
        )

    def second_copy(part):
        odd = lax.rem(part, 2)
        view = g.all_w.at[part, core, own_quarter(part)]
        target = at((1 - odd) * beside_low + odd * beside_high, me_sp)
        return send(view, view, (g.second_s, g.second_r), part, target)

    def third_copy(part):
        odd = lax.rem(part, 2)
        view = g.all_w.at[part, core, half_quarters(part)]
        target = at((1 - odd) * beside_high + odd * beside_low, me_sp)
        return send(view, view, (g.third_s, g.third_r), part, target)

    def fourth_copy(part):
        view = g.all_w.at[part, core]
        return send(view, view, (g.fourth_s, g.fourth_r), part, other_core)

    def start_first(part):
        for step in range(1, group):
            first_copy(part, step).start()
        first_local(part).start()

    def wait_first(part):
        for step in range(1, group):
            first_copy(part, step).wait_recv()
        first_local(part).wait()

    def pass_second(part):
        wait_first(part)
        second_copy(part).start()

    def pass_third(part):
        second_copy(part).wait_recv()
        third_copy(part).start()

    def pass_fourth(part):
        if part == parts - 1:
            wait_first(part)
        else:
            third_copy(part).wait_recv()
        fourth_copy(part).start()

    stages = {FIRST: start_first, SECOND: pass_second, THIRD: pass_third, FOURTH: pass_fourth}

    def reach(point):
        for stage, part in SCHEDULE.get(point, ()):
            stages[stage](part)

    for part in range(parts):
        master_load(part).wait()
        for place in range(snaps):
            cols = slice(place * quarter, (place + 1) * quarter)
            g.own_w[part, :, place] = g.mlp_part[part % 2, :, :, cols].astype(low)
        if part + 2 < parts:
            master_load(part + 2).start()
        if (FIRST, part) in SCHEDULE["a"]:
            start_first(part)

    def first_unit(rows):
        values = g.fields_in[rows, :].astype(f32)
        centred = values - jnp.mean(values, axis=-1, keepdims=True)
        scale = lax.rsqrt(jnp.mean(centred * centred, axis=-1, keepdims=True) + eps_norm)
        g.scale_one[rows, :] = scale
        g.grid[rows, :] = centred * scale

    strips(first_unit, before=lambda place: fields_load(place).wait())
    reach("b")
    for step in range(1, group):
        small_copy(step).wait_recv()
    for sp in range(group):
        g.gains[:, sp * owned : (sp + 1) * owned] = g.all_small[sp, 0:16, 0:owned]
        g.keep[sp * pairs_kept : (sp + 1) * pairs_kept, :] = g.all_small[sp, 16:, :]

    def first_norm(rows):
        unit = g.grid[rows, :]
        normed = unit * g.gains[0:1, :] + g.gains[1:2, :]
        g.unit_one[rows, :] = unit.astype(low)
        g.normed[rows, :] = normed.astype(low)
        g.grid[rows, :] = g.fields_in[rows, :].astype(f32) + normed

    half_snaps = g.arrived.shape[0] // 2

    third_rows = packed // 3
    spare = 128 - owned

    def pack(value):
        return jnp.concatenate(
            [
                jnp.concatenate(
                    [
                        value[at_row * third_rows : (at_row + 1) * third_rows],
                        value[packed:, at_row * spare : (at_row + 1) * spare],
                    ],
                    axis=1,
                )
                for at_row in range(3)
            ],
            axis=0,
        ).astype(low)

    def unpack(value):
        value = value.astype(f32)
        rest = [
            value[at_row * third_rows : (at_row + 1) * third_rows, owned:] for at_row in range(3)
        ]
        return jnp.concatenate([value[:, 0:owned], jnp.concatenate(rest, axis=1)], axis=0)

    def block_copy(which, part, step):
        target = sp_after(step)
        return send(
            g.modes.at[part, target],
            g.modes_got.at[part, me_sp],
            (g.block_s, g.block_r),
            (which, part, step),
            at(me_snap, target),
        )

    def row_copy(which, part, step):
        target = sp_after(step)
        return send(
            g.rows_out.at[part, target],
            g.rows_got.at[part, me_sp],
            (g.row_s, g.row_r),
            (which, part, step),
            at(me_snap, target),
        )

    def to_blocks(table, which, part):
        modes = dot_nn(table, g.normed[half_rows(part), :])
        for block in range(group):
            g.modes[part, block] = pack(modes[:, block * owned : (block + 1) * owned])
        for step in range(1, group):
            block_copy(which, part, step).start()
        g.modes_got[part, me_sp] = g.modes[part, me_sp]

    def take_blocks(which, part):
        for step in range(1, group):
            block_copy(which, part, step).wait_recv()
        each = g.arrived.shape[1] // group
        for sp in range(group):
            value = unpack(g.modes_got[part, sp])
            value = jnp.concatenate([value, jnp.zeros((value.shape[0], spare), f32)], axis=1)
            for index in range(half_snaps):
                g.arrived[part * half_snaps + index, sp * each : (sp + 1) * each, :] = value[
                    index * each : (index + 1) * each
                ].astype(low)

    def to_rows(which, part, tables):
        each = tables[0].shape[0] // group
        for sp in range(group):
            value = [table[sp * each : (sp + 1) * each, 0:owned] for table in tables]
            g.rows_out[part, sp] = pack(jnp.concatenate(value, axis=0))
        for step in range(1, group):
            row_copy(which, part, step).start()
        g.rows_got[part, me_sp] = g.rows_out[part, me_sp]

    def home_modes(which, part):
        for step in range(1, group):
            row_copy(which, part, step).wait_recv()
        for block in range(group):
            g.gathered[part, :, block * owned : (block + 1) * owned] = unpack(
                g.rows_got[part, block]
            )
        g.home_low[part] = g.gathered[part].astype(low)

    loads["lon_f"].wait()
    for part in range(2):
        half_strips(first_norm, part)
        reach("c" + str(part))
        to_blocks(g.lon_f_in[...], 0, part)
        reach("d" + str(part))

    loads["filt"].wait()
    for weight, first in ((g.weight_one, 0), (g.weight_two, 2)):
        weight[...] = jnp.zeros_like(weight)
        real = g.filt_in[first].astype(low)
        imag = g.filt_in[first + 1].astype(low)
        weight[0:owned, 0:owned] = real
        weight[128 : 128 + owned, 128 : 128 + owned] = real
        weight[0:owned, 128 : 128 + owned] = imag
        weight[128 : 128 + owned, 0:owned] = -imag

    def bias_row(first):
        return jnp.concatenate(
            [g.own_small[first : first + 1, :], g.own_small[first + 1 : first + 2, :]], axis=1
        )

    for place in range(tokens // strip):
        cot_load(place).wait()
    reach("e")
    loads["lat_f"].wait()
    loads["lat_b"].wait()
    pairs = g.arrived.shape[1] // 2
    half_modes = half_snaps * pairs

    def mode_half(part):
        return slice(part * half_modes, (part + 1) * half_modes)

    def spectra(out, kind, part):
        for snap in range(part * half_snaps, (part + 1) * half_snaps):
            spectrum = dot_nn(g.lat_f_in[...], g.arrived[snap]).astype(kind)
            rows = slice(snap * pairs, (snap + 1) * pairs)
            out[rows, 0:128] = spectrum[0:pairs]
            out[rows, 128:256] = spectrum[pairs:]

    def grids(values):
        tables = []
        for index in range(half_snaps):
            rows = values[index * pairs : (index + 1) * pairs]
            rows = jnp.concatenate([rows[:, 0:128], rows[:, 128:256]], axis=0)
            tables.append(dot_nn(g.lat_b_in[...], rows))
        return tables

    def keep_half():
        keep = jnp.concatenate([g.keep[...], g.keep[...]], axis=1)
        return jnp.concatenate([keep] * half_snaps, axis=0)

    for part in range(2):
        take_blocks(0, part)
        rows = mode_half(part)
        spectra(g.spectrum, low, part)
        g.pre_one[rows, :] = dot_nn(g.spectrum[rows, :], g.weight_one[...]) + bias_row(4)
        g.act_one[rows, :] = gelu_both(g.pre_one[rows, :])[0].astype(low)
        g.pre_two[rows, :] = dot_nn(g.act_one[rows, :], g.weight_two[...]) + bias_row(6)
        to_rows(0, part, grids((shrink(g.pre_two[rows, :]) * keep_half()).astype(low)))
        reach("f" + str(part))
    g.cot_turned[...] = g.cot_in[...].T
    reach("g")

    loads["lon_i"].wait()

    def second_norm(rows):
        values = g.grid[rows, :]
        centred = values - jnp.mean(values, axis=-1, keepdims=True)
        scale = lax.rsqrt(jnp.mean(centred * centred, axis=-1, keepdims=True) + eps_norm)
        centred = centred * scale
        g.unit_two[rows, :] = centred.astype(low)
        g.scale_two[rows, :] = scale
        g.normed[rows, :] = (centred * g.gains[2:3, :] + g.gains[3:4, :]).astype(low)
        g.grid[rows, :] = values + g.gains[8:9, :]
        g.back[rows, :] = jnp.zeros((sub, channel), f32)

    for part in range(2):
        home_modes(0, part)
        g.grid[half_rows(part), :] += dot_nn(g.lon_i_in[...], g.home_low[part])
        reach("h" + str(part))
        half_strips(second_norm, part)
        reach("i" + str(part))
    g.normed_turned[...] = g.normed[...].T
    reach("j")
    flat = jnp.concatenate([g.gains[9 + row : 10 + row, :] for row in range(rows_small - 9)], axis=1)
    for part in range(parts):
        g.bias[part] = flat[:, part * width : (part + 1) * width]

    def core_copy(part, matrix):
        slot = lax.rem(part, 2)
        return send(
            g.grads.at[matrix, :, 1 - core],
            g.core_got.at[slot, matrix],
            (g.core_s, g.core_r),
            (slot, matrix),
            other_core,
        )

    places_one = (snap_low, snap_high)
    places_two = (snap_high, snap_low)
    beside_one = (beside_low, beside_high)
    beside_two = (beside_high, beside_low)

    def half_copy(part, matrix):
        slot = lax.rem(part, 2)
        place = lax.rem(part, 4)
        return send(
            g.half_out.at[slot, matrix, 1 - places_one[matrix]],
            g.half_got.at[place, matrix],
            (g.half_s, g.half_r),
            (place, matrix),
            at(beside_one[matrix], me_sp),
        )

    def quarter_copy(part, matrix):
        slot = lax.rem(part, 2)
        return send(
            g.quarter_out.at[slot, matrix, 1 - places_two[matrix]],
            g.quarter_got.at[slot, matrix],
            (g.quarter_s, g.quarter_r),
            (slot, matrix),
            at(beside_two[matrix], me_sp),
        )

    def level_copy(part, step):
        slot = lax.rem(part, 2)
        place = lax.rem(part, 4)
        target = level_after(step)
        return send(
            g.level_out.at[slot, target],
            g.level_got.at[place, level],
            (g.level_s, g.level_r),
            (place, step),
            at(me_snap, 2 * target + core),
        )

    def last_copy(part, step):
        view = g.total.at[part, me_snap]
        return send(view, view, (g.last_s, g.last_r), (part, step), at(snap_after(step), me_sp))

    def half_stage(part):
        slot = lax.rem(part, 2)
        for matrix in range(2):

            if part >= 2:
                half_copy(part - 2, matrix).wait_send()

            core_copy(part, matrix).wait_recv()

            @pl.loop(0, levels)
            def _(row, matrix=matrix):
                both = g.grads[matrix, row, core].astype(f32) + g.core_got[
                    slot, matrix, row
                ].astype(f32)
                both = both.astype(low)
                g.half_out[slot, matrix, 0, row] = both[:, 0:half]
                g.half_out[slot, matrix, 1, row] = both[:, half:width]

            half_copy(part, matrix).start()

    def quarter_stage(part):
        slot = lax.rem(part, 2)
        for matrix in range(2):

            if part >= 2:
                quarter_copy(part - 2, matrix).wait_send()

            half_copy(part, matrix).wait_recv()
            for row in range(levels):
                both = g.half_out[slot, matrix, places_one[matrix], row].astype(f32) + g.half_got[
                    lax.rem(part, 4), matrix, row
                ].astype(f32)
                both = both.astype(low)
                g.quarter_out[slot, matrix, 0, row] = both[:, 0:quarter]
                g.quarter_out[slot, matrix, 1, row] = both[:, quarter:half]
            quarter_copy(part, matrix).start()

    def level_stage(part):
        slot = lax.rem(part, 2)

        if part >= 2:
            for step in range(1, levels):
                level_copy(part - 2, step).wait_send()

        for matrix in range(2):
            quarter_copy(part, matrix).wait_recv()
            for row in range(levels):
                both = g.quarter_out[slot, matrix, places_two[matrix], row].astype(
                    f32
                ) + g.quarter_got[slot, matrix, row].astype(f32)
                g.level_out[slot, row, matrix] = both.astype(low)
        for step in range(1, levels):
            level_copy(part, step).start()

    def last_stage(part):
        slot = lax.rem(part, 2)
        for step in range(1, levels):
            level_copy(part, step).wait_recv()
        for matrix in range(2):
            sums = g.level_out[slot, level, matrix].astype(f32)
            for step in range(1, levels):
                sums += g.level_got[lax.rem(part, 4), level_before(step), matrix].astype(f32)
            g.total[part, me_snap, matrix] = sums.astype(low)
        for step in range(1, snaps):
            last_copy(part, step).start()

    stages |= {HALF: half_stage, QUARTER: quarter_stage, LEVEL: level_stage, LAST: last_stage}

    def weight(part, matrix):
        return jnp.concatenate([g.all_w[part, matrix, place] for place in range(snaps)], axis=1)

    def add_products(part, rows):
        g.grid[rows, :] += dot_nt(g.act[rows, :], weight(part, 1))
        g.back[rows, :] += dot_nt(g.slope[rows, :], weight(part, 0))

    @pl.loop(0, parts)
    def _(part):
        def reach_in(point, also=True):
            for at_part in range(parts):
                if (point, at_part) in SCHEDULE:
                    pl.when((part == at_part) & also)(functools.partial(reach, (point, at_part)))

        def tile_rows(step):
            return pl.ds(pl.multiple_of(step * tile, tile), tile)

        fourth_copy(part).wait_recv()
        reach_in("k")
        g.grad_bias[part] = jnp.zeros(g.grad_bias.shape[1:], f32)

        @pl.loop(0, tokens // tile)
        def _(step):
            rows = tile_rows(step)
            act, slope = gelu_both(dot_nn(g.normed[rows, :], weight(part, 0)) + g.bias[part])
            g.act[rows, :] = act.astype(low)
            slope = (dot_nn(g.cot_in[rows, :], weight(part, 1)) * slope).astype(low)
            g.slope[rows, :] = slope
            g.grad_bias[part] += fold(slope.astype(f32))
            for at_step in range(tokens // tile):
                reach_in("k" + str(at_step), step == at_step)

        reach_in("l")

        @pl.when(part >= 1)
        def _():
            for matrix in range(2):
                core_copy(part - 1, matrix).wait_send()

        shape = g.grads.shape[1:]
        g.grads[0] = dot_nn(g.normed_turned[...], g.slope[...]).astype(low).reshape(shape)
        core_copy(part, 0).start()
        g.grads[1] = dot_nn(g.cot_turned[...], g.act[...]).astype(low).reshape(shape)
        core_copy(part, 1).start()
        reach_in("m")

        @pl.when(part < parts - 1)
        def _():
            @pl.loop(0, tokens // tile)
            def _(step):
                add_products(part, tile_rows(step))
                for at_step in range(tokens // tile):
                    reach_in("m" + str(at_step), step == at_step)

    g.folds[...] = jnp.zeros_like(g.folds)

    def second_back(rows):
        grad = g.back[rows, :]
        unit = g.unit_two[rows, :].astype(f32)
        cot = g.cot_in[rows, :].astype(f32)
        pulled = grad * g.gains[2:3, :]
        middle = jnp.mean(pulled, axis=-1, keepdims=True)
        slant = jnp.mean(pulled * unit, axis=-1, keepdims=True)
        total = cot + g.scale_two[rows, :] * (pulled - middle - unit * slant)
        g.back[rows, :] = total
        g.normed[rows, :] = total.astype(low)
        g.folds[2] += fold(grad * unit)
        g.folds[3] += fold(grad)
        g.folds[4] += fold(cot)

    loads["lon_it"].wait()
    for part in range(2):

        @pl.loop(0, half_tokens // short)
        def _(step, part=part):
            first_row = part * half_tokens + step * short
            add_products(parts - 1, pl.ds(pl.multiple_of(first_row, 16), short))

        reach("o" + str(part))
        half_strips(second_back, part)
        for step in range(1, group):
            block_copy(0, part, step).wait_send()
        to_blocks(g.lon_it_in[...], 1, part)
        reach("p" + str(part))
    reach("q")

    def low_out(rows):
        g.fields_in[rows, :] = g.grid[rows, :].astype(low)

    strips(low_out, after=lambda place: out_copy(place).start())
    reach("r")
    loads["valid"].wait()
    loads["turn"].wait()
    weigh = sum(
        dot_nn(g.valid_in[:, row, :].astype(f32).astype(low), g.turn_in[row])
        for row in range(g.valid.shape[1])
    )
    places_each = weigh.shape[1]
    precise = lax.Precision.HIGHEST
    sums = [jnp.zeros((1, 128), f32), jnp.zeros((1, 128), f32)]
    for snap in range(g.valid.shape[0]):
        variables = g.grid[snap * places_each : (snap + 1) * places_each, 0:128]
        for index, value in enumerate((variables, variables * variables)):
            sums[index] += jnp.dot(
                weigh[snap : snap + 1, :], value, precision=precise, preferred_element_type=f32
            )

    reach("s")

    def dot_tn(left, right):
        return lax.dot_general(
            left, right, (((0,), (0,)), ((), ())), preferred_element_type=f32
        )

    def filter_rows(first, grad):
        g.pair_grad[...] = grad
        real = g.pair_grad[0:128, 0:128] + g.pair_grad[128:256, 128:256]
        imag = g.pair_grad[0:128, 128:256] - g.pair_grad[128:256, 0:128]
        g.filt_out[me_snap, first] = real[0:owned].astype(low)
        g.filt_out[me_snap, first + 1] = imag[0:owned].astype(low)

    for part in range(2):
        take_blocks(1, part)
        reach("t" + str(part))
        rows = mode_half(part)
        spectra(g.grad_pre, f32, part)
        bend = jnp.tanh(g.pre_two[rows, :] / shrink_level)
        grad = (g.grad_pre[rows, :] * keep_half() * (bend * bend)).astype(low)
        g.grad_two[rows, :] = grad
        grad = dot_nt(grad, g.weight_two[...]) * gelu_both(g.pre_one[rows, :])[1]
        grad = grad.astype(low)
        g.grad_one[rows, :] = grad
        for step in range(1, group):
            row_copy(0, part, step).wait_send()
        to_rows(1, part, grids(dot_nt(grad, g.weight_one[...]).astype(low)))
        reach("u" + str(part))
    reach("v")
    bias_one = jnp.sum(g.grad_one[...].astype(f32), axis=0, keepdims=True)
    bias_two = jnp.sum(g.grad_two[...].astype(f32), axis=0, keepdims=True)
    filter_rows(2, dot_tn(g.act_one[...], g.grad_two[...]))
    filter_rows(0, dot_tn(g.spectrum[...], g.grad_one[...]))

    def filter_copy(step):
        view = g.filt_out.at[me_snap]
        return send(view, view, (g.filt_s, g.filt_r), step, at(snap_after(step), me_sp))

    for step in range(1, snaps):
        filter_copy(step).start()


    reach("w")

    loads["lon_ft"].wait()

    def first_back(rows):
        grad = g.grid[rows, :]
        unit = g.unit_one[rows, :].astype(f32)
        pulled = grad * g.gains[0:1, :]
        middle = jnp.mean(pulled, axis=-1, keepdims=True)
        slant = jnp.mean(pulled * unit, axis=-1, keepdims=True)
        g.grid[rows, :] = g.back[rows, :] + g.scale_one[rows, :] * (
            pulled - middle - unit * slant
        )
        g.folds[0] += fold(grad * unit)
        g.folds[1] += fold(grad)

    for part in range(2):
        home_modes(1, part)
        reach("x" + str(part))
        g.grid[half_rows(part), :] = g.back[half_rows(part), :] + dot_nn(
            g.lon_ft_in[...], g.home_low[part]
        )
        half_strips(first_back, part, after=lambda place: grad_copy(place).start())
        reach("y" + str(part))

    g.grad_rows[...] = jnp.zeros_like(g.grad_rows)
    for index, row in enumerate((0, 1, 2, 3, 8)):
        g.grad_rows[row : row + 1, :] = jnp.sum(g.folds[index], axis=0, keepdims=True)
    flat = jnp.concatenate(
        [jnp.sum(g.grad_bias[part], axis=0, keepdims=True) for part in range(parts)], axis=1
    )
    for row in range(rows_small - 9):
        g.grad_rows[9 + row : 10 + row, :] = flat[:, row * channel : (row + 1) * channel]
    for block in range(group):
        g.tiles[block] = jnp.zeros(g.tiles.shape[1:], f32)
        g.tiles[block, :, 0:owned] = g.grad_rows[:, block * owned : (block + 1) * owned]
        g.tiles[block, 13:14, :] = sums[0]
        g.tiles[block, 14:15, :] = sums[1]

    def tile_copy(step):
        target = sp_after(step)
        return send(
            g.tiles.at[target], g.tiles_got.at[me_sp], (g.tile_s, g.tile_r), step, at(me_snap, target)
        )

    def snap_tile_copy(step):
        view = g.snap_tiles.at[me_snap]
        return send(view, view, (g.snap_tile_s, g.snap_tile_r), step, at(snap_after(step), me_sp))

    for step in range(1, group):
        tile_copy(step).start()
    reach("z")

    g.tiles_got[me_sp] = g.tiles[me_sp]
    for step in range(1, group):
        tile_copy(step).wait_recv()
    tile_sum = g.tiles_got[0]
    for sp in range(1, group):
        tile_sum += g.tiles_got[sp]
    g.snap_tiles[me_snap] = tile_sum
    g.snap_tiles[me_snap, 4:5, :] = bias_one[:, 0:128]
    g.snap_tiles[me_snap, 5:6, :] = bias_one[:, 128:256]
    g.snap_tiles[me_snap, 6:7, :] = bias_two[:, 0:128]
    g.snap_tiles[me_snap, 7:8, :] = bias_two[:, 128:256]
    for step in range(1, snaps):
        snap_tile_copy(step).start()

    for step in range(1, snaps):
        filter_copy(step).wait_recv()
    filter_sum = g.filt_out[0].astype(f32)
    for snap in range(1, snaps):
        filter_sum += g.filt_out[snap].astype(f32)
    g.grad_filt[...] = filter_sum
    for part in range(parts):
        for step in range(1, snaps):
            last_copy(part, step).wait_recv()
    grads_out = pltpu.make_async_copy(g.total, g.grad_mlp, g.load_sem.at[3])
    grads_out.start()
    for step in range(1, snaps):
        snap_tile_copy(step).wait_recv()
    tile_sum = g.snap_tiles[0]
    for snap in range(1, snaps):
        tile_sum += g.snap_tiles[snap]
    g.grad_small[...] = tile_sum

    grads_out.wait()
    for place in range(tokens // strip):
        out_copy(place).wait()
        grad_copy(place).wait()
    for step in range(1, group):
        small_copy(step).wait_send()
        for part in range(2):
            block_copy(1, part, step).wait_send()
            row_copy(1, part, step).wait_send()
        tile_copy(step).wait_send()
        for part in range(parts):
            first_copy(part, step).wait_send()
    for part in range(parts):
        if part < parts - 1:
            second_copy(part).wait_send()
            third_copy(part).wait_send()
        fourth_copy(part).wait_send()
    for matrix in range(2):
        core_copy(parts - 1, matrix).wait_send()
    for part in (parts - 2, parts - 1):
        for matrix in range(2):
            half_copy(part, matrix).wait_send()
            quarter_copy(part, matrix).wait_send()
        for step in range(1, levels):
            level_copy(part, step).wait_send()
    for step in range(1, snaps):
        filter_copy(step).wait_send()
        snap_tile_copy(step).wait_send()
        for part in range(parts):
            last_copy(part, step).wait_send()


def block_pass(fields, cot, valid, kept, mlp, filt, small, snaps, group):
    snap_local, row_local, lon_total, channel = fields.shape
    tokens = snap_local * row_local * lon_total
    hidden = mlp.shape[2]
    lat_total = row_local * group
    modes = kept.shape[1] * group
    owned = channel // group
    width = 512
    parts = hidden // width
    levels = group // 2
    quarter = width // snaps
    low, f32 = jnp.bfloat16, jnp.float32
    half = width // 2
    half_snaps = snap_local // 2
    lon_f, lon_i = lon_matrix(lon_total, modes, half_snaps, row_local)

    def paired(array):
        return jnp.transpose(array, (0, 2, 1, 3)).reshape(-1, row_local, channel)

    lat_f = lat_matrix(lat_total, modes)
    pair = 2 * modes * row_local
    spread = half_snaps * row_local * 2 * modes
    inputs = dict(
        small=small,
        kept=kept.T,
        fields=paired(fields),
        lon_f=jnp.asarray(np.ascontiguousarray(lon_f.T)),
        filt=filt,
        lat_f=jnp.asarray(lat_f),
        lat_b=jnp.asarray(np.ascontiguousarray(lat_f.T)),
        cot=paired(cot),
        lon_i=jnp.asarray(lon_i),
        valid=valid,
        turn=jnp.asarray(lon_turn(lon_total, row_local)),
        lon_it=jnp.asarray(np.ascontiguousarray(lon_i.T)),
        lon_ft=jnp.asarray(lon_f),
        mlp=mlp,
    )
    outputs = dict(
        out=jax.ShapeDtypeStruct((tokens // row_local, row_local, channel), low),
        in_grad=jax.ShapeDtypeStruct((tokens // row_local, row_local, channel), f32),
        grad_mlp=jax.ShapeDtypeStruct((parts, snaps, 2, owned, quarter), low),
        grad_filt=jax.ShapeDtypeStruct((4, owned, 128), f32),
        grad_small=jax.ShapeDtypeStruct((16, 128), f32),
    )
    vmem = pltpu.VMEM
    dma = pltpu.SemaphoreType.DMA
    scratch = {
        name + "_in": vmem(value.shape, value.dtype)
        for name, value in inputs.items()
        if name not in ("mlp", "fields", "cot")
    }
    strip = divisor(tokens // 2, 48, 144)
    scratch |= dict(
        mlp_part=vmem((2, 2, owned, width), f32),
        fields_in=vmem((tokens, channel), low),
        fields_sem=dma((tokens // strip,)),
        cot_sem=dma((tokens // strip,)),
        cot_in=vmem((tokens, channel), low),
        grid=vmem((tokens, channel), f32),
        back=vmem((tokens, channel), f32),
        normed=vmem((tokens, channel), low),
        normed_turned=vmem((channel, tokens), low),
        cot_turned=vmem((channel, tokens), low),
        unit_one=vmem((tokens, channel), low),
        unit_two=vmem((tokens, channel), low),
        scale_one=vmem((tokens, 1), f32),
        scale_two=vmem((tokens, 1), f32),
        own_small=vmem((16 + kept.shape[0], 128), f32),
        all_small=vmem((group, 16 + kept.shape[0], 128), f32),
        gains=vmem((16, channel), f32),
        keep=vmem((lat_total * modes, 128), f32),
        own_w=vmem((parts, 2, snaps, owned, quarter), low),
        all_w=vmem((parts, 2, snaps, channel, quarter), low),
        modes=vmem((2, group, half_snaps * pair * 3 // 4, 128), low),
        modes_got=vmem((2, group, half_snaps * pair * 3 // 4, 128), low),
        rows_out=vmem((2, group, half_snaps * pair * 3 // 4, 128), low),
        rows_got=vmem((2, group, half_snaps * pair * 3 // 4, 128), low),
        arrived=vmem((snap_local, pair * group, 128), low),
        gathered=vmem((2, spread, channel), f32),
        home_low=vmem((2, spread, channel), low),
        weight_one=vmem((256, 256), low),
        weight_two=vmem((256, 256), low),
        spectrum=vmem((snap_local * lat_total * modes, 256), low),
        pre_one=vmem((snap_local * lat_total * modes, 256), f32),
        act_one=vmem((snap_local * lat_total * modes, 256), low),
        pre_two=vmem((snap_local * lat_total * modes, 256), f32),
        grad_pre=vmem((snap_local * lat_total * modes, 256), f32),
        grad_two=vmem((snap_local * lat_total * modes, 256), low),
        grad_one=vmem((snap_local * lat_total * modes, 256), low),
        folds=vmem((5, 8, channel), f32),
        pair_grad=vmem((256, 256), f32),
        act=vmem((tokens, width), low),
        slope=vmem((tokens, width), low),
        bias=vmem((parts, 1, width), f32),
        grad_bias=vmem((parts, 8, width), f32),
        grad_rows=vmem((16, channel), f32),
        grads=vmem((2, levels, 2, owned, width), low),
        core_got=vmem((2, 2, levels, owned, width), low),
        half_out=vmem((2, 2, 2, levels, owned, half), low),
        half_got=vmem((4, 2, levels, owned, half), low),
        quarter_out=vmem((2, 2, 2, levels, owned, quarter), low),
        quarter_got=vmem((2, 2, levels, owned, quarter), low),
        level_out=vmem((2, levels, 2, owned, quarter), low),
        level_got=vmem((4, levels, 2, owned, quarter), low),
        total=vmem((parts, snaps, 2, owned, quarter), low),
        filt_out=vmem((snaps, 4, owned, 128), low),
        tiles=vmem((group, 16, 128), f32),
        tiles_got=vmem((group, 16, 128), f32),
        snap_tiles=vmem((snaps, 16, 128), f32),
        load_sem=dma((len(inputs) + 1,)),
    )
    for name, shape in dict(
        small=(group,),
        first=(parts, group),
        second=(parts,),
        third=(parts,),
        fourth=(parts,),
        block=(2, 2, group),
        row=(2, 2, group),
        core=(2, 2),
        half=(4, 2),
        quarter=(2, 2),
        level=(4, levels),
        last=(parts, snaps),
        filt=(snaps,),
        tile=(group,),
        snap_tile=(snaps,),
    ).items():
        scratch[name + "_s"] = dma(shape)
        scratch[name + "_r"] = dma(shape)
    names = [*inputs, *outputs, *scratch]
    far = pl.BlockSpec(memory_space=pl.ANY)
    near = pl.BlockSpec(memory_space=pltpu.VMEM)
    results = pl.pallas_call(
        functools.partial(block_body, names, (snaps, group, parts, width)),
        in_specs=[far] * len(inputs),
        out_specs=[far, far, far, near, near],
        out_shape=list(outputs.values()),
        scratch_shapes=list(scratch.values()),
        compiler_params=pltpu.CompilerParams(
            collective_id=0, has_side_effects=True, vmem_limit_bytes=VMEM_LIMIT
        ),
        cost_estimate=pl.CostEstimate(
            flops=12 * tokens * channel * hidden,
            bytes_accessed=4 * hidden * channel,
            transcendentals=tokens * hidden,
        ),
        name="block_pass",
    )(*inputs.values())
    return results


def step_body(names, positions, *refs):
    g = Refs()
    for name, ref in zip(names, refs, strict=True):
        setattr(g, name, ref)
    parts, snaps = g.grad_mlp.shape[:2]
    quarter = g.grad_mlp.shape[4]
    width = snaps * quarter
    moments = ("w", "m", "v")
    results = ("new", "first", "second", "copy")

    pieces = g.far_sem.shape[2]
    ends = ((g.out, g.out_near, g.out_o), (g.in_grad, g.in_grad_near, g.in_grad_o))

    def passing(kind, piece, leg):
        size = ends[kind][0].shape[0] // pieces
        rows = pl.ds(piece * size, size)
        return pltpu.make_async_copy(
            ends[kind][leg].at[rows], ends[kind][leg + 1].at[rows], g.far_sem.at[leg, kind, piece]
        )

    through = [(kind, piece) for kind in range(2) for piece in range(pieces)]

    def part_cols(part):
        return pl.ds(part * width, width)

    def load(part):
        near = [
            pltpu.make_async_copy(
                getattr(g, "mlp_" + kind).at[:, :, part_cols(part)],
                g.near.at[index, part],
                g.near_sem.at[index, part],
            )
            for index, kind in enumerate(moments)
        ]
        near.append(
            pltpu.make_async_copy(g.grad_mlp.at[part], g.grad_near.at[part], g.near_sem.at[3, part])
        )
        return near

    def store(part):
        copies = [
            pltpu.make_async_copy(
                g.near.at[index, part],
                getattr(g, "mlp_" + kind).at[:, :, part_cols(part)],
                g.back_sem.at[index, part],
            )
            for index, kind in enumerate(results[:3])
        ]
        copies.append(
            pltpu.make_async_copy(
                g.low_near.at[part], g.mlp_copy.at[:, :, part_cols(part)], g.back_sem.at[3, part]
            )
        )
        return copies

    coming = [load(part) for part in range(parts)]
    going = [store(part) for part in range(parts)]
    shares = [through[part::parts] for part in range(parts)]
    for part in range(parts):
        for copy in coming[part]:
            copy.start()
        for each in shares[part]:
            passing(*each, 0).start()

    def put(prefix, values):
        for kind, value in zip(results, values, strict=True):
            getattr(g, prefix + kind)[...] = value

    owned = g.filt_w.shape[2]
    put(
        "filt_",
        adamw(g.filt_w[...], g.filt_m[...], g.filt_v[...], g.grad_filt[:, :, 0:owned], rate_filter),
    )
    rows = g.small_w.shape[0]
    put(
        "small_",
        adamw(
            g.small_w[...], g.small_m[...], g.small_v[...], g.grad_small[0:rows, 0:owned], rate_small
        ),
    )
    totals = g.grad_small[rows : rows + 2, 0 : g.run.shape[1]]
    g.stats[...] = stat_decay * g.run[...] + (1.0 - stat_decay) * totals / positions

    for part in range(parts):
        for copy in coming[part]:
            copy.wait()

        for matrix, snap in [(matrix, snap) for matrix in range(2) for snap in range(snaps)]:
            place = snap if matrix else 2 * (snap % 2) + snap // 2
            where = (matrix, slice(None), slice(place * quarter, (place + 1) * quarter))
            now = [g.near[(index, part, *where)] for index in range(3)]
            grad = g.grad_near[part, snap, matrix].astype(jnp.float32)
            values = adamw(*now, grad, rate_mlp)
            for index in range(3):
                g.near[(index, part, *where)] = values[index]
            g.low_near[(part, *where)] = values[3]
        for copy in going[part]:
            copy.start()
        for each in shares[part]:
            passing(*each, 0).wait()
            passing(*each, 1).start()
    for each in through:
        passing(*each, 1).wait()
    for part in range(parts):
        for copy in going[part]:
            copy.wait()


def step_pass(shown, grads, masters, run_stats, positions):
    grad_mlp, grad_filt, grad_small = grads
    mlp, filt, small = masters
    parts = grad_mlp.shape[0]
    width = mlp[0].shape[2] // parts
    f32, low = jnp.float32, jnp.bfloat16
    far = pl.BlockSpec(memory_space=pltpu.HBM)
    near = pl.BlockSpec(memory_space=pltpu.VMEM)
    inputs = dict(out=shown[0], in_grad=shown[1], grad_mlp=grad_mlp)
    inputs |= dict(zip(("mlp_w", "mlp_m", "mlp_v"), mlp, strict=True))
    far_in = len(inputs)
    inputs |= dict(grad_filt=grad_filt, grad_small=grad_small)
    inputs |= dict(zip(("filt_w", "filt_m", "filt_v"), filt, strict=True))
    inputs |= dict(zip(("small_w", "small_m", "small_v"), small, strict=True))
    inputs |= dict(run=run_stats)
    results = (("new", f32), ("first", f32), ("second", f32), ("copy", low))
    outputs = {
        name + "_o": jax.ShapeDtypeStruct(array.shape, array.dtype)
        for name, array in zip(("out", "in_grad"), shown, strict=True)
    }
    outputs |= {"mlp_" + kind: jax.ShapeDtypeStruct(mlp[0].shape, dt) for kind, dt in results}
    far_out = len(outputs)
    outputs |= {"filt_" + kind: jax.ShapeDtypeStruct(filt[0].shape, dt) for kind, dt in results}
    outputs |= {"small_" + kind: jax.ShapeDtypeStruct(small[0].shape, dt) for kind, dt in results}
    outputs |= dict(stats=jax.ShapeDtypeStruct(run_stats.shape, f32))
    scratch = dict(
        near=pltpu.VMEM((3, parts, 2, mlp[0].shape[1], width), f32),
        grad_near=pltpu.VMEM(grad_mlp.shape, low),
        low_near=pltpu.VMEM((parts, 2, mlp[0].shape[1], width), low),
        near_sem=pltpu.SemaphoreType.DMA((4, parts)),
        back_sem=pltpu.SemaphoreType.DMA((4, parts)),
        out_near=pltpu.VMEM(shown[0].shape, low),
        in_grad_near=pltpu.VMEM(shown[1].shape, f32),
        far_sem=pltpu.SemaphoreType.DMA((2, 2, divisor(shown[0].shape[0], 1, 4))),
    )
    return pl.pallas_call(
        functools.partial(step_body, [*inputs, *outputs, *scratch], positions),
        in_specs=[far] * far_in + [near] * (len(inputs) - far_in),
        out_specs=[far] * far_out + [near] * (len(outputs) - far_out),
        out_shape=list(outputs.values()),
        scratch_shapes=list(scratch.values()),
        compiler_params=pltpu.CompilerParams(vmem_limit_bytes=VMEM_LIMIT),
        name="step_pass",
    )(*inputs.values())


def per_device_blocks(
    fields,
    cotangent,
    valid_mask,
    kept_modes,
    mlp_master,
    mlp_first,
    mlp_second,
    filter_master,
    filter_first,
    filter_second,
    small_master,
    small_first,
    small_second,
    run_stats,
):
    snaps, group = lax.axis_size("snap"), lax.axis_size("sp")
    out, in_grad, *grads = block_pass(
        fields, cotangent, valid_mask, kept_modes, mlp_master, filter_master, small_master, snaps, group
    )
    snap_local, row_local, lon_total, channel = fields.shape
    positions = snap_local * snaps * row_local * group * lon_total
    out, in_grad, *stepped = step_pass(
        (out, in_grad),
        grads,
        (
            (mlp_master, mlp_first, mlp_second),
            (filter_master, filter_first, filter_second),
            (small_master, small_first, small_second),
        ),
        run_stats,
        positions,
    )
    rows_apart = (snap_local, lon_total, row_local, channel)
    out, in_grad = [
        jnp.transpose(array.reshape(rows_apart), (0, 2, 1, 3)) for array in (out, in_grad)
    ]
    return (out, in_grad, *stepped)


def per_device(*arrays):
    group, snaps = lax.axis_size("sp"), lax.axis_size("snap")
    channel, hidden = arrays[0].shape[3], arrays[4].shape[2]
    by_block = group == BLOCKS and snaps == 4 and arrays[3].shape[1] == 1
    if by_block and hidden == 6 * 512 and channel // group <= 128 and channel % (16 * group) == 0:
        return per_device_blocks(*arrays)
    return per_device_modes(*arrays)


def solution(mesh):
    return jax.shard_map(
        per_device,
        mesh=mesh,
        in_specs=(
            P("snap", "sp", None, None),
            P("snap", "sp", None, None),
            P("snap", "sp", None),
            P(None, "sp"),
            P(None, "sp", None),
            P(None, "sp", None),
            P(None, "sp", None),
            P(None, "sp", None),
            P(None, "sp", None),
            P(None, "sp", None),
            P(None, "sp"),
            P(None, "sp"),
            P(None, "sp"),
            P(),
        ),
        out_specs=(
            P("snap", "sp", None, None),
            P("snap", "sp", None, None),
            P(None, "sp", None),
            P(None, "sp", None),
            P(None, "sp", None),
            P(None, "sp", None),
            P(None, "sp", None),
            P(None, "sp", None),
            P(None, "sp", None),
            P(None, "sp", None),
            P(None, "sp"),
            P(None, "sp"),
            P(None, "sp"),
            P(None, "sp"),
            P(),
        ),
        check_vma=False,
    )
```

```python
import functools
import math

import jax
import jax.numpy as jnp
import ml_dtypes
import numpy as np
from jax import lax
from jax.experimental import pallas as pl
from jax.experimental.pallas import tpu as pltpu
from jax.sharding import PartitionSpec as P

BLOCKS = 8
NVAR = 20
STEP = 10
VMEM_LIMIT = 63 * 1024 * 1024


eps_norm = 1e-06
shrink_level = 0.01
beta_one = 0.5
beta_two = 0.5
adam_eps = 1e-08
decay_rate = 0.01
rate_mlp = 0.03
rate_filter = 0.1
rate_small = 0.2
stat_decay = 0.5


def layer_norm(values, gain_vec, shift_vec):
    centred = values - jnp.mean(values, axis=-1, keepdims=True)
    spread = jnp.mean(centred * centred, axis=-1, keepdims=True)
    return centred * lax.rsqrt(spread + eps_norm) * gain_vec + shift_vec


def shrink(values):
    return values - shrink_level * jnp.tanh(values / shrink_level)


def lon_tables(lon_total, mode_total):
    places = jnp.arange(lon_total, dtype=jnp.int32)
    orders = jnp.arange(mode_total, dtype=jnp.int32)
    angles = (places[:, None] * orders[None, :] % lon_total).astype(jnp.float32) * (
        2.0 * math.pi / lon_total
    )
    scaling = 1.0 / math.sqrt(lon_total)
    forward_tab = jnp.stack([jnp.cos(angles), -jnp.sin(angles)], axis=1) * scaling
    doubling = jnp.where(orders == 0, 1.0, 2.0).astype(jnp.float32)[:, None]
    inverse_tab = (
        jnp.stack([jnp.cos(angles).T * doubling, -jnp.sin(angles).T * doubling], axis=0) * scaling
    )
    return (forward_tab.astype(jnp.bfloat16), inverse_tab.astype(jnp.bfloat16))


def lat_table(lat_total):
    places = jnp.arange(lat_total, dtype=jnp.int32)
    angles = (places[:, None] * places[None, :] % lat_total).astype(jnp.float32) * (
        2.0 * math.pi / lat_total
    )
    cosine = jnp.cos(angles)
    sine_part = jnp.sin(angles)
    upper_rows = jnp.stack([cosine, sine_part], axis=1)
    bottom = jnp.stack([-sine_part, cosine], axis=1)
    return (jnp.stack([upper_rows, bottom], axis=0) / math.sqrt(lat_total)).astype(jnp.bfloat16)


def complex_pair(real_part, imag_part):
    return jnp.stack([jnp.stack([real_part, -imag_part]), jnp.stack([imag_part, real_part])])


gelu_scale = math.sqrt(2.0 / math.pi)
gelu_cubic = 0.044715


def gelu_both(value):
    bend = (gelu_scale * gelu_cubic) * (value * value)
    turn = jnp.tanh(value * (gelu_scale + bend))
    half = 0.5 + 0.5 * turn
    slope = half * (1.0 + (value * (1.0 - turn)) * (gelu_scale + 3.0 * bend))
    return value * half, slope


def dot_nt(left, right):
    return lax.dot_general(
        left, right, (((1,), (1,)), ((), ())), preferred_element_type=jnp.float32
    )


def dot_nn(left, right):
    return jnp.dot(left, right, preferred_element_type=jnp.float32)


def divisor(total, unit, most):
    return max(size for size in range(unit, most + 1, unit) if total % size == 0)


def mlp_body(
    tile,
    normed_ref,
    cot_ref,
    up_ref,
    down_ref,
    bias_ref,
    out_ref,
    back_ref,
    grad_up_ref,
    grad_down_ref,
    grad_bias_ref,
    normed_turned,
    cot_turned,
    act_ref,
    slope_ref,
):
    tokens = normed_ref.shape[0]

    @pl.when(pl.program_id(0) == 0)
    def _():
        normed_turned[...] = normed_ref[...].T
        cot_turned[...] = cot_ref[...].T
        out_ref[...] = jnp.zeros_like(out_ref)
        back_ref[...] = jnp.zeros_like(back_ref)

    grad_bias_ref[...] = jnp.zeros_like(grad_bias_ref)

    @pl.loop(0, tokens // tile)
    def _(step):
        rows = pl.ds(pl.multiple_of(step * tile, tile), tile)
        act, slope = gelu_both(dot_nn(normed_ref[rows, :], up_ref[...]) + bias_ref[...])
        act = act.astype(jnp.bfloat16)
        slope = (dot_nn(cot_ref[rows, :], down_ref[...]) * slope).astype(jnp.bfloat16)
        act_ref[rows, :] = act
        slope_ref[rows, :] = slope
        grad_bias_ref[...] += jnp.sum(slope.astype(jnp.float32), axis=0, keepdims=True)
        out_ref[rows, :] += dot_nt(act, down_ref[...])
        back_ref[rows, :] += dot_nt(slope, up_ref[...])

    grad_up_ref[...] = dot_nn(normed_turned[...], slope_ref[...]).astype(grad_up_ref.dtype)
    grad_down_ref[...] = dot_nn(cot_turned[...], act_ref[...]).astype(grad_down_ref.dtype)


def mlp_pass(normed, cot, weights, bias):
    tokens, channel = normed.shape
    hidden = weights.shape[2]
    width = divisor(hidden, 128, 512)
    tile = divisor(tokens, 16, 480)
    whole = pl.BlockSpec((tokens, channel), lambda j: (0, 0))
    block = pl.BlockSpec((channel, width), lambda j: (0, j))
    line = pl.BlockSpec((1, width), lambda j: (0, j))
    part = lambda which: pl.BlockSpec((None, channel, width), lambda j: (which, 0, j))
    total = jax.ShapeDtypeStruct((tokens, channel), jnp.float32)
    grads = jax.ShapeDtypeStruct((channel, hidden), jnp.bfloat16)
    return pl.pallas_call(
        functools.partial(mlp_body, tile),
        grid=(hidden // width,),
        in_specs=[whole, whole, part(0), part(1), line],
        out_specs=[whole, whole, block, block, line],
        out_shape=[total, total, grads, grads, jax.ShapeDtypeStruct((1, hidden), jnp.float32)],
        scratch_shapes=[
            pltpu.VMEM((channel, tokens), jnp.bfloat16),
            pltpu.VMEM((channel, tokens), jnp.bfloat16),
            pltpu.VMEM((tokens, width), jnp.bfloat16),
            pltpu.VMEM((tokens, width), jnp.bfloat16),
        ],
        compiler_params=pltpu.CompilerParams(vmem_limit_bytes=56 * 1024 * 1024),
        cost_estimate=pl.CostEstimate(
            flops=12 * tokens * channel * hidden,
            bytes_accessed=8 * channel * hidden + 12 * tokens * channel,
            transcendentals=tokens * hidden,
        ),
        name="mlp_pass",
    )(normed, cot, weights, weights, bias)


def spectral_front(arrived, lat_fwd, first_pair, second_pair, bias_one, bias_two):
    spectrum = jnp.einsum(
        "pkqr,nrqmd->nkpmd", lat_fwd, arrived, preferred_element_type=jnp.float32
    ).astype(jnp.bfloat16)
    snap_local, lat_total, pair_count, mode_local, channel = spectrum.shape
    blocked = spectrum.reshape(
        snap_local, lat_total, pair_count, mode_local, BLOCKS, channel // BLOCKS
    )
    pre_one = (
        jnp.einsum("nkqmbi,pqbio->nkpmbo", blocked, first_pair, preferred_element_type=jnp.float32)
        + bias_one
    )
    act_one = jax.nn.gelu(pre_one).astype(jnp.bfloat16)
    pre_two = (
        jnp.einsum("nkqmbi,pqbio->nkpmbo", act_one, second_pair, preferred_element_type=jnp.float32)
        + bias_two
    )
    return (blocked, pre_one, act_one, pre_two)


def adamw(master, first_mom, second_mom, gradient, step_rate):
    first_next = beta_one * first_mom + (1.0 - beta_one) * gradient
    second_next = beta_two * second_mom + (1.0 - beta_two) * gradient * gradient
    fix_one = 1.0 / (1.0 - beta_one**STEP)
    fix_two = 1.0 / (1.0 - beta_two**STEP)
    direction = first_next * fix_one / (jnp.sqrt(second_next * fix_two) + adam_eps)
    master_next = master - step_rate * (direction + decay_rate * master)
    return (master_next, first_next, second_next, master_next.astype(jnp.bfloat16))


def per_device_modes(
    fields,
    cotangent,
    valid_mask,
    kept_modes,
    mlp_master,
    mlp_first,
    mlp_second,
    filter_master,
    filter_first,
    filter_second,
    small_master,
    small_first,
    small_second,
    run_stats,
):
    group_size = lax.axis_size("sp")
    snap_local, row_local, lon_total, channel = fields.shape
    lat_total = row_local * group_size
    mode_local = kept_modes.shape[1]
    mode_total = mode_local * group_size
    block_width = channel // BLOCKS
    lon_fwd, lon_inv = lon_tables(lon_total, mode_total)
    lat_fwd = lat_table(lat_total)
    mlp_w, filt_w, small_w = (
        lax.all_gather(mlp_master.astype(jnp.bfloat16), "sp", axis=1, tiled=True),
        lax.all_gather(filter_master.astype(jnp.bfloat16), "sp", axis=1, tiled=True),
        lax.all_gather(small_master.astype(jnp.bfloat16), "sp", axis=1, tiled=True),
    )
    small_f = small_w.astype(jnp.float32)
    weights = filt_w.reshape(4, BLOCKS, block_width, block_width)
    first_pair = complex_pair(weights[0], weights[1])
    second_pair = complex_pair(weights[2], weights[3])
    bias_one = small_f[4:6].reshape(2, 1, BLOCKS, block_width)
    bias_two = small_f[6:8].reshape(2, 1, BLOCKS, block_width)
    fields_float = fields.astype(jnp.float32)
    normed, norm_pull = jax.vjp(layer_norm, fields_float, small_f[0], small_f[1])
    normed_low = normed.astype(jnp.bfloat16)
    spec_lon = jnp.einsum(
        "nrld,lqm->nrqmd", normed_low, lon_fwd, preferred_element_type=jnp.float32
    ).astype(jnp.bfloat16)
    arrived = lax.all_to_all(spec_lon, "sp", split_axis=3, concat_axis=1, tiled=True)
    spectral = spectral_front(arrived, lat_fwd, first_pair, second_pair, bias_one, bias_two)
    keep_mask = kept_modes.astype(jnp.float32)[None, :, None, :, None, None]
    masked = (shrink(spectral[3]) * keep_mask).astype(jnp.bfloat16)
    masked = masked.reshape(snap_local, lat_total, 2, mode_local, channel)
    returned = jnp.einsum(
        "pkqr,nkpmd->nrqmd", lat_fwd, masked, preferred_element_type=jnp.float32
    ).astype(jnp.bfloat16)
    home_modes = lax.all_to_all(returned, "sp", split_axis=1, concat_axis=3, tiled=True)
    filtered = jnp.einsum(
        "nrqmd,qml->nrld", home_modes, lon_inv, preferred_element_type=jnp.float32
    )
    mixture = fields_float + normed + filtered
    normed_two, norm_two_pull = jax.vjp(layer_norm, mixture, small_f[2], small_f[3])
    normed_two_low = normed_two.astype(jnp.bfloat16)
    tokens = snap_local * row_local * lon_total
    passed = mlp_pass(
        normed_two_low.reshape(tokens, channel),
        cotangent.reshape(tokens, channel),
        mlp_w,
        small_f[9:].reshape(1, -1),
    )
    output = mixture + passed[0].reshape(mixture.shape) + small_f[8]
    weight_mask = valid_mask.astype(jnp.float32)[..., None]
    variables = output[..., :NVAR]
    local_sums = jnp.stack(
        [
            jnp.sum(weight_mask * variables, axis=(0, 1, 2)),
            jnp.sum(weight_mask * variables * variables, axis=(0, 1, 2)),
        ]
    )
    total_sums = lax.psum(local_sums, ("snap", "sp"))
    positions = snap_local * lax.axis_size("snap") * lat_total * lon_total
    stats_new = stat_decay * run_stats + (1.0 - stat_decay) * total_sums / positions
    cot_float = cotangent.astype(jnp.float32)
    grad_normed_two = passed[1].reshape(mixture.shape)
    grad_bias_hidden = passed[4]
    grad_mix_norm, grad_gain_two, grad_shift_two = norm_two_pull(grad_normed_two)
    grad_mixture = cot_float + grad_mix_norm
    grad_bias_out = jnp.sum(cot_float, axis=(0, 1, 2))
    grad_filtered = grad_mixture.astype(jnp.bfloat16)
    grad_home = jnp.einsum(
        "nrld,qml->nrqmd", grad_filtered, lon_inv, preferred_element_type=jnp.float32
    ).astype(jnp.bfloat16)
    grad_returned = lax.all_to_all(grad_home, "sp", split_axis=3, concat_axis=1, tiled=True)
    grad_masked = jnp.einsum(
        "pkqr,nrqmd->nkpmd", lat_fwd, grad_returned, preferred_element_type=jnp.float32
    )
    arrived_again = lax.all_to_all(spec_lon, "sp", split_axis=3, concat_axis=1, tiled=True)
    used_front = spectral_front(arrived_again, lat_fwd, first_pair, second_pair, bias_one, bias_two)
    blocked, pre_one, act_one, pre_two = used_front
    grad_two = jax.vjp(shrink, pre_two)[1](grad_masked.reshape(pre_two.shape) * keep_mask)[
        0
    ].astype(jnp.bfloat16)
    grad_bias_two = jnp.sum(grad_two.astype(jnp.float32), axis=(0, 1, 3))
    grad_second = jnp.einsum(
        "nkqmbi,nkpmbo->pqbio", act_one, grad_two, preferred_element_type=jnp.float32
    )
    grad_act = jnp.einsum(
        "nkpmbo,pqbio->nkqmbi", grad_two, second_pair, preferred_element_type=jnp.float32
    )
    grad_one = jax.vjp(jax.nn.gelu, pre_one)[1](grad_act)[0].astype(jnp.bfloat16)
    grad_bias_one = jnp.sum(grad_one.astype(jnp.float32), axis=(0, 1, 3))
    grad_first = jnp.einsum(
        "nkqmbi,nkpmbo->pqbio", blocked, grad_one, preferred_element_type=jnp.float32
    )
    grad_spectrum = jnp.einsum(
        "nkpmbo,pqbio->nkqmbi", grad_one, first_pair, preferred_element_type=jnp.float32
    ).astype(jnp.bfloat16)
    grad_spectrum = grad_spectrum.reshape(snap_local, lat_total, 2, mode_local, channel)
    grad_lon = jnp.einsum(
        "pkqr,nkpmd->nrqmd", lat_fwd, grad_spectrum, preferred_element_type=jnp.float32
    ).astype(jnp.bfloat16)
    grad_rows = lax.all_to_all(grad_lon, "sp", split_axis=1, concat_axis=3, tiled=True)
    grad_normed = grad_mixture + jnp.einsum(
        "nrqmd,lqm->nrld", grad_rows, lon_fwd, preferred_element_type=jnp.float32
    )
    grad_field_norm, grad_gain_one, grad_shift_one = norm_pull(grad_normed)
    input_grad = grad_mixture + grad_field_norm
    grad_filter = jnp.stack(
        [
            grad_first[0, 0] + grad_first[1, 1],
            grad_first[1, 0] - grad_first[0, 1],
            grad_second[0, 0] + grad_second[1, 1],
            grad_second[1, 0] - grad_second[0, 1],
        ]
    ).reshape(4, channel, block_width)
    grad_small = jnp.concatenate(
        [
            jnp.stack([grad_gain_one, grad_shift_one, grad_gain_two, grad_shift_two]),
            grad_bias_one.reshape(2, channel),
            grad_bias_two.reshape(2, channel),
            grad_bias_out[None, :],
            grad_bias_hidden.reshape(-1, channel),
        ],
        axis=0,
    )
    shares = (
        jnp.stack([
            lax.psum_scatter(part, "sp", scatter_dimension=0, tiled=True) for part in passed[2:4]
        ]),
        lax.psum_scatter(grad_filter, "sp", scatter_dimension=1, tiled=True),
        lax.psum_scatter(grad_small, "sp", scatter_dimension=1, tiled=True),
    )
    owned = (
        lax.psum(shares[0].astype(jnp.bfloat16), "snap").astype(jnp.float32),
        lax.psum(shares[1].astype(jnp.bfloat16), "snap").astype(jnp.float32),
        lax.psum(shares[2].astype(jnp.bfloat16), "snap").astype(jnp.float32),
    )
    mlp_new, mlp_first_new, mlp_second_new, mlp_copy = adamw(
        mlp_master, mlp_first, mlp_second, owned[0], rate_mlp
    )
    filter_new, filter_first_new, filter_second_new, filter_copy = adamw(
        filter_master, filter_first, filter_second, owned[1], rate_filter
    )
    small_new, small_first_new, small_second_new, small_copy = adamw(
        small_master, small_first, small_second, owned[2], rate_small
    )
    return (
        output.astype(jnp.bfloat16),
        input_grad,
        mlp_new,
        mlp_first_new,
        mlp_second_new,
        mlp_copy,
        filter_new,
        filter_first_new,
        filter_second_new,
        filter_copy,
        small_new,
        small_first_new,
        small_second_new,
        small_copy,
        stats_new,
    )


FIRST, SECOND, THIRD, FOURTH, HALF, QUARTER, LEVEL, LAST = range(8)
SCHEDULE = {
    "a": [(FIRST, 0)],
    "b": [(FIRST, 1)],
    "c0": [(SECOND, 0)],
    "d0": [(FIRST, 2)],
    "d1": [(THIRD, 0)],
    "e": [(SECOND, 1)],
    "f0": [(SECOND, 2), (FIRST, 3)],
    "g": [(THIRD, 1)],
    "h0": [(THIRD, 2), (FIRST, 4)],
    "h1": [(FOURTH, 0), (SECOND, 3)],
    ("k0", 0): [(SECOND, 4)],
    ("m", 0): [(THIRD, 3)],
    ("m0", 0): [(FOURTH, 1), (THIRD, 4)],
    ("k", 1): [(FOURTH, 2)],
    ("k1", 1): [(FIRST, 5)],
    ("l", 1): [(HALF, 0)],
    ("k2", 2): [(FOURTH, 3)],
    ("l", 2): [(HALF, 1)],
    ("m1", 2): [(QUARTER, 0)],
    ("k0", 3): [(HALF, 2)],
    ("k1", 3): [(FOURTH, 4)],
    ("m2", 3): [(LEVEL, 0)],
    ("k", 4): [(QUARTER, 1), (HALF, 3)],
    ("k1", 4): [(FOURTH, 5)],
    ("m", 4): [(LEVEL, 1), (QUARTER, 2)],
    ("k", 5): [(LAST, 0)],
    ("k1", 5): [(LEVEL, 2), (QUARTER, 3)],
    ("k2", 5): [(HALF, 4)],
    "p0": [(LAST, 1)],
    "o1": [(LEVEL, 3), (QUARTER, 4), (HALF, 5)],
    "t0": [(LAST, 2), (LEVEL, 4)],
    "u0": [(LAST, 3), (QUARTER, 5)],
    "w": [(LAST, 4)],
    "x0": [(LEVEL, 5)],
    "z": [(LAST, 5)],
}


def lon_matrix(lon_total, mode_total, snaps, rows):
    places = np.arange(lon_total)
    orders = np.arange(mode_total)
    angles = (places[:, None] * orders[None, :] % lon_total) * (2.0 * math.pi / lon_total)
    doubling = np.where(orders == 0, 1.0, 2.0)
    scaling = 1.0 / math.sqrt(lon_total)
    forward = np.stack([np.cos(angles), -np.sin(angles)], axis=1) * scaling
    inverse = forward * doubling

    def spread(table):
        table = np.einsum(
            "ab,lx,rs->alrbsx", np.eye(snaps), table.reshape(lon_total, -1), np.eye(rows)
        )
        return table.reshape(snaps * lon_total * rows, -1).astype(ml_dtypes.bfloat16)

    return spread(forward), spread(inverse)


def lon_turn(lon_total, rows):
    turn = np.einsum("lk,rs->rlks", np.eye(lon_total), np.eye(rows))
    return turn.reshape(rows, lon_total, lon_total * rows).astype(ml_dtypes.bfloat16)


def lat_matrix(lat_total, mode_total):
    places = np.arange(lat_total)
    angles = (places[:, None] * places[None, :] % lat_total) * (2.0 * math.pi / lat_total)
    cosine, sine = np.cos(angles), np.sin(angles)
    table = np.stack([np.stack([cosine, sine], axis=1), np.stack([-sine, cosine], axis=1)])
    table = np.einsum("pkqr,ab->pakrqb", table / math.sqrt(lat_total), np.eye(mode_total))
    size = 2 * lat_total * mode_total
    return table.reshape(size, size).astype(ml_dtypes.bfloat16)


class Refs:
    pass


def block_body(names, sizes, *refs):
    g = Refs()
    for name, ref in zip(names, refs, strict=True):
        setattr(g, name, ref)
    snaps, group, parts, width = sizes
    levels = group // 2
    tokens = g.fields.shape[0] * g.fields.shape[1]
    channel = g.fields.shape[2]
    owned = channel // group
    half = width // 2
    quarter = width // snaps
    tile = tokens // 3
    short = divisor(tokens // 2, 16, 240)
    packed = g.modes.shape[2]
    strip = divisor(tokens // 2, 48, 144)
    sub = divisor(strip, 16, 48)
    low = jnp.bfloat16
    f32 = jnp.float32

    me_snap = lax.axis_index("snap")
    me_sp = lax.axis_index("sp")
    core = lax.rem(me_sp, 2)
    level = me_sp // 2

    def at(snap, sp):
        return {"snap": snap, "sp": sp}

    def sp_after(step):
        return lax.rem(me_sp + step, group)

    def sp_before(step):
        return lax.rem(me_sp + group - step, group)

    def snap_after(step):
        return lax.rem(me_snap + step, snaps)

    def snap_before(step):
        return lax.rem(me_snap + snaps - step, snaps)

    def level_after(step):
        return lax.rem(level + step, levels)

    def level_before(step):
        return lax.rem(level + levels - step, levels)

    other_core = at(me_snap, me_sp + 1 - 2 * core)

    def send(src, dst, sems, index, target):
        return pltpu.make_async_remote_copy(
            src_ref=src,
            dst_ref=dst,
            send_sem=sems[0].at[index],
            recv_sem=sems[1].at[index],
            device_id=target,
            device_id_type=pl.DeviceIdType.MESH,
        )

    half_tokens = tokens // 2

    def strips(body, first=0, count=tokens, before=None, after=None):
        @pl.loop(0, count // strip)
        def _(step):
            if before is not None:
                before(first // strip + step)
            for at_row in range(0, strip, sub):
                body(pl.ds(pl.multiple_of(first + step * strip + at_row, 16), sub))
            if after is not None:
                after(first // strip + step)

    def half_strips(body, part, **around):
        strips(body, part * half_tokens, half_tokens, **around)

    def strip_copy(near, far, sems, place, out):
        rows = pl.ds(pl.multiple_of(place * strip, strip), strip)
        ends = [near.at[rows], far.reshape(tokens, channel).at[rows]]
        if not out:
            ends.reverse()
        return pltpu.make_async_copy(*ends, sems.at[place])

    def fields_load(place):
        return strip_copy(g.fields_in, g.fields, g.fields_sem, place, False)

    def cot_load(place):
        return strip_copy(g.cot_in, g.cot, g.cot_sem, place, False)

    def out_copy(place):
        return strip_copy(g.fields_in, g.out, g.fields_sem, place, True)

    def grad_copy(place):
        return strip_copy(g.grid, g.in_grad, g.cot_sem, place, True)

    def half_rows(part):
        return slice(part * half_tokens, (part + 1) * half_tokens)

    def fold(value):
        return jnp.sum(value.reshape(-1, 8, value.shape[1]), axis=0)

    loads = {}

    def load(name, index):
        copy = pltpu.make_async_copy(getattr(g, name), getattr(g, name + "_in"), g.load_sem.at[index])
        copy.start()
        loads[name] = copy

    for index, name in enumerate(
        [name for name in names[: names.index("out")] if name not in ("mlp", "fields", "cot")]
    ):
        load(name, index)
    for copy in (fields_load, cot_load):
        for place in range(tokens // strip):
            copy(place).start()

    def master_load(part):
        return pltpu.make_async_copy(
            g.mlp.at[:, :, part * width : (part + 1) * width],
            g.mlp_part.at[part % 2],
            g.load_sem.at[len(loads) + part % 2],
        )

    master_load(0).start()
    master_load(1).start()

    barrier = pltpu.get_barrier_semaphore()
    peers = [at(me_snap, sp_after(step)) for step in range(1, group)]
    peers += [at(snap_after(step), me_sp) for step in range(1, snaps)]
    for peer in peers:
        pl.semaphore_signal(
            barrier, inc=1, device_id=peer, device_id_type=pl.DeviceIdType.MESH
        )

    loads["small"].wait()
    loads["kept"].wait()
    g.own_small[...] = jnp.zeros_like(g.own_small)
    rows_small = g.small.shape[0]
    g.own_small[0:rows_small, 0:owned] = g.small_in[...].astype(low).astype(f32)
    pairs_kept = g.kept.shape[1]
    lines = lax.broadcasted_iota(jnp.int32, (pairs_kept, pairs_kept), 0)
    places = lax.broadcasted_iota(jnp.int32, (pairs_kept, pairs_kept), 1)
    kept = jnp.where(lines == places, g.kept_in[...].astype(f32), 0.0)
    g.own_small[16:, :] = jnp.broadcast_to(
        jnp.sum(kept, axis=1, keepdims=True), (pairs_kept, g.own_small.shape[1])
    )
    pl.semaphore_wait(barrier, len(peers))

    def small_copy(step):
        return send(
            g.own_small, g.all_small.at[me_sp], (g.small_s, g.small_r), step, at(me_snap, sp_after(step))
        )

    for step in range(1, group):
        small_copy(step).start()
    g.all_small[me_sp] = g.own_small[...]

    snap_low = lax.rem(me_snap, 2)
    snap_high = me_snap // 2
    beside_low = me_snap + 1 - 2 * snap_low
    beside_high = me_snap + 2 - 4 * snap_high

    def own_quarter(part):
        odd = lax.rem(part, 2)
        return (1 - odd) * me_snap + odd * (2 * snap_low + snap_high)

    def own_place(part):
        return pl.ds(0, snaps) if part == parts - 1 else own_quarter(part)

    def half_quarters(part):
        return pl.ds(2 * (own_quarter(part) // 2), 2)

    def own_rows(sp):
        return pl.ds(pl.multiple_of(sp * owned, owned), owned)

    def first_copy(part, step):
        target = sp_after(step)
        matrix = lax.rem(target, 2)
        place = own_place(part)
        return send(
            g.own_w.at[part, matrix, place],
            g.all_w.at[part, matrix, place, own_rows(me_sp)],
            (g.first_s, g.first_r),
            (part, step),
            at(me_snap, target),
        )

    def first_local(part):
        place = own_place(part)
        return pltpu.make_async_copy(
            g.own_w.at[part, core, place],
            g.all_w.at[part, core, place, own_rows(me_sp)],
            g.first_s.at[part, 0],
        )

    def second_copy(part):
        odd = lax.rem(part, 2)
        view = g.all_w.at[part, core, own_quarter(part)]
        target = at((1 - odd) * beside_low + odd * beside_high, me_sp)
        return send(view, view, (g.second_s, g.second_r), part, target)

    def third_copy(part):
        odd = lax.rem(part, 2)
        view = g.all_w.at[part, core, half_quarters(part)]
        target = at((1 - odd) * beside_high + odd * beside_low, me_sp)
        return send(view, view, (g.third_s, g.third_r), part, target)

    def fourth_copy(part):
        view = g.all_w.at[part, core]
        return send(view, view, (g.fourth_s, g.fourth_r), part, other_core)

    def start_first(part):
        for step in range(1, group):
            first_copy(part, step).start()
        first_local(part).start()

    def wait_first(part):
        for step in range(1, group):
            first_copy(part, step).wait_recv()
        first_local(part).wait()

    def pass_second(part):
        wait_first(part)
        second_copy(part).start()

    def pass_third(part):
        second_copy(part).wait_recv()
        third_copy(part).start()

    def pass_fourth(part):
        if part == parts - 1:
            wait_first(part)
        else:
            third_copy(part).wait_recv()
        fourth_copy(part).start()

    stages = {FIRST: start_first, SECOND: pass_second, THIRD: pass_third, FOURTH: pass_fourth}

    def reach(point):
        for stage, part in SCHEDULE.get(point, ()):
            stages[stage](part)

    for part in range(parts):
        master_load(part).wait()
        for place in range(snaps):
            cols = slice(place * quarter, (place + 1) * quarter)
            g.own_w[part, :, place] = g.mlp_part[part % 2, :, :, cols].astype(low)
        if part + 2 < parts:
            master_load(part + 2).start()
        if (FIRST, part) in SCHEDULE["a"]:
            start_first(part)

    def first_unit(rows):
        values = g.fields_in[rows, :].astype(f32)
        centred = values - jnp.mean(values, axis=-1, keepdims=True)
        scale = lax.rsqrt(jnp.mean(centred * centred, axis=-1, keepdims=True) + eps_norm)
        g.scale_one[rows, :] = scale
        g.grid[rows, :] = centred * scale

    strips(first_unit, before=lambda place: fields_load(place).wait())
    reach("b")
    for step in range(1, group):
        small_copy(step).wait_recv()
    for sp in range(group):
        g.gains[:, sp * owned : (sp + 1) * owned] = g.all_small[sp, 0:16, 0:owned]
        g.keep[sp * pairs_kept : (sp + 1) * pairs_kept, :] = g.all_small[sp, 16:, :]

    def first_norm(rows):
        unit = g.grid[rows, :]
        normed = unit * g.gains[0:1, :] + g.gains[1:2, :]
        g.unit_one[rows, :] = unit.astype(low)
        g.normed[rows, :] = normed.astype(low)
        g.grid[rows, :] = g.fields_in[rows, :].astype(f32) + normed

    half_snaps = g.arrived.shape[0] // 2

    third_rows = packed // 3
    spare = 128 - owned

    def pack(value):
        return jnp.concatenate(
            [
                jnp.concatenate(
                    [
                        value[at_row * third_rows : (at_row + 1) * third_rows],
                        value[packed:, at_row * spare : (at_row + 1) * spare],
                    ],
                    axis=1,
                )
                for at_row in range(3)
            ],
            axis=0,
        ).astype(low)

    def unpack(value):
        value = value.astype(f32)
        rest = [
            value[at_row * third_rows : (at_row + 1) * third_rows, owned:] for at_row in range(3)
        ]
        return jnp.concatenate([value[:, 0:owned], jnp.concatenate(rest, axis=1)], axis=0)

    def block_copy(which, part, step):
        target = sp_after(step)
        return send(
            g.modes.at[part, target],
            g.modes_got.at[part, me_sp],
            (g.block_s, g.block_r),
            (which, part, step),
            at(me_snap, target),
        )

    def row_copy(which, part, step):
        target = sp_after(step)
        return send(
            g.rows_out.at[part, target],
            g.rows_got.at[part, me_sp],
            (g.row_s, g.row_r),
            (which, part, step),
            at(me_snap, target),
        )

    def to_blocks(table, which, part):
        modes = dot_nn(table, g.normed[half_rows(part), :])
        for block in range(group):
            g.modes[part, block] = pack(modes[:, block * owned : (block + 1) * owned])
        for step in range(1, group):
            block_copy(which, part, step).start()
        g.modes_got[part, me_sp] = g.modes[part, me_sp]

    def take_blocks(which, part):
        for step in range(1, group):
            block_copy(which, part, step).wait_recv()
        each = g.arrived.shape[1] // group
        for sp in range(group):
            value = unpack(g.modes_got[part, sp])
            value = jnp.concatenate([value, jnp.zeros((value.shape[0], spare), f32)], axis=1)
            for index in range(half_snaps):
                g.arrived[part * half_snaps + index, sp * each : (sp + 1) * each, :] = value[
                    index * each : (index + 1) * each
                ].astype(low)

    def to_rows(which, part, tables):
        each = tables[0].shape[0] // group
        for sp in range(group):
            value = [table[sp * each : (sp + 1) * each, 0:owned] for table in tables]
            g.rows_out[part, sp] = pack(jnp.concatenate(value, axis=0))
        for step in range(1, group):
            row_copy(which, part, step).start()
        g.rows_got[part, me_sp] = g.rows_out[part, me_sp]

    def home_modes(which, part):
        for step in range(1, group):
            row_copy(which, part, step).wait_recv()
        for block in range(group):
            g.gathered[part, :, block * owned : (block + 1) * owned] = unpack(
                g.rows_got[part, block]
            )
        g.home_low[part] = g.gathered[part].astype(low)

    loads["lon_f"].wait()
    for part in range(2):
        half_strips(first_norm, part)
        reach("c" + str(part))
        to_blocks(g.lon_f_in[...], 0, part)
        reach("d" + str(part))

    loads["filt"].wait()
    for weight, first in ((g.weight_one, 0), (g.weight_two, 2)):
        weight[...] = jnp.zeros_like(weight)
        real = g.filt_in[first].astype(low)
        imag = g.filt_in[first + 1].astype(low)
        weight[0:owned, 0:owned] = real
        weight[128 : 128 + owned, 128 : 128 + owned] = real
        weight[0:owned, 128 : 128 + owned] = imag
        weight[128 : 128 + owned, 0:owned] = -imag

    def bias_row(first):
        return jnp.concatenate(
            [g.own_small[first : first + 1, :], g.own_small[first + 1 : first + 2, :]], axis=1
        )

    for place in range(tokens // strip):
        cot_load(place).wait()
    reach("e")
    loads["lat_f"].wait()
    loads["lat_b"].wait()
    pairs = g.arrived.shape[1] // 2
    half_modes = half_snaps * pairs

    def mode_half(part):
        return slice(part * half_modes, (part + 1) * half_modes)

    def spectra(out, kind, part):
        for snap in range(part * half_snaps, (part + 1) * half_snaps):
            spectrum = dot_nn(g.lat_f_in[...], g.arrived[snap]).astype(kind)
            rows = slice(snap * pairs, (snap + 1) * pairs)
            out[rows, 0:128] = spectrum[0:pairs]
            out[rows, 128:256] = spectrum[pairs:]

    def grids(values):
        tables = []
        for index in range(half_snaps):
            rows = values[index * pairs : (index + 1) * pairs]
            rows = jnp.concatenate([rows[:, 0:128], rows[:, 128:256]], axis=0)
            tables.append(dot_nn(g.lat_b_in[...], rows))
        return tables

    def keep_half():
        keep = jnp.concatenate([g.keep[...], g.keep[...]], axis=1)
        return jnp.concatenate([keep] * half_snaps, axis=0)

    for part in range(2):
        take_blocks(0, part)
        rows = mode_half(part)
        spectra(g.spectrum, low, part)
        g.pre_one[rows, :] = dot_nn(g.spectrum[rows, :], g.weight_one[...]) + bias_row(4)
        g.act_one[rows, :] = gelu_both(g.pre_one[rows, :])[0].astype(low)
        g.pre_two[rows, :] = dot_nn(g.act_one[rows, :], g.weight_two[...]) + bias_row(6)
        to_rows(0, part, grids((shrink(g.pre_two[rows, :]) * keep_half()).astype(low)))
        reach("f" + str(part))
    g.cot_turned[...] = g.cot_in[...].T
    reach("g")

    loads["lon_i"].wait()

    def second_norm(rows):
        values = g.grid[rows, :]
        centred = values - jnp.mean(values, axis=-1, keepdims=True)
        scale = lax.rsqrt(jnp.mean(centred * centred, axis=-1, keepdims=True) + eps_norm)
        centred = centred * scale
        g.unit_two[rows, :] = centred.astype(low)
        g.scale_two[rows, :] = scale
        g.normed[rows, :] = (centred * g.gains[2:3, :] + g.gains[3:4, :]).astype(low)
        g.grid[rows, :] = values + g.gains[8:9, :]
        g.back[rows, :] = jnp.zeros((sub, channel), f32)

    for part in range(2):
        home_modes(0, part)
        g.grid[half_rows(part), :] += dot_nn(g.lon_i_in[...], g.home_low[part])
        reach("h" + str(part))
        half_strips(second_norm, part)
        reach("i" + str(part))
    g.normed_turned[...] = g.normed[...].T
    reach("j")
    flat = jnp.concatenate([g.gains[9 + row : 10 + row, :] for row in range(rows_small - 9)], axis=1)
    for part in range(parts):
        g.bias[part] = flat[:, part * width : (part + 1) * width]

    def core_copy(part, matrix):
        slot = lax.rem(part, 2)
        return send(
            g.grads.at[matrix, :, 1 - core],
            g.core_got.at[slot, matrix],
            (g.core_s, g.core_r),
            (slot, matrix),
            other_core,
        )

    places_one = (snap_low, snap_high)
    places_two = (snap_high, snap_low)
    beside_one = (beside_low, beside_high)
    beside_two = (beside_high, beside_low)

    def half_copy(part, matrix):
        slot = lax.rem(part, 2)
        place = lax.rem(part, 4)
        return send(
            g.half_out.at[slot, matrix, 1 - places_one[matrix]],
            g.half_got.at[place, matrix],
            (g.half_s, g.half_r),
            (place, matrix),
            at(beside_one[matrix], me_sp),
        )

    def quarter_copy(part, matrix):
        slot = lax.rem(part, 2)
        return send(
            g.quarter_out.at[slot, matrix, 1 - places_two[matrix]],
            g.quarter_got.at[slot, matrix],
            (g.quarter_s, g.quarter_r),
            (slot, matrix),
            at(beside_two[matrix], me_sp),
        )

    def level_copy(part, step):
        slot = lax.rem(part, 2)
        place = lax.rem(part, 4)
        target = level_after(step)
        return send(
            g.level_out.at[slot, target],
            g.level_got.at[place, level],
            (g.level_s, g.level_r),
            (place, step),
            at(me_snap, 2 * target + core),
        )

    def last_copy(part, step):
        view = g.total.at[part, me_snap]
        return send(view, view, (g.last_s, g.last_r), (part, step), at(snap_after(step), me_sp))

    def half_stage(part):
        slot = lax.rem(part, 2)
        for matrix in range(2):

            if part >= 2:
                half_copy(part - 2, matrix).wait_send()

            core_copy(part, matrix).wait_recv()

            @pl.loop(0, levels)
            def _(row, matrix=matrix):
                both = g.grads[matrix, row, core].astype(f32) + g.core_got[
                    slot, matrix, row
                ].astype(f32)
                both = both.astype(low)
                g.half_out[slot, matrix, 0, row] = both[:, 0:half]
                g.half_out[slot, matrix, 1, row] = both[:, half:width]

            half_copy(part, matrix).start()

    def quarter_stage(part):
        slot = lax.rem(part, 2)
        for matrix in range(2):

            if part >= 2:
                quarter_copy(part - 2, matrix).wait_send()

            half_copy(part, matrix).wait_recv()
            for row in range(levels):
                both = g.half_out[slot, matrix, places_one[matrix], row].astype(f32) + g.half_got[
                    lax.rem(part, 4), matrix, row
                ].astype(f32)
                both = both.astype(low)
                g.quarter_out[slot, matrix, 0, row] = both[:, 0:quarter]
                g.quarter_out[slot, matrix, 1, row] = both[:, quarter:half]
            quarter_copy(part, matrix).start()

    def level_stage(part):
        slot = lax.rem(part, 2)

        if part >= 2:
            for step in range(1, levels):
                level_copy(part - 2, step).wait_send()

        for matrix in range(2):
            quarter_copy(part, matrix).wait_recv()
            for row in range(levels):
                both = g.quarter_out[slot, matrix, places_two[matrix], row].astype(
                    f32
                ) + g.quarter_got[slot, matrix, row].astype(f32)
                g.level_out[slot, row, matrix] = both.astype(low)
        for step in range(1, levels):
            level_copy(part, step).start()

    def last_stage(part):
        slot = lax.rem(part, 2)
        for step in range(1, levels):
            level_copy(part, step).wait_recv()
        for matrix in range(2):
            sums = g.level_out[slot, level, matrix].astype(f32)
            for step in range(1, levels):
                sums += g.level_got[lax.rem(part, 4), level_before(step), matrix].astype(f32)
            g.total[part, me_snap, matrix] = sums.astype(low)
        for step in range(1, snaps):
            last_copy(part, step).start()

    stages |= {HALF: half_stage, QUARTER: quarter_stage, LEVEL: level_stage, LAST: last_stage}

    def weight(part, matrix):
        return jnp.concatenate([g.all_w[part, matrix, place] for place in range(snaps)], axis=1)

    def add_products(part, rows):
        g.grid[rows, :] += dot_nt(g.act[rows, :], weight(part, 1))
        g.back[rows, :] += dot_nt(g.slope[rows, :], weight(part, 0))

    @pl.loop(0, parts)
    def _(part):
        def reach_in(point, also=True):
            for at_part in range(parts):
                if (point, at_part) in SCHEDULE:
                    pl.when((part == at_part) & also)(functools.partial(reach, (point, at_part)))

        def tile_rows(step):
            return pl.ds(pl.multiple_of(step * tile, tile), tile)

        fourth_copy(part).wait_recv()
        reach_in("k")
        g.grad_bias[part] = jnp.zeros(g.grad_bias.shape[1:], f32)

        @pl.loop(0, tokens // tile)
        def _(step):
            rows = tile_rows(step)
            act, slope = gelu_both(dot_nn(g.normed[rows, :], weight(part, 0)) + g.bias[part])
            g.act[rows, :] = act.astype(low)
            slope = (dot_nn(g.cot_in[rows, :], weight(part, 1)) * slope).astype(low)
            g.slope[rows, :] = slope
            g.grad_bias[part] += fold(slope.astype(f32))
            for at_step in range(tokens // tile):
                reach_in("k" + str(at_step), step == at_step)

        reach_in("l")

        @pl.when(part >= 1)
        def _():
            for matrix in range(2):
                core_copy(part - 1, matrix).wait_send()

        shape = g.grads.shape[1:]
        g.grads[0] = dot_nn(g.normed_turned[...], g.slope[...]).astype(low).reshape(shape)
        core_copy(part, 0).start()
        g.grads[1] = dot_nn(g.cot_turned[...], g.act[...]).astype(low).reshape(shape)
        core_copy(part, 1).start()
        reach_in("m")

        @pl.when(part < parts - 1)
        def _():
            @pl.loop(0, tokens // tile)
            def _(step):
                add_products(part, tile_rows(step))
                for at_step in range(tokens // tile):
                    reach_in("m" + str(at_step), step == at_step)

    g.folds[...] = jnp.zeros_like(g.folds)

    def second_back(rows):
        grad = g.back[rows, :]
        unit = g.unit_two[rows, :].astype(f32)
        cot = g.cot_in[rows, :].astype(f32)
        pulled = grad * g.gains[2:3, :]
        middle = jnp.mean(pulled, axis=-1, keepdims=True)
        slant = jnp.mean(pulled * unit, axis=-1, keepdims=True)
        total = cot + g.scale_two[rows, :] * (pulled - middle - unit * slant)
        g.back[rows, :] = total
        g.normed[rows, :] = total.astype(low)
        g.folds[2] += fold(grad * unit)
        g.folds[3] += fold(grad)
        g.folds[4] += fold(cot)

    loads["lon_it"].wait()
    for part in range(2):

        @pl.loop(0, half_tokens // short)
        def _(step, part=part):
            first_row = part * half_tokens + step * short
            add_products(parts - 1, pl.ds(pl.multiple_of(first_row, 16), short))

        reach("o" + str(part))
        half_strips(second_back, part)
        for step in range(1, group):
            block_copy(0, part, step).wait_send()
        to_blocks(g.lon_it_in[...], 1, part)
        reach("p" + str(part))
    reach("q")

    def low_out(rows):
        g.fields_in[rows, :] = g.grid[rows, :].astype(low)

    strips(low_out, after=lambda place: out_copy(place).start())
    reach("r")
    loads["valid"].wait()
    loads["turn"].wait()
    weigh = sum(
        dot_nn(g.valid_in[:, row, :].astype(f32).astype(low), g.turn_in[row])
        for row in range(g.valid.shape[1])
    )
    places_each = weigh.shape[1]
    precise = lax.Precision.HIGHEST
    sums = [jnp.zeros((1, 128), f32), jnp.zeros((1, 128), f32)]
    for snap in range(g.valid.shape[0]):
        variables = g.grid[snap * places_each : (snap + 1) * places_each, 0:128]
        for index, value in enumerate((variables, variables * variables)):
            sums[index] += jnp.dot(
                weigh[snap : snap + 1, :], value, precision=precise, preferred_element_type=f32
            )

    reach("s")

    def dot_tn(left, right):
        return lax.dot_general(
            left, right, (((0,), (0,)), ((), ())), preferred_element_type=f32
        )

    def filter_rows(first, grad):
        g.pair_grad[...] = grad
        real = g.pair_grad[0:128, 0:128] + g.pair_grad[128:256, 128:256]
        imag = g.pair_grad[0:128, 128:256] - g.pair_grad[128:256, 0:128]
        g.filt_out[me_snap, first] = real[0:owned].astype(low)
        g.filt_out[me_snap, first + 1] = imag[0:owned].astype(low)

    for part in range(2):
        take_blocks(1, part)
        reach("t" + str(part))
        rows = mode_half(part)
        spectra(g.grad_pre, f32, part)
        bend = jnp.tanh(g.pre_two[rows, :] / shrink_level)
        grad = (g.grad_pre[rows, :] * keep_half() * (bend * bend)).astype(low)
        g.grad_two[rows, :] = grad
        grad = dot_nt(grad, g.weight_two[...]) * gelu_both(g.pre_one[rows, :])[1]
        grad = grad.astype(low)
        g.grad_one[rows, :] = grad
        for step in range(1, group):
            row_copy(0, part, step).wait_send()
        to_rows(1, part, grids(dot_nt(grad, g.weight_one[...]).astype(low)))
        reach("u" + str(part))
    reach("v")
    bias_one = jnp.sum(g.grad_one[...].astype(f32), axis=0, keepdims=True)
    bias_two = jnp.sum(g.grad_two[...].astype(f32), axis=0, keepdims=True)
    filter_rows(2, dot_tn(g.act_one[...], g.grad_two[...]))
    filter_rows(0, dot_tn(g.spectrum[...], g.grad_one[...]))

    def filter_copy(step):
        view = g.filt_out.at[me_snap]
        return send(view, view, (g.filt_s, g.filt_r), step, at(snap_after(step), me_sp))

    for step in range(1, snaps):
        filter_copy(step).start()


    reach("w")

    loads["lon_ft"].wait()

    def first_back(rows):
        grad = g.grid[rows, :]
        unit = g.unit_one[rows, :].astype(f32)
        pulled = grad * g.gains[0:1, :]
        middle = jnp.mean(pulled, axis=-1, keepdims=True)
        slant = jnp.mean(pulled * unit, axis=-1, keepdims=True)
        g.grid[rows, :] = g.back[rows, :] + g.scale_one[rows, :] * (
            pulled - middle - unit * slant
        )
        g.folds[0] += fold(grad * unit)
        g.folds[1] += fold(grad)

    for part in range(2):
        home_modes(1, part)
        reach("x" + str(part))
        g.grid[half_rows(part), :] = g.back[half_rows(part), :] + dot_nn(
            g.lon_ft_in[...], g.home_low[part]
        )
        half_strips(first_back, part, after=lambda place: grad_copy(place).start())
        reach("y" + str(part))

    g.grad_rows[...] = jnp.zeros_like(g.grad_rows)
    for index, row in enumerate((0, 1, 2, 3, 8)):
        g.grad_rows[row : row + 1, :] = jnp.sum(g.folds[index], axis=0, keepdims=True)
    flat = jnp.concatenate(
        [jnp.sum(g.grad_bias[part], axis=0, keepdims=True) for part in range(parts)], axis=1
    )
    for row in range(rows_small - 9):
        g.grad_rows[9 + row : 10 + row, :] = flat[:, row * channel : (row + 1) * channel]
    for block in range(group):
        g.tiles[block] = jnp.zeros(g.tiles.shape[1:], f32)
        g.tiles[block, :, 0:owned] = g.grad_rows[:, block * owned : (block + 1) * owned]
        g.tiles[block, 13:14, :] = sums[0]
        g.tiles[block, 14:15, :] = sums[1]

    def tile_copy(step):
        target = sp_after(step)
        return send(
            g.tiles.at[target], g.tiles_got.at[me_sp], (g.tile_s, g.tile_r), step, at(me_snap, target)
        )

    def snap_tile_copy(step):
        view = g.snap_tiles.at[me_snap]
        return send(view, view, (g.snap_tile_s, g.snap_tile_r), step, at(snap_after(step), me_sp))

    for step in range(1, group):
        tile_copy(step).start()
    reach("z")

    g.tiles_got[me_sp] = g.tiles[me_sp]
    for step in range(1, group):
        tile_copy(step).wait_recv()
    tile_sum = g.tiles_got[0]
    for sp in range(1, group):
        tile_sum += g.tiles_got[sp]
    g.snap_tiles[me_snap] = tile_sum
    g.snap_tiles[me_snap, 4:5, :] = bias_one[:, 0:128]
    g.snap_tiles[me_snap, 5:6, :] = bias_one[:, 128:256]
    g.snap_tiles[me_snap, 6:7, :] = bias_two[:, 0:128]
    g.snap_tiles[me_snap, 7:8, :] = bias_two[:, 128:256]
    for step in range(1, snaps):
        snap_tile_copy(step).start()

    for step in range(1, snaps):
        filter_copy(step).wait_recv()
    filter_sum = g.filt_out[0].astype(f32)
    for snap in range(1, snaps):
        filter_sum += g.filt_out[snap].astype(f32)
    g.grad_filt[...] = filter_sum
    for part in range(parts):
        for step in range(1, snaps):
            last_copy(part, step).wait_recv()
    grads_out = pltpu.make_async_copy(g.total, g.grad_mlp, g.load_sem.at[3])
    grads_out.start()
    for step in range(1, snaps):
        snap_tile_copy(step).wait_recv()
    tile_sum = g.snap_tiles[0]
    for snap in range(1, snaps):
        tile_sum += g.snap_tiles[snap]
    g.grad_small[...] = tile_sum

    grads_out.wait()
    for place in range(tokens // strip):
        out_copy(place).wait()
        grad_copy(place).wait()
    for step in range(1, group):
        small_copy(step).wait_send()
        for part in range(2):
            block_copy(1, part, step).wait_send()
            row_copy(1, part, step).wait_send()
        tile_copy(step).wait_send()
        for part in range(parts):
            first_copy(part, step).wait_send()
    for part in range(parts):
        if part < parts - 1:
            second_copy(part).wait_send()
            third_copy(part).wait_send()
        fourth_copy(part).wait_send()
    for matrix in range(2):
        core_copy(parts - 1, matrix).wait_send()
    for part in (parts - 2, parts - 1):
        for matrix in range(2):
            half_copy(part, matrix).wait_send()
            quarter_copy(part, matrix).wait_send()
        for step in range(1, levels):
            level_copy(part, step).wait_send()
    for step in range(1, snaps):
        filter_copy(step).wait_send()
        snap_tile_copy(step).wait_send()
        for part in range(parts):
            last_copy(part, step).wait_send()


def block_pass(fields, cot, valid, kept, mlp, filt, small, snaps, group):
    snap_local, row_local, lon_total, channel = fields.shape
    tokens = snap_local * row_local * lon_total
    hidden = mlp.shape[2]
    lat_total = row_local * group
    modes = kept.shape[1] * group
    owned = channel // group
    width = 512
    parts = hidden // width
    levels = group // 2
    quarter = width // snaps
    low, f32 = jnp.bfloat16, jnp.float32
    half = width // 2
    half_snaps = snap_local // 2
    lon_f, lon_i = lon_matrix(lon_total, modes, half_snaps, row_local)

    def paired(array):
        return jnp.transpose(array, (0, 2, 1, 3)).reshape(-1, row_local, channel)

    lat_f = lat_matrix(lat_total, modes)
    pair = 2 * modes * row_local
    spread = half_snaps * row_local * 2 * modes
    inputs = dict(
        small=small,
        kept=kept.T,
        fields=paired(fields),
        lon_f=jnp.asarray(np.ascontiguousarray(lon_f.T)),
        filt=filt,
        lat_f=jnp.asarray(lat_f),
        lat_b=jnp.asarray(np.ascontiguousarray(lat_f.T)),
        cot=paired(cot),
        lon_i=jnp.asarray(lon_i),
        valid=valid,
        turn=jnp.asarray(lon_turn(lon_total, row_local)),
        lon_it=jnp.asarray(np.ascontiguousarray(lon_i.T)),
        lon_ft=jnp.asarray(lon_f),
        mlp=mlp,
    )
    outputs = dict(
        out=jax.ShapeDtypeStruct((tokens // row_local, row_local, channel), low),
        in_grad=jax.ShapeDtypeStruct((tokens // row_local, row_local, channel), f32),
        grad_mlp=jax.ShapeDtypeStruct((parts, snaps, 2, owned, quarter), low),
        grad_filt=jax.ShapeDtypeStruct((4, owned, 128), f32),
        grad_small=jax.ShapeDtypeStruct((16, 128), f32),
    )
    vmem = pltpu.VMEM
    dma = pltpu.SemaphoreType.DMA
    scratch = {
        name + "_in": vmem(value.shape, value.dtype)
        for name, value in inputs.items()
        if name not in ("mlp", "fields", "cot")
    }
    strip = divisor(tokens // 2, 48, 144)
    scratch |= dict(
        mlp_part=vmem((2, 2, owned, width), f32),
        fields_in=vmem((tokens, channel), low),
        fields_sem=dma((tokens // strip,)),
        cot_sem=dma((tokens // strip,)),
        cot_in=vmem((tokens, channel), low),
        grid=vmem((tokens, channel), f32),
        back=vmem((tokens, channel), f32),
        normed=vmem((tokens, channel), low),
        normed_turned=vmem((channel, tokens), low),
        cot_turned=vmem((channel, tokens), low),
        unit_one=vmem((tokens, channel), low),
        unit_two=vmem((tokens, channel), low),
        scale_one=vmem((tokens, 1), f32),
        scale_two=vmem((tokens, 1), f32),
        own_small=vmem((16 + kept.shape[0], 128), f32),
        all_small=vmem((group, 16 + kept.shape[0], 128), f32),
        gains=vmem((16, channel), f32),
        keep=vmem((lat_total * modes, 128), f32),
        own_w=vmem((parts, 2, snaps, owned, quarter), low),
        all_w=vmem((parts, 2, snaps, channel, quarter), low),
        modes=vmem((2, group, half_snaps * pair * 3 // 4, 128), low),
        modes_got=vmem((2, group, half_snaps * pair * 3 // 4, 128), low),
        rows_out=vmem((2, group, half_snaps * pair * 3 // 4, 128), low),
        rows_got=vmem((2, group, half_snaps * pair * 3 // 4, 128), low),
        arrived=vmem((snap_local, pair * group, 128), low),
        gathered=vmem((2, spread, channel), f32),
        home_low=vmem((2, spread, channel), low),
        weight_one=vmem((256, 256), low),
        weight_two=vmem((256, 256), low),
        spectrum=vmem((snap_local * lat_total * modes, 256), low),
        pre_one=vmem((snap_local * lat_total * modes, 256), f32),
        act_one=vmem((snap_local * lat_total * modes, 256), low),
        pre_two=vmem((snap_local * lat_total * modes, 256), f32),
        grad_pre=vmem((snap_local * lat_total * modes, 256), f32),
        grad_two=vmem((snap_local * lat_total * modes, 256), low),
        grad_one=vmem((snap_local * lat_total * modes, 256), low),
        folds=vmem((5, 8, channel), f32),
        pair_grad=vmem((256, 256), f32),
        act=vmem((tokens, width), low),
        slope=vmem((tokens, width), low),
        bias=vmem((parts, 1, width), f32),
        grad_bias=vmem((parts, 8, width), f32),
        grad_rows=vmem((16, channel), f32),
        grads=vmem((2, levels, 2, owned, width), low),
        core_got=vmem((2, 2, levels, owned, width), low),
        half_out=vmem((2, 2, 2, levels, owned, half), low),
        half_got=vmem((4, 2, levels, owned, half), low),
        quarter_out=vmem((2, 2, 2, levels, owned, quarter), low),
        quarter_got=vmem((2, 2, levels, owned, quarter), low),
        level_out=vmem((2, levels, 2, owned, quarter), low),
        level_got=vmem((4, levels, 2, owned, quarter), low),
        total=vmem((parts, snaps, 2, owned, quarter), low),
        filt_out=vmem((snaps, 4, owned, 128), low),
        tiles=vmem((group, 16, 128), f32),
        tiles_got=vmem((group, 16, 128), f32),
        snap_tiles=vmem((snaps, 16, 128), f32),
        load_sem=dma((len(inputs) + 1,)),
    )
    for name, shape in dict(
        small=(group,),
        first=(parts, group),
        second=(parts,),
        third=(parts,),
        fourth=(parts,),
        block=(2, 2, group),
        row=(2, 2, group),
        core=(2, 2),
        half=(4, 2),
        quarter=(2, 2),
        level=(4, levels),
        last=(parts, snaps),
        filt=(snaps,),
        tile=(group,),
        snap_tile=(snaps,),
    ).items():
        scratch[name + "_s"] = dma(shape)
        scratch[name + "_r"] = dma(shape)
    names = [*inputs, *outputs, *scratch]
    far = pl.BlockSpec(memory_space=pl.ANY)
    near = pl.BlockSpec(memory_space=pltpu.VMEM)
    results = pl.pallas_call(
        functools.partial(block_body, names, (snaps, group, parts, width)),
        in_specs=[far] * len(inputs),
        out_specs=[far, far, far, near, near],
        out_shape=list(outputs.values()),
        scratch_shapes=list(scratch.values()),
        compiler_params=pltpu.CompilerParams(
            collective_id=0, has_side_effects=True, vmem_limit_bytes=VMEM_LIMIT
        ),
        cost_estimate=pl.CostEstimate(
            flops=12 * tokens * channel * hidden,
            bytes_accessed=4 * hidden * channel,
            transcendentals=tokens * hidden,
        ),
        name="block_pass",
    )(*inputs.values())
    return results


def step_body(names, positions, *refs):
    g = Refs()
    for name, ref in zip(names, refs, strict=True):
        setattr(g, name, ref)
    parts, snaps = g.grad_mlp.shape[:2]
    quarter = g.grad_mlp.shape[4]
    width = snaps * quarter
    moments = ("w", "m", "v")
    results = ("new", "first", "second", "copy")

    pieces = g.far_sem.shape[2]
    ends = ((g.out, g.out_near, g.out_o), (g.in_grad, g.in_grad_near, g.in_grad_o))

    def passing(kind, piece, leg):
        size = ends[kind][0].shape[0] // pieces
        rows = pl.ds(piece * size, size)
        return pltpu.make_async_copy(
            ends[kind][leg].at[rows], ends[kind][leg + 1].at[rows], g.far_sem.at[leg, kind, piece]
        )

    through = [(kind, piece) for kind in range(2) for piece in range(pieces)]

    def part_cols(part):
        return pl.ds(part * width, width)

    def load(part, matrix):
        near = [
            pltpu.make_async_copy(
                getattr(g, "mlp_" + kind).at[matrix, :, part_cols(part)],
                g.near.at[index, part, matrix],
                g.near_sem.at[index, part, matrix],
            )
            for index, kind in enumerate(moments)
        ]
        near.append(
            pltpu.make_async_copy(
                g.grad_mlp.at[part, :, matrix],
                g.grad_near.at[part, matrix],
                g.near_sem.at[3, part, matrix],
            )
        )
        return near

    def store(part, matrix):
        copies = [
            pltpu.make_async_copy(
                g.near.at[index, part, matrix],
                getattr(g, "mlp_" + kind).at[matrix, :, part_cols(part)],
                g.back_sem.at[index, part, matrix],
            )
            for index, kind in enumerate(results[:3])
        ]
        copies.append(
            pltpu.make_async_copy(
                g.low_near.at[part, matrix],
                g.mlp_copy.at[matrix, :, part_cols(part)],
                g.back_sem.at[3, part, matrix],
            )
        )
        return copies

    units = [(part, matrix) for part in range(parts) for matrix in range(2)]
    ahead = 4
    shares = [through[index :: len(units)] for index in range(len(units))]

    def start_unit(index):
        if index < len(units):
            for copy in load(*units[index]):
                copy.start()
            for each in shares[index]:
                passing(*each, 0).start()

    for index in range(ahead):
        start_unit(index)

    def put(prefix, values):
        for kind, value in zip(results, values, strict=True):
            getattr(g, prefix + kind)[...] = value

    owned = g.filt_w.shape[2]
    put(
        "filt_",
        adamw(g.filt_w[...], g.filt_m[...], g.filt_v[...], g.grad_filt[:, :, 0:owned], rate_filter),
    )
    rows = g.small_w.shape[0]
    put(
        "small_",
        adamw(
            g.small_w[...], g.small_m[...], g.small_v[...], g.grad_small[0:rows, 0:owned], rate_small
        ),
    )
    totals = g.grad_small[rows : rows + 2, 0 : g.run.shape[1]]
    g.stats[...] = stat_decay * g.run[...] + (1.0 - stat_decay) * totals / positions

    for index, (part, matrix) in enumerate(units):
        for copy in load(part, matrix):
            copy.wait()
        start_unit(index + ahead)
        for snap in range(snaps):
            place = snap if matrix else 2 * (snap % 2) + snap // 2
            where = (part, matrix, slice(None), slice(place * quarter, (place + 1) * quarter))
            now = [g.near[(kind, *where)] for kind in range(3)]
            grad = g.grad_near[part, matrix, snap].astype(jnp.float32)
            values = adamw(*now, grad, rate_mlp)
            for kind in range(3):
                g.near[(kind, *where)] = values[kind]
            g.low_near[where] = values[3]
        for copy in store(part, matrix):
            copy.start()
        for each in shares[index]:
            passing(*each, 0).wait()
            passing(*each, 1).start()
    for each in through:
        passing(*each, 1).wait()
    for unit in units:
        for copy in store(*unit):
            copy.wait()


def step_pass(shown, grads, masters, run_stats, positions):
    grad_mlp, grad_filt, grad_small = grads
    mlp, filt, small = masters
    parts = grad_mlp.shape[0]
    width = mlp[0].shape[2] // parts
    f32, low = jnp.float32, jnp.bfloat16
    far = pl.BlockSpec(memory_space=pltpu.HBM)
    near = pl.BlockSpec(memory_space=pltpu.VMEM)
    inputs = dict(out=shown[0], in_grad=shown[1], grad_mlp=grad_mlp)
    inputs |= dict(zip(("mlp_w", "mlp_m", "mlp_v"), mlp, strict=True))
    far_in = len(inputs)
    inputs |= dict(grad_filt=grad_filt, grad_small=grad_small)
    inputs |= dict(zip(("filt_w", "filt_m", "filt_v"), filt, strict=True))
    inputs |= dict(zip(("small_w", "small_m", "small_v"), small, strict=True))
    inputs |= dict(run=run_stats)
    results = (("new", f32), ("first", f32), ("second", f32), ("copy", low))
    outputs = {
        name + "_o": jax.ShapeDtypeStruct(array.shape, array.dtype)
        for name, array in zip(("out", "in_grad"), shown, strict=True)
    }
    outputs |= {"mlp_" + kind: jax.ShapeDtypeStruct(mlp[0].shape, dt) for kind, dt in results}
    far_out = len(outputs)
    outputs |= {"filt_" + kind: jax.ShapeDtypeStruct(filt[0].shape, dt) for kind, dt in results}
    outputs |= {"small_" + kind: jax.ShapeDtypeStruct(small[0].shape, dt) for kind, dt in results}
    outputs |= dict(stats=jax.ShapeDtypeStruct(run_stats.shape, f32))
    scratch = dict(
        near=pltpu.VMEM((3, parts, 2, mlp[0].shape[1], width), f32),
        grad_near=pltpu.VMEM((parts, 2, *grad_mlp.shape[1:2], *grad_mlp.shape[3:]), low),
        low_near=pltpu.VMEM((parts, 2, mlp[0].shape[1], width), low),
        near_sem=pltpu.SemaphoreType.DMA((4, parts, 2)),
        back_sem=pltpu.SemaphoreType.DMA((4, parts, 2)),
        out_near=pltpu.VMEM(shown[0].shape, low),
        in_grad_near=pltpu.VMEM(shown[1].shape, f32),
        far_sem=pltpu.SemaphoreType.DMA((2, 2, divisor(shown[0].shape[0], 1, 6))),
    )
    return pl.pallas_call(
        functools.partial(step_body, [*inputs, *outputs, *scratch], positions),
        in_specs=[far] * far_in + [near] * (len(inputs) - far_in),
        out_specs=[far] * far_out + [near] * (len(outputs) - far_out),
        out_shape=list(outputs.values()),
        scratch_shapes=list(scratch.values()),
        compiler_params=pltpu.CompilerParams(vmem_limit_bytes=VMEM_LIMIT),
        name="step_pass",
    )(*inputs.values())


def per_device_blocks(
    fields,
    cotangent,
    valid_mask,
    kept_modes,
    mlp_master,
    mlp_first,
    mlp_second,
    filter_master,
    filter_first,
    filter_second,
    small_master,
    small_first,
    small_second,
    run_stats,
):
    snaps, group = lax.axis_size("snap"), lax.axis_size("sp")
    out, in_grad, *grads = block_pass(
        fields, cotangent, valid_mask, kept_modes, mlp_master, filter_master, small_master, snaps, group
    )
    snap_local, row_local, lon_total, channel = fields.shape
    positions = snap_local * snaps * row_local * group * lon_total
    out, in_grad, *stepped = step_pass(
        (out, in_grad),
        grads,
        (
            (mlp_master, mlp_first, mlp_second),
            (filter_master, filter_first, filter_second),
            (small_master, small_first, small_second),
        ),
        run_stats,
        positions,
    )
    rows_apart = (snap_local, lon_total, row_local, channel)
    out, in_grad = [
        jnp.transpose(array.reshape(rows_apart), (0, 2, 1, 3)) for array in (out, in_grad)
    ]
    return (out, in_grad, *stepped)


def per_device(*arrays):
    group, snaps = lax.axis_size("sp"), lax.axis_size("snap")
    channel, hidden = arrays[0].shape[3], arrays[4].shape[2]
    by_block = group == BLOCKS and snaps == 4 and arrays[3].shape[1] == 1
    if by_block and hidden == 6 * 512 and channel // group <= 128 and channel % (16 * group) == 0:
        return per_device_blocks(*arrays)
    return per_device_modes(*arrays)


def solution(mesh):
    return jax.shard_map(
        per_device,
        mesh=mesh,
        in_specs=(
            P("snap", "sp", None, None),
            P("snap", "sp", None, None),
            P("snap", "sp", None),
            P(None, "sp"),
            P(None, "sp", None),
            P(None, "sp", None),
            P(None, "sp", None),
            P(None, "sp", None),
            P(None, "sp", None),
            P(None, "sp", None),
            P(None, "sp"),
            P(None, "sp"),
            P(None, "sp"),
            P(),
        ),
        out_specs=(
            P("snap", "sp", None, None),
            P("snap", "sp", None, None),
            P(None, "sp", None),
            P(None, "sp", None),
            P(None, "sp", None),
            P(None, "sp", None),
            P(None, "sp", None),
            P(None, "sp", None),
            P(None, "sp", None),
            P(None, "sp", None),
            P(None, "sp"),
            P(None, "sp"),
            P(None, "sp"),
            P(None, "sp"),
            P(),
        ),
        check_vma=False,
    )
```

```python
import functools
import math

import jax
import jax.numpy as jnp
import ml_dtypes
import numpy as np
from jax import lax
from jax.experimental import pallas as pl
from jax.experimental.pallas import tpu as pltpu
from jax.sharding import PartitionSpec as P

BLOCKS = 8
NVAR = 20
STEP = 10
VMEM_LIMIT = 63 * 1024 * 1024


eps_norm = 1e-06
shrink_level = 0.01
beta_one = 0.5
beta_two = 0.5
adam_eps = 1e-08
decay_rate = 0.01
rate_mlp = 0.03
rate_filter = 0.1
rate_small = 0.2
stat_decay = 0.5


def layer_norm(values, gain_vec, shift_vec):
    centred = values - jnp.mean(values, axis=-1, keepdims=True)
    spread = jnp.mean(centred * centred, axis=-1, keepdims=True)
    return centred * lax.rsqrt(spread + eps_norm) * gain_vec + shift_vec


def shrink(values):
    return values - shrink_level * jnp.tanh(values / shrink_level)


def lon_tables(lon_total, mode_total):
    places = jnp.arange(lon_total, dtype=jnp.int32)
    orders = jnp.arange(mode_total, dtype=jnp.int32)
    angles = (places[:, None] * orders[None, :] % lon_total).astype(jnp.float32) * (
        2.0 * math.pi / lon_total
    )
    scaling = 1.0 / math.sqrt(lon_total)
    forward_tab = jnp.stack([jnp.cos(angles), -jnp.sin(angles)], axis=1) * scaling
    doubling = jnp.where(orders == 0, 1.0, 2.0).astype(jnp.float32)[:, None]
    inverse_tab = (
        jnp.stack([jnp.cos(angles).T * doubling, -jnp.sin(angles).T * doubling], axis=0) * scaling
    )
    return (forward_tab.astype(jnp.bfloat16), inverse_tab.astype(jnp.bfloat16))


def lat_table(lat_total):
    places = jnp.arange(lat_total, dtype=jnp.int32)
    angles = (places[:, None] * places[None, :] % lat_total).astype(jnp.float32) * (
        2.0 * math.pi / lat_total
    )
    cosine = jnp.cos(angles)
    sine_part = jnp.sin(angles)
    upper_rows = jnp.stack([cosine, sine_part], axis=1)
    bottom = jnp.stack([-sine_part, cosine], axis=1)
    return (jnp.stack([upper_rows, bottom], axis=0) / math.sqrt(lat_total)).astype(jnp.bfloat16)


def complex_pair(real_part, imag_part):
    return jnp.stack([jnp.stack([real_part, -imag_part]), jnp.stack([imag_part, real_part])])


gelu_scale = math.sqrt(2.0 / math.pi)
gelu_cubic = 0.044715


def gelu_both(value):
    bend = (gelu_scale * gelu_cubic) * (value * value)
    turn = jnp.tanh(value * (gelu_scale + bend))
    half = 0.5 + 0.5 * turn
    slope = half * (1.0 + (value * (1.0 - turn)) * (gelu_scale + 3.0 * bend))
    return value * half, slope


def dot_nt(left, right):
    return lax.dot_general(
        left, right, (((1,), (1,)), ((), ())), preferred_element_type=jnp.float32
    )


def dot_nn(left, right):
    return jnp.dot(left, right, preferred_element_type=jnp.float32)


def divisor(total, unit, most):
    return max(size for size in range(unit, most + 1, unit) if total % size == 0)


def mlp_body(
    tile,
    normed_ref,
    cot_ref,
    up_ref,
    down_ref,
    bias_ref,
    out_ref,
    back_ref,
    grad_up_ref,
    grad_down_ref,
    grad_bias_ref,
    normed_turned,
    cot_turned,
    act_ref,
    slope_ref,
):
    tokens = normed_ref.shape[0]

    @pl.when(pl.program_id(0) == 0)
    def _():
        normed_turned[...] = normed_ref[...].T
        cot_turned[...] = cot_ref[...].T
        out_ref[...] = jnp.zeros_like(out_ref)
        back_ref[...] = jnp.zeros_like(back_ref)

    grad_bias_ref[...] = jnp.zeros_like(grad_bias_ref)

    @pl.loop(0, tokens // tile)
    def _(step):
        rows = pl.ds(pl.multiple_of(step * tile, tile), tile)
        act, slope = gelu_both(dot_nn(normed_ref[rows, :], up_ref[...]) + bias_ref[...])
        act = act.astype(jnp.bfloat16)
        slope = (dot_nn(cot_ref[rows, :], down_ref[...]) * slope).astype(jnp.bfloat16)
        act_ref[rows, :] = act
        slope_ref[rows, :] = slope
        grad_bias_ref[...] += jnp.sum(slope.astype(jnp.float32), axis=0, keepdims=True)
        out_ref[rows, :] += dot_nt(act, down_ref[...])
        back_ref[rows, :] += dot_nt(slope, up_ref[...])

    grad_up_ref[...] = dot_nn(normed_turned[...], slope_ref[...]).astype(grad_up_ref.dtype)
    grad_down_ref[...] = dot_nn(cot_turned[...], act_ref[...]).astype(grad_down_ref.dtype)


def mlp_pass(normed, cot, weights, bias):
    tokens, channel = normed.shape
    hidden = weights.shape[2]
    width = divisor(hidden, 128, 512)
    tile = divisor(tokens, 16, 480)
    whole = pl.BlockSpec((tokens, channel), lambda j: (0, 0))
    block = pl.BlockSpec((channel, width), lambda j: (0, j))
    line = pl.BlockSpec((1, width), lambda j: (0, j))
    part = lambda which: pl.BlockSpec((None, channel, width), lambda j: (which, 0, j))
    total = jax.ShapeDtypeStruct((tokens, channel), jnp.float32)
    grads = jax.ShapeDtypeStruct((channel, hidden), jnp.bfloat16)
    return pl.pallas_call(
        functools.partial(mlp_body, tile),
        grid=(hidden // width,),
        in_specs=[whole, whole, part(0), part(1), line],
        out_specs=[whole, whole, block, block, line],
        out_shape=[total, total, grads, grads, jax.ShapeDtypeStruct((1, hidden), jnp.float32)],
        scratch_shapes=[
            pltpu.VMEM((channel, tokens), jnp.bfloat16),
            pltpu.VMEM((channel, tokens), jnp.bfloat16),
            pltpu.VMEM((tokens, width), jnp.bfloat16),
            pltpu.VMEM((tokens, width), jnp.bfloat16),
        ],
        compiler_params=pltpu.CompilerParams(vmem_limit_bytes=56 * 1024 * 1024),
        cost_estimate=pl.CostEstimate(
            flops=12 * tokens * channel * hidden,
            bytes_accessed=8 * channel * hidden + 12 * tokens * channel,
            transcendentals=tokens * hidden,
        ),
        name="mlp_pass",
    )(normed, cot, weights, weights, bias)


def spectral_front(arrived, lat_fwd, first_pair, second_pair, bias_one, bias_two):
    spectrum = jnp.einsum(
        "pkqr,nrqmd->nkpmd", lat_fwd, arrived, preferred_element_type=jnp.float32
    ).astype(jnp.bfloat16)
    snap_local, lat_total, pair_count, mode_local, channel = spectrum.shape
    blocked = spectrum.reshape(
        snap_local, lat_total, pair_count, mode_local, BLOCKS, channel // BLOCKS
    )
    pre_one = (
        jnp.einsum("nkqmbi,pqbio->nkpmbo", blocked, first_pair, preferred_element_type=jnp.float32)
        + bias_one
    )
    act_one = jax.nn.gelu(pre_one).astype(jnp.bfloat16)
    pre_two = (
        jnp.einsum("nkqmbi,pqbio->nkpmbo", act_one, second_pair, preferred_element_type=jnp.float32)
        + bias_two
    )
    return (blocked, pre_one, act_one, pre_two)


def adamw(master, first_mom, second_mom, gradient, step_rate):
    first_next = beta_one * first_mom + (1.0 - beta_one) * gradient
    second_next = beta_two * second_mom + (1.0 - beta_two) * gradient * gradient
    fix_one = 1.0 / (1.0 - beta_one**STEP)
    fix_two = 1.0 / (1.0 - beta_two**STEP)
    direction = first_next * fix_one / (jnp.sqrt(second_next * fix_two) + adam_eps)
    master_next = master - step_rate * (direction + decay_rate * master)
    return (master_next, first_next, second_next, master_next.astype(jnp.bfloat16))


def per_device_modes(
    fields,
    cotangent,
    valid_mask,
    kept_modes,
    mlp_master,
    mlp_first,
    mlp_second,
    filter_master,
    filter_first,
    filter_second,
    small_master,
    small_first,
    small_second,
    run_stats,
):
    group_size = lax.axis_size("sp")
    snap_local, row_local, lon_total, channel = fields.shape
    lat_total = row_local * group_size
    mode_local = kept_modes.shape[1]
    mode_total = mode_local * group_size
    block_width = channel // BLOCKS
    lon_fwd, lon_inv = lon_tables(lon_total, mode_total)
    lat_fwd = lat_table(lat_total)
    mlp_w, filt_w, small_w = (
        lax.all_gather(mlp_master.astype(jnp.bfloat16), "sp", axis=1, tiled=True),
        lax.all_gather(filter_master.astype(jnp.bfloat16), "sp", axis=1, tiled=True),
        lax.all_gather(small_master.astype(jnp.bfloat16), "sp", axis=1, tiled=True),
    )
    small_f = small_w.astype(jnp.float32)
    weights = filt_w.reshape(4, BLOCKS, block_width, block_width)
    first_pair = complex_pair(weights[0], weights[1])
    second_pair = complex_pair(weights[2], weights[3])
    bias_one = small_f[4:6].reshape(2, 1, BLOCKS, block_width)
    bias_two = small_f[6:8].reshape(2, 1, BLOCKS, block_width)
    fields_float = fields.astype(jnp.float32)
    normed, norm_pull = jax.vjp(layer_norm, fields_float, small_f[0], small_f[1])
    normed_low = normed.astype(jnp.bfloat16)
    spec_lon = jnp.einsum(
        "nrld,lqm->nrqmd", normed_low, lon_fwd, preferred_element_type=jnp.float32
    ).astype(jnp.bfloat16)
    arrived = lax.all_to_all(spec_lon, "sp", split_axis=3, concat_axis=1, tiled=True)
    spectral = spectral_front(arrived, lat_fwd, first_pair, second_pair, bias_one, bias_two)
    keep_mask = kept_modes.astype(jnp.float32)[None, :, None, :, None, None]
    masked = (shrink(spectral[3]) * keep_mask).astype(jnp.bfloat16)
    masked = masked.reshape(snap_local, lat_total, 2, mode_local, channel)
    returned = jnp.einsum(
        "pkqr,nkpmd->nrqmd", lat_fwd, masked, preferred_element_type=jnp.float32
    ).astype(jnp.bfloat16)
    home_modes = lax.all_to_all(returned, "sp", split_axis=1, concat_axis=3, tiled=True)
    filtered = jnp.einsum(
        "nrqmd,qml->nrld", home_modes, lon_inv, preferred_element_type=jnp.float32
    )
    mixture = fields_float + normed + filtered
    normed_two, norm_two_pull = jax.vjp(layer_norm, mixture, small_f[2], small_f[3])
    normed_two_low = normed_two.astype(jnp.bfloat16)
    tokens = snap_local * row_local * lon_total
    passed = mlp_pass(
        normed_two_low.reshape(tokens, channel),
        cotangent.reshape(tokens, channel),
        mlp_w,
        small_f[9:].reshape(1, -1),
    )
    output = mixture + passed[0].reshape(mixture.shape) + small_f[8]
    weight_mask = valid_mask.astype(jnp.float32)[..., None]
    variables = output[..., :NVAR]
    local_sums = jnp.stack(
        [
            jnp.sum(weight_mask * variables, axis=(0, 1, 2)),
            jnp.sum(weight_mask * variables * variables, axis=(0, 1, 2)),
        ]
    )
    total_sums = lax.psum(local_sums, ("snap", "sp"))
    positions = snap_local * lax.axis_size("snap") * lat_total * lon_total
    stats_new = stat_decay * run_stats + (1.0 - stat_decay) * total_sums / positions
    cot_float = cotangent.astype(jnp.float32)
    grad_normed_two = passed[1].reshape(mixture.shape)
    grad_bias_hidden = passed[4]
    grad_mix_norm, grad_gain_two, grad_shift_two = norm_two_pull(grad_normed_two)
    grad_mixture = cot_float + grad_mix_norm
    grad_bias_out = jnp.sum(cot_float, axis=(0, 1, 2))
    grad_filtered = grad_mixture.astype(jnp.bfloat16)
    grad_home = jnp.einsum(
        "nrld,qml->nrqmd", grad_filtered, lon_inv, preferred_element_type=jnp.float32
    ).astype(jnp.bfloat16)
    grad_returned = lax.all_to_all(grad_home, "sp", split_axis=3, concat_axis=1, tiled=True)
    grad_masked = jnp.einsum(
        "pkqr,nrqmd->nkpmd", lat_fwd, grad_returned, preferred_element_type=jnp.float32
    )
    arrived_again = lax.all_to_all(spec_lon, "sp", split_axis=3, concat_axis=1, tiled=True)
    used_front = spectral_front(arrived_again, lat_fwd, first_pair, second_pair, bias_one, bias_two)
    blocked, pre_one, act_one, pre_two = used_front
    grad_two = jax.vjp(shrink, pre_two)[1](grad_masked.reshape(pre_two.shape) * keep_mask)[
        0
    ].astype(jnp.bfloat16)
    grad_bias_two = jnp.sum(grad_two.astype(jnp.float32), axis=(0, 1, 3))
    grad_second = jnp.einsum(
        "nkqmbi,nkpmbo->pqbio", act_one, grad_two, preferred_element_type=jnp.float32
    )
    grad_act = jnp.einsum(
        "nkpmbo,pqbio->nkqmbi", grad_two, second_pair, preferred_element_type=jnp.float32
    )
    grad_one = jax.vjp(jax.nn.gelu, pre_one)[1](grad_act)[0].astype(jnp.bfloat16)
    grad_bias_one = jnp.sum(grad_one.astype(jnp.float32), axis=(0, 1, 3))
    grad_first = jnp.einsum(
        "nkqmbi,nkpmbo->pqbio", blocked, grad_one, preferred_element_type=jnp.float32
    )
    grad_spectrum = jnp.einsum(
        "nkpmbo,pqbio->nkqmbi", grad_one, first_pair, preferred_element_type=jnp.float32
    ).astype(jnp.bfloat16)
    grad_spectrum = grad_spectrum.reshape(snap_local, lat_total, 2, mode_local, channel)
    grad_lon = jnp.einsum(
        "pkqr,nkpmd->nrqmd", lat_fwd, grad_spectrum, preferred_element_type=jnp.float32
    ).astype(jnp.bfloat16)
    grad_rows = lax.all_to_all(grad_lon, "sp", split_axis=1, concat_axis=3, tiled=True)
    grad_normed = grad_mixture + jnp.einsum(
        "nrqmd,lqm->nrld", grad_rows, lon_fwd, preferred_element_type=jnp.float32
    )
    grad_field_norm, grad_gain_one, grad_shift_one = norm_pull(grad_normed)
    input_grad = grad_mixture + grad_field_norm
    grad_filter = jnp.stack(
        [
            grad_first[0, 0] + grad_first[1, 1],
            grad_first[1, 0] - grad_first[0, 1],
            grad_second[0, 0] + grad_second[1, 1],
            grad_second[1, 0] - grad_second[0, 1],
        ]
    ).reshape(4, channel, block_width)
    grad_small = jnp.concatenate(
        [
            jnp.stack([grad_gain_one, grad_shift_one, grad_gain_two, grad_shift_two]),
            grad_bias_one.reshape(2, channel),
            grad_bias_two.reshape(2, channel),
            grad_bias_out[None, :],
            grad_bias_hidden.reshape(-1, channel),
        ],
        axis=0,
    )
    shares = (
        jnp.stack([
            lax.psum_scatter(part, "sp", scatter_dimension=0, tiled=True) for part in passed[2:4]
        ]),
        lax.psum_scatter(grad_filter, "sp", scatter_dimension=1, tiled=True),
        lax.psum_scatter(grad_small, "sp", scatter_dimension=1, tiled=True),
    )
    owned = (
        lax.psum(shares[0].astype(jnp.bfloat16), "snap").astype(jnp.float32),
        lax.psum(shares[1].astype(jnp.bfloat16), "snap").astype(jnp.float32),
        lax.psum(shares[2].astype(jnp.bfloat16), "snap").astype(jnp.float32),
    )
    mlp_new, mlp_first_new, mlp_second_new, mlp_copy = adamw(
        mlp_master, mlp_first, mlp_second, owned[0], rate_mlp
    )
    filter_new, filter_first_new, filter_second_new, filter_copy = adamw(
        filter_master, filter_first, filter_second, owned[1], rate_filter
    )
    small_new, small_first_new, small_second_new, small_copy = adamw(
        small_master, small_first, small_second, owned[2], rate_small
    )
    return (
        output.astype(jnp.bfloat16),
        input_grad,
        mlp_new,
        mlp_first_new,
        mlp_second_new,
        mlp_copy,
        filter_new,
        filter_first_new,
        filter_second_new,
        filter_copy,
        small_new,
        small_first_new,
        small_second_new,
        small_copy,
        stats_new,
    )


FIRST, SECOND, THIRD, FOURTH, HALF, QUARTER, LEVEL, LAST = range(8)
SCHEDULE = {
    "a": [(FIRST, 0), (FIRST, 1)],
    "c0": [(SECOND, 0)],
    "d1": [(SECOND, 1), (FIRST, 2)],
    "f0": [(THIRD, 0)],
    "f1": [(SECOND, 2), (FIRST, 3)],
    "g": [(THIRD, 1)],
    "h0": [(FIRST, 4)],
    "h1": [(FOURTH, 0), (THIRD, 2)],
    ("k2", 0): [(SECOND, 3), (SECOND, 4)],
    ("m", 0): [(FOURTH, 1), (FIRST, 5)],
    ("m0", 0): [(FOURTH, 2)],
    ("m1", 0): [(HALF, 0)],
    ("k1", 1): [(THIRD, 3)],
    ("k2", 1): [(THIRD, 4)],
    ("k0", 2): [(HALF, 1)],
    ("m", 2): [(FOURTH, 3)],
    ("m1", 2): [(QUARTER, 0)],
    ("m2", 2): [(HALF, 2), (FOURTH, 4)],
    ("k0", 3): [(FOURTH, 5)],
    ("m", 3): [(LEVEL, 0), (QUARTER, 1)],
    ("k", 4): [(HALF, 3)],
    ("k2", 4): [(LEVEL, 1)],
    ("l", 4): [(QUARTER, 2)],
    ("k", 5): [(LAST, 0)],
    ("k0", 5): [(LEVEL, 2)],
    ("k1", 5): [(QUARTER, 3)],
    ("k2", 5): [(HALF, 4)],
    ("m", 5): [(LAST, 1), (LEVEL, 3)],
    "o1": [(QUARTER, 4)],
    "p1": [(HALF, 5)],
    "r": [(LAST, 2), (LEVEL, 4)],
    "t1": [(QUARTER, 5)],
    "u1": [(LAST, 3), (LAST, 4)],
    "x0": [(LEVEL, 5)],
    "z": [(LAST, 5)],
}


def lon_matrix(lon_total, mode_total, snaps, rows):
    places = np.arange(lon_total)
    orders = np.arange(mode_total)
    angles = (places[:, None] * orders[None, :] % lon_total) * (2.0 * math.pi / lon_total)
    doubling = np.where(orders == 0, 1.0, 2.0)
    scaling = 1.0 / math.sqrt(lon_total)
    forward = np.stack([np.cos(angles), -np.sin(angles)], axis=1) * scaling
    inverse = forward * doubling

    def spread(table):
        table = np.einsum(
            "ab,lx,rs->alrbsx", np.eye(snaps), table.reshape(lon_total, -1), np.eye(rows)
        )
        return table.reshape(snaps * lon_total * rows, -1).astype(ml_dtypes.bfloat16)

    return spread(forward), spread(inverse)


def lon_turn(lon_total, rows):
    turn = np.einsum("lk,rs->rlks", np.eye(lon_total), np.eye(rows))
    return turn.reshape(rows, lon_total, lon_total * rows).astype(ml_dtypes.bfloat16)


def lat_matrix(lat_total, mode_total):
    places = np.arange(lat_total)
    angles = (places[:, None] * places[None, :] % lat_total) * (2.0 * math.pi / lat_total)
    cosine, sine = np.cos(angles), np.sin(angles)
    table = np.stack([np.stack([cosine, sine], axis=1), np.stack([-sine, cosine], axis=1)])
    table = np.einsum("pkqr,ab->pakrqb", table / math.sqrt(lat_total), np.eye(mode_total))
    size = 2 * lat_total * mode_total
    return table.reshape(size, size).astype(ml_dtypes.bfloat16)


class Refs:
    pass


def block_body(names, sizes, *refs):
    g = Refs()
    for name, ref in zip(names, refs, strict=True):
        setattr(g, name, ref)
    snaps, group, parts, width = sizes
    levels = group // 2
    tokens = g.fields.shape[0] * g.fields.shape[1]
    channel = g.fields.shape[2]
    owned = channel // group
    half = width // 2
    quarter = width // snaps
    tile = tokens // 3
    short = divisor(tokens // 2, 16, 240)
    strip = divisor(tokens // 2, 48, 144)
    sub = divisor(strip, 16, 48)
    low = jnp.bfloat16
    f32 = jnp.float32

    me_snap = lax.axis_index("snap")
    me_sp = lax.axis_index("sp")
    core = lax.rem(me_sp, 2)
    level = me_sp // 2

    def at(snap, sp):
        return {"snap": snap, "sp": sp}

    def sp_after(step):
        return lax.rem(me_sp + step, group)

    def sp_before(step):
        return lax.rem(me_sp + group - step, group)

    def snap_after(step):
        return lax.rem(me_snap + step, snaps)

    def snap_before(step):
        return lax.rem(me_snap + snaps - step, snaps)

    def level_after(step):
        return lax.rem(level + step, levels)

    def level_before(step):
        return lax.rem(level + levels - step, levels)

    other_core = at(me_snap, me_sp + 1 - 2 * core)

    def send(src, dst, sems, index, target):
        return pltpu.make_async_remote_copy(
            src_ref=src,
            dst_ref=dst,
            send_sem=sems[0].at[index],
            recv_sem=sems[1].at[index],
            device_id=target,
            device_id_type=pl.DeviceIdType.MESH,
        )

    half_tokens = tokens // 2

    def strips(body, first=0, count=tokens, before=None, after=None):
        @pl.loop(0, count // strip)
        def _(step):
            if before is not None:
                before(first // strip + step)
            for at_row in range(0, strip, sub):
                body(pl.ds(pl.multiple_of(first + step * strip + at_row, 16), sub))
            if after is not None:
                after(first // strip + step)

    def half_strips(body, part, **around):
        strips(body, part * half_tokens, half_tokens, **around)

    def strip_copy(near, far, sems, place, out):
        rows = pl.ds(pl.multiple_of(place * strip, strip), strip)
        ends = [near.at[rows], far.reshape(tokens, channel).at[rows]]
        if not out:
            ends.reverse()
        return pltpu.make_async_copy(*ends, sems.at[place])

    def fields_load(place):
        return strip_copy(g.fields_in, g.fields, g.fields_sem, place, False)

    def cot_load(place):
        return strip_copy(g.cot_in, g.cot, g.cot_sem, place, False)

    def out_copy(place):
        return strip_copy(g.fields_in, g.out, g.fields_sem, place, True)

    def grad_copy(place):
        return strip_copy(g.grid, g.in_grad, g.cot_sem, place, True)

    def half_rows(part):
        return slice(part * half_tokens, (part + 1) * half_tokens)

    def fold(value):
        return jnp.sum(value.reshape(-1, 8, value.shape[1]), axis=0)

    loads = {}

    def load(name, index):
        copy = pltpu.make_async_copy(getattr(g, name), getattr(g, name + "_in"), g.load_sem.at[index])
        copy.start()
        loads[name] = copy

    for index, name in enumerate(
        [name for name in names[: names.index("out")] if name not in ("mlp", "fields", "cot")]
    ):
        load(name, index)
    for copy in (fields_load, cot_load):
        for place in range(tokens // strip):
            copy(place).start()

    def master_load(part):
        return pltpu.make_async_copy(
            g.mlp.at[:, :, part * width : (part + 1) * width],
            g.mlp_part.at[part % 2],
            g.load_sem.at[len(loads) + part % 2],
        )

    master_load(0).start()
    master_load(1).start()

    barrier = pltpu.get_barrier_semaphore()
    peers = [at(me_snap, sp_after(step)) for step in range(1, group)]
    peers += [at(snap_after(step), me_sp) for step in range(1, snaps)]
    for peer in peers:
        pl.semaphore_signal(
            barrier, inc=1, device_id=peer, device_id_type=pl.DeviceIdType.MESH
        )

    loads["small"].wait()
    loads["kept"].wait()
    g.own_small[...] = jnp.zeros_like(g.own_small)
    rows_small = g.small.shape[0]
    g.own_small[0:rows_small, 0:owned] = g.small_in[...].astype(low).astype(f32)
    pairs_kept = g.kept.shape[1]
    lines = lax.broadcasted_iota(jnp.int32, (pairs_kept, pairs_kept), 0)
    places = lax.broadcasted_iota(jnp.int32, (pairs_kept, pairs_kept), 1)
    kept = jnp.where(lines == places, g.kept_in[...].astype(f32), 0.0)
    g.own_small[16:, :] = jnp.broadcast_to(
        jnp.sum(kept, axis=1, keepdims=True), (pairs_kept, g.own_small.shape[1])
    )
    pl.semaphore_wait(barrier, len(peers))

    def small_copy(step):
        return send(
            g.own_small, g.all_small.at[me_sp], (g.small_s, g.small_r), step, at(me_snap, sp_after(step))
        )

    for step in range(1, group):
        small_copy(step).start()
    g.all_small[me_sp] = g.own_small[...]

    snap_low = lax.rem(me_snap, 2)
    snap_high = me_snap // 2
    beside_low = me_snap + 1 - 2 * snap_low
    beside_high = me_snap + 2 - 4 * snap_high

    def own_quarter(part):
        odd = lax.rem(part, 2)
        return (1 - odd) * me_snap + odd * (2 * snap_low + snap_high)

    def own_place(part):
        return pl.ds(0, snaps) if part == parts - 1 else own_quarter(part)

    def half_quarters(part):
        return pl.ds(2 * (own_quarter(part) // 2), 2)

    def own_rows(sp):
        return pl.ds(pl.multiple_of(sp * owned, owned), owned)

    def spot(part):
        if isinstance(part, int):
            return part // 2 + parts // 2 * (part % 2)
        return lax.div(part, 2) + parts // 2 * lax.rem(part, 2)

    swaps = (
        (pl.ds(0, 1), own_place(0)),
        (pl.ds(3, 2), own_place(1)),
        (pl.ds(1, 2), own_place(0)),
        (pl.ds(5, 1), own_place(5)),
    )
    swapped = {0: 0, 1: 1, 2: 2, 5: 3}

    def swap_copy(batch):
        some, place = swaps[batch]
        return send(
            g.own_w.at[some, 1 - core, place],
            g.all_w.at[some, 1 - core, place, own_rows(me_sp)],
            (g.swap_s, g.swap_r),
            batch,
            other_core,
        )

    def swap_local(batch):
        some, place = swaps[batch]
        return pltpu.make_async_copy(
            g.own_w.at[some, core, place],
            g.all_w.at[some, core, place, own_rows(me_sp)],
            g.swap_l.at[batch],
        )

    def start_swap(batch):
        swap_copy(batch).start()
        swap_local(batch).start()

    def first_copy(part, step):
        rows = pl.ds(pl.multiple_of(level * 2 * owned, 2 * owned), 2 * owned)
        view = g.all_w.at[spot(part), core, own_place(part), rows]
        target = at(me_snap, 2 * level_after(step) + core)
        return send(view, view, (g.first_s, g.first_r), (part, step), target)

    def second_copy(part):
        odd = lax.rem(part, 2)
        view = g.all_w.at[spot(part), core, own_quarter(part)]
        target = at((1 - odd) * beside_low + odd * beside_high, me_sp)
        return send(view, view, (g.second_s, g.second_r), part, target)

    def third_copy(part):
        odd = lax.rem(part, 2)
        view = g.all_w.at[spot(part), core, half_quarters(part)]
        target = at((1 - odd) * beside_high + odd * beside_low, me_sp)
        return send(view, view, (g.third_s, g.third_r), part, target)

    def fourth_copy(part):
        view = g.all_w.at[spot(part), core]
        return send(view, view, (g.fourth_s, g.fourth_r), part, other_core)

    def start_first(part):
        if part in swapped:
            swap_copy(swapped[part]).wait_recv()
            swap_local(swapped[part]).wait()
        for step in range(1, levels):
            first_copy(part, step).start()

    def wait_first(part):
        for step in range(1, levels):
            first_copy(part, step).wait_recv()

    def pass_second(part):
        wait_first(part)
        second_copy(part).start()

    def pass_third(part):
        second_copy(part).wait_recv()
        third_copy(part).start()

    def pass_fourth(part):
        if part == parts - 1:
            wait_first(part)
        else:
            third_copy(part).wait_recv()
        fourth_copy(part).start()

    stages = {FIRST: start_first, SECOND: pass_second, THIRD: pass_third, FOURTH: pass_fourth}

    def reach(point):
        for stage, part in SCHEDULE.get(point, ()):
            stages[stage](part)

    for part in range(parts):
        master_load(part).wait()
        for place in range(snaps):
            cols = slice(place * quarter, (place + 1) * quarter)
            g.own_w[spot(part), :, place] = g.mlp_part[part % 2, :, :, cols].astype(low)
        if part + 2 < parts:
            master_load(part + 2).start()
        if part == 0:
            start_swap(0)
        elif part == parts - 1:
            for batch in range(1, len(swaps)):
                start_swap(batch)
    reach("a")

    def first_unit(rows):
        values = g.fields_in[rows, :].astype(f32)
        centred = values - jnp.mean(values, axis=-1, keepdims=True)
        scale = lax.rsqrt(jnp.mean(centred * centred, axis=-1, keepdims=True) + eps_norm)
        g.scale_one[rows, :] = scale
        g.grid[rows, :] = centred * scale

    strips(first_unit, before=lambda place: fields_load(place).wait())
    reach("b")
    for step in range(1, group):
        small_copy(step).wait_recv()
    for sp in range(group):
        g.gains[:, sp * owned : (sp + 1) * owned] = g.all_small[sp, 0:16, 0:owned]
        g.keep[sp * pairs_kept : (sp + 1) * pairs_kept, :] = g.all_small[sp, 16:, :]

    def first_norm(rows):
        unit = g.grid[rows, :]
        normed = unit * g.gains[0:1, :] + g.gains[1:2, :]
        g.unit_one[rows, :] = unit.astype(low)
        g.normed[rows, :] = normed.astype(low)
        g.grid[rows, :] = g.fields_in[rows, :].astype(f32) + normed

    half_snaps = g.arrived.shape[0] // 2

    def some_snaps(part):
        return pl.ds(part * half_snaps, half_snaps)

    def mode_rows(sp):
        size = g.modes.shape[3]
        return pl.ds(pl.multiple_of(sp * size, size), size)

    def block_copy(which, part, step):
        target = sp_after(step)
        return send(
            g.modes.at[part, target],
            g.arrived.at[some_snaps(part), mode_rows(me_sp), :],
            (g.block_s, g.block_r),
            (which, part, step),
            at(me_snap, target),
        )

    def row_copy(which, part, step):
        target = sp_after(step)
        return send(
            g.turned.at[some_snaps(part), mode_rows(target), :],
            g.home.at[part, me_sp],
            (g.row_s, g.row_r),
            (which, part, step),
            at(me_snap, target),
        )

    def to_blocks(table, which, part):
        modes = dot_nn(table, g.normed[half_rows(part), :])
        for block in range(group):
            cut = modes[:, block * owned : (block + 1) * owned]
            cut = jnp.concatenate([cut, jnp.zeros((cut.shape[0], 128 - owned), f32)], axis=1)
            g.modes[part, block] = cut.astype(low).reshape(g.modes.shape[2:])
        for step in range(1, group):
            block_copy(which, part, step).start()
        g.arrived[some_snaps(part), mode_rows(me_sp), :] = g.modes[part, me_sp]

    def take_blocks(which, part):
        for step in range(1, group):
            block_copy(which, part, step).wait_recv()

    def to_rows(which, part, tables):
        for index, table in enumerate(tables):
            g.turned[part * half_snaps + index] = table.astype(low)
        for step in range(1, group):
            row_copy(which, part, step).start()
        g.home[part, me_sp] = g.turned[some_snaps(part), mode_rows(me_sp), :]

    def home_modes(which, part):
        for step in range(1, group):
            row_copy(which, part, step).wait_recv()
        count = g.gathered.shape[1]
        for block in range(group):
            g.gathered[part, :, block * owned : (block + 1) * owned] = (
                g.home[part, block].reshape(count, 128)[:, 0:owned].astype(f32)
            )
        g.home_low[part] = g.gathered[part].astype(low)

    loads["lon_f"].wait()
    for part in range(2):
        half_strips(first_norm, part)
        reach("c" + str(part))
        to_blocks(g.lon_f_in[...], 0, part)
        reach("d" + str(part))

    loads["filt"].wait()
    for weight, first in ((g.weight_one, 0), (g.weight_two, 2)):
        weight[...] = jnp.zeros_like(weight)
        real = g.filt_in[first].astype(low)
        imag = g.filt_in[first + 1].astype(low)
        weight[0:owned, 0:owned] = real
        weight[128 : 128 + owned, 128 : 128 + owned] = real
        weight[0:owned, 128 : 128 + owned] = imag
        weight[128 : 128 + owned, 0:owned] = -imag

    def bias_row(first):
        return jnp.concatenate(
            [g.own_small[first : first + 1, :], g.own_small[first + 1 : first + 2, :]], axis=1
        )

    for place in range(tokens // strip):
        cot_load(place).wait()
    reach("e")
    loads["lat_f"].wait()
    loads["lat_b"].wait()
    pairs = g.arrived.shape[1] // 2
    half_modes = half_snaps * pairs

    def mode_half(part):
        return slice(part * half_modes, (part + 1) * half_modes)

    def spectra(out, kind, part):
        for snap in range(part * half_snaps, (part + 1) * half_snaps):
            spectrum = dot_nn(g.lat_f_in[...], g.arrived[snap]).astype(kind)
            rows = slice(snap * pairs, (snap + 1) * pairs)
            out[rows, 0:128] = spectrum[0:pairs]
            out[rows, 128:256] = spectrum[pairs:]

    def grids(values):
        tables = []
        for index in range(half_snaps):
            rows = values[index * pairs : (index + 1) * pairs]
            rows = jnp.concatenate([rows[:, 0:128], rows[:, 128:256]], axis=0)
            tables.append(dot_nn(g.lat_b_in[...], rows))
        return tables

    def keep_half():
        keep = jnp.concatenate([g.keep[...], g.keep[...]], axis=1)
        return jnp.concatenate([keep] * half_snaps, axis=0)

    for part in range(2):
        take_blocks(0, part)
        rows = mode_half(part)
        spectra(g.spectrum, low, part)
        g.pre_one[rows, :] = dot_nn(g.spectrum[rows, :], g.weight_one[...]) + bias_row(4)
        g.act_one[rows, :] = gelu_both(g.pre_one[rows, :])[0].astype(low)
        g.pre_two[rows, :] = dot_nn(g.act_one[rows, :], g.weight_two[...]) + bias_row(6)
        to_rows(0, part, grids((shrink(g.pre_two[rows, :]) * keep_half()).astype(low)))
        reach("f" + str(part))
    g.cot_turned[...] = g.cot_in[...].T
    reach("g")

    loads["lon_i"].wait()

    def second_norm(rows):
        values = g.grid[rows, :]
        centred = values - jnp.mean(values, axis=-1, keepdims=True)
        scale = lax.rsqrt(jnp.mean(centred * centred, axis=-1, keepdims=True) + eps_norm)
        centred = centred * scale
        g.unit_two[rows, :] = centred.astype(low)
        g.scale_two[rows, :] = scale
        g.normed[rows, :] = (centred * g.gains[2:3, :] + g.gains[3:4, :]).astype(low)
        g.grid[rows, :] = values + g.gains[8:9, :]
        g.back[rows, :] = jnp.zeros((sub, channel), f32)

    for part in range(2):
        home_modes(0, part)
        g.grid[half_rows(part), :] += dot_nn(g.lon_i_in[...], g.home_low[part])
        reach("h" + str(part))
        half_strips(second_norm, part)
        reach("i" + str(part))
    g.normed_turned[...] = g.normed[...].T
    reach("j")
    flat = jnp.concatenate([g.gains[9 + row : 10 + row, :] for row in range(rows_small - 9)], axis=1)
    for part in range(parts):
        g.bias[part] = flat[:, part * width : (part + 1) * width]

    def core_copy(part, matrix):
        slot = lax.rem(part, 2)
        return send(
            g.grads.at[matrix, :, 1 - core],
            g.core_got.at[slot, matrix],
            (g.core_s, g.core_r),
            (slot, matrix),
            other_core,
        )

    places_one = (snap_low, snap_high)
    places_two = (snap_high, snap_low)
    beside_one = (beside_low, beside_high)
    beside_two = (beside_high, beside_low)

    def half_copy(part, matrix):
        slot = lax.rem(part, 2)
        place = lax.rem(part, 4)
        return send(
            g.half_out.at[slot, matrix, 1 - places_one[matrix]],
            g.half_got.at[place, matrix],
            (g.half_s, g.half_r),
            (place, matrix),
            at(beside_one[matrix], me_sp),
        )

    def quarter_copy(part, matrix):
        slot = lax.rem(part, 2)
        return send(
            g.quarter_out.at[slot, matrix, 1 - places_two[matrix]],
            g.quarter_got.at[slot, matrix],
            (g.quarter_s, g.quarter_r),
            (slot, matrix),
            at(beside_two[matrix], me_sp),
        )

    def level_copy(part, step):
        slot = lax.rem(part, 2)
        place = lax.rem(part, 4)
        target = level_after(step)
        return send(
            g.level_out.at[slot, target],
            g.level_got.at[place, level],
            (g.level_s, g.level_r),
            (place, step),
            at(me_snap, 2 * target + core),
        )

    batches = (pl.ds(0, parts - 2), pl.ds(parts - 2, 1), pl.ds(parts - 1, 1))

    def last_copy(batch, step):
        view = g.total.at[batches[batch], me_snap]
        return send(view, view, (g.last_s, g.last_r), (batch, step), at(snap_after(step), me_sp))

    def half_stage(part):
        slot = lax.rem(part, 2)
        for matrix in range(2):

            if part >= 2:
                half_copy(part - 2, matrix).wait_send()

            core_copy(part, matrix).wait_recv()

            @pl.loop(0, levels)
            def _(row, matrix=matrix):
                both = g.grads[matrix, row, core].astype(f32) + g.core_got[
                    slot, matrix, row
                ].astype(f32)
                both = both.astype(low)
                g.half_out[slot, matrix, 0, row] = both[:, 0:half]
                g.half_out[slot, matrix, 1, row] = both[:, half:width]

            half_copy(part, matrix).start()

    def quarter_stage(part):
        slot = lax.rem(part, 2)
        for matrix in range(2):

            if part >= 2:
                quarter_copy(part - 2, matrix).wait_send()

            half_copy(part, matrix).wait_recv()
            for row in range(levels):
                both = g.half_out[slot, matrix, places_one[matrix], row].astype(f32) + g.half_got[
                    lax.rem(part, 4), matrix, row
                ].astype(f32)
                both = both.astype(low)
                g.quarter_out[slot, matrix, 0, row] = both[:, 0:quarter]
                g.quarter_out[slot, matrix, 1, row] = both[:, quarter:half]
            quarter_copy(part, matrix).start()

    def level_stage(part):
        slot = lax.rem(part, 2)

        if part >= 2:
            for step in range(1, levels):
                level_copy(part - 2, step).wait_send()

        for matrix in range(2):
            quarter_copy(part, matrix).wait_recv()
            for row in range(levels):
                both = g.quarter_out[slot, matrix, places_two[matrix], row].astype(
                    f32
                ) + g.quarter_got[slot, matrix, row].astype(f32)
                g.level_out[slot, row, matrix] = both.astype(low)
        for step in range(1, levels):
            level_copy(part, step).start()

    def last_stage(part):
        slot = lax.rem(part, 2)
        for step in range(1, levels):
            level_copy(part, step).wait_recv()
        for matrix in range(2):
            sums = g.level_out[slot, level, matrix].astype(f32)
            for step in range(1, levels):
                sums += g.level_got[lax.rem(part, 4), level_before(step), matrix].astype(f32)
            g.total[part, me_snap, matrix] = sums.astype(low)
        if part >= parts - 3:
            for step in range(1, snaps):
                last_copy(part - (parts - 3), step).start()

    stages |= {HALF: half_stage, QUARTER: quarter_stage, LEVEL: level_stage, LAST: last_stage}

    def weight(part, matrix):
        return jnp.concatenate([g.all_w[spot(part), matrix, place] for place in range(snaps)], axis=1)

    def add_products(part, rows):
        g.grid[rows, :] += dot_nt(g.act[rows, :], weight(part, 1))
        g.back[rows, :] += dot_nt(g.slope[rows, :], weight(part, 0))

    @pl.loop(0, parts)
    def _(part):
        def reach_in(point, also=True):
            for at_part in range(parts):
                if (point, at_part) in SCHEDULE:
                    pl.when((part == at_part) & also)(functools.partial(reach, (point, at_part)))

        def tile_rows(step):
            return pl.ds(pl.multiple_of(step * tile, tile), tile)

        fourth_copy(part).wait_recv()
        reach_in("k")
        g.grad_bias[part] = jnp.zeros(g.grad_bias.shape[1:], f32)

        @pl.loop(0, tokens // tile)
        def _(step):
            rows = tile_rows(step)
            act, slope = gelu_both(dot_nn(g.normed[rows, :], weight(part, 0)) + g.bias[part])
            g.act[rows, :] = act.astype(low)
            slope = (dot_nn(g.cot_in[rows, :], weight(part, 1)) * slope).astype(low)
            g.slope[rows, :] = slope
            g.grad_bias[part] += fold(slope.astype(f32))
            for at_step in range(tokens // tile):
                reach_in("k" + str(at_step), step == at_step)

        reach_in("l")

        @pl.when(part >= 1)
        def _():
            for matrix in range(2):
                core_copy(part - 1, matrix).wait_send()

        shape = g.grads.shape[1:]
        g.grads[0] = dot_nn(g.normed_turned[...], g.slope[...]).astype(low).reshape(shape)
        core_copy(part, 0).start()
        g.grads[1] = dot_nn(g.cot_turned[...], g.act[...]).astype(low).reshape(shape)
        core_copy(part, 1).start()
        reach_in("m")

        @pl.when(part < parts - 1)
        def _():
            @pl.loop(0, tokens // tile)
            def _(step):
                add_products(part, tile_rows(step))
                for at_step in range(tokens // tile):
                    reach_in("m" + str(at_step), step == at_step)

    g.folds[...] = jnp.zeros_like(g.folds)

    def second_back(rows):
        grad = g.back[rows, :]
        unit = g.unit_two[rows, :].astype(f32)
        cot = g.cot_in[rows, :].astype(f32)
        pulled = grad * g.gains[2:3, :]
        middle = jnp.mean(pulled, axis=-1, keepdims=True)
        slant = jnp.mean(pulled * unit, axis=-1, keepdims=True)
        total = cot + g.scale_two[rows, :] * (pulled - middle - unit * slant)
        g.back[rows, :] = total
        g.normed[rows, :] = total.astype(low)
        g.folds[2] += fold(grad * unit)
        g.folds[3] += fold(grad)
        g.folds[4] += fold(cot)

    loads["lon_it"].wait()
    for part in range(2):

        @pl.loop(0, half_tokens // short)
        def _(step, part=part):
            first_row = part * half_tokens + step * short
            add_products(parts - 1, pl.ds(pl.multiple_of(first_row, 16), short))

        reach("o" + str(part))
        half_strips(second_back, part)
        for step in range(1, group):
            block_copy(0, part, step).wait_send()
        to_blocks(g.lon_it_in[...], 1, part)
        reach("p" + str(part))
    reach("q")

    def low_out(rows):
        g.fields_in[rows, :] = g.grid[rows, :].astype(low)

    strips(low_out, after=lambda place: out_copy(place).start())
    reach("r")
    loads["valid"].wait()
    loads["turn"].wait()
    weigh = sum(
        dot_nn(g.valid_in[:, row, :].astype(f32).astype(low), g.turn_in[row])
        for row in range(g.valid.shape[1])
    )
    places_each = weigh.shape[1]
    precise = lax.Precision.HIGHEST
    sums = [jnp.zeros((1, 128), f32), jnp.zeros((1, 128), f32)]
    for snap in range(g.valid.shape[0]):
        variables = g.grid[snap * places_each : (snap + 1) * places_each, 0:128]
        for index, value in enumerate((variables, variables * variables)):
            sums[index] += jnp.dot(
                weigh[snap : snap + 1, :], value, precision=precise, preferred_element_type=f32
            )

    reach("s")

    def dot_tn(left, right):
        return lax.dot_general(
            left, right, (((0,), (0,)), ((), ())), preferred_element_type=f32
        )

    def filter_rows(first, grad):
        g.pair_grad[...] = grad
        real = g.pair_grad[0:128, 0:128] + g.pair_grad[128:256, 128:256]
        imag = g.pair_grad[0:128, 128:256] - g.pair_grad[128:256, 0:128]
        g.filt_out[me_snap, first] = real[0:owned].astype(low)
        g.filt_out[me_snap, first + 1] = imag[0:owned].astype(low)

    for part in range(2):
        take_blocks(1, part)
        reach("t" + str(part))
        rows = mode_half(part)
        spectra(g.grad_pre, f32, part)
        bend = jnp.tanh(g.pre_two[rows, :] / shrink_level)
        grad = (g.grad_pre[rows, :] * keep_half() * (bend * bend)).astype(low)
        g.grad_two[rows, :] = grad
        grad = dot_nt(grad, g.weight_two[...]) * gelu_both(g.pre_one[rows, :])[1]
        grad = grad.astype(low)
        g.grad_one[rows, :] = grad
        for step in range(1, group):
            row_copy(0, part, step).wait_send()
        to_rows(1, part, grids(dot_nt(grad, g.weight_one[...]).astype(low)))
        reach("u" + str(part))
    reach("v")
    bias_one = jnp.sum(g.grad_one[...].astype(f32), axis=0, keepdims=True)
    bias_two = jnp.sum(g.grad_two[...].astype(f32), axis=0, keepdims=True)
    filter_rows(2, dot_tn(g.act_one[...], g.grad_two[...]))
    filter_rows(0, dot_tn(g.spectrum[...], g.grad_one[...]))

    def filter_copy(step):
        view = g.filt_out.at[me_snap]
        return send(view, view, (g.filt_s, g.filt_r), step, at(snap_after(step), me_sp))

    for step in range(1, snaps):
        filter_copy(step).start()


    reach("w")

    loads["lon_ft"].wait()

    def first_back(rows):
        grad = g.grid[rows, :]
        unit = g.unit_one[rows, :].astype(f32)
        pulled = grad * g.gains[0:1, :]
        middle = jnp.mean(pulled, axis=-1, keepdims=True)
        slant = jnp.mean(pulled * unit, axis=-1, keepdims=True)
        g.grid[rows, :] = g.back[rows, :] + g.scale_one[rows, :] * (
            pulled - middle - unit * slant
        )
        g.folds[0] += fold(grad * unit)
        g.folds[1] += fold(grad)

    for part in range(2):
        home_modes(1, part)
        reach("x" + str(part))
        g.grid[half_rows(part), :] = g.back[half_rows(part), :] + dot_nn(
            g.lon_ft_in[...], g.home_low[part]
        )
        half_strips(first_back, part, after=lambda place: grad_copy(place).start())
        reach("y" + str(part))

    g.grad_rows[...] = jnp.zeros_like(g.grad_rows)
    for index, row in enumerate((0, 1, 2, 3, 8)):
        g.grad_rows[row : row + 1, :] = jnp.sum(g.folds[index], axis=0, keepdims=True)
    flat = jnp.concatenate(
        [jnp.sum(g.grad_bias[part], axis=0, keepdims=True) for part in range(parts)], axis=1
    )
    for row in range(rows_small - 9):
        g.grad_rows[9 + row : 10 + row, :] = flat[:, row * channel : (row + 1) * channel]
    for block in range(group):
        g.tiles[block] = jnp.zeros(g.tiles.shape[1:], f32)
        g.tiles[block, :, 0:owned] = g.grad_rows[:, block * owned : (block + 1) * owned]
        g.tiles[block, 13:14, :] = sums[0]
        g.tiles[block, 14:15, :] = sums[1]

    def tile_copy(step):
        target = sp_after(step)
        return send(
            g.tiles.at[target], g.tiles_got.at[me_sp], (g.tile_s, g.tile_r), step, at(me_snap, target)
        )

    def snap_tile_copy(step):
        view = g.snap_tiles.at[me_snap]
        return send(view, view, (g.snap_tile_s, g.snap_tile_r), step, at(snap_after(step), me_sp))

    for step in range(1, group):
        tile_copy(step).start()
    reach("z")

    for batch in range(len(swaps)):
        swap_copy(batch).wait_send()
    for part in range(parts):
        if part < parts - 1:
            second_copy(part).wait_send()
            third_copy(part).wait_send()
        fourth_copy(part).wait_send()
        for step in range(1, levels):
            first_copy(part, step).wait_send()
    for step in range(1, group):
        small_copy(step).wait_send()
        for part in range(2):
            block_copy(1, part, step).wait_send()
            row_copy(1, part, step).wait_send()
    for matrix in range(2):
        core_copy(parts - 1, matrix).wait_send()
        for part in (parts - 2, parts - 1):
            half_copy(part, matrix).wait_send()
            quarter_copy(part, matrix).wait_send()
    for step in range(1, levels):
        level_copy(parts - 2, step).wait_send()
    for step in range(1, snaps):
        filter_copy(step).wait_send()

    g.tiles_got[me_sp] = g.tiles[me_sp]
    for step in range(1, group):
        tile_copy(step).wait_recv()
    tile_sum = g.tiles_got[0]
    for sp in range(1, group):
        tile_sum += g.tiles_got[sp]
    g.snap_tiles[me_snap] = tile_sum
    g.snap_tiles[me_snap, 4:5, :] = bias_one[:, 0:128]
    g.snap_tiles[me_snap, 5:6, :] = bias_one[:, 128:256]
    g.snap_tiles[me_snap, 6:7, :] = bias_two[:, 0:128]
    g.snap_tiles[me_snap, 7:8, :] = bias_two[:, 128:256]
    for step in range(1, snaps):
        snap_tile_copy(step).start()

    for step in range(1, snaps):
        filter_copy(step).wait_recv()
    filter_sum = g.filt_out[0].astype(f32)
    for snap in range(1, snaps):
        filter_sum += g.filt_out[snap].astype(f32)
    g.grad_filt[...] = filter_sum
    for batch in range(3):
        for step in range(1, snaps):
            last_copy(batch, step).wait_recv()
    grads_out = pltpu.make_async_copy(g.total, g.grad_mlp, g.load_sem.at[3])
    grads_out.start()
    for step in range(1, snaps):
        snap_tile_copy(step).wait_recv()
    tile_sum = g.snap_tiles[0]
    for snap in range(1, snaps):
        tile_sum += g.snap_tiles[snap]
    g.grad_small[...] = tile_sum

    grads_out.wait()
    for place in range(tokens // strip):
        out_copy(place).wait()
        grad_copy(place).wait()
    for step in range(1, levels):
        level_copy(parts - 1, step).wait_send()
    for step in range(1, group):
        tile_copy(step).wait_send()
    for step in range(1, snaps):
        snap_tile_copy(step).wait_send()
        for batch in range(3):
            last_copy(batch, step).wait_send()


def block_pass(fields, cot, valid, kept, mlp, filt, small, snaps, group):
    snap_local, row_local, lon_total, channel = fields.shape
    tokens = snap_local * row_local * lon_total
    hidden = mlp.shape[2]
    lat_total = row_local * group
    modes = kept.shape[1] * group
    owned = channel // group
    width = 512
    parts = hidden // width
    levels = group // 2
    quarter = width // snaps
    low, f32 = jnp.bfloat16, jnp.float32
    half = width // 2
    half_snaps = snap_local // 2
    lon_f, lon_i = lon_matrix(lon_total, modes, half_snaps, row_local)

    def paired(array):
        return jnp.transpose(array, (0, 2, 1, 3)).reshape(-1, row_local, channel)

    lat_f = lat_matrix(lat_total, modes)
    pair = 2 * modes * row_local
    spread = half_snaps * row_local * 2 * modes
    inputs = dict(
        small=small,
        kept=kept.T,
        fields=paired(fields),
        lon_f=jnp.asarray(np.ascontiguousarray(lon_f.T)),
        filt=filt,
        lat_f=jnp.asarray(lat_f),
        lat_b=jnp.asarray(np.ascontiguousarray(lat_f.T)),
        cot=paired(cot),
        lon_i=jnp.asarray(lon_i),
        valid=valid,
        turn=jnp.asarray(lon_turn(lon_total, row_local)),
        lon_it=jnp.asarray(np.ascontiguousarray(lon_i.T)),
        lon_ft=jnp.asarray(lon_f),
        mlp=mlp,
    )
    outputs = dict(
        out=jax.ShapeDtypeStruct((tokens // row_local, row_local, channel), low),
        in_grad=jax.ShapeDtypeStruct((tokens // row_local, row_local, channel), f32),
        grad_mlp=jax.ShapeDtypeStruct((parts, snaps, 2, owned, quarter), low),
        grad_filt=jax.ShapeDtypeStruct((4, owned, 128), f32),
        grad_small=jax.ShapeDtypeStruct((16, 128), f32),
    )
    vmem = pltpu.VMEM
    dma = pltpu.SemaphoreType.DMA
    scratch = {
        name + "_in": vmem(value.shape, value.dtype)
        for name, value in inputs.items()
        if name not in ("mlp", "fields", "cot")
    }
    strip = divisor(tokens // 2, 48, 144)
    scratch |= dict(
        mlp_part=vmem((2, 2, owned, width), f32),
        fields_in=vmem((tokens, channel), low),
        fields_sem=dma((tokens // strip,)),
        cot_sem=dma((tokens // strip,)),
        cot_in=vmem((tokens, channel), low),
        grid=vmem((tokens, channel), f32),
        back=vmem((tokens, channel), f32),
        normed=vmem((tokens, channel), low),
        normed_turned=vmem((channel, tokens), low),
        cot_turned=vmem((channel, tokens), low),
        unit_one=vmem((tokens, channel), low),
        unit_two=vmem((tokens, channel), low),
        scale_one=vmem((tokens, 1), f32),
        scale_two=vmem((tokens, 1), f32),
        own_small=vmem((16 + kept.shape[0], 128), f32),
        all_small=vmem((group, 16 + kept.shape[0], 128), f32),
        gains=vmem((16, channel), f32),
        keep=vmem((lat_total * modes, 128), f32),
        own_w=vmem((parts, 2, snaps, owned, quarter), low),
        all_w=vmem((parts, 2, snaps, channel, quarter), low),
        modes=vmem((2, group, half_snaps, pair, 128), low),
        arrived=vmem((snap_local, pair * group, 128), low),
        turned=vmem((snap_local, pair * group, 128), low),
        home=vmem((2, group, half_snaps, pair, 128), low),
        gathered=vmem((2, spread, channel), f32),
        home_low=vmem((2, spread, channel), low),
        weight_one=vmem((256, 256), low),
        weight_two=vmem((256, 256), low),
        spectrum=vmem((snap_local * lat_total * modes, 256), low),
        pre_one=vmem((snap_local * lat_total * modes, 256), f32),
        act_one=vmem((snap_local * lat_total * modes, 256), low),
        pre_two=vmem((snap_local * lat_total * modes, 256), f32),
        grad_pre=vmem((snap_local * lat_total * modes, 256), f32),
        grad_two=vmem((snap_local * lat_total * modes, 256), low),
        grad_one=vmem((snap_local * lat_total * modes, 256), low),
        folds=vmem((5, 8, channel), f32),
        pair_grad=vmem((256, 256), f32),
        act=vmem((tokens, width), low),
        slope=vmem((tokens, width), low),
        bias=vmem((parts, 1, width), f32),
        grad_bias=vmem((parts, 8, width), f32),
        grad_rows=vmem((16, channel), f32),
        grads=vmem((2, levels, 2, owned, width), low),
        core_got=vmem((2, 2, levels, owned, width), low),
        half_out=vmem((2, 2, 2, levels, owned, half), low),
        half_got=vmem((4, 2, levels, owned, half), low),
        quarter_out=vmem((2, 2, 2, levels, owned, quarter), low),
        quarter_got=vmem((2, 2, levels, owned, quarter), low),
        level_out=vmem((2, levels, 2, owned, quarter), low),
        level_got=vmem((4, levels, 2, owned, quarter), low),
        total=vmem((parts, snaps, 2, owned, quarter), low),
        filt_out=vmem((snaps, 4, owned, 128), low),
        tiles=vmem((group, 16, 128), f32),
        tiles_got=vmem((group, 16, 128), f32),
        snap_tiles=vmem((snaps, 16, 128), f32),
        swap_l=dma((4,)),
        load_sem=dma((len(inputs) + 1,)),
    )
    for name, shape in dict(
        small=(group,),
        swap=(4,),
        first=(parts, levels),
        second=(parts,),
        third=(parts,),
        fourth=(parts,),
        block=(2, 2, group),
        row=(2, 2, group),
        core=(2, 2),
        half=(4, 2),
        quarter=(2, 2),
        level=(4, levels),
        last=(3, snaps),
        filt=(snaps,),
        tile=(group,),
        snap_tile=(snaps,),
    ).items():
        scratch[name + "_s"] = dma(shape)
        scratch[name + "_r"] = dma(shape)
    names = [*inputs, *outputs, *scratch]
    far = pl.BlockSpec(memory_space=pl.ANY)
    near = pl.BlockSpec(memory_space=pltpu.VMEM)
    results = pl.pallas_call(
        functools.partial(block_body, names, (snaps, group, parts, width)),
        in_specs=[far] * len(inputs),
        out_specs=[far, far, far, near, near],
        out_shape=list(outputs.values()),
        scratch_shapes=list(scratch.values()),
        compiler_params=pltpu.CompilerParams(
            collective_id=0, has_side_effects=True, vmem_limit_bytes=VMEM_LIMIT
        ),
        cost_estimate=pl.CostEstimate(
            flops=12 * tokens * channel * hidden,
            bytes_accessed=4 * hidden * channel,
            transcendentals=tokens * hidden,
        ),
        name="block_pass",
    )(*inputs.values())
    return results


def step_body(names, positions, *refs):
    g = Refs()
    for name, ref in zip(names, refs, strict=True):
        setattr(g, name, ref)
    parts, snaps = g.grad_mlp.shape[:2]
    quarter = g.grad_mlp.shape[4]
    width = snaps * quarter
    moments = ("w", "m", "v")
    results = ("new", "first", "second", "copy")

    pieces = g.far_sem.shape[2]
    ends = ((g.out, g.out_near, g.out_o), (g.in_grad, g.in_grad_near, g.in_grad_o))

    def passing(kind, piece, leg):
        size = ends[kind][0].shape[0] // pieces
        rows = pl.ds(piece * size, size)
        return pltpu.make_async_copy(
            ends[kind][leg].at[rows], ends[kind][leg + 1].at[rows], g.far_sem.at[leg, kind, piece]
        )

    through = [(kind, piece) for kind in range(2) for piece in range(pieces)]

    def part_cols(part):
        return pl.ds(part * width, width)

    def load(part):
        near = [
            pltpu.make_async_copy(
                getattr(g, "mlp_" + kind).at[:, :, part_cols(part)],
                g.near.at[index, part],
                g.near_sem.at[index, part],
            )
            for index, kind in enumerate(moments)
        ]
        near.append(
            pltpu.make_async_copy(g.grad_mlp.at[part], g.grad_near.at[part], g.near_sem.at[3, part])
        )
        return near

    def store(part):
        copies = [
            pltpu.make_async_copy(
                g.near.at[index, part],
                getattr(g, "mlp_" + kind).at[:, :, part_cols(part)],
                g.back_sem.at[index, part],
            )
            for index, kind in enumerate(results[:3])
        ]
        copies.append(
            pltpu.make_async_copy(
                g.low_near.at[part], g.mlp_copy.at[:, :, part_cols(part)], g.back_sem.at[3, part]
            )
        )
        return copies

    coming = [load(part) for part in range(parts)]
    going = [store(part) for part in range(parts)]
    shares = [through[part::parts] for part in range(parts)]
    for part in range(parts):
        for copy in coming[part]:
            copy.start()
        for each in shares[part]:
            passing(*each, 0).start()

    def put(prefix, values):
        for kind, value in zip(results, values, strict=True):
            getattr(g, prefix + kind)[...] = value

    owned = g.filt_w.shape[2]
    put(
        "filt_",
        adamw(g.filt_w[...], g.filt_m[...], g.filt_v[...], g.grad_filt[:, :, 0:owned], rate_filter),
    )
    rows = g.small_w.shape[0]
    put(
        "small_",
        adamw(
            g.small_w[...], g.small_m[...], g.small_v[...], g.grad_small[0:rows, 0:owned], rate_small
        ),
    )
    totals = g.grad_small[rows : rows + 2, 0 : g.run.shape[1]]
    g.stats[...] = stat_decay * g.run[...] + (1.0 - stat_decay) * totals / positions

    for part in range(parts):
        for copy in coming[part]:
            copy.wait()

        for matrix, snap in [(matrix, snap) for matrix in range(2) for snap in range(snaps)]:
            place = snap if matrix else 2 * (snap % 2) + snap // 2
            where = (matrix, slice(None), slice(place * quarter, (place + 1) * quarter))
            now = [g.near[(index, part, *where)] for index in range(3)]
            grad = g.grad_near[part, snap, matrix].astype(jnp.float32)
            values = adamw(*now, grad, rate_mlp)
            for index in range(3):
                g.near[(index, part, *where)] = values[index]
            g.low_near[(part, *where)] = values[3]
        for copy in going[part]:
            copy.start()
        for each in shares[part]:
            passing(*each, 0).wait()
            passing(*each, 1).start()
    for each in through:
        passing(*each, 1).wait()
    for part in range(parts):
        for copy in going[part]:
            copy.wait()


def step_pass(shown, grads, masters, run_stats, positions):
    grad_mlp, grad_filt, grad_small = grads
    mlp, filt, small = masters
    parts = grad_mlp.shape[0]
    width = mlp[0].shape[2] // parts
    f32, low = jnp.float32, jnp.bfloat16
    far = pl.BlockSpec(memory_space=pltpu.HBM)
    near = pl.BlockSpec(memory_space=pltpu.VMEM)
    inputs = dict(out=shown[0], in_grad=shown[1], grad_mlp=grad_mlp)
    inputs |= dict(zip(("mlp_w", "mlp_m", "mlp_v"), mlp, strict=True))
    far_in = len(inputs)
    inputs |= dict(grad_filt=grad_filt, grad_small=grad_small)
    inputs |= dict(zip(("filt_w", "filt_m", "filt_v"), filt, strict=True))
    inputs |= dict(zip(("small_w", "small_m", "small_v"), small, strict=True))
    inputs |= dict(run=run_stats)
    results = (("new", f32), ("first", f32), ("second", f32), ("copy", low))
    outputs = {
        name + "_o": jax.ShapeDtypeStruct(array.shape, array.dtype)
        for name, array in zip(("out", "in_grad"), shown, strict=True)
    }
    outputs |= {"mlp_" + kind: jax.ShapeDtypeStruct(mlp[0].shape, dt) for kind, dt in results}
    far_out = len(outputs)
    outputs |= {"filt_" + kind: jax.ShapeDtypeStruct(filt[0].shape, dt) for kind, dt in results}
    outputs |= {"small_" + kind: jax.ShapeDtypeStruct(small[0].shape, dt) for kind, dt in results}
    outputs |= dict(stats=jax.ShapeDtypeStruct(run_stats.shape, f32))
    scratch = dict(
        near=pltpu.VMEM((3, parts, 2, mlp[0].shape[1], width), f32),
        grad_near=pltpu.VMEM(grad_mlp.shape, low),
        low_near=pltpu.VMEM((parts, 2, mlp[0].shape[1], width), low),
        near_sem=pltpu.SemaphoreType.DMA((4, parts)),
        back_sem=pltpu.SemaphoreType.DMA((4, parts)),
        out_near=pltpu.VMEM(shown[0].shape, low),
        in_grad_near=pltpu.VMEM(shown[1].shape, f32),
        far_sem=pltpu.SemaphoreType.DMA((2, 2, divisor(shown[0].shape[0], 1, 4))),
    )
    return pl.pallas_call(
        functools.partial(step_body, [*inputs, *outputs, *scratch], positions),
        in_specs=[far] * far_in + [near] * (len(inputs) - far_in),
        out_specs=[far] * far_out + [near] * (len(outputs) - far_out),
        out_shape=list(outputs.values()),
        scratch_shapes=list(scratch.values()),
        compiler_params=pltpu.CompilerParams(vmem_limit_bytes=VMEM_LIMIT),
        name="step_pass",
    )(*inputs.values())


def per_device_blocks(
    fields,
    cotangent,
    valid_mask,
    kept_modes,
    mlp_master,
    mlp_first,
    mlp_second,
    filter_master,
    filter_first,
    filter_second,
    small_master,
    small_first,
    small_second,
    run_stats,
):
    snaps, group = lax.axis_size("snap"), lax.axis_size("sp")
    out, in_grad, *grads = block_pass(
        fields, cotangent, valid_mask, kept_modes, mlp_master, filter_master, small_master, snaps, group
    )
    snap_local, row_local, lon_total, channel = fields.shape
    positions = snap_local * snaps * row_local * group * lon_total
    out, in_grad, *stepped = step_pass(
        (out, in_grad),
        grads,
        (
            (mlp_master, mlp_first, mlp_second),
            (filter_master, filter_first, filter_second),
            (small_master, small_first, small_second),
        ),
        run_stats,
        positions,
    )
    rows_apart = (snap_local, lon_total, row_local, channel)
    out, in_grad = [
        jnp.transpose(array.reshape(rows_apart), (0, 2, 1, 3)) for array in (out, in_grad)
    ]
    return (out, in_grad, *stepped)


def per_device(*arrays):
    group, snaps = lax.axis_size("sp"), lax.axis_size("snap")
    channel, hidden = arrays[0].shape[3], arrays[4].shape[2]
    by_block = group == BLOCKS and snaps == 4 and arrays[3].shape[1] == 1
    if by_block and hidden == 6 * 512 and channel // group <= 128 and channel % (16 * group) == 0:
        return per_device_blocks(*arrays)
    return per_device_modes(*arrays)


def solution(mesh):
    return jax.shard_map(
        per_device,
        mesh=mesh,
        in_specs=(
            P("snap", "sp", None, None),
            P("snap", "sp", None, None),
            P("snap", "sp", None),
            P(None, "sp"),
            P(None, "sp", None),
            P(None, "sp", None),
            P(None, "sp", None),
            P(None, "sp", None),
            P(None, "sp", None),
            P(None, "sp", None),
            P(None, "sp"),
            P(None, "sp"),
            P(None, "sp"),
            P(),
        ),
        out_specs=(
            P("snap", "sp", None, None),
            P("snap", "sp", None, None),
            P(None, "sp", None),
            P(None, "sp", None),
            P(None, "sp", None),
            P(None, "sp", None),
            P(None, "sp", None),
            P(None, "sp", None),
            P(None, "sp", None),
            P(None, "sp", None),
            P(None, "sp"),
            P(None, "sp"),
            P(None, "sp"),
            P(None, "sp"),
            P(),
        ),
        check_vma=False,
    )
```

```python
import functools
import math

import jax
import jax.numpy as jnp
import ml_dtypes
import numpy as np
from jax import lax
from jax.experimental import pallas as pl
from jax.experimental.pallas import tpu as pltpu
from jax.sharding import PartitionSpec as P

BLOCKS = 8
NVAR = 20
STEP = 10
VMEM_LIMIT = 63 * 1024 * 1024


eps_norm = 1e-06
shrink_level = 0.01
beta_one = 0.5
beta_two = 0.5
adam_eps = 1e-08
decay_rate = 0.01
rate_mlp = 0.03
rate_filter = 0.1
rate_small = 0.2
stat_decay = 0.5


def layer_norm(values, gain_vec, shift_vec):
    centred = values - jnp.mean(values, axis=-1, keepdims=True)
    spread = jnp.mean(centred * centred, axis=-1, keepdims=True)
    return centred * lax.rsqrt(spread + eps_norm) * gain_vec + shift_vec


def shrink(values):
    return values - shrink_level * jnp.tanh(values / shrink_level)


def lon_tables(lon_total, mode_total):
    places = jnp.arange(lon_total, dtype=jnp.int32)
    orders = jnp.arange(mode_total, dtype=jnp.int32)
    angles = (places[:, None] * orders[None, :] % lon_total).astype(jnp.float32) * (
        2.0 * math.pi / lon_total
    )
    scaling = 1.0 / math.sqrt(lon_total)
    forward_tab = jnp.stack([jnp.cos(angles), -jnp.sin(angles)], axis=1) * scaling
    doubling = jnp.where(orders == 0, 1.0, 2.0).astype(jnp.float32)[:, None]
    inverse_tab = (
        jnp.stack([jnp.cos(angles).T * doubling, -jnp.sin(angles).T * doubling], axis=0) * scaling
    )
    return (forward_tab.astype(jnp.bfloat16), inverse_tab.astype(jnp.bfloat16))


def lat_table(lat_total):
    places = jnp.arange(lat_total, dtype=jnp.int32)
    angles = (places[:, None] * places[None, :] % lat_total).astype(jnp.float32) * (
        2.0 * math.pi / lat_total
    )
    cosine = jnp.cos(angles)
    sine_part = jnp.sin(angles)
    upper_rows = jnp.stack([cosine, sine_part], axis=1)
    bottom = jnp.stack([-sine_part, cosine], axis=1)
    return (jnp.stack([upper_rows, bottom], axis=0) / math.sqrt(lat_total)).astype(jnp.bfloat16)


def complex_pair(real_part, imag_part):
    return jnp.stack([jnp.stack([real_part, -imag_part]), jnp.stack([imag_part, real_part])])


gelu_scale = math.sqrt(2.0 / math.pi)
gelu_cubic = 0.044715


def gelu_both(value):
    bend = (gelu_scale * gelu_cubic) * (value * value)
    turn = jnp.tanh(value * (gelu_scale + bend))
    half = 0.5 + 0.5 * turn
    slope = half * (1.0 + (value * (1.0 - turn)) * (gelu_scale + 3.0 * bend))
    return value * half, slope


def dot_nt(left, right):
    return lax.dot_general(
        left, right, (((1,), (1,)), ((), ())), preferred_element_type=jnp.float32
    )


def dot_nn(left, right):
    return jnp.dot(left, right, preferred_element_type=jnp.float32)


def divisor(total, unit, most):
    return max(size for size in range(unit, most + 1, unit) if total % size == 0)


def mlp_body(
    tile,
    normed_ref,
    cot_ref,
    up_ref,
    down_ref,
    bias_ref,
    out_ref,
    back_ref,
    grad_up_ref,
    grad_down_ref,
    grad_bias_ref,
    normed_turned,
    cot_turned,
    act_ref,
    slope_ref,
):
    tokens = normed_ref.shape[0]

    @pl.when(pl.program_id(0) == 0)
    def _():
        normed_turned[...] = normed_ref[...].T
        cot_turned[...] = cot_ref[...].T
        out_ref[...] = jnp.zeros_like(out_ref)
        back_ref[...] = jnp.zeros_like(back_ref)

    grad_bias_ref[...] = jnp.zeros_like(grad_bias_ref)

    @pl.loop(0, tokens // tile)
    def _(step):
        rows = pl.ds(pl.multiple_of(step * tile, tile), tile)
        act, slope = gelu_both(dot_nn(normed_ref[rows, :], up_ref[...]) + bias_ref[...])
        act = act.astype(jnp.bfloat16)
        slope = (dot_nn(cot_ref[rows, :], down_ref[...]) * slope).astype(jnp.bfloat16)
        act_ref[rows, :] = act
        slope_ref[rows, :] = slope
        grad_bias_ref[...] += jnp.sum(slope.astype(jnp.float32), axis=0, keepdims=True)
        out_ref[rows, :] += dot_nt(act, down_ref[...])
        back_ref[rows, :] += dot_nt(slope, up_ref[...])

    grad_up_ref[...] = dot_nn(normed_turned[...], slope_ref[...]).astype(grad_up_ref.dtype)
    grad_down_ref[...] = dot_nn(cot_turned[...], act_ref[...]).astype(grad_down_ref.dtype)


def mlp_pass(normed, cot, weights, bias):
    tokens, channel = normed.shape
    hidden = weights.shape[2]
    width = divisor(hidden, 128, 512)
    tile = divisor(tokens, 16, 480)
    whole = pl.BlockSpec((tokens, channel), lambda j: (0, 0))
    block = pl.BlockSpec((channel, width), lambda j: (0, j))
    line = pl.BlockSpec((1, width), lambda j: (0, j))
    part = lambda which: pl.BlockSpec((None, channel, width), lambda j: (which, 0, j))
    total = jax.ShapeDtypeStruct((tokens, channel), jnp.float32)
    grads = jax.ShapeDtypeStruct((channel, hidden), jnp.bfloat16)
    return pl.pallas_call(
        functools.partial(mlp_body, tile),
        grid=(hidden // width,),
        in_specs=[whole, whole, part(0), part(1), line],
        out_specs=[whole, whole, block, block, line],
        out_shape=[total, total, grads, grads, jax.ShapeDtypeStruct((1, hidden), jnp.float32)],
        scratch_shapes=[
            pltpu.VMEM((channel, tokens), jnp.bfloat16),
            pltpu.VMEM((channel, tokens), jnp.bfloat16),
            pltpu.VMEM((tokens, width), jnp.bfloat16),
            pltpu.VMEM((tokens, width), jnp.bfloat16),
        ],
        compiler_params=pltpu.CompilerParams(vmem_limit_bytes=56 * 1024 * 1024),
        cost_estimate=pl.CostEstimate(
            flops=12 * tokens * channel * hidden,
            bytes_accessed=8 * channel * hidden + 12 * tokens * channel,
            transcendentals=tokens * hidden,
        ),
        name="mlp_pass",
    )(normed, cot, weights, weights, bias)


def spectral_front(arrived, lat_fwd, first_pair, second_pair, bias_one, bias_two):
    spectrum = jnp.einsum(
        "pkqr,nrqmd->nkpmd", lat_fwd, arrived, preferred_element_type=jnp.float32
    ).astype(jnp.bfloat16)
    snap_local, lat_total, pair_count, mode_local, channel = spectrum.shape
    blocked = spectrum.reshape(
        snap_local, lat_total, pair_count, mode_local, BLOCKS, channel // BLOCKS
    )
    pre_one = (
        jnp.einsum("nkqmbi,pqbio->nkpmbo", blocked, first_pair, preferred_element_type=jnp.float32)
        + bias_one
    )
    act_one = jax.nn.gelu(pre_one).astype(jnp.bfloat16)
    pre_two = (
        jnp.einsum("nkqmbi,pqbio->nkpmbo", act_one, second_pair, preferred_element_type=jnp.float32)
        + bias_two
    )
    return (blocked, pre_one, act_one, pre_two)


def adamw(master, first_mom, second_mom, gradient, step_rate):
    first_next = beta_one * first_mom + (1.0 - beta_one) * gradient
    second_next = beta_two * second_mom + (1.0 - beta_two) * gradient * gradient
    fix_one = 1.0 / (1.0 - beta_one**STEP)
    fix_two = 1.0 / (1.0 - beta_two**STEP)
    direction = first_next * fix_one / (jnp.sqrt(second_next * fix_two) + adam_eps)
    master_next = master - step_rate * (direction + decay_rate * master)
    return (master_next, first_next, second_next, master_next.astype(jnp.bfloat16))


def per_device_modes(
    fields,
    cotangent,
    valid_mask,
    kept_modes,
    mlp_master,
    mlp_first,
    mlp_second,
    filter_master,
    filter_first,
    filter_second,
    small_master,
    small_first,
    small_second,
    run_stats,
):
    group_size = lax.axis_size("sp")
    snap_local, row_local, lon_total, channel = fields.shape
    lat_total = row_local * group_size
    mode_local = kept_modes.shape[1]
    mode_total = mode_local * group_size
    block_width = channel // BLOCKS
    lon_fwd, lon_inv = lon_tables(lon_total, mode_total)
    lat_fwd = lat_table(lat_total)
    mlp_w, filt_w, small_w = (
        lax.all_gather(mlp_master.astype(jnp.bfloat16), "sp", axis=1, tiled=True),
        lax.all_gather(filter_master.astype(jnp.bfloat16), "sp", axis=1, tiled=True),
        lax.all_gather(small_master.astype(jnp.bfloat16), "sp", axis=1, tiled=True),
    )
    small_f = small_w.astype(jnp.float32)
    weights = filt_w.reshape(4, BLOCKS, block_width, block_width)
    first_pair = complex_pair(weights[0], weights[1])
    second_pair = complex_pair(weights[2], weights[3])
    bias_one = small_f[4:6].reshape(2, 1, BLOCKS, block_width)
    bias_two = small_f[6:8].reshape(2, 1, BLOCKS, block_width)
    fields_float = fields.astype(jnp.float32)
    normed, norm_pull = jax.vjp(layer_norm, fields_float, small_f[0], small_f[1])
    normed_low = normed.astype(jnp.bfloat16)
    spec_lon = jnp.einsum(
        "nrld,lqm->nrqmd", normed_low, lon_fwd, preferred_element_type=jnp.float32
    ).astype(jnp.bfloat16)
    arrived = lax.all_to_all(spec_lon, "sp", split_axis=3, concat_axis=1, tiled=True)
    spectral = spectral_front(arrived, lat_fwd, first_pair, second_pair, bias_one, bias_two)
    keep_mask = kept_modes.astype(jnp.float32)[None, :, None, :, None, None]
    masked = (shrink(spectral[3]) * keep_mask).astype(jnp.bfloat16)
    masked = masked.reshape(snap_local, lat_total, 2, mode_local, channel)
    returned = jnp.einsum(
        "pkqr,nkpmd->nrqmd", lat_fwd, masked, preferred_element_type=jnp.float32
    ).astype(jnp.bfloat16)
    home_modes = lax.all_to_all(returned, "sp", split_axis=1, concat_axis=3, tiled=True)
    filtered = jnp.einsum(
        "nrqmd,qml->nrld", home_modes, lon_inv, preferred_element_type=jnp.float32
    )
    mixture = fields_float + normed + filtered
    normed_two, norm_two_pull = jax.vjp(layer_norm, mixture, small_f[2], small_f[3])
    normed_two_low = normed_two.astype(jnp.bfloat16)
    tokens = snap_local * row_local * lon_total
    passed = mlp_pass(
        normed_two_low.reshape(tokens, channel),
        cotangent.reshape(tokens, channel),
        mlp_w,
        small_f[9:].reshape(1, -1),
    )
    output = mixture + passed[0].reshape(mixture.shape) + small_f[8]
    weight_mask = valid_mask.astype(jnp.float32)[..., None]
    variables = output[..., :NVAR]
    local_sums = jnp.stack(
        [
            jnp.sum(weight_mask * variables, axis=(0, 1, 2)),
            jnp.sum(weight_mask * variables * variables, axis=(0, 1, 2)),
        ]
    )
    total_sums = lax.psum(local_sums, ("snap", "sp"))
    positions = snap_local * lax.axis_size("snap") * lat_total * lon_total
    stats_new = stat_decay * run_stats + (1.0 - stat_decay) * total_sums / positions
    cot_float = cotangent.astype(jnp.float32)
    grad_normed_two = passed[1].reshape(mixture.shape)
    grad_bias_hidden = passed[4]
    grad_mix_norm, grad_gain_two, grad_shift_two = norm_two_pull(grad_normed_two)
    grad_mixture = cot_float + grad_mix_norm
    grad_bias_out = jnp.sum(cot_float, axis=(0, 1, 2))
    grad_filtered = grad_mixture.astype(jnp.bfloat16)
    grad_home = jnp.einsum(
        "nrld,qml->nrqmd", grad_filtered, lon_inv, preferred_element_type=jnp.float32
    ).astype(jnp.bfloat16)
    grad_returned = lax.all_to_all(grad_home, "sp", split_axis=3, concat_axis=1, tiled=True)
    grad_masked = jnp.einsum(
        "pkqr,nrqmd->nkpmd", lat_fwd, grad_returned, preferred_element_type=jnp.float32
    )
    arrived_again = lax.all_to_all(spec_lon, "sp", split_axis=3, concat_axis=1, tiled=True)
    used_front = spectral_front(arrived_again, lat_fwd, first_pair, second_pair, bias_one, bias_two)
    blocked, pre_one, act_one, pre_two = used_front
    grad_two = jax.vjp(shrink, pre_two)[1](grad_masked.reshape(pre_two.shape) * keep_mask)[
        0
    ].astype(jnp.bfloat16)
    grad_bias_two = jnp.sum(grad_two.astype(jnp.float32), axis=(0, 1, 3))
    grad_second = jnp.einsum(
        "nkqmbi,nkpmbo->pqbio", act_one, grad_two, preferred_element_type=jnp.float32
    )
    grad_act = jnp.einsum(
        "nkpmbo,pqbio->nkqmbi", grad_two, second_pair, preferred_element_type=jnp.float32
    )
    grad_one = jax.vjp(jax.nn.gelu, pre_one)[1](grad_act)[0].astype(jnp.bfloat16)
    grad_bias_one = jnp.sum(grad_one.astype(jnp.float32), axis=(0, 1, 3))
    grad_first = jnp.einsum(
        "nkqmbi,nkpmbo->pqbio", blocked, grad_one, preferred_element_type=jnp.float32
    )
    grad_spectrum = jnp.einsum(
        "nkpmbo,pqbio->nkqmbi", grad_one, first_pair, preferred_element_type=jnp.float32
    ).astype(jnp.bfloat16)
    grad_spectrum = grad_spectrum.reshape(snap_local, lat_total, 2, mode_local, channel)
    grad_lon = jnp.einsum(
        "pkqr,nkpmd->nrqmd", lat_fwd, grad_spectrum, preferred_element_type=jnp.float32
    ).astype(jnp.bfloat16)
    grad_rows = lax.all_to_all(grad_lon, "sp", split_axis=1, concat_axis=3, tiled=True)
    grad_normed = grad_mixture + jnp.einsum(
        "nrqmd,lqm->nrld", grad_rows, lon_fwd, preferred_element_type=jnp.float32
    )
    grad_field_norm, grad_gain_one, grad_shift_one = norm_pull(grad_normed)
    input_grad = grad_mixture + grad_field_norm
    grad_filter = jnp.stack(
        [
            grad_first[0, 0] + grad_first[1, 1],
            grad_first[1, 0] - grad_first[0, 1],
            grad_second[0, 0] + grad_second[1, 1],
            grad_second[1, 0] - grad_second[0, 1],
        ]
    ).reshape(4, channel, block_width)
    grad_small = jnp.concatenate(
        [
            jnp.stack([grad_gain_one, grad_shift_one, grad_gain_two, grad_shift_two]),
            grad_bias_one.reshape(2, channel),
            grad_bias_two.reshape(2, channel),
            grad_bias_out[None, :],
            grad_bias_hidden.reshape(-1, channel),
        ],
        axis=0,
    )
    shares = (
        jnp.stack([
            lax.psum_scatter(part, "sp", scatter_dimension=0, tiled=True) for part in passed[2:4]
        ]),
        lax.psum_scatter(grad_filter, "sp", scatter_dimension=1, tiled=True),
        lax.psum_scatter(grad_small, "sp", scatter_dimension=1, tiled=True),
    )
    owned = (
        lax.psum(shares[0].astype(jnp.bfloat16), "snap").astype(jnp.float32),
        lax.psum(shares[1].astype(jnp.bfloat16), "snap").astype(jnp.float32),
        lax.psum(shares[2].astype(jnp.bfloat16), "snap").astype(jnp.float32),
    )
    mlp_new, mlp_first_new, mlp_second_new, mlp_copy = adamw(
        mlp_master, mlp_first, mlp_second, owned[0], rate_mlp
    )
    filter_new, filter_first_new, filter_second_new, filter_copy = adamw(
        filter_master, filter_first, filter_second, owned[1], rate_filter
    )
    small_new, small_first_new, small_second_new, small_copy = adamw(
        small_master, small_first, small_second, owned[2], rate_small
    )
    return (
        output.astype(jnp.bfloat16),
        input_grad,
        mlp_new,
        mlp_first_new,
        mlp_second_new,
        mlp_copy,
        filter_new,
        filter_first_new,
        filter_second_new,
        filter_copy,
        small_new,
        small_first_new,
        small_second_new,
        small_copy,
        stats_new,
    )


FIRST, SECOND, THIRD, FOURTH, HALF, QUARTER, LEVEL, LAST = range(8)
SCHEDULE = {
    "a": [(FIRST, 0), (FIRST, 1)],
    "c0": [(SECOND, 0)],
    "d1": [(SECOND, 1), (FIRST, 2)],
    "f0": [(THIRD, 0)],
    "f1": [(SECOND, 2), (FIRST, 3)],
    "g": [(THIRD, 1)],
    "h0": [(FIRST, 4)],
    "h1": [(FOURTH, 0), (THIRD, 2)],
    ("k2", 0): [(SECOND, 3), (SECOND, 4)],
    ("m", 0): [(FOURTH, 1), (FIRST, 5)],
    ("m0", 0): [(FOURTH, 2)],
    ("m1", 0): [(HALF, 0)],
    ("k1", 1): [(THIRD, 3)],
    ("k2", 1): [(THIRD, 4)],
    ("k0", 2): [(HALF, 1)],
    ("m", 2): [(FOURTH, 3)],
    ("m1", 2): [(QUARTER, 0)],
    ("m2", 2): [(HALF, 2), (FOURTH, 4)],
    ("k0", 3): [(FOURTH, 5)],
    ("m", 3): [(LEVEL, 0), (QUARTER, 1)],
    ("k", 4): [(HALF, 3)],
    ("k2", 4): [(LEVEL, 1)],
    ("l", 4): [(QUARTER, 2)],
    ("k", 5): [(LAST, 0)],
    ("k0", 5): [(LEVEL, 2)],
    ("k1", 5): [(QUARTER, 3)],
    ("k2", 5): [(HALF, 4)],
    ("m", 5): [(LAST, 1), (LEVEL, 3)],
    "o1": [(QUARTER, 4)],
    "p1": [(HALF, 5)],
    "r": [(LAST, 2), (LEVEL, 4)],
    "t1": [(QUARTER, 5)],
    "u1": [(LAST, 3), (LAST, 4)],
    "x0": [(LEVEL, 5)],
    "z": [(LAST, 5)],
}


def lon_matrix(lon_total, mode_total, snaps, rows):
    places = np.arange(lon_total)
    orders = np.arange(mode_total)
    angles = (places[:, None] * orders[None, :] % lon_total) * (2.0 * math.pi / lon_total)
    doubling = np.where(orders == 0, 1.0, 2.0)
    scaling = 1.0 / math.sqrt(lon_total)
    forward = np.stack([np.cos(angles), -np.sin(angles)], axis=1) * scaling
    inverse = forward * doubling

    def spread(table):
        table = np.einsum(
            "ab,lx,rs->alrbsx", np.eye(snaps), table.reshape(lon_total, -1), np.eye(rows)
        )
        return table.reshape(snaps * lon_total * rows, -1).astype(ml_dtypes.bfloat16)

    return spread(forward), spread(inverse)


def lon_turn(lon_total, rows):
    turn = np.einsum("lk,rs->rlks", np.eye(lon_total), np.eye(rows))
    return turn.reshape(rows, lon_total, lon_total * rows).astype(ml_dtypes.bfloat16)


def lat_matrix(lat_total, mode_total):
    places = np.arange(lat_total)
    angles = (places[:, None] * places[None, :] % lat_total) * (2.0 * math.pi / lat_total)
    cosine, sine = np.cos(angles), np.sin(angles)
    table = np.stack([np.stack([cosine, sine], axis=1), np.stack([-sine, cosine], axis=1)])
    table = np.einsum("pkqr,ab->pakrqb", table / math.sqrt(lat_total), np.eye(mode_total))
    size = 2 * lat_total * mode_total
    return table.reshape(size, size).astype(ml_dtypes.bfloat16)


class Refs:
    pass


def block_body(names, sizes, *refs):
    g = Refs()
    for name, ref in zip(names, refs, strict=True):
        setattr(g, name, ref)
    snaps, group, parts, width = sizes
    levels = group // 2
    tokens = g.fields.shape[0] * g.fields.shape[1]
    channel = g.fields.shape[2]
    owned = channel // group
    half = width // 2
    quarter = width // snaps
    tile = tokens // 3
    short = divisor(tokens // 2, 16, 240)
    packed = g.modes.shape[2]
    strip = divisor(tokens // 2, 48, 144)
    sub = divisor(strip, 16, 48)
    low = jnp.bfloat16
    f32 = jnp.float32

    me_snap = lax.axis_index("snap")
    me_sp = lax.axis_index("sp")
    core = lax.rem(me_sp, 2)
    level = me_sp // 2

    def at(snap, sp):
        return {"snap": snap, "sp": sp}

    def sp_after(step):
        return lax.rem(me_sp + step, group)

    def sp_before(step):
        return lax.rem(me_sp + group - step, group)

    def snap_after(step):
        return lax.rem(me_snap + step, snaps)

    def snap_before(step):
        return lax.rem(me_snap + snaps - step, snaps)

    def level_after(step):
        return lax.rem(level + step, levels)

    def level_before(step):
        return lax.rem(level + levels - step, levels)

    other_core = at(me_snap, me_sp + 1 - 2 * core)

    def send(src, dst, sems, index, target):
        return pltpu.make_async_remote_copy(
            src_ref=src,
            dst_ref=dst,
            send_sem=sems[0].at[index],
            recv_sem=sems[1].at[index],
            device_id=target,
            device_id_type=pl.DeviceIdType.MESH,
        )

    half_tokens = tokens // 2

    def strips(body, first=0, count=tokens, before=None, after=None):
        @pl.loop(0, count // strip)
        def _(step):
            if before is not None:
                before(first // strip + step)
            for at_row in range(0, strip, sub):
                body(pl.ds(pl.multiple_of(first + step * strip + at_row, 16), sub))
            if after is not None:
                after(first // strip + step)

    def half_strips(body, part, **around):
        strips(body, part * half_tokens, half_tokens, **around)

    def strip_copy(near, far, sems, place, out):
        rows = pl.ds(pl.multiple_of(place * strip, strip), strip)
        ends = [near.at[rows], far.reshape(tokens, channel).at[rows]]
        if not out:
            ends.reverse()
        return pltpu.make_async_copy(*ends, sems.at[place])

    def fields_load(place):
        return strip_copy(g.fields_in, g.fields, g.fields_sem, place, False)

    def cot_load(place):
        return strip_copy(g.cot_in, g.cot, g.cot_sem, place, False)

    def out_copy(place):
        return strip_copy(g.fields_in, g.out, g.fields_sem, place, True)

    def grad_copy(place):
        return strip_copy(g.grid, g.in_grad, g.cot_sem, place, True)

    def half_rows(part):
        return slice(part * half_tokens, (part + 1) * half_tokens)

    def fold(value):
        return jnp.sum(value.reshape(-1, 8, value.shape[1]), axis=0)

    loads = {}

    def load(name, index):
        copy = pltpu.make_async_copy(getattr(g, name), getattr(g, name + "_in"), g.load_sem.at[index])
        copy.start()
        loads[name] = copy

    for index, name in enumerate(
        [name for name in names[: names.index("out")] if name not in ("mlp", "fields", "cot")]
    ):
        load(name, index)
    for copy in (fields_load, cot_load):
        for place in range(tokens // strip):
            copy(place).start()

    def master_load(part):
        return pltpu.make_async_copy(
            g.mlp.at[:, :, part * width : (part + 1) * width],
            g.mlp_part.at[part % 2],
            g.load_sem.at[len(loads) + part % 2],
        )

    master_load(0).start()
    master_load(1).start()

    barrier = pltpu.get_barrier_semaphore()
    peers = [at(me_snap, sp_after(step)) for step in range(1, group)]
    peers += [at(snap_after(step), me_sp) for step in range(1, snaps)]
    for peer in peers:
        pl.semaphore_signal(
            barrier, inc=1, device_id=peer, device_id_type=pl.DeviceIdType.MESH
        )

    loads["small"].wait()
    loads["kept"].wait()
    g.own_small[...] = jnp.zeros_like(g.own_small)
    rows_small = g.small.shape[0]
    g.own_small[0:rows_small, 0:owned] = g.small_in[...].astype(low).astype(f32)
    pairs_kept = g.kept.shape[1]
    lines = lax.broadcasted_iota(jnp.int32, (pairs_kept, pairs_kept), 0)
    places = lax.broadcasted_iota(jnp.int32, (pairs_kept, pairs_kept), 1)
    kept = jnp.where(lines == places, g.kept_in[...].astype(f32), 0.0)
    g.own_small[16:, :] = jnp.broadcast_to(
        jnp.sum(kept, axis=1, keepdims=True), (pairs_kept, g.own_small.shape[1])
    )
    pl.semaphore_wait(barrier, len(peers))

    def small_copy(step):
        return send(
            g.own_small, g.all_small.at[me_sp], (g.small_s, g.small_r), step, at(me_snap, sp_after(step))
        )

    for step in range(1, group):
        small_copy(step).start()
    g.all_small[me_sp] = g.own_small[...]

    snap_low = lax.rem(me_snap, 2)
    snap_high = me_snap // 2
    beside_low = me_snap + 1 - 2 * snap_low
    beside_high = me_snap + 2 - 4 * snap_high

    def own_quarter(part):
        odd = lax.rem(part, 2)
        return (1 - odd) * me_snap + odd * (2 * snap_low + snap_high)

    def own_place(part):
        return pl.ds(0, snaps) if part == parts - 1 else own_quarter(part)

    def half_quarters(part):
        return pl.ds(2 * (own_quarter(part) // 2), 2)

    def own_rows(sp):
        return pl.ds(pl.multiple_of(sp * owned, owned), owned)

    def spot(part):
        if isinstance(part, int):
            return part // 2 + parts // 2 * (part % 2)
        return lax.div(part, 2) + parts // 2 * lax.rem(part, 2)

    swaps = (
        (pl.ds(0, 1), own_place(0)),
        (pl.ds(3, 2), own_place(1)),
        (pl.ds(1, 2), own_place(0)),
        (pl.ds(5, 1), own_place(5)),
    )
    swapped = {0: 0, 1: 1, 2: 2, 5: 3}

    def swap_copy(batch):
        some, place = swaps[batch]
        return send(
            g.own_w.at[some, 1 - core, place],
            g.all_w.at[some, 1 - core, place, own_rows(me_sp)],
            (g.swap_s, g.swap_r),
            batch,
            other_core,
        )

    def swap_local(batch):
        some, place = swaps[batch]
        return pltpu.make_async_copy(
            g.own_w.at[some, core, place],
            g.all_w.at[some, core, place, own_rows(me_sp)],
            g.swap_l.at[batch],
        )

    def start_swap(batch):
        swap_copy(batch).start()
        swap_local(batch).start()

    def first_copy(part, step):
        rows = pl.ds(pl.multiple_of(level * 2 * owned, 2 * owned), 2 * owned)
        view = g.all_w.at[spot(part), core, own_place(part), rows]
        target = at(me_snap, 2 * level_after(step) + core)
        return send(view, view, (g.first_s, g.first_r), (part, step), target)

    def second_copy(part):
        odd = lax.rem(part, 2)
        view = g.all_w.at[spot(part), core, own_quarter(part)]
        target = at((1 - odd) * beside_low + odd * beside_high, me_sp)
        return send(view, view, (g.second_s, g.second_r), part, target)

    def third_copy(part):
        odd = lax.rem(part, 2)
        view = g.all_w.at[spot(part), core, half_quarters(part)]
        target = at((1 - odd) * beside_high + odd * beside_low, me_sp)
        return send(view, view, (g.third_s, g.third_r), part, target)

    def fourth_copy(part):
        view = g.all_w.at[spot(part), core]
        return send(view, view, (g.fourth_s, g.fourth_r), part, other_core)

    def start_first(part):
        if part in swapped:
            swap_copy(swapped[part]).wait_recv()
            swap_local(swapped[part]).wait()
        for step in range(1, levels):
            first_copy(part, step).start()

    def wait_first(part):
        for step in range(1, levels):
            first_copy(part, step).wait_recv()

    def pass_second(part):
        wait_first(part)
        second_copy(part).start()

    def pass_third(part):
        second_copy(part).wait_recv()
        third_copy(part).start()

    def pass_fourth(part):
        if part == parts - 1:
            wait_first(part)
        else:
            third_copy(part).wait_recv()
        fourth_copy(part).start()

    stages = {FIRST: start_first, SECOND: pass_second, THIRD: pass_third, FOURTH: pass_fourth}

    def reach(point):
        for stage, part in SCHEDULE.get(point, ()):
            stages[stage](part)

    for part in range(parts):
        master_load(part).wait()
        for place in range(snaps):
            cols = slice(place * quarter, (place + 1) * quarter)
            g.own_w[spot(part), :, place] = g.mlp_part[part % 2, :, :, cols].astype(low)
        if part + 2 < parts:
            master_load(part + 2).start()
        if part == 0:
            start_swap(0)
        elif part == parts - 1:
            for batch in range(1, len(swaps)):
                start_swap(batch)
    reach("a")

    def first_unit(rows):
        values = g.fields_in[rows, :].astype(f32)
        centred = values - jnp.mean(values, axis=-1, keepdims=True)
        scale = lax.rsqrt(jnp.mean(centred * centred, axis=-1, keepdims=True) + eps_norm)
        g.scale_one[rows, :] = scale
        g.grid[rows, :] = centred * scale

    strips(first_unit, before=lambda place: fields_load(place).wait())
    reach("b")
    for step in range(1, group):
        small_copy(step).wait_recv()
    for sp in range(group):
        g.gains[:, sp * owned : (sp + 1) * owned] = g.all_small[sp, 0:16, 0:owned]
        g.keep[sp * pairs_kept : (sp + 1) * pairs_kept, :] = g.all_small[sp, 16:, :]

    def first_norm(rows):
        unit = g.grid[rows, :]
        normed = unit * g.gains[0:1, :] + g.gains[1:2, :]
        g.unit_one[rows, :] = unit.astype(low)
        g.normed[rows, :] = normed.astype(low)
        g.grid[rows, :] = g.fields_in[rows, :].astype(f32) + normed

    half_snaps = g.arrived.shape[0] // 2

    third_rows = packed // 3
    spare = 128 - owned

    def pack(value):
        return jnp.concatenate(
            [
                jnp.concatenate(
                    [
                        value[at_row * third_rows : (at_row + 1) * third_rows],
                        value[packed:, at_row * spare : (at_row + 1) * spare],
                    ],
                    axis=1,
                )
                for at_row in range(3)
            ],
            axis=0,
        ).astype(low)

    def unpack(value):
        value = value.astype(f32)
        rest = [
            value[at_row * third_rows : (at_row + 1) * third_rows, owned:] for at_row in range(3)
        ]
        return jnp.concatenate([value[:, 0:owned], jnp.concatenate(rest, axis=1)], axis=0)

    def block_copy(which, part, step):
        target = sp_after(step)
        return send(
            g.modes.at[part, target],
            g.modes_got.at[part, me_sp],
            (g.block_s, g.block_r),
            (which, part, step),
            at(me_snap, target),
        )

    def row_copy(which, part, step):
        target = sp_after(step)
        return send(
            g.rows_out.at[part, target],
            g.rows_got.at[part, me_sp],
            (g.row_s, g.row_r),
            (which, part, step),
            at(me_snap, target),
        )

    def to_blocks(table, which, part):
        modes = dot_nn(table, g.normed[half_rows(part), :])
        for block in range(group):
            g.modes[part, block] = pack(modes[:, block * owned : (block + 1) * owned])
        for step in range(1, group):
            block_copy(which, part, step).start()
        g.modes_got[part, me_sp] = g.modes[part, me_sp]

    def take_blocks(which, part):
        for step in range(1, group):
            block_copy(which, part, step).wait_recv()
        each = g.arrived.shape[1] // group
        for sp in range(group):
            value = unpack(g.modes_got[part, sp])
            value = jnp.concatenate([value, jnp.zeros((value.shape[0], spare), f32)], axis=1)
            for index in range(half_snaps):
                g.arrived[part * half_snaps + index, sp * each : (sp + 1) * each, :] = value[
                    index * each : (index + 1) * each
                ].astype(low)

    def to_rows(which, part, tables):
        each = tables[0].shape[0] // group
        for sp in range(group):
            value = [table[sp * each : (sp + 1) * each, 0:owned] for table in tables]
            g.rows_out[part, sp] = pack(jnp.concatenate(value, axis=0))
        for step in range(1, group):
            row_copy(which, part, step).start()
        g.rows_got[part, me_sp] = g.rows_out[part, me_sp]

    def home_modes(which, part):
        for step in range(1, group):
            row_copy(which, part, step).wait_recv()
        for block in range(group):
            g.gathered[part, :, block * owned : (block + 1) * owned] = unpack(
                g.rows_got[part, block]
            )
        g.home_low[part] = g.gathered[part].astype(low)

    loads["lon_f"].wait()
    for part in range(2):
        half_strips(first_norm, part)
        reach("c" + str(part))
        to_blocks(g.lon_f_in[...], 0, part)
        reach("d" + str(part))

    loads["filt"].wait()
    for weight, first in ((g.weight_one, 0), (g.weight_two, 2)):
        weight[...] = jnp.zeros_like(weight)
        real = g.filt_in[first].astype(low)
        imag = g.filt_in[first + 1].astype(low)
        weight[0:owned, 0:owned] = real
        weight[128 : 128 + owned, 128 : 128 + owned] = real
        weight[0:owned, 128 : 128 + owned] = imag
        weight[128 : 128 + owned, 0:owned] = -imag

    def bias_row(first):
        return jnp.concatenate(
            [g.own_small[first : first + 1, :], g.own_small[first + 1 : first + 2, :]], axis=1
        )

    for place in range(tokens // strip):
        cot_load(place).wait()
    reach("e")
    loads["lat_f"].wait()
    loads["lat_b"].wait()
    pairs = g.arrived.shape[1] // 2
    half_modes = half_snaps * pairs

    def mode_half(part):
        return slice(part * half_modes, (part + 1) * half_modes)

    def spectra(out, kind, part):
        for snap in range(part * half_snaps, (part + 1) * half_snaps):
            spectrum = dot_nn(g.lat_f_in[...], g.arrived[snap]).astype(kind)
            rows = slice(snap * pairs, (snap + 1) * pairs)
            out[rows, 0:128] = spectrum[0:pairs]
            out[rows, 128:256] = spectrum[pairs:]

    def grids(values):
        tables = []
        for index in range(half_snaps):
            rows = values[index * pairs : (index + 1) * pairs]
            rows = jnp.concatenate([rows[:, 0:128], rows[:, 128:256]], axis=0)
            tables.append(dot_nn(g.lat_b_in[...], rows))
        return tables

    def keep_half():
        keep = jnp.concatenate([g.keep[...], g.keep[...]], axis=1)
        return jnp.concatenate([keep] * half_snaps, axis=0)

    for part in range(2):
        take_blocks(0, part)
        rows = mode_half(part)
        spectra(g.spectrum, low, part)
        g.pre_one[rows, :] = dot_nn(g.spectrum[rows, :], g.weight_one[...]) + bias_row(4)
        g.act_one[rows, :] = gelu_both(g.pre_one[rows, :])[0].astype(low)
        g.pre_two[rows, :] = dot_nn(g.act_one[rows, :], g.weight_two[...]) + bias_row(6)
        to_rows(0, part, grids((shrink(g.pre_two[rows, :]) * keep_half()).astype(low)))
        reach("f" + str(part))
    g.cot_turned[...] = g.cot_in[...].T
    reach("g")

    loads["lon_i"].wait()

    def second_norm(rows):
        values = g.grid[rows, :]
        centred = values - jnp.mean(values, axis=-1, keepdims=True)
        scale = lax.rsqrt(jnp.mean(centred * centred, axis=-1, keepdims=True) + eps_norm)
        centred = centred * scale
        g.unit_two[rows, :] = centred.astype(low)
        g.scale_two[rows, :] = scale
        g.normed[rows, :] = (centred * g.gains[2:3, :] + g.gains[3:4, :]).astype(low)
        g.grid[rows, :] = values + g.gains[8:9, :]
        g.back[rows, :] = jnp.zeros((sub, channel), f32)

    for part in range(2):
        home_modes(0, part)
        g.grid[half_rows(part), :] += dot_nn(g.lon_i_in[...], g.home_low[part])
        reach("h" + str(part))
        half_strips(second_norm, part)
        reach("i" + str(part))
    g.normed_turned[...] = g.normed[...].T
    reach("j")
    flat = jnp.concatenate([g.gains[9 + row : 10 + row, :] for row in range(rows_small - 9)], axis=1)
    for part in range(parts):
        g.bias[part] = flat[:, part * width : (part + 1) * width]

    def core_copy(part, matrix):
        slot = lax.rem(part, 2)
        return send(
            g.grads.at[matrix, :, 1 - core],
            g.core_got.at[slot, matrix],
            (g.core_s, g.core_r),
            (slot, matrix),
            other_core,
        )

    places_one = (snap_low, snap_high)
    places_two = (snap_high, snap_low)
    beside_one = (beside_low, beside_high)
    beside_two = (beside_high, beside_low)

    def half_copy(part, matrix):
        slot = lax.rem(part, 2)
        place = lax.rem(part, 4)
        return send(
            g.half_out.at[slot, matrix, 1 - places_one[matrix]],
            g.half_got.at[place, matrix],
            (g.half_s, g.half_r),
            (place, matrix),
            at(beside_one[matrix], me_sp),
        )

    def quarter_copy(part, matrix):
        slot = lax.rem(part, 2)
        return send(
            g.quarter_out.at[slot, matrix, 1 - places_two[matrix]],
            g.quarter_got.at[slot, matrix],
            (g.quarter_s, g.quarter_r),
            (slot, matrix),
            at(beside_two[matrix], me_sp),
        )

    def level_copy(part, step):
        slot = lax.rem(part, 2)
        place = lax.rem(part, 4)
        target = level_after(step)
        return send(
            g.level_out.at[slot, target],
            g.level_got.at[place, level],
            (g.level_s, g.level_r),
            (place, step),
            at(me_snap, 2 * target + core),
        )

    def last_copy(part, step):
        view = g.total.at[part, me_snap]
        return send(view, view, (g.last_s, g.last_r), (part, step), at(snap_after(step), me_sp))

    def half_stage(part):
        slot = lax.rem(part, 2)
        for matrix in range(2):

            if part >= 2:
                half_copy(part - 2, matrix).wait_send()

            core_copy(part, matrix).wait_recv()

            @pl.loop(0, levels)
            def _(row, matrix=matrix):
                both = g.grads[matrix, row, core].astype(f32) + g.core_got[
                    slot, matrix, row
                ].astype(f32)
                both = both.astype(low)
                g.half_out[slot, matrix, 0, row] = both[:, 0:half]
                g.half_out[slot, matrix, 1, row] = both[:, half:width]

            half_copy(part, matrix).start()

    def quarter_stage(part):
        slot = lax.rem(part, 2)
        for matrix in range(2):

            if part >= 2:
                quarter_copy(part - 2, matrix).wait_send()

            half_copy(part, matrix).wait_recv()
            for row in range(levels):
                both = g.half_out[slot, matrix, places_one[matrix], row].astype(f32) + g.half_got[
                    lax.rem(part, 4), matrix, row
                ].astype(f32)
                both = both.astype(low)
                g.quarter_out[slot, matrix, 0, row] = both[:, 0:quarter]
                g.quarter_out[slot, matrix, 1, row] = both[:, quarter:half]
            quarter_copy(part, matrix).start()

    def level_stage(part):
        slot = lax.rem(part, 2)

        if part >= 2:
            for step in range(1, levels):
                level_copy(part - 2, step).wait_send()

        for matrix in range(2):
            quarter_copy(part, matrix).wait_recv()
            for row in range(levels):
                both = g.quarter_out[slot, matrix, places_two[matrix], row].astype(
                    f32
                ) + g.quarter_got[slot, matrix, row].astype(f32)
                g.level_out[slot, row, matrix] = both.astype(low)
        for step in range(1, levels):
            level_copy(part, step).start()

    def last_stage(part):
        slot = lax.rem(part, 2)
        for step in range(1, levels):
            level_copy(part, step).wait_recv()
        for matrix in range(2):
            sums = g.level_out[slot, level, matrix].astype(f32)
            for step in range(1, levels):
                sums += g.level_got[lax.rem(part, 4), level_before(step), matrix].astype(f32)
            g.total[part, me_snap, matrix] = sums.astype(low)
        for step in range(1, snaps):
            last_copy(part, step).start()

    stages |= {HALF: half_stage, QUARTER: quarter_stage, LEVEL: level_stage, LAST: last_stage}

    def weight(part, matrix):
        return jnp.concatenate([g.all_w[spot(part), matrix, place] for place in range(snaps)], axis=1)

    def add_products(part, rows):
        g.grid[rows, :] += dot_nt(g.act[rows, :], weight(part, 1))
        g.back[rows, :] += dot_nt(g.slope[rows, :], weight(part, 0))

    @pl.loop(0, parts)
    def _(part):
        def reach_in(point, also=True):
            for at_part in range(parts):
                if (point, at_part) in SCHEDULE:
                    pl.when((part == at_part) & also)(functools.partial(reach, (point, at_part)))

        def tile_rows(step):
            return pl.ds(pl.multiple_of(step * tile, tile), tile)

        fourth_copy(part).wait_recv()
        reach_in("k")
        g.grad_bias[part] = jnp.zeros(g.grad_bias.shape[1:], f32)

        @pl.loop(0, tokens // tile)
        def _(step):
            rows = tile_rows(step)
            act, slope = gelu_both(dot_nn(g.normed[rows, :], weight(part, 0)) + g.bias[part])
            g.act[rows, :] = act.astype(low)
            slope = (dot_nn(g.cot_in[rows, :], weight(part, 1)) * slope).astype(low)
            g.slope[rows, :] = slope
            g.grad_bias[part] += fold(slope.astype(f32))
            for at_step in range(tokens // tile):
                reach_in("k" + str(at_step), step == at_step)

        reach_in("l")

        @pl.when(part >= 1)
        def _():
            for matrix in range(2):
                core_copy(part - 1, matrix).wait_send()

        shape = g.grads.shape[1:]
        g.grads[0] = dot_nn(g.normed_turned[...], g.slope[...]).astype(low).reshape(shape)
        core_copy(part, 0).start()
        g.grads[1] = dot_nn(g.cot_turned[...], g.act[...]).astype(low).reshape(shape)
        core_copy(part, 1).start()
        reach_in("m")

        @pl.when(part < parts - 1)
        def _():
            @pl.loop(0, tokens // tile)
            def _(step):
                add_products(part, tile_rows(step))
                for at_step in range(tokens // tile):
                    reach_in("m" + str(at_step), step == at_step)

    g.folds[...] = jnp.zeros_like(g.folds)

    def second_back(rows):
        grad = g.back[rows, :]
        unit = g.unit_two[rows, :].astype(f32)
        cot = g.cot_in[rows, :].astype(f32)
        pulled = grad * g.gains[2:3, :]
        middle = jnp.mean(pulled, axis=-1, keepdims=True)
        slant = jnp.mean(pulled * unit, axis=-1, keepdims=True)
        total = cot + g.scale_two[rows, :] * (pulled - middle - unit * slant)
        g.back[rows, :] = total
        g.normed[rows, :] = total.astype(low)
        g.folds[2] += fold(grad * unit)
        g.folds[3] += fold(grad)
        g.folds[4] += fold(cot)

    loads["lon_it"].wait()
    for part in range(2):

        @pl.loop(0, half_tokens // short)
        def _(step, part=part):
            first_row = part * half_tokens + step * short
            add_products(parts - 1, pl.ds(pl.multiple_of(first_row, 16), short))

        reach("o" + str(part))
        half_strips(second_back, part)
        for step in range(1, group):
            block_copy(0, part, step).wait_send()
        to_blocks(g.lon_it_in[...], 1, part)
        reach("p" + str(part))
    reach("q")

    def low_out(rows):
        g.fields_in[rows, :] = g.grid[rows, :].astype(low)

    strips(low_out, after=lambda place: out_copy(place).start())
    reach("r")
    loads["valid"].wait()
    loads["turn"].wait()
    weigh = sum(
        dot_nn(g.valid_in[:, row, :].astype(f32).astype(low), g.turn_in[row])
        for row in range(g.valid.shape[1])
    )
    places_each = weigh.shape[1]
    precise = lax.Precision.HIGHEST
    sums = [jnp.zeros((1, 128), f32), jnp.zeros((1, 128), f32)]
    for snap in range(g.valid.shape[0]):
        variables = g.grid[snap * places_each : (snap + 1) * places_each, 0:128]
        for index, value in enumerate((variables, variables * variables)):
            sums[index] += jnp.dot(
                weigh[snap : snap + 1, :], value, precision=precise, preferred_element_type=f32
            )

    reach("s")

    def dot_tn(left, right):
        return lax.dot_general(
            left, right, (((0,), (0,)), ((), ())), preferred_element_type=f32
        )

    def filter_rows(first, grad):
        g.pair_grad[...] = grad
        real = g.pair_grad[0:128, 0:128] + g.pair_grad[128:256, 128:256]
        imag = g.pair_grad[0:128, 128:256] - g.pair_grad[128:256, 0:128]
        g.filt_out[me_snap, first] = real[0:owned].astype(low)
        g.filt_out[me_snap, first + 1] = imag[0:owned].astype(low)

    for part in range(2):
        take_blocks(1, part)
        reach("t" + str(part))
        rows = mode_half(part)
        spectra(g.grad_pre, f32, part)
        bend = jnp.tanh(g.pre_two[rows, :] / shrink_level)
        grad = (g.grad_pre[rows, :] * keep_half() * (bend * bend)).astype(low)
        g.grad_two[rows, :] = grad
        grad = dot_nt(grad, g.weight_two[...]) * gelu_both(g.pre_one[rows, :])[1]
        grad = grad.astype(low)
        g.grad_one[rows, :] = grad
        for step in range(1, group):
            row_copy(0, part, step).wait_send()
        to_rows(1, part, grids(dot_nt(grad, g.weight_one[...]).astype(low)))
        reach("u" + str(part))
    reach("v")
    bias_one = jnp.sum(g.grad_one[...].astype(f32), axis=0, keepdims=True)
    bias_two = jnp.sum(g.grad_two[...].astype(f32), axis=0, keepdims=True)
    filter_rows(2, dot_tn(g.act_one[...], g.grad_two[...]))
    filter_rows(0, dot_tn(g.spectrum[...], g.grad_one[...]))

    def filter_copy(step):
        view = g.filt_out.at[me_snap]
        return send(view, view, (g.filt_s, g.filt_r), step, at(snap_after(step), me_sp))

    for step in range(1, snaps):
        filter_copy(step).start()


    reach("w")

    loads["lon_ft"].wait()

    def first_back(rows):
        grad = g.grid[rows, :]
        unit = g.unit_one[rows, :].astype(f32)
        pulled = grad * g.gains[0:1, :]
        middle = jnp.mean(pulled, axis=-1, keepdims=True)
        slant = jnp.mean(pulled * unit, axis=-1, keepdims=True)
        g.grid[rows, :] = g.back[rows, :] + g.scale_one[rows, :] * (
            pulled - middle - unit * slant
        )
        g.folds[0] += fold(grad * unit)
        g.folds[1] += fold(grad)

    for part in range(2):
        home_modes(1, part)
        reach("x" + str(part))
        g.grid[half_rows(part), :] = g.back[half_rows(part), :] + dot_nn(
            g.lon_ft_in[...], g.home_low[part]
        )
        half_strips(first_back, part, after=lambda place: grad_copy(place).start())
        reach("y" + str(part))

    g.grad_rows[...] = jnp.zeros_like(g.grad_rows)
    for index, row in enumerate((0, 1, 2, 3, 8)):
        g.grad_rows[row : row + 1, :] = jnp.sum(g.folds[index], axis=0, keepdims=True)
    flat = jnp.concatenate(
        [jnp.sum(g.grad_bias[part], axis=0, keepdims=True) for part in range(parts)], axis=1
    )
    for row in range(rows_small - 9):
        g.grad_rows[9 + row : 10 + row, :] = flat[:, row * channel : (row + 1) * channel]
    for block in range(group):
        g.tiles[block] = jnp.zeros(g.tiles.shape[1:], f32)
        g.tiles[block, :, 0:owned] = g.grad_rows[:, block * owned : (block + 1) * owned]
        g.tiles[block, 13:14, :] = sums[0]
        g.tiles[block, 14:15, :] = sums[1]

    def tile_copy(step):
        target = sp_after(step)
        return send(
            g.tiles.at[target], g.tiles_got.at[me_sp], (g.tile_s, g.tile_r), step, at(me_snap, target)
        )

    def snap_tile_copy(step):
        view = g.snap_tiles.at[me_snap]
        return send(view, view, (g.snap_tile_s, g.snap_tile_r), step, at(snap_after(step), me_sp))

    for step in range(1, group):
        tile_copy(step).start()
    reach("z")

    for batch in range(len(swaps)):
        swap_copy(batch).wait_send()
    for part in range(parts):
        if part < parts - 1:
            second_copy(part).wait_send()
            third_copy(part).wait_send()
        fourth_copy(part).wait_send()
        for step in range(1, levels):
            first_copy(part, step).wait_send()
    for step in range(1, group):
        small_copy(step).wait_send()
        for part in range(2):
            block_copy(1, part, step).wait_send()
            row_copy(1, part, step).wait_send()
    for matrix in range(2):
        core_copy(parts - 1, matrix).wait_send()
        for part in (parts - 2, parts - 1):
            half_copy(part, matrix).wait_send()
            quarter_copy(part, matrix).wait_send()
    for step in range(1, levels):
        level_copy(parts - 2, step).wait_send()
    for step in range(1, snaps):
        filter_copy(step).wait_send()

    g.tiles_got[me_sp] = g.tiles[me_sp]
    for step in range(1, group):
        tile_copy(step).wait_recv()
    tile_sum = g.tiles_got[0]
    for sp in range(1, group):
        tile_sum += g.tiles_got[sp]
    g.snap_tiles[me_snap] = tile_sum
    g.snap_tiles[me_snap, 4:5, :] = bias_one[:, 0:128]
    g.snap_tiles[me_snap, 5:6, :] = bias_one[:, 128:256]
    g.snap_tiles[me_snap, 6:7, :] = bias_two[:, 0:128]
    g.snap_tiles[me_snap, 7:8, :] = bias_two[:, 128:256]
    for step in range(1, snaps):
        snap_tile_copy(step).start()

    for step in range(1, snaps):
        filter_copy(step).wait_recv()
    filter_sum = g.filt_out[0].astype(f32)
    for snap in range(1, snaps):
        filter_sum += g.filt_out[snap].astype(f32)
    g.grad_filt[...] = filter_sum
    for part in range(parts):
        for step in range(1, snaps):
            last_copy(part, step).wait_recv()
    grads_out = pltpu.make_async_copy(g.total, g.grad_mlp, g.load_sem.at[3])
    grads_out.start()
    for step in range(1, snaps):
        snap_tile_copy(step).wait_recv()
    tile_sum = g.snap_tiles[0]
    for snap in range(1, snaps):
        tile_sum += g.snap_tiles[snap]
    g.grad_small[...] = tile_sum

    grads_out.wait()
    for place in range(tokens // strip):
        out_copy(place).wait()
        grad_copy(place).wait()
    for step in range(1, levels):
        level_copy(parts - 1, step).wait_send()
    for step in range(1, group):
        tile_copy(step).wait_send()
    for step in range(1, snaps):
        snap_tile_copy(step).wait_send()
        for part in range(parts):
            last_copy(part, step).wait_send()


def block_pass(fields, cot, valid, kept, mlp, filt, small, snaps, group):
    snap_local, row_local, lon_total, channel = fields.shape
    tokens = snap_local * row_local * lon_total
    hidden = mlp.shape[2]
    lat_total = row_local * group
    modes = kept.shape[1] * group
    owned = channel // group
    width = 512
    parts = hidden // width
    levels = group // 2
    quarter = width // snaps
    low, f32 = jnp.bfloat16, jnp.float32
    half = width // 2
    half_snaps = snap_local // 2
    lon_f, lon_i = lon_matrix(lon_total, modes, half_snaps, row_local)

    def paired(array):
        return jnp.transpose(array, (0, 2, 1, 3)).reshape(-1, row_local, channel)

    lat_f = lat_matrix(lat_total, modes)
    pair = 2 * modes * row_local
    spread = half_snaps * row_local * 2 * modes
    inputs = dict(
        small=small,
        kept=kept.T,
        fields=paired(fields),
        lon_f=jnp.asarray(np.ascontiguousarray(lon_f.T)),
        filt=filt,
        lat_f=jnp.asarray(lat_f),
        lat_b=jnp.asarray(np.ascontiguousarray(lat_f.T)),
        cot=paired(cot),
        lon_i=jnp.asarray(lon_i),
        valid=valid,
        turn=jnp.asarray(lon_turn(lon_total, row_local)),
        lon_it=jnp.asarray(np.ascontiguousarray(lon_i.T)),
        lon_ft=jnp.asarray(lon_f),
        mlp=mlp,
    )
    outputs = dict(
        out=jax.ShapeDtypeStruct((tokens // row_local, row_local, channel), low),
        in_grad=jax.ShapeDtypeStruct((tokens // row_local, row_local, channel), f32),
        grad_mlp=jax.ShapeDtypeStruct((parts, snaps, 2, owned, quarter), low),
        grad_filt=jax.ShapeDtypeStruct((4, owned, 128), f32),
        grad_small=jax.ShapeDtypeStruct((16, 128), f32),
    )
    vmem = pltpu.VMEM
    dma = pltpu.SemaphoreType.DMA
    scratch = {
        name + "_in": vmem(value.shape, value.dtype)
        for name, value in inputs.items()
        if name not in ("mlp", "fields", "cot")
    }
    strip = divisor(tokens // 2, 48, 144)
    scratch |= dict(
        mlp_part=vmem((2, 2, owned, width), f32),
        fields_in=vmem((tokens, channel), low),
        fields_sem=dma((tokens // strip,)),
        cot_sem=dma((tokens // strip,)),
        cot_in=vmem((tokens, channel), low),
        grid=vmem((tokens, channel), f32),
        back=vmem((tokens, channel), f32),
        normed=vmem((tokens, channel), low),
        normed_turned=vmem((channel, tokens), low),
        cot_turned=vmem((channel, tokens), low),
        unit_one=vmem((tokens, channel), low),
        unit_two=vmem((tokens, channel), low),
        scale_one=vmem((tokens, 1), f32),
        scale_two=vmem((tokens, 1), f32),
        own_small=vmem((16 + kept.shape[0], 128), f32),
        all_small=vmem((group, 16 + kept.shape[0], 128), f32),
        gains=vmem((16, channel), f32),
        keep=vmem((lat_total * modes, 128), f32),
        own_w=vmem((parts, 2, snaps, owned, quarter), low),
        all_w=vmem((parts, 2, snaps, channel, quarter), low),
        modes=vmem((2, group, half_snaps * pair * 3 // 4, 128), low),
        modes_got=vmem((2, group, half_snaps * pair * 3 // 4, 128), low),
        rows_out=vmem((2, group, half_snaps * pair * 3 // 4, 128), low),
        rows_got=vmem((2, group, half_snaps * pair * 3 // 4, 128), low),
        arrived=vmem((snap_local, pair * group, 128), low),
        gathered=vmem((2, spread, channel), f32),
        home_low=vmem((2, spread, channel), low),
        weight_one=vmem((256, 256), low),
        weight_two=vmem((256, 256), low),
        spectrum=vmem((snap_local * lat_total * modes, 256), low),
        pre_one=vmem((snap_local * lat_total * modes, 256), f32),
        act_one=vmem((snap_local * lat_total * modes, 256), low),
        pre_two=vmem((snap_local * lat_total * modes, 256), f32),
        grad_pre=vmem((snap_local * lat_total * modes, 256), f32),
        grad_two=vmem((snap_local * lat_total * modes, 256), low),
        grad_one=vmem((snap_local * lat_total * modes, 256), low),
        folds=vmem((5, 8, channel), f32),
        pair_grad=vmem((256, 256), f32),
        act=vmem((tokens, width), low),
        slope=vmem((tokens, width), low),
        bias=vmem((parts, 1, width), f32),
        grad_bias=vmem((parts, 8, width), f32),
        grad_rows=vmem((16, channel), f32),
        grads=vmem((2, levels, 2, owned, width), low),
        core_got=vmem((2, 2, levels, owned, width), low),
        half_out=vmem((2, 2, 2, levels, owned, half), low),
        half_got=vmem((4, 2, levels, owned, half), low),
        quarter_out=vmem((2, 2, 2, levels, owned, quarter), low),
        quarter_got=vmem((2, 2, levels, owned, quarter), low),
        level_out=vmem((2, levels, 2, owned, quarter), low),
        level_got=vmem((4, levels, 2, owned, quarter), low),
        total=vmem((parts, snaps, 2, owned, quarter), low),
        filt_out=vmem((snaps, 4, owned, 128), low),
        tiles=vmem((group, 16, 128), f32),
        tiles_got=vmem((group, 16, 128), f32),
        snap_tiles=vmem((snaps, 16, 128), f32),
        swap_l=dma((4,)),
        load_sem=dma((len(inputs) + 1,)),
    )
    for name, shape in dict(
        small=(group,),
        swap=(4,),
        first=(parts, levels),
        second=(parts,),
        third=(parts,),
        fourth=(parts,),
        block=(2, 2, group),
        row=(2, 2, group),
        core=(2, 2),
        half=(4, 2),
        quarter=(2, 2),
        level=(4, levels),
        last=(parts, snaps),
        filt=(snaps,),
        tile=(group,),
        snap_tile=(snaps,),
    ).items():
        scratch[name + "_s"] = dma(shape)
        scratch[name + "_r"] = dma(shape)
    names = [*inputs, *outputs, *scratch]
    far = pl.BlockSpec(memory_space=pl.ANY)
    near = pl.BlockSpec(memory_space=pltpu.VMEM)
    results = pl.pallas_call(
        functools.partial(block_body, names, (snaps, group, parts, width)),
        in_specs=[far] * len(inputs),
        out_specs=[far, far, far, near, near],
        out_shape=list(outputs.values()),
        scratch_shapes=list(scratch.values()),
        compiler_params=pltpu.CompilerParams(
            collective_id=0, has_side_effects=True, vmem_limit_bytes=VMEM_LIMIT
        ),
        cost_estimate=pl.CostEstimate(
            flops=12 * tokens * channel * hidden,
            bytes_accessed=4 * hidden * channel,
            transcendentals=tokens * hidden,
        ),
        name="block_pass",
    )(*inputs.values())
    return results


def step_body(names, positions, *refs):
    g = Refs()
    for name, ref in zip(names, refs, strict=True):
        setattr(g, name, ref)
    parts, snaps = g.grad_mlp.shape[:2]
    quarter = g.grad_mlp.shape[4]
    width = snaps * quarter
    moments = ("w", "m", "v")
    results = ("new", "first", "second", "copy")

    def part_cols(part):
        return pl.ds(part * width, width)

    def load(part):
        near = [
            pltpu.make_async_copy(
                getattr(g, "mlp_" + kind).at[:, :, part_cols(part)],
                g.near.at[index, part],
                g.near_sem.at[index, part],
            )
            for index, kind in enumerate(moments)
        ]
        near.append(
            pltpu.make_async_copy(g.grad_mlp.at[part], g.grad_near.at[part], g.near_sem.at[3, part])
        )
        return near

    def store(part):
        copies = [
            pltpu.make_async_copy(
                g.near.at[index, part],
                getattr(g, "mlp_" + kind).at[:, :, part_cols(part)],
                g.back_sem.at[index, part],
            )
            for index, kind in enumerate(results[:3])
        ]
        copies.append(
            pltpu.make_async_copy(
                g.low_near.at[part], g.mlp_copy.at[:, :, part_cols(part)], g.back_sem.at[3, part]
            )
        )
        return copies

    coming = [load(part) for part in range(parts)]
    going = [store(part) for part in range(parts)]
    for part in range(parts):
        for copy in coming[part]:
            copy.start()

    def put(prefix, values):
        for kind, value in zip(results, values, strict=True):
            getattr(g, prefix + kind)[...] = value

    owned = g.filt_w.shape[2]
    put(
        "filt_",
        adamw(g.filt_w[...], g.filt_m[...], g.filt_v[...], g.grad_filt[:, :, 0:owned], rate_filter),
    )
    rows = g.small_w.shape[0]
    put(
        "small_",
        adamw(
            g.small_w[...], g.small_m[...], g.small_v[...], g.grad_small[0:rows, 0:owned], rate_small
        ),
    )
    totals = g.grad_small[rows : rows + 2, 0 : g.run.shape[1]]
    g.stats[...] = stat_decay * g.run[...] + (1.0 - stat_decay) * totals / positions

    for part in range(parts):
        for copy in coming[part]:
            copy.wait()

        for matrix, snap in [(matrix, snap) for matrix in range(2) for snap in range(snaps)]:
            place = snap if matrix else 2 * (snap % 2) + snap // 2
            where = (matrix, slice(None), slice(place * quarter, (place + 1) * quarter))
            now = [g.near[(index, part, *where)] for index in range(3)]
            grad = g.grad_near[part, snap, matrix].astype(jnp.float32)
            values = adamw(*now, grad, rate_mlp)
            for index in range(3):
                g.near[(index, part, *where)] = values[index]
            g.low_near[(part, *where)] = values[3]
        for copy in going[part]:
            copy.start()
    for part in range(parts):
        for copy in going[part]:
            copy.wait()


def step_pass(grads, masters, run_stats, positions):
    grad_mlp, grad_filt, grad_small = grads
    mlp, filt, small = masters
    parts = grad_mlp.shape[0]
    width = mlp[0].shape[2] // parts
    f32, low = jnp.float32, jnp.bfloat16
    far = pl.BlockSpec(memory_space=pltpu.HBM)
    near = pl.BlockSpec(memory_space=pltpu.VMEM)
    inputs = dict(grad_mlp=grad_mlp)
    inputs |= dict(zip(("mlp_w", "mlp_m", "mlp_v"), mlp, strict=True))
    far_in = len(inputs)
    inputs |= dict(grad_filt=grad_filt, grad_small=grad_small)
    inputs |= dict(zip(("filt_w", "filt_m", "filt_v"), filt, strict=True))
    inputs |= dict(zip(("small_w", "small_m", "small_v"), small, strict=True))
    inputs |= dict(run=run_stats)
    results = (("new", f32), ("first", f32), ("second", f32), ("copy", low))
    outputs = {"mlp_" + kind: jax.ShapeDtypeStruct(mlp[0].shape, dt) for kind, dt in results}
    far_out = len(outputs)
    outputs |= {"filt_" + kind: jax.ShapeDtypeStruct(filt[0].shape, dt) for kind, dt in results}
    outputs |= {"small_" + kind: jax.ShapeDtypeStruct(small[0].shape, dt) for kind, dt in results}
    outputs |= dict(stats=jax.ShapeDtypeStruct(run_stats.shape, f32))
    scratch = dict(
        near=pltpu.VMEM((3, parts, 2, mlp[0].shape[1], width), f32),
        grad_near=pltpu.VMEM(grad_mlp.shape, low),
        low_near=pltpu.VMEM((parts, 2, mlp[0].shape[1], width), low),
        near_sem=pltpu.SemaphoreType.DMA((4, parts)),
        back_sem=pltpu.SemaphoreType.DMA((4, parts)),
    )
    return pl.pallas_call(
        functools.partial(step_body, [*inputs, *outputs, *scratch], positions),
        in_specs=[far] * far_in + [near] * (len(inputs) - far_in),
        out_specs=[far] * far_out + [near] * (len(outputs) - far_out),
        out_shape=list(outputs.values()),
        scratch_shapes=list(scratch.values()),
        compiler_params=pltpu.CompilerParams(vmem_limit_bytes=VMEM_LIMIT),
        name="step_pass",
    )(*inputs.values())


def per_device_blocks(
    fields,
    cotangent,
    valid_mask,
    kept_modes,
    mlp_master,
    mlp_first,
    mlp_second,
    filter_master,
    filter_first,
    filter_second,
    small_master,
    small_first,
    small_second,
    run_stats,
):
    snaps, group = lax.axis_size("snap"), lax.axis_size("sp")
    out, in_grad, *grads = block_pass(
        fields, cotangent, valid_mask, kept_modes, mlp_master, filter_master, small_master, snaps, group
    )
    snap_local, row_local, lon_total, channel = fields.shape
    positions = snap_local * snaps * row_local * group * lon_total
    stepped = step_pass(
        grads,
        (
            (mlp_master, mlp_first, mlp_second),
            (filter_master, filter_first, filter_second),
            (small_master, small_first, small_second),
        ),
        run_stats,
        positions,
    )
    rows_apart = (snap_local, lon_total, row_local, channel)
    out, in_grad = [
        jnp.transpose(array.reshape(rows_apart), (0, 2, 1, 3)) for array in (out, in_grad)
    ]
    return (out, in_grad, *stepped)


def per_device(*arrays):
    group, snaps = lax.axis_size("sp"), lax.axis_size("snap")
    channel, hidden = arrays[0].shape[3], arrays[4].shape[2]
    by_block = group == BLOCKS and snaps == 4 and arrays[3].shape[1] == 1
    if by_block and hidden == 6 * 512 and channel // group <= 128 and channel % (16 * group) == 0:
        return per_device_blocks(*arrays)
    return per_device_modes(*arrays)


def solution(mesh):
    return jax.shard_map(
        per_device,
        mesh=mesh,
        in_specs=(
            P("snap", "sp", None, None),
            P("snap", "sp", None, None),
            P("snap", "sp", None),
            P(None, "sp"),
            P(None, "sp", None),
            P(None, "sp", None),
            P(None, "sp", None),
            P(None, "sp", None),
            P(None, "sp", None),
            P(None, "sp", None),
            P(None, "sp"),
            P(None, "sp"),
            P(None, "sp"),
            P(),
        ),
        out_specs=(
            P("snap", "sp", None, None),
            P("snap", "sp", None, None),
            P(None, "sp", None),
            P(None, "sp", None),
            P(None, "sp", None),
            P(None, "sp", None),
            P(None, "sp", None),
            P(None, "sp", None),
            P(None, "sp", None),
            P(None, "sp", None),
            P(None, "sp"),
            P(None, "sp"),
            P(None, "sp"),
            P(None, "sp"),
            P(),
        ),
        check_vma=False,
    )
```

```python
import functools
import math

import jax
import jax.numpy as jnp
import ml_dtypes
import numpy as np
from jax import lax
from jax.experimental import pallas as pl
from jax.experimental.pallas import tpu as pltpu
from jax.sharding import PartitionSpec as P

BLOCKS = 8
NVAR = 20
STEP = 10
VMEM_LIMIT = 63 * 1024 * 1024


eps_norm = 1e-06
shrink_level = 0.01
beta_one = 0.5
beta_two = 0.5
adam_eps = 1e-08
decay_rate = 0.01
rate_mlp = 0.03
rate_filter = 0.1
rate_small = 0.2
stat_decay = 0.5


def layer_norm(values, gain_vec, shift_vec):
    centred = values - jnp.mean(values, axis=-1, keepdims=True)
    spread = jnp.mean(centred * centred, axis=-1, keepdims=True)
    return centred * lax.rsqrt(spread + eps_norm) * gain_vec + shift_vec


def shrink(values):
    return values - shrink_level * jnp.tanh(values / shrink_level)


def lon_tables(lon_total, mode_total):
    places = jnp.arange(lon_total, dtype=jnp.int32)
    orders = jnp.arange(mode_total, dtype=jnp.int32)
    angles = (places[:, None] * orders[None, :] % lon_total).astype(jnp.float32) * (
        2.0 * math.pi / lon_total
    )
    scaling = 1.0 / math.sqrt(lon_total)
    forward_tab = jnp.stack([jnp.cos(angles), -jnp.sin(angles)], axis=1) * scaling
    doubling = jnp.where(orders == 0, 1.0, 2.0).astype(jnp.float32)[:, None]
    inverse_tab = (
        jnp.stack([jnp.cos(angles).T * doubling, -jnp.sin(angles).T * doubling], axis=0) * scaling
    )
    return (forward_tab.astype(jnp.bfloat16), inverse_tab.astype(jnp.bfloat16))


def lat_table(lat_total):
    places = jnp.arange(lat_total, dtype=jnp.int32)
    angles = (places[:, None] * places[None, :] % lat_total).astype(jnp.float32) * (
        2.0 * math.pi / lat_total
    )
    cosine = jnp.cos(angles)
    sine_part = jnp.sin(angles)
    upper_rows = jnp.stack([cosine, sine_part], axis=1)
    bottom = jnp.stack([-sine_part, cosine], axis=1)
    return (jnp.stack([upper_rows, bottom], axis=0) / math.sqrt(lat_total)).astype(jnp.bfloat16)


def complex_pair(real_part, imag_part):
    return jnp.stack([jnp.stack([real_part, -imag_part]), jnp.stack([imag_part, real_part])])


gelu_scale = math.sqrt(2.0 / math.pi)
gelu_cubic = 0.044715


def gelu_both(value):
    bend = (gelu_scale * gelu_cubic) * (value * value)
    turn = jnp.tanh(value * (gelu_scale + bend))
    half = 0.5 + 0.5 * turn
    slope = half * (1.0 + (value * (1.0 - turn)) * (gelu_scale + 3.0 * bend))
    return value * half, slope


def dot_nt(left, right):
    return lax.dot_general(
        left, right, (((1,), (1,)), ((), ())), preferred_element_type=jnp.float32
    )


def dot_nn(left, right):
    return jnp.dot(left, right, preferred_element_type=jnp.float32)


def divisor(total, unit, most):
    return max(size for size in range(unit, most + 1, unit) if total % size == 0)


def mlp_body(
    tile,
    normed_ref,
    cot_ref,
    up_ref,
    down_ref,
    bias_ref,
    out_ref,
    back_ref,
    grad_up_ref,
    grad_down_ref,
    grad_bias_ref,
    normed_turned,
    cot_turned,
    act_ref,
    slope_ref,
):
    tokens = normed_ref.shape[0]

    @pl.when(pl.program_id(0) == 0)
    def _():
        normed_turned[...] = normed_ref[...].T
        cot_turned[...] = cot_ref[...].T
        out_ref[...] = jnp.zeros_like(out_ref)
        back_ref[...] = jnp.zeros_like(back_ref)

    grad_bias_ref[...] = jnp.zeros_like(grad_bias_ref)

    @pl.loop(0, tokens // tile)
    def _(step):
        rows = pl.ds(pl.multiple_of(step * tile, tile), tile)
        act, slope = gelu_both(dot_nn(normed_ref[rows, :], up_ref[...]) + bias_ref[...])
        act = act.astype(jnp.bfloat16)
        slope = (dot_nn(cot_ref[rows, :], down_ref[...]) * slope).astype(jnp.bfloat16)
        act_ref[rows, :] = act
        slope_ref[rows, :] = slope
        grad_bias_ref[...] += jnp.sum(slope.astype(jnp.float32), axis=0, keepdims=True)
        out_ref[rows, :] += dot_nt(act, down_ref[...])
        back_ref[rows, :] += dot_nt(slope, up_ref[...])

    grad_up_ref[...] = dot_nn(normed_turned[...], slope_ref[...]).astype(grad_up_ref.dtype)
    grad_down_ref[...] = dot_nn(cot_turned[...], act_ref[...]).astype(grad_down_ref.dtype)


def mlp_pass(normed, cot, weights, bias):
    tokens, channel = normed.shape
    hidden = weights.shape[2]
    width = divisor(hidden, 128, 512)
    tile = divisor(tokens, 16, 480)
    whole = pl.BlockSpec((tokens, channel), lambda j: (0, 0))
    block = pl.BlockSpec((channel, width), lambda j: (0, j))
    line = pl.BlockSpec((1, width), lambda j: (0, j))
    part = lambda which: pl.BlockSpec((None, channel, width), lambda j: (which, 0, j))
    total = jax.ShapeDtypeStruct((tokens, channel), jnp.float32)
    grads = jax.ShapeDtypeStruct((channel, hidden), jnp.bfloat16)
    return pl.pallas_call(
        functools.partial(mlp_body, tile),
        grid=(hidden // width,),
        in_specs=[whole, whole, part(0), part(1), line],
        out_specs=[whole, whole, block, block, line],
        out_shape=[total, total, grads, grads, jax.ShapeDtypeStruct((1, hidden), jnp.float32)],
        scratch_shapes=[
            pltpu.VMEM((channel, tokens), jnp.bfloat16),
            pltpu.VMEM((channel, tokens), jnp.bfloat16),
            pltpu.VMEM((tokens, width), jnp.bfloat16),
            pltpu.VMEM((tokens, width), jnp.bfloat16),
        ],
        compiler_params=pltpu.CompilerParams(vmem_limit_bytes=56 * 1024 * 1024),
        cost_estimate=pl.CostEstimate(
            flops=12 * tokens * channel * hidden,
            bytes_accessed=8 * channel * hidden + 12 * tokens * channel,
            transcendentals=tokens * hidden,
        ),
        name="mlp_pass",
    )(normed, cot, weights, weights, bias)


def spectral_front(arrived, lat_fwd, first_pair, second_pair, bias_one, bias_two):
    spectrum = jnp.einsum(
        "pkqr,nrqmd->nkpmd", lat_fwd, arrived, preferred_element_type=jnp.float32
    ).astype(jnp.bfloat16)
    snap_local, lat_total, pair_count, mode_local, channel = spectrum.shape
    blocked = spectrum.reshape(
        snap_local, lat_total, pair_count, mode_local, BLOCKS, channel // BLOCKS
    )
    pre_one = (
        jnp.einsum("nkqmbi,pqbio->nkpmbo", blocked, first_pair, preferred_element_type=jnp.float32)
        + bias_one
    )
    act_one = jax.nn.gelu(pre_one).astype(jnp.bfloat16)
    pre_two = (
        jnp.einsum("nkqmbi,pqbio->nkpmbo", act_one, second_pair, preferred_element_type=jnp.float32)
        + bias_two
    )
    return (blocked, pre_one, act_one, pre_two)


def adamw(master, first_mom, second_mom, gradient, step_rate):
    first_next = beta_one * first_mom + (1.0 - beta_one) * gradient
    second_next = beta_two * second_mom + (1.0 - beta_two) * gradient * gradient
    fix_one = 1.0 / (1.0 - beta_one**STEP)
    fix_two = 1.0 / (1.0 - beta_two**STEP)
    direction = first_next * fix_one / (jnp.sqrt(second_next * fix_two) + adam_eps)
    master_next = master - step_rate * (direction + decay_rate * master)
    return (master_next, first_next, second_next, master_next.astype(jnp.bfloat16))


def per_device_modes(
    fields,
    cotangent,
    valid_mask,
    kept_modes,
    mlp_master,
    mlp_first,
    mlp_second,
    filter_master,
    filter_first,
    filter_second,
    small_master,
    small_first,
    small_second,
    run_stats,
):
    group_size = lax.axis_size("sp")
    snap_local, row_local, lon_total, channel = fields.shape
    lat_total = row_local * group_size
    mode_local = kept_modes.shape[1]
    mode_total = mode_local * group_size
    block_width = channel // BLOCKS
    lon_fwd, lon_inv = lon_tables(lon_total, mode_total)
    lat_fwd = lat_table(lat_total)
    mlp_w, filt_w, small_w = (
        lax.all_gather(mlp_master.astype(jnp.bfloat16), "sp", axis=1, tiled=True),
        lax.all_gather(filter_master.astype(jnp.bfloat16), "sp", axis=1, tiled=True),
        lax.all_gather(small_master.astype(jnp.bfloat16), "sp", axis=1, tiled=True),
    )
    small_f = small_w.astype(jnp.float32)
    weights = filt_w.reshape(4, BLOCKS, block_width, block_width)
    first_pair = complex_pair(weights[0], weights[1])
    second_pair = complex_pair(weights[2], weights[3])
    bias_one = small_f[4:6].reshape(2, 1, BLOCKS, block_width)
    bias_two = small_f[6:8].reshape(2, 1, BLOCKS, block_width)
    fields_float = fields.astype(jnp.float32)
    normed, norm_pull = jax.vjp(layer_norm, fields_float, small_f[0], small_f[1])
    normed_low = normed.astype(jnp.bfloat16)
    spec_lon = jnp.einsum(
        "nrld,lqm->nrqmd", normed_low, lon_fwd, preferred_element_type=jnp.float32
    ).astype(jnp.bfloat16)
    arrived = lax.all_to_all(spec_lon, "sp", split_axis=3, concat_axis=1, tiled=True)
    spectral = spectral_front(arrived, lat_fwd, first_pair, second_pair, bias_one, bias_two)
    keep_mask = kept_modes.astype(jnp.float32)[None, :, None, :, None, None]
    masked = (shrink(spectral[3]) * keep_mask).astype(jnp.bfloat16)
    masked = masked.reshape(snap_local, lat_total, 2, mode_local, channel)
    returned = jnp.einsum(
        "pkqr,nkpmd->nrqmd", lat_fwd, masked, preferred_element_type=jnp.float32
    ).astype(jnp.bfloat16)
    home_modes = lax.all_to_all(returned, "sp", split_axis=1, concat_axis=3, tiled=True)
    filtered = jnp.einsum(
        "nrqmd,qml->nrld", home_modes, lon_inv, preferred_element_type=jnp.float32
    )
    mixture = fields_float + normed + filtered
    normed_two, norm_two_pull = jax.vjp(layer_norm, mixture, small_f[2], small_f[3])
    normed_two_low = normed_two.astype(jnp.bfloat16)
    tokens = snap_local * row_local * lon_total
    passed = mlp_pass(
        normed_two_low.reshape(tokens, channel),
        cotangent.reshape(tokens, channel),
        mlp_w,
        small_f[9:].reshape(1, -1),
    )
    output = mixture + passed[0].reshape(mixture.shape) + small_f[8]
    weight_mask = valid_mask.astype(jnp.float32)[..., None]
    variables = output[..., :NVAR]
    local_sums = jnp.stack(
        [
            jnp.sum(weight_mask * variables, axis=(0, 1, 2)),
            jnp.sum(weight_mask * variables * variables, axis=(0, 1, 2)),
        ]
    )
    total_sums = lax.psum(local_sums, ("snap", "sp"))
    positions = snap_local * lax.axis_size("snap") * lat_total * lon_total
    stats_new = stat_decay * run_stats + (1.0 - stat_decay) * total_sums / positions
    cot_float = cotangent.astype(jnp.float32)
    grad_normed_two = passed[1].reshape(mixture.shape)
    grad_bias_hidden = passed[4]
    grad_mix_norm, grad_gain_two, grad_shift_two = norm_two_pull(grad_normed_two)
    grad_mixture = cot_float + grad_mix_norm
    grad_bias_out = jnp.sum(cot_float, axis=(0, 1, 2))
    grad_filtered = grad_mixture.astype(jnp.bfloat16)
    grad_home = jnp.einsum(
        "nrld,qml->nrqmd", grad_filtered, lon_inv, preferred_element_type=jnp.float32
    ).astype(jnp.bfloat16)
    grad_returned = lax.all_to_all(grad_home, "sp", split_axis=3, concat_axis=1, tiled=True)
    grad_masked = jnp.einsum(
        "pkqr,nrqmd->nkpmd", lat_fwd, grad_returned, preferred_element_type=jnp.float32
    )
    arrived_again = lax.all_to_all(spec_lon, "sp", split_axis=3, concat_axis=1, tiled=True)
    used_front = spectral_front(arrived_again, lat_fwd, first_pair, second_pair, bias_one, bias_two)
    blocked, pre_one, act_one, pre_two = used_front
    grad_two = jax.vjp(shrink, pre_two)[1](grad_masked.reshape(pre_two.shape) * keep_mask)[
        0
    ].astype(jnp.bfloat16)
    grad_bias_two = jnp.sum(grad_two.astype(jnp.float32), axis=(0, 1, 3))
    grad_second = jnp.einsum(
        "nkqmbi,nkpmbo->pqbio", act_one, grad_two, preferred_element_type=jnp.float32
    )
    grad_act = jnp.einsum(
        "nkpmbo,pqbio->nkqmbi", grad_two, second_pair, preferred_element_type=jnp.float32
    )
    grad_one = jax.vjp(jax.nn.gelu, pre_one)[1](grad_act)[0].astype(jnp.bfloat16)
    grad_bias_one = jnp.sum(grad_one.astype(jnp.float32), axis=(0, 1, 3))
    grad_first = jnp.einsum(
        "nkqmbi,nkpmbo->pqbio", blocked, grad_one, preferred_element_type=jnp.float32
    )
    grad_spectrum = jnp.einsum(
        "nkpmbo,pqbio->nkqmbi", grad_one, first_pair, preferred_element_type=jnp.float32
    ).astype(jnp.bfloat16)
    grad_spectrum = grad_spectrum.reshape(snap_local, lat_total, 2, mode_local, channel)
    grad_lon = jnp.einsum(
        "pkqr,nkpmd->nrqmd", lat_fwd, grad_spectrum, preferred_element_type=jnp.float32
    ).astype(jnp.bfloat16)
    grad_rows = lax.all_to_all(grad_lon, "sp", split_axis=1, concat_axis=3, tiled=True)
    grad_normed = grad_mixture + jnp.einsum(
        "nrqmd,lqm->nrld", grad_rows, lon_fwd, preferred_element_type=jnp.float32
    )
    grad_field_norm, grad_gain_one, grad_shift_one = norm_pull(grad_normed)
    input_grad = grad_mixture + grad_field_norm
    grad_filter = jnp.stack(
        [
            grad_first[0, 0] + grad_first[1, 1],
            grad_first[1, 0] - grad_first[0, 1],
            grad_second[0, 0] + grad_second[1, 1],
            grad_second[1, 0] - grad_second[0, 1],
        ]
    ).reshape(4, channel, block_width)
    grad_small = jnp.concatenate(
        [
            jnp.stack([grad_gain_one, grad_shift_one, grad_gain_two, grad_shift_two]),
            grad_bias_one.reshape(2, channel),
            grad_bias_two.reshape(2, channel),
            grad_bias_out[None, :],
            grad_bias_hidden.reshape(-1, channel),
        ],
        axis=0,
    )
    shares = (
        jnp.stack([
            lax.psum_scatter(part, "sp", scatter_dimension=0, tiled=True) for part in passed[2:4]
        ]),
        lax.psum_scatter(grad_filter, "sp", scatter_dimension=1, tiled=True),
        lax.psum_scatter(grad_small, "sp", scatter_dimension=1, tiled=True),
    )
    owned = (
        lax.psum(shares[0].astype(jnp.bfloat16), "snap").astype(jnp.float32),
        lax.psum(shares[1].astype(jnp.bfloat16), "snap").astype(jnp.float32),
        lax.psum(shares[2].astype(jnp.bfloat16), "snap").astype(jnp.float32),
    )
    mlp_new, mlp_first_new, mlp_second_new, mlp_copy = adamw(
        mlp_master, mlp_first, mlp_second, owned[0], rate_mlp
    )
    filter_new, filter_first_new, filter_second_new, filter_copy = adamw(
        filter_master, filter_first, filter_second, owned[1], rate_filter
    )
    small_new, small_first_new, small_second_new, small_copy = adamw(
        small_master, small_first, small_second, owned[2], rate_small
    )
    return (
        output.astype(jnp.bfloat16),
        input_grad,
        mlp_new,
        mlp_first_new,
        mlp_second_new,
        mlp_copy,
        filter_new,
        filter_first_new,
        filter_second_new,
        filter_copy,
        small_new,
        small_first_new,
        small_second_new,
        small_copy,
        stats_new,
    )


FIRST, SECOND, THIRD, FOURTH, HALF, QUARTER, LEVEL, LAST = range(8)
SCHEDULE = {
    "a": [(FIRST, 0), (FIRST, 1)],
    "c0": [(SECOND, 0)],
    "d1": [(SECOND, 1), (FIRST, 2)],
    "f0": [(THIRD, 0)],
    "f1": [(SECOND, 2), (FIRST, 3)],
    "g": [(THIRD, 1)],
    "h0": [(FIRST, 4)],
    "h1": [(FOURTH, 0), (THIRD, 2)],
    ("k2", 0): [(SECOND, 3), (SECOND, 4)],
    ("m", 0): [(FOURTH, 1), (FIRST, 5)],
    ("m0", 0): [(FOURTH, 2)],
    ("m1", 0): [(HALF, 0)],
    ("k1", 1): [(THIRD, 3)],
    ("k2", 1): [(THIRD, 4)],
    ("k0", 2): [(HALF, 1)],
    ("m", 2): [(FOURTH, 3)],
    ("m1", 2): [(QUARTER, 0)],
    ("m2", 2): [(HALF, 2), (FOURTH, 4)],
    ("k0", 3): [(FOURTH, 5)],
    ("m", 3): [(LEVEL, 0), (QUARTER, 1)],
    ("k", 4): [(HALF, 3)],
    ("k2", 4): [(LEVEL, 1)],
    ("l", 4): [(QUARTER, 2)],
    ("k", 5): [(LAST, 0)],
    ("k0", 5): [(LEVEL, 2)],
    ("k1", 5): [(QUARTER, 3)],
    ("k2", 5): [(HALF, 4)],
    ("m", 5): [(LAST, 1), (LEVEL, 3)],
    "o1": [(QUARTER, 4)],
    "p1": [(HALF, 5)],
    "r": [(LAST, 2), (LEVEL, 4)],
    "t1": [(QUARTER, 5)],
    "u1": [(LAST, 3), (LAST, 4)],
    "x0": [(LEVEL, 5)],
    "z": [(LAST, 5)],
}


def lon_matrix(lon_total, mode_total, snaps, rows):
    places = np.arange(lon_total)
    orders = np.arange(mode_total)
    angles = (places[:, None] * orders[None, :] % lon_total) * (2.0 * math.pi / lon_total)
    doubling = np.where(orders == 0, 1.0, 2.0)
    scaling = 1.0 / math.sqrt(lon_total)
    forward = np.stack([np.cos(angles), -np.sin(angles)], axis=1) * scaling
    inverse = forward * doubling

    def spread(table):
        table = np.einsum(
            "ab,lx,rs->alrbsx", np.eye(snaps), table.reshape(lon_total, -1), np.eye(rows)
        )
        return table.reshape(snaps * lon_total * rows, -1).astype(ml_dtypes.bfloat16)

    return spread(forward), spread(inverse)


def lon_turn(lon_total, rows):
    turn = np.einsum("lk,rs->rlks", np.eye(lon_total), np.eye(rows))
    return turn.reshape(rows, lon_total, lon_total * rows).astype(ml_dtypes.bfloat16)


def lat_matrix(lat_total, mode_total):
    places = np.arange(lat_total)
    angles = (places[:, None] * places[None, :] % lat_total) * (2.0 * math.pi / lat_total)
    cosine, sine = np.cos(angles), np.sin(angles)
    table = np.stack([np.stack([cosine, sine], axis=1), np.stack([-sine, cosine], axis=1)])
    table = np.einsum("pkqr,ab->pakrqb", table / math.sqrt(lat_total), np.eye(mode_total))
    size = 2 * lat_total * mode_total
    return table.reshape(size, size).astype(ml_dtypes.bfloat16)


class Refs:
    pass


def block_body(names, sizes, *refs):
    g = Refs()
    for name, ref in zip(names, refs, strict=True):
        setattr(g, name, ref)
    snaps, group, parts, width = sizes
    levels = group // 2
    tokens = g.fields.shape[0] * g.fields.shape[1]
    channel = g.fields.shape[2]
    owned = channel // group
    half = width // 2
    quarter = width // snaps
    tile = tokens // 2
    short = divisor(tokens // 2, 16, 240)
    packed = g.modes.shape[2]
    strip = divisor(tokens // 2, 48, 144)
    sub = divisor(strip, 16, 48)
    low = jnp.bfloat16
    f32 = jnp.float32

    me_snap = lax.axis_index("snap")
    me_sp = lax.axis_index("sp")
    core = lax.rem(me_sp, 2)
    level = me_sp // 2

    def at(snap, sp):
        return {"snap": snap, "sp": sp}

    def sp_after(step):
        return lax.rem(me_sp + step, group)

    def sp_before(step):
        return lax.rem(me_sp + group - step, group)

    def snap_after(step):
        return lax.rem(me_snap + step, snaps)

    def snap_before(step):
        return lax.rem(me_snap + snaps - step, snaps)

    def level_after(step):
        return lax.rem(level + step, levels)

    def level_before(step):
        return lax.rem(level + levels - step, levels)

    other_core = at(me_snap, me_sp + 1 - 2 * core)

    def send(src, dst, sems, index, target):
        return pltpu.make_async_remote_copy(
            src_ref=src,
            dst_ref=dst,
            send_sem=sems[0].at[index],
            recv_sem=sems[1].at[index],
            device_id=target,
            device_id_type=pl.DeviceIdType.MESH,
        )

    half_tokens = tokens // 2

    def strips(body, first=0, count=tokens, before=None, after=None):
        @pl.loop(0, count // strip)
        def _(step):
            if before is not None:
                before(first // strip + step)
            for at_row in range(0, strip, sub):
                body(pl.ds(pl.multiple_of(first + step * strip + at_row, 16), sub))
            if after is not None:
                after(first // strip + step)

    def half_strips(body, part, **around):
        strips(body, part * half_tokens, half_tokens, **around)

    def strip_copy(near, far, sems, place, out):
        rows = pl.ds(pl.multiple_of(place * strip, strip), strip)
        ends = [near.at[rows], far.reshape(tokens, channel).at[rows]]
        if not out:
            ends.reverse()
        return pltpu.make_async_copy(*ends, sems.at[place])

    def fields_load(place):
        return strip_copy(g.fields_in, g.fields, g.fields_sem, place, False)

    def cot_load(place):
        return strip_copy(g.cot_in, g.cot, g.cot_sem, place, False)

    def out_copy(place):
        return strip_copy(g.fields_in, g.out, g.fields_sem, place, True)

    def grad_copy(place):
        return strip_copy(g.grid, g.in_grad, g.cot_sem, place, True)

    def half_rows(part):
        return slice(part * half_tokens, (part + 1) * half_tokens)

    def fold(value):
        return jnp.sum(value.reshape(-1, 8, value.shape[1]), axis=0)

    loads = {}

    def load(name, index):
        copy = pltpu.make_async_copy(getattr(g, name), getattr(g, name + "_in"), g.load_sem.at[index])
        copy.start()
        loads[name] = copy

    for index, name in enumerate(
        [name for name in names[: names.index("out")] if name not in ("mlp", "fields", "cot")]
    ):
        load(name, index)
    for copy in (fields_load, cot_load):
        for place in range(tokens // strip):
            copy(place).start()

    def master_load(part):
        return pltpu.make_async_copy(
            g.mlp.at[:, :, part * width : (part + 1) * width],
            g.mlp_part.at[part % 2],
            g.load_sem.at[len(loads) + part % 2],
        )

    master_load(0).start()
    master_load(1).start()

    barrier = pltpu.get_barrier_semaphore()
    peers = [at(me_snap, sp_after(step)) for step in range(1, group)]
    peers += [at(snap_after(step), me_sp) for step in range(1, snaps)]
    for peer in peers:
        pl.semaphore_signal(
            barrier, inc=1, device_id=peer, device_id_type=pl.DeviceIdType.MESH
        )

    loads["small"].wait()
    loads["kept"].wait()
    g.own_small[...] = jnp.zeros_like(g.own_small)
    rows_small = g.small.shape[0]
    g.own_small[0:rows_small, 0:owned] = g.small_in[...].astype(low).astype(f32)
    pairs_kept = g.kept.shape[1]
    lines = lax.broadcasted_iota(jnp.int32, (pairs_kept, pairs_kept), 0)
    places = lax.broadcasted_iota(jnp.int32, (pairs_kept, pairs_kept), 1)
    kept = jnp.where(lines == places, g.kept_in[...].astype(f32), 0.0)
    g.own_small[16:, :] = jnp.broadcast_to(
        jnp.sum(kept, axis=1, keepdims=True), (pairs_kept, g.own_small.shape[1])
    )
    pl.semaphore_wait(barrier, len(peers))

    def small_copy(step):
        return send(
            g.own_small, g.all_small.at[me_sp], (g.small_s, g.small_r), step, at(me_snap, sp_after(step))
        )

    for step in range(1, group):
        small_copy(step).start()
    g.all_small[me_sp] = g.own_small[...]

    snap_low = lax.rem(me_snap, 2)
    snap_high = me_snap // 2
    beside_low = me_snap + 1 - 2 * snap_low
    beside_high = me_snap + 2 - 4 * snap_high

    def own_quarter(part):
        odd = lax.rem(part, 2)
        return (1 - odd) * me_snap + odd * (2 * snap_low + snap_high)

    def own_place(part):
        return pl.ds(0, snaps) if part == parts - 1 else own_quarter(part)

    def half_quarters(part):
        return pl.ds(2 * (own_quarter(part) // 2), 2)

    def own_rows(sp):
        return pl.ds(pl.multiple_of(sp * owned, owned), owned)

    def spot(part):
        if isinstance(part, int):
            return part // 2 + parts // 2 * (part % 2)
        return lax.div(part, 2) + parts // 2 * lax.rem(part, 2)

    swaps = (
        (pl.ds(0, 1), own_place(0)),
        (pl.ds(3, 2), own_place(1)),
        (pl.ds(1, 2), own_place(0)),
        (pl.ds(5, 1), own_place(5)),
    )
    swapped = {0: 0, 1: 1, 2: 2, 5: 3}

    def swap_copy(batch):
        some, place = swaps[batch]
        return send(
            g.own_w.at[some, 1 - core, place],
            g.all_w.at[some, 1 - core, place, own_rows(me_sp)],
            (g.swap_s, g.swap_r),
            batch,
            other_core,
        )

    def swap_local(batch):
        some, place = swaps[batch]
        return pltpu.make_async_copy(
            g.own_w.at[some, core, place],
            g.all_w.at[some, core, place, own_rows(me_sp)],
            g.swap_l.at[batch],
        )

    def start_swap(batch):
        swap_copy(batch).start()
        swap_local(batch).start()

    def first_copy(part, step):
        rows = pl.ds(pl.multiple_of(level * 2 * owned, 2 * owned), 2 * owned)
        view = g.all_w.at[spot(part), core, own_place(part), rows]
        target = at(me_snap, 2 * level_after(step) + core)
        return send(view, view, (g.first_s, g.first_r), (part, step), target)

    def second_copy(part):
        odd = lax.rem(part, 2)
        view = g.all_w.at[spot(part), core, own_quarter(part)]
        target = at((1 - odd) * beside_low + odd * beside_high, me_sp)
        return send(view, view, (g.second_s, g.second_r), part, target)

    def third_copy(part):
        odd = lax.rem(part, 2)
        view = g.all_w.at[spot(part), core, half_quarters(part)]
        target = at((1 - odd) * beside_high + odd * beside_low, me_sp)
        return send(view, view, (g.third_s, g.third_r), part, target)

    def fourth_copy(part):
        view = g.all_w.at[spot(part), core]
        return send(view, view, (g.fourth_s, g.fourth_r), part, other_core)

    def start_first(part):
        if part in swapped:
            swap_copy(swapped[part]).wait_recv()
            swap_local(swapped[part]).wait()
        for step in range(1, levels):
            first_copy(part, step).start()

    def wait_first(part):
        for step in range(1, levels):
            first_copy(part, step).wait_recv()

    def pass_second(part):
        wait_first(part)
        second_copy(part).start()

    def pass_third(part):
        second_copy(part).wait_recv()
        third_copy(part).start()

    def pass_fourth(part):
        if part == parts - 1:
            wait_first(part)
        else:
            third_copy(part).wait_recv()
        fourth_copy(part).start()

    stages = {FIRST: start_first, SECOND: pass_second, THIRD: pass_third, FOURTH: pass_fourth}

    def reach(point):
        for stage, part in SCHEDULE.get(point, ()):
            stages[stage](part)

    for part in range(parts):
        master_load(part).wait()
        for place in range(snaps):
            cols = slice(place * quarter, (place + 1) * quarter)
            g.own_w[spot(part), :, place] = g.mlp_part[part % 2, :, :, cols].astype(low)
        if part + 2 < parts:
            master_load(part + 2).start()
        if part == 0:
            start_swap(0)
        elif part == parts - 1:
            for batch in range(1, len(swaps)):
                start_swap(batch)
    reach("a")

    def first_unit(rows):
        values = g.fields_in[rows, :].astype(f32)
        centred = values - jnp.mean(values, axis=-1, keepdims=True)
        scale = lax.rsqrt(jnp.mean(centred * centred, axis=-1, keepdims=True) + eps_norm)
        g.scale_one[rows, :] = scale
        g.grid[rows, :] = centred * scale

    strips(first_unit, before=lambda place: fields_load(place).wait())
    reach("b")
    for step in range(1, group):
        small_copy(step).wait_recv()
    for sp in range(group):
        g.gains[:, sp * owned : (sp + 1) * owned] = g.all_small[sp, 0:16, 0:owned]
        g.keep[sp * pairs_kept : (sp + 1) * pairs_kept, :] = g.all_small[sp, 16:, :]

    def first_norm(rows):
        unit = g.grid[rows, :]
        normed = unit * g.gains[0:1, :] + g.gains[1:2, :]
        g.unit_one[rows, :] = unit.astype(low)
        g.normed[rows, :] = normed.astype(low)
        g.grid[rows, :] = g.fields_in[rows, :].astype(f32) + normed

    half_snaps = g.arrived.shape[0] // 2

    third_rows = packed // 3
    spare = 128 - owned

    def pack(value):
        return jnp.concatenate(
            [
                jnp.concatenate(
                    [
                        value[at_row * third_rows : (at_row + 1) * third_rows],
                        value[packed:, at_row * spare : (at_row + 1) * spare],
                    ],
                    axis=1,
                )
                for at_row in range(3)
            ],
            axis=0,
        ).astype(low)

    def unpack(value):
        value = value.astype(f32)
        rest = [
            value[at_row * third_rows : (at_row + 1) * third_rows, owned:] for at_row in range(3)
        ]
        return jnp.concatenate([value[:, 0:owned], jnp.concatenate(rest, axis=1)], axis=0)

    def block_copy(which, part, step):
        target = sp_after(step)
        return send(
            g.modes.at[part, target],
            g.modes_got.at[part, me_sp],
            (g.block_s, g.block_r),
            (which, part, step),
            at(me_snap, target),
        )

    def row_copy(which, part, step):
        target = sp_after(step)
        return send(
            g.rows_out.at[part, target],
            g.rows_got.at[part, me_sp],
            (g.row_s, g.row_r),
            (which, part, step),
            at(me_snap, target),
        )

    def to_blocks(table, which, part):
        modes = dot_nn(table, g.normed[half_rows(part), :])
        for block in range(group):
            g.modes[part, block] = pack(modes[:, block * owned : (block + 1) * owned])
        for step in range(1, group):
            block_copy(which, part, step).start()
        g.modes_got[part, me_sp] = g.modes[part, me_sp]

    def take_blocks(which, part):
        for step in range(1, group):
            block_copy(which, part, step).wait_recv()
        each = g.arrived.shape[1] // group
        for sp in range(group):
            value = unpack(g.modes_got[part, sp])
            value = jnp.concatenate([value, jnp.zeros((value.shape[0], spare), f32)], axis=1)
            for index in range(half_snaps):
                g.arrived[part * half_snaps + index, sp * each : (sp + 1) * each, :] = value[
                    index * each : (index + 1) * each
                ].astype(low)

    def to_rows(which, part, tables):
        each = tables[0].shape[0] // group
        for sp in range(group):
            value = [table[sp * each : (sp + 1) * each, 0:owned] for table in tables]
            g.rows_out[part, sp] = pack(jnp.concatenate(value, axis=0))
        for step in range(1, group):
            row_copy(which, part, step).start()
        g.rows_got[part, me_sp] = g.rows_out[part, me_sp]

    def home_modes(which, part):
        for step in range(1, group):
            row_copy(which, part, step).wait_recv()
        for block in range(group):
            g.gathered[part, :, block * owned : (block + 1) * owned] = unpack(
                g.rows_got[part, block]
            )
        g.home_low[part] = g.gathered[part].astype(low)

    loads["lon_f"].wait()
    for part in range(2):
        half_strips(first_norm, part)
        reach("c" + str(part))
        to_blocks(g.lon_f_in[...], 0, part)
        reach("d" + str(part))

    loads["filt"].wait()
    for weight, first in ((g.weight_one, 0), (g.weight_two, 2)):
        weight[...] = jnp.zeros_like(weight)
        real = g.filt_in[first].astype(low)
        imag = g.filt_in[first + 1].astype(low)
        weight[0:owned, 0:owned] = real
        weight[128 : 128 + owned, 128 : 128 + owned] = real
        weight[0:owned, 128 : 128 + owned] = imag
        weight[128 : 128 + owned, 0:owned] = -imag

    def bias_row(first):
        return jnp.concatenate(
            [g.own_small[first : first + 1, :], g.own_small[first + 1 : first + 2, :]], axis=1
        )

    for place in range(tokens // strip):
        cot_load(place).wait()
    reach("e")
    loads["lat_f"].wait()
    loads["lat_b"].wait()
    pairs = g.arrived.shape[1] // 2
    half_modes = half_snaps * pairs

    def mode_half(part):
        return slice(part * half_modes, (part + 1) * half_modes)

    def spectra(out, kind, part):
        for snap in range(part * half_snaps, (part + 1) * half_snaps):
            spectrum = dot_nn(g.lat_f_in[...], g.arrived[snap]).astype(kind)
            rows = slice(snap * pairs, (snap + 1) * pairs)
            out[rows, 0:128] = spectrum[0:pairs]
            out[rows, 128:256] = spectrum[pairs:]

    def grids(values):
        tables = []
        for index in range(half_snaps):
            rows = values[index * pairs : (index + 1) * pairs]
            rows = jnp.concatenate([rows[:, 0:128], rows[:, 128:256]], axis=0)
            tables.append(dot_nn(g.lat_b_in[...], rows))
        return tables

    def keep_half():
        keep = jnp.concatenate([g.keep[...], g.keep[...]], axis=1)
        return jnp.concatenate([keep] * half_snaps, axis=0)

    for part in range(2):
        take_blocks(0, part)
        rows = mode_half(part)
        spectra(g.spectrum, low, part)
        g.pre_one[rows, :] = dot_nn(g.spectrum[rows, :], g.weight_one[...]) + bias_row(4)
        g.act_one[rows, :] = gelu_both(g.pre_one[rows, :])[0].astype(low)
        g.pre_two[rows, :] = dot_nn(g.act_one[rows, :], g.weight_two[...]) + bias_row(6)
        to_rows(0, part, grids((shrink(g.pre_two[rows, :]) * keep_half()).astype(low)))
        reach("f" + str(part))
    g.cot_turned[...] = g.cot_in[...].T
    reach("g")

    loads["lon_i"].wait()

    def second_norm(rows):
        values = g.grid[rows, :]
        centred = values - jnp.mean(values, axis=-1, keepdims=True)
        scale = lax.rsqrt(jnp.mean(centred * centred, axis=-1, keepdims=True) + eps_norm)
        centred = centred * scale
        g.unit_two[rows, :] = centred.astype(low)
        g.scale_two[rows, :] = scale
        g.normed[rows, :] = (centred * g.gains[2:3, :] + g.gains[3:4, :]).astype(low)
        g.grid[rows, :] = values + g.gains[8:9, :]
        g.back[rows, :] = jnp.zeros((sub, channel), f32)

    for part in range(2):
        home_modes(0, part)
        g.grid[half_rows(part), :] += dot_nn(g.lon_i_in[...], g.home_low[part])
        reach("h" + str(part))
        half_strips(second_norm, part)
        reach("i" + str(part))
    g.normed_turned[...] = g.normed[...].T
    reach("j")
    flat = jnp.concatenate([g.gains[9 + row : 10 + row, :] for row in range(rows_small - 9)], axis=1)
    for part in range(parts):
        g.bias[part] = flat[:, part * width : (part + 1) * width]

    def core_copy(part, matrix):
        slot = lax.rem(part, 2)
        return send(
            g.grads.at[matrix, :, 1 - core],
            g.core_got.at[slot, matrix],
            (g.core_s, g.core_r),
            (slot, matrix),
            other_core,
        )

    places_one = (snap_low, snap_high)
    places_two = (snap_high, snap_low)
    beside_one = (beside_low, beside_high)
    beside_two = (beside_high, beside_low)

    def half_copy(part, matrix):
        slot = lax.rem(part, 2)
        place = lax.rem(part, 4)
        return send(
            g.half_out.at[slot, matrix, 1 - places_one[matrix]],
            g.half_got.at[place, matrix],
            (g.half_s, g.half_r),
            (place, matrix),
            at(beside_one[matrix], me_sp),
        )

    def quarter_copy(part, matrix):
        slot = lax.rem(part, 2)
        return send(
            g.quarter_out.at[slot, matrix, 1 - places_two[matrix]],
            g.quarter_got.at[slot, matrix],
            (g.quarter_s, g.quarter_r),
            (slot, matrix),
            at(beside_two[matrix], me_sp),
        )

    def level_copy(part, step):
        slot = lax.rem(part, 2)
        place = lax.rem(part, 4)
        target = level_after(step)
        return send(
            g.level_out.at[slot, target],
            g.level_got.at[place, level],
            (g.level_s, g.level_r),
            (place, step),
            at(me_snap, 2 * target + core),
        )

    def last_copy(part, step):
        view = g.total.at[part, me_snap]
        return send(view, view, (g.last_s, g.last_r), (part, step), at(snap_after(step), me_sp))

    def half_stage(part):
        slot = lax.rem(part, 2)
        for matrix in range(2):

            if part >= 2:
                half_copy(part - 2, matrix).wait_send()

            core_copy(part, matrix).wait_recv()

            @pl.loop(0, levels)
            def _(row, matrix=matrix):
                both = g.grads[matrix, row, core].astype(f32) + g.core_got[
                    slot, matrix, row
                ].astype(f32)
                both = both.astype(low)
                g.half_out[slot, matrix, 0, row] = both[:, 0:half]
                g.half_out[slot, matrix, 1, row] = both[:, half:width]

            half_copy(part, matrix).start()

    def quarter_stage(part):
        slot = lax.rem(part, 2)
        for matrix in range(2):

            if part >= 2:
                quarter_copy(part - 2, matrix).wait_send()

            half_copy(part, matrix).wait_recv()
            for row in range(levels):
                both = g.half_out[slot, matrix, places_one[matrix], row].astype(f32) + g.half_got[
                    lax.rem(part, 4), matrix, row
                ].astype(f32)
                both = both.astype(low)
                g.quarter_out[slot, matrix, 0, row] = both[:, 0:quarter]
                g.quarter_out[slot, matrix, 1, row] = both[:, quarter:half]
            quarter_copy(part, matrix).start()

    def level_stage(part):
        slot = lax.rem(part, 2)

        if part >= 2:
            for step in range(1, levels):
                level_copy(part - 2, step).wait_send()

        for matrix in range(2):
            quarter_copy(part, matrix).wait_recv()
            for row in range(levels):
                both = g.quarter_out[slot, matrix, places_two[matrix], row].astype(
                    f32
                ) + g.quarter_got[slot, matrix, row].astype(f32)
                g.level_out[slot, row, matrix] = both.astype(low)
        for step in range(1, levels):
            level_copy(part, step).start()

    def last_stage(part):
        slot = lax.rem(part, 2)
        for step in range(1, levels):
            level_copy(part, step).wait_recv()
        for matrix in range(2):
            sums = g.level_out[slot, level, matrix].astype(f32)
            for step in range(1, levels):
                sums += g.level_got[lax.rem(part, 4), level_before(step), matrix].astype(f32)
            g.total[part, me_snap, matrix] = sums.astype(low)
        for step in range(1, snaps):
            last_copy(part, step).start()

    stages |= {HALF: half_stage, QUARTER: quarter_stage, LEVEL: level_stage, LAST: last_stage}

    def weight(part, matrix):
        return jnp.concatenate([g.all_w[spot(part), matrix, place] for place in range(snaps)], axis=1)

    def add_products(part, rows):
        g.grid[rows, :] += dot_nt(g.act[rows, :], weight(part, 1))
        g.back[rows, :] += dot_nt(g.slope[rows, :], weight(part, 0))

    @pl.loop(0, parts)
    def _(part):
        def reach_in(point, also=True):
            for at_part in range(parts):
                if (point, at_part) in SCHEDULE:
                    pl.when((part == at_part) & also)(functools.partial(reach, (point, at_part)))

        def tile_rows(step):
            return pl.ds(pl.multiple_of(step * tile, tile), tile)

        fourth_copy(part).wait_recv()
        reach_in("k")
        g.grad_bias[part] = jnp.zeros(g.grad_bias.shape[1:], f32)

        @pl.loop(0, tokens // tile)
        def _(step):
            rows = tile_rows(step)
            act, slope = gelu_both(dot_nn(g.normed[rows, :], weight(part, 0)) + g.bias[part])
            g.act[rows, :] = act.astype(low)
            slope = (dot_nn(g.cot_in[rows, :], weight(part, 1)) * slope).astype(low)
            g.slope[rows, :] = slope
            g.grad_bias[part] += fold(slope.astype(f32))
            for at_step in range(3):
                reach_in("k" + str(at_step), step == (at_step + 1) // 2)

        reach_in("l")

        @pl.when(part >= 1)
        def _():
            for matrix in range(2):
                core_copy(part - 1, matrix).wait_send()

        shape = g.grads.shape[1:]
        g.grads[0] = dot_nn(g.normed_turned[...], g.slope[...]).astype(low).reshape(shape)
        core_copy(part, 0).start()
        g.grads[1] = dot_nn(g.cot_turned[...], g.act[...]).astype(low).reshape(shape)
        core_copy(part, 1).start()
        reach_in("m")

        @pl.when(part < parts - 1)
        def _():
            @pl.loop(0, tokens // tile)
            def _(step):
                add_products(part, tile_rows(step))
                for at_step in range(3):
                    reach_in("m" + str(at_step), step == (at_step + 1) // 2)

    g.folds[...] = jnp.zeros_like(g.folds)

    def second_back(rows):
        grad = g.back[rows, :]
        unit = g.unit_two[rows, :].astype(f32)
        cot = g.cot_in[rows, :].astype(f32)
        pulled = grad * g.gains[2:3, :]
        middle = jnp.mean(pulled, axis=-1, keepdims=True)
        slant = jnp.mean(pulled * unit, axis=-1, keepdims=True)
        total = cot + g.scale_two[rows, :] * (pulled - middle - unit * slant)
        g.back[rows, :] = total
        g.normed[rows, :] = total.astype(low)
        g.folds[2] += fold(grad * unit)
        g.folds[3] += fold(grad)
        g.folds[4] += fold(cot)

    loads["lon_it"].wait()
    for part in range(2):

        @pl.loop(0, half_tokens // short)
        def _(step, part=part):
            first_row = part * half_tokens + step * short
            add_products(parts - 1, pl.ds(pl.multiple_of(first_row, 16), short))

        reach("o" + str(part))
        half_strips(second_back, part)
        for step in range(1, group):
            block_copy(0, part, step).wait_send()
        to_blocks(g.lon_it_in[...], 1, part)
        reach("p" + str(part))
    reach("q")

    def low_out(rows):
        g.fields_in[rows, :] = g.grid[rows, :].astype(low)

    strips(low_out, after=lambda place: out_copy(place).start())
    reach("r")
    loads["valid"].wait()
    loads["turn"].wait()
    weigh = sum(
        dot_nn(g.valid_in[:, row, :].astype(f32).astype(low), g.turn_in[row])
        for row in range(g.valid.shape[1])
    )
    places_each = weigh.shape[1]
    precise = lax.Precision.HIGHEST
    sums = [jnp.zeros((1, 128), f32), jnp.zeros((1, 128), f32)]
    for snap in range(g.valid.shape[0]):
        variables = g.grid[snap * places_each : (snap + 1) * places_each, 0:128]
        for index, value in enumerate((variables, variables * variables)):
            sums[index] += jnp.dot(
                weigh[snap : snap + 1, :], value, precision=precise, preferred_element_type=f32
            )

    reach("s")

    def dot_tn(left, right):
        return lax.dot_general(
            left, right, (((0,), (0,)), ((), ())), preferred_element_type=f32
        )

    def filter_rows(first, grad):
        g.pair_grad[...] = grad
        real = g.pair_grad[0:128, 0:128] + g.pair_grad[128:256, 128:256]
        imag = g.pair_grad[0:128, 128:256] - g.pair_grad[128:256, 0:128]
        g.filt_out[me_snap, first] = real[0:owned].astype(low)
        g.filt_out[me_snap, first + 1] = imag[0:owned].astype(low)

    for part in range(2):
        take_blocks(1, part)
        reach("t" + str(part))
        rows = mode_half(part)
        spectra(g.grad_pre, f32, part)
        bend = jnp.tanh(g.pre_two[rows, :] / shrink_level)
        grad = (g.grad_pre[rows, :] * keep_half() * (bend * bend)).astype(low)
        g.grad_two[rows, :] = grad
        grad = dot_nt(grad, g.weight_two[...]) * gelu_both(g.pre_one[rows, :])[1]
        grad = grad.astype(low)
        g.grad_one[rows, :] = grad
        for step in range(1, group):
            row_copy(0, part, step).wait_send()
        to_rows(1, part, grids(dot_nt(grad, g.weight_one[...]).astype(low)))
        reach("u" + str(part))
    reach("v")
    bias_one = jnp.sum(g.grad_one[...].astype(f32), axis=0, keepdims=True)
    bias_two = jnp.sum(g.grad_two[...].astype(f32), axis=0, keepdims=True)
    filter_rows(2, dot_tn(g.act_one[...], g.grad_two[...]))
    filter_rows(0, dot_tn(g.spectrum[...], g.grad_one[...]))

    def filter_copy(step):
        view = g.filt_out.at[me_snap]
        return send(view, view, (g.filt_s, g.filt_r), step, at(snap_after(step), me_sp))

    for step in range(1, snaps):
        filter_copy(step).start()


    reach("w")

    loads["lon_ft"].wait()

    def first_back(rows):
        grad = g.grid[rows, :]
        unit = g.unit_one[rows, :].astype(f32)
        pulled = grad * g.gains[0:1, :]
        middle = jnp.mean(pulled, axis=-1, keepdims=True)
        slant = jnp.mean(pulled * unit, axis=-1, keepdims=True)
        g.grid[rows, :] = g.back[rows, :] + g.scale_one[rows, :] * (
            pulled - middle - unit * slant
        )
        g.folds[0] += fold(grad * unit)
        g.folds[1] += fold(grad)

    for part in range(2):
        home_modes(1, part)
        reach("x" + str(part))
        g.grid[half_rows(part), :] = g.back[half_rows(part), :] + dot_nn(
            g.lon_ft_in[...], g.home_low[part]
        )
        half_strips(first_back, part, after=lambda place: grad_copy(place).start())
        reach("y" + str(part))

    g.grad_rows[...] = jnp.zeros_like(g.grad_rows)
    for index, row in enumerate((0, 1, 2, 3, 8)):
        g.grad_rows[row : row + 1, :] = jnp.sum(g.folds[index], axis=0, keepdims=True)
    flat = jnp.concatenate(
        [jnp.sum(g.grad_bias[part], axis=0, keepdims=True) for part in range(parts)], axis=1
    )
    for row in range(rows_small - 9):
        g.grad_rows[9 + row : 10 + row, :] = flat[:, row * channel : (row + 1) * channel]
    for block in range(group):
        g.tiles[block] = jnp.zeros(g.tiles.shape[1:], f32)
        g.tiles[block, :, 0:owned] = g.grad_rows[:, block * owned : (block + 1) * owned]
        g.tiles[block, 13:14, :] = sums[0]
        g.tiles[block, 14:15, :] = sums[1]

    def tile_copy(step):
        target = sp_after(step)
        return send(
            g.tiles.at[target], g.tiles_got.at[me_sp], (g.tile_s, g.tile_r), step, at(me_snap, target)
        )

    def snap_tile_copy(step):
        view = g.snap_tiles.at[me_snap]
        return send(view, view, (g.snap_tile_s, g.snap_tile_r), step, at(snap_after(step), me_sp))

    for step in range(1, group):
        tile_copy(step).start()
    reach("z")

    for batch in range(len(swaps)):
        swap_copy(batch).wait_send()
    for part in range(parts):
        if part < parts - 1:
            second_copy(part).wait_send()
            third_copy(part).wait_send()
        fourth_copy(part).wait_send()
        for step in range(1, levels):
            first_copy(part, step).wait_send()
    for step in range(1, group):
        small_copy(step).wait_send()
        for part in range(2):
            block_copy(1, part, step).wait_send()
            row_copy(1, part, step).wait_send()
    for matrix in range(2):
        core_copy(parts - 1, matrix).wait_send()
        for part in (parts - 2, parts - 1):
            half_copy(part, matrix).wait_send()
            quarter_copy(part, matrix).wait_send()
    for step in range(1, levels):
        level_copy(parts - 2, step).wait_send()
    for step in range(1, snaps):
        filter_copy(step).wait_send()

    g.tiles_got[me_sp] = g.tiles[me_sp]
    for step in range(1, group):
        tile_copy(step).wait_recv()
    tile_sum = g.tiles_got[0]
    for sp in range(1, group):
        tile_sum += g.tiles_got[sp]
    g.snap_tiles[me_snap] = tile_sum
    g.snap_tiles[me_snap, 4:5, :] = bias_one[:, 0:128]
    g.snap_tiles[me_snap, 5:6, :] = bias_one[:, 128:256]
    g.snap_tiles[me_snap, 6:7, :] = bias_two[:, 0:128]
    g.snap_tiles[me_snap, 7:8, :] = bias_two[:, 128:256]
    for step in range(1, snaps):
        snap_tile_copy(step).start()

    for step in range(1, snaps):
        filter_copy(step).wait_recv()
    filter_sum = g.filt_out[0].astype(f32)
    for snap in range(1, snaps):
        filter_sum += g.filt_out[snap].astype(f32)
    g.grad_filt[...] = filter_sum
    for part in range(parts):
        for step in range(1, snaps):
            last_copy(part, step).wait_recv()
    grads_out = pltpu.make_async_copy(g.total, g.grad_mlp, g.load_sem.at[3])
    grads_out.start()
    for step in range(1, snaps):
        snap_tile_copy(step).wait_recv()
    tile_sum = g.snap_tiles[0]
    for snap in range(1, snaps):
        tile_sum += g.snap_tiles[snap]
    g.grad_small[...] = tile_sum

    grads_out.wait()
    for place in range(tokens // strip):
        out_copy(place).wait()
        grad_copy(place).wait()
    for step in range(1, levels):
        level_copy(parts - 1, step).wait_send()
    for step in range(1, group):
        tile_copy(step).wait_send()
    for step in range(1, snaps):
        snap_tile_copy(step).wait_send()
        for part in range(parts):
            last_copy(part, step).wait_send()


def block_pass(fields, cot, valid, kept, mlp, filt, small, snaps, group):
    snap_local, row_local, lon_total, channel = fields.shape
    tokens = snap_local * row_local * lon_total
    hidden = mlp.shape[2]
    lat_total = row_local * group
    modes = kept.shape[1] * group
    owned = channel // group
    width = 512
    parts = hidden // width
    levels = group // 2
    quarter = width // snaps
    low, f32 = jnp.bfloat16, jnp.float32
    half = width // 2
    half_snaps = snap_local // 2
    lon_f, lon_i = lon_matrix(lon_total, modes, half_snaps, row_local)

    def paired(array):
        return jnp.transpose(array, (0, 2, 1, 3)).reshape(-1, row_local, channel)

    lat_f = lat_matrix(lat_total, modes)
    pair = 2 * modes * row_local
    spread = half_snaps * row_local * 2 * modes
    inputs = dict(
        small=small,
        kept=kept.T,
        fields=paired(fields),
        lon_f=jnp.asarray(np.ascontiguousarray(lon_f.T)),
        filt=filt,
        lat_f=jnp.asarray(lat_f),
        lat_b=jnp.asarray(np.ascontiguousarray(lat_f.T)),
        cot=paired(cot),
        lon_i=jnp.asarray(lon_i),
        valid=valid,
        turn=jnp.asarray(lon_turn(lon_total, row_local)),
        lon_it=jnp.asarray(np.ascontiguousarray(lon_i.T)),
        lon_ft=jnp.asarray(lon_f),
        mlp=mlp,
    )
    outputs = dict(
        out=jax.ShapeDtypeStruct((tokens // row_local, row_local, channel), low),
        in_grad=jax.ShapeDtypeStruct((tokens // row_local, row_local, channel), f32),
        grad_mlp=jax.ShapeDtypeStruct((parts, snaps, 2, owned, quarter), low),
        grad_filt=jax.ShapeDtypeStruct((4, owned, 128), f32),
        grad_small=jax.ShapeDtypeStruct((16, 128), f32),
    )
    vmem = pltpu.VMEM
    dma = pltpu.SemaphoreType.DMA
    scratch = {
        name + "_in": vmem(value.shape, value.dtype)
        for name, value in inputs.items()
        if name not in ("mlp", "fields", "cot")
    }
    strip = divisor(tokens // 2, 48, 144)
    scratch |= dict(
        mlp_part=vmem((2, 2, owned, width), f32),
        fields_in=vmem((tokens, channel), low),
        fields_sem=dma((tokens // strip,)),
        cot_sem=dma((tokens // strip,)),
        cot_in=vmem((tokens, channel), low),
        grid=vmem((tokens, channel), f32),
        back=vmem((tokens, channel), f32),
        normed=vmem((tokens, channel), low),
        normed_turned=vmem((channel, tokens), low),
        cot_turned=vmem((channel, tokens), low),
        unit_one=vmem((tokens, channel), low),
        unit_two=vmem((tokens, channel), low),
        scale_one=vmem((tokens, 1), f32),
        scale_two=vmem((tokens, 1), f32),
        own_small=vmem((16 + kept.shape[0], 128), f32),
        all_small=vmem((group, 16 + kept.shape[0], 128), f32),
        gains=vmem((16, channel), f32),
        keep=vmem((lat_total * modes, 128), f32),
        own_w=vmem((parts, 2, snaps, owned, quarter), low),
        all_w=vmem((parts, 2, snaps, channel, quarter), low),
        modes=vmem((2, group, half_snaps * pair * 3 // 4, 128), low),
        modes_got=vmem((2, group, half_snaps * pair * 3 // 4, 128), low),
        rows_out=vmem((2, group, half_snaps * pair * 3 // 4, 128), low),
        rows_got=vmem((2, group, half_snaps * pair * 3 // 4, 128), low),
        arrived=vmem((snap_local, pair * group, 128), low),
        gathered=vmem((2, spread, channel), f32),
        home_low=vmem((2, spread, channel), low),
        weight_one=vmem((256, 256), low),
        weight_two=vmem((256, 256), low),
        spectrum=vmem((snap_local * lat_total * modes, 256), low),
        pre_one=vmem((snap_local * lat_total * modes, 256), f32),
        act_one=vmem((snap_local * lat_total * modes, 256), low),
        pre_two=vmem((snap_local * lat_total * modes, 256), f32),
        grad_pre=vmem((snap_local * lat_total * modes, 256), f32),
        grad_two=vmem((snap_local * lat_total * modes, 256), low),
        grad_one=vmem((snap_local * lat_total * modes, 256), low),
        folds=vmem((5, 8, channel), f32),
        pair_grad=vmem((256, 256), f32),
        act=vmem((tokens, width), low),
        slope=vmem((tokens, width), low),
        bias=vmem((parts, 1, width), f32),
        grad_bias=vmem((parts, 8, width), f32),
        grad_rows=vmem((16, channel), f32),
        grads=vmem((2, levels, 2, owned, width), low),
        core_got=vmem((2, 2, levels, owned, width), low),
        half_out=vmem((2, 2, 2, levels, owned, half), low),
        half_got=vmem((4, 2, levels, owned, half), low),
        quarter_out=vmem((2, 2, 2, levels, owned, quarter), low),
        quarter_got=vmem((2, 2, levels, owned, quarter), low),
        level_out=vmem((2, levels, 2, owned, quarter), low),
        level_got=vmem((4, levels, 2, owned, quarter), low),
        total=vmem((parts, snaps, 2, owned, quarter), low),
        filt_out=vmem((snaps, 4, owned, 128), low),
        tiles=vmem((group, 16, 128), f32),
        tiles_got=vmem((group, 16, 128), f32),
        snap_tiles=vmem((snaps, 16, 128), f32),
        swap_l=dma((4,)),
        load_sem=dma((len(inputs) + 1,)),
    )
    for name, shape in dict(
        small=(group,),
        swap=(4,),
        first=(parts, levels),
        second=(parts,),
        third=(parts,),
        fourth=(parts,),
        block=(2, 2, group),
        row=(2, 2, group),
        core=(2, 2),
        half=(4, 2),
        quarter=(2, 2),
        level=(4, levels),
        last=(parts, snaps),
        filt=(snaps,),
        tile=(group,),
        snap_tile=(snaps,),
    ).items():
        scratch[name + "_s"] = dma(shape)
        scratch[name + "_r"] = dma(shape)
    names = [*inputs, *outputs, *scratch]
    far = pl.BlockSpec(memory_space=pl.ANY)
    near = pl.BlockSpec(memory_space=pltpu.VMEM)
    results = pl.pallas_call(
        functools.partial(block_body, names, (snaps, group, parts, width)),
        in_specs=[far] * len(inputs),
        out_specs=[far, far, far, near, near],
        out_shape=list(outputs.values()),
        scratch_shapes=list(scratch.values()),
        compiler_params=pltpu.CompilerParams(
            collective_id=0, has_side_effects=True, vmem_limit_bytes=VMEM_LIMIT
        ),
        cost_estimate=pl.CostEstimate(
            flops=12 * tokens * channel * hidden,
            bytes_accessed=4 * hidden * channel,
            transcendentals=tokens * hidden,
        ),
        name="block_pass",
    )(*inputs.values())
    return results


def adamw_near(master, first_mom, second_mom, gradient, step_rate):
    first_next = beta_one * (first_mom + gradient)
    second_next = beta_two * (second_mom + gradient * gradient)
    fix_one = 1.0 / (1.0 - beta_one**STEP)
    fix_two = 1.0 / (1.0 - beta_two**STEP)
    grown = second_next * fix_two
    bottom = grown * lax.rsqrt(grown) + adam_eps
    master_next = (1.0 - step_rate * decay_rate) * master - (
        (step_rate * fix_one) * first_next
    ) / bottom
    return (master_next, first_next, second_next, master_next.astype(jnp.bfloat16))


def step_body(names, positions, *refs):
    g = Refs()
    for name, ref in zip(names, refs, strict=True):
        setattr(g, name, ref)
    parts, snaps = g.grad_mlp.shape[:2]
    quarter = g.grad_mlp.shape[4]
    width = snaps * quarter
    chunks = g.near.shape[1]
    some = parts // chunks
    moments = ("w", "m", "v")
    results = ("new", "first", "second", "copy")

    pieces = g.far_sem.shape[2]
    ends = ((g.out, g.out_near, g.out_o), (g.in_grad, g.in_grad_near, g.in_grad_o))

    def passing(kind, piece, leg):
        size = ends[kind][0].shape[0] // pieces
        rows = pl.ds(piece * size, size)
        return pltpu.make_async_copy(
            ends[kind][leg].at[rows], ends[kind][leg + 1].at[rows], g.far_sem.at[leg, kind, piece]
        )

    through = [(kind, piece) for piece in range(pieces) for kind in range(2)]

    def chunk_cols(chunk):
        return pl.ds(chunk * some * width, some * width)

    def load(chunk):
        near = [
            pltpu.make_async_copy(
                g.grad_mlp.at[pl.ds(chunk * some, some)], g.grad_near.at[chunk], g.near_sem.at[3, chunk]
            )
        ]
        for index, kind in enumerate(moments):
            near.append(
                pltpu.make_async_copy(
                    getattr(g, "mlp_" + kind).at[:, :, chunk_cols(chunk)],
                    g.near.at[index, chunk],
                    g.near_sem.at[index, chunk],
                )
            )
        return near

    def store(chunk):
        copies = [
            pltpu.make_async_copy(
                g.near.at[index, chunk],
                getattr(g, "mlp_" + kind).at[:, :, chunk_cols(chunk)],
                g.back_sem.at[index, chunk],
            )
            for index, kind in enumerate(results[:3])
        ]
        copies.append(
            pltpu.make_async_copy(
                g.low_near.at[chunk], g.mlp_copy.at[:, :, chunk_cols(chunk)], g.back_sem.at[3, chunk]
            )
        )
        return copies

    coming = [load(chunk) for chunk in range(chunks)]
    going = [store(chunk) for chunk in range(chunks)]
    for chunk in range(chunks):
        for copy in coming[chunk]:
            copy.start()
        for each in through[chunk::chunks]:
            passing(*each, 0).start()

    def put(prefix, values):
        for kind, value in zip(results, values, strict=True):
            getattr(g, prefix + kind)[...] = value

    owned = g.filt_w.shape[2]
    put(
        "filt_",
        adamw(g.filt_w[...], g.filt_m[...], g.filt_v[...], g.grad_filt[:, :, 0:owned], rate_filter),
    )
    rows = g.small_w.shape[0]
    put(
        "small_",
        adamw(
            g.small_w[...], g.small_m[...], g.small_v[...], g.grad_small[0:rows, 0:owned], rate_small
        ),
    )
    totals = g.grad_small[rows : rows + 2, 0 : g.run.shape[1]]
    g.stats[...] = stat_decay * g.run[...] + (1.0 - stat_decay) * totals / positions

    for chunk in range(chunks):
        for copy in coming[chunk]:
            copy.wait()
        for part, matrix, snap in [
            (part, matrix, snap)
            for part in range(some)
            for matrix in range(2)
            for snap in range(snaps)
        ]:
            place = snap if matrix else 2 * (snap % 2) + snap // 2
            first_col = part * width + place * quarter
            where = (chunk, matrix, slice(None), slice(first_col, first_col + quarter))
            now = [g.near[(kind, *where)] for kind in range(3)]
            grad = g.grad_near[chunk, part, snap, matrix].astype(jnp.float32)
            values = adamw_near(*now, grad, rate_mlp)
            for kind in range(3):
                g.near[(kind, *where)] = values[kind]
            g.low_near[where] = values[3]
        for copy in going[chunk]:
            copy.start()
        for each in through[chunk::chunks]:
            passing(*each, 0).wait()
            passing(*each, 1).start()
    for each in through:
        passing(*each, 1).wait()
    for chunk in range(chunks):
        for copy in going[chunk]:
            copy.wait()


def step_pass(shown, grads, masters, run_stats, positions):
    grad_mlp, grad_filt, grad_small = grads
    mlp, filt, small = masters
    chunks = grad_mlp.shape[0] // 2
    width = mlp[0].shape[2] // chunks
    f32, low = jnp.float32, jnp.bfloat16
    far = pl.BlockSpec(memory_space=pltpu.HBM)
    near = pl.BlockSpec(memory_space=pltpu.VMEM)
    inputs = dict(out=shown[0], in_grad=shown[1], grad_mlp=grad_mlp)
    inputs |= dict(zip(("mlp_w", "mlp_m", "mlp_v"), mlp, strict=True))
    far_in = len(inputs)
    inputs |= dict(grad_filt=grad_filt, grad_small=grad_small)
    inputs |= dict(zip(("filt_w", "filt_m", "filt_v"), filt, strict=True))
    inputs |= dict(zip(("small_w", "small_m", "small_v"), small, strict=True))
    inputs |= dict(run=run_stats)
    results = (("new", f32), ("first", f32), ("second", f32), ("copy", low))
    outputs = {
        name + "_o": jax.ShapeDtypeStruct(array.shape, array.dtype)
        for name, array in zip(("out", "in_grad"), shown, strict=True)
    }
    outputs |= {"mlp_" + kind: jax.ShapeDtypeStruct(mlp[0].shape, dt) for kind, dt in results}
    far_out = len(outputs)
    outputs |= {"filt_" + kind: jax.ShapeDtypeStruct(filt[0].shape, dt) for kind, dt in results}
    outputs |= {"small_" + kind: jax.ShapeDtypeStruct(small[0].shape, dt) for kind, dt in results}
    outputs |= dict(stats=jax.ShapeDtypeStruct(run_stats.shape, f32))
    scratch = dict(
        near=pltpu.VMEM((3, chunks, 2, mlp[0].shape[1], width), f32),
        grad_near=pltpu.VMEM((chunks, 2, *grad_mlp.shape[1:]), low),
        low_near=pltpu.VMEM((chunks, 2, mlp[0].shape[1], width), low),
        near_sem=pltpu.SemaphoreType.DMA((4, chunks)),
        back_sem=pltpu.SemaphoreType.DMA((4, chunks)),
        out_near=pltpu.VMEM(shown[0].shape, low),
        in_grad_near=pltpu.VMEM(shown[1].shape, f32),
        far_sem=pltpu.SemaphoreType.DMA((2, 2, divisor(shown[0].shape[0], 1, 3))),
    )
    return pl.pallas_call(
        functools.partial(step_body, [*inputs, *outputs, *scratch], positions),
        in_specs=[far] * far_in + [near] * (len(inputs) - far_in),
        out_specs=[far] * far_out + [near] * (len(outputs) - far_out),
        out_shape=list(outputs.values()),
        scratch_shapes=list(scratch.values()),
        compiler_params=pltpu.CompilerParams(vmem_limit_bytes=VMEM_LIMIT),
        name="step_pass",
    )(*inputs.values())


def per_device_blocks(
    fields,
    cotangent,
    valid_mask,
    kept_modes,
    mlp_master,
    mlp_first,
    mlp_second,
    filter_master,
    filter_first,
    filter_second,
    small_master,
    small_first,
    small_second,
    run_stats,
):
    snaps, group = lax.axis_size("snap"), lax.axis_size("sp")
    out, in_grad, *grads = block_pass(
        fields, cotangent, valid_mask, kept_modes, mlp_master, filter_master, small_master, snaps, group
    )
    snap_local, row_local, lon_total, channel = fields.shape
    positions = snap_local * snaps * row_local * group * lon_total
    out, in_grad, *stepped = step_pass(
        (out, in_grad),
        grads,
        (
            (mlp_master, mlp_first, mlp_second),
            (filter_master, filter_first, filter_second),
            (small_master, small_first, small_second),
        ),
        run_stats,
        positions,
    )
    rows_apart = (snap_local, lon_total, row_local, channel)
    out, in_grad = [
        jnp.transpose(array.reshape(rows_apart), (0, 2, 1, 3)) for array in (out, in_grad)
    ]
    return (out, in_grad, *stepped)


def per_device(*arrays):
    group, snaps = lax.axis_size("sp"), lax.axis_size("snap")
    channel, hidden = arrays[0].shape[3], arrays[4].shape[2]
    by_block = group == BLOCKS and snaps == 4 and arrays[3].shape[1] == 1
    if by_block and hidden == 6 * 512 and channel // group <= 128 and channel % (16 * group) == 0:
        return per_device_blocks(*arrays)
    return per_device_modes(*arrays)


def solution(mesh):
    return jax.shard_map(
        per_device,
        mesh=mesh,
        in_specs=(
            P("snap", "sp", None, None),
            P("snap", "sp", None, None),
            P("snap", "sp", None),
            P(None, "sp"),
            P(None, "sp", None),
            P(None, "sp", None),
            P(None, "sp", None),
            P(None, "sp", None),
            P(None, "sp", None),
            P(None, "sp", None),
            P(None, "sp"),
            P(None, "sp"),
            P(None, "sp"),
            P(),
        ),
        out_specs=(
            P("snap", "sp", None, None),
            P("snap", "sp", None, None),
            P(None, "sp", None),
            P(None, "sp", None),
            P(None, "sp", None),
            P(None, "sp", None),
            P(None, "sp", None),
            P(None, "sp", None),
            P(None, "sp", None),
            P(None, "sp", None),
            P(None, "sp"),
            P(None, "sp"),
            P(None, "sp"),
            P(None, "sp"),
            P(),
        ),
        check_vma=False,
    )
```

```python
import functools
import math

import jax
import jax.numpy as jnp
import ml_dtypes
import numpy as np
from jax import lax
from jax.experimental import pallas as pl
from jax.experimental.pallas import tpu as pltpu
from jax.sharding import PartitionSpec as P

BLOCKS = 8
NVAR = 20
STEP = 10
VMEM_LIMIT = 63 * 1024 * 1024


eps_norm = 1e-06
shrink_level = 0.01
beta_one = 0.5
beta_two = 0.5
adam_eps = 1e-08
decay_rate = 0.01
rate_mlp = 0.03
rate_filter = 0.1
rate_small = 0.2
stat_decay = 0.5


def layer_norm(values, gain_vec, shift_vec):
    centred = values - jnp.mean(values, axis=-1, keepdims=True)
    spread = jnp.mean(centred * centred, axis=-1, keepdims=True)
    return centred * lax.rsqrt(spread + eps_norm) * gain_vec + shift_vec


def shrink(values):
    return values - shrink_level * jnp.tanh(values / shrink_level)


def lon_tables(lon_total, mode_total):
    places = jnp.arange(lon_total, dtype=jnp.int32)
    orders = jnp.arange(mode_total, dtype=jnp.int32)
    angles = (places[:, None] * orders[None, :] % lon_total).astype(jnp.float32) * (
        2.0 * math.pi / lon_total
    )
    scaling = 1.0 / math.sqrt(lon_total)
    forward_tab = jnp.stack([jnp.cos(angles), -jnp.sin(angles)], axis=1) * scaling
    doubling = jnp.where(orders == 0, 1.0, 2.0).astype(jnp.float32)[:, None]
    inverse_tab = (
        jnp.stack([jnp.cos(angles).T * doubling, -jnp.sin(angles).T * doubling], axis=0) * scaling
    )
    return (forward_tab.astype(jnp.bfloat16), inverse_tab.astype(jnp.bfloat16))


def lat_table(lat_total):
    places = jnp.arange(lat_total, dtype=jnp.int32)
    angles = (places[:, None] * places[None, :] % lat_total).astype(jnp.float32) * (
        2.0 * math.pi / lat_total
    )
    cosine = jnp.cos(angles)
    sine_part = jnp.sin(angles)
    upper_rows = jnp.stack([cosine, sine_part], axis=1)
    bottom = jnp.stack([-sine_part, cosine], axis=1)
    return (jnp.stack([upper_rows, bottom], axis=0) / math.sqrt(lat_total)).astype(jnp.bfloat16)


def complex_pair(real_part, imag_part):
    return jnp.stack([jnp.stack([real_part, -imag_part]), jnp.stack([imag_part, real_part])])


gelu_scale = math.sqrt(2.0 / math.pi)
gelu_cubic = 0.044715


def gelu_both(value):
    bend = (gelu_scale * gelu_cubic) * (value * value)
    turn = jnp.tanh(value * (gelu_scale + bend))
    half = 0.5 + 0.5 * turn
    slope = half * (1.0 + (value * (1.0 - turn)) * (gelu_scale + 3.0 * bend))
    return value * half, slope


def dot_nt(left, right):
    return lax.dot_general(
        left, right, (((1,), (1,)), ((), ())), preferred_element_type=jnp.float32
    )


def dot_nn(left, right):
    return jnp.dot(left, right, preferred_element_type=jnp.float32)


def divisor(total, unit, most):
    return max(size for size in range(unit, most + 1, unit) if total % size == 0)


def mlp_body(
    tile,
    normed_ref,
    cot_ref,
    up_ref,
    down_ref,
    bias_ref,
    out_ref,
    back_ref,
    grad_up_ref,
    grad_down_ref,
    grad_bias_ref,
    normed_turned,
    cot_turned,
    act_ref,
    slope_ref,
):
    tokens = normed_ref.shape[0]

    @pl.when(pl.program_id(0) == 0)
    def _():
        normed_turned[...] = normed_ref[...].T
        cot_turned[...] = cot_ref[...].T
        out_ref[...] = jnp.zeros_like(out_ref)
        back_ref[...] = jnp.zeros_like(back_ref)

    grad_bias_ref[...] = jnp.zeros_like(grad_bias_ref)

    @pl.loop(0, tokens // tile)
    def _(step):
        rows = pl.ds(pl.multiple_of(step * tile, tile), tile)
        act, slope = gelu_both(dot_nn(normed_ref[rows, :], up_ref[...]) + bias_ref[...])
        act = act.astype(jnp.bfloat16)
        slope = (dot_nn(cot_ref[rows, :], down_ref[...]) * slope).astype(jnp.bfloat16)
        act_ref[rows, :] = act
        slope_ref[rows, :] = slope
        grad_bias_ref[...] += jnp.sum(slope.astype(jnp.float32), axis=0, keepdims=True)
        out_ref[rows, :] += dot_nt(act, down_ref[...])
        back_ref[rows, :] += dot_nt(slope, up_ref[...])

    grad_up_ref[...] = dot_nn(normed_turned[...], slope_ref[...]).astype(grad_up_ref.dtype)
    grad_down_ref[...] = dot_nn(cot_turned[...], act_ref[...]).astype(grad_down_ref.dtype)


def mlp_pass(normed, cot, weights, bias):
    tokens, channel = normed.shape
    hidden = weights.shape[2]
    width = divisor(hidden, 128, 512)
    tile = divisor(tokens, 16, 480)
    whole = pl.BlockSpec((tokens, channel), lambda j: (0, 0))
    block = pl.BlockSpec((channel, width), lambda j: (0, j))
    line = pl.BlockSpec((1, width), lambda j: (0, j))
    part = lambda which: pl.BlockSpec((None, channel, width), lambda j: (which, 0, j))
    total = jax.ShapeDtypeStruct((tokens, channel), jnp.float32)
    grads = jax.ShapeDtypeStruct((channel, hidden), jnp.bfloat16)
    return pl.pallas_call(
        functools.partial(mlp_body, tile),
        grid=(hidden // width,),
        in_specs=[whole, whole, part(0), part(1), line],
        out_specs=[whole, whole, block, block, line],
        out_shape=[total, total, grads, grads, jax.ShapeDtypeStruct((1, hidden), jnp.float32)],
        scratch_shapes=[
            pltpu.VMEM((channel, tokens), jnp.bfloat16),
            pltpu.VMEM((channel, tokens), jnp.bfloat16),
            pltpu.VMEM((tokens, width), jnp.bfloat16),
            pltpu.VMEM((tokens, width), jnp.bfloat16),
        ],
        compiler_params=pltpu.CompilerParams(vmem_limit_bytes=56 * 1024 * 1024),
        cost_estimate=pl.CostEstimate(
            flops=12 * tokens * channel * hidden,
            bytes_accessed=8 * channel * hidden + 12 * tokens * channel,
            transcendentals=tokens * hidden,
        ),
        name="mlp_pass",
    )(normed, cot, weights, weights, bias)


def spectral_front(arrived, lat_fwd, first_pair, second_pair, bias_one, bias_two):
    spectrum = jnp.einsum(
        "pkqr,nrqmd->nkpmd", lat_fwd, arrived, preferred_element_type=jnp.float32
    ).astype(jnp.bfloat16)
    snap_local, lat_total, pair_count, mode_local, channel = spectrum.shape
    blocked = spectrum.reshape(
        snap_local, lat_total, pair_count, mode_local, BLOCKS, channel // BLOCKS
    )
    pre_one = (
        jnp.einsum("nkqmbi,pqbio->nkpmbo", blocked, first_pair, preferred_element_type=jnp.float32)
        + bias_one
    )
    act_one = jax.nn.gelu(pre_one).astype(jnp.bfloat16)
    pre_two = (
        jnp.einsum("nkqmbi,pqbio->nkpmbo", act_one, second_pair, preferred_element_type=jnp.float32)
        + bias_two
    )
    return (blocked, pre_one, act_one, pre_two)


def adamw(master, first_mom, second_mom, gradient, step_rate):
    first_next = beta_one * first_mom + (1.0 - beta_one) * gradient
    second_next = beta_two * second_mom + (1.0 - beta_two) * gradient * gradient
    fix_one = 1.0 / (1.0 - beta_one**STEP)
    fix_two = 1.0 / (1.0 - beta_two**STEP)
    direction = first_next * fix_one / (jnp.sqrt(second_next * fix_two) + adam_eps)
    master_next = master - step_rate * (direction + decay_rate * master)
    return (master_next, first_next, second_next, master_next.astype(jnp.bfloat16))


def per_device_modes(
    fields,
    cotangent,
    valid_mask,
    kept_modes,
    mlp_master,
    mlp_first,
    mlp_second,
    filter_master,
    filter_first,
    filter_second,
    small_master,
    small_first,
    small_second,
    run_stats,
):
    group_size = lax.axis_size("sp")
    snap_local, row_local, lon_total, channel = fields.shape
    lat_total = row_local * group_size
    mode_local = kept_modes.shape[1]
    mode_total = mode_local * group_size
    block_width = channel // BLOCKS
    lon_fwd, lon_inv = lon_tables(lon_total, mode_total)
    lat_fwd = lat_table(lat_total)
    mlp_w, filt_w, small_w = (
        lax.all_gather(mlp_master.astype(jnp.bfloat16), "sp", axis=1, tiled=True),
        lax.all_gather(filter_master.astype(jnp.bfloat16), "sp", axis=1, tiled=True),
        lax.all_gather(small_master.astype(jnp.bfloat16), "sp", axis=1, tiled=True),
    )
    small_f = small_w.astype(jnp.float32)
    weights = filt_w.reshape(4, BLOCKS, block_width, block_width)
    first_pair = complex_pair(weights[0], weights[1])
    second_pair = complex_pair(weights[2], weights[3])
    bias_one = small_f[4:6].reshape(2, 1, BLOCKS, block_width)
    bias_two = small_f[6:8].reshape(2, 1, BLOCKS, block_width)
    fields_float = fields.astype(jnp.float32)
    normed, norm_pull = jax.vjp(layer_norm, fields_float, small_f[0], small_f[1])
    normed_low = normed.astype(jnp.bfloat16)
    spec_lon = jnp.einsum(
        "nrld,lqm->nrqmd", normed_low, lon_fwd, preferred_element_type=jnp.float32
    ).astype(jnp.bfloat16)
    arrived = lax.all_to_all(spec_lon, "sp", split_axis=3, concat_axis=1, tiled=True)
    spectral = spectral_front(arrived, lat_fwd, first_pair, second_pair, bias_one, bias_two)
    keep_mask = kept_modes.astype(jnp.float32)[None, :, None, :, None, None]
    masked = (shrink(spectral[3]) * keep_mask).astype(jnp.bfloat16)
    masked = masked.reshape(snap_local, lat_total, 2, mode_local, channel)
    returned = jnp.einsum(
        "pkqr,nkpmd->nrqmd", lat_fwd, masked, preferred_element_type=jnp.float32
    ).astype(jnp.bfloat16)
    home_modes = lax.all_to_all(returned, "sp", split_axis=1, concat_axis=3, tiled=True)
    filtered = jnp.einsum(
        "nrqmd,qml->nrld", home_modes, lon_inv, preferred_element_type=jnp.float32
    )
    mixture = fields_float + normed + filtered
    normed_two, norm_two_pull = jax.vjp(layer_norm, mixture, small_f[2], small_f[3])
    normed_two_low = normed_two.astype(jnp.bfloat16)
    tokens = snap_local * row_local * lon_total
    passed = mlp_pass(
        normed_two_low.reshape(tokens, channel),
        cotangent.reshape(tokens, channel),
        mlp_w,
        small_f[9:].reshape(1, -1),
    )
    output = mixture + passed[0].reshape(mixture.shape) + small_f[8]
    weight_mask = valid_mask.astype(jnp.float32)[..., None]
    variables = output[..., :NVAR]
    local_sums = jnp.stack(
        [
            jnp.sum(weight_mask * variables, axis=(0, 1, 2)),
            jnp.sum(weight_mask * variables * variables, axis=(0, 1, 2)),
        ]
    )
    total_sums = lax.psum(local_sums, ("snap", "sp"))
    positions = snap_local * lax.axis_size("snap") * lat_total * lon_total
    stats_new = stat_decay * run_stats + (1.0 - stat_decay) * total_sums / positions
    cot_float = cotangent.astype(jnp.float32)
    grad_normed_two = passed[1].reshape(mixture.shape)
    grad_bias_hidden = passed[4]
    grad_mix_norm, grad_gain_two, grad_shift_two = norm_two_pull(grad_normed_two)
    grad_mixture = cot_float + grad_mix_norm
    grad_bias_out = jnp.sum(cot_float, axis=(0, 1, 2))
    grad_filtered = grad_mixture.astype(jnp.bfloat16)
    grad_home = jnp.einsum(
        "nrld,qml->nrqmd", grad_filtered, lon_inv, preferred_element_type=jnp.float32
    ).astype(jnp.bfloat16)
    grad_returned = lax.all_to_all(grad_home, "sp", split_axis=3, concat_axis=1, tiled=True)
    grad_masked = jnp.einsum(
        "pkqr,nrqmd->nkpmd", lat_fwd, grad_returned, preferred_element_type=jnp.float32
    )
    arrived_again = lax.all_to_all(spec_lon, "sp", split_axis=3, concat_axis=1, tiled=True)
    used_front = spectral_front(arrived_again, lat_fwd, first_pair, second_pair, bias_one, bias_two)
    blocked, pre_one, act_one, pre_two = used_front
    grad_two = jax.vjp(shrink, pre_two)[1](grad_masked.reshape(pre_two.shape) * keep_mask)[
        0
    ].astype(jnp.bfloat16)
    grad_bias_two = jnp.sum(grad_two.astype(jnp.float32), axis=(0, 1, 3))
    grad_second = jnp.einsum(
        "nkqmbi,nkpmbo->pqbio", act_one, grad_two, preferred_element_type=jnp.float32
    )
    grad_act = jnp.einsum(
        "nkpmbo,pqbio->nkqmbi", grad_two, second_pair, preferred_element_type=jnp.float32
    )
    grad_one = jax.vjp(jax.nn.gelu, pre_one)[1](grad_act)[0].astype(jnp.bfloat16)
    grad_bias_one = jnp.sum(grad_one.astype(jnp.float32), axis=(0, 1, 3))
    grad_first = jnp.einsum(
        "nkqmbi,nkpmbo->pqbio", blocked, grad_one, preferred_element_type=jnp.float32
    )
    grad_spectrum = jnp.einsum(
        "nkpmbo,pqbio->nkqmbi", grad_one, first_pair, preferred_element_type=jnp.float32
    ).astype(jnp.bfloat16)
    grad_spectrum = grad_spectrum.reshape(snap_local, lat_total, 2, mode_local, channel)
    grad_lon = jnp.einsum(
        "pkqr,nkpmd->nrqmd", lat_fwd, grad_spectrum, preferred_element_type=jnp.float32
    ).astype(jnp.bfloat16)
    grad_rows = lax.all_to_all(grad_lon, "sp", split_axis=1, concat_axis=3, tiled=True)
    grad_normed = grad_mixture + jnp.einsum(
        "nrqmd,lqm->nrld", grad_rows, lon_fwd, preferred_element_type=jnp.float32
    )
    grad_field_norm, grad_gain_one, grad_shift_one = norm_pull(grad_normed)
    input_grad = grad_mixture + grad_field_norm
    grad_filter = jnp.stack(
        [
            grad_first[0, 0] + grad_first[1, 1],
            grad_first[1, 0] - grad_first[0, 1],
            grad_second[0, 0] + grad_second[1, 1],
            grad_second[1, 0] - grad_second[0, 1],
        ]
    ).reshape(4, channel, block_width)
    grad_small = jnp.concatenate(
        [
            jnp.stack([grad_gain_one, grad_shift_one, grad_gain_two, grad_shift_two]),
            grad_bias_one.reshape(2, channel),
            grad_bias_two.reshape(2, channel),
            grad_bias_out[None, :],
            grad_bias_hidden.reshape(-1, channel),
        ],
        axis=0,
    )
    shares = (
        jnp.stack([
            lax.psum_scatter(part, "sp", scatter_dimension=0, tiled=True) for part in passed[2:4]
        ]),
        lax.psum_scatter(grad_filter, "sp", scatter_dimension=1, tiled=True),
        lax.psum_scatter(grad_small, "sp", scatter_dimension=1, tiled=True),
    )
    owned = (
        lax.psum(shares[0].astype(jnp.bfloat16), "snap").astype(jnp.float32),
        lax.psum(shares[1].astype(jnp.bfloat16), "snap").astype(jnp.float32),
        lax.psum(shares[2].astype(jnp.bfloat16), "snap").astype(jnp.float32),
    )
    mlp_new, mlp_first_new, mlp_second_new, mlp_copy = adamw(
        mlp_master, mlp_first, mlp_second, owned[0], rate_mlp
    )
    filter_new, filter_first_new, filter_second_new, filter_copy = adamw(
        filter_master, filter_first, filter_second, owned[1], rate_filter
    )
    small_new, small_first_new, small_second_new, small_copy = adamw(
        small_master, small_first, small_second, owned[2], rate_small
    )
    return (
        output.astype(jnp.bfloat16),
        input_grad,
        mlp_new,
        mlp_first_new,
        mlp_second_new,
        mlp_copy,
        filter_new,
        filter_first_new,
        filter_second_new,
        filter_copy,
        small_new,
        small_first_new,
        small_second_new,
        small_copy,
        stats_new,
    )


FIRST, SECOND, THIRD, FOURTH, HALF, QUARTER, LEVEL, LAST = range(8)
SCHEDULE = {
    "a": [(FIRST, 0)],
    "b": [(FIRST, 1)],
    "c0": [(SECOND, 0)],
    "d1": [(SECOND, 1), (FIRST, 2)],
    "f0": [(THIRD, 0)],
    "f1": [(SECOND, 2), (FIRST, 3)],
    "g": [(THIRD, 1)],
    "h0": [(FIRST, 4)],
    "h1": [(FOURTH, 0), (THIRD, 2)],
    ("k2", 0): [(SECOND, 3), (SECOND, 4)],
    ("m", 0): [(FOURTH, 1), (FIRST, 5)],
    ("m0", 0): [(FOURTH, 2)],
    ("m1", 0): [(HALF, 0)],
    ("k1", 1): [(THIRD, 3)],
    ("k2", 1): [(THIRD, 4)],
    ("k0", 2): [(HALF, 1)],
    ("m", 2): [(FOURTH, 3)],
    ("m1", 2): [(QUARTER, 0)],
    ("m2", 2): [(HALF, 2), (FOURTH, 4)],
    ("k0", 3): [(FOURTH, 5)],
    ("m", 3): [(LEVEL, 0), (QUARTER, 1)],
    ("k", 4): [(HALF, 3)],
    ("k2", 4): [(LEVEL, 1)],
    ("l", 4): [(QUARTER, 2)],
    ("k", 5): [(LAST, 0)],
    ("k0", 5): [(LEVEL, 2)],
    ("k1", 5): [(QUARTER, 3)],
    ("k2", 5): [(HALF, 4)],
    ("m", 5): [(LAST, 1), (LEVEL, 3)],
    "o1": [(QUARTER, 4)],
    "p1": [(HALF, 5)],
    "r": [(LAST, 2), (LEVEL, 4)],
    "t1": [(QUARTER, 5)],
    "u1": [(LAST, 3), (LAST, 4)],
    "x0": [(LEVEL, 5)],
    "z": [(LAST, 5)],
}


def lon_matrix(lon_total, mode_total, snaps, rows):
    places = np.arange(lon_total)
    orders = np.arange(mode_total)
    angles = (places[:, None] * orders[None, :] % lon_total) * (2.0 * math.pi / lon_total)
    doubling = np.where(orders == 0, 1.0, 2.0)
    scaling = 1.0 / math.sqrt(lon_total)
    forward = np.stack([np.cos(angles), -np.sin(angles)], axis=1) * scaling
    inverse = forward * doubling

    def spread(table):
        table = np.einsum(
            "ab,lx,rs->alrbsx", np.eye(snaps), table.reshape(lon_total, -1), np.eye(rows)
        )
        return table.reshape(snaps * lon_total * rows, -1).astype(ml_dtypes.bfloat16)

    return spread(forward), spread(inverse)


def lon_turn(lon_total, rows):
    turn = np.einsum("lk,rs->rlks", np.eye(lon_total), np.eye(rows))
    return turn.reshape(rows, lon_total, lon_total * rows).astype(ml_dtypes.bfloat16)


def lat_matrix(lat_total, mode_total):
    places = np.arange(lat_total)
    angles = (places[:, None] * places[None, :] % lat_total) * (2.0 * math.pi / lat_total)
    cosine, sine = np.cos(angles), np.sin(angles)
    table = np.stack([np.stack([cosine, sine], axis=1), np.stack([-sine, cosine], axis=1)])
    table = np.einsum("pkqr,ab->pakrqb", table / math.sqrt(lat_total), np.eye(mode_total))
    size = 2 * lat_total * mode_total
    return table.reshape(size, size).astype(ml_dtypes.bfloat16)


class Refs:
    pass


def block_body(names, sizes, *refs):
    g = Refs()
    for name, ref in zip(names, refs, strict=True):
        setattr(g, name, ref)
    snaps, group, parts, width = sizes
    levels = group // 2
    tokens = g.fields.shape[0] * g.fields.shape[1]
    channel = g.fields.shape[2]
    owned = channel // group
    half = width // 2
    quarter = width // snaps
    tile = tokens // 2
    short = divisor(tokens // 2, 16, 720)
    packed = g.modes.shape[2]
    strip = divisor(tokens // 2, 48, 144)
    sub = divisor(strip, 16, 48)
    low = jnp.bfloat16
    f32 = jnp.float32

    me_snap = lax.axis_index("snap")
    me_sp = lax.axis_index("sp")
    core = lax.rem(me_sp, 2)
    level = me_sp // 2

    def at(snap, sp):
        return {"snap": snap, "sp": sp}

    def sp_after(step):
        return lax.rem(me_sp + step, group)

    def sp_before(step):
        return lax.rem(me_sp + group - step, group)

    def snap_after(step):
        return lax.rem(me_snap + step, snaps)

    def snap_before(step):
        return lax.rem(me_snap + snaps - step, snaps)

    def level_after(step):
        return lax.rem(level + step, levels)

    def level_before(step):
        return lax.rem(level + levels - step, levels)

    other_core = at(me_snap, me_sp + 1 - 2 * core)

    def send(src, dst, sems, index, target):
        return pltpu.make_async_remote_copy(
            src_ref=src,
            dst_ref=dst,
            send_sem=sems[0].at[index],
            recv_sem=sems[1].at[index],
            device_id=target,
            device_id_type=pl.DeviceIdType.MESH,
        )

    half_tokens = tokens // 2

    def strips(body, first=0, count=tokens, before=None, after=None):
        @pl.loop(0, count // strip)
        def _(step):
            if before is not None:
                before(first // strip + step)
            for at_row in range(0, strip, sub):
                body(pl.ds(pl.multiple_of(first + step * strip + at_row, 16), sub))
            if after is not None:
                after(first // strip + step)

    def half_strips(body, part, **around):
        strips(body, part * half_tokens, half_tokens, **around)

    def strip_copy(near, far, sems, place, out):
        rows = pl.ds(pl.multiple_of(place * strip, strip), strip)
        ends = [near.at[rows], far.reshape(tokens, channel).at[rows]]
        if not out:
            ends.reverse()
        return pltpu.make_async_copy(*ends, sems.at[place])

    def fields_load(place):
        return strip_copy(g.fields_in, g.fields, g.fields_sem, place, False)

    def cot_load(place):
        return strip_copy(g.cot_in, g.cot, g.cot_sem, place, False)

    def out_copy(place):
        return strip_copy(g.fields_in, g.out, g.fields_sem, place, True)

    def grad_copy(place):
        return strip_copy(g.grid, g.in_grad, g.cot_sem, place, True)

    def half_rows(part):
        return slice(part * half_tokens, (part + 1) * half_tokens)

    def fold(value):
        return jnp.sum(value.reshape(-1, 8, value.shape[1]), axis=0)

    loads = {}

    def load(name, index):
        copy = pltpu.make_async_copy(getattr(g, name), getattr(g, name + "_in"), g.load_sem.at[index])
        copy.start()
        loads[name] = copy

    for index, name in enumerate(
        [name for name in names[: names.index("out")] if name not in ("mlp", "fields", "cot")]
    ):
        load(name, index)
    for copy in (fields_load, cot_load):
        for place in range(tokens // strip):
            copy(place).start()

    def master_load(part):
        return pltpu.make_async_copy(
            g.mlp.at[:, :, part * width : (part + 1) * width],
            g.mlp_part.at[part % 2],
            g.load_sem.at[len(loads) + part % 2],
        )

    master_load(0).start()
    master_load(1).start()

    barrier = pltpu.get_barrier_semaphore()
    peers = [at(me_snap, sp_after(step)) for step in range(1, group)]
    peers += [at(snap_after(step), me_sp) for step in range(1, snaps)]
    for peer in peers:
        pl.semaphore_signal(
            barrier, inc=1, device_id=peer, device_id_type=pl.DeviceIdType.MESH
        )

    loads["small"].wait()
    loads["kept"].wait()
    g.own_small[...] = jnp.zeros_like(g.own_small)
    rows_small = g.small.shape[0]
    g.own_small[0:rows_small, 0:owned] = g.small_in[...].astype(low).astype(f32)
    pairs_kept = g.kept.shape[1]
    lines = lax.broadcasted_iota(jnp.int32, (pairs_kept, pairs_kept), 0)
    places = lax.broadcasted_iota(jnp.int32, (pairs_kept, pairs_kept), 1)
    kept = jnp.where(lines == places, g.kept_in[...].astype(f32), 0.0)
    g.own_small[16:, :] = jnp.broadcast_to(
        jnp.sum(kept, axis=1, keepdims=True), (pairs_kept, g.own_small.shape[1])
    )
    pl.semaphore_wait(barrier, len(peers))

    def small_copy(step):
        return send(
            g.own_small, g.all_small.at[me_sp], (g.small_s, g.small_r), step, at(me_snap, sp_after(step))
        )

    for step in range(1, group):
        small_copy(step).start()
    g.all_small[me_sp] = g.own_small[...]

    snap_low = lax.rem(me_snap, 2)
    snap_high = me_snap // 2
    beside_low = me_snap + 1 - 2 * snap_low
    beside_high = me_snap + 2 - 4 * snap_high

    def own_quarter(part):
        odd = lax.rem(part, 2)
        return (1 - odd) * me_snap + odd * (2 * snap_low + snap_high)

    def own_place(part):
        return pl.ds(0, snaps) if part == parts - 1 else own_quarter(part)

    def half_quarters(part):
        return pl.ds(2 * (own_quarter(part) // 2), 2)

    def own_rows(sp):
        return pl.ds(pl.multiple_of(sp * owned, owned), owned)

    def spot(part):
        if isinstance(part, int):
            return part // 2 + parts // 2 * (part % 2)
        return lax.div(part, 2) + parts // 2 * lax.rem(part, 2)

    swaps = (
        (pl.ds(0, 1), own_place(0)),
        (pl.ds(3, 2), own_place(1)),
        (pl.ds(1, 2), own_place(0)),
        (pl.ds(5, 1), own_place(5)),
    )
    swapped = {0: 0, 1: 1, 2: 2, 5: 3}

    def swap_copy(batch):
        some, place = swaps[batch]
        return send(
            g.own_w.at[some, 1 - core, place],
            g.all_w.at[some, 1 - core, place, own_rows(me_sp)],
            (g.swap_s, g.swap_r),
            batch,
            other_core,
        )

    def swap_local(batch):
        some, place = swaps[batch]
        return pltpu.make_async_copy(
            g.own_w.at[some, core, place],
            g.all_w.at[some, core, place, own_rows(me_sp)],
            g.swap_l.at[batch],
        )

    def start_swap(batch):
        swap_copy(batch).start()
        swap_local(batch).start()

    def first_copy(part, step):
        rows = pl.ds(pl.multiple_of(level * 2 * owned, 2 * owned), 2 * owned)
        view = g.all_w.at[spot(part), core, own_place(part), rows]
        target = at(me_snap, 2 * level_after(step) + core)
        return send(view, view, (g.first_s, g.first_r), (part, step), target)

    def second_copy(part):
        odd = lax.rem(part, 2)
        view = g.all_w.at[spot(part), core, own_quarter(part)]
        target = at((1 - odd) * beside_low + odd * beside_high, me_sp)
        return send(view, view, (g.second_s, g.second_r), part, target)

    def third_copy(part):
        odd = lax.rem(part, 2)
        view = g.all_w.at[spot(part), core, half_quarters(part)]
        target = at((1 - odd) * beside_high + odd * beside_low, me_sp)
        return send(view, view, (g.third_s, g.third_r), part, target)

    def fourth_copy(part):
        view = g.all_w.at[spot(part), core]
        return send(view, view, (g.fourth_s, g.fourth_r), part, other_core)

    def start_first(part):
        if part in swapped:
            swap_copy(swapped[part]).wait_recv()
            swap_local(swapped[part]).wait()
        for step in range(1, levels):
            first_copy(part, step).start()

    def wait_first(part):
        for step in range(1, levels):
            first_copy(part, step).wait_recv()

    def pass_second(part):
        wait_first(part)
        second_copy(part).start()

    def pass_third(part):
        second_copy(part).wait_recv()
        third_copy(part).start()

    def pass_fourth(part):
        if part == parts - 1:
            wait_first(part)
        else:
            third_copy(part).wait_recv()
        fourth_copy(part).start()

    stages = {FIRST: start_first, SECOND: pass_second, THIRD: pass_third, FOURTH: pass_fourth}

    def reach(point):
        for stage, part in SCHEDULE.get(point, ()):
            stages[stage](part)

    for part in range(parts):
        master_load(part).wait()
        for place in range(snaps):
            cols = slice(place * quarter, (place + 1) * quarter)
            g.own_w[spot(part), :, place] = g.mlp_part[part % 2, :, :, cols].astype(low)
        if part + 2 < parts:
            master_load(part + 2).start()
        if part == 0:
            start_swap(0)
        elif part == parts - 1:
            for batch in range(1, len(swaps)):
                start_swap(batch)
    reach("a")

    def first_unit(rows):
        values = g.fields_in[rows, :].astype(f32)
        centred = values - jnp.mean(values, axis=-1, keepdims=True)
        scale = lax.rsqrt(jnp.mean(centred * centred, axis=-1, keepdims=True) + eps_norm)
        g.scale_one[rows, :] = scale
        g.grid[rows, :] = centred * scale

    strips(first_unit, before=lambda place: fields_load(place).wait())
    reach("b")
    for step in range(1, group):
        small_copy(step).wait_recv()
    for sp in range(group):
        g.gains[:, sp * owned : (sp + 1) * owned] = g.all_small[sp, 0:16, 0:owned]
        g.keep[sp * pairs_kept : (sp + 1) * pairs_kept, :] = g.all_small[sp, 16:, :]

    def first_norm(rows):
        unit = g.grid[rows, :]
        normed = unit * g.gains[0:1, :] + g.gains[1:2, :]
        g.unit_one[rows, :] = unit.astype(low)
        g.normed[rows, :] = normed.astype(low)
        g.grid[rows, :] = g.fields_in[rows, :].astype(f32) + normed

    half_snaps = g.arrived.shape[0] // 2

    third_rows = packed // 3
    spare = 128 - owned

    def pack(value):
        return jnp.concatenate(
            [
                jnp.concatenate(
                    [
                        value[at_row * third_rows : (at_row + 1) * third_rows],
                        value[packed:, at_row * spare : (at_row + 1) * spare],
                    ],
                    axis=1,
                )
                for at_row in range(3)
            ],
            axis=0,
        ).astype(low)

    def unpack(value):
        value = value.astype(f32)
        rest = [
            value[at_row * third_rows : (at_row + 1) * third_rows, owned:] for at_row in range(3)
        ]
        return jnp.concatenate([value[:, 0:owned], jnp.concatenate(rest, axis=1)], axis=0)

    def block_copy(which, part, step):
        target = sp_after(step)
        return send(
            g.modes.at[part, target],
            g.modes_got.at[part, me_sp],
            (g.block_s, g.block_r),
            (which, part, step),
            at(me_snap, target),
        )

    def row_copy(which, part, step):
        target = sp_after(step)
        return send(
            g.rows_out.at[part, target],
            g.rows_got.at[part, me_sp],
            (g.row_s, g.row_r),
            (which, part, step),
            at(me_snap, target),
        )

    def to_blocks(table, which, part):
        modes = dot_nn(table, g.normed[half_rows(part), :])
        for block in range(group):
            g.modes[part, block] = pack(modes[:, block * owned : (block + 1) * owned])
        for step in range(1, group):
            block_copy(which, part, step).start()
        g.modes_got[part, me_sp] = g.modes[part, me_sp]

    def take_blocks(which, part):
        for step in range(1, group):
            block_copy(which, part, step).wait_recv()
        each = g.arrived.shape[1] // group
        for sp in range(group):
            value = unpack(g.modes_got[part, sp])
            value = jnp.concatenate([value, jnp.zeros((value.shape[0], spare), f32)], axis=1)
            for index in range(half_snaps):
                g.arrived[part * half_snaps + index, sp * each : (sp + 1) * each, :] = value[
                    index * each : (index + 1) * each
                ].astype(low)

    def to_rows(which, part, tables):
        each = tables[0].shape[0] // group
        for sp in range(group):
            value = [table[sp * each : (sp + 1) * each, 0:owned] for table in tables]
            g.rows_out[part, sp] = pack(jnp.concatenate(value, axis=0))
        for step in range(1, group):
            row_copy(which, part, step).start()
        g.rows_got[part, me_sp] = g.rows_out[part, me_sp]

    def home_modes(which, part):
        for step in range(1, group):
            row_copy(which, part, step).wait_recv()
        for block in range(group):
            g.gathered[part, :, block * owned : (block + 1) * owned] = unpack(
                g.rows_got[part, block]
            )
        g.home_low[part] = g.gathered[part].astype(low)

    loads["lon_f"].wait()
    for part in range(2):
        half_strips(first_norm, part)
        reach("c" + str(part))
        to_blocks(g.lon_f_in[...], 0, part)
        reach("d" + str(part))

    loads["filt"].wait()
    for weight, first in ((g.weight_one, 0), (g.weight_two, 2)):
        weight[...] = jnp.zeros_like(weight)
        real = g.filt_in[first].astype(low)
        imag = g.filt_in[first + 1].astype(low)
        weight[0:owned, 0:owned] = real
        weight[128 : 128 + owned, 128 : 128 + owned] = real
        weight[0:owned, 128 : 128 + owned] = imag
        weight[128 : 128 + owned, 0:owned] = -imag

    def bias_row(first):
        return jnp.concatenate(
            [g.own_small[first : first + 1, :], g.own_small[first + 1 : first + 2, :]], axis=1
        )

    for place in range(tokens // strip):
        cot_load(place).wait()
    reach("e")
    loads["lat_f"].wait()
    loads["lat_b"].wait()
    pairs = g.arrived.shape[1] // 2
    half_modes = half_snaps * pairs

    def mode_half(part):
        return slice(part * half_modes, (part + 1) * half_modes)

    def spectra(out, kind, part):
        for snap in range(part * half_snaps, (part + 1) * half_snaps):
            spectrum = dot_nn(g.lat_f_in[...], g.arrived[snap]).astype(kind)
            rows = slice(snap * pairs, (snap + 1) * pairs)
            out[rows, 0:128] = spectrum[0:pairs]
            out[rows, 128:256] = spectrum[pairs:]

    def grids(values):
        tables = []
        for index in range(half_snaps):
            rows = values[index * pairs : (index + 1) * pairs]
            rows = jnp.concatenate([rows[:, 0:128], rows[:, 128:256]], axis=0)
            tables.append(dot_nn(g.lat_b_in[...], rows))
        return tables

    def keep_half():
        keep = jnp.concatenate([g.keep[...], g.keep[...]], axis=1)
        return jnp.concatenate([keep] * half_snaps, axis=0)

    for part in range(2):
        take_blocks(0, part)
        rows = mode_half(part)
        spectra(g.spectrum, low, part)
        g.pre_one[rows, :] = dot_nn(g.spectrum[rows, :], g.weight_one[...]) + bias_row(4)
        g.act_one[rows, :] = gelu_both(g.pre_one[rows, :])[0].astype(low)
        g.pre_two[rows, :] = dot_nn(g.act_one[rows, :], g.weight_two[...]) + bias_row(6)
        to_rows(0, part, grids((shrink(g.pre_two[rows, :]) * keep_half()).astype(low)))
        reach("f" + str(part))
    g.cot_turned[...] = g.cot_in[...].T
    reach("g")

    loads["lon_i"].wait()

    def second_norm(rows):
        values = g.grid[rows, :]
        centred = values - jnp.mean(values, axis=-1, keepdims=True)
        scale = lax.rsqrt(jnp.mean(centred * centred, axis=-1, keepdims=True) + eps_norm)
        centred = centred * scale
        g.unit_two[rows, :] = centred.astype(low)
        g.scale_two[rows, :] = scale
        g.normed[rows, :] = (centred * g.gains[2:3, :] + g.gains[3:4, :]).astype(low)
        g.grid[rows, :] = values + g.gains[8:9, :]
        g.back[rows, :] = jnp.zeros((sub, channel), f32)

    for part in range(2):
        home_modes(0, part)
        g.grid[half_rows(part), :] += dot_nn(g.lon_i_in[...], g.home_low[part])
        reach("h" + str(part))
        half_strips(second_norm, part)
        reach("i" + str(part))
    g.normed_turned[...] = g.normed[...].T
    reach("j")
    flat = jnp.concatenate([g.gains[9 + row : 10 + row, :] for row in range(rows_small - 9)], axis=1)
    for part in range(parts):
        g.bias[part] = flat[:, part * width : (part + 1) * width]

    def core_copy(part, matrix):
        slot = lax.rem(part, 2)
        return send(
            g.grads.at[matrix, :, 1 - core],
            g.core_got.at[slot, matrix],
            (g.core_s, g.core_r),
            (slot, matrix),
            other_core,
        )

    places_one = (snap_low, snap_high)
    places_two = (snap_high, snap_low)
    beside_one = (beside_low, beside_high)
    beside_two = (beside_high, beside_low)

    def half_copy(part, matrix):
        slot = lax.rem(part, 2)
        place = lax.rem(part, 4)
        return send(
            g.half_out.at[slot, matrix, 1 - places_one[matrix]],
            g.half_got.at[place, matrix],
            (g.half_s, g.half_r),
            (place, matrix),
            at(beside_one[matrix], me_sp),
        )

    def quarter_copy(part, matrix):
        slot = lax.rem(part, 2)
        return send(
            g.quarter_out.at[slot, matrix, 1 - places_two[matrix]],
            g.quarter_got.at[slot, matrix],
            (g.quarter_s, g.quarter_r),
            (slot, matrix),
            at(beside_two[matrix], me_sp),
        )

    def level_copy(part, step):
        slot = lax.rem(part, 2)
        place = lax.rem(part, 4)
        target = level_after(step)
        return send(
            g.level_out.at[slot, target],
            g.level_got.at[place, level],
            (g.level_s, g.level_r),
            (place, step),
            at(me_snap, 2 * target + core),
        )

    def last_copy(part, step):
        view = g.total.at[part, me_snap]
        return send(view, view, (g.last_s, g.last_r), (part, step), at(snap_after(step), me_sp))

    def half_stage(part):
        slot = lax.rem(part, 2)
        for matrix in range(2):

            if part >= 2:
                half_copy(part - 2, matrix).wait_send()

            core_copy(part, matrix).wait_recv()

            @pl.loop(0, levels)
            def _(row, matrix=matrix):
                both = g.grads[matrix, row, core].astype(f32) + g.core_got[
                    slot, matrix, row
                ].astype(f32)
                both = both.astype(low)
                g.half_out[slot, matrix, 0, row] = both[:, 0:half]
                g.half_out[slot, matrix, 1, row] = both[:, half:width]

            half_copy(part, matrix).start()

    def quarter_stage(part):
        slot = lax.rem(part, 2)
        for matrix in range(2):

            if part >= 2:
                quarter_copy(part - 2, matrix).wait_send()

            half_copy(part, matrix).wait_recv()
            for row in range(levels):
                both = g.half_out[slot, matrix, places_one[matrix], row].astype(f32) + g.half_got[
                    lax.rem(part, 4), matrix, row
                ].astype(f32)
                both = both.astype(low)
                g.quarter_out[slot, matrix, 0, row] = both[:, 0:quarter]
                g.quarter_out[slot, matrix, 1, row] = both[:, quarter:half]
            quarter_copy(part, matrix).start()

    def level_stage(part):
        slot = lax.rem(part, 2)

        if part >= 2:
            for step in range(1, levels):
                level_copy(part - 2, step).wait_send()

        for matrix in range(2):
            quarter_copy(part, matrix).wait_recv()
            for row in range(levels):
                both = g.quarter_out[slot, matrix, places_two[matrix], row].astype(
                    f32
                ) + g.quarter_got[slot, matrix, row].astype(f32)
                g.level_out[slot, row, matrix] = both.astype(low)
        for step in range(1, levels):
            level_copy(part, step).start()

    def last_stage(part):
        slot = lax.rem(part, 2)
        for step in range(1, levels):
            level_copy(part, step).wait_recv()
        for matrix in range(2):
            sums = g.level_out[slot, level, matrix].astype(f32)
            for step in range(1, levels):
                sums += g.level_got[lax.rem(part, 4), level_before(step), matrix].astype(f32)
            g.total[part, me_snap, matrix] = sums.astype(low)
        for step in range(1, snaps):
            last_copy(part, step).start()

    stages |= {HALF: half_stage, QUARTER: quarter_stage, LEVEL: level_stage, LAST: last_stage}

    def weight(part, matrix):
        return jnp.concatenate([g.all_w[spot(part), matrix, place] for place in range(snaps)], axis=1)

    def add_products(part, rows):
        g.grid[rows, :] += dot_nt(g.act[rows, :], weight(part, 1))
        g.back[rows, :] += dot_nt(g.slope[rows, :], weight(part, 0))

    @pl.loop(0, parts)
    def _(part):
        def reach_in(point, also=True):
            for at_part in range(parts):
                if (point, at_part) in SCHEDULE:
                    pl.when((part == at_part) & also)(functools.partial(reach, (point, at_part)))

        def tile_rows(step):
            return pl.ds(pl.multiple_of(step * tile, tile), tile)

        fourth_copy(part).wait_recv()
        reach_in("k")
        g.grad_bias[part] = jnp.zeros(g.grad_bias.shape[1:], f32)

        @pl.loop(0, tokens // tile)
        def _(step):
            rows = tile_rows(step)
            act, slope = gelu_both(dot_nn(g.normed[rows, :], weight(part, 0)) + g.bias[part])
            g.act[rows, :] = act.astype(low)
            slope = (dot_nn(g.cot_in[rows, :], weight(part, 1)) * slope).astype(low)
            g.slope[rows, :] = slope
            g.grad_bias[part] += fold(slope.astype(f32))
            for at_step in range(3):
                reach_in("k" + str(at_step), step == (at_step + 1) // 2)

        reach_in("l")

        @pl.when(part >= 1)
        def _():
            for matrix in range(2):
                core_copy(part - 1, matrix).wait_send()

        shape = g.grads.shape[1:]
        g.grads[0] = dot_nn(g.normed_turned[...], g.slope[...]).astype(low).reshape(shape)
        core_copy(part, 0).start()
        g.grads[1] = dot_nn(g.cot_turned[...], g.act[...]).astype(low).reshape(shape)
        core_copy(part, 1).start()
        reach_in("m")

        @pl.when(part < parts - 1)
        def _():
            @pl.loop(0, tokens // tile)
            def _(step):
                add_products(part, tile_rows(step))
                for at_step in range(3):
                    reach_in("m" + str(at_step), step == (at_step + 1) // 2)

    g.folds[...] = jnp.zeros_like(g.folds)

    def second_back(rows):
        grad = g.back[rows, :]
        unit = g.unit_two[rows, :].astype(f32)
        cot = g.cot_in[rows, :].astype(f32)
        pulled = grad * g.gains[2:3, :]
        middle = jnp.mean(pulled, axis=-1, keepdims=True)
        slant = jnp.mean(pulled * unit, axis=-1, keepdims=True)
        total = cot + g.scale_two[rows, :] * (pulled - middle - unit * slant)
        g.back[rows, :] = total
        g.normed[rows, :] = total.astype(low)
        g.folds[2] += fold(grad * unit)
        g.folds[3] += fold(grad)
        g.folds[4] += fold(cot)

    loads["lon_it"].wait()
    for part in range(2):

        @pl.loop(0, half_tokens // short)
        def _(step, part=part):
            first_row = part * half_tokens + step * short
            add_products(parts - 1, pl.ds(pl.multiple_of(first_row, 16), short))

        reach("o" + str(part))
        half_strips(second_back, part)
        for step in range(1, group):
            block_copy(0, part, step).wait_send()
        to_blocks(g.lon_it_in[...], 1, part)
        reach("p" + str(part))
    reach("q")

    def low_out(rows):
        g.fields_in[rows, :] = g.grid[rows, :].astype(low)

    strips(low_out, after=lambda place: out_copy(place).start())
    reach("r")
    loads["valid"].wait()
    loads["turn"].wait()
    weigh = sum(
        dot_nn(g.valid_in[:, row, :].astype(f32).astype(low), g.turn_in[row])
        for row in range(g.valid.shape[1])
    )
    places_each = weigh.shape[1]
    precise = lax.Precision.HIGHEST
    sums = [jnp.zeros((1, 128), f32), jnp.zeros((1, 128), f32)]
    for snap in range(g.valid.shape[0]):
        variables = g.grid[snap * places_each : (snap + 1) * places_each, 0:128]
        for index, value in enumerate((variables, variables * variables)):
            sums[index] += jnp.dot(
                weigh[snap : snap + 1, :], value, precision=precise, preferred_element_type=f32
            )

    reach("s")

    def dot_tn(left, right):
        return lax.dot_general(
            left, right, (((0,), (0,)), ((), ())), preferred_element_type=f32
        )

    def filter_rows(first, grad):
        g.pair_grad[...] = grad
        real = g.pair_grad[0:128, 0:128] + g.pair_grad[128:256, 128:256]
        imag = g.pair_grad[0:128, 128:256] - g.pair_grad[128:256, 0:128]
        g.filt_out[me_snap, first] = real[0:owned].astype(low)
        g.filt_out[me_snap, first + 1] = imag[0:owned].astype(low)

    for part in range(2):
        take_blocks(1, part)
        reach("t" + str(part))
        rows = mode_half(part)
        spectra(g.grad_pre, f32, part)
        bend = jnp.tanh(g.pre_two[rows, :] / shrink_level)
        grad = (g.grad_pre[rows, :] * keep_half() * (bend * bend)).astype(low)
        g.grad_two[rows, :] = grad
        grad = dot_nt(grad, g.weight_two[...]) * gelu_both(g.pre_one[rows, :])[1]
        grad = grad.astype(low)
        g.grad_one[rows, :] = grad
        for step in range(1, group):
            row_copy(0, part, step).wait_send()
        to_rows(1, part, grids(dot_nt(grad, g.weight_one[...]).astype(low)))
        reach("u" + str(part))
    reach("v")
    bias_one = jnp.sum(g.grad_one[...].astype(f32), axis=0, keepdims=True)
    bias_two = jnp.sum(g.grad_two[...].astype(f32), axis=0, keepdims=True)
    filter_rows(2, dot_tn(g.act_one[...], g.grad_two[...]))
    filter_rows(0, dot_tn(g.spectrum[...], g.grad_one[...]))

    def filter_copy(step):
        view = g.filt_out.at[me_snap]
        return send(view, view, (g.filt_s, g.filt_r), step, at(snap_after(step), me_sp))

    for step in range(1, snaps):
        filter_copy(step).start()


    reach("w")

    loads["lon_ft"].wait()

    def first_back(rows):
        grad = g.grid[rows, :]
        unit = g.unit_one[rows, :].astype(f32)
        pulled = grad * g.gains[0:1, :]
        middle = jnp.mean(pulled, axis=-1, keepdims=True)
        slant = jnp.mean(pulled * unit, axis=-1, keepdims=True)
        g.grid[rows, :] = g.back[rows, :] + g.scale_one[rows, :] * (
            pulled - middle - unit * slant
        )
        g.folds[0] += fold(grad * unit)
        g.folds[1] += fold(grad)

    for part in range(2):
        home_modes(1, part)
        reach("x" + str(part))
        g.grid[half_rows(part), :] = g.back[half_rows(part), :] + dot_nn(
            g.lon_ft_in[...], g.home_low[part]
        )
        half_strips(first_back, part, after=lambda place: grad_copy(place).start())
        reach("y" + str(part))

    g.grad_rows[...] = jnp.zeros_like(g.grad_rows)
    for index, row in enumerate((0, 1, 2, 3, 8)):
        g.grad_rows[row : row + 1, :] = jnp.sum(g.folds[index], axis=0, keepdims=True)
    flat = jnp.concatenate(
        [jnp.sum(g.grad_bias[part], axis=0, keepdims=True) for part in range(parts)], axis=1
    )
    for row in range(rows_small - 9):
        g.grad_rows[9 + row : 10 + row, :] = flat[:, row * channel : (row + 1) * channel]
    for block in range(group):
        g.tiles[block] = jnp.zeros(g.tiles.shape[1:], f32)
        g.tiles[block, :, 0:owned] = g.grad_rows[:, block * owned : (block + 1) * owned]
        g.tiles[block, 13:14, :] = sums[0]
        g.tiles[block, 14:15, :] = sums[1]

    def tile_copy(step):
        target = sp_after(step)
        return send(
            g.tiles.at[target], g.tiles_got.at[me_sp], (g.tile_s, g.tile_r), step, at(me_snap, target)
        )

    def snap_tile_copy(step):
        view = g.snap_tiles.at[me_snap]
        return send(view, view, (g.snap_tile_s, g.snap_tile_r), step, at(snap_after(step), me_sp))

    for step in range(1, group):
        tile_copy(step).start()
    reach("z")

    for batch in range(len(swaps)):
        swap_copy(batch).wait_send()
    for part in range(parts):
        if part < parts - 1:
            second_copy(part).wait_send()
            third_copy(part).wait_send()
        fourth_copy(part).wait_send()
        for step in range(1, levels):
            first_copy(part, step).wait_send()
    for step in range(1, group):
        small_copy(step).wait_send()
        for part in range(2):
            block_copy(1, part, step).wait_send()
            row_copy(1, part, step).wait_send()
    for matrix in range(2):
        core_copy(parts - 1, matrix).wait_send()
        for part in (parts - 2, parts - 1):
            half_copy(part, matrix).wait_send()
            quarter_copy(part, matrix).wait_send()
    for step in range(1, levels):
        level_copy(parts - 2, step).wait_send()
    for step in range(1, snaps):
        filter_copy(step).wait_send()

    g.tiles_got[me_sp] = g.tiles[me_sp]
    for step in range(1, group):
        tile_copy(step).wait_recv()
    tile_sum = g.tiles_got[0]
    for sp in range(1, group):
        tile_sum += g.tiles_got[sp]
    g.snap_tiles[me_snap] = tile_sum
    g.snap_tiles[me_snap, 4:5, :] = bias_one[:, 0:128]
    g.snap_tiles[me_snap, 5:6, :] = bias_one[:, 128:256]
    g.snap_tiles[me_snap, 6:7, :] = bias_two[:, 0:128]
    g.snap_tiles[me_snap, 7:8, :] = bias_two[:, 128:256]
    for step in range(1, snaps):
        snap_tile_copy(step).start()

    for step in range(1, snaps):
        filter_copy(step).wait_recv()
    filter_sum = g.filt_out[0].astype(f32)
    for snap in range(1, snaps):
        filter_sum += g.filt_out[snap].astype(f32)
    g.grad_filt[...] = filter_sum
    for part in range(parts):
        for step in range(1, snaps):
            last_copy(part, step).wait_recv()
    grads_out = pltpu.make_async_copy(g.total, g.grad_mlp, g.load_sem.at[3])
    grads_out.start()
    for step in range(1, snaps):
        snap_tile_copy(step).wait_recv()
    tile_sum = g.snap_tiles[0]
    for snap in range(1, snaps):
        tile_sum += g.snap_tiles[snap]
    g.grad_small[...] = tile_sum

    grads_out.wait()
    for place in range(tokens // strip):
        out_copy(place).wait()
        grad_copy(place).wait()
    for step in range(1, levels):
        level_copy(parts - 1, step).wait_send()
    for step in range(1, group):
        tile_copy(step).wait_send()
    for step in range(1, snaps):
        snap_tile_copy(step).wait_send()
        for part in range(parts):
            last_copy(part, step).wait_send()


def block_pass(fields, cot, valid, kept, mlp, filt, small, snaps, group):
    snap_local, row_local, lon_total, channel = fields.shape
    tokens = snap_local * row_local * lon_total
    hidden = mlp.shape[2]
    lat_total = row_local * group
    modes = kept.shape[1] * group
    owned = channel // group
    width = 512
    parts = hidden // width
    levels = group // 2
    quarter = width // snaps
    low, f32 = jnp.bfloat16, jnp.float32
    half = width // 2
    half_snaps = snap_local // 2
    lon_f, lon_i = lon_matrix(lon_total, modes, half_snaps, row_local)

    def paired(array):
        return jnp.transpose(array, (0, 2, 1, 3)).reshape(-1, row_local, channel)

    lat_f = lat_matrix(lat_total, modes)
    pair = 2 * modes * row_local
    spread = half_snaps * row_local * 2 * modes
    inputs = dict(
        small=small,
        kept=kept.T,
        fields=paired(fields),
        lon_f=jnp.asarray(np.ascontiguousarray(lon_f.T)),
        filt=filt,
        lat_f=jnp.asarray(lat_f),
        lat_b=jnp.asarray(np.ascontiguousarray(lat_f.T)),
        cot=paired(cot),
        lon_i=jnp.asarray(lon_i),
        valid=valid,
        turn=jnp.asarray(lon_turn(lon_total, row_local)),
        lon_it=jnp.asarray(np.ascontiguousarray(lon_i.T)),
        lon_ft=jnp.asarray(lon_f),
        mlp=mlp,
    )
    outputs = dict(
        out=jax.ShapeDtypeStruct((tokens // row_local, row_local, channel), low),
        in_grad=jax.ShapeDtypeStruct((tokens // row_local, row_local, channel), f32),
        grad_mlp=jax.ShapeDtypeStruct((parts, snaps, 2, owned, quarter), low),
        grad_filt=jax.ShapeDtypeStruct((4, owned, 128), f32),
        grad_small=jax.ShapeDtypeStruct((16, 128), f32),
    )
    vmem = pltpu.VMEM
    dma = pltpu.SemaphoreType.DMA
    scratch = {
        name + "_in": vmem(value.shape, value.dtype)
        for name, value in inputs.items()
        if name not in ("mlp", "fields", "cot")
    }
    strip = divisor(tokens // 2, 48, 144)
    scratch |= dict(
        mlp_part=vmem((2, 2, owned, width), f32),
        fields_in=vmem((tokens, channel), low),
        fields_sem=dma((tokens // strip,)),
        cot_sem=dma((tokens // strip,)),
        cot_in=vmem((tokens, channel), low),
        grid=vmem((tokens, channel), f32),
        back=vmem((tokens, channel), f32),
        normed=vmem((tokens, channel), low),
        normed_turned=vmem((channel, tokens), low),
        cot_turned=vmem((channel, tokens), low),
        unit_one=vmem((tokens, channel), low),
        unit_two=vmem((tokens, channel), low),
        scale_one=vmem((tokens, 1), f32),
        scale_two=vmem((tokens, 1), f32),
        own_small=vmem((16 + kept.shape[0], 128), f32),
        all_small=vmem((group, 16 + kept.shape[0], 128), f32),
        gains=vmem((16, channel), f32),
        keep=vmem((lat_total * modes, 128), f32),
        own_w=vmem((parts, 2, snaps, owned, quarter), low),
        all_w=vmem((parts, 2, snaps, channel, quarter), low),
        modes=vmem((2, group, half_snaps * pair * 3 // 4, 128), low),
        modes_got=vmem((2, group, half_snaps * pair * 3 // 4, 128), low),
        rows_out=vmem((2, group, half_snaps * pair * 3 // 4, 128), low),
        rows_got=vmem((2, group, half_snaps * pair * 3 // 4, 128), low),
        arrived=vmem((snap_local, pair * group, 128), low),
        gathered=vmem((2, spread, channel), f32),
        home_low=vmem((2, spread, channel), low),
        weight_one=vmem((256, 256), low),
        weight_two=vmem((256, 256), low),
        spectrum=vmem((snap_local * lat_total * modes, 256), low),
        pre_one=vmem((snap_local * lat_total * modes, 256), f32),
        act_one=vmem((snap_local * lat_total * modes, 256), low),
        pre_two=vmem((snap_local * lat_total * modes, 256), f32),
        grad_pre=vmem((snap_local * lat_total * modes, 256), f32),
        grad_two=vmem((snap_local * lat_total * modes, 256), low),
        grad_one=vmem((snap_local * lat_total * modes, 256), low),
        folds=vmem((5, 8, channel), f32),
        pair_grad=vmem((256, 256), f32),
        act=vmem((tokens, width), low),
        slope=vmem((tokens, width), low),
        bias=vmem((parts, 1, width), f32),
        grad_bias=vmem((parts, 8, width), f32),
        grad_rows=vmem((16, channel), f32),
        grads=vmem((2, levels, 2, owned, width), low),
        core_got=vmem((2, 2, levels, owned, width), low),
        half_out=vmem((2, 2, 2, levels, owned, half), low),
        half_got=vmem((4, 2, levels, owned, half), low),
        quarter_out=vmem((2, 2, 2, levels, owned, quarter), low),
        quarter_got=vmem((2, 2, levels, owned, quarter), low),
        level_out=vmem((2, levels, 2, owned, quarter), low),
        level_got=vmem((4, levels, 2, owned, quarter), low),
        total=vmem((parts, snaps, 2, owned, quarter), low),
        filt_out=vmem((snaps, 4, owned, 128), low),
        tiles=vmem((group, 16, 128), f32),
        tiles_got=vmem((group, 16, 128), f32),
        snap_tiles=vmem((snaps, 16, 128), f32),
        swap_l=dma((4,)),
        load_sem=dma((len(inputs) + 1,)),
    )
    for name, shape in dict(
        small=(group,),
        swap=(4,),
        first=(parts, levels),
        second=(parts,),
        third=(parts,),
        fourth=(parts,),
        block=(2, 2, group),
        row=(2, 2, group),
        core=(2, 2),
        half=(4, 2),
        quarter=(2, 2),
        level=(4, levels),
        last=(parts, snaps),
        filt=(snaps,),
        tile=(group,),
        snap_tile=(snaps,),
    ).items():
        scratch[name + "_s"] = dma(shape)
        scratch[name + "_r"] = dma(shape)
    names = [*inputs, *outputs, *scratch]
    far = pl.BlockSpec(memory_space=pl.ANY)
    near = pl.BlockSpec(memory_space=pltpu.VMEM)
    results = pl.pallas_call(
        functools.partial(block_body, names, (snaps, group, parts, width)),
        in_specs=[far] * len(inputs),
        out_specs=[far, far, far, near, near],
        out_shape=list(outputs.values()),
        scratch_shapes=list(scratch.values()),
        compiler_params=pltpu.CompilerParams(
            collective_id=0, has_side_effects=True, vmem_limit_bytes=VMEM_LIMIT
        ),
        cost_estimate=pl.CostEstimate(
            flops=12 * tokens * channel * hidden,
            bytes_accessed=4 * hidden * channel,
            transcendentals=tokens * hidden,
        ),
        name="block_pass",
    )(*inputs.values())
    return results


def adamw_near(master, first_mom, second_mom, gradient, step_rate):
    first_next = beta_one * (first_mom + gradient)
    second_next = beta_two * (second_mom + gradient * gradient)
    fix_one = 1.0 / (1.0 - beta_one**STEP)
    fix_two = 1.0 / (1.0 - beta_two**STEP)
    grown = second_next * fix_two
    bottom = grown * lax.rsqrt(grown) + adam_eps
    master_next = (1.0 - step_rate * decay_rate) * master - (
        (step_rate * fix_one) * first_next
    ) / bottom
    return (master_next, first_next, second_next, master_next.astype(jnp.bfloat16))


def step_body(names, positions, *refs):
    g = Refs()
    for name, ref in zip(names, refs, strict=True):
        setattr(g, name, ref)
    parts, snaps = g.grad_mlp.shape[:2]
    quarter = g.grad_mlp.shape[4]
    width = snaps * quarter
    chunks = g.near.shape[1]
    some = parts // chunks
    moments = ("w", "m", "v")
    results = ("new", "first", "second", "copy")

    pieces = g.far_sem.shape[2]
    ends = ((g.out, g.out_near, g.out_o), (g.in_grad, g.in_grad_near, g.in_grad_o))

    def passing(kind, piece, leg):
        size = ends[kind][0].shape[0] // pieces
        rows = pl.ds(piece * size, size)
        return pltpu.make_async_copy(
            ends[kind][leg].at[rows], ends[kind][leg + 1].at[rows], g.far_sem.at[leg, kind, piece]
        )

    through = [(kind, piece) for piece in range(pieces) for kind in range(2)]

    def chunk_cols(chunk):
        return pl.ds(chunk * some * width, some * width)

    def load(chunk):
        near = [
            pltpu.make_async_copy(
                g.grad_mlp.at[pl.ds(chunk * some, some)], g.grad_near.at[chunk], g.near_sem.at[3, chunk]
            )
        ]
        for index, kind in enumerate(moments):
            near.append(
                pltpu.make_async_copy(
                    getattr(g, "mlp_" + kind).at[:, :, chunk_cols(chunk)],
                    g.near.at[index, chunk],
                    g.near_sem.at[index, chunk],
                )
            )
        return near

    def store(chunk):
        copies = [
            pltpu.make_async_copy(
                g.near.at[index, chunk],
                getattr(g, "mlp_" + kind).at[:, :, chunk_cols(chunk)],
                g.back_sem.at[index, chunk],
            )
            for index, kind in enumerate(results[:3])
        ]
        copies.append(
            pltpu.make_async_copy(
                g.low_near.at[chunk], g.mlp_copy.at[:, :, chunk_cols(chunk)], g.back_sem.at[3, chunk]
            )
        )
        return copies

    coming = [load(chunk) for chunk in range(chunks)]
    going = [store(chunk) for chunk in range(chunks)]
    for chunk in range(chunks):
        for copy in coming[chunk]:
            copy.start()
        for each in through[chunk::chunks]:
            passing(*each, 0).start()

    def put(prefix, values):
        for kind, value in zip(results, values, strict=True):
            getattr(g, prefix + kind)[...] = value

    owned = g.filt_w.shape[2]
    put(
        "filt_",
        adamw(g.filt_w[...], g.filt_m[...], g.filt_v[...], g.grad_filt[:, :, 0:owned], rate_filter),
    )
    rows = g.small_w.shape[0]
    put(
        "small_",
        adamw(
            g.small_w[...], g.small_m[...], g.small_v[...], g.grad_small[0:rows, 0:owned], rate_small
        ),
    )
    totals = g.grad_small[rows : rows + 2, 0 : g.run.shape[1]]
    g.stats[...] = stat_decay * g.run[...] + (1.0 - stat_decay) * totals / positions

    for chunk in range(chunks):
        for copy in coming[chunk]:
            copy.wait()
        for part, matrix, snap in [
            (part, matrix, snap)
            for part in range(some)
            for matrix in range(2)
            for snap in range(snaps)
        ]:
            place = snap if matrix else 2 * (snap % 2) + snap // 2
            first_col = part * width + place * quarter
            where = (chunk, matrix, slice(None), slice(first_col, first_col + quarter))
            now = [g.near[(kind, *where)] for kind in range(3)]
            grad = g.grad_near[chunk, part, snap, matrix].astype(jnp.float32)
            values = adamw_near(*now, grad, rate_mlp)
            for kind in range(3):
                g.near[(kind, *where)] = values[kind]
            g.low_near[where] = values[3]
        for copy in going[chunk]:
            copy.start()
        for each in through[chunk::chunks]:
            passing(*each, 0).wait()
            passing(*each, 1).start()
    for each in through:
        passing(*each, 1).wait()
    for chunk in range(chunks):
        for copy in going[chunk]:
            copy.wait()


def step_pass(shown, grads, masters, run_stats, positions):
    grad_mlp, grad_filt, grad_small = grads
    mlp, filt, small = masters
    chunks = grad_mlp.shape[0]
    width = mlp[0].shape[2] // chunks
    f32, low = jnp.float32, jnp.bfloat16
    far = pl.BlockSpec(memory_space=pltpu.HBM)
    near = pl.BlockSpec(memory_space=pltpu.VMEM)
    inputs = dict(out=shown[0], in_grad=shown[1], grad_mlp=grad_mlp)
    inputs |= dict(zip(("mlp_w", "mlp_m", "mlp_v"), mlp, strict=True))
    far_in = len(inputs)
    inputs |= dict(grad_filt=grad_filt, grad_small=grad_small)
    inputs |= dict(zip(("filt_w", "filt_m", "filt_v"), filt, strict=True))
    inputs |= dict(zip(("small_w", "small_m", "small_v"), small, strict=True))
    inputs |= dict(run=run_stats)
    results = (("new", f32), ("first", f32), ("second", f32), ("copy", low))
    outputs = {
        name + "_o": jax.ShapeDtypeStruct(array.shape, array.dtype)
        for name, array in zip(("out", "in_grad"), shown, strict=True)
    }
    outputs |= {"mlp_" + kind: jax.ShapeDtypeStruct(mlp[0].shape, dt) for kind, dt in results}
    far_out = len(outputs)
    outputs |= {"filt_" + kind: jax.ShapeDtypeStruct(filt[0].shape, dt) for kind, dt in results}
    outputs |= {"small_" + kind: jax.ShapeDtypeStruct(small[0].shape, dt) for kind, dt in results}
    outputs |= dict(stats=jax.ShapeDtypeStruct(run_stats.shape, f32))
    scratch = dict(
        near=pltpu.VMEM((3, chunks, 2, mlp[0].shape[1], width), f32),
        grad_near=pltpu.VMEM((chunks, grad_mlp.shape[0] // chunks, *grad_mlp.shape[1:]), low),
        low_near=pltpu.VMEM((chunks, 2, mlp[0].shape[1], width), low),
        near_sem=pltpu.SemaphoreType.DMA((4, chunks)),
        back_sem=pltpu.SemaphoreType.DMA((4, chunks)),
        out_near=pltpu.VMEM(shown[0].shape, low),
        in_grad_near=pltpu.VMEM(shown[1].shape, f32),
        far_sem=pltpu.SemaphoreType.DMA((2, 2, divisor(shown[0].shape[0], 1, 4))),
    )
    return pl.pallas_call(
        functools.partial(step_body, [*inputs, *outputs, *scratch], positions),
        in_specs=[far] * far_in + [near] * (len(inputs) - far_in),
        out_specs=[far] * far_out + [near] * (len(outputs) - far_out),
        out_shape=list(outputs.values()),
        scratch_shapes=list(scratch.values()),
        compiler_params=pltpu.CompilerParams(vmem_limit_bytes=VMEM_LIMIT),
        name="step_pass",
    )(*inputs.values())


def per_device_blocks(
    fields,
    cotangent,
    valid_mask,
    kept_modes,
    mlp_master,
    mlp_first,
    mlp_second,
    filter_master,
    filter_first,
    filter_second,
    small_master,
    small_first,
    small_second,
    run_stats,
):
    snaps, group = lax.axis_size("snap"), lax.axis_size("sp")
    out, in_grad, *grads = block_pass(
        fields, cotangent, valid_mask, kept_modes, mlp_master, filter_master, small_master, snaps, group
    )
    snap_local, row_local, lon_total, channel = fields.shape
    positions = snap_local * snaps * row_local * group * lon_total
    out, in_grad, *stepped = step_pass(
        (out, in_grad),
        grads,
        (
            (mlp_master, mlp_first, mlp_second),
            (filter_master, filter_first, filter_second),
            (small_master, small_first, small_second),
        ),
        run_stats,
        positions,
    )
    rows_apart = (snap_local, lon_total, row_local, channel)
    out, in_grad = [
        jnp.transpose(array.reshape(rows_apart), (0, 2, 1, 3)) for array in (out, in_grad)
    ]
    return (out, in_grad, *stepped)


def per_device(*arrays):
    group, snaps = lax.axis_size("sp"), lax.axis_size("snap")
    channel, hidden = arrays[0].shape[3], arrays[4].shape[2]
    by_block = group == BLOCKS and snaps == 4 and arrays[3].shape[1] == 1
    if by_block and hidden == 6 * 512 and channel // group <= 128 and channel % (16 * group) == 0:
        return per_device_blocks(*arrays)
    return per_device_modes(*arrays)


def solution(mesh):
    return jax.shard_map(
        per_device,
        mesh=mesh,
        in_specs=(
            P("snap", "sp", None, None),
            P("snap", "sp", None, None),
            P("snap", "sp", None),
            P(None, "sp"),
            P(None, "sp", None),
            P(None, "sp", None),
            P(None, "sp", None),
            P(None, "sp", None),
            P(None, "sp", None),
            P(None, "sp", None),
            P(None, "sp"),
            P(None, "sp"),
            P(None, "sp"),
            P(),
        ),
        out_specs=(
            P("snap", "sp", None, None),
            P("snap", "sp", None, None),
            P(None, "sp", None),
            P(None, "sp", None),
            P(None, "sp", None),
            P(None, "sp", None),
            P(None, "sp", None),
            P(None, "sp", None),
            P(None, "sp", None),
            P(None, "sp", None),
            P(None, "sp"),
            P(None, "sp"),
            P(None, "sp"),
            P(None, "sp"),
            P(),
        ),
        check_vma=False,
    )
```

```python
import functools
import math

import jax
import jax.numpy as jnp
import ml_dtypes
import numpy as np
from jax import lax
from jax.experimental import pallas as pl
from jax.experimental.pallas import tpu as pltpu
from jax.sharding import PartitionSpec as P

BLOCKS = 8
NVAR = 20
STEP = 10
VMEM_LIMIT = 63 * 1024 * 1024


eps_norm = 1e-06
shrink_level = 0.01
beta_one = 0.5
beta_two = 0.5
adam_eps = 1e-08
decay_rate = 0.01
rate_mlp = 0.03
rate_filter = 0.1
rate_small = 0.2
stat_decay = 0.5


def layer_norm(values, gain_vec, shift_vec):
    centred = values - jnp.mean(values, axis=-1, keepdims=True)
    spread = jnp.mean(centred * centred, axis=-1, keepdims=True)
    return centred * lax.rsqrt(spread + eps_norm) * gain_vec + shift_vec


def shrink(values):
    return values - shrink_level * jnp.tanh(values / shrink_level)


def lon_tables(lon_total, mode_total):
    places = jnp.arange(lon_total, dtype=jnp.int32)
    orders = jnp.arange(mode_total, dtype=jnp.int32)
    angles = (places[:, None] * orders[None, :] % lon_total).astype(jnp.float32) * (
        2.0 * math.pi / lon_total
    )
    scaling = 1.0 / math.sqrt(lon_total)
    forward_tab = jnp.stack([jnp.cos(angles), -jnp.sin(angles)], axis=1) * scaling
    doubling = jnp.where(orders == 0, 1.0, 2.0).astype(jnp.float32)[:, None]
    inverse_tab = (
        jnp.stack([jnp.cos(angles).T * doubling, -jnp.sin(angles).T * doubling], axis=0) * scaling
    )
    return (forward_tab.astype(jnp.bfloat16), inverse_tab.astype(jnp.bfloat16))


def lat_table(lat_total):
    places = jnp.arange(lat_total, dtype=jnp.int32)
    angles = (places[:, None] * places[None, :] % lat_total).astype(jnp.float32) * (
        2.0 * math.pi / lat_total
    )
    cosine = jnp.cos(angles)
    sine_part = jnp.sin(angles)
    upper_rows = jnp.stack([cosine, sine_part], axis=1)
    bottom = jnp.stack([-sine_part, cosine], axis=1)
    return (jnp.stack([upper_rows, bottom], axis=0) / math.sqrt(lat_total)).astype(jnp.bfloat16)


def complex_pair(real_part, imag_part):
    return jnp.stack([jnp.stack([real_part, -imag_part]), jnp.stack([imag_part, real_part])])


gelu_scale = math.sqrt(2.0 / math.pi)
gelu_cubic = 0.044715


def gelu_both(value):
    bend = (gelu_scale * gelu_cubic) * (value * value)
    turn = jnp.tanh(value * (gelu_scale + bend))
    half = 0.5 + 0.5 * turn
    slope = half * (1.0 + (value * (1.0 - turn)) * (gelu_scale + 3.0 * bend))
    return value * half, slope


def dot_nt(left, right):
    return lax.dot_general(
        left, right, (((1,), (1,)), ((), ())), preferred_element_type=jnp.float32
    )


def dot_nn(left, right):
    return jnp.dot(left, right, preferred_element_type=jnp.float32)


def divisor(total, unit, most):
    return max(size for size in range(unit, most + 1, unit) if total % size == 0)


def mlp_body(
    tile,
    normed_ref,
    cot_ref,
    up_ref,
    down_ref,
    bias_ref,
    out_ref,
    back_ref,
    grad_up_ref,
    grad_down_ref,
    grad_bias_ref,
    normed_turned,
    cot_turned,
    act_ref,
    slope_ref,
):
    tokens = normed_ref.shape[0]

    @pl.when(pl.program_id(0) == 0)
    def _():
        normed_turned[...] = normed_ref[...].T
        cot_turned[...] = cot_ref[...].T
        out_ref[...] = jnp.zeros_like(out_ref)
        back_ref[...] = jnp.zeros_like(back_ref)

    grad_bias_ref[...] = jnp.zeros_like(grad_bias_ref)

    @pl.loop(0, tokens // tile)
    def _(step):
        rows = pl.ds(pl.multiple_of(step * tile, tile), tile)
        act, slope = gelu_both(dot_nn(normed_ref[rows, :], up_ref[...]) + bias_ref[...])
        act = act.astype(jnp.bfloat16)
        slope = (dot_nn(cot_ref[rows, :], down_ref[...]) * slope).astype(jnp.bfloat16)
        act_ref[rows, :] = act
        slope_ref[rows, :] = slope
        grad_bias_ref[...] += jnp.sum(slope.astype(jnp.float32), axis=0, keepdims=True)
        out_ref[rows, :] += dot_nt(act, down_ref[...])
        back_ref[rows, :] += dot_nt(slope, up_ref[...])

    grad_up_ref[...] = dot_nn(normed_turned[...], slope_ref[...]).astype(grad_up_ref.dtype)
    grad_down_ref[...] = dot_nn(cot_turned[...], act_ref[...]).astype(grad_down_ref.dtype)


def mlp_pass(normed, cot, weights, bias):
    tokens, channel = normed.shape
    hidden = weights.shape[2]
    width = divisor(hidden, 128, 512)
    tile = divisor(tokens, 16, 480)
    whole = pl.BlockSpec((tokens, channel), lambda j: (0, 0))
    block = pl.BlockSpec((channel, width), lambda j: (0, j))
    line = pl.BlockSpec((1, width), lambda j: (0, j))
    part = lambda which: pl.BlockSpec((None, channel, width), lambda j: (which, 0, j))
    total = jax.ShapeDtypeStruct((tokens, channel), jnp.float32)
    grads = jax.ShapeDtypeStruct((channel, hidden), jnp.bfloat16)
    return pl.pallas_call(
        functools.partial(mlp_body, tile),
        grid=(hidden // width,),
        in_specs=[whole, whole, part(0), part(1), line],
        out_specs=[whole, whole, block, block, line],
        out_shape=[total, total, grads, grads, jax.ShapeDtypeStruct((1, hidden), jnp.float32)],
        scratch_shapes=[
            pltpu.VMEM((channel, tokens), jnp.bfloat16),
            pltpu.VMEM((channel, tokens), jnp.bfloat16),
            pltpu.VMEM((tokens, width), jnp.bfloat16),
            pltpu.VMEM((tokens, width), jnp.bfloat16),
        ],
        compiler_params=pltpu.CompilerParams(vmem_limit_bytes=56 * 1024 * 1024),
        cost_estimate=pl.CostEstimate(
            flops=12 * tokens * channel * hidden,
            bytes_accessed=8 * channel * hidden + 12 * tokens * channel,
            transcendentals=tokens * hidden,
        ),
        name="mlp_pass",
    )(normed, cot, weights, weights, bias)


def spectral_front(arrived, lat_fwd, first_pair, second_pair, bias_one, bias_two):
    spectrum = jnp.einsum(
        "pkqr,nrqmd->nkpmd", lat_fwd, arrived, preferred_element_type=jnp.float32
    ).astype(jnp.bfloat16)
    snap_local, lat_total, pair_count, mode_local, channel = spectrum.shape
    blocked = spectrum.reshape(
        snap_local, lat_total, pair_count, mode_local, BLOCKS, channel // BLOCKS
    )
    pre_one = (
        jnp.einsum("nkqmbi,pqbio->nkpmbo", blocked, first_pair, preferred_element_type=jnp.float32)
        + bias_one
    )
    act_one = jax.nn.gelu(pre_one).astype(jnp.bfloat16)
    pre_two = (
        jnp.einsum("nkqmbi,pqbio->nkpmbo", act_one, second_pair, preferred_element_type=jnp.float32)
        + bias_two
    )
    return (blocked, pre_one, act_one, pre_two)


def adamw(master, first_mom, second_mom, gradient, step_rate):
    first_next = beta_one * first_mom + (1.0 - beta_one) * gradient
    second_next = beta_two * second_mom + (1.0 - beta_two) * gradient * gradient
    fix_one = 1.0 / (1.0 - beta_one**STEP)
    fix_two = 1.0 / (1.0 - beta_two**STEP)
    direction = first_next * fix_one / (jnp.sqrt(second_next * fix_two) + adam_eps)
    master_next = master - step_rate * (direction + decay_rate * master)
    return (master_next, first_next, second_next, master_next.astype(jnp.bfloat16))


def per_device_modes(
    fields,
    cotangent,
    valid_mask,
    kept_modes,
    mlp_master,
    mlp_first,
    mlp_second,
    filter_master,
    filter_first,
    filter_second,
    small_master,
    small_first,
    small_second,
    run_stats,
):
    group_size = lax.axis_size("sp")
    snap_local, row_local, lon_total, channel = fields.shape
    lat_total = row_local * group_size
    mode_local = kept_modes.shape[1]
    mode_total = mode_local * group_size
    block_width = channel // BLOCKS
    lon_fwd, lon_inv = lon_tables(lon_total, mode_total)
    lat_fwd = lat_table(lat_total)
    mlp_w, filt_w, small_w = (
        lax.all_gather(mlp_master.astype(jnp.bfloat16), "sp", axis=1, tiled=True),
        lax.all_gather(filter_master.astype(jnp.bfloat16), "sp", axis=1, tiled=True),
        lax.all_gather(small_master.astype(jnp.bfloat16), "sp", axis=1, tiled=True),
    )
    small_f = small_w.astype(jnp.float32)
    weights = filt_w.reshape(4, BLOCKS, block_width, block_width)
    first_pair = complex_pair(weights[0], weights[1])
    second_pair = complex_pair(weights[2], weights[3])
    bias_one = small_f[4:6].reshape(2, 1, BLOCKS, block_width)
    bias_two = small_f[6:8].reshape(2, 1, BLOCKS, block_width)
    fields_float = fields.astype(jnp.float32)
    normed, norm_pull = jax.vjp(layer_norm, fields_float, small_f[0], small_f[1])
    normed_low = normed.astype(jnp.bfloat16)
    spec_lon = jnp.einsum(
        "nrld,lqm->nrqmd", normed_low, lon_fwd, preferred_element_type=jnp.float32
    ).astype(jnp.bfloat16)
    arrived = lax.all_to_all(spec_lon, "sp", split_axis=3, concat_axis=1, tiled=True)
    spectral = spectral_front(arrived, lat_fwd, first_pair, second_pair, bias_one, bias_two)
    keep_mask = kept_modes.astype(jnp.float32)[None, :, None, :, None, None]
    masked = (shrink(spectral[3]) * keep_mask).astype(jnp.bfloat16)
    masked = masked.reshape(snap_local, lat_total, 2, mode_local, channel)
    returned = jnp.einsum(
        "pkqr,nkpmd->nrqmd", lat_fwd, masked, preferred_element_type=jnp.float32
    ).astype(jnp.bfloat16)
    home_modes = lax.all_to_all(returned, "sp", split_axis=1, concat_axis=3, tiled=True)
    filtered = jnp.einsum(
        "nrqmd,qml->nrld", home_modes, lon_inv, preferred_element_type=jnp.float32
    )
    mixture = fields_float + normed + filtered
    normed_two, norm_two_pull = jax.vjp(layer_norm, mixture, small_f[2], small_f[3])
    normed_two_low = normed_two.astype(jnp.bfloat16)
    tokens = snap_local * row_local * lon_total
    passed = mlp_pass(
        normed_two_low.reshape(tokens, channel),
        cotangent.reshape(tokens, channel),
        mlp_w,
        small_f[9:].reshape(1, -1),
    )
    output = mixture + passed[0].reshape(mixture.shape) + small_f[8]
    weight_mask = valid_mask.astype(jnp.float32)[..., None]
    variables = output[..., :NVAR]
    local_sums = jnp.stack(
        [
            jnp.sum(weight_mask * variables, axis=(0, 1, 2)),
            jnp.sum(weight_mask * variables * variables, axis=(0, 1, 2)),
        ]
    )
    total_sums = lax.psum(local_sums, ("snap", "sp"))
    positions = snap_local * lax.axis_size("snap") * lat_total * lon_total
    stats_new = stat_decay * run_stats + (1.0 - stat_decay) * total_sums / positions
    cot_float = cotangent.astype(jnp.float32)
    grad_normed_two = passed[1].reshape(mixture.shape)
    grad_bias_hidden = passed[4]
    grad_mix_norm, grad_gain_two, grad_shift_two = norm_two_pull(grad_normed_two)
    grad_mixture = cot_float + grad_mix_norm
    grad_bias_out = jnp.sum(cot_float, axis=(0, 1, 2))
    grad_filtered = grad_mixture.astype(jnp.bfloat16)
    grad_home = jnp.einsum(
        "nrld,qml->nrqmd", grad_filtered, lon_inv, preferred_element_type=jnp.float32
    ).astype(jnp.bfloat16)
    grad_returned = lax.all_to_all(grad_home, "sp", split_axis=3, concat_axis=1, tiled=True)
    grad_masked = jnp.einsum(
        "pkqr,nrqmd->nkpmd", lat_fwd, grad_returned, preferred_element_type=jnp.float32
    )
    arrived_again = lax.all_to_all(spec_lon, "sp", split_axis=3, concat_axis=1, tiled=True)
    used_front = spectral_front(arrived_again, lat_fwd, first_pair, second_pair, bias_one, bias_two)
    blocked, pre_one, act_one, pre_two = used_front
    grad_two = jax.vjp(shrink, pre_two)[1](grad_masked.reshape(pre_two.shape) * keep_mask)[
        0
    ].astype(jnp.bfloat16)
    grad_bias_two = jnp.sum(grad_two.astype(jnp.float32), axis=(0, 1, 3))
    grad_second = jnp.einsum(
        "nkqmbi,nkpmbo->pqbio", act_one, grad_two, preferred_element_type=jnp.float32
    )
    grad_act = jnp.einsum(
        "nkpmbo,pqbio->nkqmbi", grad_two, second_pair, preferred_element_type=jnp.float32
    )
    grad_one = jax.vjp(jax.nn.gelu, pre_one)[1](grad_act)[0].astype(jnp.bfloat16)
    grad_bias_one = jnp.sum(grad_one.astype(jnp.float32), axis=(0, 1, 3))
    grad_first = jnp.einsum(
        "nkqmbi,nkpmbo->pqbio", blocked, grad_one, preferred_element_type=jnp.float32
    )
    grad_spectrum = jnp.einsum(
        "nkpmbo,pqbio->nkqmbi", grad_one, first_pair, preferred_element_type=jnp.float32
    ).astype(jnp.bfloat16)
    grad_spectrum = grad_spectrum.reshape(snap_local, lat_total, 2, mode_local, channel)
    grad_lon = jnp.einsum(
        "pkqr,nkpmd->nrqmd", lat_fwd, grad_spectrum, preferred_element_type=jnp.float32
    ).astype(jnp.bfloat16)
    grad_rows = lax.all_to_all(grad_lon, "sp", split_axis=1, concat_axis=3, tiled=True)
    grad_normed = grad_mixture + jnp.einsum(
        "nrqmd,lqm->nrld", grad_rows, lon_fwd, preferred_element_type=jnp.float32
    )
    grad_field_norm, grad_gain_one, grad_shift_one = norm_pull(grad_normed)
    input_grad = grad_mixture + grad_field_norm
    grad_filter = jnp.stack(
        [
            grad_first[0, 0] + grad_first[1, 1],
            grad_first[1, 0] - grad_first[0, 1],
            grad_second[0, 0] + grad_second[1, 1],
            grad_second[1, 0] - grad_second[0, 1],
        ]
    ).reshape(4, channel, block_width)
    grad_small = jnp.concatenate(
        [
            jnp.stack([grad_gain_one, grad_shift_one, grad_gain_two, grad_shift_two]),
            grad_bias_one.reshape(2, channel),
            grad_bias_two.reshape(2, channel),
            grad_bias_out[None, :],
            grad_bias_hidden.reshape(-1, channel),
        ],
        axis=0,
    )
    shares = (
        jnp.stack([
            lax.psum_scatter(part, "sp", scatter_dimension=0, tiled=True) for part in passed[2:4]
        ]),
        lax.psum_scatter(grad_filter, "sp", scatter_dimension=1, tiled=True),
        lax.psum_scatter(grad_small, "sp", scatter_dimension=1, tiled=True),
    )
    owned = (
        lax.psum(shares[0].astype(jnp.bfloat16), "snap").astype(jnp.float32),
        lax.psum(shares[1].astype(jnp.bfloat16), "snap").astype(jnp.float32),
        lax.psum(shares[2].astype(jnp.bfloat16), "snap").astype(jnp.float32),
    )
    mlp_new, mlp_first_new, mlp_second_new, mlp_copy = adamw(
        mlp_master, mlp_first, mlp_second, owned[0], rate_mlp
    )
    filter_new, filter_first_new, filter_second_new, filter_copy = adamw(
        filter_master, filter_first, filter_second, owned[1], rate_filter
    )
    small_new, small_first_new, small_second_new, small_copy = adamw(
        small_master, small_first, small_second, owned[2], rate_small
    )
    return (
        output.astype(jnp.bfloat16),
        input_grad,
        mlp_new,
        mlp_first_new,
        mlp_second_new,
        mlp_copy,
        filter_new,
        filter_first_new,
        filter_second_new,
        filter_copy,
        small_new,
        small_first_new,
        small_second_new,
        small_copy,
        stats_new,
    )


FIRST, SECOND, THIRD, FOURTH, HALF, QUARTER, LEVEL, LAST = range(8)
SCHEDULE = {
    "a": [(FIRST, 0)],
    "b": [(FIRST, 1)],
    "c0": [(SECOND, 0)],
    "d1": [(SECOND, 1), (FIRST, 2)],
    "f0": [(THIRD, 0)],
    "f1": [(SECOND, 2), (FIRST, 3)],
    "g": [(THIRD, 1)],
    "h0": [(FIRST, 4)],
    "h1": [(FOURTH, 0), (THIRD, 2)],
    ("k2", 0): [(SECOND, 3), (SECOND, 4)],
    ("m", 0): [(FOURTH, 1), (FIRST, 5)],
    ("m0", 0): [(FOURTH, 2)],
    ("m1", 0): [(HALF, 0)],
    ("k1", 1): [(THIRD, 3)],
    ("k2", 1): [(THIRD, 4)],
    ("k0", 2): [(HALF, 1)],
    ("m", 2): [(FOURTH, 3)],
    ("m1", 2): [(QUARTER, 0)],
    ("m2", 2): [(HALF, 2), (FOURTH, 4)],
    ("k0", 3): [(FOURTH, 5)],
    ("m", 3): [(LEVEL, 0), (QUARTER, 1)],
    ("k", 4): [(HALF, 3)],
    ("k2", 4): [(LEVEL, 1)],
    ("l", 4): [(QUARTER, 2)],
    ("k", 5): [(LAST, 0)],
    ("k0", 5): [(LEVEL, 2)],
    ("k1", 5): [(QUARTER, 3)],
    ("k2", 5): [(HALF, 4)],
    ("m", 5): [(LAST, 1), (LEVEL, 3)],
    "o1": [(QUARTER, 4)],
    "p1": [(HALF, 5)],
    "r": [(LAST, 2), (LEVEL, 4)],
    "t1": [(QUARTER, 5)],
    "u1": [(LAST, 3), (LAST, 4)],
    "x0": [(LEVEL, 5)],
    "z": [(LAST, 5)],
}


def lon_matrix(lon_total, mode_total, snaps, rows):
    places = np.arange(lon_total)
    orders = np.arange(mode_total)
    angles = (places[:, None] * orders[None, :] % lon_total) * (2.0 * math.pi / lon_total)
    doubling = np.where(orders == 0, 1.0, 2.0)
    scaling = 1.0 / math.sqrt(lon_total)
    forward = np.stack([np.cos(angles), -np.sin(angles)], axis=1) * scaling
    inverse = forward * doubling

    def spread(table):
        table = np.einsum(
            "ab,lx,rs->alrbsx", np.eye(snaps), table.reshape(lon_total, -1), np.eye(rows)
        )
        return table.reshape(snaps * lon_total * rows, -1).astype(ml_dtypes.bfloat16)

    return spread(forward), spread(inverse)


def lon_turn(lon_total, rows):
    turn = np.einsum("lk,rs->rlks", np.eye(lon_total), np.eye(rows))
    return turn.reshape(rows, lon_total, lon_total * rows).astype(ml_dtypes.bfloat16)


def lat_matrix(lat_total, mode_total):
    places = np.arange(lat_total)
    angles = (places[:, None] * places[None, :] % lat_total) * (2.0 * math.pi / lat_total)
    cosine, sine = np.cos(angles), np.sin(angles)
    table = np.stack([np.stack([cosine, sine], axis=1), np.stack([-sine, cosine], axis=1)])
    table = np.einsum("pkqr,ab->pakrqb", table / math.sqrt(lat_total), np.eye(mode_total))
    size = 2 * lat_total * mode_total
    return table.reshape(size, size).astype(ml_dtypes.bfloat16)


class Refs:
    pass


def block_body(names, sizes, *refs):
    g = Refs()
    for name, ref in zip(names, refs, strict=True):
        setattr(g, name, ref)
    snaps, group, parts, width = sizes
    levels = group // 2
    tokens = g.fields.shape[0] * g.fields.shape[1]
    channel = g.fields.shape[2]
    owned = channel // group
    half = width // 2
    quarter = width // snaps
    tile = tokens // 2
    short = divisor(tokens // 2, 16, 720)
    packed = g.modes.shape[2]
    strip = divisor(tokens // 2, 48, 144)
    sub = divisor(strip, 16, 48)
    low = jnp.bfloat16
    f32 = jnp.float32

    me_snap = lax.axis_index("snap")
    me_sp = lax.axis_index("sp")
    core = lax.rem(me_sp, 2)
    level = me_sp // 2

    def at(snap, sp):
        return {"snap": snap, "sp": sp}

    def sp_after(step):
        return lax.rem(me_sp + step, group)

    def sp_before(step):
        return lax.rem(me_sp + group - step, group)

    def snap_after(step):
        return lax.rem(me_snap + step, snaps)

    def snap_before(step):
        return lax.rem(me_snap + snaps - step, snaps)

    def level_after(step):
        return lax.rem(level + step, levels)

    def level_before(step):
        return lax.rem(level + levels - step, levels)

    other_core = at(me_snap, me_sp + 1 - 2 * core)

    def send(src, dst, sems, index, target):
        return pltpu.make_async_remote_copy(
            src_ref=src,
            dst_ref=dst,
            send_sem=sems[0].at[index],
            recv_sem=sems[1].at[index],
            device_id=target,
            device_id_type=pl.DeviceIdType.MESH,
        )

    half_tokens = tokens // 2

    def strips(body, first=0, count=tokens, before=None, after=None):
        @pl.loop(0, count // strip)
        def _(step):
            if before is not None:
                before(first // strip + step)
            for at_row in range(0, strip, sub):
                body(pl.ds(pl.multiple_of(first + step * strip + at_row, 16), sub))
            if after is not None:
                after(first // strip + step)

    def half_strips(body, part, **around):
        strips(body, part * half_tokens, half_tokens, **around)

    def strip_copy(near, far, sems, place, out):
        rows = pl.ds(pl.multiple_of(place * strip, strip), strip)
        ends = [near.at[rows], far.reshape(tokens, channel).at[rows]]
        if not out:
            ends.reverse()
        return pltpu.make_async_copy(*ends, sems.at[place])

    def fields_load(place):
        return strip_copy(g.fields_in, g.fields, g.fields_sem, place, False)

    def cot_load(place):
        return strip_copy(g.cot_in, g.cot, g.cot_sem, place, False)

    def out_copy(place):
        return strip_copy(g.fields_in, g.out, g.fields_sem, place, True)

    def grad_copy(place):
        return strip_copy(g.grid, g.in_grad, g.cot_sem, place, True)

    def half_rows(part):
        return slice(part * half_tokens, (part + 1) * half_tokens)

    def fold(value):
        return jnp.sum(value.reshape(-1, 8, value.shape[1]), axis=0)

    loads = {}

    def load(name, index):
        copy = pltpu.make_async_copy(getattr(g, name), getattr(g, name + "_in"), g.load_sem.at[index])
        copy.start()
        loads[name] = copy

    for index, name in enumerate(
        [name for name in names[: names.index("out")] if name not in ("mlp", "fields", "cot")]
    ):
        load(name, index)
    for copy in (fields_load, cot_load):
        for place in range(tokens // strip):
            copy(place).start()

    def master_load(part):
        return pltpu.make_async_copy(
            g.mlp.at[:, :, part * width : (part + 1) * width],
            g.mlp_part.at[part % 2],
            g.load_sem.at[len(loads) + part % 2],
        )

    master_load(0).start()
    master_load(1).start()

    barrier = pltpu.get_barrier_semaphore()
    peers = [at(me_snap, sp_after(step)) for step in range(1, group)]
    peers += [at(snap_after(step), me_sp) for step in range(1, snaps)]
    for peer in peers:
        pl.semaphore_signal(
            barrier, inc=1, device_id=peer, device_id_type=pl.DeviceIdType.MESH
        )

    loads["small"].wait()
    loads["kept"].wait()
    g.own_small[...] = jnp.zeros_like(g.own_small)
    rows_small = g.small.shape[0]
    g.own_small[0:rows_small, 0:owned] = g.small_in[...].astype(low).astype(f32)
    pairs_kept = g.kept.shape[1]
    lines = lax.broadcasted_iota(jnp.int32, (pairs_kept, pairs_kept), 0)
    places = lax.broadcasted_iota(jnp.int32, (pairs_kept, pairs_kept), 1)
    kept = jnp.where(lines == places, g.kept_in[...].astype(f32), 0.0)
    g.own_small[16:, :] = jnp.broadcast_to(
        jnp.sum(kept, axis=1, keepdims=True), (pairs_kept, g.own_small.shape[1])
    )
    pl.semaphore_wait(barrier, len(peers))

    def small_copy(step):
        return send(
            g.own_small, g.all_small.at[me_sp], (g.small_s, g.small_r), step, at(me_snap, sp_after(step))
        )

    for step in range(1, group):
        small_copy(step).start()
    g.all_small[me_sp] = g.own_small[...]

    snap_low = lax.rem(me_snap, 2)
    snap_high = me_snap // 2
    beside_low = me_snap + 1 - 2 * snap_low
    beside_high = me_snap + 2 - 4 * snap_high

    def own_quarter(part):
        odd = lax.rem(part, 2)
        return (1 - odd) * me_snap + odd * (2 * snap_low + snap_high)

    def own_place(part):
        return pl.ds(0, snaps) if part == parts - 1 else own_quarter(part)

    def half_quarters(part):
        return pl.ds(2 * (own_quarter(part) // 2), 2)

    def own_rows(sp):
        return pl.ds(pl.multiple_of(sp * owned, owned), owned)

    def spot(part):
        if isinstance(part, int):
            return part // 2 + parts // 2 * (part % 2)
        return lax.div(part, 2) + parts // 2 * lax.rem(part, 2)

    swaps = (
        (pl.ds(0, 1), own_place(0)),
        (pl.ds(3, 2), own_place(1)),
        (pl.ds(1, 2), own_place(0)),
        (pl.ds(5, 1), own_place(5)),
    )
    swapped = {0: 0, 1: 1, 2: 2, 5: 3}

    def swap_copy(batch):
        some, place = swaps[batch]
        return send(
            g.own_w.at[some, 1 - core, place],
            g.all_w.at[some, 1 - core, place, own_rows(me_sp)],
            (g.swap_s, g.swap_r),
            batch,
            other_core,
        )

    def swap_local(batch):
        some, place = swaps[batch]
        return pltpu.make_async_copy(
            g.own_w.at[some, core, place],
            g.all_w.at[some, core, place, own_rows(me_sp)],
            g.swap_l.at[batch],
        )

    def start_swap(batch):
        swap_copy(batch).start()
        swap_local(batch).start()

    def first_copy(part, step):
        rows = pl.ds(pl.multiple_of(level * 2 * owned, 2 * owned), 2 * owned)
        view = g.all_w.at[spot(part), core, own_place(part), rows]
        target = at(me_snap, 2 * level_after(step) + core)
        return send(view, view, (g.first_s, g.first_r), (part, step), target)

    def second_copy(part):
        odd = lax.rem(part, 2)
        view = g.all_w.at[spot(part), core, own_quarter(part)]
        target = at((1 - odd) * beside_low + odd * beside_high, me_sp)
        return send(view, view, (g.second_s, g.second_r), part, target)

    def third_copy(part):
        odd = lax.rem(part, 2)
        view = g.all_w.at[spot(part), core, half_quarters(part)]
        target = at((1 - odd) * beside_high + odd * beside_low, me_sp)
        return send(view, view, (g.third_s, g.third_r), part, target)

    def fourth_copy(part):
        view = g.all_w.at[spot(part), core]
        return send(view, view, (g.fourth_s, g.fourth_r), part, other_core)

    def start_first(part):
        if part in swapped:
            swap_copy(swapped[part]).wait_recv()
            swap_local(swapped[part]).wait()
        for step in range(1, levels):
            first_copy(part, step).start()

    def wait_first(part):
        for step in range(1, levels):
            first_copy(part, step).wait_recv()

    def pass_second(part):
        wait_first(part)
        second_copy(part).start()

    def pass_third(part):
        second_copy(part).wait_recv()
        third_copy(part).start()

    def pass_fourth(part):
        if part == parts - 1:
            wait_first(part)
        else:
            third_copy(part).wait_recv()
        fourth_copy(part).start()

    stages = {FIRST: start_first, SECOND: pass_second, THIRD: pass_third, FOURTH: pass_fourth}

    def reach(point):
        for stage, part in SCHEDULE.get(point, ()):
            stages[stage](part)

    for part in range(parts):
        master_load(part).wait()
        for place in range(snaps):
            cols = slice(place * quarter, (place + 1) * quarter)
            g.own_w[spot(part), :, place] = g.mlp_part[part % 2, :, :, cols].astype(low)
        if part + 2 < parts:
            master_load(part + 2).start()
        if part == 0:
            start_swap(0)
        elif part == parts - 1:
            for batch in range(1, len(swaps)):
                start_swap(batch)
    reach("a")

    def first_unit(rows):
        values = g.fields_in[rows, :].astype(f32)
        centred = values - jnp.mean(values, axis=-1, keepdims=True)
        scale = lax.rsqrt(jnp.mean(centred * centred, axis=-1, keepdims=True) + eps_norm)
        g.scale_one[rows, :] = scale
        g.grid[rows, :] = centred * scale

    strips(first_unit, before=lambda place: fields_load(place).wait())
    reach("b")
    for step in range(1, group):
        small_copy(step).wait_recv()
    for sp in range(group):
        g.gains[:, sp * owned : (sp + 1) * owned] = g.all_small[sp, 0:16, 0:owned]
        g.keep[sp * pairs_kept : (sp + 1) * pairs_kept, :] = g.all_small[sp, 16:, :]

    def first_norm(rows):
        unit = g.grid[rows, :]
        normed = unit * g.gains[0:1, :] + g.gains[1:2, :]
        g.unit_one[rows, :] = unit.astype(low)
        g.normed[rows, :] = normed.astype(low)
        g.grid[rows, :] = g.fields_in[rows, :].astype(f32) + normed

    half_snaps = g.arrived.shape[0] // 2

    third_rows = packed // 3
    spare = 128 - owned

    def pack(value):
        return jnp.concatenate(
            [
                jnp.concatenate(
                    [
                        value[at_row * third_rows : (at_row + 1) * third_rows],
                        value[packed:, at_row * spare : (at_row + 1) * spare],
                    ],
                    axis=1,
                )
                for at_row in range(3)
            ],
            axis=0,
        ).astype(low)

    def unpack(value):
        value = value.astype(f32)
        rest = [
            value[at_row * third_rows : (at_row + 1) * third_rows, owned:] for at_row in range(3)
        ]
        return jnp.concatenate([value[:, 0:owned], jnp.concatenate(rest, axis=1)], axis=0)

    def block_copy(which, part, step):
        target = sp_after(step)
        return send(
            g.modes.at[part, target],
            g.modes_got.at[part, me_sp],
            (g.block_s, g.block_r),
            (which, part, step),
            at(me_snap, target),
        )

    def row_copy(which, part, step):
        target = sp_after(step)
        return send(
            g.rows_out.at[part, target],
            g.rows_got.at[part, me_sp],
            (g.row_s, g.row_r),
            (which, part, step),
            at(me_snap, target),
        )

    def to_blocks(table, which, part):
        modes = dot_nn(table, g.normed[half_rows(part), :])
        for block in range(group):
            g.modes[part, block] = pack(modes[:, block * owned : (block + 1) * owned])
        for step in range(1, group):
            block_copy(which, part, step).start()
        g.modes_got[part, me_sp] = g.modes[part, me_sp]

    def take_blocks(which, part):
        for step in range(1, group):
            block_copy(which, part, step).wait_recv()
        each = g.arrived.shape[1] // group
        for sp in range(group):
            value = unpack(g.modes_got[part, sp])
            value = jnp.concatenate([value, jnp.zeros((value.shape[0], spare), f32)], axis=1)
            for index in range(half_snaps):
                g.arrived[part * half_snaps + index, sp * each : (sp + 1) * each, :] = value[
                    index * each : (index + 1) * each
                ].astype(low)

    def to_rows(which, part, tables):
        each = tables[0].shape[0] // group
        for sp in range(group):
            value = [table[sp * each : (sp + 1) * each, 0:owned] for table in tables]
            g.rows_out[part, sp] = pack(jnp.concatenate(value, axis=0))
        for step in range(1, group):
            row_copy(which, part, step).start()
        g.rows_got[part, me_sp] = g.rows_out[part, me_sp]

    def home_modes(which, part):
        for step in range(1, group):
            row_copy(which, part, step).wait_recv()
        for block in range(group):
            g.gathered[part, :, block * owned : (block + 1) * owned] = unpack(
                g.rows_got[part, block]
            )
        g.home_low[part] = g.gathered[part].astype(low)

    loads["lon_f"].wait()
    for part in range(2):
        half_strips(first_norm, part)
        reach("c" + str(part))
        to_blocks(g.lon_f_in[...], 0, part)
        reach("d" + str(part))

    loads["filt"].wait()
    for weight, first in ((g.weight_one, 0), (g.weight_two, 2)):
        weight[...] = jnp.zeros_like(weight)
        real = g.filt_in[first].astype(low)
        imag = g.filt_in[first + 1].astype(low)
        weight[0:owned, 0:owned] = real
        weight[128 : 128 + owned, 128 : 128 + owned] = real
        weight[0:owned, 128 : 128 + owned] = imag
        weight[128 : 128 + owned, 0:owned] = -imag

    def bias_row(first):
        return jnp.concatenate(
            [g.own_small[first : first + 1, :], g.own_small[first + 1 : first + 2, :]], axis=1
        )

    for place in range(tokens // strip):
        cot_load(place).wait()
    reach("e")
    loads["lat_f"].wait()
    loads["lat_b"].wait()
    pairs = g.arrived.shape[1] // 2
    half_modes = half_snaps * pairs

    def mode_half(part):
        return slice(part * half_modes, (part + 1) * half_modes)

    def spectra(out, kind, part):
        for snap in range(part * half_snaps, (part + 1) * half_snaps):
            spectrum = dot_nn(g.lat_f_in[...], g.arrived[snap]).astype(kind)
            rows = slice(snap * pairs, (snap + 1) * pairs)
            out[rows, 0:128] = spectrum[0:pairs]
            out[rows, 128:256] = spectrum[pairs:]

    def grids(values):
        tables = []
        for index in range(half_snaps):
            rows = values[index * pairs : (index + 1) * pairs]
            rows = jnp.concatenate([rows[:, 0:128], rows[:, 128:256]], axis=0)
            tables.append(dot_nn(g.lat_b_in[...], rows))
        return tables

    def keep_half():
        keep = jnp.concatenate([g.keep[...], g.keep[...]], axis=1)
        return jnp.concatenate([keep] * half_snaps, axis=0)

    for part in range(2):
        take_blocks(0, part)
        rows = mode_half(part)
        spectra(g.spectrum, low, part)
        g.pre_one[rows, :] = dot_nn(g.spectrum[rows, :], g.weight_one[...]) + bias_row(4)
        g.act_one[rows, :] = gelu_both(g.pre_one[rows, :])[0].astype(low)
        g.pre_two[rows, :] = dot_nn(g.act_one[rows, :], g.weight_two[...]) + bias_row(6)
        to_rows(0, part, grids((shrink(g.pre_two[rows, :]) * keep_half()).astype(low)))
        reach("f" + str(part))
    g.cot_turned[...] = g.cot_in[...].T
    reach("g")

    loads["lon_i"].wait()

    def second_norm(rows):
        values = g.grid[rows, :]
        centred = values - jnp.mean(values, axis=-1, keepdims=True)
        scale = lax.rsqrt(jnp.mean(centred * centred, axis=-1, keepdims=True) + eps_norm)
        centred = centred * scale
        g.unit_two[rows, :] = centred.astype(low)
        g.scale_two[rows, :] = scale
        g.normed[rows, :] = (centred * g.gains[2:3, :] + g.gains[3:4, :]).astype(low)
        g.grid[rows, :] = values + g.gains[8:9, :]
        g.back[rows, :] = jnp.zeros((sub, channel), f32)

    for part in range(2):
        home_modes(0, part)
        g.grid[half_rows(part), :] += dot_nn(g.lon_i_in[...], g.home_low[part])
        reach("h" + str(part))
        half_strips(second_norm, part)
        reach("i" + str(part))
    g.normed_turned[...] = g.normed[...].T
    reach("j")
    flat = jnp.concatenate([g.gains[9 + row : 10 + row, :] for row in range(rows_small - 9)], axis=1)
    for part in range(parts):
        g.bias[part] = flat[:, part * width : (part + 1) * width]

    def core_copy(part, matrix):
        slot = lax.rem(part, 2)
        return send(
            g.grads.at[matrix, :, 1 - core],
            g.core_got.at[slot, matrix],
            (g.core_s, g.core_r),
            (slot, matrix),
            other_core,
        )

    places_one = (snap_low, snap_high)
    places_two = (snap_high, snap_low)
    beside_one = (beside_low, beside_high)
    beside_two = (beside_high, beside_low)

    def half_copy(part, matrix):
        slot = lax.rem(part, 2)
        place = lax.rem(part, 4)
        return send(
            g.half_out.at[slot, matrix, 1 - places_one[matrix]],
            g.half_got.at[place, matrix],
            (g.half_s, g.half_r),
            (place, matrix),
            at(beside_one[matrix], me_sp),
        )

    def quarter_copy(part, matrix):
        slot = lax.rem(part, 2)
        return send(
            g.quarter_out.at[slot, matrix, 1 - places_two[matrix]],
            g.quarter_got.at[slot, matrix],
            (g.quarter_s, g.quarter_r),
            (slot, matrix),
            at(beside_two[matrix], me_sp),
        )

    def level_copy(part, step):
        slot = lax.rem(part, 2)
        place = lax.rem(part, 4)
        target = level_after(step)
        return send(
            g.level_out.at[slot, target],
            g.level_got.at[place, level],
            (g.level_s, g.level_r),
            (place, step),
            at(me_snap, 2 * target + core),
        )

    def last_copy(part, step):
        view = g.total.at[part, me_snap]
        return send(view, view, (g.last_s, g.last_r), (part, step), at(snap_after(step), me_sp))

    def half_stage(part):
        slot = lax.rem(part, 2)
        for matrix in range(2):

            if part >= 2:
                half_copy(part - 2, matrix).wait_send()

            core_copy(part, matrix).wait_recv()

            @pl.loop(0, levels)
            def _(row, matrix=matrix):
                both = g.grads[matrix, row, core].astype(f32) + g.core_got[
                    slot, matrix, row
                ].astype(f32)
                both = both.astype(low)
                g.half_out[slot, matrix, 0, row] = both[:, 0:half]
                g.half_out[slot, matrix, 1, row] = both[:, half:width]

            half_copy(part, matrix).start()

    def quarter_stage(part):
        slot = lax.rem(part, 2)
        for matrix in range(2):

            if part >= 2:
                quarter_copy(part - 2, matrix).wait_send()

            half_copy(part, matrix).wait_recv()
            for row in range(levels):
                both = g.half_out[slot, matrix, places_one[matrix], row].astype(f32) + g.half_got[
                    lax.rem(part, 4), matrix, row
                ].astype(f32)
                both = both.astype(low)
                g.quarter_out[slot, matrix, 0, row] = both[:, 0:quarter]
                g.quarter_out[slot, matrix, 1, row] = both[:, quarter:half]
            quarter_copy(part, matrix).start()

    def level_stage(part):
        slot = lax.rem(part, 2)

        if part >= 2:
            for step in range(1, levels):
                level_copy(part - 2, step).wait_send()

        for matrix in range(2):
            quarter_copy(part, matrix).wait_recv()
            for row in range(levels):
                both = g.quarter_out[slot, matrix, places_two[matrix], row].astype(
                    f32
                ) + g.quarter_got[slot, matrix, row].astype(f32)
                g.level_out[slot, row, matrix] = both.astype(low)
        for step in range(1, levels):
            level_copy(part, step).start()

    def last_stage(part):
        slot = lax.rem(part, 2)
        for step in range(1, levels):
            level_copy(part, step).wait_recv()
        for matrix in range(2):
            sums = g.level_out[slot, level, matrix].astype(f32)
            for step in range(1, levels):
                sums += g.level_got[lax.rem(part, 4), level_before(step), matrix].astype(f32)
            g.total[part, me_snap, matrix] = sums.astype(low)
        for step in range(1, snaps):
            last_copy(part, step).start()

    stages |= {HALF: half_stage, QUARTER: quarter_stage, LEVEL: level_stage, LAST: last_stage}

    def weight(part, matrix):
        return jnp.concatenate([g.all_w[spot(part), matrix, place] for place in range(snaps)], axis=1)

    def add_products(part, rows):
        g.grid[rows, :] += dot_nt(g.act[rows, :], weight(part, 1))
        g.back[rows, :] += dot_nt(g.slope[rows, :], weight(part, 0))

    @pl.loop(0, parts)
    def _(part):
        def reach_in(point, also=True):
            for at_part in range(parts):
                if (point, at_part) in SCHEDULE:
                    pl.when((part == at_part) & also)(functools.partial(reach, (point, at_part)))

        def tile_rows(step):
            return pl.ds(pl.multiple_of(step * tile, tile), tile)

        fourth_copy(part).wait_recv()
        reach_in("k")
        g.grad_bias[part] = jnp.zeros(g.grad_bias.shape[1:], f32)

        act, slope = gelu_both(dot_nn(g.normed[...], weight(part, 0)) + g.bias[part])
        g.act[...] = act.astype(low)
        slope = (dot_nn(g.cot_in[...], weight(part, 1)) * slope).astype(low)
        g.slope[...] = slope
        g.grad_bias[part] += fold(slope.astype(f32))
        for at_step in range(3):
            reach_in("k" + str(at_step))

        reach_in("l")

        @pl.when(part >= 1)
        def _():
            for matrix in range(2):
                core_copy(part - 1, matrix).wait_send()

        shape = g.grads.shape[1:]
        g.grads[0] = dot_nn(g.normed_turned[...], g.slope[...]).astype(low).reshape(shape)
        core_copy(part, 0).start()
        g.grads[1] = dot_nn(g.cot_turned[...], g.act[...]).astype(low).reshape(shape)
        core_copy(part, 1).start()
        reach_in("m")

        @pl.when(part < parts - 1)
        def _():
            @pl.loop(0, tokens // tile)
            def _(step):
                add_products(part, tile_rows(step))
                for at_step in range(3):
                    reach_in("m" + str(at_step), step == (at_step + 1) // 2)

    g.folds[...] = jnp.zeros_like(g.folds)

    def second_back(rows):
        grad = g.back[rows, :]
        unit = g.unit_two[rows, :].astype(f32)
        cot = g.cot_in[rows, :].astype(f32)
        pulled = grad * g.gains[2:3, :]
        middle = jnp.mean(pulled, axis=-1, keepdims=True)
        slant = jnp.mean(pulled * unit, axis=-1, keepdims=True)
        total = cot + g.scale_two[rows, :] * (pulled - middle - unit * slant)
        g.back[rows, :] = total
        g.normed[rows, :] = total.astype(low)
        g.folds[2] += fold(grad * unit)
        g.folds[3] += fold(grad)
        g.folds[4] += fold(cot)

    loads["lon_it"].wait()
    for part in range(2):

        @pl.loop(0, half_tokens // short)
        def _(step, part=part):
            first_row = part * half_tokens + step * short
            add_products(parts - 1, pl.ds(pl.multiple_of(first_row, 16), short))

        reach("o" + str(part))
        half_strips(second_back, part)
        for step in range(1, group):
            block_copy(0, part, step).wait_send()
        to_blocks(g.lon_it_in[...], 1, part)
        reach("p" + str(part))
    reach("q")

    def low_out(rows):
        g.fields_in[rows, :] = g.grid[rows, :].astype(low)

    strips(low_out, after=lambda place: out_copy(place).start())
    reach("r")
    loads["valid"].wait()
    loads["turn"].wait()
    weigh = sum(
        dot_nn(g.valid_in[:, row, :].astype(f32).astype(low), g.turn_in[row])
        for row in range(g.valid.shape[1])
    )
    places_each = weigh.shape[1]
    precise = lax.Precision.HIGHEST
    sums = [jnp.zeros((1, 128), f32), jnp.zeros((1, 128), f32)]
    for snap in range(g.valid.shape[0]):
        variables = g.grid[snap * places_each : (snap + 1) * places_each, 0:128]
        for index, value in enumerate((variables, variables * variables)):
            sums[index] += jnp.dot(
                weigh[snap : snap + 1, :], value, precision=precise, preferred_element_type=f32
            )

    reach("s")

    def dot_tn(left, right):
        return lax.dot_general(
            left, right, (((0,), (0,)), ((), ())), preferred_element_type=f32
        )

    def filter_rows(first, grad):
        g.pair_grad[...] = grad
        real = g.pair_grad[0:128, 0:128] + g.pair_grad[128:256, 128:256]
        imag = g.pair_grad[0:128, 128:256] - g.pair_grad[128:256, 0:128]
        g.filt_out[me_snap, first] = real[0:owned].astype(low)
        g.filt_out[me_snap, first + 1] = imag[0:owned].astype(low)

    for part in range(2):
        take_blocks(1, part)
        reach("t" + str(part))
        rows = mode_half(part)
        spectra(g.grad_pre, f32, part)
        bend = jnp.tanh(g.pre_two[rows, :] / shrink_level)
        grad = (g.grad_pre[rows, :] * keep_half() * (bend * bend)).astype(low)
        g.grad_two[rows, :] = grad
        grad = dot_nt(grad, g.weight_two[...]) * gelu_both(g.pre_one[rows, :])[1]
        grad = grad.astype(low)
        g.grad_one[rows, :] = grad
        for step in range(1, group):
            row_copy(0, part, step).wait_send()
        to_rows(1, part, grids(dot_nt(grad, g.weight_one[...]).astype(low)))
        reach("u" + str(part))
    reach("v")
    bias_one = jnp.sum(g.grad_one[...].astype(f32), axis=0, keepdims=True)
    bias_two = jnp.sum(g.grad_two[...].astype(f32), axis=0, keepdims=True)
    filter_rows(2, dot_tn(g.act_one[...], g.grad_two[...]))
    filter_rows(0, dot_tn(g.spectrum[...], g.grad_one[...]))

    def filter_copy(step):
        view = g.filt_out.at[me_snap]
        return send(view, view, (g.filt_s, g.filt_r), step, at(snap_after(step), me_sp))

    for step in range(1, snaps):
        filter_copy(step).start()


    reach("w")

    loads["lon_ft"].wait()

    def first_back(rows):
        grad = g.grid[rows, :]
        unit = g.unit_one[rows, :].astype(f32)
        pulled = grad * g.gains[0:1, :]
        middle = jnp.mean(pulled, axis=-1, keepdims=True)
        slant = jnp.mean(pulled * unit, axis=-1, keepdims=True)
        g.grid[rows, :] = g.back[rows, :] + g.scale_one[rows, :] * (
            pulled - middle - unit * slant
        )
        g.folds[0] += fold(grad * unit)
        g.folds[1] += fold(grad)

    for part in range(2):
        home_modes(1, part)
        reach("x" + str(part))
        g.grid[half_rows(part), :] = g.back[half_rows(part), :] + dot_nn(
            g.lon_ft_in[...], g.home_low[part]
        )
        half_strips(first_back, part, after=lambda place: grad_copy(place).start())
        reach("y" + str(part))

    g.grad_rows[...] = jnp.zeros_like(g.grad_rows)
    for index, row in enumerate((0, 1, 2, 3, 8)):
        g.grad_rows[row : row + 1, :] = jnp.sum(g.folds[index], axis=0, keepdims=True)
    flat = jnp.concatenate(
        [jnp.sum(g.grad_bias[part], axis=0, keepdims=True) for part in range(parts)], axis=1
    )
    for row in range(rows_small - 9):
        g.grad_rows[9 + row : 10 + row, :] = flat[:, row * channel : (row + 1) * channel]
    for block in range(group):
        g.tiles[block] = jnp.zeros(g.tiles.shape[1:], f32)
        g.tiles[block, :, 0:owned] = g.grad_rows[:, block * owned : (block + 1) * owned]
        g.tiles[block, 13:14, :] = sums[0]
        g.tiles[block, 14:15, :] = sums[1]

    def tile_copy(step):
        target = sp_after(step)
        return send(
            g.tiles.at[target], g.tiles_got.at[me_sp], (g.tile_s, g.tile_r), step, at(me_snap, target)
        )

    def snap_tile_copy(step):
        view = g.snap_tiles.at[me_snap]
        return send(view, view, (g.snap_tile_s, g.snap_tile_r), step, at(snap_after(step), me_sp))

    for step in range(1, group):
        tile_copy(step).start()
    reach("z")

    for batch in range(len(swaps)):
        swap_copy(batch).wait_send()
    for part in range(parts):
        if part < parts - 1:
            second_copy(part).wait_send()
            third_copy(part).wait_send()
        fourth_copy(part).wait_send()
        for step in range(1, levels):
            first_copy(part, step).wait_send()
    for step in range(1, group):
        small_copy(step).wait_send()
        for part in range(2):
            block_copy(1, part, step).wait_send()
            row_copy(1, part, step).wait_send()
    for matrix in range(2):
        core_copy(parts - 1, matrix).wait_send()
        for part in (parts - 2, parts - 1):
            half_copy(part, matrix).wait_send()
            quarter_copy(part, matrix).wait_send()
    for step in range(1, levels):
        level_copy(parts - 2, step).wait_send()
    for step in range(1, snaps):
        filter_copy(step).wait_send()

    g.tiles_got[me_sp] = g.tiles[me_sp]
    for step in range(1, group):
        tile_copy(step).wait_recv()
    tile_sum = g.tiles_got[0]
    for sp in range(1, group):
        tile_sum += g.tiles_got[sp]
    g.snap_tiles[me_snap] = tile_sum
    g.snap_tiles[me_snap, 4:5, :] = bias_one[:, 0:128]
    g.snap_tiles[me_snap, 5:6, :] = bias_one[:, 128:256]
    g.snap_tiles[me_snap, 6:7, :] = bias_two[:, 0:128]
    g.snap_tiles[me_snap, 7:8, :] = bias_two[:, 128:256]
    for step in range(1, snaps):
        snap_tile_copy(step).start()

    for step in range(1, snaps):
        filter_copy(step).wait_recv()
    filter_sum = g.filt_out[0].astype(f32)
    for snap in range(1, snaps):
        filter_sum += g.filt_out[snap].astype(f32)
    g.grad_filt[...] = filter_sum
    for part in range(parts):
        for step in range(1, snaps):
            last_copy(part, step).wait_recv()
    grads_out = pltpu.make_async_copy(g.total, g.grad_mlp, g.load_sem.at[3])
    grads_out.start()
    for step in range(1, snaps):
        snap_tile_copy(step).wait_recv()
    tile_sum = g.snap_tiles[0]
    for snap in range(1, snaps):
        tile_sum += g.snap_tiles[snap]
    g.grad_small[...] = tile_sum

    grads_out.wait()
    for place in range(tokens // strip):
        out_copy(place).wait()
        grad_copy(place).wait()
    for step in range(1, levels):
        level_copy(parts - 1, step).wait_send()
    for step in range(1, group):
        tile_copy(step).wait_send()
    for step in range(1, snaps):
        snap_tile_copy(step).wait_send()
        for part in range(parts):
            last_copy(part, step).wait_send()


def block_pass(fields, cot, valid, kept, mlp, filt, small, snaps, group):
    snap_local, row_local, lon_total, channel = fields.shape
    tokens = snap_local * row_local * lon_total
    hidden = mlp.shape[2]
    lat_total = row_local * group
    modes = kept.shape[1] * group
    owned = channel // group
    width = 512
    parts = hidden // width
    levels = group // 2
    quarter = width // snaps
    low, f32 = jnp.bfloat16, jnp.float32
    half = width // 2
    half_snaps = snap_local // 2
    lon_f, lon_i = lon_matrix(lon_total, modes, half_snaps, row_local)

    def paired(array):
        return jnp.transpose(array, (0, 2, 1, 3)).reshape(-1, row_local, channel)

    lat_f = lat_matrix(lat_total, modes)
    pair = 2 * modes * row_local
    spread = half_snaps * row_local * 2 * modes
    inputs = dict(
        small=small,
        kept=kept.T,
        fields=paired(fields),
        lon_f=jnp.asarray(np.ascontiguousarray(lon_f.T)),
        filt=filt,
        lat_f=jnp.asarray(lat_f),
        lat_b=jnp.asarray(np.ascontiguousarray(lat_f.T)),
        cot=paired(cot),
        lon_i=jnp.asarray(lon_i),
        valid=valid,
        turn=jnp.asarray(lon_turn(lon_total, row_local)),
        lon_it=jnp.asarray(np.ascontiguousarray(lon_i.T)),
        lon_ft=jnp.asarray(lon_f),
        mlp=mlp,
    )
    outputs = dict(
        out=jax.ShapeDtypeStruct((tokens // row_local, row_local, channel), low),
        in_grad=jax.ShapeDtypeStruct((tokens // row_local, row_local, channel), f32),
        grad_mlp=jax.ShapeDtypeStruct((parts, snaps, 2, owned, quarter), low),
        grad_filt=jax.ShapeDtypeStruct((4, owned, 128), f32),
        grad_small=jax.ShapeDtypeStruct((16, 128), f32),
    )
    vmem = pltpu.VMEM
    dma = pltpu.SemaphoreType.DMA
    scratch = {
        name + "_in": vmem(value.shape, value.dtype)
        for name, value in inputs.items()
        if name not in ("mlp", "fields", "cot")
    }
    strip = divisor(tokens // 2, 48, 144)
    scratch |= dict(
        mlp_part=vmem((2, 2, owned, width), f32),
        fields_in=vmem((tokens, channel), low),
        fields_sem=dma((tokens // strip,)),
        cot_sem=dma((tokens // strip,)),
        cot_in=vmem((tokens, channel), low),
        grid=vmem((tokens, channel), f32),
        back=vmem((tokens, channel), f32),
        normed=vmem((tokens, channel), low),
        normed_turned=vmem((channel, tokens), low),
        cot_turned=vmem((channel, tokens), low),
        unit_one=vmem((tokens, channel), low),
        unit_two=vmem((tokens, channel), low),
        scale_one=vmem((tokens, 1), f32),
        scale_two=vmem((tokens, 1), f32),
        own_small=vmem((16 + kept.shape[0], 128), f32),
        all_small=vmem((group, 16 + kept.shape[0], 128), f32),
        gains=vmem((16, channel), f32),
        keep=vmem((lat_total * modes, 128), f32),
        own_w=vmem((parts, 2, snaps, owned, quarter), low),
        all_w=vmem((parts, 2, snaps, channel, quarter), low),
        modes=vmem((2, group, half_snaps * pair * 3 // 4, 128), low),
        modes_got=vmem((2, group, half_snaps * pair * 3 // 4, 128), low),
        rows_out=vmem((2, group, half_snaps * pair * 3 // 4, 128), low),
        rows_got=vmem((2, group, half_snaps * pair * 3 // 4, 128), low),
        arrived=vmem((snap_local, pair * group, 128), low),
        gathered=vmem((2, spread, channel), f32),
        home_low=vmem((2, spread, channel), low),
        weight_one=vmem((256, 256), low),
        weight_two=vmem((256, 256), low),
        spectrum=vmem((snap_local * lat_total * modes, 256), low),
        pre_one=vmem((snap_local * lat_total * modes, 256), f32),
        act_one=vmem((snap_local * lat_total * modes, 256), low),
        pre_two=vmem((snap_local * lat_total * modes, 256), f32),
        grad_pre=vmem((snap_local * lat_total * modes, 256), f32),
        grad_two=vmem((snap_local * lat_total * modes, 256), low),
        grad_one=vmem((snap_local * lat_total * modes, 256), low),
        folds=vmem((5, 8, channel), f32),
        pair_grad=vmem((256, 256), f32),
        act=vmem((tokens, width), low),
        slope=vmem((tokens, width), low),
        bias=vmem((parts, 1, width), f32),
        grad_bias=vmem((parts, 8, width), f32),
        grad_rows=vmem((16, channel), f32),
        grads=vmem((2, levels, 2, owned, width), low),
        core_got=vmem((2, 2, levels, owned, width), low),
        half_out=vmem((2, 2, 2, levels, owned, half), low),
        half_got=vmem((4, 2, levels, owned, half), low),
        quarter_out=vmem((2, 2, 2, levels, owned, quarter), low),
        quarter_got=vmem((2, 2, levels, owned, quarter), low),
        level_out=vmem((2, levels, 2, owned, quarter), low),
        level_got=vmem((4, levels, 2, owned, quarter), low),
        total=vmem((parts, snaps, 2, owned, quarter), low),
        filt_out=vmem((snaps, 4, owned, 128), low),
        tiles=vmem((group, 16, 128), f32),
        tiles_got=vmem((group, 16, 128), f32),
        snap_tiles=vmem((snaps, 16, 128), f32),
        swap_l=dma((4,)),
        load_sem=dma((len(inputs) + 1,)),
    )
    for name, shape in dict(
        small=(group,),
        swap=(4,),
        first=(parts, levels),
        second=(parts,),
        third=(parts,),
        fourth=(parts,),
        block=(2, 2, group),
        row=(2, 2, group),
        core=(2, 2),
        half=(4, 2),
        quarter=(2, 2),
        level=(4, levels),
        last=(parts, snaps),
        filt=(snaps,),
        tile=(group,),
        snap_tile=(snaps,),
    ).items():
        scratch[name + "_s"] = dma(shape)
        scratch[name + "_r"] = dma(shape)
    names = [*inputs, *outputs, *scratch]
    far = pl.BlockSpec(memory_space=pl.ANY)
    near = pl.BlockSpec(memory_space=pltpu.VMEM)
    results = pl.pallas_call(
        functools.partial(block_body, names, (snaps, group, parts, width)),
        in_specs=[far] * len(inputs),
        out_specs=[far, far, far, near, near],
        out_shape=list(outputs.values()),
        scratch_shapes=list(scratch.values()),
        compiler_params=pltpu.CompilerParams(
            collective_id=0, has_side_effects=True, vmem_limit_bytes=VMEM_LIMIT
        ),
        cost_estimate=pl.CostEstimate(
            flops=12 * tokens * channel * hidden,
            bytes_accessed=4 * hidden * channel,
            transcendentals=tokens * hidden,
        ),
        name="block_pass",
    )(*inputs.values())
    return results


def adamw_near(master, first_mom, second_mom, gradient, step_rate):
    first_next = beta_one * (first_mom + gradient)
    second_next = beta_two * (second_mom + gradient * gradient)
    fix_one = 1.0 / (1.0 - beta_one**STEP)
    fix_two = 1.0 / (1.0 - beta_two**STEP)
    grown = second_next * fix_two
    bottom = grown * lax.rsqrt(grown) + adam_eps
    master_next = (1.0 - step_rate * decay_rate) * master - (
        (step_rate * fix_one) * first_next
    ) / bottom
    return (master_next, first_next, second_next, master_next.astype(jnp.bfloat16))


def step_body(names, positions, *refs):
    g = Refs()
    for name, ref in zip(names, refs, strict=True):
        setattr(g, name, ref)
    parts, snaps = g.grad_mlp.shape[:2]
    quarter = g.grad_mlp.shape[4]
    width = snaps * quarter
    chunks = g.near.shape[1]
    some = parts // chunks
    moments = ("w", "m", "v")
    results = ("new", "first", "second", "copy")

    pieces = g.far_sem.shape[2]
    ends = ((g.out, g.out_near, g.out_o), (g.in_grad, g.in_grad_near, g.in_grad_o))

    def passing(kind, piece, leg):
        size = ends[kind][0].shape[0] // pieces
        rows = pl.ds(piece * size, size)
        return pltpu.make_async_copy(
            ends[kind][leg].at[rows], ends[kind][leg + 1].at[rows], g.far_sem.at[leg, kind, piece]
        )

    through = [(kind, piece) for kind in range(2) for piece in range(pieces)]

    def chunk_cols(chunk):
        return pl.ds(chunk * some * width, some * width)

    def load(chunk):
        near = [
            pltpu.make_async_copy(
                getattr(g, "mlp_" + kind).at[:, :, chunk_cols(chunk)],
                g.near.at[index, chunk],
                g.near_sem.at[index, chunk],
            )
            for index, kind in enumerate(moments)
        ]
        near.append(
            pltpu.make_async_copy(
                g.grad_mlp.at[pl.ds(chunk * some, some)], g.grad_near.at[chunk], g.near_sem.at[3, chunk]
            )
        )
        return near

    def store(chunk):
        copies = [
            pltpu.make_async_copy(
                g.near.at[index, chunk],
                getattr(g, "mlp_" + kind).at[:, :, chunk_cols(chunk)],
                g.back_sem.at[index, chunk],
            )
            for index, kind in enumerate(results[:3])
        ]
        copies.append(
            pltpu.make_async_copy(
                g.low_near.at[chunk], g.mlp_copy.at[:, :, chunk_cols(chunk)], g.back_sem.at[3, chunk]
            )
        )
        return copies

    coming = [load(chunk) for chunk in range(chunks)]
    going = [store(chunk) for chunk in range(chunks)]
    for chunk in range(chunks):
        for copy in coming[chunk]:
            copy.start()
        for each in through[chunk::chunks]:
            passing(*each, 0).start()

    def put(prefix, values):
        for kind, value in zip(results, values, strict=True):
            getattr(g, prefix + kind)[...] = value

    owned = g.filt_w.shape[2]
    put(
        "filt_",
        adamw(g.filt_w[...], g.filt_m[...], g.filt_v[...], g.grad_filt[:, :, 0:owned], rate_filter),
    )
    rows = g.small_w.shape[0]
    put(
        "small_",
        adamw(
            g.small_w[...], g.small_m[...], g.small_v[...], g.grad_small[0:rows, 0:owned], rate_small
        ),
    )
    totals = g.grad_small[rows : rows + 2, 0 : g.run.shape[1]]
    g.stats[...] = stat_decay * g.run[...] + (1.0 - stat_decay) * totals / positions

    for chunk in range(chunks):
        for copy in coming[chunk]:
            copy.wait()
        for part, matrix, snap in [
            (part, matrix, snap)
            for part in range(some)
            for matrix in range(2)
            for snap in range(snaps)
        ]:
            place = snap if matrix else 2 * (snap % 2) + snap // 2
            first_col = part * width + place * quarter
            where = (chunk, matrix, slice(None), slice(first_col, first_col + quarter))
            now = [g.near[(kind, *where)] for kind in range(3)]
            grad = g.grad_near[chunk, part, snap, matrix].astype(jnp.float32)
            values = adamw_near(*now, grad, rate_mlp)
            for kind in range(3):
                g.near[(kind, *where)] = values[kind]
            g.low_near[where] = values[3]
        for copy in going[chunk]:
            copy.start()
        for each in through[chunk::chunks]:
            passing(*each, 0).wait()
            passing(*each, 1).start()
    for each in through:
        passing(*each, 1).wait()
    for chunk in range(chunks):
        for copy in going[chunk]:
            copy.wait()


def step_pass(shown, grads, masters, run_stats, positions):
    grad_mlp, grad_filt, grad_small = grads
    mlp, filt, small = masters
    chunks = grad_mlp.shape[0]
    width = mlp[0].shape[2] // chunks
    f32, low = jnp.float32, jnp.bfloat16
    far = pl.BlockSpec(memory_space=pltpu.HBM)
    near = pl.BlockSpec(memory_space=pltpu.VMEM)
    inputs = dict(out=shown[0], in_grad=shown[1], grad_mlp=grad_mlp)
    inputs |= dict(zip(("mlp_w", "mlp_m", "mlp_v"), mlp, strict=True))
    far_in = len(inputs)
    inputs |= dict(grad_filt=grad_filt, grad_small=grad_small)
    inputs |= dict(zip(("filt_w", "filt_m", "filt_v"), filt, strict=True))
    inputs |= dict(zip(("small_w", "small_m", "small_v"), small, strict=True))
    inputs |= dict(run=run_stats)
    results = (("new", f32), ("first", f32), ("second", f32), ("copy", low))
    outputs = {
        name + "_o": jax.ShapeDtypeStruct(array.shape, array.dtype)
        for name, array in zip(("out", "in_grad"), shown, strict=True)
    }
    outputs |= {"mlp_" + kind: jax.ShapeDtypeStruct(mlp[0].shape, dt) for kind, dt in results}
    far_out = len(outputs)
    outputs |= {"filt_" + kind: jax.ShapeDtypeStruct(filt[0].shape, dt) for kind, dt in results}
    outputs |= {"small_" + kind: jax.ShapeDtypeStruct(small[0].shape, dt) for kind, dt in results}
    outputs |= dict(stats=jax.ShapeDtypeStruct(run_stats.shape, f32))
    scratch = dict(
        near=pltpu.VMEM((3, chunks, 2, mlp[0].shape[1], width), f32),
        grad_near=pltpu.VMEM((chunks, grad_mlp.shape[0] // chunks, *grad_mlp.shape[1:]), low),
        low_near=pltpu.VMEM((chunks, 2, mlp[0].shape[1], width), low),
        near_sem=pltpu.SemaphoreType.DMA((4, chunks)),
        back_sem=pltpu.SemaphoreType.DMA((4, chunks)),
        out_near=pltpu.VMEM(shown[0].shape, low),
        in_grad_near=pltpu.VMEM(shown[1].shape, f32),
        far_sem=pltpu.SemaphoreType.DMA((2, 2, divisor(shown[0].shape[0], 1, 4))),
    )
    return pl.pallas_call(
        functools.partial(step_body, [*inputs, *outputs, *scratch], positions),
        in_specs=[far] * far_in + [near] * (len(inputs) - far_in),
        out_specs=[far] * far_out + [near] * (len(outputs) - far_out),
        out_shape=list(outputs.values()),
        scratch_shapes=list(scratch.values()),
        compiler_params=pltpu.CompilerParams(vmem_limit_bytes=VMEM_LIMIT),
        name="step_pass",
    )(*inputs.values())


def per_device_blocks(
    fields,
    cotangent,
    valid_mask,
    kept_modes,
    mlp_master,
    mlp_first,
    mlp_second,
    filter_master,
    filter_first,
    filter_second,
    small_master,
    small_first,
    small_second,
    run_stats,
):
    snaps, group = lax.axis_size("snap"), lax.axis_size("sp")
    out, in_grad, *grads = block_pass(
        fields, cotangent, valid_mask, kept_modes, mlp_master, filter_master, small_master, snaps, group
    )
    snap_local, row_local, lon_total, channel = fields.shape
    positions = snap_local * snaps * row_local * group * lon_total
    out, in_grad, *stepped = step_pass(
        (out, in_grad),
        grads,
        (
            (mlp_master, mlp_first, mlp_second),
            (filter_master, filter_first, filter_second),
            (small_master, small_first, small_second),
        ),
        run_stats,
        positions,
    )
    rows_apart = (snap_local, lon_total, row_local, channel)
    out, in_grad = [
        jnp.transpose(array.reshape(rows_apart), (0, 2, 1, 3)) for array in (out, in_grad)
    ]
    return (out, in_grad, *stepped)


def per_device(*arrays):
    group, snaps = lax.axis_size("sp"), lax.axis_size("snap")
    channel, hidden = arrays[0].shape[3], arrays[4].shape[2]
    by_block = group == BLOCKS and snaps == 4 and arrays[3].shape[1] == 1
    if by_block and hidden == 6 * 512 and channel // group <= 128 and channel % (16 * group) == 0:
        return per_device_blocks(*arrays)
    return per_device_modes(*arrays)


def solution(mesh):
    return jax.shard_map(
        per_device,
        mesh=mesh,
        in_specs=(
            P("snap", "sp", None, None),
            P("snap", "sp", None, None),
            P("snap", "sp", None),
            P(None, "sp"),
            P(None, "sp", None),
            P(None, "sp", None),
            P(None, "sp", None),
            P(None, "sp", None),
            P(None, "sp", None),
            P(None, "sp", None),
            P(None, "sp"),
            P(None, "sp"),
            P(None, "sp"),
            P(),
        ),
        out_specs=(
            P("snap", "sp", None, None),
            P("snap", "sp", None, None),
            P(None, "sp", None),
            P(None, "sp", None),
            P(None, "sp", None),
            P(None, "sp", None),
            P(None, "sp", None),
            P(None, "sp", None),
            P(None, "sp", None),
            P(None, "sp", None),
            P(None, "sp"),
            P(None, "sp"),
            P(None, "sp"),
            P(None, "sp"),
            P(),
        ),
        check_vma=False,
    )
```

```python
import functools
import math

import jax
import jax.numpy as jnp
import ml_dtypes
import numpy as np
from jax import lax
from jax.experimental import pallas as pl
from jax.experimental.pallas import tpu as pltpu
from jax.sharding import PartitionSpec as P

BLOCKS = 8
NVAR = 20
STEP = 10
VMEM_LIMIT = 63 * 1024 * 1024


eps_norm = 1e-06
shrink_level = 0.01
beta_one = 0.5
beta_two = 0.5
adam_eps = 1e-08
decay_rate = 0.01
rate_mlp = 0.03
rate_filter = 0.1
rate_small = 0.2
stat_decay = 0.5


def layer_norm(values, gain_vec, shift_vec):
    centred = values - jnp.mean(values, axis=-1, keepdims=True)
    spread = jnp.mean(centred * centred, axis=-1, keepdims=True)
    return centred * lax.rsqrt(spread + eps_norm) * gain_vec + shift_vec


def shrink(values):
    return values - shrink_level * jnp.tanh(values / shrink_level)


def lon_tables(lon_total, mode_total):
    places = jnp.arange(lon_total, dtype=jnp.int32)
    orders = jnp.arange(mode_total, dtype=jnp.int32)
    angles = (places[:, None] * orders[None, :] % lon_total).astype(jnp.float32) * (
        2.0 * math.pi / lon_total
    )
    scaling = 1.0 / math.sqrt(lon_total)
    forward_tab = jnp.stack([jnp.cos(angles), -jnp.sin(angles)], axis=1) * scaling
    doubling = jnp.where(orders == 0, 1.0, 2.0).astype(jnp.float32)[:, None]
    inverse_tab = (
        jnp.stack([jnp.cos(angles).T * doubling, -jnp.sin(angles).T * doubling], axis=0) * scaling
    )
    return (forward_tab.astype(jnp.bfloat16), inverse_tab.astype(jnp.bfloat16))


def lat_table(lat_total):
    places = jnp.arange(lat_total, dtype=jnp.int32)
    angles = (places[:, None] * places[None, :] % lat_total).astype(jnp.float32) * (
        2.0 * math.pi / lat_total
    )
    cosine = jnp.cos(angles)
    sine_part = jnp.sin(angles)
    upper_rows = jnp.stack([cosine, sine_part], axis=1)
    bottom = jnp.stack([-sine_part, cosine], axis=1)
    return (jnp.stack([upper_rows, bottom], axis=0) / math.sqrt(lat_total)).astype(jnp.bfloat16)


def complex_pair(real_part, imag_part):
    return jnp.stack([jnp.stack([real_part, -imag_part]), jnp.stack([imag_part, real_part])])


gelu_scale = math.sqrt(2.0 / math.pi)
gelu_cubic = 0.044715


def gelu_both(value):
    bend = (gelu_scale * gelu_cubic) * (value * value)
    turn = jnp.tanh(value * (gelu_scale + bend))
    half = 0.5 + 0.5 * turn
    slope = half * (1.0 + (value * (1.0 - turn)) * (gelu_scale + 3.0 * bend))
    return value * half, slope


def dot_nt(left, right):
    return lax.dot_general(
        left, right, (((1,), (1,)), ((), ())), preferred_element_type=jnp.float32
    )


def dot_nn(left, right):
    return jnp.dot(left, right, preferred_element_type=jnp.float32)


def divisor(total, unit, most):
    return max(size for size in range(unit, most + 1, unit) if total % size == 0)


def mlp_body(
    tile,
    normed_ref,
    cot_ref,
    up_ref,
    down_ref,
    bias_ref,
    out_ref,
    back_ref,
    grad_up_ref,
    grad_down_ref,
    grad_bias_ref,
    normed_turned,
    cot_turned,
    act_ref,
    slope_ref,
):
    tokens = normed_ref.shape[0]

    @pl.when(pl.program_id(0) == 0)
    def _():
        normed_turned[...] = normed_ref[...].T
        cot_turned[...] = cot_ref[...].T
        out_ref[...] = jnp.zeros_like(out_ref)
        back_ref[...] = jnp.zeros_like(back_ref)

    grad_bias_ref[...] = jnp.zeros_like(grad_bias_ref)

    @pl.loop(0, tokens // tile)
    def _(step):
        rows = pl.ds(pl.multiple_of(step * tile, tile), tile)
        act, slope = gelu_both(dot_nn(normed_ref[rows, :], up_ref[...]) + bias_ref[...])
        act = act.astype(jnp.bfloat16)
        slope = (dot_nn(cot_ref[rows, :], down_ref[...]) * slope).astype(jnp.bfloat16)
        act_ref[rows, :] = act
        slope_ref[rows, :] = slope
        grad_bias_ref[...] += jnp.sum(slope.astype(jnp.float32), axis=0, keepdims=True)
        out_ref[rows, :] += dot_nt(act, down_ref[...])
        back_ref[rows, :] += dot_nt(slope, up_ref[...])

    grad_up_ref[...] = dot_nn(normed_turned[...], slope_ref[...]).astype(grad_up_ref.dtype)
    grad_down_ref[...] = dot_nn(cot_turned[...], act_ref[...]).astype(grad_down_ref.dtype)


def mlp_pass(normed, cot, weights, bias):
    tokens, channel = normed.shape
    hidden = weights.shape[2]
    width = divisor(hidden, 128, 512)
    tile = divisor(tokens, 16, 480)
    whole = pl.BlockSpec((tokens, channel), lambda j: (0, 0))
    block = pl.BlockSpec((channel, width), lambda j: (0, j))
    line = pl.BlockSpec((1, width), lambda j: (0, j))
    part = lambda which: pl.BlockSpec((None, channel, width), lambda j: (which, 0, j))
    total = jax.ShapeDtypeStruct((tokens, channel), jnp.float32)
    grads = jax.ShapeDtypeStruct((channel, hidden), jnp.bfloat16)
    return pl.pallas_call(
        functools.partial(mlp_body, tile),
        grid=(hidden // width,),
        in_specs=[whole, whole, part(0), part(1), line],
        out_specs=[whole, whole, block, block, line],
        out_shape=[total, total, grads, grads, jax.ShapeDtypeStruct((1, hidden), jnp.float32)],
        scratch_shapes=[
            pltpu.VMEM((channel, tokens), jnp.bfloat16),
            pltpu.VMEM((channel, tokens), jnp.bfloat16),
            pltpu.VMEM((tokens, width), jnp.bfloat16),
            pltpu.VMEM((tokens, width), jnp.bfloat16),
        ],
        compiler_params=pltpu.CompilerParams(vmem_limit_bytes=56 * 1024 * 1024),
        cost_estimate=pl.CostEstimate(
            flops=12 * tokens * channel * hidden,
            bytes_accessed=8 * channel * hidden + 12 * tokens * channel,
            transcendentals=tokens * hidden,
        ),
        name="mlp_pass",
    )(normed, cot, weights, weights, bias)


def spectral_front(arrived, lat_fwd, first_pair, second_pair, bias_one, bias_two):
    spectrum = jnp.einsum(
        "pkqr,nrqmd->nkpmd", lat_fwd, arrived, preferred_element_type=jnp.float32
    ).astype(jnp.bfloat16)
    snap_local, lat_total, pair_count, mode_local, channel = spectrum.shape
    blocked = spectrum.reshape(
        snap_local, lat_total, pair_count, mode_local, BLOCKS, channel // BLOCKS
    )
    pre_one = (
        jnp.einsum("nkqmbi,pqbio->nkpmbo", blocked, first_pair, preferred_element_type=jnp.float32)
        + bias_one
    )
    act_one = jax.nn.gelu(pre_one).astype(jnp.bfloat16)
    pre_two = (
        jnp.einsum("nkqmbi,pqbio->nkpmbo", act_one, second_pair, preferred_element_type=jnp.float32)
        + bias_two
    )
    return (blocked, pre_one, act_one, pre_two)


def adamw(master, first_mom, second_mom, gradient, step_rate):
    first_next = beta_one * first_mom + (1.0 - beta_one) * gradient
    second_next = beta_two * second_mom + (1.0 - beta_two) * gradient * gradient
    fix_one = 1.0 / (1.0 - beta_one**STEP)
    fix_two = 1.0 / (1.0 - beta_two**STEP)
    direction = first_next * fix_one / (jnp.sqrt(second_next * fix_two) + adam_eps)
    master_next = master - step_rate * (direction + decay_rate * master)
    return (master_next, first_next, second_next, master_next.astype(jnp.bfloat16))


def per_device_modes(
    fields,
    cotangent,
    valid_mask,
    kept_modes,
    mlp_master,
    mlp_first,
    mlp_second,
    filter_master,
    filter_first,
    filter_second,
    small_master,
    small_first,
    small_second,
    run_stats,
):
    group_size = lax.axis_size("sp")
    snap_local, row_local, lon_total, channel = fields.shape
    lat_total = row_local * group_size
    mode_local = kept_modes.shape[1]
    mode_total = mode_local * group_size
    block_width = channel // BLOCKS
    lon_fwd, lon_inv = lon_tables(lon_total, mode_total)
    lat_fwd = lat_table(lat_total)
    mlp_w, filt_w, small_w = (
        lax.all_gather(mlp_master.astype(jnp.bfloat16), "sp", axis=1, tiled=True),
        lax.all_gather(filter_master.astype(jnp.bfloat16), "sp", axis=1, tiled=True),
        lax.all_gather(small_master.astype(jnp.bfloat16), "sp", axis=1, tiled=True),
    )
    small_f = small_w.astype(jnp.float32)
    weights = filt_w.reshape(4, BLOCKS, block_width, block_width)
    first_pair = complex_pair(weights[0], weights[1])
    second_pair = complex_pair(weights[2], weights[3])
    bias_one = small_f[4:6].reshape(2, 1, BLOCKS, block_width)
    bias_two = small_f[6:8].reshape(2, 1, BLOCKS, block_width)
    fields_float = fields.astype(jnp.float32)
    normed, norm_pull = jax.vjp(layer_norm, fields_float, small_f[0], small_f[1])
    normed_low = normed.astype(jnp.bfloat16)
    spec_lon = jnp.einsum(
        "nrld,lqm->nrqmd", normed_low, lon_fwd, preferred_element_type=jnp.float32
    ).astype(jnp.bfloat16)
    arrived = lax.all_to_all(spec_lon, "sp", split_axis=3, concat_axis=1, tiled=True)
    spectral = spectral_front(arrived, lat_fwd, first_pair, second_pair, bias_one, bias_two)
    keep_mask = kept_modes.astype(jnp.float32)[None, :, None, :, None, None]
    masked = (shrink(spectral[3]) * keep_mask).astype(jnp.bfloat16)
    masked = masked.reshape(snap_local, lat_total, 2, mode_local, channel)
    returned = jnp.einsum(
        "pkqr,nkpmd->nrqmd", lat_fwd, masked, preferred_element_type=jnp.float32
    ).astype(jnp.bfloat16)
    home_modes = lax.all_to_all(returned, "sp", split_axis=1, concat_axis=3, tiled=True)
    filtered = jnp.einsum(
        "nrqmd,qml->nrld", home_modes, lon_inv, preferred_element_type=jnp.float32
    )
    mixture = fields_float + normed + filtered
    normed_two, norm_two_pull = jax.vjp(layer_norm, mixture, small_f[2], small_f[3])
    normed_two_low = normed_two.astype(jnp.bfloat16)
    tokens = snap_local * row_local * lon_total
    passed = mlp_pass(
        normed_two_low.reshape(tokens, channel),
        cotangent.reshape(tokens, channel),
        mlp_w,
        small_f[9:].reshape(1, -1),
    )
    output = mixture + passed[0].reshape(mixture.shape) + small_f[8]
    weight_mask = valid_mask.astype(jnp.float32)[..., None]
    variables = output[..., :NVAR]
    local_sums = jnp.stack(
        [
            jnp.sum(weight_mask * variables, axis=(0, 1, 2)),
            jnp.sum(weight_mask * variables * variables, axis=(0, 1, 2)),
        ]
    )
    total_sums = lax.psum(local_sums, ("snap", "sp"))
    positions = snap_local * lax.axis_size("snap") * lat_total * lon_total
    stats_new = stat_decay * run_stats + (1.0 - stat_decay) * total_sums / positions
    cot_float = cotangent.astype(jnp.float32)
    grad_normed_two = passed[1].reshape(mixture.shape)
    grad_bias_hidden = passed[4]
    grad_mix_norm, grad_gain_two, grad_shift_two = norm_two_pull(grad_normed_two)
    grad_mixture = cot_float + grad_mix_norm
    grad_bias_out = jnp.sum(cot_float, axis=(0, 1, 2))
    grad_filtered = grad_mixture.astype(jnp.bfloat16)
    grad_home = jnp.einsum(
        "nrld,qml->nrqmd", grad_filtered, lon_inv, preferred_element_type=jnp.float32
    ).astype(jnp.bfloat16)
    grad_returned = lax.all_to_all(grad_home, "sp", split_axis=3, concat_axis=1, tiled=True)
    grad_masked = jnp.einsum(
        "pkqr,nrqmd->nkpmd", lat_fwd, grad_returned, preferred_element_type=jnp.float32
    )
    arrived_again = lax.all_to_all(spec_lon, "sp", split_axis=3, concat_axis=1, tiled=True)
    used_front = spectral_front(arrived_again, lat_fwd, first_pair, second_pair, bias_one, bias_two)
    blocked, pre_one, act_one, pre_two = used_front
    grad_two = jax.vjp(shrink, pre_two)[1](grad_masked.reshape(pre_two.shape) * keep_mask)[
        0
    ].astype(jnp.bfloat16)
    grad_bias_two = jnp.sum(grad_two.astype(jnp.float32), axis=(0, 1, 3))
    grad_second = jnp.einsum(
        "nkqmbi,nkpmbo->pqbio", act_one, grad_two, preferred_element_type=jnp.float32
    )
    grad_act = jnp.einsum(
        "nkpmbo,pqbio->nkqmbi", grad_two, second_pair, preferred_element_type=jnp.float32
    )
    grad_one = jax.vjp(jax.nn.gelu, pre_one)[1](grad_act)[0].astype(jnp.bfloat16)
    grad_bias_one = jnp.sum(grad_one.astype(jnp.float32), axis=(0, 1, 3))
    grad_first = jnp.einsum(
        "nkqmbi,nkpmbo->pqbio", blocked, grad_one, preferred_element_type=jnp.float32
    )
    grad_spectrum = jnp.einsum(
        "nkpmbo,pqbio->nkqmbi", grad_one, first_pair, preferred_element_type=jnp.float32
    ).astype(jnp.bfloat16)
    grad_spectrum = grad_spectrum.reshape(snap_local, lat_total, 2, mode_local, channel)
    grad_lon = jnp.einsum(
        "pkqr,nkpmd->nrqmd", lat_fwd, grad_spectrum, preferred_element_type=jnp.float32
    ).astype(jnp.bfloat16)
    grad_rows = lax.all_to_all(grad_lon, "sp", split_axis=1, concat_axis=3, tiled=True)
    grad_normed = grad_mixture + jnp.einsum(
        "nrqmd,lqm->nrld", grad_rows, lon_fwd, preferred_element_type=jnp.float32
    )
    grad_field_norm, grad_gain_one, grad_shift_one = norm_pull(grad_normed)
    input_grad = grad_mixture + grad_field_norm
    grad_filter = jnp.stack(
        [
            grad_first[0, 0] + grad_first[1, 1],
            grad_first[1, 0] - grad_first[0, 1],
            grad_second[0, 0] + grad_second[1, 1],
            grad_second[1, 0] - grad_second[0, 1],
        ]
    ).reshape(4, channel, block_width)
    grad_small = jnp.concatenate(
        [
            jnp.stack([grad_gain_one, grad_shift_one, grad_gain_two, grad_shift_two]),
            grad_bias_one.reshape(2, channel),
            grad_bias_two.reshape(2, channel),
            grad_bias_out[None, :],
            grad_bias_hidden.reshape(-1, channel),
        ],
        axis=0,
    )
    shares = (
        jnp.stack([
            lax.psum_scatter(part, "sp", scatter_dimension=0, tiled=True) for part in passed[2:4]
        ]),
        lax.psum_scatter(grad_filter, "sp", scatter_dimension=1, tiled=True),
        lax.psum_scatter(grad_small, "sp", scatter_dimension=1, tiled=True),
    )
    owned = (
        lax.psum(shares[0].astype(jnp.bfloat16), "snap").astype(jnp.float32),
        lax.psum(shares[1].astype(jnp.bfloat16), "snap").astype(jnp.float32),
        lax.psum(shares[2].astype(jnp.bfloat16), "snap").astype(jnp.float32),
    )
    mlp_new, mlp_first_new, mlp_second_new, mlp_copy = adamw(
        mlp_master, mlp_first, mlp_second, owned[0], rate_mlp
    )
    filter_new, filter_first_new, filter_second_new, filter_copy = adamw(
        filter_master, filter_first, filter_second, owned[1], rate_filter
    )
    small_new, small_first_new, small_second_new, small_copy = adamw(
        small_master, small_first, small_second, owned[2], rate_small
    )
    return (
        output.astype(jnp.bfloat16),
        input_grad,
        mlp_new,
        mlp_first_new,
        mlp_second_new,
        mlp_copy,
        filter_new,
        filter_first_new,
        filter_second_new,
        filter_copy,
        small_new,
        small_first_new,
        small_second_new,
        small_copy,
        stats_new,
    )


FIRST, SECOND, THIRD, FOURTH, HALF, QUARTER, LEVEL, LAST = range(8)
SCHEDULE = {
    "a": [(FIRST, 0)],
    "b": [(FIRST, 1)],
    "c0": [(SECOND, 0)],
    "d1": [(SECOND, 1), (FIRST, 2)],
    "f0": [(THIRD, 0)],
    "f1": [(SECOND, 2), (FIRST, 3)],
    "g": [(THIRD, 1)],
    "h0": [(FIRST, 4)],
    "h1": [(FOURTH, 0), (THIRD, 2)],
    ("k2", 0): [(SECOND, 3), (SECOND, 4)],
    ("m", 0): [(FOURTH, 1), (FIRST, 5)],
    ("m0", 0): [(FOURTH, 2)],
    ("m1", 0): [(HALF, 0)],
    ("k", 1): [(THIRD, 3), (THIRD, 4)],
    ("k0", 2): [(HALF, 1)],
    ("m", 2): [(FOURTH, 3)],
    ("m1", 2): [(QUARTER, 0)],
    ("m2", 2): [(HALF, 2), (FOURTH, 4)],
    ("k", 3): [(FOURTH, 5)],
    ("m", 3): [(LEVEL, 0), (QUARTER, 1)],
    ("k", 4): [(HALF, 3)],
    ("k2", 4): [(LEVEL, 1)],
    ("l", 4): [(QUARTER, 2)],
    ("k", 5): [(LAST, 0), (LEVEL, 2), (QUARTER, 3)],
    ("k2", 5): [(HALF, 4)],
    ("m", 5): [(LAST, 1), (LEVEL, 3)],
    "o1": [(QUARTER, 4)],
    "p1": [(HALF, 5)],
    "r": [(LAST, 2), (LEVEL, 4)],
    "t1": [(QUARTER, 5)],
    "u1": [(LAST, 3), (LAST, 4)],
    "x0": [(LEVEL, 5)],
    "z": [(LAST, 5)],
}


def lon_matrix(lon_total, mode_total, snaps, rows):
    places = np.arange(lon_total)
    orders = np.arange(mode_total)
    angles = (places[:, None] * orders[None, :] % lon_total) * (2.0 * math.pi / lon_total)
    doubling = np.where(orders == 0, 1.0, 2.0)
    scaling = 1.0 / math.sqrt(lon_total)
    forward = np.stack([np.cos(angles), -np.sin(angles)], axis=1) * scaling
    inverse = forward * doubling

    def spread(table):
        table = np.einsum(
            "ab,lx,rs->alrbsx", np.eye(snaps), table.reshape(lon_total, -1), np.eye(rows)
        )
        return table.reshape(snaps * lon_total * rows, -1).astype(ml_dtypes.bfloat16)

    return spread(forward), spread(inverse)


def lon_turn(lon_total, rows):
    turn = np.einsum("lk,rs->rlks", np.eye(lon_total), np.eye(rows))
    return turn.reshape(rows, lon_total, lon_total * rows).astype(ml_dtypes.bfloat16)


def lat_matrix(lat_total, mode_total):
    places = np.arange(lat_total)
    angles = (places[:, None] * places[None, :] % lat_total) * (2.0 * math.pi / lat_total)
    cosine, sine = np.cos(angles), np.sin(angles)
    table = np.stack([np.stack([cosine, sine], axis=1), np.stack([-sine, cosine], axis=1)])
    table = np.einsum("pkqr,ab->pakrqb", table / math.sqrt(lat_total), np.eye(mode_total))
    size = 2 * lat_total * mode_total
    return table.reshape(size, size).astype(ml_dtypes.bfloat16)


class Refs:
    pass


def block_body(names, sizes, *refs):
    g = Refs()
    for name, ref in zip(names, refs, strict=True):
        setattr(g, name, ref)
    snaps, group, parts, width = sizes
    levels = group // 2
    tokens = g.fields.shape[0] * g.fields.shape[1]
    channel = g.fields.shape[2]
    owned = channel // group
    half = width // 2
    quarter = width // snaps
    tile = tokens // 2
    short = divisor(tokens // 2, 16, 720)
    packed = g.modes.shape[2]
    strip = divisor(tokens // 2, 48, 144)
    sub = divisor(strip, 16, 48)
    low = jnp.bfloat16
    f32 = jnp.float32

    me_snap = lax.axis_index("snap")
    me_sp = lax.axis_index("sp")
    core = lax.rem(me_sp, 2)
    level = me_sp // 2

    def at(snap, sp):
        return {"snap": snap, "sp": sp}

    def sp_after(step):
        return lax.rem(me_sp + step, group)

    def sp_before(step):
        return lax.rem(me_sp + group - step, group)

    def snap_after(step):
        return lax.rem(me_snap + step, snaps)

    def snap_before(step):
        return lax.rem(me_snap + snaps - step, snaps)

    def level_after(step):
        return lax.rem(level + step, levels)

    def level_before(step):
        return lax.rem(level + levels - step, levels)

    other_core = at(me_snap, me_sp + 1 - 2 * core)

    def send(src, dst, sems, index, target):
        return pltpu.make_async_remote_copy(
            src_ref=src,
            dst_ref=dst,
            send_sem=sems[0].at[index],
            recv_sem=sems[1].at[index],
            device_id=target,
            device_id_type=pl.DeviceIdType.MESH,
        )

    half_tokens = tokens // 2

    def strips(body, first=0, count=tokens, before=None, after=None):
        @pl.loop(0, count // strip)
        def _(step):
            if before is not None:
                before(first // strip + step)
            for at_row in range(0, strip, sub):
                body(pl.ds(pl.multiple_of(first + step * strip + at_row, 16), sub))
            if after is not None:
                after(first // strip + step)

    def half_strips(body, part, **around):
        strips(body, part * half_tokens, half_tokens, **around)

    def strip_copy(near, far, sems, place, out):
        rows = pl.ds(pl.multiple_of(place * strip, strip), strip)
        ends = [near.at[rows], far.reshape(tokens, channel).at[rows]]
        if not out:
            ends.reverse()
        return pltpu.make_async_copy(*ends, sems.at[place])

    def fields_load(place):
        return strip_copy(g.fields_in, g.fields, g.fields_sem, place, False)

    def cot_load(place):
        return strip_copy(g.cot_in, g.cot, g.cot_sem, place, False)

    def out_copy(place):
        return strip_copy(g.fields_in, g.out, g.fields_sem, place, True)

    def grad_copy(place):
        return strip_copy(g.grid, g.in_grad, g.cot_sem, place, True)

    def half_rows(part):
        return slice(part * half_tokens, (part + 1) * half_tokens)

    def fold(value):
        return jnp.sum(value.reshape(-1, 8, value.shape[1]), axis=0)

    loads = {}

    def load(name, index):
        copy = pltpu.make_async_copy(getattr(g, name), getattr(g, name + "_in"), g.load_sem.at[index])
        copy.start()
        loads[name] = copy

    for index, name in enumerate(
        [name for name in names[: names.index("out")] if name not in ("mlp", "fields", "cot")]
    ):
        load(name, index)
    for copy in (fields_load, cot_load):
        for place in range(tokens // strip):
            copy(place).start()

    def master_load(part):
        return pltpu.make_async_copy(
            g.mlp.at[:, :, part * width : (part + 1) * width],
            g.mlp_part.at[part % 2],
            g.load_sem.at[len(loads) + part % 2],
        )

    master_load(0).start()
    master_load(1).start()

    barrier = pltpu.get_barrier_semaphore()
    peers = [at(me_snap, sp_after(step)) for step in range(1, group)]
    peers += [at(snap_after(step), me_sp) for step in range(1, snaps)]
    for peer in peers:
        pl.semaphore_signal(
            barrier, inc=1, device_id=peer, device_id_type=pl.DeviceIdType.MESH
        )

    loads["small"].wait()
    loads["kept"].wait()
    g.own_small[...] = jnp.zeros_like(g.own_small)
    rows_small = g.small.shape[0]
    g.own_small[0:rows_small, 0:owned] = g.small_in[...].astype(low).astype(f32)
    pairs_kept = g.kept.shape[1]
    lines = lax.broadcasted_iota(jnp.int32, (pairs_kept, pairs_kept), 0)
    places = lax.broadcasted_iota(jnp.int32, (pairs_kept, pairs_kept), 1)
    kept = jnp.where(lines == places, g.kept_in[...].astype(f32), 0.0)
    g.own_small[16:, :] = jnp.broadcast_to(
        jnp.sum(kept, axis=1, keepdims=True), (pairs_kept, g.own_small.shape[1])
    )
    pl.semaphore_wait(barrier, len(peers))

    def small_copy(step):
        return send(
            g.own_small, g.all_small.at[me_sp], (g.small_s, g.small_r), step, at(me_snap, sp_after(step))
        )

    for step in range(1, group):
        small_copy(step).start()
    g.all_small[me_sp] = g.own_small[...]

    snap_low = lax.rem(me_snap, 2)
    snap_high = me_snap // 2
    beside_low = me_snap + 1 - 2 * snap_low
    beside_high = me_snap + 2 - 4 * snap_high

    def own_quarter(part):
        odd = lax.rem(part, 2)
        return (1 - odd) * me_snap + odd * (2 * snap_low + snap_high)

    def own_place(part):
        return pl.ds(0, snaps) if part == parts - 1 else own_quarter(part)

    def half_quarters(part):
        return pl.ds(2 * (own_quarter(part) // 2), 2)

    def own_rows(sp):
        return pl.ds(pl.multiple_of(sp * owned, owned), owned)

    def spot(part):
        if isinstance(part, int):
            return part // 2 + parts // 2 * (part % 2)
        return lax.div(part, 2) + parts // 2 * lax.rem(part, 2)

    swaps = (
        (pl.ds(0, 1), own_place(0)),
        (pl.ds(3, 2), own_place(1)),
        (pl.ds(1, 2), own_place(0)),
        (pl.ds(5, 1), own_place(5)),
    )
    swapped = {0: 0, 1: 1, 2: 2, 5: 3}

    def swap_copy(batch):
        some, place = swaps[batch]
        return send(
            g.own_w.at[some, 1 - core, place],
            g.all_w.at[some, 1 - core, place, own_rows(me_sp)],
            (g.swap_s, g.swap_r),
            batch,
            other_core,
        )

    def swap_local(batch):
        some, place = swaps[batch]
        return pltpu.make_async_copy(
            g.own_w.at[some, core, place],
            g.all_w.at[some, core, place, own_rows(me_sp)],
            g.swap_l.at[batch],
        )

    def start_swap(batch):
        swap_copy(batch).start()
        swap_local(batch).start()

    def first_copy(part, step):
        rows = pl.ds(pl.multiple_of(level * 2 * owned, 2 * owned), 2 * owned)
        view = g.all_w.at[spot(part), core, own_place(part), rows]
        target = at(me_snap, 2 * level_after(step) + core)
        return send(view, view, (g.first_s, g.first_r), (part, step), target)

    def second_copy(part):
        odd = lax.rem(part, 2)
        view = g.all_w.at[spot(part), core, own_quarter(part)]
        target = at((1 - odd) * beside_low + odd * beside_high, me_sp)
        return send(view, view, (g.second_s, g.second_r), part, target)

    def third_copy(part):
        odd = lax.rem(part, 2)
        view = g.all_w.at[spot(part), core, half_quarters(part)]
        target = at((1 - odd) * beside_high + odd * beside_low, me_sp)
        return send(view, view, (g.third_s, g.third_r), part, target)

    def fourth_copy(part):
        view = g.all_w.at[spot(part), core]
        return send(view, view, (g.fourth_s, g.fourth_r), part, other_core)

    def start_first(part):
        if part in swapped:
            swap_copy(swapped[part]).wait_recv()
            swap_local(swapped[part]).wait()
        for step in range(1, levels):
            first_copy(part, step).start()

    def wait_first(part):
        for step in range(1, levels):
            first_copy(part, step).wait_recv()

    def pass_second(part):
        wait_first(part)
        second_copy(part).start()

    def pass_third(part):
        second_copy(part).wait_recv()
        third_copy(part).start()

    def pass_fourth(part):
        if part == parts - 1:
            wait_first(part)
        else:
            third_copy(part).wait_recv()
        fourth_copy(part).start()

    stages = {FIRST: start_first, SECOND: pass_second, THIRD: pass_third, FOURTH: pass_fourth}

    def reach(point):
        for stage, part in SCHEDULE.get(point, ()):
            stages[stage](part)

    for part in range(parts):
        master_load(part).wait()
        for place in range(snaps):
            cols = slice(place * quarter, (place + 1) * quarter)
            g.own_w[spot(part), :, place] = g.mlp_part[part % 2, :, :, cols].astype(low)
        if part + 2 < parts:
            master_load(part + 2).start()
        if part == 0:
            start_swap(0)
        elif part == parts - 1:
            for batch in range(1, len(swaps)):
                start_swap(batch)
    reach("a")

    def first_unit(rows):
        values = g.fields_in[rows, :].astype(f32)
        centred = values - jnp.mean(values, axis=-1, keepdims=True)
        scale = lax.rsqrt(jnp.mean(centred * centred, axis=-1, keepdims=True) + eps_norm)
        g.scale_one[rows, :] = scale
        g.grid[rows, :] = centred * scale

    strips(first_unit, before=lambda place: fields_load(place).wait())
    reach("b")
    for step in range(1, group):
        small_copy(step).wait_recv()
    for sp in range(group):
        g.gains[:, sp * owned : (sp + 1) * owned] = g.all_small[sp, 0:16, 0:owned]
        g.keep[sp * pairs_kept : (sp + 1) * pairs_kept, :] = g.all_small[sp, 16:, :]

    def first_norm(rows):
        unit = g.grid[rows, :]
        normed = unit * g.gains[0:1, :] + g.gains[1:2, :]
        g.unit_one[rows, :] = unit.astype(low)
        g.normed[rows, :] = normed.astype(low)
        g.grid[rows, :] = g.fields_in[rows, :].astype(f32) + normed

    half_snaps = g.arrived.shape[0] // 2

    third_rows = packed // 3
    spare = 128 - owned

    def pack(value):
        return jnp.concatenate(
            [
                jnp.concatenate(
                    [
                        value[at_row * third_rows : (at_row + 1) * third_rows],
                        value[packed:, at_row * spare : (at_row + 1) * spare],
                    ],
                    axis=1,
                )
                for at_row in range(3)
            ],
            axis=0,
        ).astype(low)

    def unpack(value):
        value = value.astype(f32)
        rest = [
            value[at_row * third_rows : (at_row + 1) * third_rows, owned:] for at_row in range(3)
        ]
        return jnp.concatenate([value[:, 0:owned], jnp.concatenate(rest, axis=1)], axis=0)

    def block_copy(which, part, step):
        target = sp_after(step)
        return send(
            g.modes.at[part, target],
            g.modes_got.at[part, me_sp],
            (g.block_s, g.block_r),
            (which, part, step),
            at(me_snap, target),
        )

    def row_copy(which, part, step):
        target = sp_after(step)
        return send(
            g.rows_out.at[part, target],
            g.rows_got.at[part, me_sp],
            (g.row_s, g.row_r),
            (which, part, step),
            at(me_snap, target),
        )

    def to_blocks(table, which, part):
        modes = dot_nn(table, g.normed[half_rows(part), :])
        for block in range(group):
            g.modes[part, block] = pack(modes[:, block * owned : (block + 1) * owned])
        for step in range(1, group):
            block_copy(which, part, step).start()
        g.modes_got[part, me_sp] = g.modes[part, me_sp]

    def take_blocks(which, part):
        for step in range(1, group):
            block_copy(which, part, step).wait_recv()
        each = g.arrived.shape[1] // group
        for sp in range(group):
            value = unpack(g.modes_got[part, sp])
            value = jnp.concatenate([value, jnp.zeros((value.shape[0], spare), f32)], axis=1)
            for index in range(half_snaps):
                g.arrived[part * half_snaps + index, sp * each : (sp + 1) * each, :] = value[
                    index * each : (index + 1) * each
                ].astype(low)

    def to_rows(which, part, tables):
        each = tables[0].shape[0] // group
        for sp in range(group):
            value = [table[sp * each : (sp + 1) * each, 0:owned] for table in tables]
            g.rows_out[part, sp] = pack(jnp.concatenate(value, axis=0))
        for step in range(1, group):
            row_copy(which, part, step).start()
        g.rows_got[part, me_sp] = g.rows_out[part, me_sp]

    def home_modes(which, part):
        for step in range(1, group):
            row_copy(which, part, step).wait_recv()
        for block in range(group):
            g.gathered[part, :, block * owned : (block + 1) * owned] = unpack(
                g.rows_got[part, block]
            )
        g.home_low[part] = g.gathered[part].astype(low)

    loads["lon_f"].wait()
    for part in range(2):
        half_strips(first_norm, part)
        reach("c" + str(part))
        to_blocks(g.lon_f_in[...], 0, part)
        reach("d" + str(part))

    loads["filt"].wait()
    for weight, first in ((g.weight_one, 0), (g.weight_two, 2)):
        weight[...] = jnp.zeros_like(weight)
        real = g.filt_in[first].astype(low)
        imag = g.filt_in[first + 1].astype(low)
        weight[0:owned, 0:owned] = real
        weight[128 : 128 + owned, 128 : 128 + owned] = real
        weight[0:owned, 128 : 128 + owned] = imag
        weight[128 : 128 + owned, 0:owned] = -imag

    def bias_row(first):
        return jnp.concatenate(
            [g.own_small[first : first + 1, :], g.own_small[first + 1 : first + 2, :]], axis=1
        )

    for place in range(tokens // strip):
        cot_load(place).wait()
    reach("e")
    loads["lat_f"].wait()
    loads["lat_b"].wait()
    pairs = g.arrived.shape[1] // 2
    half_modes = half_snaps * pairs

    def mode_half(part):
        return slice(part * half_modes, (part + 1) * half_modes)

    def spectra(out, kind, part):
        for snap in range(part * half_snaps, (part + 1) * half_snaps):
            spectrum = dot_nn(g.lat_f_in[...], g.arrived[snap]).astype(kind)
            rows = slice(snap * pairs, (snap + 1) * pairs)
            out[rows, 0:128] = spectrum[0:pairs]
            out[rows, 128:256] = spectrum[pairs:]

    def grids(values):
        tables = []
        for index in range(half_snaps):
            rows = values[index * pairs : (index + 1) * pairs]
            rows = jnp.concatenate([rows[:, 0:128], rows[:, 128:256]], axis=0)
            tables.append(dot_nn(g.lat_b_in[...], rows))
        return tables

    def keep_half():
        keep = jnp.concatenate([g.keep[...], g.keep[...]], axis=1)
        return jnp.concatenate([keep] * half_snaps, axis=0)

    for part in range(2):
        take_blocks(0, part)
        rows = mode_half(part)
        spectra(g.spectrum, low, part)
        g.pre_one[rows, :] = dot_nn(g.spectrum[rows, :], g.weight_one[...]) + bias_row(4)
        g.act_one[rows, :] = gelu_both(g.pre_one[rows, :])[0].astype(low)
        g.pre_two[rows, :] = dot_nn(g.act_one[rows, :], g.weight_two[...]) + bias_row(6)
        to_rows(0, part, grids((shrink(g.pre_two[rows, :]) * keep_half()).astype(low)))
        reach("f" + str(part))
    g.cot_turned[...] = g.cot_in[...].T
    reach("g")

    loads["lon_i"].wait()

    def second_norm(rows):
        values = g.grid[rows, :]
        centred = values - jnp.mean(values, axis=-1, keepdims=True)
        scale = lax.rsqrt(jnp.mean(centred * centred, axis=-1, keepdims=True) + eps_norm)
        centred = centred * scale
        g.unit_two[rows, :] = centred.astype(low)
        g.scale_two[rows, :] = scale
        g.normed[rows, :] = (centred * g.gains[2:3, :] + g.gains[3:4, :]).astype(low)
        g.grid[rows, :] = values + g.gains[8:9, :]
        g.back[rows, :] = jnp.zeros((sub, channel), f32)

    for part in range(2):
        home_modes(0, part)
        g.grid[half_rows(part), :] += dot_nn(g.lon_i_in[...], g.home_low[part])
        reach("h" + str(part))
        half_strips(second_norm, part)
        reach("i" + str(part))
    g.normed_turned[...] = g.normed[...].T
    reach("j")
    flat = jnp.concatenate([g.gains[9 + row : 10 + row, :] for row in range(rows_small - 9)], axis=1)
    for part in range(parts):
        g.bias[part] = flat[:, part * width : (part + 1) * width]

    def core_copy(part, matrix):
        slot = lax.rem(part, 2)
        return send(
            g.grads.at[matrix, :, 1 - core],
            g.core_got.at[slot, matrix],
            (g.core_s, g.core_r),
            (slot, matrix),
            other_core,
        )

    places_one = (snap_low, snap_high)
    places_two = (snap_high, snap_low)
    beside_one = (beside_low, beside_high)
    beside_two = (beside_high, beside_low)

    def half_copy(part, matrix):
        slot = lax.rem(part, 2)
        place = lax.rem(part, 4)
        return send(
            g.half_out.at[slot, matrix, 1 - places_one[matrix]],
            g.half_got.at[place, matrix],
            (g.half_s, g.half_r),
            (place, matrix),
            at(beside_one[matrix], me_sp),
        )

    def quarter_copy(part, matrix):
        slot = lax.rem(part, 2)
        return send(
            g.quarter_out.at[slot, matrix, 1 - places_two[matrix]],
            g.quarter_got.at[slot, matrix],
            (g.quarter_s, g.quarter_r),
            (slot, matrix),
            at(beside_two[matrix], me_sp),
        )

    def level_copy(part, step):
        slot = lax.rem(part, 2)
        place = lax.rem(part, 4)
        target = level_after(step)
        return send(
            g.level_out.at[slot, target],
            g.level_got.at[place, level],
            (g.level_s, g.level_r),
            (place, step),
            at(me_snap, 2 * target + core),
        )

    def last_copy(part, step):
        view = g.total.at[part, me_snap]
        return send(view, view, (g.last_s, g.last_r), (part, step), at(snap_after(step), me_sp))

    def half_stage(part):
        slot = lax.rem(part, 2)
        for matrix in range(2):

            if part >= 2:
                half_copy(part - 2, matrix).wait_send()

            core_copy(part, matrix).wait_recv()

            @pl.loop(0, levels)
            def _(row, matrix=matrix):
                both = g.grads[matrix, row, core].astype(f32) + g.core_got[
                    slot, matrix, row
                ].astype(f32)
                both = both.astype(low)
                g.half_out[slot, matrix, 0, row] = both[:, 0:half]
                g.half_out[slot, matrix, 1, row] = both[:, half:width]

            half_copy(part, matrix).start()

    def quarter_stage(part):
        slot = lax.rem(part, 2)
        for matrix in range(2):

            if part >= 2:
                quarter_copy(part - 2, matrix).wait_send()

            half_copy(part, matrix).wait_recv()
            for row in range(levels):
                both = g.half_out[slot, matrix, places_one[matrix], row].astype(f32) + g.half_got[
                    lax.rem(part, 4), matrix, row
                ].astype(f32)
                both = both.astype(low)
                g.quarter_out[slot, matrix, 0, row] = both[:, 0:quarter]
                g.quarter_out[slot, matrix, 1, row] = both[:, quarter:half]
            quarter_copy(part, matrix).start()

    def level_stage(part):
        slot = lax.rem(part, 2)

        if part >= 2:
            for step in range(1, levels):
                level_copy(part - 2, step).wait_send()

        for matrix in range(2):
            quarter_copy(part, matrix).wait_recv()
            for row in range(levels):
                both = g.quarter_out[slot, matrix, places_two[matrix], row].astype(
                    f32
                ) + g.quarter_got[slot, matrix, row].astype(f32)
                g.level_out[slot, row, matrix] = both.astype(low)
        for step in range(1, levels):
            level_copy(part, step).start()

    def last_stage(part):
        slot = lax.rem(part, 2)
        for step in range(1, levels):
            level_copy(part, step).wait_recv()
        for matrix in range(2):
            sums = g.level_out[slot, level, matrix].astype(f32)
            for step in range(1, levels):
                sums += g.level_got[lax.rem(part, 4), level_before(step), matrix].astype(f32)
            g.total[part, me_snap, matrix] = sums.astype(low)
        for step in range(1, snaps):
            last_copy(part, step).start()

    stages |= {HALF: half_stage, QUARTER: quarter_stage, LEVEL: level_stage, LAST: last_stage}

    def weight(part, matrix):
        return jnp.concatenate([g.all_w[spot(part), matrix, place] for place in range(snaps)], axis=1)

    def add_products(part, rows):
        g.grid[rows, :] += dot_nt(g.act[rows, :], weight(part, 1))
        g.back[rows, :] += dot_nt(g.slope[rows, :], weight(part, 0))

    @pl.loop(0, parts)
    def _(part):
        def reach_in(point, also=True):
            for at_part in range(parts):
                if (point, at_part) in SCHEDULE:
                    pl.when((part == at_part) & also)(functools.partial(reach, (point, at_part)))

        def tile_rows(step):
            return pl.ds(pl.multiple_of(step * tile, tile), tile)

        fourth_copy(part).wait_recv()
        reach_in("k")
        g.grad_bias[part] = jnp.zeros(g.grad_bias.shape[1:], f32)

        act, slope = gelu_both(dot_nn(g.normed[...], weight(part, 0)) + g.bias[part])
        g.act[...] = act.astype(low)
        slope = (dot_nn(g.cot_in[...], weight(part, 1)) * slope).astype(low)
        g.slope[...] = slope
        g.grad_bias[part] += fold(slope.astype(f32))
        for at_step in range(3):
            reach_in("k" + str(at_step))

        reach_in("l")

        @pl.when(part >= 1)
        def _():
            for matrix in range(2):
                core_copy(part - 1, matrix).wait_send()

        shape = g.grads.shape[1:]
        g.grads[0] = dot_nn(g.normed_turned[...], g.slope[...]).astype(low).reshape(shape)
        core_copy(part, 0).start()
        g.grads[1] = dot_nn(g.cot_turned[...], g.act[...]).astype(low).reshape(shape)
        core_copy(part, 1).start()
        reach_in("m")

        @pl.when(part < parts - 1)
        def _():
            @pl.loop(0, tokens // tile)
            def _(step):
                add_products(part, tile_rows(step))
                for at_step in range(3):
                    reach_in("m" + str(at_step), step == (at_step + 1) // 2)

    g.folds[...] = jnp.zeros_like(g.folds)

    def second_back(rows):
        grad = g.back[rows, :]
        unit = g.unit_two[rows, :].astype(f32)
        cot = g.cot_in[rows, :].astype(f32)
        pulled = grad * g.gains[2:3, :]
        middle = jnp.mean(pulled, axis=-1, keepdims=True)
        slant = jnp.mean(pulled * unit, axis=-1, keepdims=True)
        total = cot + g.scale_two[rows, :] * (pulled - middle - unit * slant)
        g.back[rows, :] = total
        g.normed[rows, :] = total.astype(low)
        g.folds[2] += fold(grad * unit)
        g.folds[3] += fold(grad)
        g.folds[4] += fold(cot)

    loads["lon_it"].wait()
    for part in range(2):

        @pl.loop(0, half_tokens // short)
        def _(step, part=part):
            first_row = part * half_tokens + step * short
            add_products(parts - 1, pl.ds(pl.multiple_of(first_row, 16), short))

        reach("o" + str(part))
        half_strips(second_back, part)
        for step in range(1, group):
            block_copy(0, part, step).wait_send()
        to_blocks(g.lon_it_in[...], 1, part)
        reach("p" + str(part))
    reach("q")

    def low_out(rows):
        g.fields_in[rows, :] = g.grid[rows, :].astype(low)

    strips(low_out, after=lambda place: out_copy(place).start())
    reach("r")
    loads["valid"].wait()
    loads["turn"].wait()
    weigh = sum(
        dot_nn(g.valid_in[:, row, :].astype(f32).astype(low), g.turn_in[row])
        for row in range(g.valid.shape[1])
    )
    places_each = weigh.shape[1]
    precise = lax.Precision.HIGHEST
    sums = [jnp.zeros((1, 128), f32), jnp.zeros((1, 128), f32)]
    for snap in range(g.valid.shape[0]):
        variables = g.grid[snap * places_each : (snap + 1) * places_each, 0:128]
        for index, value in enumerate((variables, variables * variables)):
            sums[index] += jnp.dot(
                weigh[snap : snap + 1, :], value, precision=precise, preferred_element_type=f32
            )

    reach("s")

    def dot_tn(left, right):
        return lax.dot_general(
            left, right, (((0,), (0,)), ((), ())), preferred_element_type=f32
        )

    def filter_rows(first, grad):
        g.pair_grad[...] = grad
        real = g.pair_grad[0:128, 0:128] + g.pair_grad[128:256, 128:256]
        imag = g.pair_grad[0:128, 128:256] - g.pair_grad[128:256, 0:128]
        g.filt_out[me_snap, first] = real[0:owned].astype(low)
        g.filt_out[me_snap, first + 1] = imag[0:owned].astype(low)

    for part in range(2):
        take_blocks(1, part)
        reach("t" + str(part))
        rows = mode_half(part)
        spectra(g.grad_pre, f32, part)
        bend = jnp.tanh(g.pre_two[rows, :] / shrink_level)
        grad = (g.grad_pre[rows, :] * keep_half() * (bend * bend)).astype(low)
        g.grad_two[rows, :] = grad
        grad = dot_nt(grad, g.weight_two[...]) * gelu_both(g.pre_one[rows, :])[1]
        grad = grad.astype(low)
        g.grad_one[rows, :] = grad
        for step in range(1, group):
            row_copy(0, part, step).wait_send()
        to_rows(1, part, grids(dot_nt(grad, g.weight_one[...]).astype(low)))
        reach("u" + str(part))
    reach("v")
    bias_one = jnp.sum(g.grad_one[...].astype(f32), axis=0, keepdims=True)
    bias_two = jnp.sum(g.grad_two[...].astype(f32), axis=0, keepdims=True)
    filter_rows(2, dot_tn(g.act_one[...], g.grad_two[...]))
    filter_rows(0, dot_tn(g.spectrum[...], g.grad_one[...]))

    def filter_copy(step):
        view = g.filt_out.at[me_snap]
        return send(view, view, (g.filt_s, g.filt_r), step, at(snap_after(step), me_sp))

    for step in range(1, snaps):
        filter_copy(step).start()


    reach("w")

    loads["lon_ft"].wait()

    def first_back(rows):
        grad = g.grid[rows, :]
        unit = g.unit_one[rows, :].astype(f32)
        pulled = grad * g.gains[0:1, :]
        middle = jnp.mean(pulled, axis=-1, keepdims=True)
        slant = jnp.mean(pulled * unit, axis=-1, keepdims=True)
        g.grid[rows, :] = g.back[rows, :] + g.scale_one[rows, :] * (
            pulled - middle - unit * slant
        )
        g.folds[0] += fold(grad * unit)
        g.folds[1] += fold(grad)

    for part in range(2):
        home_modes(1, part)
        reach("x" + str(part))
        g.grid[half_rows(part), :] = g.back[half_rows(part), :] + dot_nn(
            g.lon_ft_in[...], g.home_low[part]
        )
        half_strips(first_back, part, after=lambda place: grad_copy(place).start())
        reach("y" + str(part))

    g.grad_rows[...] = jnp.zeros_like(g.grad_rows)
    for index, row in enumerate((0, 1, 2, 3, 8)):
        g.grad_rows[row : row + 1, :] = jnp.sum(g.folds[index], axis=0, keepdims=True)
    flat = jnp.concatenate(
        [jnp.sum(g.grad_bias[part], axis=0, keepdims=True) for part in range(parts)], axis=1
    )
    for row in range(rows_small - 9):
        g.grad_rows[9 + row : 10 + row, :] = flat[:, row * channel : (row + 1) * channel]
    for block in range(group):
        g.tiles[block] = jnp.zeros(g.tiles.shape[1:], f32)
        g.tiles[block, :, 0:owned] = g.grad_rows[:, block * owned : (block + 1) * owned]
        g.tiles[block, 13:14, :] = sums[0]
        g.tiles[block, 14:15, :] = sums[1]

    def tile_copy(step):
        target = sp_after(step)
        return send(
            g.tiles.at[target], g.tiles_got.at[me_sp], (g.tile_s, g.tile_r), step, at(me_snap, target)
        )

    def snap_tile_copy(step):
        view = g.snap_tiles.at[me_snap]
        return send(view, view, (g.snap_tile_s, g.snap_tile_r), step, at(snap_after(step), me_sp))

    for step in range(1, group):
        tile_copy(step).start()
    reach("z")

    for batch in range(len(swaps)):
        swap_copy(batch).wait_send()
    for part in range(parts):
        if part < parts - 1:
            second_copy(part).wait_send()
            third_copy(part).wait_send()
        fourth_copy(part).wait_send()
        for step in range(1, levels):
            first_copy(part, step).wait_send()
    for step in range(1, group):
        small_copy(step).wait_send()
        for part in range(2):
            block_copy(1, part, step).wait_send()
            row_copy(1, part, step).wait_send()
    for matrix in range(2):
        core_copy(parts - 1, matrix).wait_send()
        for part in (parts - 2, parts - 1):
            half_copy(part, matrix).wait_send()
            quarter_copy(part, matrix).wait_send()
    for step in range(1, levels):
        level_copy(parts - 2, step).wait_send()
    for step in range(1, snaps):
        filter_copy(step).wait_send()

    g.tiles_got[me_sp] = g.tiles[me_sp]
    for step in range(1, group):
        tile_copy(step).wait_recv()
    tile_sum = g.tiles_got[0]
    for sp in range(1, group):
        tile_sum += g.tiles_got[sp]
    g.snap_tiles[me_snap] = tile_sum
    g.snap_tiles[me_snap, 4:5, :] = bias_one[:, 0:128]
    g.snap_tiles[me_snap, 5:6, :] = bias_one[:, 128:256]
    g.snap_tiles[me_snap, 6:7, :] = bias_two[:, 0:128]
    g.snap_tiles[me_snap, 7:8, :] = bias_two[:, 128:256]
    for step in range(1, snaps):
        snap_tile_copy(step).start()

    for step in range(1, snaps):
        filter_copy(step).wait_recv()
    filter_sum = g.filt_out[0].astype(f32)
    for snap in range(1, snaps):
        filter_sum += g.filt_out[snap].astype(f32)
    g.grad_filt[...] = filter_sum
    for part in range(parts):
        for step in range(1, snaps):
            last_copy(part, step).wait_recv()
    grads_out = pltpu.make_async_copy(g.total, g.grad_mlp, g.load_sem.at[3])
    grads_out.start()
    for step in range(1, snaps):
        snap_tile_copy(step).wait_recv()
    tile_sum = g.snap_tiles[0]
    for snap in range(1, snaps):
        tile_sum += g.snap_tiles[snap]
    g.grad_small[...] = tile_sum

    grads_out.wait()
    for place in range(tokens // strip):
        out_copy(place).wait()
        grad_copy(place).wait()
    for step in range(1, levels):
        level_copy(parts - 1, step).wait_send()
    for step in range(1, group):
        tile_copy(step).wait_send()
    for step in range(1, snaps):
        snap_tile_copy(step).wait_send()
        for part in range(parts):
            last_copy(part, step).wait_send()


def block_pass(fields, cot, valid, kept, mlp, filt, small, snaps, group):
    snap_local, row_local, lon_total, channel = fields.shape
    tokens = snap_local * row_local * lon_total
    hidden = mlp.shape[2]
    lat_total = row_local * group
    modes = kept.shape[1] * group
    owned = channel // group
    width = 512
    parts = hidden // width
    levels = group // 2
    quarter = width // snaps
    low, f32 = jnp.bfloat16, jnp.float32
    half = width // 2
    half_snaps = snap_local // 2
    lon_f, lon_i = lon_matrix(lon_total, modes, half_snaps, row_local)

    def paired(array):
        return jnp.transpose(array, (0, 2, 1, 3)).reshape(-1, row_local, channel)

    lat_f = lat_matrix(lat_total, modes)
    pair = 2 * modes * row_local
    spread = half_snaps * row_local * 2 * modes
    inputs = dict(
        small=small,
        kept=kept.T,
        fields=paired(fields),
        lon_f=jnp.asarray(np.ascontiguousarray(lon_f.T)),
        filt=filt,
        lat_f=jnp.asarray(lat_f),
        lat_b=jnp.asarray(np.ascontiguousarray(lat_f.T)),
        cot=paired(cot),
        lon_i=jnp.asarray(lon_i),
        valid=valid,
        turn=jnp.asarray(lon_turn(lon_total, row_local)),
        lon_it=jnp.asarray(np.ascontiguousarray(lon_i.T)),
        lon_ft=jnp.asarray(lon_f),
        mlp=mlp,
    )
    outputs = dict(
        out=jax.ShapeDtypeStruct((tokens // row_local, row_local, channel), low),
        in_grad=jax.ShapeDtypeStruct((tokens // row_local, row_local, channel), f32),
        grad_mlp=jax.ShapeDtypeStruct((parts, snaps, 2, owned, quarter), low),
        grad_filt=jax.ShapeDtypeStruct((4, owned, 128), f32),
        grad_small=jax.ShapeDtypeStruct((16, 128), f32),
    )
    vmem = pltpu.VMEM
    dma = pltpu.SemaphoreType.DMA
    scratch = {
        name + "_in": vmem(value.shape, value.dtype)
        for name, value in inputs.items()
        if name not in ("mlp", "fields", "cot")
    }
    strip = divisor(tokens // 2, 48, 144)
    scratch |= dict(
        mlp_part=vmem((2, 2, owned, width), f32),
        fields_in=vmem((tokens, channel), low),
        fields_sem=dma((tokens // strip,)),
        cot_sem=dma((tokens // strip,)),
        cot_in=vmem((tokens, channel), low),
        grid=vmem((tokens, channel), f32),
        back=vmem((tokens, channel), f32),
        normed=vmem((tokens, channel), low),
        normed_turned=vmem((channel, tokens), low),
        cot_turned=vmem((channel, tokens), low),
        unit_one=vmem((tokens, channel), low),
        unit_two=vmem((tokens, channel), low),
        scale_one=vmem((tokens, 1), f32),
        scale_two=vmem((tokens, 1), f32),
        own_small=vmem((16 + kept.shape[0], 128), f32),
        all_small=vmem((group, 16 + kept.shape[0], 128), f32),
        gains=vmem((16, channel), f32),
        keep=vmem((lat_total * modes, 128), f32),
        own_w=vmem((parts, 2, snaps, owned, quarter), low),
        all_w=vmem((parts, 2, snaps, channel, quarter), low),
        modes=vmem((2, group, half_snaps * pair * 3 // 4, 128), low),
        modes_got=vmem((2, group, half_snaps * pair * 3 // 4, 128), low),
        rows_out=vmem((2, group, half_snaps * pair * 3 // 4, 128), low),
        rows_got=vmem((2, group, half_snaps * pair * 3 // 4, 128), low),
        arrived=vmem((snap_local, pair * group, 128), low),
        gathered=vmem((2, spread, channel), f32),
        home_low=vmem((2, spread, channel), low),
        weight_one=vmem((256, 256), low),
        weight_two=vmem((256, 256), low),
        spectrum=vmem((snap_local * lat_total * modes, 256), low),
        pre_one=vmem((snap_local * lat_total * modes, 256), f32),
        act_one=vmem((snap_local * lat_total * modes, 256), low),
        pre_two=vmem((snap_local * lat_total * modes, 256), f32),
        grad_pre=vmem((snap_local * lat_total * modes, 256), f32),
        grad_two=vmem((snap_local * lat_total * modes, 256), low),
        grad_one=vmem((snap_local * lat_total * modes, 256), low),
        folds=vmem((5, 8, channel), f32),
        pair_grad=vmem((256, 256), f32),
        act=vmem((tokens, width), low),
        slope=vmem((tokens, width), low),
        bias=vmem((parts, 1, width), f32),
        grad_bias=vmem((parts, 8, width), f32),
        grad_rows=vmem((16, channel), f32),
        grads=vmem((2, levels, 2, owned, width), low),
        core_got=vmem((2, 2, levels, owned, width), low),
        half_out=vmem((2, 2, 2, levels, owned, half), low),
        half_got=vmem((4, 2, levels, owned, half), low),
        quarter_out=vmem((2, 2, 2, levels, owned, quarter), low),
        quarter_got=vmem((2, 2, levels, owned, quarter), low),
        level_out=vmem((2, levels, 2, owned, quarter), low),
        level_got=vmem((4, levels, 2, owned, quarter), low),
        total=vmem((parts, snaps, 2, owned, quarter), low),
        filt_out=vmem((snaps, 4, owned, 128), low),
        tiles=vmem((group, 16, 128), f32),
        tiles_got=vmem((group, 16, 128), f32),
        snap_tiles=vmem((snaps, 16, 128), f32),
        swap_l=dma((4,)),
        load_sem=dma((len(inputs) + 1,)),
    )
    for name, shape in dict(
        small=(group,),
        swap=(4,),
        first=(parts, levels),
        second=(parts,),
        third=(parts,),
        fourth=(parts,),
        block=(2, 2, group),
        row=(2, 2, group),
        core=(2, 2),
        half=(4, 2),
        quarter=(2, 2),
        level=(4, levels),
        last=(parts, snaps),
        filt=(snaps,),
        tile=(group,),
        snap_tile=(snaps,),
    ).items():
        scratch[name + "_s"] = dma(shape)
        scratch[name + "_r"] = dma(shape)
    names = [*inputs, *outputs, *scratch]
    far = pl.BlockSpec(memory_space=pl.ANY)
    near = pl.BlockSpec(memory_space=pltpu.VMEM)
    results = pl.pallas_call(
        functools.partial(block_body, names, (snaps, group, parts, width)),
        in_specs=[far] * len(inputs),
        out_specs=[far, far, far, near, near],
        out_shape=list(outputs.values()),
        scratch_shapes=list(scratch.values()),
        compiler_params=pltpu.CompilerParams(
            collective_id=0, has_side_effects=True, vmem_limit_bytes=VMEM_LIMIT
        ),
        cost_estimate=pl.CostEstimate(
            flops=12 * tokens * channel * hidden,
            bytes_accessed=4 * hidden * channel,
            transcendentals=tokens * hidden,
        ),
        name="block_pass",
    )(*inputs.values())
    return results


def adamw_near(master, first_mom, second_mom, gradient, step_rate):
    first_next = beta_one * (first_mom + gradient)
    second_next = beta_two * (second_mom + gradient * gradient)
    fix_one = 1.0 / (1.0 - beta_one**STEP)
    fix_two = 1.0 / (1.0 - beta_two**STEP)
    grown = second_next * fix_two
    bottom = grown * lax.rsqrt(grown) + adam_eps
    master_next = (1.0 - step_rate * decay_rate) * master - (
        (step_rate * fix_one) * first_next
    ) / bottom
    return (master_next, first_next, second_next, master_next.astype(jnp.bfloat16))


def step_body(names, positions, *refs):
    g = Refs()
    for name, ref in zip(names, refs, strict=True):
        setattr(g, name, ref)
    parts, snaps = g.grad_mlp.shape[:2]
    quarter = g.grad_mlp.shape[4]
    width = snaps * quarter
    chunks = g.near.shape[1]
    some = parts // chunks
    moments = ("w", "m", "v")
    results = ("new", "first", "second", "copy")

    pieces = g.far_sem.shape[2]
    ends = ((g.out, g.out_near, g.out_o), (g.in_grad, g.in_grad_near, g.in_grad_o))

    def passing(kind, piece, leg):
        size = ends[kind][0].shape[0] // pieces
        rows = pl.ds(piece * size, size)
        return pltpu.make_async_copy(
            ends[kind][leg].at[rows], ends[kind][leg + 1].at[rows], g.far_sem.at[leg, kind, piece]
        )

    through = [(kind, piece) for kind in range(2) for piece in range(pieces)]

    def chunk_cols(chunk):
        return pl.ds(chunk * some * width, some * width)

    def load(chunk):
        near = [
            pltpu.make_async_copy(
                getattr(g, "mlp_" + kind).at[:, :, chunk_cols(chunk)],
                g.near.at[index, chunk],
                g.near_sem.at[index, chunk],
            )
            for index, kind in enumerate(moments)
        ]
        near.append(
            pltpu.make_async_copy(
                g.grad_mlp.at[pl.ds(chunk * some, some)], g.grad_near.at[chunk], g.near_sem.at[3, chunk]
            )
        )
        return near

    def store(chunk):
        copies = [
            pltpu.make_async_copy(
                g.near.at[index, chunk],
                getattr(g, "mlp_" + kind).at[:, :, chunk_cols(chunk)],
                g.back_sem.at[index, chunk],
            )
            for index, kind in enumerate(results[:3])
        ]
        copies.append(
            pltpu.make_async_copy(
                g.low_near.at[chunk], g.mlp_copy.at[:, :, chunk_cols(chunk)], g.back_sem.at[3, chunk]
            )
        )
        return copies

    coming = [load(chunk) for chunk in range(chunks)]
    going = [store(chunk) for chunk in range(chunks)]
    for chunk in range(chunks):
        for copy in coming[chunk]:
            copy.start()
        for each in through[chunk::chunks]:
            passing(*each, 0).start()

    def put(prefix, values):
        for kind, value in zip(results, values, strict=True):
            getattr(g, prefix + kind)[...] = value

    owned = g.filt_w.shape[2]
    put(
        "filt_",
        adamw(g.filt_w[...], g.filt_m[...], g.filt_v[...], g.grad_filt[:, :, 0:owned], rate_filter),
    )
    rows = g.small_w.shape[0]
    put(
        "small_",
        adamw(
            g.small_w[...], g.small_m[...], g.small_v[...], g.grad_small[0:rows, 0:owned], rate_small
        ),
    )
    totals = g.grad_small[rows : rows + 2, 0 : g.run.shape[1]]
    g.stats[...] = stat_decay * g.run[...] + (1.0 - stat_decay) * totals / positions

    for chunk in range(chunks):
        for copy in coming[chunk]:
            copy.wait()
        for part, matrix, snap in [
            (part, matrix, snap)
            for part in range(some)
            for matrix in range(2)
            for snap in range(snaps)
        ]:
            place = snap if matrix else 2 * (snap % 2) + snap // 2
            first_col = part * width + place * quarter
            where = (chunk, matrix, slice(None), slice(first_col, first_col + quarter))
            now = [g.near[(kind, *where)] for kind in range(3)]
            grad = g.grad_near[chunk, part, snap, matrix].astype(jnp.float32)
            values = adamw_near(*now, grad, rate_mlp)
            for kind in range(3):
                g.near[(kind, *where)] = values[kind]
            g.low_near[where] = values[3]
        for copy in going[chunk]:
            copy.start()
        for each in through[chunk::chunks]:
            passing(*each, 0).wait()
            passing(*each, 1).start()
    for each in through:
        passing(*each, 1).wait()
    for chunk in range(chunks):
        for copy in going[chunk]:
            copy.wait()


def step_pass(shown, grads, masters, run_stats, positions):
    grad_mlp, grad_filt, grad_small = grads
    mlp, filt, small = masters
    chunks = grad_mlp.shape[0]
    width = mlp[0].shape[2] // chunks
    f32, low = jnp.float32, jnp.bfloat16
    far = pl.BlockSpec(memory_space=pltpu.HBM)
    near = pl.BlockSpec(memory_space=pltpu.VMEM)
    inputs = dict(out=shown[0], in_grad=shown[1], grad_mlp=grad_mlp)
    inputs |= dict(zip(("mlp_w", "mlp_m", "mlp_v"), mlp, strict=True))
    far_in = len(inputs)
    inputs |= dict(grad_filt=grad_filt, grad_small=grad_small)
    inputs |= dict(zip(("filt_w", "filt_m", "filt_v"), filt, strict=True))
    inputs |= dict(zip(("small_w", "small_m", "small_v"), small, strict=True))
    inputs |= dict(run=run_stats)
    results = (("new", f32), ("first", f32), ("second", f32), ("copy", low))
    outputs = {
        name + "_o": jax.ShapeDtypeStruct(array.shape, array.dtype)
        for name, array in zip(("out", "in_grad"), shown, strict=True)
    }
    outputs |= {"mlp_" + kind: jax.ShapeDtypeStruct(mlp[0].shape, dt) for kind, dt in results}
    far_out = len(outputs)
    outputs |= {"filt_" + kind: jax.ShapeDtypeStruct(filt[0].shape, dt) for kind, dt in results}
    outputs |= {"small_" + kind: jax.ShapeDtypeStruct(small[0].shape, dt) for kind, dt in results}
    outputs |= dict(stats=jax.ShapeDtypeStruct(run_stats.shape, f32))
    scratch = dict(
        near=pltpu.VMEM((3, chunks, 2, mlp[0].shape[1], width), f32),
        grad_near=pltpu.VMEM((chunks, grad_mlp.shape[0] // chunks, *grad_mlp.shape[1:]), low),
        low_near=pltpu.VMEM((chunks, 2, mlp[0].shape[1], width), low),
        near_sem=pltpu.SemaphoreType.DMA((4, chunks)),
        back_sem=pltpu.SemaphoreType.DMA((4, chunks)),
        out_near=pltpu.VMEM(shown[0].shape, low),
        in_grad_near=pltpu.VMEM(shown[1].shape, f32),
        far_sem=pltpu.SemaphoreType.DMA((2, 2, divisor(shown[0].shape[0], 1, 4))),
    )
    return pl.pallas_call(
        functools.partial(step_body, [*inputs, *outputs, *scratch], positions),
        in_specs=[far] * far_in + [near] * (len(inputs) - far_in),
        out_specs=[far] * far_out + [near] * (len(outputs) - far_out),
        out_shape=list(outputs.values()),
        scratch_shapes=list(scratch.values()),
        compiler_params=pltpu.CompilerParams(vmem_limit_bytes=VMEM_LIMIT),
        name="step_pass",
    )(*inputs.values())


def per_device_blocks(
    fields,
    cotangent,
    valid_mask,
    kept_modes,
    mlp_master,
    mlp_first,
    mlp_second,
    filter_master,
    filter_first,
    filter_second,
    small_master,
    small_first,
    small_second,
    run_stats,
):
    snaps, group = lax.axis_size("snap"), lax.axis_size("sp")
    out, in_grad, *grads = block_pass(
        fields, cotangent, valid_mask, kept_modes, mlp_master, filter_master, small_master, snaps, group
    )
    snap_local, row_local, lon_total, channel = fields.shape
    positions = snap_local * snaps * row_local * group * lon_total
    out, in_grad, *stepped = step_pass(
        (out, in_grad),
        grads,
        (
            (mlp_master, mlp_first, mlp_second),
            (filter_master, filter_first, filter_second),
            (small_master, small_first, small_second),
        ),
        run_stats,
        positions,
    )
    rows_apart = (snap_local, lon_total, row_local, channel)
    out, in_grad = [
        jnp.transpose(array.reshape(rows_apart), (0, 2, 1, 3)) for array in (out, in_grad)
    ]
    return (out, in_grad, *stepped)


def per_device(*arrays):
    group, snaps = lax.axis_size("sp"), lax.axis_size("snap")
    channel, hidden = arrays[0].shape[3], arrays[4].shape[2]
    by_block = group == BLOCKS and snaps == 4 and arrays[3].shape[1] == 1
    if by_block and hidden == 6 * 512 and channel // group <= 128 and channel % (16 * group) == 0:
        return per_device_blocks(*arrays)
    return per_device_modes(*arrays)


def solution(mesh):
    return jax.shard_map(
        per_device,
        mesh=mesh,
        in_specs=(
            P("snap", "sp", None, None),
            P("snap", "sp", None, None),
            P("snap", "sp", None),
            P(None, "sp"),
            P(None, "sp", None),
            P(None, "sp", None),
            P(None, "sp", None),
            P(None, "sp", None),
            P(None, "sp", None),
            P(None, "sp", None),
            P(None, "sp"),
            P(None, "sp"),
            P(None, "sp"),
            P(),
        ),
        out_specs=(
            P("snap", "sp", None, None),
            P("snap", "sp", None, None),
            P(None, "sp", None),
            P(None, "sp", None),
            P(None, "sp", None),
            P(None, "sp", None),
            P(None, "sp", None),
            P(None, "sp", None),
            P(None, "sp", None),
            P(None, "sp", None),
            P(None, "sp"),
            P(None, "sp"),
            P(None, "sp"),
            P(None, "sp"),
            P(),
        ),
        check_vma=False,
    )
```

```python
import functools
import math

import jax
import jax.numpy as jnp
import ml_dtypes
import numpy as np
from jax import lax
from jax.experimental import pallas as pl
from jax.experimental.pallas import tpu as pltpu
from jax.sharding import PartitionSpec as P

BLOCKS = 8
NVAR = 20
STEP = 10
VMEM_LIMIT = 63 * 1024 * 1024


eps_norm = 1e-06
shrink_level = 0.01
beta_one = 0.5
beta_two = 0.5
adam_eps = 1e-08
decay_rate = 0.01
rate_mlp = 0.03
rate_filter = 0.1
rate_small = 0.2
stat_decay = 0.5


def layer_norm(values, gain_vec, shift_vec):
    centred = values - jnp.mean(values, axis=-1, keepdims=True)
    spread = jnp.mean(centred * centred, axis=-1, keepdims=True)
    return centred * lax.rsqrt(spread + eps_norm) * gain_vec + shift_vec


def shrink(values):
    return values - shrink_level * jnp.tanh(values / shrink_level)


def lon_tables(lon_total, mode_total):
    places = jnp.arange(lon_total, dtype=jnp.int32)
    orders = jnp.arange(mode_total, dtype=jnp.int32)
    angles = (places[:, None] * orders[None, :] % lon_total).astype(jnp.float32) * (
        2.0 * math.pi / lon_total
    )
    scaling = 1.0 / math.sqrt(lon_total)
    forward_tab = jnp.stack([jnp.cos(angles), -jnp.sin(angles)], axis=1) * scaling
    doubling = jnp.where(orders == 0, 1.0, 2.0).astype(jnp.float32)[:, None]
    inverse_tab = (
        jnp.stack([jnp.cos(angles).T * doubling, -jnp.sin(angles).T * doubling], axis=0) * scaling
    )
    return (forward_tab.astype(jnp.bfloat16), inverse_tab.astype(jnp.bfloat16))


def lat_table(lat_total):
    places = jnp.arange(lat_total, dtype=jnp.int32)
    angles = (places[:, None] * places[None, :] % lat_total).astype(jnp.float32) * (
        2.0 * math.pi / lat_total
    )
    cosine = jnp.cos(angles)
    sine_part = jnp.sin(angles)
    upper_rows = jnp.stack([cosine, sine_part], axis=1)
    bottom = jnp.stack([-sine_part, cosine], axis=1)
    return (jnp.stack([upper_rows, bottom], axis=0) / math.sqrt(lat_total)).astype(jnp.bfloat16)


def complex_pair(real_part, imag_part):
    return jnp.stack([jnp.stack([real_part, -imag_part]), jnp.stack([imag_part, real_part])])


gelu_scale = math.sqrt(2.0 / math.pi)
gelu_cubic = 0.044715


def gelu_both(value):
    bend = (gelu_scale * gelu_cubic) * (value * value)
    turn = jnp.tanh(value * (gelu_scale + bend))
    half = 0.5 + 0.5 * turn
    slope = half * (1.0 + (value * (1.0 - turn)) * (gelu_scale + 3.0 * bend))
    return value * half, slope


def dot_nt(left, right):
    return lax.dot_general(
        left, right, (((1,), (1,)), ((), ())), preferred_element_type=jnp.float32
    )


def dot_nn(left, right):
    return jnp.dot(left, right, preferred_element_type=jnp.float32)


def divisor(total, unit, most):
    return max(size for size in range(unit, most + 1, unit) if total % size == 0)


def mlp_body(
    tile,
    normed_ref,
    cot_ref,
    up_ref,
    down_ref,
    bias_ref,
    out_ref,
    back_ref,
    grad_up_ref,
    grad_down_ref,
    grad_bias_ref,
    normed_turned,
    cot_turned,
    act_ref,
    slope_ref,
):
    tokens = normed_ref.shape[0]

    @pl.when(pl.program_id(0) == 0)
    def _():
        normed_turned[...] = normed_ref[...].T
        cot_turned[...] = cot_ref[...].T
        out_ref[...] = jnp.zeros_like(out_ref)
        back_ref[...] = jnp.zeros_like(back_ref)

    grad_bias_ref[...] = jnp.zeros_like(grad_bias_ref)

    @pl.loop(0, tokens // tile)
    def _(step):
        rows = pl.ds(pl.multiple_of(step * tile, tile), tile)
        act, slope = gelu_both(dot_nn(normed_ref[rows, :], up_ref[...]) + bias_ref[...])
        act = act.astype(jnp.bfloat16)
        slope = (dot_nn(cot_ref[rows, :], down_ref[...]) * slope).astype(jnp.bfloat16)
        act_ref[rows, :] = act
        slope_ref[rows, :] = slope
        grad_bias_ref[...] += jnp.sum(slope.astype(jnp.float32), axis=0, keepdims=True)
        out_ref[rows, :] += dot_nt(act, down_ref[...])
        back_ref[rows, :] += dot_nt(slope, up_ref[...])

    grad_up_ref[...] = dot_nn(normed_turned[...], slope_ref[...]).astype(grad_up_ref.dtype)
    grad_down_ref[...] = dot_nn(cot_turned[...], act_ref[...]).astype(grad_down_ref.dtype)


def mlp_pass(normed, cot, weights, bias):
    tokens, channel = normed.shape
    hidden = weights.shape[2]
    width = divisor(hidden, 128, 512)
    tile = divisor(tokens, 16, 480)
    whole = pl.BlockSpec((tokens, channel), lambda j: (0, 0))
    block = pl.BlockSpec((channel, width), lambda j: (0, j))
    line = pl.BlockSpec((1, width), lambda j: (0, j))
    part = lambda which: pl.BlockSpec((None, channel, width), lambda j: (which, 0, j))
    total = jax.ShapeDtypeStruct((tokens, channel), jnp.float32)
    grads = jax.ShapeDtypeStruct((channel, hidden), jnp.bfloat16)
    return pl.pallas_call(
        functools.partial(mlp_body, tile),
        grid=(hidden // width,),
        in_specs=[whole, whole, part(0), part(1), line],
        out_specs=[whole, whole, block, block, line],
        out_shape=[total, total, grads, grads, jax.ShapeDtypeStruct((1, hidden), jnp.float32)],
        scratch_shapes=[
            pltpu.VMEM((channel, tokens), jnp.bfloat16),
            pltpu.VMEM((channel, tokens), jnp.bfloat16),
            pltpu.VMEM((tokens, width), jnp.bfloat16),
            pltpu.VMEM((tokens, width), jnp.bfloat16),
        ],
        compiler_params=pltpu.CompilerParams(vmem_limit_bytes=56 * 1024 * 1024),
        cost_estimate=pl.CostEstimate(
            flops=12 * tokens * channel * hidden,
            bytes_accessed=8 * channel * hidden + 12 * tokens * channel,
            transcendentals=tokens * hidden,
        ),
        name="mlp_pass",
    )(normed, cot, weights, weights, bias)


def spectral_front(arrived, lat_fwd, first_pair, second_pair, bias_one, bias_two):
    spectrum = jnp.einsum(
        "pkqr,nrqmd->nkpmd", lat_fwd, arrived, preferred_element_type=jnp.float32
    ).astype(jnp.bfloat16)
    snap_local, lat_total, pair_count, mode_local, channel = spectrum.shape
    blocked = spectrum.reshape(
        snap_local, lat_total, pair_count, mode_local, BLOCKS, channel // BLOCKS
    )
    pre_one = (
        jnp.einsum("nkqmbi,pqbio->nkpmbo", blocked, first_pair, preferred_element_type=jnp.float32)
        + bias_one
    )
    act_one = jax.nn.gelu(pre_one).astype(jnp.bfloat16)
    pre_two = (
        jnp.einsum("nkqmbi,pqbio->nkpmbo", act_one, second_pair, preferred_element_type=jnp.float32)
        + bias_two
    )
    return (blocked, pre_one, act_one, pre_two)


def adamw(master, first_mom, second_mom, gradient, step_rate):
    first_next = beta_one * first_mom + (1.0 - beta_one) * gradient
    second_next = beta_two * second_mom + (1.0 - beta_two) * gradient * gradient
    fix_one = 1.0 / (1.0 - beta_one**STEP)
    fix_two = 1.0 / (1.0 - beta_two**STEP)
    direction = first_next * fix_one / (jnp.sqrt(second_next * fix_two) + adam_eps)
    master_next = master - step_rate * (direction + decay_rate * master)
    return (master_next, first_next, second_next, master_next.astype(jnp.bfloat16))


def per_device_modes(
    fields,
    cotangent,
    valid_mask,
    kept_modes,
    mlp_master,
    mlp_first,
    mlp_second,
    filter_master,
    filter_first,
    filter_second,
    small_master,
    small_first,
    small_second,
    run_stats,
):
    group_size = lax.axis_size("sp")
    snap_local, row_local, lon_total, channel = fields.shape
    lat_total = row_local * group_size
    mode_local = kept_modes.shape[1]
    mode_total = mode_local * group_size
    block_width = channel // BLOCKS
    lon_fwd, lon_inv = lon_tables(lon_total, mode_total)
    lat_fwd = lat_table(lat_total)
    mlp_w, filt_w, small_w = (
        lax.all_gather(mlp_master.astype(jnp.bfloat16), "sp", axis=1, tiled=True),
        lax.all_gather(filter_master.astype(jnp.bfloat16), "sp", axis=1, tiled=True),
        lax.all_gather(small_master.astype(jnp.bfloat16), "sp", axis=1, tiled=True),
    )
    small_f = small_w.astype(jnp.float32)
    weights = filt_w.reshape(4, BLOCKS, block_width, block_width)
    first_pair = complex_pair(weights[0], weights[1])
    second_pair = complex_pair(weights[2], weights[3])
    bias_one = small_f[4:6].reshape(2, 1, BLOCKS, block_width)
    bias_two = small_f[6:8].reshape(2, 1, BLOCKS, block_width)
    fields_float = fields.astype(jnp.float32)
    normed, norm_pull = jax.vjp(layer_norm, fields_float, small_f[0], small_f[1])
    normed_low = normed.astype(jnp.bfloat16)
    spec_lon = jnp.einsum(
        "nrld,lqm->nrqmd", normed_low, lon_fwd, preferred_element_type=jnp.float32
    ).astype(jnp.bfloat16)
    arrived = lax.all_to_all(spec_lon, "sp", split_axis=3, concat_axis=1, tiled=True)
    spectral = spectral_front(arrived, lat_fwd, first_pair, second_pair, bias_one, bias_two)
    keep_mask = kept_modes.astype(jnp.float32)[None, :, None, :, None, None]
    masked = (shrink(spectral[3]) * keep_mask).astype(jnp.bfloat16)
    masked = masked.reshape(snap_local, lat_total, 2, mode_local, channel)
    returned = jnp.einsum(
        "pkqr,nkpmd->nrqmd", lat_fwd, masked, preferred_element_type=jnp.float32
    ).astype(jnp.bfloat16)
    home_modes = lax.all_to_all(returned, "sp", split_axis=1, concat_axis=3, tiled=True)
    filtered = jnp.einsum(
        "nrqmd,qml->nrld", home_modes, lon_inv, preferred_element_type=jnp.float32
    )
    mixture = fields_float + normed + filtered
    normed_two, norm_two_pull = jax.vjp(layer_norm, mixture, small_f[2], small_f[3])
    normed_two_low = normed_two.astype(jnp.bfloat16)
    tokens = snap_local * row_local * lon_total
    passed = mlp_pass(
        normed_two_low.reshape(tokens, channel),
        cotangent.reshape(tokens, channel),
        mlp_w,
        small_f[9:].reshape(1, -1),
    )
    output = mixture + passed[0].reshape(mixture.shape) + small_f[8]
    weight_mask = valid_mask.astype(jnp.float32)[..., None]
    variables = output[..., :NVAR]
    local_sums = jnp.stack(
        [
            jnp.sum(weight_mask * variables, axis=(0, 1, 2)),
            jnp.sum(weight_mask * variables * variables, axis=(0, 1, 2)),
        ]
    )
    total_sums = lax.psum(local_sums, ("snap", "sp"))
    positions = snap_local * lax.axis_size("snap") * lat_total * lon_total
    stats_new = stat_decay * run_stats + (1.0 - stat_decay) * total_sums / positions
    cot_float = cotangent.astype(jnp.float32)
    grad_normed_two = passed[1].reshape(mixture.shape)
    grad_bias_hidden = passed[4]
    grad_mix_norm, grad_gain_two, grad_shift_two = norm_two_pull(grad_normed_two)
    grad_mixture = cot_float + grad_mix_norm
    grad_bias_out = jnp.sum(cot_float, axis=(0, 1, 2))
    grad_filtered = grad_mixture.astype(jnp.bfloat16)
    grad_home = jnp.einsum(
        "nrld,qml->nrqmd", grad_filtered, lon_inv, preferred_element_type=jnp.float32
    ).astype(jnp.bfloat16)
    grad_returned = lax.all_to_all(grad_home, "sp", split_axis=3, concat_axis=1, tiled=True)
    grad_masked = jnp.einsum(
        "pkqr,nrqmd->nkpmd", lat_fwd, grad_returned, preferred_element_type=jnp.float32
    )
    arrived_again = lax.all_to_all(spec_lon, "sp", split_axis=3, concat_axis=1, tiled=True)
    used_front = spectral_front(arrived_again, lat_fwd, first_pair, second_pair, bias_one, bias_two)
    blocked, pre_one, act_one, pre_two = used_front
    grad_two = jax.vjp(shrink, pre_two)[1](grad_masked.reshape(pre_two.shape) * keep_mask)[
        0
    ].astype(jnp.bfloat16)
    grad_bias_two = jnp.sum(grad_two.astype(jnp.float32), axis=(0, 1, 3))
    grad_second = jnp.einsum(
        "nkqmbi,nkpmbo->pqbio", act_one, grad_two, preferred_element_type=jnp.float32
    )
    grad_act = jnp.einsum(
        "nkpmbo,pqbio->nkqmbi", grad_two, second_pair, preferred_element_type=jnp.float32
    )
    grad_one = jax.vjp(jax.nn.gelu, pre_one)[1](grad_act)[0].astype(jnp.bfloat16)
    grad_bias_one = jnp.sum(grad_one.astype(jnp.float32), axis=(0, 1, 3))
    grad_first = jnp.einsum(
        "nkqmbi,nkpmbo->pqbio", blocked, grad_one, preferred_element_type=jnp.float32
    )
    grad_spectrum = jnp.einsum(
        "nkpmbo,pqbio->nkqmbi", grad_one, first_pair, preferred_element_type=jnp.float32
    ).astype(jnp.bfloat16)
    grad_spectrum = grad_spectrum.reshape(snap_local, lat_total, 2, mode_local, channel)
    grad_lon = jnp.einsum(
        "pkqr,nkpmd->nrqmd", lat_fwd, grad_spectrum, preferred_element_type=jnp.float32
    ).astype(jnp.bfloat16)
    grad_rows = lax.all_to_all(grad_lon, "sp", split_axis=1, concat_axis=3, tiled=True)
    grad_normed = grad_mixture + jnp.einsum(
        "nrqmd,lqm->nrld", grad_rows, lon_fwd, preferred_element_type=jnp.float32
    )
    grad_field_norm, grad_gain_one, grad_shift_one = norm_pull(grad_normed)
    input_grad = grad_mixture + grad_field_norm
    grad_filter = jnp.stack(
        [
            grad_first[0, 0] + grad_first[1, 1],
            grad_first[1, 0] - grad_first[0, 1],
            grad_second[0, 0] + grad_second[1, 1],
            grad_second[1, 0] - grad_second[0, 1],
        ]
    ).reshape(4, channel, block_width)
    grad_small = jnp.concatenate(
        [
            jnp.stack([grad_gain_one, grad_shift_one, grad_gain_two, grad_shift_two]),
            grad_bias_one.reshape(2, channel),
            grad_bias_two.reshape(2, channel),
            grad_bias_out[None, :],
            grad_bias_hidden.reshape(-1, channel),
        ],
        axis=0,
    )
    shares = (
        jnp.stack([
            lax.psum_scatter(part, "sp", scatter_dimension=0, tiled=True) for part in passed[2:4]
        ]),
        lax.psum_scatter(grad_filter, "sp", scatter_dimension=1, tiled=True),
        lax.psum_scatter(grad_small, "sp", scatter_dimension=1, tiled=True),
    )
    owned = (
        lax.psum(shares[0].astype(jnp.bfloat16), "snap").astype(jnp.float32),
        lax.psum(shares[1].astype(jnp.bfloat16), "snap").astype(jnp.float32),
        lax.psum(shares[2].astype(jnp.bfloat16), "snap").astype(jnp.float32),
    )
    mlp_new, mlp_first_new, mlp_second_new, mlp_copy = adamw(
        mlp_master, mlp_first, mlp_second, owned[0], rate_mlp
    )
    filter_new, filter_first_new, filter_second_new, filter_copy = adamw(
        filter_master, filter_first, filter_second, owned[1], rate_filter
    )
    small_new, small_first_new, small_second_new, small_copy = adamw(
        small_master, small_first, small_second, owned[2], rate_small
    )
    return (
        output.astype(jnp.bfloat16),
        input_grad,
        mlp_new,
        mlp_first_new,
        mlp_second_new,
        mlp_copy,
        filter_new,
        filter_first_new,
        filter_second_new,
        filter_copy,
        small_new,
        small_first_new,
        small_second_new,
        small_copy,
        stats_new,
    )


FIRST, SECOND, THIRD, FOURTH, HALF, QUARTER, LEVEL, LAST = range(8)
SCHEDULE = {
    "a": [(FIRST, 0)],
    "b": [(FIRST, 1)],
    "c0": [(SECOND, 0)],
    "d1": [(SECOND, 1), (FIRST, 2)],
    "f0": [(THIRD, 0)],
    "f1": [(SECOND, 2), (FIRST, 3)],
    "g": [(THIRD, 1)],
    "h0": [(FIRST, 4)],
    "h1": [(FOURTH, 0), (THIRD, 2)],
    ("k2", 0): [(SECOND, 3), (SECOND, 4)],
    ("m", 0): [(FOURTH, 1), (FIRST, 5)],
    ("m0", 0): [(FOURTH, 2)],
    ("m1", 0): [(HALF, 0)],
    ("k", 1): [(THIRD, 3), (THIRD, 4)],
    ("k0", 2): [(HALF, 1)],
    ("m", 2): [(FOURTH, 3)],
    ("m1", 2): [(QUARTER, 0)],
    ("m2", 2): [(HALF, 2), (FOURTH, 4)],
    ("k", 3): [(FOURTH, 5)],
    ("m", 3): [(LEVEL, 0), (QUARTER, 1)],
    ("k", 4): [(HALF, 3)],
    ("k2", 4): [(LEVEL, 1)],
    ("l", 4): [(QUARTER, 2)],
    ("k", 5): [(LAST, 0), (LEVEL, 2), (QUARTER, 3)],
    ("k2", 5): [(HALF, 4)],
    ("m", 5): [(LAST, 1), (LEVEL, 3)],
    "o0": [(HALF, 5)],
    "o1": [(QUARTER, 4)],
    "r": [(LAST, 2), (LEVEL, 4)],
    "s": [(QUARTER, 5)],
    "u1": [(LAST, 3), (LAST, 4), (LEVEL, 5)],
    "x1": [(LAST, 5)],
}


def lon_matrix(lon_total, mode_total, snaps, rows):
    places = np.arange(lon_total)
    orders = np.arange(mode_total)
    angles = (places[:, None] * orders[None, :] % lon_total) * (2.0 * math.pi / lon_total)
    doubling = np.where(orders == 0, 1.0, 2.0)
    scaling = 1.0 / math.sqrt(lon_total)
    forward = np.stack([np.cos(angles), -np.sin(angles)], axis=1) * scaling
    inverse = forward * doubling

    def spread(table):
        table = np.einsum(
            "ab,lx,rs->alrbsx", np.eye(snaps), table.reshape(lon_total, -1), np.eye(rows)
        )
        return table.reshape(snaps * lon_total * rows, -1).astype(ml_dtypes.bfloat16)

    return spread(forward), spread(inverse)


def lon_turn(lon_total, rows):
    turn = np.einsum("lk,rs->rlks", np.eye(lon_total), np.eye(rows))
    return turn.reshape(rows, lon_total, lon_total * rows).astype(ml_dtypes.bfloat16)


def lat_matrix(lat_total, mode_total):
    places = np.arange(lat_total)
    angles = (places[:, None] * places[None, :] % lat_total) * (2.0 * math.pi / lat_total)
    cosine, sine = np.cos(angles), np.sin(angles)
    table = np.stack([np.stack([cosine, sine], axis=1), np.stack([-sine, cosine], axis=1)])
    table = np.einsum("pkqr,ab->pakrqb", table / math.sqrt(lat_total), np.eye(mode_total))
    size = 2 * lat_total * mode_total
    return table.reshape(size, size).astype(ml_dtypes.bfloat16)


class Refs:
    pass


def block_body(names, sizes, *refs):
    g = Refs()
    for name, ref in zip(names, refs, strict=True):
        setattr(g, name, ref)
    snaps, group, parts, width = sizes
    levels = group // 2
    tokens = g.fields.shape[0] * g.fields.shape[1]
    channel = g.fields.shape[2]
    owned = channel // group
    half = width // 2
    quarter = width // snaps
    tile = tokens // 2
    short = divisor(tokens // 2, 16, 720)
    packed = g.modes.shape[2]
    strip = divisor(tokens // 2, 48, 144)
    sub = divisor(strip, 16, 48)
    low = jnp.bfloat16
    f32 = jnp.float32

    me_snap = lax.axis_index("snap")
    me_sp = lax.axis_index("sp")
    core = lax.rem(me_sp, 2)
    level = me_sp // 2

    def at(snap, sp):
        return {"snap": snap, "sp": sp}

    def sp_after(step):
        return lax.rem(me_sp + step, group)

    def sp_before(step):
        return lax.rem(me_sp + group - step, group)

    def snap_after(step):
        return lax.rem(me_snap + step, snaps)

    def snap_before(step):
        return lax.rem(me_snap + snaps - step, snaps)

    def level_after(step):
        return lax.rem(level + step, levels)

    def level_before(step):
        return lax.rem(level + levels - step, levels)

    other_core = at(me_snap, me_sp + 1 - 2 * core)

    def send(src, dst, sems, index, target):
        return pltpu.make_async_remote_copy(
            src_ref=src,
            dst_ref=dst,
            send_sem=sems[0].at[index],
            recv_sem=sems[1].at[index],
            device_id=target,
            device_id_type=pl.DeviceIdType.MESH,
        )

    half_tokens = tokens // 2

    def strips(body, first=0, count=tokens, before=None, after=None):
        @pl.loop(0, count // strip)
        def _(step):
            if before is not None:
                before(first // strip + step)
            for at_row in range(0, strip, sub):
                body(pl.ds(pl.multiple_of(first + step * strip + at_row, 16), sub))
            if after is not None:
                after(first // strip + step)

    def half_strips(body, part, **around):
        strips(body, part * half_tokens, half_tokens, **around)

    def strip_copy(near, far, sems, place, out):
        rows = pl.ds(pl.multiple_of(place * strip, strip), strip)
        ends = [near.at[rows], far.reshape(tokens, channel).at[rows]]
        if not out:
            ends.reverse()
        return pltpu.make_async_copy(*ends, sems.at[place])

    def fields_load(place):
        return strip_copy(g.fields_in, g.fields, g.fields_sem, place, False)

    def cot_load(place):
        return strip_copy(g.cot_in, g.cot, g.cot_sem, place, False)

    def out_copy(place):
        return strip_copy(g.fields_in, g.out, g.fields_sem, place, True)

    def grad_copy(place):
        return strip_copy(g.grid, g.in_grad, g.cot_sem, place, True)

    def half_rows(part):
        return slice(part * half_tokens, (part + 1) * half_tokens)

    def fold(value):
        return jnp.sum(value.reshape(-1, 8, value.shape[1]), axis=0)

    loads = {}

    def load(name, index):
        copy = pltpu.make_async_copy(getattr(g, name), getattr(g, name + "_in"), g.load_sem.at[index])
        copy.start()
        loads[name] = copy

    for index, name in enumerate(
        [name for name in names[: names.index("out")] if name not in ("mlp", "fields", "cot")]
    ):
        load(name, index)
    for copy in (fields_load, cot_load):
        for place in range(tokens // strip):
            copy(place).start()

    def master_load(part):
        return pltpu.make_async_copy(
            g.mlp.at[:, :, part * width : (part + 1) * width],
            g.mlp_part.at[part % 2],
            g.load_sem.at[len(loads) + part % 2],
        )

    master_load(0).start()
    master_load(1).start()

    barrier = pltpu.get_barrier_semaphore()
    peers = [at(me_snap, sp_after(step)) for step in range(1, group)]
    peers += [at(snap_after(step), me_sp) for step in range(1, snaps)]
    for peer in peers:
        pl.semaphore_signal(
            barrier, inc=1, device_id=peer, device_id_type=pl.DeviceIdType.MESH
        )

    loads["small"].wait()
    loads["kept"].wait()
    g.own_small[...] = jnp.zeros_like(g.own_small)
    rows_small = g.small.shape[0]
    g.own_small[0:rows_small, 0:owned] = g.small_in[...].astype(low).astype(f32)
    pairs_kept = g.kept.shape[1]
    lines = lax.broadcasted_iota(jnp.int32, (pairs_kept, pairs_kept), 0)
    places = lax.broadcasted_iota(jnp.int32, (pairs_kept, pairs_kept), 1)
    kept = jnp.where(lines == places, g.kept_in[...].astype(f32), 0.0)
    g.own_small[16:, :] = jnp.broadcast_to(
        jnp.sum(kept, axis=1, keepdims=True), (pairs_kept, g.own_small.shape[1])
    )
    pl.semaphore_wait(barrier, len(peers))

    def small_copy(step):
        return send(
            g.own_small, g.all_small.at[me_sp], (g.small_s, g.small_r), step, at(me_snap, sp_after(step))
        )

    for step in range(1, group):
        small_copy(step).start()
    g.all_small[me_sp] = g.own_small[...]

    snap_low = lax.rem(me_snap, 2)
    snap_high = me_snap // 2
    beside_low = me_snap + 1 - 2 * snap_low
    beside_high = me_snap + 2 - 4 * snap_high

    def own_quarter(part):
        odd = lax.rem(part, 2)
        return (1 - odd) * me_snap + odd * (2 * snap_low + snap_high)

    def own_place(part):
        return pl.ds(0, snaps) if part == parts - 1 else own_quarter(part)

    def half_quarters(part):
        return pl.ds(2 * (own_quarter(part) // 2), 2)

    def own_rows(sp):
        return pl.ds(pl.multiple_of(sp * owned, owned), owned)

    def spot(part):
        if isinstance(part, int):
            return part // 2 + parts // 2 * (part % 2)
        return lax.div(part, 2) + parts // 2 * lax.rem(part, 2)

    swaps = (
        (pl.ds(0, 1), own_place(0)),
        (pl.ds(3, 2), own_place(1)),
        (pl.ds(1, 2), own_place(0)),
        (pl.ds(5, 1), own_place(5)),
    )
    swapped = {0: 0, 1: 1, 2: 2, 5: 3}

    def swap_copy(batch):
        some, place = swaps[batch]
        return send(
            g.own_w.at[some, 1 - core, place],
            g.all_w.at[some, 1 - core, place, own_rows(me_sp)],
            (g.swap_s, g.swap_r),
            batch,
            other_core,
        )

    def swap_local(batch):
        some, place = swaps[batch]
        return pltpu.make_async_copy(
            g.own_w.at[some, core, place],
            g.all_w.at[some, core, place, own_rows(me_sp)],
            g.swap_l.at[batch],
        )

    def start_swap(batch):
        swap_copy(batch).start()
        swap_local(batch).start()

    def first_copy(part, step):
        rows = pl.ds(pl.multiple_of(level * 2 * owned, 2 * owned), 2 * owned)
        view = g.all_w.at[spot(part), core, own_place(part), rows]
        target = at(me_snap, 2 * level_after(step) + core)
        return send(view, view, (g.first_s, g.first_r), (part, step), target)

    def second_copy(part):
        odd = lax.rem(part, 2)
        view = g.all_w.at[spot(part), core, own_quarter(part)]
        target = at((1 - odd) * beside_low + odd * beside_high, me_sp)
        return send(view, view, (g.second_s, g.second_r), part, target)

    def third_copy(part):
        odd = lax.rem(part, 2)
        view = g.all_w.at[spot(part), core, half_quarters(part)]
        target = at((1 - odd) * beside_high + odd * beside_low, me_sp)
        return send(view, view, (g.third_s, g.third_r), part, target)

    def fourth_copy(part):
        view = g.all_w.at[spot(part), core]
        return send(view, view, (g.fourth_s, g.fourth_r), part, other_core)

    def start_first(part):
        if part in swapped:
            swap_copy(swapped[part]).wait_recv()
            swap_local(swapped[part]).wait()
        for step in range(1, levels):
            first_copy(part, step).start()

    def wait_first(part):
        for step in range(1, levels):
            first_copy(part, step).wait_recv()

    def pass_second(part):
        wait_first(part)
        second_copy(part).start()

    def pass_third(part):
        second_copy(part).wait_recv()
        third_copy(part).start()

    def pass_fourth(part):
        if part == parts - 1:
            wait_first(part)
        else:
            third_copy(part).wait_recv()
        fourth_copy(part).start()

    stages = {FIRST: start_first, SECOND: pass_second, THIRD: pass_third, FOURTH: pass_fourth}

    def reach(point):
        for stage, part in SCHEDULE.get(point, ()):
            stages[stage](part)

    for part in range(parts):
        master_load(part).wait()
        for place in range(snaps):
            cols = slice(place * quarter, (place + 1) * quarter)
            g.own_w[spot(part), :, place] = g.mlp_part[part % 2, :, :, cols].astype(low)
        if part + 2 < parts:
            master_load(part + 2).start()
        if part == 0:
            start_swap(0)
        elif part == parts - 1:
            for batch in range(1, len(swaps)):
                start_swap(batch)
    reach("a")

    def first_unit(rows):
        values = g.fields_in[rows, :].astype(f32)
        centred = values - jnp.mean(values, axis=-1, keepdims=True)
        scale = lax.rsqrt(jnp.mean(centred * centred, axis=-1, keepdims=True) + eps_norm)
        g.scale_one[rows, :] = scale
        g.grid[rows, :] = centred * scale

    strips(first_unit, before=lambda place: fields_load(place).wait())
    reach("b")
    for step in range(1, group):
        small_copy(step).wait_recv()
    for sp in range(group):
        g.gains[:, sp * owned : (sp + 1) * owned] = g.all_small[sp, 0:16, 0:owned]
        g.keep[sp * pairs_kept : (sp + 1) * pairs_kept, :] = g.all_small[sp, 16:, :]

    def first_norm(rows):
        unit = g.grid[rows, :]
        normed = unit * g.gains[0:1, :] + g.gains[1:2, :]
        g.unit_one[rows, :] = unit.astype(low)
        g.normed[rows, :] = normed.astype(low)
        g.grid[rows, :] = g.fields_in[rows, :].astype(f32) + normed

    half_snaps = g.arrived.shape[0] // 2

    third_rows = packed // 3
    spare = 128 - owned

    def pack(value):
        return jnp.concatenate(
            [
                jnp.concatenate(
                    [
                        value[at_row * third_rows : (at_row + 1) * third_rows],
                        value[packed:, at_row * spare : (at_row + 1) * spare],
                    ],
                    axis=1,
                )
                for at_row in range(3)
            ],
            axis=0,
        ).astype(low)

    def unpack(value):
        value = value.astype(f32)
        rest = [
            value[at_row * third_rows : (at_row + 1) * third_rows, owned:] for at_row in range(3)
        ]
        return jnp.concatenate([value[:, 0:owned], jnp.concatenate(rest, axis=1)], axis=0)

    def block_copy(which, part, step):
        target = sp_after(step)
        return send(
            g.modes.at[part, target],
            g.modes_got.at[part, me_sp],
            (g.block_s, g.block_r),
            (which, part, step),
            at(me_snap, target),
        )

    def row_copy(which, part, step):
        target = sp_after(step)
        return send(
            g.rows_out.at[part, target],
            g.rows_got.at[part, me_sp],
            (g.row_s, g.row_r),
            (which, part, step),
            at(me_snap, target),
        )

    def to_blocks(table, which, part):
        modes = dot_nn(table, g.normed[half_rows(part), :])
        for block in range(group):
            g.modes[part, block] = pack(modes[:, block * owned : (block + 1) * owned])
        for step in range(1, group):
            block_copy(which, part, step).start()
        g.modes_got[part, me_sp] = g.modes[part, me_sp]

    def take_blocks(which, part):
        for step in range(1, group):
            block_copy(which, part, step).wait_recv()
        each = g.arrived.shape[1] // group
        for sp in range(group):
            value = unpack(g.modes_got[part, sp])
            value = jnp.concatenate([value, jnp.zeros((value.shape[0], spare), f32)], axis=1)
            for index in range(half_snaps):
                g.arrived[part * half_snaps + index, sp * each : (sp + 1) * each, :] = value[
                    index * each : (index + 1) * each
                ].astype(low)

    def to_rows(which, part, tables):
        each = tables[0].shape[0] // group
        for sp in range(group):
            value = [table[sp * each : (sp + 1) * each, 0:owned] for table in tables]
            g.rows_out[part, sp] = pack(jnp.concatenate(value, axis=0))
        for step in range(1, group):
            row_copy(which, part, step).start()
        g.rows_got[part, me_sp] = g.rows_out[part, me_sp]

    def home_modes(which, part):
        for step in range(1, group):
            row_copy(which, part, step).wait_recv()
        for block in range(group):
            g.gathered[part, :, block * owned : (block + 1) * owned] = unpack(
                g.rows_got[part, block]
            )
        g.home_low[part] = g.gathered[part].astype(low)

    loads["lon_f"].wait()
    for part in range(2):
        half_strips(first_norm, part)
        reach("c" + str(part))
        to_blocks(g.lon_f_in[...], 0, part)
        reach("d" + str(part))

    loads["filt"].wait()
    for weight, first in ((g.weight_one, 0), (g.weight_two, 2)):
        weight[...] = jnp.zeros_like(weight)
        real = g.filt_in[first].astype(low)
        imag = g.filt_in[first + 1].astype(low)
        weight[0:owned, 0:owned] = real
        weight[128 : 128 + owned, 128 : 128 + owned] = real
        weight[0:owned, 128 : 128 + owned] = imag
        weight[128 : 128 + owned, 0:owned] = -imag

    def bias_row(first):
        return jnp.concatenate(
            [g.own_small[first : first + 1, :], g.own_small[first + 1 : first + 2, :]], axis=1
        )

    for place in range(tokens // strip):
        cot_load(place).wait()
    reach("e")
    loads["lat_f"].wait()
    loads["lat_b"].wait()
    pairs = g.arrived.shape[1] // 2
    half_modes = half_snaps * pairs

    def mode_half(part):
        return slice(part * half_modes, (part + 1) * half_modes)

    def spectra(out, kind, part):
        for snap in range(part * half_snaps, (part + 1) * half_snaps):
            spectrum = dot_nn(g.lat_f_in[...], g.arrived[snap]).astype(kind)
            rows = slice(snap * pairs, (snap + 1) * pairs)
            out[rows, 0:128] = spectrum[0:pairs]
            out[rows, 128:256] = spectrum[pairs:]

    def grids(values):
        tables = []
        for index in range(half_snaps):
            rows = values[index * pairs : (index + 1) * pairs]
            rows = jnp.concatenate([rows[:, 0:128], rows[:, 128:256]], axis=0)
            tables.append(dot_nn(g.lat_b_in[...], rows))
        return tables

    def keep_half():
        keep = jnp.concatenate([g.keep[...], g.keep[...]], axis=1)
        return jnp.concatenate([keep] * half_snaps, axis=0)

    for part in range(2):
        take_blocks(0, part)
        rows = mode_half(part)
        spectra(g.spectrum, low, part)
        g.pre_one[rows, :] = dot_nn(g.spectrum[rows, :], g.weight_one[...]) + bias_row(4)
        g.act_one[rows, :] = gelu_both(g.pre_one[rows, :])[0].astype(low)
        g.pre_two[rows, :] = dot_nn(g.act_one[rows, :], g.weight_two[...]) + bias_row(6)
        to_rows(0, part, grids((shrink(g.pre_two[rows, :]) * keep_half()).astype(low)))
        reach("f" + str(part))
    g.cot_turned[...] = g.cot_in[...].T
    reach("g")

    loads["lon_i"].wait()

    def second_norm(rows):
        values = g.grid[rows, :]
        centred = values - jnp.mean(values, axis=-1, keepdims=True)
        scale = lax.rsqrt(jnp.mean(centred * centred, axis=-1, keepdims=True) + eps_norm)
        centred = centred * scale
        g.unit_two[rows, :] = centred.astype(low)
        g.scale_two[rows, :] = scale
        g.normed[rows, :] = (centred * g.gains[2:3, :] + g.gains[3:4, :]).astype(low)
        g.grid[rows, :] = values + g.gains[8:9, :]
        g.back[rows, :] = jnp.zeros((sub, channel), f32)

    for part in range(2):
        home_modes(0, part)
        g.grid[half_rows(part), :] += dot_nn(g.lon_i_in[...], g.home_low[part])
        reach("h" + str(part))
        half_strips(second_norm, part)
        reach("i" + str(part))
    g.normed_turned[...] = g.normed[...].T
    reach("j")
    flat = jnp.concatenate([g.gains[9 + row : 10 + row, :] for row in range(rows_small - 9)], axis=1)
    for part in range(parts):
        g.bias[part] = flat[:, part * width : (part + 1) * width]

    def core_copy(part, matrix):
        slot = lax.rem(part, 2)
        return send(
            g.grads.at[matrix, :, 1 - core],
            g.core_got.at[slot, matrix],
            (g.core_s, g.core_r),
            (slot, matrix),
            other_core,
        )

    places_one = (snap_low, snap_high)
    places_two = (snap_high, snap_low)
    beside_one = (beside_low, beside_high)
    beside_two = (beside_high, beside_low)

    def half_copy(part, matrix):
        slot = lax.rem(part, 2)
        place = lax.rem(part, 4)
        return send(
            g.half_out.at[slot, matrix, 1 - places_one[matrix]],
            g.half_got.at[place, matrix],
            (g.half_s, g.half_r),
            (place, matrix),
            at(beside_one[matrix], me_sp),
        )

    def quarter_copy(part, matrix):
        slot = lax.rem(part, 2)
        return send(
            g.quarter_out.at[slot, matrix, 1 - places_two[matrix]],
            g.quarter_got.at[slot, matrix],
            (g.quarter_s, g.quarter_r),
            (slot, matrix),
            at(beside_two[matrix], me_sp),
        )

    def level_copy(part, step):
        slot = lax.rem(part, 2)
        place = lax.rem(part, 4)
        target = level_after(step)
        return send(
            g.level_out.at[slot, target],
            g.level_got.at[place, level],
            (g.level_s, g.level_r),
            (place, step),
            at(me_snap, 2 * target + core),
        )

    def last_copy(part, step):
        view = g.total.at[part, me_snap]
        return send(view, view, (g.last_s, g.last_r), (part, step), at(snap_after(step), me_sp))

    def half_stage(part):
        slot = lax.rem(part, 2)
        for matrix in range(2):

            if part >= 2:
                half_copy(part - 2, matrix).wait_send()

            core_copy(part, matrix).wait_recv()

            @pl.loop(0, levels)
            def _(row, matrix=matrix):
                both = g.grads[matrix, row, core].astype(f32) + g.core_got[
                    slot, matrix, row
                ].astype(f32)
                both = both.astype(low)
                g.half_out[slot, matrix, 0, row] = both[:, 0:half]
                g.half_out[slot, matrix, 1, row] = both[:, half:width]

            half_copy(part, matrix).start()

    def quarter_stage(part):
        slot = lax.rem(part, 2)
        for matrix in range(2):

            if part >= 2:
                quarter_copy(part - 2, matrix).wait_send()

            half_copy(part, matrix).wait_recv()
            for row in range(levels):
                both = g.half_out[slot, matrix, places_one[matrix], row].astype(f32) + g.half_got[
                    lax.rem(part, 4), matrix, row
                ].astype(f32)
                both = both.astype(low)
                g.quarter_out[slot, matrix, 0, row] = both[:, 0:quarter]
                g.quarter_out[slot, matrix, 1, row] = both[:, quarter:half]
            quarter_copy(part, matrix).start()

    def level_stage(part):
        slot = lax.rem(part, 2)

        if part >= 2:
            for step in range(1, levels):
                level_copy(part - 2, step).wait_send()

        for matrix in range(2):
            quarter_copy(part, matrix).wait_recv()
            for row in range(levels):
                both = g.quarter_out[slot, matrix, places_two[matrix], row].astype(
                    f32
                ) + g.quarter_got[slot, matrix, row].astype(f32)
                g.level_out[slot, row, matrix] = both.astype(low)
        for step in range(1, levels):
            level_copy(part, step).start()

    def last_stage(part):
        slot = lax.rem(part, 2)
        for step in range(1, levels):
            level_copy(part, step).wait_recv()
        for matrix in range(2):
            sums = g.level_out[slot, level, matrix].astype(f32)
            for step in range(1, levels):
                sums += g.level_got[lax.rem(part, 4), level_before(step), matrix].astype(f32)
            g.total[part, me_snap, matrix] = sums.astype(low)
        for step in range(1, snaps):
            last_copy(part, step).start()

    stages |= {HALF: half_stage, QUARTER: quarter_stage, LEVEL: level_stage, LAST: last_stage}

    def weight(part, matrix):
        return jnp.concatenate([g.all_w[spot(part), matrix, place] for place in range(snaps)], axis=1)

    def add_products(part, rows):
        g.grid[rows, :] += dot_nt(g.act[rows, :], weight(part, 1))
        g.back[rows, :] += dot_nt(g.slope[rows, :], weight(part, 0))

    @pl.loop(0, parts)
    def _(part):
        def reach_in(point, also=True):
            for at_part in range(parts):
                if (point, at_part) in SCHEDULE:
                    pl.when((part == at_part) & also)(functools.partial(reach, (point, at_part)))

        def tile_rows(step):
            return pl.ds(pl.multiple_of(step * tile, tile), tile)

        fourth_copy(part).wait_recv()
        reach_in("k")
        g.grad_bias[part] = jnp.zeros(g.grad_bias.shape[1:], f32)

        act, slope = gelu_both(dot_nn(g.normed[...], weight(part, 0)) + g.bias[part])
        g.act[...] = act.astype(low)
        slope = (dot_nn(g.cot_in[...], weight(part, 1)) * slope).astype(low)
        g.slope[...] = slope
        g.grad_bias[part] += fold(slope.astype(f32))
        for at_step in range(3):
            reach_in("k" + str(at_step))

        reach_in("l")

        @pl.when(part >= 1)
        def _():
            for matrix in range(2):
                core_copy(part - 1, matrix).wait_send()

        shape = g.grads.shape[1:]
        g.grads[0] = dot_nn(g.normed_turned[...], g.slope[...]).astype(low).reshape(shape)
        core_copy(part, 0).start()
        g.grads[1] = dot_nn(g.cot_turned[...], g.act[...]).astype(low).reshape(shape)
        core_copy(part, 1).start()
        reach_in("m")

        @pl.when(part < parts - 1)
        def _():
            @pl.loop(0, tokens // tile)
            def _(step):
                add_products(part, tile_rows(step))
                for at_step in range(3):
                    reach_in("m" + str(at_step), step == (at_step + 1) // 2)

    g.folds[...] = jnp.zeros_like(g.folds)

    def second_back(rows):
        grad = g.back[rows, :]
        unit = g.unit_two[rows, :].astype(f32)
        cot = g.cot_in[rows, :].astype(f32)
        pulled = grad * g.gains[2:3, :]
        middle = jnp.mean(pulled, axis=-1, keepdims=True)
        slant = jnp.mean(pulled * unit, axis=-1, keepdims=True)
        total = cot + g.scale_two[rows, :] * (pulled - middle - unit * slant)
        g.back[rows, :] = total
        g.normed[rows, :] = total.astype(low)
        g.folds[2] += fold(grad * unit)
        g.folds[3] += fold(grad)
        g.folds[4] += fold(cot)

    loads["lon_it"].wait()
    for part in range(2):

        @pl.loop(0, half_tokens // short)
        def _(step, part=part):
            first_row = part * half_tokens + step * short
            add_products(parts - 1, pl.ds(pl.multiple_of(first_row, 16), short))

        reach("o" + str(part))
        half_strips(second_back, part)
        for step in range(1, group):
            block_copy(0, part, step).wait_send()
        to_blocks(g.lon_it_in[...], 1, part)
        reach("p" + str(part))
    reach("q")

    def low_out(rows):
        g.fields_in[rows, :] = g.grid[rows, :].astype(low)

    strips(low_out, after=lambda place: out_copy(place).start())
    reach("r")
    loads["valid"].wait()
    loads["turn"].wait()
    weigh = sum(
        dot_nn(g.valid_in[:, row, :].astype(f32).astype(low), g.turn_in[row])
        for row in range(g.valid.shape[1])
    )
    places_each = weigh.shape[1]
    precise = lax.Precision.HIGHEST
    sums = [jnp.zeros((1, 128), f32), jnp.zeros((1, 128), f32)]
    for snap in range(g.valid.shape[0]):
        variables = g.grid[snap * places_each : (snap + 1) * places_each, 0:128]
        for index, value in enumerate((variables, variables * variables)):
            sums[index] += jnp.dot(
                weigh[snap : snap + 1, :], value, precision=precise, preferred_element_type=f32
            )

    reach("s")

    def dot_tn(left, right):
        return lax.dot_general(
            left, right, (((0,), (0,)), ((), ())), preferred_element_type=f32
        )

    def filter_rows(first, grad):
        g.pair_grad[...] = grad
        real = g.pair_grad[0:128, 0:128] + g.pair_grad[128:256, 128:256]
        imag = g.pair_grad[0:128, 128:256] - g.pair_grad[128:256, 0:128]
        g.filt_out[me_snap, first] = real[0:owned].astype(low)
        g.filt_out[me_snap, first + 1] = imag[0:owned].astype(low)

    for part in range(2):
        take_blocks(1, part)
        reach("t" + str(part))
        rows = mode_half(part)
        spectra(g.grad_pre, f32, part)
        bend = jnp.tanh(g.pre_two[rows, :] / shrink_level)
        grad = (g.grad_pre[rows, :] * keep_half() * (bend * bend)).astype(low)
        g.grad_two[rows, :] = grad
        grad = dot_nt(grad, g.weight_two[...]) * gelu_both(g.pre_one[rows, :])[1]
        grad = grad.astype(low)
        g.grad_one[rows, :] = grad
        for step in range(1, group):
            row_copy(0, part, step).wait_send()
        to_rows(1, part, grids(dot_nt(grad, g.weight_one[...]).astype(low)))
        reach("u" + str(part))
    reach("v")
    bias_one = jnp.sum(g.grad_one[...].astype(f32), axis=0, keepdims=True)
    bias_two = jnp.sum(g.grad_two[...].astype(f32), axis=0, keepdims=True)
    filter_rows(2, dot_tn(g.act_one[...], g.grad_two[...]))
    filter_rows(0, dot_tn(g.spectrum[...], g.grad_one[...]))

    def filter_copy(step):
        view = g.filt_out.at[me_snap]
        return send(view, view, (g.filt_s, g.filt_r), step, at(snap_after(step), me_sp))

    for step in range(1, snaps):
        filter_copy(step).start()


    reach("w")

    loads["lon_ft"].wait()

    def first_back(rows):
        grad = g.grid[rows, :]
        unit = g.unit_one[rows, :].astype(f32)
        pulled = grad * g.gains[0:1, :]
        middle = jnp.mean(pulled, axis=-1, keepdims=True)
        slant = jnp.mean(pulled * unit, axis=-1, keepdims=True)
        g.grid[rows, :] = g.back[rows, :] + g.scale_one[rows, :] * (
            pulled - middle - unit * slant
        )
        g.folds[0] += fold(grad * unit)
        g.folds[1] += fold(grad)

    for part in range(2):
        home_modes(1, part)
        reach("x" + str(part))
        g.grid[half_rows(part), :] = g.back[half_rows(part), :] + dot_nn(
            g.lon_ft_in[...], g.home_low[part]
        )
        half_strips(first_back, part, after=lambda place: grad_copy(place).start())
        reach("y" + str(part))

    g.grad_rows[...] = jnp.zeros_like(g.grad_rows)
    for index, row in enumerate((0, 1, 2, 3, 8)):
        g.grad_rows[row : row + 1, :] = jnp.sum(g.folds[index], axis=0, keepdims=True)
    flat = jnp.concatenate(
        [jnp.sum(g.grad_bias[part], axis=0, keepdims=True) for part in range(parts)], axis=1
    )
    for row in range(rows_small - 9):
        g.grad_rows[9 + row : 10 + row, :] = flat[:, row * channel : (row + 1) * channel]
    for block in range(group):
        g.tiles[block] = jnp.zeros(g.tiles.shape[1:], f32)
        g.tiles[block, :, 0:owned] = g.grad_rows[:, block * owned : (block + 1) * owned]
        g.tiles[block, 13:14, :] = sums[0]
        g.tiles[block, 14:15, :] = sums[1]

    def tile_copy(step):
        target = sp_after(step)
        return send(
            g.tiles.at[target], g.tiles_got.at[me_sp], (g.tile_s, g.tile_r), step, at(me_snap, target)
        )

    def snap_tile_copy(step):
        view = g.snap_tiles.at[me_snap]
        return send(view, view, (g.snap_tile_s, g.snap_tile_r), step, at(snap_after(step), me_sp))

    for step in range(1, group):
        tile_copy(step).start()
    reach("z")

    for batch in range(len(swaps)):
        swap_copy(batch).wait_send()
    for part in range(parts):
        if part < parts - 1:
            second_copy(part).wait_send()
            third_copy(part).wait_send()
        fourth_copy(part).wait_send()
        for step in range(1, levels):
            first_copy(part, step).wait_send()
    for step in range(1, group):
        small_copy(step).wait_send()
        for part in range(2):
            block_copy(1, part, step).wait_send()
            row_copy(1, part, step).wait_send()
    for matrix in range(2):
        core_copy(parts - 1, matrix).wait_send()
        for part in (parts - 2, parts - 1):
            half_copy(part, matrix).wait_send()
            quarter_copy(part, matrix).wait_send()
    for step in range(1, levels):
        level_copy(parts - 2, step).wait_send()
    for step in range(1, snaps):
        filter_copy(step).wait_send()

    g.tiles_got[me_sp] = g.tiles[me_sp]
    for step in range(1, group):
        tile_copy(step).wait_recv()
    tile_sum = g.tiles_got[0]
    for sp in range(1, group):
        tile_sum += g.tiles_got[sp]
    g.snap_tiles[me_snap] = tile_sum
    g.snap_tiles[me_snap, 4:5, :] = bias_one[:, 0:128]
    g.snap_tiles[me_snap, 5:6, :] = bias_one[:, 128:256]
    g.snap_tiles[me_snap, 6:7, :] = bias_two[:, 0:128]
    g.snap_tiles[me_snap, 7:8, :] = bias_two[:, 128:256]
    for step in range(1, snaps):
        snap_tile_copy(step).start()

    for step in range(1, snaps):
        filter_copy(step).wait_recv()
    filter_sum = g.filt_out[0].astype(f32)
    for snap in range(1, snaps):
        filter_sum += g.filt_out[snap].astype(f32)
    g.grad_filt[...] = filter_sum
    for part in range(parts):
        for step in range(1, snaps):
            last_copy(part, step).wait_recv()
    grads_out = pltpu.make_async_copy(g.total, g.grad_mlp, g.load_sem.at[3])
    grads_out.start()
    for step in range(1, snaps):
        snap_tile_copy(step).wait_recv()
    tile_sum = g.snap_tiles[0]
    for snap in range(1, snaps):
        tile_sum += g.snap_tiles[snap]
    g.grad_small[...] = tile_sum

    grads_out.wait()
    for place in range(tokens // strip):
        out_copy(place).wait()
        grad_copy(place).wait()
    for step in range(1, levels):
        level_copy(parts - 1, step).wait_send()
    for step in range(1, group):
        tile_copy(step).wait_send()
    for step in range(1, snaps):
        snap_tile_copy(step).wait_send()
        for part in range(parts):
            last_copy(part, step).wait_send()


def block_pass(fields, cot, valid, kept, mlp, filt, small, snaps, group):
    snap_local, row_local, lon_total, channel = fields.shape
    tokens = snap_local * row_local * lon_total
    hidden = mlp.shape[2]
    lat_total = row_local * group
    modes = kept.shape[1] * group
    owned = channel // group
    width = 512
    parts = hidden // width
    levels = group // 2
    quarter = width // snaps
    low, f32 = jnp.bfloat16, jnp.float32
    half = width // 2
    half_snaps = snap_local // 2
    lon_f, lon_i = lon_matrix(lon_total, modes, half_snaps, row_local)

    def paired(array):
        return jnp.transpose(array, (0, 2, 1, 3)).reshape(-1, row_local, channel)

    lat_f = lat_matrix(lat_total, modes)
    pair = 2 * modes * row_local
    spread = half_snaps * row_local * 2 * modes
    inputs = dict(
        small=small,
        kept=kept.T,
        fields=paired(fields),
        lon_f=jnp.asarray(np.ascontiguousarray(lon_f.T)),
        filt=filt,
        lat_f=jnp.asarray(lat_f),
        lat_b=jnp.asarray(np.ascontiguousarray(lat_f.T)),
        cot=paired(cot),
        lon_i=jnp.asarray(lon_i),
        valid=valid,
        turn=jnp.asarray(lon_turn(lon_total, row_local)),
        lon_it=jnp.asarray(np.ascontiguousarray(lon_i.T)),
        lon_ft=jnp.asarray(lon_f),
        mlp=mlp,
    )
    outputs = dict(
        out=jax.ShapeDtypeStruct((tokens // row_local, row_local, channel), low),
        in_grad=jax.ShapeDtypeStruct((tokens // row_local, row_local, channel), f32),
        grad_mlp=jax.ShapeDtypeStruct((parts, snaps, 2, owned, quarter), low),
        grad_filt=jax.ShapeDtypeStruct((4, owned, 128), f32),
        grad_small=jax.ShapeDtypeStruct((16, 128), f32),
    )
    vmem = pltpu.VMEM
    dma = pltpu.SemaphoreType.DMA
    scratch = {
        name + "_in": vmem(value.shape, value.dtype)
        for name, value in inputs.items()
        if name not in ("mlp", "fields", "cot")
    }
    strip = divisor(tokens // 2, 48, 144)
    scratch |= dict(
        mlp_part=vmem((2, 2, owned, width), f32),
        fields_in=vmem((tokens, channel), low),
        fields_sem=dma((tokens // strip,)),
        cot_sem=dma((tokens // strip,)),
        cot_in=vmem((tokens, channel), low),
        grid=vmem((tokens, channel), f32),
        back=vmem((tokens, channel), f32),
        normed=vmem((tokens, channel), low),
        normed_turned=vmem((channel, tokens), low),
        cot_turned=vmem((channel, tokens), low),
        unit_one=vmem((tokens, channel), low),
        unit_two=vmem((tokens, channel), low),
        scale_one=vmem((tokens, 1), f32),
        scale_two=vmem((tokens, 1), f32),
        own_small=vmem((16 + kept.shape[0], 128), f32),
        all_small=vmem((group, 16 + kept.shape[0], 128), f32),
        gains=vmem((16, channel), f32),
        keep=vmem((lat_total * modes, 128), f32),
        own_w=vmem((parts, 2, snaps, owned, quarter), low),
        all_w=vmem((parts, 2, snaps, channel, quarter), low),
        modes=vmem((2, group, half_snaps * pair * 3 // 4, 128), low),
        modes_got=vmem((2, group, half_snaps * pair * 3 // 4, 128), low),
        rows_out=vmem((2, group, half_snaps * pair * 3 // 4, 128), low),
        rows_got=vmem((2, group, half_snaps * pair * 3 // 4, 128), low),
        arrived=vmem((snap_local, pair * group, 128), low),
        gathered=vmem((2, spread, channel), f32),
        home_low=vmem((2, spread, channel), low),
        weight_one=vmem((256, 256), low),
        weight_two=vmem((256, 256), low),
        spectrum=vmem((snap_local * lat_total * modes, 256), low),
        pre_one=vmem((snap_local * lat_total * modes, 256), f32),
        act_one=vmem((snap_local * lat_total * modes, 256), low),
        pre_two=vmem((snap_local * lat_total * modes, 256), f32),
        grad_pre=vmem((snap_local * lat_total * modes, 256), f32),
        grad_two=vmem((snap_local * lat_total * modes, 256), low),
        grad_one=vmem((snap_local * lat_total * modes, 256), low),
        folds=vmem((5, 8, channel), f32),
        pair_grad=vmem((256, 256), f32),
        act=vmem((tokens, width), low),
        slope=vmem((tokens, width), low),
        bias=vmem((parts, 1, width), f32),
        grad_bias=vmem((parts, 8, width), f32),
        grad_rows=vmem((16, channel), f32),
        grads=vmem((2, levels, 2, owned, width), low),
        core_got=vmem((2, 2, levels, owned, width), low),
        half_out=vmem((2, 2, 2, levels, owned, half), low),
        half_got=vmem((4, 2, levels, owned, half), low),
        quarter_out=vmem((2, 2, 2, levels, owned, quarter), low),
        quarter_got=vmem((2, 2, levels, owned, quarter), low),
        level_out=vmem((2, levels, 2, owned, quarter), low),
        level_got=vmem((4, levels, 2, owned, quarter), low),
        total=vmem((parts, snaps, 2, owned, quarter), low),
        filt_out=vmem((snaps, 4, owned, 128), low),
        tiles=vmem((group, 16, 128), f32),
        tiles_got=vmem((group, 16, 128), f32),
        snap_tiles=vmem((snaps, 16, 128), f32),
        swap_l=dma((4,)),
        load_sem=dma((len(inputs) + 1,)),
    )
    for name, shape in dict(
        small=(group,),
        swap=(4,),
        first=(parts, levels),
        second=(parts,),
        third=(parts,),
        fourth=(parts,),
        block=(2, 2, group),
        row=(2, 2, group),
        core=(2, 2),
        half=(4, 2),
        quarter=(2, 2),
        level=(4, levels),
        last=(parts, snaps),
        filt=(snaps,),
        tile=(group,),
        snap_tile=(snaps,),
    ).items():
        scratch[name + "_s"] = dma(shape)
        scratch[name + "_r"] = dma(shape)
    names = [*inputs, *outputs, *scratch]
    far = pl.BlockSpec(memory_space=pl.ANY)
    near = pl.BlockSpec(memory_space=pltpu.VMEM)
    results = pl.pallas_call(
        functools.partial(block_body, names, (snaps, group, parts, width)),
        in_specs=[far] * len(inputs),
        out_specs=[far, far, far, near, near],
        out_shape=list(outputs.values()),
        scratch_shapes=list(scratch.values()),
        compiler_params=pltpu.CompilerParams(
            collective_id=0, has_side_effects=True, vmem_limit_bytes=VMEM_LIMIT
        ),
        cost_estimate=pl.CostEstimate(
            flops=12 * tokens * channel * hidden,
            bytes_accessed=4 * hidden * channel,
            transcendentals=tokens * hidden,
        ),
        name="block_pass",
    )(*inputs.values())
    return results


def adamw_near(master, first_mom, second_mom, gradient, step_rate):
    first_next = beta_one * (first_mom + gradient)
    second_next = beta_two * (second_mom + gradient * gradient)
    fix_one = 1.0 / (1.0 - beta_one**STEP)
    fix_two = 1.0 / (1.0 - beta_two**STEP)
    grown = second_next * fix_two
    bottom = grown * lax.rsqrt(grown) + adam_eps
    master_next = (1.0 - step_rate * decay_rate) * master - (
        (step_rate * fix_one) * first_next
    ) / bottom
    return (master_next, first_next, second_next, master_next.astype(jnp.bfloat16))


def step_body(names, positions, *refs):
    g = Refs()
    for name, ref in zip(names, refs, strict=True):
        setattr(g, name, ref)
    parts, snaps = g.grad_mlp.shape[:2]
    quarter = g.grad_mlp.shape[4]
    width = snaps * quarter
    chunks = g.near.shape[1]
    some = parts // chunks
    moments = ("w", "m", "v")
    results = ("new", "first", "second", "copy")

    pieces = g.far_sem.shape[2]
    ends = ((g.out, g.out_near, g.out_o), (g.in_grad, g.in_grad_near, g.in_grad_o))

    def passing(kind, piece, leg):
        size = ends[kind][0].shape[0] // pieces
        rows = pl.ds(piece * size, size)
        return pltpu.make_async_copy(
            ends[kind][leg].at[rows], ends[kind][leg + 1].at[rows], g.far_sem.at[leg, kind, piece]
        )

    through = [(kind, piece) for kind in range(2) for piece in range(pieces)]

    def chunk_cols(chunk):
        return pl.ds(chunk * some * width, some * width)

    def load(chunk):
        near = [
            pltpu.make_async_copy(
                getattr(g, "mlp_" + kind).at[:, :, chunk_cols(chunk)],
                g.near.at[index, chunk],
                g.near_sem.at[index, chunk],
            )
            for index, kind in enumerate(moments)
        ]
        near.append(
            pltpu.make_async_copy(
                g.grad_mlp.at[pl.ds(chunk * some, some)], g.grad_near.at[chunk], g.near_sem.at[3, chunk]
            )
        )
        return near

    def store(chunk):
        copies = [
            pltpu.make_async_copy(
                g.near.at[index, chunk],
                getattr(g, "mlp_" + kind).at[:, :, chunk_cols(chunk)],
                g.back_sem.at[index, chunk],
            )
            for index, kind in enumerate(results[:3])
        ]
        copies.append(
            pltpu.make_async_copy(
                g.low_near.at[chunk], g.mlp_copy.at[:, :, chunk_cols(chunk)], g.back_sem.at[3, chunk]
            )
        )
        return copies

    coming = [load(chunk) for chunk in range(chunks)]
    going = [store(chunk) for chunk in range(chunks)]
    for chunk in range(chunks):
        for copy in coming[chunk]:
            copy.start()
        for each in through[chunk::chunks]:
            passing(*each, 0).start()

    def put(prefix, values):
        for kind, value in zip(results, values, strict=True):
            getattr(g, prefix + kind)[...] = value

    owned = g.filt_w.shape[2]
    put(
        "filt_",
        adamw(g.filt_w[...], g.filt_m[...], g.filt_v[...], g.grad_filt[:, :, 0:owned], rate_filter),
    )
    rows = g.small_w.shape[0]
    put(
        "small_",
        adamw(
            g.small_w[...], g.small_m[...], g.small_v[...], g.grad_small[0:rows, 0:owned], rate_small
        ),
    )
    totals = g.grad_small[rows : rows + 2, 0 : g.run.shape[1]]
    g.stats[...] = stat_decay * g.run[...] + (1.0 - stat_decay) * totals / positions

    for chunk in range(chunks):
        for copy in coming[chunk]:
            copy.wait()
        for part, matrix, snap in [
            (part, matrix, snap)
            for part in range(some)
            for matrix in range(2)
            for snap in range(snaps)
        ]:
            place = snap if matrix else 2 * (snap % 2) + snap // 2
            first_col = part * width + place * quarter
            where = (chunk, matrix, slice(None), slice(first_col, first_col + quarter))
            now = [g.near[(kind, *where)] for kind in range(3)]
            grad = g.grad_near[chunk, part, snap, matrix].astype(jnp.float32)
            values = adamw_near(*now, grad, rate_mlp)
            for kind in range(3):
                g.near[(kind, *where)] = values[kind]
            g.low_near[where] = values[3]
        for copy in going[chunk]:
            copy.start()
        for each in through[chunk::chunks]:
            passing(*each, 0).wait()
            passing(*each, 1).start()
    for each in through:
        passing(*each, 1).wait()
    for chunk in range(chunks):
        for copy in going[chunk]:
            copy.wait()


def step_pass(shown, grads, masters, run_stats, positions):
    grad_mlp, grad_filt, grad_small = grads
    mlp, filt, small = masters
    chunks = grad_mlp.shape[0]
    width = mlp[0].shape[2] // chunks
    f32, low = jnp.float32, jnp.bfloat16
    far = pl.BlockSpec(memory_space=pltpu.HBM)
    near = pl.BlockSpec(memory_space=pltpu.VMEM)
    inputs = dict(out=shown[0], in_grad=shown[1], grad_mlp=grad_mlp)
    inputs |= dict(zip(("mlp_w", "mlp_m", "mlp_v"), mlp, strict=True))
    far_in = len(inputs)
    inputs |= dict(grad_filt=grad_filt, grad_small=grad_small)
    inputs |= dict(zip(("filt_w", "filt_m", "filt_v"), filt, strict=True))
    inputs |= dict(zip(("small_w", "small_m", "small_v"), small, strict=True))
    inputs |= dict(run=run_stats)
    results = (("new", f32), ("first", f32), ("second", f32), ("copy", low))
    outputs = {
        name + "_o": jax.ShapeDtypeStruct(array.shape, array.dtype)
        for name, array in zip(("out", "in_grad"), shown, strict=True)
    }
    outputs |= {"mlp_" + kind: jax.ShapeDtypeStruct(mlp[0].shape, dt) for kind, dt in results}
    far_out = len(outputs)
    outputs |= {"filt_" + kind: jax.ShapeDtypeStruct(filt[0].shape, dt) for kind, dt in results}
    outputs |= {"small_" + kind: jax.ShapeDtypeStruct(small[0].shape, dt) for kind, dt in results}
    outputs |= dict(stats=jax.ShapeDtypeStruct(run_stats.shape, f32))
    scratch = dict(
        near=pltpu.VMEM((3, chunks, 2, mlp[0].shape[1], width), f32),
        grad_near=pltpu.VMEM((chunks, grad_mlp.shape[0] // chunks, *grad_mlp.shape[1:]), low),
        low_near=pltpu.VMEM((chunks, 2, mlp[0].shape[1], width), low),
        near_sem=pltpu.SemaphoreType.DMA((4, chunks)),
        back_sem=pltpu.SemaphoreType.DMA((4, chunks)),
        out_near=pltpu.VMEM(shown[0].shape, low),
        in_grad_near=pltpu.VMEM(shown[1].shape, f32),
        far_sem=pltpu.SemaphoreType.DMA((2, 2, divisor(shown[0].shape[0], 1, 4))),
    )
    return pl.pallas_call(
        functools.partial(step_body, [*inputs, *outputs, *scratch], positions),
        in_specs=[far] * far_in + [near] * (len(inputs) - far_in),
        out_specs=[far] * far_out + [near] * (len(outputs) - far_out),
        out_shape=list(outputs.values()),
        scratch_shapes=list(scratch.values()),
        compiler_params=pltpu.CompilerParams(vmem_limit_bytes=VMEM_LIMIT),
        name="step_pass",
    )(*inputs.values())


def per_device_blocks(
    fields,
    cotangent,
    valid_mask,
    kept_modes,
    mlp_master,
    mlp_first,
    mlp_second,
    filter_master,
    filter_first,
    filter_second,
    small_master,
    small_first,
    small_second,
    run_stats,
):
    snaps, group = lax.axis_size("snap"), lax.axis_size("sp")
    out, in_grad, *grads = block_pass(
        fields, cotangent, valid_mask, kept_modes, mlp_master, filter_master, small_master, snaps, group
    )
    snap_local, row_local, lon_total, channel = fields.shape
    positions = snap_local * snaps * row_local * group * lon_total
    out, in_grad, *stepped = step_pass(
        (out, in_grad),
        grads,
        (
            (mlp_master, mlp_first, mlp_second),
            (filter_master, filter_first, filter_second),
            (small_master, small_first, small_second),
        ),
        run_stats,
        positions,
    )
    rows_apart = (snap_local, lon_total, row_local, channel)
    out, in_grad = [
        jnp.transpose(array.reshape(rows_apart), (0, 2, 1, 3)) for array in (out, in_grad)
    ]
    return (out, in_grad, *stepped)


def per_device(*arrays):
    group, snaps = lax.axis_size("sp"), lax.axis_size("snap")
    channel, hidden = arrays[0].shape[3], arrays[4].shape[2]
    by_block = group == BLOCKS and snaps == 4 and arrays[3].shape[1] == 1
    if by_block and hidden == 6 * 512 and channel // group <= 128 and channel % (16 * group) == 0:
        return per_device_blocks(*arrays)
    return per_device_modes(*arrays)


def solution(mesh):
    return jax.shard_map(
        per_device,
        mesh=mesh,
        in_specs=(
            P("snap", "sp", None, None),
            P("snap", "sp", None, None),
            P("snap", "sp", None),
            P(None, "sp"),
            P(None, "sp", None),
            P(None, "sp", None),
            P(None, "sp", None),
            P(None, "sp", None),
            P(None, "sp", None),
            P(None, "sp", None),
            P(None, "sp"),
            P(None, "sp"),
            P(None, "sp"),
            P(),
        ),
        out_specs=(
            P("snap", "sp", None, None),
            P("snap", "sp", None, None),
            P(None, "sp", None),
            P(None, "sp", None),
            P(None, "sp", None),
            P(None, "sp", None),
            P(None, "sp", None),
            P(None, "sp", None),
            P(None, "sp", None),
            P(None, "sp", None),
            P(None, "sp"),
            P(None, "sp"),
            P(None, "sp"),
            P(None, "sp"),
            P(),
        ),
        check_vma=False,
    )
```
